32 devices in a mesh: section: 4 (over y, x), dp: 8 (over z, core).
Axes of the slice: x: 2, y: 2, z: 4, core: 2. Of those that a mesh axis runs over, the one named last changes fastest.
Arguments:
- tokens: bfloat16 [96, 237, 768], P(('section', 'dp')), may hold values from -6 to 6
- caption_lengths: int32 [96], P(('section', 'dp')), may hold values from 8 to 40, as said below
- attend_gain: float32 [4, 768], P('section'), may hold values from 0.5 to 1.5
- attend_shift: float32 [4, 768], P('section'), may hold values from -1.25 to 1.25
- attend_inputs: bfloat16 [4, 768, 2304], P('section'), may hold values from -0.21875 to 0.21875
- attend_bias: float32 [4, 2304], P('section'), may hold values from -1.25 to 1.25
- attend_output: bfloat16 [4, 768, 768], P('section'), may hold values from -1.75 to 1.75
- expert_gain: float32 [4, 768], P('section'), may hold values from 0.5 to 1.5
- expert_shift: float32 [4, 768], P('section'), may hold values from -1.25 to 1.25
- expert_inputs: bfloat16 [4, 768, 3072], P('section'), may hold values from -0.21875 to 0.21875
- expert_inner_bias: float32 [4, 3072], P('section'), may hold values from -1.75 to 1.75
- expert_outputs: bfloat16 [4, 3072, 768], P('section'), may hold values from -0.109375 to 0.109375
- expert_outer_bias: float32 [4, 768], P('section'), may hold values from -1.25 to 1.25
- cotangent: bfloat16 [96, 237, 768], P(('section', 'dp')), may hold values from -6 to 6
Outputs:
- layer_output: bfloat16 [96, 237, 768], P(('section', 'dp'))
- tokens_grad: bfloat16 [96, 237, 768], P(('section', 'dp'))
- attend_gain_grad: float32 [4, 768], P('section')
- attend_shift_grad: float32 [4, 768], P('section')
- attend_inputs_grad: float32 [4, 768, 2304], P('section')
- attend_bias_grad: float32 [4, 2304], P('section')
- attend_output_grad: float32 [4, 768, 768], P('section')
- expert_gain_grad: float32 [4, 768], P('section')
- expert_shift_grad: float32 [4, 768], P('section')
- expert_inputs_grad: float32 [4, 768, 3072], P('section')
- expert_inner_bias_grad: float32 [4, 3072], P('section')
- expert_outputs_grad: float32 [4, 3072, 768], P('section')
- expert_outer_bias_grad: float32 [4, 768], P('section')
- expert_counts: int32 [3], replicated
The draws below stay inside these ranges and needn't reach their ends.
Inputs may be any that keep to these rules, and one draw needn't show every extreme that they name: `caption_lengths`: number of true caption tokens of an item; the rest of its 40 caption slots is padding.
All inputs are finite; a program needn't handle non-finite values.
Results may differ from the reference program's by a relative error of at most 0.02.
Values may be sent and summed in bfloat16 or wider, within the bound.
No kernel may reach another device: no remote copies, remote signals or barrier semaphores. Data moves between devices by JAX's collectives and lax.ppermute only.
A program may use at most 256 MiB of HBM per device.

```python
import jax
import jax.numpy as jnp
from jax import lax

D = 768
HEADS = 12
HEAD_DIM = 64
FF = 3072
PATCHES = 197
CAPTION = 40
CAP_MIN = 8
ITEMS_MB = 3
SEQ = 237
ITEMS = 96
N_SECTION = 4


def draw_caption_lengths(key, part):
    key = jax.random.fold_in(key, 11)
    item_index = jnp.arange(ITEMS)
    length_room = CAPTION - CAP_MIN
    length_span = length_room * (item_index + 1) // ITEMS
    random_extra = jax.random.randint(key, (ITEMS,), 0, length_room + 1)
    lengths = CAP_MIN + random_extra % (length_span + 1)
    lengths = jnp.where(item_index == ITEMS - 1, CAPTION, lengths)
    return lengths.astype(jnp.int32)


def shard_levels(own_key, extent, shards, low, largest):
    level = 1.0
    for position, shards_of in shards:
        heights = jax.random.uniform(jax.random.fold_in(jax.random.fold_in(own_key, 6), position), (shards_of,), jnp.float32, low / len(shards), largest / len(shards))
        level = level * jnp.repeat(jnp.exp(heights), extent[position] // shards_of).reshape((-1,) + (1,) * (len(extent) - 1 - position))
    return level


def centred(key, extent, scale, reach, shards=(), kind=jnp.bfloat16):
    drawn = scale * jax.random.normal(key, extent, jnp.float32)
    if shards:
        drawn = drawn * shard_levels(key, extent, shards, -0.22, 0.18)
    return jnp.clip(drawn, -reach, reach).astype(kind)


def setup_inputs(seed: int = 0) -> dict:
    seeds = jax.random.split(jax.random.key(seed), 15)
    tokens = centred(seeds[0], (ITEMS, SEQ, D), 1.0, 6.0, ((0, 32),))
    caption_lengths = draw_caption_lengths(jax.random.fold_in(seeds[14], 71), 0)
    attend_gain = jnp.clip(1.0 + 0.1 * jax.random.normal(seeds[2], (N_SECTION, D), jnp.float32), 0.5, 1.5)
    attend_shift = centred(seeds[3], (N_SECTION, D), 0.2, 1.25, ((0, 4),), jnp.float32)
    attend_inputs = centred(seeds[4], (N_SECTION, D, 3 * D), D ** -0.5, 0.21875, ((0, 4),))
    attend_bias = centred(seeds[5], (N_SECTION, 3 * D), 0.2, 1.25, ((0, 4),), jnp.float32)
    attend_output = centred(seeds[6], (N_SECTION, D, D), (D * 4 // SEQ) ** -0.5, 1.75, ((0, 4),))
    expert_gain = jnp.clip(1.0 + 0.1 * jax.random.normal(seeds[7], (N_SECTION, D), jnp.float32), 0.5, 1.5)
    expert_shift = centred(seeds[8], (N_SECTION, D), 0.2, 1.25, ((0, 4),), jnp.float32)
    expert_inputs = centred(seeds[9], (N_SECTION, D, FF), D ** -0.5, 0.21875, ((0, 4),))
    expert_inner_bias = centred(seeds[10], (N_SECTION, FF), 0.3, 1.75, ((0, 4),), jnp.float32)
    expert_outputs = centred(seeds[11], (N_SECTION, FF, D), FF ** -0.5, 0.109375, ((0, 4),))
    expert_outer_bias = centred(seeds[12], (N_SECTION, D), 0.2, 1.25, ((0, 4),), jnp.float32)
    cotangent = centred(seeds[13], (ITEMS, SEQ, D), 1.0, 6.0, ((0, 32),))
    return dict(tokens=tokens, caption_lengths=caption_lengths, attend_gain=attend_gain, attend_shift=attend_shift, attend_inputs=attend_inputs, attend_bias=attend_bias, attend_output=attend_output, expert_gain=expert_gain, expert_shift=expert_shift, expert_inputs=expert_inputs, expert_inner_bias=expert_inner_bias, expert_outputs=expert_outputs, expert_outer_bias=expert_outer_bias, cotangent=cotangent)


@jax.custom_vjp
def low(v):
    return lax.optimization_barrier(v.astype(jnp.bfloat16)).astype(jnp.float32)

@jax.custom_vjp
def low_back(v):
    return v

def low_keep(v):
    return (low(v), None)

def low_pass(kept, grad):
    return (grad,)

def back_keep(v):
    return (v, None)

def back_low(kept, grad):
    return (low(grad),)
low.defvjp(low_keep, low_pass)
low_back.defvjp(back_keep, back_low)

def layer_norm(inputs, gain_row, shift_row):
    centre = inputs - lax.optimization_barrier(jnp.mean(inputs, axis=-1, keepdims=True))
    spread = lax.optimization_barrier(jnp.mean(centre * centre, axis=-1, keepdims=True))
    return centre * lax.rsqrt(spread + 1e-06) * gain_row + shift_row

def project(inputs, matrix):
    return jnp.einsum('bpi,ij->bpj', inputs, matrix, precision=lax.Precision.HIGHEST)

def attention_block(hidden, token_mask, gain_row, shift_row, inputs, bias_row, output):
    item_count, positions, features = hidden.shape
    head_shape = (item_count, positions, HEADS, HEAD_DIM)
    normed = low(layer_norm(hidden, gain_row, shift_row))
    projected = project(normed, inputs)
    queries = (projected[..., :features] + bias_row[:features]) * HEAD_DIM ** (-0.5)
    key_heads = projected[..., features:2 * features]
    value_heads = projected[..., 2 * features:] + bias_row[features:2 * features]
    queries = low_back(low(queries)).reshape(head_shape)
    key_heads = low_back(low(key_heads)).reshape(head_shape)
    value_heads = low_back(low(value_heads)).reshape(head_shape)
    scores = jnp.einsum('bqhd,bkhd->bhqk', queries, key_heads, precision=lax.Precision.HIGHEST)
    scores = low_back(scores)
    scores = jnp.where(token_mask[:, None, None, :] > 0, scores, -1000000000.0)
    attention = low(jax.nn.softmax(scores, axis=-1))
    mixed_heads = jnp.einsum('bhqk,bkhd->bqhd', attention, value_heads, precision=lax.Precision.HIGHEST)
    mixed_heads = low_back(low(mixed_heads.reshape(item_count, positions, features)))
    branch = low_back(project(mixed_heads, output) + bias_row[2 * features:])
    return hidden + token_mask[..., None] * branch

def expert_block(hidden, token_mask, gain_row, shift_row, inputs, inner_bias, outputs, outer_bias):
    normed = low(layer_norm(hidden, gain_row, shift_row))
    inner_pre = low_back(project(normed, inputs) + inner_bias)
    activated = low(jax.nn.gelu(inner_pre, approximate=False))
    branch = low_back(project(activated, outputs) + outer_bias)
    return hidden + token_mask[..., None] * branch

def forward(tokens, lengths, params):
    attend_gain, attend_shift, attend_inputs, attend_bias, attend_output, expert_gain, expert_shift, expert_inputs, expert_inner_bias, expert_outputs, expert_outer_bias = params
    positions = jnp.arange(SEQ)
    token_mask = ((positions[None, :] < PATCHES) | (positions[None, :] - PATCHES < lengths[:, None])).astype(jnp.float32)

    def attend(hidden, slot_index):
        return attention_block(hidden, token_mask, attend_gain[slot_index], attend_shift[slot_index], attend_inputs[slot_index], attend_bias[slot_index], attend_output[slot_index])

    def expert(hidden, slot_index, first_row, last_row):
        return expert_block(hidden[:, first_row:last_row], token_mask[:, first_row:last_row], expert_gain[slot_index], expert_shift[slot_index], expert_inputs[slot_index], expert_inner_bias[slot_index], expert_outputs[slot_index], expert_outer_bias[slot_index])
    hidden = attend(tokens, 0)
    hidden = jnp.concatenate([hidden[:, :PATCHES], expert(hidden, 0, PATCHES, SEQ)], axis=1)
    hidden = low_back(low(hidden))
    hidden = jnp.concatenate([expert(hidden, 1, 0, PATCHES), hidden[:, PATCHES:]], axis=1)
    hidden = low_back(low(hidden))
    hidden = low_back(low(attend(hidden, 2)))
    return expert(hidden, 3, 0, SEQ)

def reference(tokens, caption_lengths, attend_gain, attend_shift, attend_inputs, attend_bias, attend_output, expert_gain, expert_shift, expert_inputs, expert_inner_bias, expert_outputs, expert_outer_bias, cotangent):
    params = tuple((argument.astype(jnp.float32) for argument in (attend_gain, attend_shift, attend_inputs, attend_bias, attend_output, expert_gain, expert_shift, expert_inputs, expert_inner_bias, expert_outputs, expert_outer_bias)))
    group_items = ITEMS_MB * N_SECTION
    group_count = tokens.shape[0] // group_items

    def one_group(totals, group_block):
        group_tokens, group_lengths, group_cotangent = group_block
        output, pullback = jax.vjp(lambda inputs, weights: forward(inputs, group_lengths, weights), group_tokens.astype(jnp.float32), params)
        tokens_grad, weight_grads = pullback(group_cotangent.astype(jnp.float32))
        totals = tuple((total_sum + grad_part for total_sum, grad_part in zip(totals, weight_grads)))
        return (totals, (output.astype(jnp.bfloat16), tokens_grad.astype(jnp.bfloat16)))
    zero_sums = tuple((jnp.zeros_like(argument) for argument in params))
    stacked = (tokens.reshape(group_count, group_items, SEQ, D), caption_lengths.reshape(group_count, group_items), cotangent.reshape(group_count, group_items, SEQ, D))
    totals, (output, tokens_grad) = lax.scan(one_group, zero_sums, stacked)
    language_count = jnp.sum(caption_lengths, dtype=jnp.int32)
    vision_count = jnp.full((), PATCHES * caption_lengths.shape[0], jnp.int32)
    counts = jnp.stack([vision_count, language_count, vision_count + language_count])
    as_float = counts.astype(jnp.float32)
    one_value = jnp.ones((), jnp.float32)
    attend_scale = jnp.stack([as_float[2], one_value, as_float[2], one_value])
    expert_scale = jnp.stack([as_float[1], as_float[0], one_value, as_float[2]])
    scaled_grads = [total_sum / attend_scale.reshape((N_SECTION,) + (1,) * (total_sum.ndim - 1)) for total_sum in totals[:5]]
    scaled_grads += [total_sum / expert_scale.reshape((N_SECTION,) + (1,) * (total_sum.ndim - 1)) for total_sum in totals[5:]]
    return (output.reshape(tokens.shape), tokens_grad.reshape(tokens.shape), scaled_grads[0], scaled_grads[1], scaled_grads[2], scaled_grads[3], scaled_grads[4], scaled_grads[5], scaled_grads[6], scaled_grads[7], scaled_grads[8], scaled_grads[9], scaled_grads[10], counts)
```

```python
from functools import partial

import jax
import jax.numpy as jnp
from jax import lax
from jax.experimental import pallas as pl
from jax.experimental.pallas import tpu as pltpu
from jax.sharding import PartitionSpec as P

HEADS = 12
HEAD_DIM = 64
PATCHES = 197
ROWS = 256
CHUNK = 512
EVERYWHERE = ("dp", "section")
VMEM_BYTES = 56 * 1024 * 1024
F32 = jnp.float32
BF16 = jnp.bfloat16


def dot_plain(left, right):
    return jnp.dot(left, right, preferred_element_type=F32)


def dot_last(left, right):
    return lax.dot_general(left, right, (((1,), (1,)), ((), ())), preferred_element_type=F32)


def dot_first(left, right):
    return lax.dot_general(left, right, (((0,), (0,)), ((), ())), preferred_element_type=F32)


def norm_parts(rows):
    centre = rows - jnp.mean(rows, axis=-1, keepdims=True)
    scale = lax.rsqrt(jnp.mean(centre * centre, axis=-1, keepdims=True) + 1e-06)
    return centre * scale, scale


def norm_back(normed_grad, unit, scale, gain):
    unit_grad = normed_grad * gain
    along = jnp.mean(unit_grad * unit, axis=-1, keepdims=True)
    return scale * (unit_grad - jnp.mean(unit_grad, axis=-1, keepdims=True) - unit * along)


def true_positions(length, first, count, axis, kind):
    shape = (count, 1) if axis == 0 else (1, count)
    position = first + lax.broadcasted_iota(jnp.int32, shape, axis)
    patch = position < PATCHES
    if kind == "patch":
        return patch
    caption = (position >= PATCHES) & (position - PATCHES < length)
    return caption if kind == "caption" else patch | caption


def head_masks():
    lane = lax.broadcasted_iota(jnp.int32, (1, 2 * HEAD_DIM), 1)
    even = (lane < HEAD_DIM).astype(F32).astype(BF16)
    odd = (lane >= HEAD_DIM).astype(F32).astype(BF16)
    return lane < HEAD_DIM, even, odd


def split_pair(pair, even, odd):
    return jnp.concatenate([pair * even, pair * odd], axis=0)


def attend_forward_kernel(
    lens, x_ref, gain_ref, shift_ref, inputs_ref, output_ref, bias_ref, y_ref, qkv_ref, mixed_ref
):
    length = lens[pl.program_id(0)]
    width = x_ref.shape[-1]
    x = x_ref[0].astype(F32)
    unit, _ = norm_parts(x)
    normed = (unit * gain_ref[...] + shift_ref[...]).astype(BF16)
    queries = dot_plain(normed, inputs_ref[:, :width]) + bias_ref[:, :width]
    qkv_ref[0, :, :width] = (queries * HEAD_DIM ** (-0.5)).astype(BF16)
    qkv_ref[0, :, width : 2 * width] = dot_plain(normed, inputs_ref[:, width : 2 * width]).astype(
        BF16
    )
    values = dot_plain(normed, inputs_ref[:, 2 * width :]) + bias_ref[:, width : 2 * width]
    qkv_ref[0, :, 2 * width :] = values.astype(BF16)
    key_true = true_positions(length, 0, ROWS, 1, "all")
    low_half, even, odd = head_masks()
    ones = jnp.ones((ROWS, 2 * HEAD_DIM), BF16)
    for pair in range(HEADS // 2):
        at = pair * 2 * HEAD_DIM
        q2 = qkv_ref[0, :, at : at + 2 * HEAD_DIM]
        k2 = qkv_ref[0, :, width + at : width + at + 2 * HEAD_DIM]
        v2 = qkv_ref[0, :, 2 * width + at : 2 * width + at + 2 * HEAD_DIM]
        scores = jnp.where(key_true, dot_last(split_pair(q2, even, odd), k2), -1e9)
        largest = jnp.max(scores, axis=-1, keepdims=True)
        weight = jnp.exp(scores - largest).astype(BF16)
        summed = dot_plain(weight, jnp.concatenate([v2, ones], axis=1))
        top = jnp.where(low_half, summed[:ROWS, : 2 * HEAD_DIM], summed[ROWS:, : 2 * HEAD_DIM])
        below = jnp.where(low_half, summed[:ROWS, 2 * HEAD_DIM :], summed[ROWS:, 2 * HEAD_DIM :])
        mixed_ref[0, :, at : at + 2 * HEAD_DIM] = (top / below).astype(BF16)
    branch = dot_plain(mixed_ref[0], output_ref[...]) + bias_ref[:, 2 * width :]
    row_true = true_positions(length, 0, ROWS, 0, "all")
    y_ref[0] = (x + jnp.where(row_true, branch, 0.0)).astype(y_ref.dtype)


def attend_backward_kernel(
    lens,
    x_ref,
    gain_ref,
    shift_ref,
    inputs_ref,
    output_ref,
    qkv_ref,
    mixed_ref,
    grad_ref,
    out_ref,
    weight_ref,
    gain_grad_ref,
    shift_grad_ref,
    bias_grad_ref,
    normed_turned,
    mixed_turned,
    branch_all,
    projected,
    mixed_grad,
):
    item = pl.program_id(0)
    items = pl.num_programs(0)
    length = lens[item]
    width = x_ref.shape[-1]
    here = pl.ds(pl.multiple_of(item * ROWS, ROWS), ROWS)
    x = x_ref[0].astype(F32)
    unit, scale = norm_parts(x)
    normed = (unit * gain_ref[...] + shift_ref[...]).astype(BF16)
    incoming = grad_ref[0].astype(F32)
    row_true = true_positions(length, 0, ROWS, 0, "all")
    branch = jnp.where(row_true, incoming, 0.0).astype(BF16)
    branch_all[here, :] = branch
    normed_turned[:, here] = normed.T
    mixed_turned[:, here] = mixed_ref[0].T
    mixed_grad[...] = dot_last(branch, output_ref[...]).astype(BF16)
    key_true = true_positions(length, 0, ROWS, 0, "all")
    _, even, odd = head_masks()
    for pair in range(HEADS // 2):
        at = pair * 2 * HEAD_DIM
        q2 = split_pair(qkv_ref[0, :, at : at + 2 * HEAD_DIM], even, odd)
        k2 = qkv_ref[0, :, width + at : width + at + 2 * HEAD_DIM]
        v2 = qkv_ref[0, :, 2 * width + at : 2 * width + at + 2 * HEAD_DIM]
        g2 = split_pair(mixed_grad[:, at : at + 2 * HEAD_DIM], even, odd)
        scores = jnp.where(key_true, dot_last(k2, q2), -1e9)
        weight = jnp.exp(scores - jnp.max(scores, axis=0, keepdims=True))
        weight = weight / jnp.sum(weight, axis=0, keepdims=True)
        weight_grad = dot_last(v2, g2)
        along = jnp.sum(weight * weight_grad, axis=0, keepdims=True)
        score_grad = (weight * (weight_grad - along)).astype(BF16)
        values_grad = dot_plain(weight.astype(BF16), g2).astype(BF16)
        keys_grad = dot_plain(score_grad, q2).astype(BF16)
        k2_split = split_pair(k2, even, odd)
        stacked = jnp.concatenate([score_grad[:, :ROWS], score_grad[:, ROWS:]], axis=0)
        queries_grad = dot_first(stacked, k2_split).astype(BF16)
        queries_grad = (queries_grad.astype(F32) * HEAD_DIM ** (-0.5)).astype(BF16)
        projected[here, at : at + 2 * HEAD_DIM] = queries_grad
        projected[here, width + at : width + at + 2 * HEAD_DIM] = keys_grad
        projected[here, 2 * width + at : 2 * width + at + 2 * HEAD_DIM] = values_grad
    normed_grad = dot_last(projected[here, :], inputs_ref[...])
    out_ref[0] = (incoming + norm_back(normed_grad, unit, scale, gain_ref[...])).astype(
        out_ref.dtype
    )
    gain_part = jnp.sum(normed_grad * unit, axis=0, keepdims=True)
    shift_part = jnp.sum(normed_grad, axis=0, keepdims=True)

    @pl.when(item == 0)
    def _():
        gain_grad_ref[...] = gain_part
        shift_grad_ref[...] = shift_part

    @pl.when(item > 0)
    def _():
        gain_grad_ref[...] += gain_part
        shift_grad_ref[...] += shift_part

    @pl.when(item == items - 1)
    def _():
        for at in range(0, 3 * width, width):
            weight_ref[:, at : at + width] = dot_plain(
                normed_turned[...], projected[:, at : at + width]
            ).astype(BF16)
        weight_ref[:, 3 * width :] = dot_plain(mixed_turned[...], branch_all[...]).astype(BF16)
        bias_grad_ref[:, :width] = jnp.sum(
            projected[:, :width].astype(F32), axis=0, keepdims=True
        )
        bias_grad_ref[:, width : 2 * width] = jnp.sum(
            projected[:, 2 * width :].astype(F32), axis=0, keepdims=True
        )
        bias_grad_ref[:, 2 * width :] = jnp.sum(
            branch_all[...].astype(F32), axis=0, keepdims=True
        )


def whole_block(shape):
    return pl.BlockSpec(shape, lambda step, lens: (0,) * len(shape))


def item_block(shape):
    return pl.BlockSpec((1,) + shape[1:], lambda step, lens: (step,) + (0,) * (len(shape) - 1))


def attend_forward(x, lengths, gain, shift, weights, bias, kind):
    items, _, width = x.shape
    flops = 2 * items * ROWS * width * (4 * width + 4 * ROWS)
    return pl.pallas_call(
        attend_forward_kernel,
        grid_spec=pltpu.PrefetchScalarGridSpec(
            num_scalar_prefetch=1,
            grid=(items,),
            in_specs=[
                item_block(x.shape),
                whole_block((1, width)),
                whole_block((1, width)),
                pl.BlockSpec((width, 3 * width), lambda step, lens: (0, 0)),
                pl.BlockSpec((width, width), lambda step, lens: (0, 3)),
                whole_block((1, 3 * width)),
            ],
            out_specs=[
                item_block(x.shape),
                item_block((items, ROWS, 3 * width)),
                item_block((items, ROWS, width)),
            ],
        ),
        out_shape=[
            jax.ShapeDtypeStruct(x.shape, kind),
            jax.ShapeDtypeStruct((items, ROWS, 3 * width), BF16),
            jax.ShapeDtypeStruct((items, ROWS, width), BF16),
        ],
        compiler_params=pltpu.CompilerParams(vmem_limit_bytes=VMEM_BYTES),
        cost_estimate=pl.CostEstimate(
            flops=flops, bytes_accessed=16_000_000, transcendentals=items * HEADS * ROWS * ROWS
        ),
        name="attend_forward",
    )(lengths, x, gain, shift, weights, weights, bias)


def attend_backward(x, lengths, gain, shift, weights, qkv, mixed, incoming, kind):
    items, _, width = x.shape
    flops = 4 * items * ROWS * width * (4 * width + 5 * ROWS)
    return pl.pallas_call(
        attend_backward_kernel,
        grid_spec=pltpu.PrefetchScalarGridSpec(
            num_scalar_prefetch=1,
            grid=(items,),
            in_specs=[
                item_block(x.shape),
                whole_block((1, width)),
                whole_block((1, width)),
                pl.BlockSpec((width, 3 * width), lambda step, lens: (0, 0)),
                pl.BlockSpec((width, width), lambda step, lens: (0, 3)),
                item_block(qkv.shape),
                item_block(mixed.shape),
                item_block(incoming.shape),
            ],
            out_specs=[
                item_block(x.shape),
                whole_block((width, 4 * width)),
                whole_block((1, width)),
                whole_block((1, width)),
                whole_block((1, 3 * width)),
            ],
            scratch_shapes=[
                pltpu.VMEM((width, items * ROWS), BF16),
                pltpu.VMEM((width, items * ROWS), BF16),
                pltpu.VMEM((items * ROWS, width), BF16),
                pltpu.VMEM((items * ROWS, 3 * width), BF16),
                pltpu.VMEM((ROWS, width), BF16),
            ],
        ),
        out_shape=[
            jax.ShapeDtypeStruct(x.shape, kind),
            jax.ShapeDtypeStruct((width, 4 * width), BF16),
            jax.ShapeDtypeStruct((1, width), F32),
            jax.ShapeDtypeStruct((1, width), F32),
            jax.ShapeDtypeStruct((1, 3 * width), F32),
        ],
        compiler_params=pltpu.CompilerParams(vmem_limit_bytes=VMEM_BYTES),
        cost_estimate=pl.CostEstimate(
            flops=flops, bytes_accessed=24_000_000, transcendentals=items * HEADS * ROWS * ROWS
        ),
        name="attend_backward",
    )(lengths, x, gain, shift, weights, weights, qkv, mixed, incoming)


def normal_parts(u):
    size = jnp.abs(u) * 0.7071067811865476
    t = 1.0 / (1.0 + 0.3275911 * size)
    bell = jnp.exp(-size * size)
    poly = t * (
        0.254829592
        + t * (-0.284496736 + t * (1.421413741 + t * (-1.453152027 + t * 1.061405429)))
    )
    tail = 0.5 * poly * bell
    return jnp.where(u < 0, tail, 1.0 - tail), 0.3989422804014327 * bell


def expert_forward_kernel(
    first,
    count,
    kind,
    lens,
    x_ref,
    other_ref,
    gain_ref,
    shift_ref,
    inputs_ref,
    inner_ref,
    outputs_ref,
    outer_ref,
    y_ref,
    act_ref,
    slope_ref,
    normed,
    total,
):
    step = pl.program_id(0)
    items = x_ref.shape[0]

    @pl.when(step == 0)
    def _():
        for item in range(items):
            unit, _ = norm_parts(x_ref[item, first : first + count].astype(F32))
            normed[item * count : (item + 1) * count] = (
                unit * gain_ref[...] + shift_ref[...]
            ).astype(BF16)

    part = None
    for at in range(0, inputs_ref.shape[1], 256):
        inner = dot_plain(normed[...], inputs_ref[:, at : at + 256]) + inner_ref[:, at : at + 256]
        cumulative, density = normal_parts(inner)
        act = (inner * cumulative).astype(BF16)
        act_ref[:, at : at + 256] = act
        slope_ref[:, at : at + 256] = (cumulative + inner * density).astype(BF16)
        term = dot_plain(act, outputs_ref[at : at + 256])
        part = term if part is None else part + term

    @pl.when(step == 0)
    def _():
        total[...] = part

    @pl.when(step > 0)
    def _():
        total[...] += part

    @pl.when(step == pl.num_programs(0) - 1)
    def _():
        for item in range(items):
            row_true = true_positions(lens[item], first, count, 0, kind)
            branch = total[item * count : (item + 1) * count] + outer_ref[...]
            x = x_ref[item, first : first + count].astype(F32)
            y = x + jnp.where(row_true, branch, 0.0)
            if kind == "all":
                y_ref[item, :count] = y.astype(BF16)
                if count < ROWS:
                    y_ref[item, count:] = jnp.zeros((ROWS - count, y.shape[1]), BF16)
            elif kind == "caption":
                y_ref[item] = y.astype(BF16)
            else:
                start = ROWS - other_ref.shape[1]
                captions = other_ref[item].astype(F32)
                y = jnp.concatenate([y, jnp.zeros((ROWS - count, y.shape[1]), F32)], axis=0)
                captions = jnp.concatenate(
                    [jnp.zeros((start, y.shape[1]), F32), captions], axis=0
                )
                position = lax.broadcasted_iota(jnp.int32, (ROWS, 1), 0)
                y_ref[item] = jnp.where(position < PATCHES, y, captions).astype(BF16)


def expert_backward_kernel(
    first,
    count,
    kind,
    lens,
    x_ref,
    gain_ref,
    shift_ref,
    inputs_ref,
    outputs_ref,
    act_ref,
    slope_ref,
    grad_ref,
    out_ref,
    inputs_grad_ref,
    outputs_grad_ref,
    gain_grad_ref,
    shift_grad_ref,
    inner_grad_ref,
    outer_grad_ref,
    normed_turned,
    branch,
    total,
):
    step = pl.program_id(0)
    items = x_ref.shape[0]

    @pl.when(step == 0)
    def _():
        outer = None
        for item in range(items):
            unit, _ = norm_parts(x_ref[item, first : first + count].astype(F32))
            normed = (unit * gain_ref[...] + shift_ref[...]).astype(BF16)
            normed_turned[:, item * count : (item + 1) * count] = normed.T
            row_true = true_positions(lens[item], first, count, 0, kind)
            incoming = grad_ref[item, first : first + count].astype(F32)
            here = jnp.where(row_true, incoming, 0.0).astype(BF16)
            branch[item * count : (item + 1) * count] = here
            term = jnp.sum(here.astype(F32), axis=0, keepdims=True)
            outer = term if outer is None else outer + term
        outer_grad_ref[...] = outer

    part = None
    for at in range(0, inputs_ref.shape[1], 256):
        act_grad = dot_last(branch[...], outputs_ref[at : at + 256])
        inner = (slope_ref[:, at : at + 256].astype(F32) * act_grad).astype(BF16)
        inner_grad_ref[:, at : at + 256] = jnp.sum(inner.astype(F32), axis=0, keepdims=True)
        inputs_grad_ref[:, at : at + 256] = dot_plain(normed_turned[...], inner).astype(BF16)
        outputs_grad_ref[at : at + 256] = dot_first(
            act_ref[:, at : at + 256], branch[...]
        ).astype(BF16)
        term = dot_last(inner, inputs_ref[:, at : at + 256])
        part = term if part is None else part + term

    @pl.when(step == 0)
    def _():
        total[...] = part

    @pl.when(step > 0)
    def _():
        total[...] += part

    @pl.when(step == pl.num_programs(0) - 1)
    def _():
        gain_sum, shift_sum = None, None
        for item in range(items):
            unit, scale = norm_parts(x_ref[item, first : first + count].astype(F32))
            normed_grad = total[item * count : (item + 1) * count]
            gain_part = jnp.sum(normed_grad * unit, axis=0, keepdims=True)
            shift_part = jnp.sum(normed_grad, axis=0, keepdims=True)
            gain_sum = gain_part if gain_sum is None else gain_sum + gain_part
            shift_sum = shift_part if shift_sum is None else shift_sum + shift_part
            incoming = grad_ref[item, first : first + count].astype(F32)
            hidden = incoming + norm_back(normed_grad, unit, scale, gain_ref[...])
            if first > 0:
                out_ref[item, :first] = grad_ref[item, :first].astype(out_ref.dtype)
            out_ref[item, first : first + count] = hidden.astype(out_ref.dtype)
            if first + count < ROWS:
                out_ref[item, first + count :] = grad_ref[item, first + count :].astype(
                    out_ref.dtype
                )
        gain_grad_ref[...] = gain_sum
        shift_grad_ref[...] = shift_sum


def chunk_columns(rows):
    return pl.BlockSpec((rows, CHUNK), lambda step, lens: (0, step))


def chunk_rows(columns):
    return pl.BlockSpec((CHUNK, columns), lambda step, lens: (step, 0))


def expert_forward(x, other, lengths, gain, shift, inputs, inner, outputs, outer, place):
    first, count, kind = place
    items, _, width = x.shape
    hidden = inputs.shape[1]
    y_rows = count if kind == "caption" else ROWS
    return pl.pallas_call(
        partial(expert_forward_kernel, first, count, kind),
        grid_spec=pltpu.PrefetchScalarGridSpec(
            num_scalar_prefetch=1,
            grid=(hidden // CHUNK,),
            in_specs=[
                whole_block(x.shape),
                whole_block(other.shape),
                whole_block((1, width)),
                whole_block((1, width)),
                chunk_columns(width),
                chunk_columns(1),
                chunk_rows(width),
                whole_block((1, width)),
            ],
            out_specs=[
                whole_block((items, y_rows, width)),
                chunk_columns(items * count),
                chunk_columns(items * count),
            ],
            scratch_shapes=[
                pltpu.VMEM((items * count, width), BF16),
                pltpu.VMEM((items * count, width), F32),
            ],
        ),
        out_shape=[
            jax.ShapeDtypeStruct((items, y_rows, width), BF16),
            jax.ShapeDtypeStruct((items * count, hidden), BF16),
            jax.ShapeDtypeStruct((items * count, hidden), BF16),
        ],
        compiler_params=pltpu.CompilerParams(vmem_limit_bytes=VMEM_BYTES),
        cost_estimate=pl.CostEstimate(
            flops=4 * items * count * width * hidden,
            bytes_accessed=22_000_000,
            transcendentals=2 * items * count * hidden,
        ),
        name="expert_forward_" + kind,
    )(lengths, x, other, gain, shift, inputs, inner, outputs, outer)


def expert_backward(x, lengths, gain, shift, inputs, outputs, act, slope, incoming, out_kind, place):
    first, count, kind = place
    items, _, width = x.shape
    hidden = inputs.shape[1]
    return pl.pallas_call(
        partial(expert_backward_kernel, first, count, kind),
        grid_spec=pltpu.PrefetchScalarGridSpec(
            num_scalar_prefetch=1,
            grid=(hidden // CHUNK,),
            in_specs=[
                whole_block(x.shape),
                whole_block((1, width)),
                whole_block((1, width)),
                chunk_columns(width),
                chunk_rows(width),
                chunk_columns(items * count),
                chunk_columns(items * count),
                whole_block(incoming.shape),
            ],
            out_specs=[
                whole_block(incoming.shape),
                chunk_columns(width),
                chunk_rows(width),
                whole_block((1, width)),
                whole_block((1, width)),
                chunk_columns(1),
                whole_block((1, width)),
            ],
            scratch_shapes=[
                pltpu.VMEM((width, items * count), BF16),
                pltpu.VMEM((items * count, width), BF16),
                pltpu.VMEM((items * count, width), F32),
            ],
        ),
        out_shape=[
            jax.ShapeDtypeStruct(incoming.shape, out_kind),
            jax.ShapeDtypeStruct((width, hidden), BF16),
            jax.ShapeDtypeStruct((hidden, width), BF16),
            jax.ShapeDtypeStruct((1, width), F32),
            jax.ShapeDtypeStruct((1, width), F32),
            jax.ShapeDtypeStruct((1, hidden), F32),
            jax.ShapeDtypeStruct((1, width), F32),
        ],
        compiler_params=pltpu.CompilerParams(vmem_limit_bytes=VMEM_BYTES),
        cost_estimate=pl.CostEstimate(
            flops=8 * items * count * width * hidden,
            bytes_accessed=40_000_000,
            transcendentals=0,
        ),
        name="expert_backward_" + kind,
    )(lengths, x, gain, shift, inputs, outputs, act, slope, incoming)


WHOLE_PLACE = (0, 256, "all")
PATCH_PLACE = (0, 208, "patch")
CAPTION_PLACE = (192, 64, "caption")


def per_device(
    tokens,
    caption_lengths,
    attend_gain,
    attend_shift,
    attend_inputs,
    attend_bias,
    attend_output,
    expert_gain,
    expert_shift,
    expert_inputs,
    expert_inner_bias,
    expert_outputs,
    expert_outer_bias,
    cotangent,
):
    section = lax.axis_index("section")
    sections = lax.axis_size("section")
    group = lax.axis_index("dp")
    groups = lax.axis_size("dp")
    items, positions, width = tokens.shape
    hidden = expert_inputs.shape[-1]

    def to_every_section(matrix):
        rows = matrix.shape[0] // (groups * sections)
        own = matrix.reshape(groups, sections, rows, matrix.shape[1])
        own = lax.dynamic_index_in_dim(own, group, 0, keepdims=False)
        return lax.all_to_all(own, "section", 0, 0, tiled=True)

    def whole(piece):
        return lax.all_gather(piece, EVERYWHERE, axis=0, tiled=True)

    attend_pieces = to_every_section(jnp.concatenate([attend_inputs[0], attend_output[0]], axis=1))
    inputs_pieces = to_every_section(expert_inputs[0])
    outputs_pieces = to_every_section(expert_outputs[0])
    attend_weights = {slot: whole(attend_pieces[slot]) for slot in (0, 2)}
    inputs_weights = {slot: whole(inputs_pieces[slot]) for slot in (0, 1, 3)}
    outputs_weights = {slot: whole(outputs_pieces[slot]) for slot in (0, 1, 3)}
    rows = jnp.concatenate(
        [
            attend_gain,
            attend_shift,
            attend_bias,
            expert_gain,
            expert_shift,
            expert_inner_bias,
            expert_outer_bias,
        ],
        axis=1,
    )
    rows = lax.all_gather(rows, "section", axis=0, tiled=True)
    sizes = [width, width, 3 * width, width, width, hidden, width]
    ends = [sum(sizes[: at + 1]) for at in range(len(sizes))]

    def row(slot, which):
        return rows[slot : slot + 1, ends[which] - sizes[which] : ends[which]]

    language_count = jnp.sum(caption_lengths)
    vision_count = jnp.full((), PATCHES * caption_lengths.size, jnp.int32)
    counts = lax.psum(
        jnp.stack([vision_count, language_count, vision_count + language_count]), EVERYWHERE
    )

    pad = ((0, 0), (0, ROWS - positions), (0, 0))
    x0 = jnp.pad(tokens, pad)
    last_grad = jnp.pad(cotangent, pad)
    lens = caption_lengths

    y0, qkv0, mixed0 = attend_forward(
        x0, lens, row(0, 0), row(0, 1), attend_weights[0], row(0, 2), F32
    )
    captions, act0, slope0 = expert_forward(
        y0,
        lens.reshape(1, -1).astype(F32),
        lens,
        row(0, 3),
        row(0, 4),
        inputs_weights[0],
        row(0, 5),
        outputs_weights[0],
        row(0, 6),
        CAPTION_PLACE,
    )
    x1 = y0.astype(BF16)
    x2, act1, slope1 = expert_forward(
        x1,
        captions,
        lens,
        row(1, 3),
        row(1, 4),
        inputs_weights[1],
        row(1, 5),
        outputs_weights[1],
        row(1, 6),
        PATCH_PLACE,
    )
    x3, qkv2, mixed2 = attend_forward(
        x2, lens, row(2, 0), row(2, 1), attend_weights[2], row(2, 2), BF16
    )
    layer_output, act3, slope3 = expert_forward(
        x3,
        lens.reshape(1, -1).astype(F32),
        lens,
        row(3, 3),
        row(3, 4),
        inputs_weights[3],
        row(3, 5),
        outputs_weights[3],
        row(3, 6),
        WHOLE_PLACE,
    )

    grad3, inputs3, outputs3, *small3 = expert_backward(
        x3,
        lens,
        row(3, 3),
        row(3, 4),
        inputs_weights[3],
        outputs_weights[3],
        act3,
        slope3,
        last_grad,
        BF16,
        WHOLE_PLACE,
    )

    def scattered(matrix):
        return lax.psum_scatter(matrix, EVERYWHERE, scatter_dimension=0, tiled=True)

    inputs3, outputs3 = scattered(inputs3), scattered(outputs3)
    grad2, weights2, *small2 = attend_backward(
        x2, lens, row(2, 0), row(2, 1), attend_weights[2], qkv2, mixed2, grad3, BF16
    )
    weights2 = scattered(weights2)
    grad1, inputs1, outputs1, *small1 = expert_backward(
        x1,
        lens,
        row(1, 3),
        row(1, 4),
        inputs_weights[1],
        outputs_weights[1],
        act1,
        slope1,
        grad2,
        BF16,
        PATCH_PLACE,
    )
    inputs1, outputs1 = scattered(inputs1), scattered(outputs1)
    grad_y0, inputs0, outputs0, *small0 = expert_backward(
        y0,
        lens,
        row(0, 3),
        row(0, 4),
        inputs_weights[0],
        outputs_weights[0],
        act0,
        slope0,
        grad1,
        F32,
        CAPTION_PLACE,
    )
    inputs0, outputs0 = scattered(inputs0), scattered(outputs0)
    tokens_grad, weights0, *small_first = attend_backward(
        x0, lens, row(0, 0), row(0, 1), attend_weights[0], qkv0, mixed0, grad_y0, BF16
    )
    weights0 = scattered(weights0)

    as_float = counts.astype(F32)
    one = jnp.ones((), F32)
    attend_scales = jnp.stack([as_float[2], one, as_float[2], one])
    expert_scales = jnp.stack([as_float[1], as_float[0], one, as_float[2]])

    def at_home(pieces, scales):
        blank = jnp.zeros_like(next(piece for piece in pieces if piece is not None))
        stacked = jnp.stack([blank if piece is None else piece for piece in pieces]).astype(F32)
        stacked = (stacked / scales.reshape(-1, 1, 1)).astype(BF16)
        moved = lax.all_to_all(stacked, "section", 0, 0, tiled=True)
        moved = moved.reshape(-1, moved.shape[-1])
        return lax.all_gather(moved, "dp", axis=0, tiled=True).astype(F32)

    attend_whole = at_home([weights0, None, weights2, None], attend_scales)
    inputs_whole = at_home([inputs0, inputs1, None, inputs3], expert_scales)
    outputs_whole = at_home([outputs0, outputs1, None, outputs3], expert_scales)

    small = [jnp.concatenate(parts, axis=1) for parts in (small_first, small2)]
    small += [jnp.concatenate(parts, axis=1) for parts in (small0, small1, small3)]
    small = lax.psum(jnp.concatenate(small, axis=1), EVERYWHERE)[0]
    attend_size, expert_size = 5 * width, 3 * width + hidden
    cuts = [attend_size, 2 * attend_size]
    cuts += [cuts[1] + expert_size, cuts[1] + 2 * expert_size]
    small = jnp.split(small, cuts)
    none_attend, none_expert = jnp.zeros_like(small[0]), jnp.zeros_like(small[2])
    attend_small = jnp.stack([small[0], none_attend, small[1], none_attend])
    expert_small = jnp.stack([small[2], small[3], none_expert, small[4]])
    attend_small = attend_small / attend_scales.reshape(-1, 1)
    expert_small = expert_small / expert_scales.reshape(-1, 1)
    attend_small = lax.dynamic_index_in_dim(attend_small, section, 0)
    expert_small = lax.dynamic_index_in_dim(expert_small, section, 0)
    return (
        layer_output[:, :positions],
        tokens_grad[:, :positions],
        attend_small[:, :width],
        attend_small[:, width : 2 * width],
        attend_whole[None, :, : 3 * width],
        attend_small[:, 2 * width :],
        attend_whole[None, :, 3 * width :],
        expert_small[:, :width],
        expert_small[:, width : 2 * width],
        inputs_whole[None],
        expert_small[:, 2 * width : 2 * width + hidden],
        outputs_whole[None],
        expert_small[:, 2 * width + hidden :],
        counts,
    )


def solution(mesh):
    items = P(("section", "dp"), None, None)
    flat = P("section", None)
    matrix = P("section", None, None)
    placed = (
        items,
        P(("section", "dp")),
        flat,
        flat,
        matrix,
        flat,
        matrix,
        flat,
        flat,
        matrix,
        flat,
        matrix,
        flat,
        items,
    )
    return jax.shard_map(
        per_device,
        mesh=mesh,
        in_specs=placed,
        out_specs=(
            items,
            items,
            flat,
            flat,
            matrix,
            flat,
            matrix,
            flat,
            flat,
            matrix,
            flat,
            matrix,
            flat,
            P(),
        ),
        check_vma=False,
    )
```

```python
from functools import partial

import jax
import jax.numpy as jnp
from jax import lax
from jax.experimental import pallas as pl
from jax.experimental.pallas import tpu as pltpu
from jax.sharding import Mesh
from jax.sharding import PartitionSpec as P

HEADS = 12
HEAD_DIM = 64
PATCHES = 197
ROWS = 256
CAP_FIRST, CAP_ROWS = 192, 48
PATCH_ROWS = 208
PAIR = 2 * HEAD_DIM
SECTIONS = 4
PIECE_ROWS = 48
VMEM_BYTES = 58 * 1024 * 1024
F32 = jnp.float32
BF16 = jnp.bfloat16

PLAN = (
    ({0: "a0", 1: "e0", 2: "c0", 3: "f0"}, {0: "a1", 1: "e2", 2: "c0", 3: "f0"}),
    ({0: "a1", 1: "e1", 2: "a1", 3: "e2"}, {0: "a0", 1: "a0", 2: "c1", 3: "f1"}),
    ({0: "g3", 1: "e2", 2: "c1", 3: "f1"}, {0: "e0", 1: "e3", 2: "f0", 3: "f2"}),
    ({0: "g1", 1: "e3", 2: "e0", 3: "e3"}, {0: "e1", 1: "e1", 2: "f1", 3: "f3"}),
    ({0: "c1", 1: "f2", 3: "f2"}, {0: "g2", 1: "g3", 3: "c0"}),
    ({1: "f3", 3: "f3"}, {}),
)
HOMES = {"a": 0, "c": 2, "e": 1, "f": 3, "g": 0}
ATTEND_BLOCKS = ((0, 1), (2, 3))
EXPERT_BLOCKS = ((0, 1), (4, 5), (2, 3), (6, 7))


def dot_plain(left, right):
    return jnp.dot(left, right, preferred_element_type=F32)


def dot_last(left, right):
    return lax.dot_general(left, right, (((1,), (1,)), ((), ())), preferred_element_type=F32)


def dot_first(left, right):
    return lax.dot_general(left, right, (((0,), (0,)), ((), ())), preferred_element_type=F32)


def column_sum(matrix):
    return jnp.sum(matrix.astype(F32), axis=0, keepdims=True)


def norm_parts(rows):
    centre = rows - jnp.mean(rows, axis=-1, keepdims=True)
    scale = lax.rsqrt(jnp.mean(centre * centre, axis=-1, keepdims=True) + 1e-06)
    return centre * scale, scale


def norm_back(normed_grad, unit, scale, gain):
    unit_grad = normed_grad * gain
    along = jnp.mean(unit_grad * unit, axis=-1, keepdims=True)
    return scale * (unit_grad - jnp.mean(unit_grad, axis=-1, keepdims=True) - unit * along)


def true_positions(length, first, count, axis, kind):
    shape = (count, 1) if axis == 0 else (1, count)
    position = first + lax.broadcasted_iota(jnp.int32, shape, axis)
    patch = position < PATCHES
    if kind == "patch":
        return patch
    caption = (position >= PATCHES) & (position - PATCHES < length)
    return caption if kind == "caption" else patch | caption


def head_masks():
    lane = lax.broadcasted_iota(jnp.int32, (1, PAIR), 1)
    even = (lane < HEAD_DIM).astype(F32).astype(BF16)
    odd = (lane >= HEAD_DIM).astype(F32).astype(BF16)
    return lane < HEAD_DIM, even, odd


def split_pair(pair, even, odd):
    return jnp.concatenate([pair * even, pair * odd], axis=0)


def start_weights(section, core, refs, plan, blocks, sems):
    half = blocks.shape[1] // 2
    for at in range(SECTIONS):

        @pl.when(section == at)
        def _(at=at):
            for block, source in plan[at]:
                if source[0] == "own":
                    _, which, row, column = source
                    width = blocks.shape[2]
                    for part in range(2):
                        pltpu.make_async_copy(
                            refs[which].at[
                                pl.ds(row + part * half, half), pl.ds(column, width)
                            ],
                            blocks.at[block, pl.ds(part * half, half)],
                            sems.at[block],
                        ).start()
                else:
                    _, mine, theirs, index = source
                    pltpu.make_async_copy(
                        refs[mine].at[index],
                        blocks.at[block, pl.ds(pl.multiple_of(core * half, half), half)],
                        sems.at[block],
                    ).start()
                    pltpu.make_async_copy(
                        refs[theirs].at[index],
                        blocks.at[block, pl.ds(pl.multiple_of((1 - core) * half, half), half)],
                        sems.at[block],
                    ).start()


def wait_block(blocks, block, sems):
    pltpu.make_async_copy(blocks.at[block], blocks.at[block], sems.at[block]).wait()


def store_turned(target, turned, columns, section, core):
    half = target.shape[0] // 2
    for piece in range(16):
        path, owner = (piece >> 2) & 1, piece & 3
        away = owner ^ section
        place = ((away & 1) << 1) | (away >> 1) if path == 0 else away
        row = ((piece >> 3) ^ core) * half + path * (half // 2) + place * PIECE_ROWS
        target[pl.ds(pl.multiple_of(row, 16), PIECE_ROWS), columns] = turned[
            piece * PIECE_ROWS : (piece + 1) * PIECE_ROWS
        ]


def attend_forward_kernel(plan, weight_count, merge, info, *refs):
    weights, refs = refs[:weight_count], refs[weight_count:]
    if merge:
        x_ref, before_ref, *parts, outer_ref, gain_ref, shift_ref, bias_ref = refs[:10]
        y_ref, qkv_ref, mixed_ref, joined_ref, blocks, sems, joined = refs[10:]
    else:
        x_ref, gain_ref, shift_ref, bias_ref, next_gain_ref, next_shift_ref = refs[:6]
        y_ref, qkv_ref, mixed_ref, caption_ref, blocks, sems = refs[6:]
    item = pl.program_id(0)
    items = pl.num_programs(0)
    length = info[item]
    width = x_ref.shape[-1]

    @pl.when(item == 0)
    def _():
        start_weights(info[items], info[items + 1], weights, plan, blocks, sems)

    cap = slice(CAP_FIRST, CAP_FIRST + CAP_ROWS)
    if merge:
        joined[...] = x_ref[0].astype(F32)
        branch = outer_ref[...]
        for part in parts:
            branch = branch + part[0].astype(F32)
        is_true = true_positions(length, CAP_FIRST, CAP_ROWS, 0, "caption")
        captions = before_ref[0, cap] + jnp.where(is_true, branch, 0.0)
        position = CAP_FIRST + lax.broadcasted_iota(jnp.int32, (CAP_ROWS, 1), 0)
        captions = captions.astype(BF16).astype(F32)
        joined[cap] = jnp.where(position < PATCHES, joined[cap], captions)
        x = joined[...]
        joined_ref[0] = x.astype(BF16)
    else:
        x = x_ref[0].astype(F32)
    unit, _ = norm_parts(x)
    normed = (unit * gain_ref[...] + shift_ref[...]).astype(BF16)

    @pl.when(item == 0)
    def _():
        for block in range(4):
            wait_block(blocks, block, sems)

    queries = dot_plain(normed, blocks[0]) + bias_ref[:, :width]
    qkv_ref[0, :, :width] = (queries * HEAD_DIM ** (-0.5)).astype(BF16)
    qkv_ref[0, :, width : 2 * width] = dot_plain(normed, blocks[1]).astype(BF16)
    values = dot_plain(normed, blocks[2]) + bias_ref[:, width : 2 * width]
    qkv_ref[0, :, 2 * width :] = values.astype(BF16)
    key_true = true_positions(length, 0, ROWS, 1, "all")
    low_half, even, odd = head_masks()
    ones = jnp.ones((ROWS, PAIR), BF16)
    for pair in range(HEADS // 2):
        at = pair * PAIR
        q2 = qkv_ref[0, :, at : at + PAIR]
        k2 = qkv_ref[0, :, width + at : width + at + PAIR]
        v2 = qkv_ref[0, :, 2 * width + at : 2 * width + at + PAIR]
        scores = jnp.where(key_true, dot_last(split_pair(q2, even, odd), k2), -1e9)
        largest = jnp.max(scores, axis=-1, keepdims=True)
        weight = jnp.exp(scores - largest).astype(BF16)
        summed = dot_plain(weight, jnp.concatenate([v2, ones], axis=1))
        top = jnp.where(low_half, summed[:ROWS, :PAIR], summed[ROWS:, :PAIR])
        below = jnp.where(low_half, summed[:ROWS, PAIR:], summed[ROWS:, PAIR:])
        mixed_ref[0, :, at : at + PAIR] = (top / below).astype(BF16)
    branch = dot_plain(mixed_ref[0], blocks[3]) + bias_ref[:, 2 * width :]
    row_true = true_positions(length, 0, ROWS, 0, "all")
    y = x + jnp.where(row_true, branch, 0.0)
    y_ref[0] = y.astype(y_ref.dtype)
    if not merge:
        unit, _ = norm_parts(y[cap])
        caption_ref[0] = (unit * next_gain_ref[...] + next_shift_ref[...]).astype(BF16)


def attend_backward_kernel(plan, weight_count, first, info, *refs):
    weights, refs = refs[:weight_count], refs[weight_count:]
    x_ref, gain_ref, shift_ref, qkv_ref, mixed_ref, grad_ref = refs[:6]
    if first:
        after_ref, next_gain_ref, *parts = refs[6:12]
        refs = refs[12:]
    else:
        refs = refs[6:]
    out_ref, keep_ref, send_ref, gain_grad_ref, shift_grad_ref, bias_grad_ref = refs[:6]
    if first:
        next_gain_grad_ref, next_shift_grad_ref, joined = refs[6], refs[7], refs[-1]
    else:
        caption_ref = refs[6]
    blocks, sems, normed_turned, mixed_turned, branch_all, projected, mixed_grad = refs[
        8 if first else 7 :
    ][:7]
    item = pl.program_id(0)
    items = pl.num_programs(0)
    length = info[item]
    section, core = info[items], info[items + 1]
    width = x_ref.shape[-1]
    here = pl.ds(pl.multiple_of(item * ROWS, ROWS), ROWS)
    cap = slice(CAP_FIRST, CAP_FIRST + CAP_ROWS)

    @pl.when(item == 0)
    def _():
        start_weights(section, core, weights, plan, blocks, sems)

    def add_to(ref, part):
        @pl.when(item == 0)
        def _():
            ref[...] = part

        @pl.when(item > 0)
        def _():
            ref[...] += part

    x = x_ref[0].astype(F32)
    unit, scale = norm_parts(x)
    normed = (unit * gain_ref[...] + shift_ref[...]).astype(BF16)
    incoming = grad_ref[0].astype(F32)
    if first:
        after_unit, after_scale = norm_parts(after_ref[0, cap])
        caption_grad = parts[0][0].astype(F32)
        for part in parts[1:]:
            caption_grad = caption_grad + part[0].astype(F32)
        joined[...] = incoming
        joined[cap] += norm_back(caption_grad, after_unit, after_scale, next_gain_ref[...])
        incoming = joined[...]
        add_to(next_gain_grad_ref, jnp.sum(caption_grad * after_unit, axis=0, keepdims=True))
        add_to(next_shift_grad_ref, jnp.sum(caption_grad, axis=0, keepdims=True))
    row_true = true_positions(length, 0, ROWS, 0, "all")
    branch = jnp.where(row_true, incoming, 0.0).astype(BF16)
    branch_all[here, :] = branch
    store_turned(normed_turned, normed.T, here, section, core)
    store_turned(mixed_turned, mixed_ref[0].T, here, section, core)

    @pl.when(item == 0)
    def _():
        for block in range(4):
            wait_block(blocks, block, sems)

    mixed_grad[...] = dot_last(branch, blocks[3]).astype(BF16)
    key_true = true_positions(length, 0, ROWS, 0, "all")
    _, even, odd = head_masks()
    for pair in range(HEADS // 2):
        at = pair * PAIR
        q2 = split_pair(qkv_ref[0, :, at : at + PAIR], even, odd)
        k2 = qkv_ref[0, :, width + at : width + at + PAIR]
        v2 = qkv_ref[0, :, 2 * width + at : 2 * width + at + PAIR]
        g2 = split_pair(mixed_grad[:, at : at + PAIR], even, odd)
        scores = jnp.where(key_true, dot_last(k2, q2), -1e9)
        weight = jnp.exp(scores - jnp.max(scores, axis=0, keepdims=True))
        weight = weight / jnp.sum(weight, axis=0, keepdims=True)
        weight_grad = dot_last(v2, g2)
        along = jnp.sum(weight * weight_grad, axis=0, keepdims=True)
        score_grad = (weight * (weight_grad - along)).astype(BF16)
        values_grad = dot_plain(weight.astype(BF16), g2).astype(BF16)
        keys_grad = dot_plain(score_grad, q2).astype(BF16)
        k2_split = split_pair(k2, even, odd)
        stacked = jnp.concatenate([score_grad[:, :ROWS], score_grad[:, ROWS:]], axis=0)
        queries_grad = dot_first(stacked, k2_split).astype(BF16)
        queries_grad = (queries_grad.astype(F32) * HEAD_DIM ** (-0.5)).astype(BF16)
        projected[here, at : at + PAIR] = queries_grad
        projected[here, width + at : width + at + PAIR] = keys_grad
        projected[here, 2 * width + at : 2 * width + at + PAIR] = values_grad
    normed_grad = dot_last(projected[here, :width], blocks[0])
    normed_grad += dot_last(projected[here, width : 2 * width], blocks[1])
    normed_grad += dot_last(projected[here, 2 * width :], blocks[2])
    out = (incoming + norm_back(normed_grad, unit, scale, gain_ref[...])).astype(BF16)
    out_ref[0] = out
    if not first:
        is_true = true_positions(length, CAP_FIRST, CAP_ROWS, 0, "caption")
        caption_ref[0] = jnp.where(is_true, out[cap].astype(F32), 0.0).astype(BF16)
    add_to(gain_grad_ref, jnp.sum(normed_grad * unit, axis=0, keepdims=True))
    add_to(shift_grad_ref, jnp.sum(normed_grad, axis=0, keepdims=True))

    @pl.when(item == items - 1)
    def _():
        half = width // 2
        for block in range(4):
            columns = slice(block * width, (block + 1) * width)
            left = normed_turned if block < 3 else mixed_turned
            right = projected[:, columns] if block < 3 else branch_all[...]
            keep_ref[0, :, columns] = dot_plain(left[:half], right).astype(BF16)
            send_ref[0, :, columns] = dot_plain(left[half:], right).astype(BF16)
        bias_grad_ref[:, :width] = column_sum(projected[:, :width])
        bias_grad_ref[:, width : 2 * width] = column_sum(projected[:, 2 * width :])
        bias_grad_ref[:, 2 * width :] = column_sum(branch_all[...])


ANYWHERE = pl.BlockSpec(memory_space=pl.ANY)


def whole_block(shape):
    return pl.BlockSpec(shape, lambda step, info: (0,) * len(shape))


def item_block(shape):
    return pl.BlockSpec((1,) + shape[1:], lambda step, info: (step,) + (0,) * (len(shape) - 1))


def blocks_scratch(count, width):
    return [pltpu.VMEM((count, width, width), BF16), pltpu.SemaphoreType.DMA((count,))]


def attend_forward(x, info, weights, gain, shift, bias, merge=None, following=None):
    arrays, plan = weights
    items, _, width = x.shape
    flops = 2 * items * ROWS * width * (4 * width + 4 * ROWS)
    row = whole_block((1, width))
    bias_row = whole_block((1, 3 * width))
    caption_shape = (items, CAP_ROWS, width)
    if merge is not None:
        before, parts, outer = merge
        operands = (x, before, *parts, outer, gain, shift, bias)
        specs = [item_block(x.shape), item_block(x.shape)]
        specs += [item_block(caption_shape)] * 4 + [row, row, row, bias_row]
        last_shape, kind, scratch = x.shape, BF16, [pltpu.VMEM((ROWS, width), F32)]
    else:
        operands = (x, gain, shift, bias, *following)
        specs = [item_block(x.shape), row, row, bias_row, row, row]
        last_shape, kind, scratch = caption_shape, F32, []
    return pl.pallas_call(
        partial(attend_forward_kernel, plan, len(arrays), merge is not None),
        grid_spec=pltpu.PrefetchScalarGridSpec(
            num_scalar_prefetch=1,
            grid=(items,),
            in_specs=[ANYWHERE] * len(arrays) + specs,
            out_specs=[
                item_block(x.shape),
                item_block((items, ROWS, 3 * width)),
                item_block((items, ROWS, width)),
                item_block(last_shape),
            ],
            scratch_shapes=blocks_scratch(4, width) + scratch,
        ),
        out_shape=[
            jax.ShapeDtypeStruct(x.shape, kind),
            jax.ShapeDtypeStruct((items, ROWS, 3 * width), BF16),
            jax.ShapeDtypeStruct((items, ROWS, width), BF16),
            jax.ShapeDtypeStruct(last_shape, BF16),
        ],
        compiler_params=pltpu.CompilerParams(vmem_limit_bytes=VMEM_BYTES),
        cost_estimate=pl.CostEstimate(
            flops=flops, bytes_accessed=16_000_000, transcendentals=items * HEADS * ROWS * ROWS
        ),
        name="attend_forward",
    )(info, *arrays, *operands)


def attend_backward(x, info, weights, gain, shift, qkv, mixed, incoming, first=None):
    arrays, plan = weights
    items, _, width = x.shape
    half = width // 2
    flops = 4 * items * ROWS * width * (4 * width + 5 * ROWS)
    row = whole_block((1, width))
    caption_shape = (items, CAP_ROWS, width)
    operands = (x, gain, shift, qkv, mixed, incoming)
    specs = [item_block(x.shape), row, row, item_block(qkv.shape), item_block(mixed.shape)]
    specs += [item_block(incoming.shape)]
    outs = [
        (item_block(x.shape), x.shape, BF16),
        (whole_block((1, half, 4 * width)), (1, half, 4 * width), BF16),
        (whole_block((1, half, 4 * width)), (1, half, 4 * width), BF16),
        (row, (1, width), F32),
        (row, (1, width), F32),
        (whole_block((1, 3 * width)), (1, 3 * width), F32),
    ]
    scratch = []
    if first is not None:
        after, next_gain, parts = first
        operands += (after, next_gain, *parts)
        specs += [item_block(after.shape), row] + [item_block(caption_shape)] * 4
        outs += [(row, (1, width), F32)] * 2
        scratch = [pltpu.VMEM((ROWS, width), F32)]
    else:
        outs += [(item_block(caption_shape), caption_shape, BF16)]
    return pl.pallas_call(
        partial(attend_backward_kernel, plan, len(arrays), first is not None),
        grid_spec=pltpu.PrefetchScalarGridSpec(
            num_scalar_prefetch=1,
            grid=(items,),
            in_specs=[ANYWHERE] * len(arrays) + specs,
            out_specs=[spec for spec, _, _ in outs],
            scratch_shapes=blocks_scratch(4, width)
            + [
                pltpu.VMEM((width, items * ROWS), BF16),
                pltpu.VMEM((width, items * ROWS), BF16),
                pltpu.VMEM((items * ROWS, width), BF16),
                pltpu.VMEM((items * ROWS, 3 * width), BF16),
                pltpu.VMEM((ROWS, width), BF16),
            ]
            + scratch,
        ),
        out_shape=[jax.ShapeDtypeStruct(shape, kind) for _, shape, kind in outs],
        compiler_params=pltpu.CompilerParams(vmem_limit_bytes=VMEM_BYTES),
        cost_estimate=pl.CostEstimate(
            flops=flops, bytes_accessed=24_000_000, transcendentals=items * HEADS * ROWS * ROWS
        ),
        name="attend_backward",
    )(info, *arrays, *operands)


def normal_parts(u):
    size = jnp.abs(u) * 0.7071067811865476
    t = 1.0 / (1.0 + 0.3275911 * size)
    bell = jnp.exp(-size * size)
    poly = t * (
        0.254829592
        + t * (-0.284496736 + t * (1.421413741 + t * (-1.453152027 + t * 1.061405429)))
    )
    tail = 0.5 * poly * bell
    return jnp.where(u < 0, tail, 1.0 - tail), 0.3989422804014327 * bell


def inner_forward(normed, matrix, bias):
    inner = dot_plain(normed, matrix) + bias
    cumulative, density = normal_parts(inner)
    return (inner * cumulative).astype(BF16), (cumulative + inner * density).astype(BF16)


def expert_forward_kernel(plan, weight_count, count, kind, info, *refs):
    weights, refs = refs[:weight_count], refs[weight_count:]
    x_ref, gain_ref, shift_ref, inner_ref, outer_ref = refs[:5]
    y_ref, act_ref, slope_ref, blocks, sems, normed, total = refs[5:]
    step = pl.program_id(0)
    items, _, width = x_ref.shape

    @pl.when(step == 0)
    def _():
        start_weights(info[items], info[items + 1], weights, plan, blocks, sems)
        for item in range(items):
            x = x_ref[item, :count].astype(BF16).astype(F32)
            unit, _ = norm_parts(x)
            normed[item * count : (item + 1) * count] = (
                unit * gain_ref[...] + shift_ref[...]
            ).astype(BF16)

    wait_block(blocks, step, sems)
    wait_block(blocks, step + 4, sems)
    part = None
    for at in range(0, width, 256):
        columns = slice(at, at + 256)
        act, slope = inner_forward(normed[...], blocks[step, :, columns], inner_ref[:, columns])
        act_ref[:, columns] = act
        slope_ref[:, columns] = slope
        term = dot_plain(act, blocks[step + 4, columns])
        part = term if part is None else part + term

    @pl.when(step == 0)
    def _():
        total[...] = part

    @pl.when(step > 0)
    def _():
        total[...] += part

    @pl.when(step == pl.num_programs(0) - 1)
    def _():
        for item in range(items):
            row_true = true_positions(info[item], 0, count, 0, kind)
            branch = total[item * count : (item + 1) * count] + outer_ref[...]
            x = x_ref[item, :count].astype(BF16).astype(F32)
            y_ref[item, :count] = (x + jnp.where(row_true, branch, 0.0)).astype(BF16)
            if count < ROWS:
                y_ref[item, count:] = jnp.zeros((ROWS - count, width), BF16)


def expert_backward_kernel(plan, weight_count, count, kind, info, *refs):
    weights, refs = refs[:weight_count], refs[weight_count:]
    x_ref, gain_ref, shift_ref, act_ref, slope_ref, grad_ref = refs[:6]
    out_ref, keep_ref, send_ref, gain_grad_ref, shift_grad_ref, inner_grad_ref, outer_grad_ref = (
        refs[6:13]
    )
    blocks, sems, normed_turned, branch_turned, branch, total = refs[13:]
    step = pl.program_id(0)
    items, _, width = x_ref.shape
    half = width // 2
    section, core = info[items], info[items + 1]

    @pl.when(step == 0)
    def _():
        start_weights(section, core, weights, plan, blocks, sems)
        outer = None
        for item in range(items):
            here = slice(item * count, (item + 1) * count)
            unit, _ = norm_parts(x_ref[item, :count].astype(BF16).astype(F32))
            normed = (unit * gain_ref[...] + shift_ref[...]).astype(BF16)
            row_true = true_positions(info[item], 0, count, 0, kind)
            incoming = grad_ref[item, :count].astype(F32)
            masked = jnp.where(row_true, incoming, 0.0).astype(BF16)
            branch[here] = masked
            store_turned(normed_turned, normed.T, here, section, core)
            store_turned(branch_turned, masked.T, here, section, core)
            term = column_sum(masked)
            outer = term if outer is None else outer + term
        outer_grad_ref[...] = outer

    wait_block(blocks, step, sems)
    wait_block(blocks, step + 4, sems)
    part = None
    for at in range(0, width, 256):
        columns = slice(at, at + 256)
        act_grad = dot_last(branch[...], blocks[step + 4, columns])
        inner = (slope_ref[:, columns].astype(F32) * act_grad).astype(BF16)
        inner_grad_ref[:, columns] = column_sum(inner)
        keep_ref[0, :, columns] = dot_plain(normed_turned[:half], inner).astype(BF16)
        send_ref[0, :, columns] = dot_plain(normed_turned[half:], inner).astype(BF16)
        act = act_ref[:, columns]
        keep_ref[1, :, columns] = dot_plain(branch_turned[:half], act).astype(BF16)
        send_ref[1, :, columns] = dot_plain(branch_turned[half:], act).astype(BF16)
        term = dot_last(inner, blocks[step, :, columns])
        part = term if part is None else part + term

    @pl.when(step == 0)
    def _():
        total[...] = part

    @pl.when(step > 0)
    def _():
        total[...] += part

    @pl.when(step == pl.num_programs(0) - 1)
    def _():
        gain_sum, shift_sum = None, None
        for item in range(items):
            unit, scale = norm_parts(x_ref[item, :count].astype(BF16).astype(F32))
            normed_grad = total[item * count : (item + 1) * count]
            gain_part = jnp.sum(normed_grad * unit, axis=0, keepdims=True)
            shift_part = jnp.sum(normed_grad, axis=0, keepdims=True)
            gain_sum = gain_part if gain_sum is None else gain_sum + gain_part
            shift_sum = shift_part if shift_sum is None else shift_sum + shift_part
            incoming = grad_ref[item, :count].astype(F32)
            hidden = incoming + norm_back(normed_grad, unit, scale, gain_ref[...])
            out_ref[item, :count] = hidden.astype(BF16)
            if count < ROWS:
                out_ref[item, count:] = grad_ref[item, count:]
        gain_grad_ref[...] = gain_sum
        shift_grad_ref[...] = shift_sum


def shared_forward_kernel(plan, weight_count, info, *refs):
    weights, refs = refs[:weight_count], refs[weight_count:]
    *rows_refs, inner_ref = refs[:5]
    act_ref, slope_ref, part_ref, blocks, sems, normed = refs[5:]
    count = rows_refs[0].shape[0]
    width = inner_ref.shape[1]
    at = info.shape[0] - 2
    start_weights(info[at], info[at + 1], weights, plan, blocks, sems)
    for index, ref in enumerate(rows_refs):
        normed[index * count : (index + 1) * count] = ref[...]
    wait_block(blocks, 0, sems)
    wait_block(blocks, 1, sems)
    part = None
    for at in range(0, width, 256):
        columns = slice(at, at + 256)
        act, slope = inner_forward(normed[...], blocks[0, :, columns], inner_ref[:, columns])
        act_ref[:, columns] = act
        slope_ref[:, columns] = slope
        term = dot_plain(act, blocks[1, columns])
        part = term if part is None else part + term
    for index in range(SECTIONS):
        part_ref[index] = part[index * count : (index + 1) * count].astype(BF16)


def shared_backward_kernel(plan, weight_count, info, *refs):
    weights, refs = refs[:weight_count], refs[weight_count:]
    rows_refs, grad_refs = refs[:4], refs[4:8]
    act_ref, slope_ref, part_ref, keep_ref, send_ref, inner_grad_ref, outer_grad_ref = refs[8:15]
    blocks, sems, normed, branch, matrix = refs[15:]
    count, width = rows_refs[0].shape
    half = width // 2
    at = info.shape[0] - 2
    core = info[at + 1]
    start_weights(info[at], core, weights, plan, blocks, sems)
    for index in range(SECTIONS):
        here = slice(index * count, (index + 1) * count)
        normed[here] = rows_refs[index][...]
        branch[here] = grad_refs[index][...]
    outer_grad_ref[...] = column_sum(grad_refs[0][...])
    wait_block(blocks, 0, sems)
    wait_block(blocks, 1, sems)
    part = None
    for at in range(0, width, 256):
        columns = slice(at, at + 256)
        act_grad = dot_last(branch[...], blocks[1, columns])
        inner = (slope_ref[:, columns].astype(F32) * act_grad).astype(BF16)
        inner_grad_ref[:, columns] = column_sum(inner)
        matrix[0, :, columns] = dot_first(normed[...], inner).astype(BF16)
        matrix[1, :, columns] = dot_first(branch[...], act_ref[:, columns]).astype(BF16)
        term = dot_last(inner, blocks[0, :, columns])
        part = term if part is None else part + term
    for index in range(SECTIONS):
        part_ref[index] = part[index * count : (index + 1) * count].astype(BF16)
    quarter = half // 4
    for which in range(2):
        for group in range(4):
            columns = slice(group * width, (group + 1) * width)
            mine = pl.multiple_of(core * half, 16) + group * quarter
            other = pl.multiple_of((1 - core) * half, 16) + group * quarter
            keep_ref[which, :, columns] = matrix[which, pl.ds(pl.multiple_of(mine, 16), quarter)]
            send_ref[which, :, columns] = matrix[which, pl.ds(pl.multiple_of(other, 16), quarter)]


def chunk_columns(rows, width):
    return pl.BlockSpec((rows, width), lambda step, info: (0, step))


def expert_forward(x, info, weights, gain, shift, inner, outer, count, kind):
    arrays, plan = weights
    items, _, width = x.shape
    hidden = inner.shape[1]
    row = whole_block((1, width))
    return pl.pallas_call(
        partial(expert_forward_kernel, plan, len(arrays), count, kind),
        grid_spec=pltpu.PrefetchScalarGridSpec(
            num_scalar_prefetch=1,
            grid=(hidden // width,),
            in_specs=[ANYWHERE] * len(arrays)
            + [whole_block(x.shape), row, row, chunk_columns(1, width), row],
            out_specs=[
                whole_block((items, ROWS, width)),
                chunk_columns(items * count, width),
                chunk_columns(items * count, width),
            ],
            scratch_shapes=blocks_scratch(8, width)
            + [
                pltpu.VMEM((items * count, width), BF16),
                pltpu.VMEM((items * count, width), F32),
            ],
        ),
        out_shape=[
            jax.ShapeDtypeStruct((items, ROWS, width), BF16),
            jax.ShapeDtypeStruct((items * count, hidden), BF16),
            jax.ShapeDtypeStruct((items * count, hidden), BF16),
        ],
        compiler_params=pltpu.CompilerParams(vmem_limit_bytes=VMEM_BYTES),
        cost_estimate=pl.CostEstimate(
            flops=4 * items * count * width * hidden,
            bytes_accessed=22_000_000,
            transcendentals=2 * items * count * hidden,
        ),
        name="expert_forward_" + kind,
    )(info, *arrays, x, gain, shift, inner, outer)


def expert_backward(x, info, weights, gain, shift, act, slope, incoming, count, kind):
    arrays, plan = weights
    items, _, width = x.shape
    half = width // 2
    hidden = act.shape[1]
    row = whole_block((1, width))
    travel = pl.BlockSpec((2, half, width), lambda step, info: (0, 0, step))
    return pl.pallas_call(
        partial(expert_backward_kernel, plan, len(arrays), count, kind),
        grid_spec=pltpu.PrefetchScalarGridSpec(
            num_scalar_prefetch=1,
            grid=(hidden // width,),
            in_specs=[ANYWHERE] * len(arrays)
            + [
                whole_block(x.shape),
                row,
                row,
                chunk_columns(items * count, width),
                chunk_columns(items * count, width),
                whole_block(incoming.shape),
            ],
            out_specs=[
                whole_block(incoming.shape),
                travel,
                travel,
                row,
                row,
                chunk_columns(1, width),
                row,
            ],
            scratch_shapes=blocks_scratch(8, width)
            + [
                pltpu.VMEM((width, items * count), BF16),
                pltpu.VMEM((width, items * count), BF16),
                pltpu.VMEM((items * count, width), BF16),
                pltpu.VMEM((items * count, width), F32),
            ],
        ),
        out_shape=[
            jax.ShapeDtypeStruct(incoming.shape, BF16),
            jax.ShapeDtypeStruct((2, half, hidden), BF16),
            jax.ShapeDtypeStruct((2, half, hidden), BF16),
            jax.ShapeDtypeStruct((1, width), F32),
            jax.ShapeDtypeStruct((1, width), F32),
            jax.ShapeDtypeStruct((1, hidden), F32),
            jax.ShapeDtypeStruct((1, width), F32),
        ],
        compiler_params=pltpu.CompilerParams(vmem_limit_bytes=VMEM_BYTES),
        cost_estimate=pl.CostEstimate(
            flops=8 * items * count * width * hidden,
            bytes_accessed=40_000_000,
            transcendentals=0,
        ),
        name="expert_backward_" + kind,
    )(info, *arrays, x, gain, shift, act, slope, incoming)


IN_VMEM = pl.BlockSpec(memory_space=pltpu.VMEM)
IN_SMEM = pl.BlockSpec(memory_space=pltpu.SMEM)


def shared_forward(rows, info, weights, inner):
    arrays, plan = weights
    count, width = rows[0].shape
    total = SECTIONS * count
    return pl.pallas_call(
        partial(shared_forward_kernel, plan, len(arrays)),
        in_specs=[IN_SMEM] + [ANYWHERE] * len(arrays) + [IN_VMEM] * 5,
        out_specs=[IN_VMEM] * 3,
        scratch_shapes=blocks_scratch(2, width) + [pltpu.VMEM((total, width), BF16)],
        out_shape=[
            jax.ShapeDtypeStruct((total, width), BF16),
            jax.ShapeDtypeStruct((total, width), BF16),
            jax.ShapeDtypeStruct((SECTIONS, count, width), BF16),
        ],
        compiler_params=pltpu.CompilerParams(vmem_limit_bytes=VMEM_BYTES),
        cost_estimate=pl.CostEstimate(
            flops=4 * total * width * width,
            bytes_accessed=7_000_000,
            transcendentals=2 * total * width,
        ),
        name="shared_forward",
    )(info, *arrays, *rows, inner)


def shared_backward(rows, grads, info, weights, act, slope):
    arrays, plan = weights
    count, width = rows[0].shape
    total = SECTIONS * count
    travel = (2, width // 8, 4 * width)
    return pl.pallas_call(
        partial(shared_backward_kernel, plan, len(arrays)),
        in_specs=[IN_SMEM] + [ANYWHERE] * len(arrays) + [IN_VMEM] * 10,
        out_specs=[IN_VMEM] * 5,
        scratch_shapes=blocks_scratch(2, width)
        + [
            pltpu.VMEM((total, width), BF16),
            pltpu.VMEM((total, width), BF16),
            pltpu.VMEM((2, width, width), BF16),
        ],
        out_shape=[
            jax.ShapeDtypeStruct((SECTIONS, count, width), BF16),
            jax.ShapeDtypeStruct(travel, BF16),
            jax.ShapeDtypeStruct(travel, BF16),
            jax.ShapeDtypeStruct((1, width), F32),
            jax.ShapeDtypeStruct((1, width), F32),
        ],
        compiler_params=pltpu.CompilerParams(vmem_limit_bytes=VMEM_BYTES),
        cost_estimate=pl.CostEstimate(
            flops=8 * total * width * width, bytes_accessed=12_000_000, transcendentals=0
        ),
        name="shared_backward",
    )(info, *arrays, *rows, *grads, act, slope)


def finish_kernel(info, scale_ref, mine_ref, theirs_ref, *refs):
    step = pl.program_id(0)
    count = mine_ref.shape[1]
    placed = refs[-1]
    outs = refs[:-1]
    width = placed.shape[1]
    half = width // 2
    at = info.shape[0] - 2
    section, core = info[at], info[at + 1]
    scale = scale_ref[0, 0]
    columns = pl.ds(pl.multiple_of(step * width, width), width)

    def place(which):
        def by_rows():
            for side, ref in enumerate((mine_ref, theirs_ref)):
                for away in range(SECTIONS):
                    for path in range(2):
                        row = (core ^ side) * half + path * (half // 2)
                        row = row + (section ^ away) * PIECE_ROWS
                        placed[pl.ds(pl.multiple_of(row, 16), PIECE_ROWS), :] = ref[
                            away, which, path * PIECE_ROWS : (path + 1) * PIECE_ROWS, columns
                        ].astype(F32)

        def by_columns():
            for side, ref in enumerate((mine_ref, theirs_ref)):
                for group in range(4):
                    quarter = half // 4
                    row = (core ^ side) * half + group * quarter
                    placed[pl.ds(pl.multiple_of(row, 16), quarter), :] = ref[
                        step, which, :, group * width : (group + 1) * width
                    ].astype(F32)

        if count == 1:
            by_rows()
        else:
            pl.when(section != 0)(by_rows)
            pl.when(section == 0)(by_columns)

    place(0)
    if count == 1:

        @pl.when(step < 3)
        def _():
            outs[0][0] = placed[...] / scale

        @pl.when(step == 3)
        def _():
            outs[1][0] = placed[...] / scale

    else:
        outs[0][0] = placed[...] / scale
        place(1)
        outs[1][0] = (placed[...] / scale).T


def finish(info, scale, mine, theirs):
    count, hidden = mine.shape[1], mine.shape[3]
    width = hidden // 4
    if count == 1:
        shapes = [(1, width, 3 * width), (1, width, width)]
        maps = [lambda step, info: (0, 0, jnp.minimum(step, 2)), lambda step, info: (0, 0, 0)]
    else:
        shapes = [(1, width, hidden), (1, hidden, width)]
        maps = [lambda step, info: (0, 0, step), lambda step, info: (0, step, 0)]
    return pl.pallas_call(
        finish_kernel,
        grid_spec=pltpu.PrefetchScalarGridSpec(
            num_scalar_prefetch=1,
            grid=(4,),
            in_specs=[IN_SMEM, whole_block(mine.shape), whole_block(mine.shape)],
            out_specs=[pl.BlockSpec((1, width, width), at) for at in maps],
            scratch_shapes=[pltpu.VMEM((width, width), F32)],
        ),
        out_shape=[jax.ShapeDtypeStruct(shape, F32) for shape in shapes],
        compiler_params=pltpu.CompilerParams(vmem_limit_bytes=VMEM_BYTES),
        cost_estimate=pl.CostEstimate(
            flops=0, bytes_accessed=15_000_000 * count, transcendentals=0
        ),
        name="finish",
    )(info, scale, mine, theirs)


def over_section(value, bits, sources=range(SECTIONS)):
    return lax.ppermute(value, "section", [(at, at ^ bits) for at in sources])


def over_core(value):
    return lax.ppermute(value, "core", [(0, 1), (1, 0)])


def added(left, right):
    return (left.astype(F32) + right.astype(F32)).astype(BF16)


def by_section(section, values):
    result, last = None, None
    for at in sorted(values):
        if result is None:
            result = values[at]
        elif values[at] is not last:
            result = jnp.where(section >= at, values[at], result)
        last = values[at]
    return result


def per_device(
    tokens,
    caption_lengths,
    attend_gain,
    attend_shift,
    attend_inputs,
    attend_bias,
    attend_output,
    expert_gain,
    expert_shift,
    expert_inputs,
    expert_inner_bias,
    expert_outputs,
    expert_outer_bias,
    cotangent,
):
    section = lax.axis_index("section")
    core = lax.axis_index("core")
    items, positions, width = tokens.shape
    half = width // 2
    hidden = expert_inputs.shape[-1]
    own = (attend_inputs[0], attend_output[0], expert_inputs[0], expert_outputs[0])

    def cut(which, row, column):
        return lax.dynamic_slice(own[which], (row + core * half, column), (half, width))

    attend_cut = [cut(0, 0, block * width) for block in range(3)] + [cut(1, 0, 0)]
    expert_cut = [cut(2, 0, block * width) for block in range(4)]
    expert_cut += [cut(3, block * width, 0) for block in range(4)]

    def own_piece(name):
        kind, index = name[0], int(name[1])
        if kind in "ac":
            return jnp.stack([attend_cut[block] for block in ATTEND_BLOCKS[index]])
        if kind == "g":
            return jnp.stack([expert_cut[index], expert_cut[4 + index]])
        return jnp.stack([expert_cut[block] for block in EXPERT_BLOCKS[index]])

    arrived = {}
    mine, theirs = {}, {}
    for step, links in enumerate(PLAN):
        for link, sends in enumerate(links):
            if not sends:
                continue
            payload = {}
            for at, name in sends.items():
                if HOMES[name[0]] == at:
                    payload[at] = own_piece(name)
                else:
                    payload[at] = mine[arrived[at, name]]
            bits = link + 1
            moved = over_section(by_section(section, payload), bits, sorted(sends))
            mine[step, link] = moved
            theirs[step, link] = over_core(moved)
        for link, sends in enumerate(links):
            for at, name in sends.items():
                arrived[at ^ (link + 1), name] = (step, link)

    def weight_plan(layer):
        arrays, places = list(own), {}

        def place(array):
            if id(array) not in places:
                places[id(array)] = len(arrays)
                arrays.append(array)
            return places[id(array)]

        if layer in "ac":
            names = [(layer + str(index), ATTEND_BLOCKS[index]) for index in range(2)]
        else:
            names = [(layer + str(index), EXPERT_BLOCKS[index]) for index in range(4)]
        plan = []
        for at in range(SECTIONS):
            if layer == "g":
                names = [("g" + str(at), (0, 1))]
            steps = []
            for name, blocks in names:
                for index, block in enumerate(blocks):
                    if HOMES[layer] == at:
                        if layer in "ac":
                            source = (0, 0, block * width) if block < 3 else (1, 0, 0)
                        elif layer == "g":
                            source = (2, 0, 0) if block == 0 else (3, 0, 0)
                        elif block < 4:
                            source = (2, 0, block * width)
                        else:
                            source = (3, (block - 4) * width, 0)
                        steps.append((block, ("own",) + source))
                    else:
                        key = arrived[at, name]
                        steps.append((block, ("piece", place(mine[key]), place(theirs[key]), index)))
            plan.append(steps)
        return arrays, plan

    rows = jnp.concatenate(
        [
            attend_gain,
            attend_shift,
            attend_bias,
            expert_gain,
            expert_shift,
            expert_inner_bias,
            expert_outer_bias,
        ],
        axis=1,
    )
    rows = lax.all_gather(rows, "section", axis=0, tiled=True)
    sizes = [width, width, 3 * width, width, width, hidden, width]
    ends = [sum(sizes[: at + 1]) for at in range(len(sizes))]

    def row(slot, which):
        return rows[slot : slot + 1, ends[which] - sizes[which] : ends[which]]

    language_count = jnp.sum(caption_lengths)
    vision_count = jnp.full((), PATCHES * caption_lengths.size, jnp.int32)
    counts = lax.psum(
        jnp.stack([vision_count, language_count, vision_count + language_count]),
        ("section", "z", "core"),
    )
    info = jnp.concatenate(
        [caption_lengths, section.reshape(1).astype(jnp.int32), core.reshape(1).astype(jnp.int32)]
    )

    pad = ((0, 0), (0, ROWS - positions), (0, 0))
    x0 = jnp.pad(tokens, pad)
    last_grad = jnp.pad(cotangent, pad)
    attend0, attend2 = weight_plan("a"), weight_plan("c")
    expert0, expert1, expert3 = weight_plan("g"), weight_plan("e"), weight_plan("f")

    def to_sections(value):
        return [value] + [over_section(value, bits) for bits in (1, 2, 3)]

    def back_from_sections(value):
        return [value[0]] + [over_section(value[bits], bits) for bits in (1, 2, 3)]

    def items_of(parts):
        return [part.reshape(items, CAP_ROWS, width) for part in parts]

    y0, qkv0, mixed0, caption_rows = attend_forward(
        x0, info, attend0, row(0, 0), row(0, 1), row(0, 2), following=(row(0, 3), row(0, 4))
    )
    caption_rows = to_sections(caption_rows.reshape(-1, width))
    x2, act1, slope1 = expert_forward(
        y0, info, expert1, row(1, 3), row(1, 4), row(1, 5), row(1, 6), PATCH_ROWS, "patch"
    )
    inner_quarter = lax.dynamic_slice(row(0, 5), (0, section * width), (1, width))
    act0, slope0, parts = shared_forward(caption_rows, info, expert0, inner_quarter)
    parts = items_of(back_from_sections(parts))
    x3, qkv2, mixed2, x2 = attend_forward(
        x2,
        info,
        attend2,
        row(2, 0),
        row(2, 1),
        row(2, 2),
        merge=(y0, parts, row(0, 6)),
    )
    layer_output, act3, slope3 = expert_forward(
        x3, info, expert3, row(3, 3), row(3, 4), row(3, 5), row(3, 6), ROWS, "all"
    )

    def halved(keep, send):
        keep = added(keep, over_core(send))
        middle = keep.shape[1] // 2
        quarter, eighth = middle // 2, middle // 4
        first, second = keep[:, :middle], keep[:, middle:]
        first = added(first[:, :quarter], over_section(first[:, quarter:], 1))
        second = added(second[:, :quarter], over_section(second[:, quarter:], 2))
        first = added(first[:, :eighth], over_section(first[:, eighth:], 2))
        second = added(second[:, :eighth], over_section(second[:, eighth:], 1))
        return jnp.concatenate([first, second], axis=1)

    grad3, keep, send, *small3 = expert_backward(
        x3, info, expert3, row(3, 3), row(3, 4), act3, slope3, last_grad, ROWS, "all"
    )
    sum3 = lax.psum(halved(keep, send), "z")

    def after(value, earlier):
        return lax.optimization_barrier((value, earlier))[0]

    grad2, keep, send, *small2, caption_grad = attend_backward(
        x2, info, attend2, row(2, 0), row(2, 1), qkv2, mixed2, grad3
    )
    sum2 = lax.psum(after(halved(keep, send), sum3), "z")
    caption_grads = to_sections(caption_grad.reshape(-1, width))
    grad1, keep, send, *small1 = expert_backward(
        y0, info, expert1, row(1, 3), row(1, 4), act1, slope1, grad2, PATCH_ROWS, "patch"
    )
    sum1 = lax.psum(after(halved(keep, send), sum2), "z")
    parts, keep, send, inner_grad, outer_grad = shared_backward(
        caption_rows, caption_grads, info, expert0, act0, slope0
    )
    sum0 = lax.psum(after(added(keep, over_core(send)), sum1), "z")
    parts = items_of(back_from_sections(parts))
    tokens_grad, keep, send, *small_first, gain_grad, shift_grad = attend_backward(
        x0,
        info,
        attend0,
        row(0, 0),
        row(0, 1),
        qkv0,
        mixed0,
        grad1,
        first=(y0, row(0, 3), parts),
    )
    inner_grad = lax.dynamic_update_slice(
        jnp.zeros((1, hidden), F32), inner_grad, (0, section * width)
    )
    small0 = [gain_grad, shift_grad, inner_grad, outer_grad]
    small = jnp.concatenate(
        small_first + small2 + small0 + small1 + small3, axis=1
    )
    small_rows = 8
    small = jnp.pad(small, ((0, 0), (0, small_rows * hidden - small.shape[1])))
    small = small.reshape(small_rows, hidden)
    small = small + over_core(small)
    small = small + over_section(small, 1)
    small = small + over_section(small, 2)
    last = jnp.concatenate([halved(keep, send)[0], small.astype(BF16)], axis=0)
    last = lax.psum(after(last, sum0), "z")
    sum_first, small = last[:-small_rows][None], last[-small_rows:].astype(F32)

    as_float = counts.astype(F32)
    one = jnp.ones((), F32)
    attend_scales = jnp.stack([as_float[2], one, as_float[2], one])
    expert_scales = jnp.stack([as_float[1], as_float[0], one, as_float[2]])

    def at_home(sums, scales):
        targets = sorted(sums)
        blank = jnp.zeros_like(sums[targets[0]])
        pieces = [by_section(section, {at: sums.get(at, blank) for at in range(SECTIONS)})]
        for bits in (1, 2, 3):
            sends = {at ^ bits: sums[at] for at in targets}
            pieces.append(over_section(by_section(section, sends), bits, sorted(sends)))
        pieces = jnp.stack(pieces)
        scale = lax.dynamic_index_in_dim(scales, section, 0).reshape(1, 1)
        return finish(info, scale, pieces, over_core(pieces))

    inputs_whole, outputs_whole = at_home({0: sum0, 1: sum1, 3: sum3}, expert_scales)
    attend_whole, output_whole = at_home({0: sum_first, 2: sum2}, attend_scales)

    small = small.reshape(-1)
    attend_size, expert_size = 5 * width, 3 * width + hidden
    cuts = [attend_size, 2 * attend_size]
    cuts += [cuts[1] + expert_size, cuts[1] + 2 * expert_size, cuts[1] + 3 * expert_size]
    small = jnp.split(small, cuts)
    none_attend, none_expert = jnp.zeros_like(small[0]), jnp.zeros_like(small[2])
    attend_small = jnp.stack([small[0], none_attend, small[1], none_attend])
    expert_small = jnp.stack([small[2], small[3], none_expert, small[4]])
    attend_small = attend_small / attend_scales.reshape(-1, 1)
    expert_small = expert_small / expert_scales.reshape(-1, 1)
    attend_small = lax.dynamic_index_in_dim(attend_small, section, 0)
    expert_small = lax.dynamic_index_in_dim(expert_small, section, 0)
    return (
        layer_output[:, :positions],
        tokens_grad[:, :positions],
        attend_small[:, :width],
        attend_small[:, width : 2 * width],
        attend_whole,
        attend_small[:, 2 * width :],
        output_whole,
        expert_small[:, :width],
        expert_small[:, width : 2 * width],
        inputs_whole,
        expert_small[:, 2 * width : 2 * width + hidden],
        outputs_whole,
        expert_small[:, 2 * width + hidden :],
        counts,
    )


def solution(mesh):
    sections, groups = mesh.shape["section"], mesh.shape["dp"]
    split = Mesh(mesh.devices.reshape(sections, groups // 2, 2), ("section", "z", "core"))
    items = P(("section", "z", "core"), None, None)
    flat = P("section", None)
    matrix = P("section", None, None)
    placed = (
        items,
        P(("section", "z", "core")),
        flat,
        flat,
        matrix,
        flat,
        matrix,
        flat,
        flat,
        matrix,
        flat,
        matrix,
        flat,
        items,
    )
    return jax.shard_map(
        per_device,
        mesh=split,
        in_specs=placed,
        out_specs=(
            items,
            items,
            flat,
            flat,
            matrix,
            flat,
            matrix,
            flat,
            flat,
            matrix,
            flat,
            matrix,
            flat,
            P(),
        ),
        check_vma=False,
    )
```

```python
from functools import partial

import jax
import jax.numpy as jnp
from jax import lax
from jax.experimental import pallas as pl
from jax.experimental.pallas import tpu as pltpu
from jax.sharding import Mesh
from jax.sharding import PartitionSpec as P

HEADS = 12
HEAD_DIM = 64
PATCHES = 197
ROWS = 256
CAP_FIRST, CAP_ROWS = 192, 48
PATCH_ROWS = 208
PAIR = 2 * HEAD_DIM
SECTIONS = 4
PIECE_ROWS = 48
VMEM_BYTES = 58 * 1024 * 1024
F32 = jnp.float32
BF16 = jnp.bfloat16

PLAN_FOUR = (
    ({0: "a0", 1: "e0", 2: "c0", 3: "F"}, {0: "a1", 1: "e2", 2: "c0", 3: "F"}),
    ({0: "a1", 1: "e1", 2: "a1", 3: "e2"}, {0: "a0", 1: "a0", 2: "F", 3: "c0"}),
    ({0: "g3", 1: "e2", 2: "c1"}, {0: "e0", 1: "e3", 2: "c1"}),
    ({0: "g1", 1: "e3", 2: "e0", 3: "e3"}, {0: "e1", 1: "e1", 3: "c1"}),
    ({}, {0: "g2", 1: "g3"}),
)
PLAN_ANY = (
    ({0: "a0", 1: "e0", 2: "c0", 3: "f0"}, {0: "a1", 1: "e2", 2: "c0", 3: "f0"}),
    ({0: "a1", 1: "e1", 2: "a1", 3: "e2"}, {0: "a0", 1: "a0", 2: "c1", 3: "f1"}),
    ({0: "g3", 1: "e2", 2: "c1", 3: "f1"}, {0: "e0", 1: "e3", 2: "f0", 3: "f2"}),
    ({0: "g1", 1: "e3", 2: "e0", 3: "e3"}, {0: "e1", 1: "e1", 2: "f1", 3: "f3"}),
    ({0: "c1", 1: "f2", 3: "f2"}, {0: "g2", 1: "g3", 3: "c0"}),
    ({1: "f3", 3: "f3"}, {}),
)
EARLY_STEPS = 3
HOMES = {"a": 0, "c": 2, "e": 1, "f": 3, "F": 3, "g": 0}
ATTEND_BLOCKS = ((0, 1), (2, 3))
EXPERT_BLOCKS = ((0, 1), (4, 5), (2, 3), (6, 7))


def dot_plain(left, right):
    return jnp.dot(left, right, preferred_element_type=F32)


def dot_last(left, right):
    return lax.dot_general(left, right, (((1,), (1,)), ((), ())), preferred_element_type=F32)


def dot_first(left, right):
    return lax.dot_general(left, right, (((0,), (0,)), ((), ())), preferred_element_type=F32)


def column_sum(matrix):
    return jnp.sum(matrix.astype(F32), axis=0, keepdims=True)


def norm_parts(rows):
    centre = rows - jnp.mean(rows, axis=-1, keepdims=True)
    scale = lax.rsqrt(jnp.mean(centre * centre, axis=-1, keepdims=True) + 1e-06)
    return centre * scale, scale


def norm_back(normed_grad, unit, scale, gain):
    unit_grad = normed_grad * gain
    along = jnp.mean(unit_grad * unit, axis=-1, keepdims=True)
    return scale * (unit_grad - jnp.mean(unit_grad, axis=-1, keepdims=True) - unit * along)


def true_positions(length, first, count, axis, kind):
    shape = (count, 1) if axis == 0 else (1, count)
    position = first + lax.broadcasted_iota(jnp.int32, shape, axis)
    patch = position < PATCHES
    if kind == "patch":
        return patch
    caption = (position >= PATCHES) & (position - PATCHES < length)
    return caption if kind == "caption" else patch | caption


def head_masks():
    lane = lax.broadcasted_iota(jnp.int32, (1, PAIR), 1)
    even = (lane < HEAD_DIM).astype(F32).astype(BF16)
    odd = (lane >= HEAD_DIM).astype(F32).astype(BF16)
    return lane < HEAD_DIM, even, odd


def split_pair(pair, even, odd):
    return jnp.concatenate([pair * even, pair * odd], axis=0)


def start_weights(info, first, refs, plan, blocks, sems):
    half = blocks.shape[1] // 2
    section, core, plane = info[first], info[first + 1], info[first + 2]
    for at, at_plane, steps in plan:
        here = section == at
        if at_plane is not None:
            here = here & (plane == at_plane)

        @pl.when(here)
        def _(steps=steps):
            for block, source in steps:
                if source[0] == "own":
                    _, which, row, column = source
                    width = blocks.shape[2]
                    for part in range(2):
                        pltpu.make_async_copy(
                            refs[which].at[
                                pl.ds(row + part * half, half), pl.ds(column, width)
                            ],
                            blocks.at[block, pl.ds(part * half, half)],
                            sems.at[block],
                        ).start()
                else:
                    _, mine, theirs, index = source
                    pltpu.make_async_copy(
                        refs[mine].at[index],
                        blocks.at[block, pl.ds(pl.multiple_of(core * half, half), half)],
                        sems.at[block],
                    ).start()
                    pltpu.make_async_copy(
                        refs[theirs].at[index],
                        blocks.at[block, pl.ds(pl.multiple_of((1 - core) * half, half), half)],
                        sems.at[block],
                    ).start()


def wait_block(blocks, block, sems):
    pltpu.make_async_copy(blocks.at[block], blocks.at[block], sems.at[block]).wait()


def store_turned(target, turned, columns, section, core):
    half = target.shape[0] // 2
    for piece in range(16):
        path, owner = (piece >> 2) & 1, piece & 3
        away = owner ^ section
        place = ((away & 1) << 1) | (away >> 1) if path == 0 else away
        row = ((piece >> 3) ^ core) * half + path * (half // 2) + place * PIECE_ROWS
        target[pl.ds(pl.multiple_of(row, 16), PIECE_ROWS), columns] = turned[
            piece * PIECE_ROWS : (piece + 1) * PIECE_ROWS
        ]


def attend_forward_kernel(plan, weight_count, merge, info, *refs):
    weights, refs = refs[:weight_count], refs[weight_count:]
    if merge:
        x_ref, before_ref, part_ref, outer_ref, gain_ref, shift_ref, bias_ref = refs[:7]
        y_ref, qkv_ref, mixed_ref, joined_ref, blocks, sems, joined = refs[7:]
    else:
        x_ref, gain_ref, shift_ref, bias_ref, next_gain_ref, next_shift_ref = refs[:6]
        y_ref, qkv_ref, mixed_ref, caption_ref, blocks, sems = refs[6:]
    item = pl.program_id(0)
    items = pl.num_programs(0)
    length = info[item]
    width = x_ref.shape[-1]

    @pl.when(item == 0)
    def _():
        start_weights(info, items, weights, plan, blocks, sems)

    cap = slice(CAP_FIRST, CAP_FIRST + CAP_ROWS)
    if merge:
        joined[...] = x_ref[0].astype(F32)
        branch = part_ref[0].astype(F32) + outer_ref[...]
        is_true = true_positions(length, CAP_FIRST, CAP_ROWS, 0, "caption")
        captions = before_ref[0, cap] + jnp.where(is_true, branch, 0.0)
        position = CAP_FIRST + lax.broadcasted_iota(jnp.int32, (CAP_ROWS, 1), 0)
        captions = captions.astype(BF16).astype(F32)
        joined[cap] = jnp.where(position < PATCHES, joined[cap], captions)
        x = joined[...]
        joined_ref[0] = x.astype(BF16)
    else:
        x = x_ref[0].astype(F32)
    unit, _ = norm_parts(x)
    normed = (unit * gain_ref[...] + shift_ref[...]).astype(BF16)

    @pl.when(item == 0)
    def _():
        for block in range(4):
            wait_block(blocks, block, sems)

    queries = dot_plain(normed, blocks[0]) + bias_ref[:, :width]
    qkv_ref[0, :, :width] = (queries * HEAD_DIM ** (-0.5)).astype(BF16)
    qkv_ref[0, :, width : 2 * width] = dot_plain(normed, blocks[1]).astype(BF16)
    values = dot_plain(normed, blocks[2]) + bias_ref[:, width : 2 * width]
    qkv_ref[0, :, 2 * width :] = values.astype(BF16)
    key_true = true_positions(length, 0, ROWS, 1, "all")
    low_half, even, odd = head_masks()
    ones = jnp.ones((ROWS, PAIR), BF16)
    for pair in range(HEADS // 2):
        at = pair * PAIR
        q2 = qkv_ref[0, :, at : at + PAIR]
        k2 = qkv_ref[0, :, width + at : width + at + PAIR]
        v2 = qkv_ref[0, :, 2 * width + at : 2 * width + at + PAIR]
        scores = jnp.where(key_true, dot_last(split_pair(q2, even, odd), k2), -1e9)
        largest = jnp.max(scores, axis=-1, keepdims=True)
        weight = jnp.exp(scores - largest).astype(BF16)
        summed = dot_plain(weight, jnp.concatenate([v2, ones], axis=1))
        top = jnp.where(low_half, summed[:ROWS, :PAIR], summed[ROWS:, :PAIR])
        below = jnp.where(low_half, summed[:ROWS, PAIR:], summed[ROWS:, PAIR:])
        mixed_ref[0, :, at : at + PAIR] = (top / below).astype(BF16)
    branch = dot_plain(mixed_ref[0], blocks[3]) + bias_ref[:, 2 * width :]
    row_true = true_positions(length, 0, ROWS, 0, "all")
    y = x + jnp.where(row_true, branch, 0.0)
    y_ref[0] = y.astype(y_ref.dtype)
    if not merge:
        unit, _ = norm_parts(y[cap])
        caption_ref[0] = (unit * next_gain_ref[...] + next_shift_ref[...]).astype(BF16)


def attend_backward_kernel(plan, weight_count, first, info, *refs):
    weights, refs = refs[:weight_count], refs[weight_count:]
    x_ref, gain_ref, shift_ref, qkv_ref, mixed_ref, grad_ref = refs[:6]
    if first:
        after_ref, next_gain_ref, *parts = refs[6:12]
        refs = refs[12:]
    else:
        refs = refs[6:]
    out_ref, keep_ref, send_ref, gain_grad_ref, shift_grad_ref, bias_grad_ref = refs[:6]
    if first:
        next_gain_grad_ref, next_shift_grad_ref, joined = refs[6], refs[7], refs[-1]
    else:
        caption_ref = refs[6]
    blocks, sems, normed_turned, mixed_turned, branch_all, projected, mixed_grad = refs[
        8 if first else 7 :
    ][:7]
    item = pl.program_id(0)
    items = pl.num_programs(0)
    length = info[item]
    section, core = info[items], info[items + 1]
    width = x_ref.shape[-1]
    here = pl.ds(pl.multiple_of(item * ROWS, ROWS), ROWS)
    cap = slice(CAP_FIRST, CAP_FIRST + CAP_ROWS)

    @pl.when(item == 0)
    def _():
        start_weights(info, items, weights, plan, blocks, sems)

    def add_to(ref, part):
        @pl.when(item == 0)
        def _():
            ref[...] = part

        @pl.when(item > 0)
        def _():
            ref[...] += part

    x = x_ref[0].astype(F32)
    unit, scale = norm_parts(x)
    normed = (unit * gain_ref[...] + shift_ref[...]).astype(BF16)
    incoming = grad_ref[0].astype(F32)
    if first:
        after_unit, after_scale = norm_parts(after_ref[0, cap])
        caption_grad = parts[0][0].astype(F32)
        for part in parts[1:]:
            caption_grad = caption_grad + part[0].astype(F32)
        joined[...] = incoming
        joined[cap] += norm_back(caption_grad, after_unit, after_scale, next_gain_ref[...])
        incoming = joined[...]
        add_to(next_gain_grad_ref, jnp.sum(caption_grad * after_unit, axis=0, keepdims=True))
        add_to(next_shift_grad_ref, jnp.sum(caption_grad, axis=0, keepdims=True))
    row_true = true_positions(length, 0, ROWS, 0, "all")
    branch = jnp.where(row_true, incoming, 0.0).astype(BF16)
    branch_all[here, :] = branch
    store_turned(normed_turned, normed.T, here, section, core)
    store_turned(mixed_turned, mixed_ref[0].T, here, section, core)

    @pl.when(item == 0)
    def _():
        for block in range(4):
            wait_block(blocks, block, sems)

    mixed_grad[...] = dot_last(branch, blocks[3]).astype(BF16)
    key_true = true_positions(length, 0, ROWS, 0, "all")
    _, even, odd = head_masks()
    for pair in range(HEADS // 2):
        at = pair * PAIR
        q2 = split_pair(qkv_ref[0, :, at : at + PAIR], even, odd)
        k2 = qkv_ref[0, :, width + at : width + at + PAIR]
        v2 = qkv_ref[0, :, 2 * width + at : 2 * width + at + PAIR]
        g2 = split_pair(mixed_grad[:, at : at + PAIR], even, odd)
        scores = jnp.where(key_true, dot_last(k2, q2), -1e9)
        weight = jnp.exp(scores - jnp.max(scores, axis=0, keepdims=True))
        weight = weight / jnp.sum(weight, axis=0, keepdims=True)
        weight_grad = dot_last(v2, g2)
        along = jnp.sum(weight * weight_grad, axis=0, keepdims=True)
        score_grad = (weight * (weight_grad - along)).astype(BF16)
        values_grad = dot_plain(weight.astype(BF16), g2).astype(BF16)
        keys_grad = dot_plain(score_grad, q2).astype(BF16)
        k2_split = split_pair(k2, even, odd)
        stacked = jnp.concatenate([score_grad[:, :ROWS], score_grad[:, ROWS:]], axis=0)
        queries_grad = dot_first(stacked, k2_split).astype(BF16)
        queries_grad = (queries_grad.astype(F32) * HEAD_DIM ** (-0.5)).astype(BF16)
        projected[here, at : at + PAIR] = queries_grad
        projected[here, width + at : width + at + PAIR] = keys_grad
        projected[here, 2 * width + at : 2 * width + at + PAIR] = values_grad
    normed_grad = dot_last(projected[here, :width], blocks[0])
    normed_grad += dot_last(projected[here, width : 2 * width], blocks[1])
    normed_grad += dot_last(projected[here, 2 * width :], blocks[2])
    out = (incoming + norm_back(normed_grad, unit, scale, gain_ref[...])).astype(BF16)
    out_ref[0] = out
    if not first:
        is_true = true_positions(length, CAP_FIRST, CAP_ROWS, 0, "caption")
        caption_ref[0] = jnp.where(is_true, out[cap].astype(F32), 0.0).astype(BF16)
    add_to(gain_grad_ref, jnp.sum(normed_grad * unit, axis=0, keepdims=True))
    add_to(shift_grad_ref, jnp.sum(normed_grad, axis=0, keepdims=True))

    @pl.when(item == items - 1)
    def _():
        half = width // 2
        for block in range(4):
            columns = slice(block * width, (block + 1) * width)
            left = normed_turned if block < 3 else mixed_turned
            right = projected[:, columns] if block < 3 else branch_all[...]
            keep_ref[0, :, columns] = dot_plain(left[:half], right).astype(BF16)
            send_ref[0, :, columns] = dot_plain(left[half:], right).astype(BF16)
        bias_grad_ref[:, :width] = column_sum(projected[:, :width])
        bias_grad_ref[:, width : 2 * width] = column_sum(projected[:, 2 * width :])
        bias_grad_ref[:, 2 * width :] = column_sum(branch_all[...])


SHORT = pl.CostEstimate(flops=0, bytes_accessed=100_000, transcendentals=0)
ANYWHERE = pl.BlockSpec(memory_space=pl.ANY)


def whole_block(shape):
    return pl.BlockSpec(shape, lambda step, info: (0,) * len(shape))


def item_block(shape):
    return pl.BlockSpec((1,) + shape[1:], lambda step, info: (step,) + (0,) * (len(shape) - 1))


def blocks_scratch(count, width):
    return [pltpu.VMEM((count, width, width), BF16), pltpu.SemaphoreType.DMA((count,))]


def attend_forward(x, info, weights, gain, shift, bias, merge=None, following=None):
    arrays, plan = weights
    items, _, width = x.shape
    row = whole_block((1, width))
    bias_row = whole_block((1, 3 * width))
    caption_shape = (items, CAP_ROWS, width)
    if merge is not None:
        before, part, outer = merge
        operands = (x, before, part, outer, gain, shift, bias)
        specs = [item_block(x.shape), item_block(x.shape), item_block(caption_shape)]
        specs += [row, row, row, bias_row]
        last_shape, kind, scratch = x.shape, BF16, [pltpu.VMEM((ROWS, width), F32)]
    else:
        operands = (x, gain, shift, bias, *following)
        specs = [item_block(x.shape), row, row, bias_row, row, row]
        last_shape, kind, scratch = caption_shape, F32, []
    return pl.pallas_call(
        partial(attend_forward_kernel, plan, len(arrays), merge is not None),
        grid_spec=pltpu.PrefetchScalarGridSpec(
            num_scalar_prefetch=1,
            grid=(items,),
            in_specs=[ANYWHERE] * len(arrays) + specs,
            out_specs=[
                item_block(x.shape),
                item_block((items, ROWS, 3 * width)),
                item_block((items, ROWS, width)),
                item_block(last_shape),
            ],
            scratch_shapes=blocks_scratch(4, width) + scratch,
        ),
        out_shape=[
            jax.ShapeDtypeStruct(x.shape, kind),
            jax.ShapeDtypeStruct((items, ROWS, 3 * width), BF16),
            jax.ShapeDtypeStruct((items, ROWS, width), BF16),
            jax.ShapeDtypeStruct(last_shape, BF16),
        ],
        compiler_params=pltpu.CompilerParams(vmem_limit_bytes=VMEM_BYTES),
        cost_estimate=SHORT,
        name="attend_forward",
    )(info, *arrays, *operands)


def attend_backward(x, info, weights, gain, shift, qkv, mixed, incoming, first=None):
    arrays, plan = weights
    items, _, width = x.shape
    half = width // 2
    row = whole_block((1, width))
    caption_shape = (items, CAP_ROWS, width)
    operands = (x, gain, shift, qkv, mixed, incoming)
    specs = [item_block(x.shape), row, row, item_block(qkv.shape), item_block(mixed.shape)]
    specs += [item_block(incoming.shape)]
    outs = [
        (item_block(x.shape), x.shape, BF16),
        (whole_block((1, half, 4 * width)), (1, half, 4 * width), BF16),
        (whole_block((1, half, 4 * width)), (1, half, 4 * width), BF16),
        (row, (1, width), F32),
        (row, (1, width), F32),
        (whole_block((1, 3 * width)), (1, 3 * width), F32),
    ]
    scratch = []
    if first is not None:
        after, next_gain, parts = first
        operands += (after, next_gain, *parts)
        specs += [item_block(after.shape), row] + [item_block(caption_shape)] * 4
        outs += [(row, (1, width), F32)] * 2
        scratch = [pltpu.VMEM((ROWS, width), F32)]
    else:
        outs += [(item_block(caption_shape), caption_shape, BF16)]
    return pl.pallas_call(
        partial(attend_backward_kernel, plan, len(arrays), first is not None),
        grid_spec=pltpu.PrefetchScalarGridSpec(
            num_scalar_prefetch=1,
            grid=(items,),
            in_specs=[ANYWHERE] * len(arrays) + specs,
            out_specs=[spec for spec, _, _ in outs],
            scratch_shapes=blocks_scratch(4, width)
            + [
                pltpu.VMEM((width, items * ROWS), BF16),
                pltpu.VMEM((width, items * ROWS), BF16),
                pltpu.VMEM((items * ROWS, width), BF16),
                pltpu.VMEM((items * ROWS, 3 * width), BF16),
                pltpu.VMEM((ROWS, width), BF16),
            ]
            + scratch,
        ),
        out_shape=[jax.ShapeDtypeStruct(shape, kind) for _, shape, kind in outs],
        compiler_params=pltpu.CompilerParams(vmem_limit_bytes=VMEM_BYTES),
        cost_estimate=SHORT,
        name="attend_backward",
    )(info, *arrays, *operands)


def normal_parts(u):
    size = jnp.abs(u) * 0.7071067811865476
    t = 1.0 / (1.0 + 0.3275911 * size)
    bell = jnp.exp(-size * size)
    poly = t * (
        0.254829592
        + t * (-0.284496736 + t * (1.421413741 + t * (-1.453152027 + t * 1.061405429)))
    )
    tail = 0.5 * poly * bell
    return jnp.where(u < 0, tail, 1.0 - tail), 0.3989422804014327 * bell


def inner_forward(normed, matrix, bias):
    inner = dot_plain(normed, matrix) + bias
    cumulative, density = normal_parts(inner)
    return (inner * cumulative).astype(BF16), (cumulative + inner * density).astype(BF16)


def expert_forward_kernel(plan, weight_count, count, kind, info, *refs):
    weights, refs = refs[:weight_count], refs[weight_count:]
    x_ref, gain_ref, shift_ref, inner_ref, outer_ref = refs[:5]
    y_ref, act_ref, slope_ref, blocks, sems, normed, total = refs[5:]
    step = pl.program_id(0)
    items, _, width = x_ref.shape

    @pl.when(step == 0)
    def _():
        start_weights(info, items, weights, plan, blocks, sems)
        for item in range(items):
            x = x_ref[item, :count].astype(BF16).astype(F32)
            unit, _ = norm_parts(x)
            normed[item * count : (item + 1) * count] = (
                unit * gain_ref[...] + shift_ref[...]
            ).astype(BF16)

    wait_block(blocks, step, sems)
    wait_block(blocks, step + 4, sems)
    for at in range(0, width, 256):
        columns = slice(at, at + 256)
        act, slope = inner_forward(normed[...], blocks[step, :, columns], inner_ref[:, columns])
        act_ref[:, columns] = act
        slope_ref[:, columns] = slope
    part = dot_plain(act_ref[...], blocks[step + 4])

    @pl.when(step == 0)
    def _():
        total[...] = part

    @pl.when(step > 0)
    def _():
        total[...] += part

    @pl.when(step == pl.num_programs(0) - 1)
    def _():
        for item in range(items):
            row_true = true_positions(info[item], 0, count, 0, kind)
            branch = total[item * count : (item + 1) * count] + outer_ref[...]
            x = x_ref[item, :count].astype(BF16).astype(F32)
            y_ref[item, :count] = (x + jnp.where(row_true, branch, 0.0)).astype(BF16)
            if count < ROWS:
                y_ref[item, count:] = jnp.zeros((ROWS - count, width), BF16)


def expert_backward_kernel(plan, weight_count, count, kind, info, *refs):
    weights, refs = refs[:weight_count], refs[weight_count:]
    x_ref, gain_ref, shift_ref, act_ref, slope_ref, grad_ref = refs[:6]
    out_ref, keep_ref, send_ref, gain_grad_ref, shift_grad_ref, inner_grad_ref, outer_grad_ref = (
        refs[6:13]
    )
    blocks, sems, normed_turned, branch_turned, branch, inner_all, total = refs[13:]
    step = pl.program_id(0)
    items, _, width = x_ref.shape
    half = width // 2
    section, core = info[items], info[items + 1]

    @pl.when(step == 0)
    def _():
        start_weights(info, items, weights, plan, blocks, sems)
        outer = None
        for item in range(items):
            here = slice(item * count, (item + 1) * count)
            unit, _ = norm_parts(x_ref[item, :count].astype(BF16).astype(F32))
            normed = (unit * gain_ref[...] + shift_ref[...]).astype(BF16)
            row_true = true_positions(info[item], 0, count, 0, kind)
            incoming = grad_ref[item, :count].astype(F32)
            masked = jnp.where(row_true, incoming, 0.0).astype(BF16)
            branch[here] = masked
            store_turned(normed_turned, normed.T, here, section, core)
            store_turned(branch_turned, masked.T, here, section, core)
            term = column_sum(masked)
            outer = term if outer is None else outer + term
        outer_grad_ref[...] = outer

    wait_block(blocks, step, sems)
    wait_block(blocks, step + 4, sems)
    for at in range(0, width, 256):
        columns = slice(at, at + 256)
        act_grad = dot_last(branch[...], blocks[step + 4, columns])
        inner = (slope_ref[:, columns].astype(F32) * act_grad).astype(BF16)
        inner_all[:, columns] = inner
        inner_grad_ref[:, columns] = column_sum(inner)
        keep_ref[0, :, columns] = dot_plain(normed_turned[:half], inner).astype(BF16)
        send_ref[0, :, columns] = dot_plain(normed_turned[half:], inner).astype(BF16)
        act = act_ref[:, columns]
        keep_ref[1, :, columns] = dot_plain(branch_turned[:half], act).astype(BF16)
        send_ref[1, :, columns] = dot_plain(branch_turned[half:], act).astype(BF16)
    part = dot_last(inner_all[...], blocks[step])

    @pl.when(step == 0)
    def _():
        total[...] = part

    @pl.when(step > 0)
    def _():
        total[...] += part

    @pl.when(step == pl.num_programs(0) - 1)
    def _():
        gain_sum, shift_sum = None, None
        for item in range(items):
            unit, scale = norm_parts(x_ref[item, :count].astype(BF16).astype(F32))
            normed_grad = total[item * count : (item + 1) * count]
            gain_part = jnp.sum(normed_grad * unit, axis=0, keepdims=True)
            shift_part = jnp.sum(normed_grad, axis=0, keepdims=True)
            gain_sum = gain_part if gain_sum is None else gain_sum + gain_part
            shift_sum = shift_part if shift_sum is None else shift_sum + shift_part
            incoming = grad_ref[item, :count].astype(F32)
            hidden = incoming + norm_back(normed_grad, unit, scale, gain_ref[...])
            out_ref[item, :count] = hidden.astype(BF16)
            if count < ROWS:
                out_ref[item, count:] = grad_ref[item, count:]
        gain_grad_ref[...] = gain_sum
        shift_grad_ref[...] = shift_sum


def shared_forward_kernel(*refs):
    *rows_refs, inputs_ref, inner_ref, outputs_ref, part_ref, normed, total = refs
    count = rows_refs[0].shape[0]
    step = pl.program_id(0)

    @pl.when(step == 0)
    def _():
        for index, ref in enumerate(rows_refs):
            normed[index * count : (index + 1) * count] = ref[...]
        total[...] = jnp.zeros_like(total)

    act, _ = inner_forward(normed[...], inputs_ref[...], inner_ref[...])
    total[...] += dot_plain(act, outputs_ref[...])

    @pl.when(step == pl.num_programs(0) - 1)
    def _():
        for index in range(SECTIONS):
            part_ref[index] = total[index * count : (index + 1) * count].astype(BF16)


def shared_backward_kernel(plan, weight_count, info, *refs):
    weights, refs = refs[:weight_count], refs[weight_count:]
    rows_refs, grad_refs, inner_ref = refs[:4], refs[4:8], refs[8]
    part_ref, keep_ref, send_ref, inner_grad_ref, outer_grad_ref = refs[9:14]
    blocks, sems, normed, branch, matrix = refs[14:]
    count, width = rows_refs[0].shape
    half = width // 2
    first = info.shape[0] - 3
    core = info[first + 1]
    start_weights(info, first, weights, plan, blocks, sems)
    for index in range(SECTIONS):
        here = slice(index * count, (index + 1) * count)
        normed[here] = rows_refs[index][...]
        branch[here] = grad_refs[index][...]
    outer_grad_ref[...] = column_sum(grad_refs[0][...])
    wait_block(blocks, 0, sems)
    wait_block(blocks, 1, sems)
    part = None
    for at in range(0, width, 256):
        columns = slice(at, at + 256)
        act, slope = inner_forward(normed[...], blocks[0, :, columns], inner_ref[:, columns])
        act_grad = dot_last(branch[...], blocks[1, columns])
        inner = (slope.astype(F32) * act_grad).astype(BF16)
        inner_grad_ref[:, columns] = column_sum(inner)
        matrix[0, :, columns] = dot_first(normed[...], inner).astype(BF16)
        matrix[1, :, columns] = dot_first(branch[...], act).astype(BF16)
        term = dot_last(inner, blocks[0, :, columns])
        part = term if part is None else part + term
    for index in range(SECTIONS):
        part_ref[index] = part[index * count : (index + 1) * count].astype(BF16)
    quarter = half // 4
    for which in range(2):
        for group in range(4):
            columns = slice(group * width, (group + 1) * width)
            mine = pl.multiple_of(core * half, 16) + group * quarter
            other = pl.multiple_of((1 - core) * half, 16) + group * quarter
            keep_ref[which, :, columns] = matrix[which, pl.ds(pl.multiple_of(mine, 16), quarter)]
            send_ref[which, :, columns] = matrix[which, pl.ds(pl.multiple_of(other, 16), quarter)]


def chunk_columns(rows, width):
    return pl.BlockSpec((rows, width), lambda step, info: (0, step))


def expert_forward(x, info, weights, gain, shift, inner, outer, count, kind):
    arrays, plan = weights
    items, _, width = x.shape
    hidden = inner.shape[1]
    row = whole_block((1, width))
    return pl.pallas_call(
        partial(expert_forward_kernel, plan, len(arrays), count, kind),
        grid_spec=pltpu.PrefetchScalarGridSpec(
            num_scalar_prefetch=1,
            grid=(hidden // width,),
            in_specs=[ANYWHERE] * len(arrays)
            + [whole_block(x.shape), row, row, chunk_columns(1, width), row],
            out_specs=[
                whole_block((items, ROWS, width)),
                chunk_columns(items * count, width),
                chunk_columns(items * count, width),
            ],
            scratch_shapes=blocks_scratch(8, width)
            + [
                pltpu.VMEM((items * count, width), BF16),
                pltpu.VMEM((items * count, width), F32),
            ],
        ),
        out_shape=[
            jax.ShapeDtypeStruct((items, ROWS, width), BF16),
            jax.ShapeDtypeStruct((items * count, hidden), BF16),
            jax.ShapeDtypeStruct((items * count, hidden), BF16),
        ],
        compiler_params=pltpu.CompilerParams(vmem_limit_bytes=VMEM_BYTES),
        cost_estimate=SHORT,
        name="expert_forward_" + kind,
    )(info, *arrays, x, gain, shift, inner, outer)


def expert_backward(x, info, weights, gain, shift, act, slope, incoming, count, kind):
    arrays, plan = weights
    items, _, width = x.shape
    half = width // 2
    hidden = act.shape[1]
    row = whole_block((1, width))
    travel = pl.BlockSpec((2, half, width), lambda step, info: (0, 0, step))
    return pl.pallas_call(
        partial(expert_backward_kernel, plan, len(arrays), count, kind),
        grid_spec=pltpu.PrefetchScalarGridSpec(
            num_scalar_prefetch=1,
            grid=(hidden // width,),
            in_specs=[ANYWHERE] * len(arrays)
            + [
                whole_block(x.shape),
                row,
                row,
                chunk_columns(items * count, width),
                chunk_columns(items * count, width),
                whole_block(incoming.shape),
            ],
            out_specs=[
                whole_block(incoming.shape),
                travel,
                travel,
                row,
                row,
                chunk_columns(1, width),
                row,
            ],
            scratch_shapes=blocks_scratch(8, width)
            + [
                pltpu.VMEM((width, items * count), BF16),
                pltpu.VMEM((width, items * count), BF16),
                pltpu.VMEM((items * count, width), BF16),
                pltpu.VMEM((items * count, width), BF16),
                pltpu.VMEM((items * count, width), F32),
            ],
        ),
        out_shape=[
            jax.ShapeDtypeStruct(incoming.shape, BF16),
            jax.ShapeDtypeStruct((2, half, hidden), BF16),
            jax.ShapeDtypeStruct((2, half, hidden), BF16),
            jax.ShapeDtypeStruct((1, width), F32),
            jax.ShapeDtypeStruct((1, width), F32),
            jax.ShapeDtypeStruct((1, hidden), F32),
            jax.ShapeDtypeStruct((1, width), F32),
        ],
        compiler_params=pltpu.CompilerParams(vmem_limit_bytes=VMEM_BYTES),
        cost_estimate=SHORT,
        name="expert_backward_" + kind,
    )(info, *arrays, x, gain, shift, act, slope, incoming)


IN_VMEM = pl.BlockSpec(memory_space=pltpu.VMEM)
IN_SMEM = pl.BlockSpec(memory_space=pltpu.SMEM)


def shared_forward(rows, inputs, inner, outputs):
    count, width = rows[0].shape
    total = SECTIONS * count
    hidden = inner.shape[1]
    return pl.pallas_call(
        shared_forward_kernel,
        grid=(hidden // width,),
        in_specs=[pl.BlockSpec(rows[0].shape, lambda step: (0, 0))] * 4
        + [
            pl.BlockSpec((width, width), lambda step: (0, step)),
            pl.BlockSpec((1, width), lambda step: (0, step)),
            pl.BlockSpec((width, width), lambda step: (step, 0)),
        ],
        out_specs=pl.BlockSpec((SECTIONS, count, width), lambda step: (0, 0, 0)),
        scratch_shapes=[pltpu.VMEM((total, width), BF16), pltpu.VMEM((total, width), F32)],
        out_shape=jax.ShapeDtypeStruct((SECTIONS, count, width), BF16),
        compiler_params=pltpu.CompilerParams(vmem_limit_bytes=VMEM_BYTES),
        cost_estimate=SHORT,
        name="shared_forward",
    )(*rows, inputs, inner, outputs)


def shared_backward(rows, grads, info, weights, inner):
    arrays, plan = weights
    count, width = rows[0].shape
    total = SECTIONS * count
    travel = (2, width // 8, 4 * width)
    return pl.pallas_call(
        partial(shared_backward_kernel, plan, len(arrays)),
        in_specs=[IN_SMEM] + [ANYWHERE] * len(arrays) + [IN_VMEM] * 9,
        out_specs=[IN_VMEM] * 5,
        scratch_shapes=blocks_scratch(2, width)
        + [
            pltpu.VMEM((total, width), BF16),
            pltpu.VMEM((total, width), BF16),
            pltpu.VMEM((2, width, width), BF16),
        ],
        out_shape=[
            jax.ShapeDtypeStruct((SECTIONS, count, width), BF16),
            jax.ShapeDtypeStruct(travel, BF16),
            jax.ShapeDtypeStruct(travel, BF16),
            jax.ShapeDtypeStruct((1, width), F32),
            jax.ShapeDtypeStruct((1, width), F32),
        ],
        compiler_params=pltpu.CompilerParams(vmem_limit_bytes=VMEM_BYTES),
        cost_estimate=SHORT,
        name="shared_backward",
    )(info, *arrays, *rows, *grads, inner)


def plane_turn(plane, planes):
    return ((plane & 1) << 1) | (plane >> 1) if planes == 4 else 0


def finish_kernel(planes, info, scale_ref, mine_ref, theirs_ref, *refs):
    step = pl.program_id(0)
    count = mine_ref.shape[1]
    placed = refs[-1]
    outs = refs[:-1]
    width = placed.shape[1]
    half = width // 2
    at = info.shape[0] - 3
    section, core = info[at], info[at + 1]
    turn = plane_turn(info[at + 2], planes)
    turned = turn if count == 1 else 0
    scale = scale_ref[0, 0]
    columns = pl.ds(pl.multiple_of((step ^ turned) * width, width), width)

    def place(which):
        def by_rows():
            for side, ref in enumerate((mine_ref, theirs_ref)):
                for away in range(SECTIONS):
                    for path in range(2):
                        row = (core ^ side) * half + path * (half // 2)
                        row = row + (section ^ away) * PIECE_ROWS
                        placed[pl.ds(pl.multiple_of(row, 16), PIECE_ROWS), :] = ref[
                            away, which, path * PIECE_ROWS : (path + 1) * PIECE_ROWS, columns
                        ].astype(F32)

        def by_columns():
            for side, ref in enumerate((mine_ref, theirs_ref)):
                for group in range(4):
                    quarter = half // 4
                    row = (core ^ side) * half + group * quarter
                    column = pl.multiple_of((group ^ turn) * width, width)
                    placed[pl.ds(pl.multiple_of(row, 16), quarter), :] = ref[
                        step, which, :, pl.ds(column, width)
                    ].astype(F32)

        if count == 1:
            by_rows()
        else:
            pl.when(section != 0)(by_rows)
            pl.when(section == 0)(by_columns)

    place(0)
    if count == 1:

        @pl.when(step < 3)
        def _():
            outs[0][0] = placed[...] / scale

        @pl.when(step == 3)
        def _():
            outs[1][0] = placed[...] / scale

    else:
        outs[0][0] = placed[...] / scale
        place(1)
        outs[1][0] = (placed[...] / scale).T


def finish(info, scale, mine, theirs, planes):
    count, hidden = mine.shape[1], mine.shape[3]
    width = hidden // 4
    if count == 1:
        shapes = [(1, width, 3 * width), (1, width, width)]
        maps = [lambda step, info: (0, 0, jnp.minimum(step, 2)), lambda step, info: (0, 0, 0)]
    else:
        shapes = [(1, width, hidden), (1, hidden, width)]
        maps = [lambda step, info: (0, 0, step), lambda step, info: (0, step, 0)]
    return pl.pallas_call(
        partial(finish_kernel, planes),
        grid_spec=pltpu.PrefetchScalarGridSpec(
            num_scalar_prefetch=1,
            grid=(4,),
            in_specs=[IN_SMEM, whole_block(mine.shape), whole_block(mine.shape)],
            out_specs=[pl.BlockSpec((1, width, width), at) for at in maps],
            scratch_shapes=[pltpu.VMEM((width, width), F32)],
        ),
        out_shape=[jax.ShapeDtypeStruct(shape, F32) for shape in shapes],
        compiler_params=pltpu.CompilerParams(vmem_limit_bytes=VMEM_BYTES),
        cost_estimate=SHORT,
        name="finish",
    )(info, scale, mine, theirs)


def over_section(value, bits, sources=range(SECTIONS)):
    return lax.ppermute(value, "section", [(at, at ^ bits) for at in sources])


def over_core(value):
    return lax.ppermute(value, "core", [(0, 1), (1, 0)])


def over_plane(value, pairs):
    return lax.ppermute(value, "z", pairs)


def added(left, right):
    return (left.astype(F32) + right.astype(F32)).astype(BF16)


def after(value, *earlier):
    return lax.optimization_barrier((value,) + earlier)[0]


def by_section(section, values):
    result, last = None, None
    for at in sorted(values):
        if result is None:
            result = values[at]
        elif values[at] is not last:
            result = jnp.where(section >= at, values[at], result)
        last = values[at]
    return result


class Planes:
    def __init__(self, value, plane, planes):
        self.value, self.plane, self.planes, self.turn = value, plane, planes, 0

    def sends(self, *earlier):
        value = after(self.value, *earlier) if earlier else self.value
        if self.planes != 4:
            return (value,)
        bits = (1, 2, 2, 1)[self.turn]
        if self.turn < 2:
            bit = (self.plane & 1, self.plane >> 1)[self.turn]
            size = value.shape[-1] // 2
            value = lax.dynamic_slice_in_dim(value, (1 - bit) * size, size, value.ndim - 1)
        return (over_plane(value, [(at, at ^ bits) for at in range(4)]),)

    def take(self, arrived):
        if self.planes != 4:
            self.value = lax.psum(arrived, "z") if self.turn == 3 else arrived
        elif self.turn < 2:
            bit = (self.plane & 1, self.plane >> 1)[self.turn]
            size = self.value.shape[-1] // 2
            keep = lax.dynamic_slice_in_dim(self.value, bit * size, size, self.value.ndim - 1)
            self.value = added(keep, arrived)
        else:
            self.value = jnp.concatenate([self.value, arrived], axis=-1)
        self.turn += 1

    def in_order(self, value):
        if self.planes != 4:
            return value
        size, turn = value.shape[-1] // 4, plane_turn(self.plane, 4)
        parts = [
            lax.dynamic_slice_in_dim(value, (at ^ turn) * size, size, value.ndim - 1)
            for at in range(4)
        ]
        return jnp.concatenate(parts, axis=-1)


class Weights:
    def __init__(self, own, section, core, plane, planes):
        self.own, self.section, self.core, self.plane = own, section, core, plane
        self.four = planes == 4
        self.plan = PLAN_FOUR if self.four else PLAN_ANY
        self.half, self.width = own[1].shape[0] // 2, own[1].shape[1]
        self.mine, self.theirs, self.arrived, self.cuts = {}, {}, {}, {}

    def cut(self, which, row, column):
        key = (which, row, column)
        if key not in self.cuts:
            self.cuts[key] = lax.dynamic_slice(
                self.own[which], (row + self.core * self.half, column), (self.half, self.width)
            )
        return self.cuts[key]

    def place(self, layer, block):
        if layer in "ac":
            return (0, 0, block * self.width) if block < 3 else (1, 0, 0)
        if layer == "g":
            return (2, 0, block * self.width) if block < 4 else (3, (block - 4) * self.width, 0)
        return (2, 0, block * self.width) if block < 4 else (3, (block - 4) * self.width, 0)

    def own_piece(self, name):
        if name == "F":
            pieces = [self.own_piece("f" + str(index)) for index in range(4)]
            return by_section(self.plane, dict(enumerate(pieces)))
        layer, index = name[0], int(name[1])
        if layer in "ac":
            blocks = ATTEND_BLOCKS[index]
        else:
            blocks = (index, 4 + index) if layer == "g" else EXPERT_BLOCKS[index]
        return jnp.stack([self.cut(*self.place(layer, block)) for block in blocks])

    def holds(self, name):
        home = HOMES[name[0]]
        return lambda at: self.own_piece(name) if at == home else self.mine[self.arrived[at, name]]

    def run_step(self, step, *earlier):
        for link, sends in enumerate(self.plan[step]):
            if sends:
                payload = {at: self.holds(name)(at) for at, name in sends.items()}
                payload = by_section(self.section, payload)
                if earlier:
                    payload = after(payload, *earlier)
                moved = over_section(payload, link + 1, sorted(sends))
                self.mine[step, link] = moved
        for link, sends in enumerate(self.plan[step]):
            for at, name in sends.items():
                self.arrived[at ^ (link + 1), name] = (step, link)

    def run_planes(self, step, *earlier):
        if not self.four:
            return ()
        if step == 1:
            own = by_section(self.section, {at: self.holds("F")(at) for at in range(SECTIONS)})
            self.mine["plane", 0] = own
        up, down = self.mine["plane", step - 1], self.mine["plane", 1 - step]
        if earlier:
            up, down = after(up, *earlier), after(down, *earlier)
        up = over_plane(up, [(at, at + 1) for at in range(step - 1, 3)])
        down = over_plane(down, [(at, at - 1) for at in range(4 - step, 0, -1)])
        self.mine["plane", step], self.mine["plane", -step] = up, down
        return up, down

    def hand_over(self, steps, *earlier):
        for key in [key for key in self.mine if key[0] in steps and key not in self.theirs]:
            mine = after(self.mine[key], *earlier) if earlier else self.mine[key]
            self.theirs[key] = over_core(mine)
        return [self.theirs[key] for key in self.theirs if key[0] in steps]

    def set_mine(self, keys, values):
        for key, value in zip(keys, values):
            self.mine[key] = value

    def layer(self, layer):
        arrays, places = list(self.own), {}

        def place(key):
            if key not in self.theirs:
                self.theirs[key] = over_core(self.mine[key])
            if key not in places:
                places[key] = len(arrays)
                arrays.extend([self.mine[key], self.theirs[key]])
            return places[key], places[key] + 1

        if layer in "ac":
            names = [(layer + str(index), ATTEND_BLOCKS[index]) for index in range(2)]
        else:
            names = [(layer + str(index), EXPERT_BLOCKS[index]) for index in range(4)]
        plan = []
        for at in range(SECTIONS):
            if layer == "g":
                names = [("g" + str(at), (0, 1))]
            if HOMES[layer] == at:
                steps = []
                for name, blocks in names:
                    for block in blocks:
                        source = block * 4 if layer == "g" else block
                        steps.append((block, ("own",) + self.place(layer, source)))
                plan.append((at, None, steps))
                continue
            by_plane = layer == "f" and self.four
            for plane in range(4) if by_plane else (None,):
                steps = []
                for index, (name, blocks) in enumerate(names):
                    key = ("plane", plane - index) if by_plane else self.arrived[at, name]
                    for which, block in enumerate(blocks):
                        steps.append((block, ("piece",) + place(key) + (which,)))
                plan.append((at, plane, steps))
        return arrays, plan


def per_device(
    tokens,
    caption_lengths,
    attend_gain,
    attend_shift,
    attend_inputs,
    attend_bias,
    attend_output,
    expert_gain,
    expert_shift,
    expert_inputs,
    expert_inner_bias,
    expert_outputs,
    expert_outer_bias,
    cotangent,
):
    section, core, plane = lax.axis_index("section"), lax.axis_index("core"), lax.axis_index("z")
    planes = lax.axis_size("z")
    items, positions, width = tokens.shape
    hidden = expert_inputs.shape[-1]
    weights = Weights(
        (attend_inputs[0], attend_output[0], expert_inputs[0], expert_outputs[0]),
        section,
        core,
        plane,
        planes,
    )

    def to_sections(value):
        return [value] + [over_section(value, bits) for bits in (1, 2, 3)]

    def items_of(part):
        return part.reshape(items, CAP_ROWS, width)

    def under(outputs, *arrivals):
        joined = lax.optimization_barrier(tuple(outputs) + arrivals)
        return joined[: len(outputs)], joined[len(outputs) :]

    for step in range(EARLY_STEPS):
        weights.run_step(step)
    rows = jnp.concatenate(
        [
            attend_gain,
            attend_shift,
            attend_bias,
            expert_gain,
            expert_shift,
            expert_inner_bias,
            expert_outer_bias,
            jnp.full((1, 128), jnp.sum(caption_lengths), F32),
        ],
        axis=1,
    )
    rows = jnp.concatenate(to_sections(rows), axis=0)
    language_count = jnp.sum(rows[:, -128:], axis=0, keepdims=True)
    language_count = language_count + over_core(language_count)
    if planes == 4:
        language_count = language_count + over_plane(language_count, [(at, at ^ 1) for at in range(4)])
        language_count = language_count + over_plane(language_count, [(at, at ^ 2) for at in range(4)])
    else:
        language_count = lax.psum(language_count, "z")
    language_count = language_count[0, 0].astype(jnp.int32)
    vision_count = PATCHES * items * SECTIONS * 2 * planes
    counts = jnp.stack(
        [jnp.full((), vision_count, jnp.int32), language_count, language_count + vision_count]
    )
    rows = [lax.dynamic_index_in_dim(rows, at ^ section, 0) for at in range(SECTIONS)]
    sizes = [width, width, 3 * width, width, width, hidden, width]
    ends = [sum(sizes[: at + 1]) for at in range(len(sizes))]

    def row(slot, which):
        return rows[slot][:, ends[which] - sizes[which] : ends[which]]

    info = [value.reshape(1).astype(jnp.int32) for value in (section, core, plane)]
    info = after(jnp.concatenate([caption_lengths] + info), counts, *weights.hand_over((0, 1)))

    pad = ((0, 0), (0, ROWS - positions), (0, 0))
    x0 = jnp.pad(tokens, pad)
    last_grad = jnp.pad(cotangent, pad)
    attend0 = weights.layer("a")
    y0, qkv0, mixed0, caption_rows = attend_forward(
        x0, info, attend0, row(0, 0), row(0, 1), row(0, 2), following=(row(0, 3), row(0, 4))
    )
    caption_rows = to_sections(caption_rows.reshape(-1, width))
    planes_moved = weights.run_planes(1)
    weights.run_step(EARLY_STEPS, *caption_rows[1:], *weights.hand_over((2,), caption_rows[0]))
    late_keys = [key for key in weights.mine if key[0] == EARLY_STEPS]
    caption_rows[0] = after(caption_rows[0], *planes_moved)
    planes_moved = weights.run_planes(2, caption_rows[1])
    outputs = shared_forward(caption_rows, expert_inputs[0], expert_inner_bias, expert_outputs[0])
    if weights.four:
        late_keys += [("plane", 2), ("plane", -2)]
    (part,), moved = under([outputs], *[weights.mine[key] for key in late_keys])
    weights.set_mine(late_keys, moved)
    branch = {at: over_section(part[at], at, [0]) for at in range(1, SECTIONS)}
    branch[0] = part[0]
    weights.run_planes(3, part)
    expert1 = weights.layer("e")
    outputs = expert_forward(
        y0, info, expert1, row(1, 3), row(1, 4), row(1, 5), row(1, 6), PATCH_ROWS, "patch"
    )
    if weights.four:
        last_moved = [("plane", 3), ("plane", -3)]
    else:
        last_moved = []
        for step in range(EARLY_STEPS + 1, len(weights.plan)):
            weights.run_step(step, part)
    (x2, act1, slope1), moved = under(outputs, *[weights.mine[key] for key in last_moved])
    weights.set_mine(last_moved, moved)
    branch = items_of(by_section(section, branch))
    attend2 = weights.layer("c")
    x3, qkv2, mixed2, x2 = attend_forward(
        x2, info, attend2, row(2, 0), row(2, 1), row(2, 2), merge=(y0, branch, row(0, 6))
    )
    expert3 = weights.layer("f")
    layer_output, act3, slope3 = expert_forward(
        x3, info, expert3, row(3, 3), row(3, 4), row(3, 5), row(3, 6), ROWS, "all"
    )

    def send_first(keep):
        middle = keep.shape[1] // 2
        return keep[:, middle // 2 : middle], keep[:, middle + middle // 2 :]

    def sum_first(keep, from_x, from_y):
        middle = keep.shape[1] // 2
        return (
            added(keep[:, : middle // 2], from_x),
            added(keep[:, middle : middle + middle // 2], from_y),
        )

    def send_second(first, second):
        eighth = first.shape[1] // 2
        return second[:, eighth:], first[:, eighth:]

    def sum_second(first, second, from_x, from_y):
        eighth = first.shape[1] // 2
        first = added(first[:, :eighth], from_y)
        return jnp.concatenate([first, added(second[:, :eighth], from_x)], axis=1)

    def over_links(sends):
        return over_section(sends[0], 1), over_section(sends[1], 2)

    def together(sends):
        arrived = []
        for bits, parts in ((1, [x for x, _ in sends]), (2, [y for _, y in sends])):
            flat = [part.reshape(-1, hidden) for part in parts]
            moved = over_section(jnp.concatenate(flat, axis=0), bits)
            ends, at = [], 0
            for part, rows_of in zip(parts, flat):
                ends.append(moved[at : at + rows_of.shape[0]].reshape(part.shape))
                at += rows_of.shape[0]
            arrived.append(ends)
        return list(zip(*arrived))

    def to_home(sums):
        got = [by_section(section, sums)]
        for bits in (1, 2, 3):
            sends = {at ^ bits: sums[at] for at in sums}
            got.append(over_section(by_section(section, sends), bits, sorted(sends)))
        return got

    last_moved = []
    if weights.four:
        weights.run_step(EARLY_STEPS + 1, x3)
        last_moved = [key for key in weights.mine if key[0] == EARLY_STEPS + 1]
    outputs = expert_backward(
        x3, info, expert3, row(3, 3), row(3, 4), act3, slope3, last_grad, ROWS, "all"
    )
    outputs, moved = under(outputs, *[weights.mine[key] for key in last_moved])
    weights.set_mine(last_moved, moved)
    grad3, keep, send, *small3 = outputs
    keep3 = added(keep, over_core(send))
    moved = over_links(send_first(keep3))
    grad3 = after(grad3, keep3)
    outputs = attend_backward(
        x2, info, attend2, row(2, 0), row(2, 1), qkv2, mixed2, grad3
    )
    (grad2, keep, send, *small2, caption_grad), moved = under(outputs, *moved)
    caption_grads = to_sections(caption_grad.reshape(-1, width))
    part3 = sum_first(keep3, *moved)
    keep2 = added(keep, over_core(send))
    moved3, moved2 = together([send_second(*part3), send_first(keep2)])
    grad2 = after(grad2, keep2, *part3)
    outputs = expert_backward(
        y0, info, expert1, row(1, 3), row(1, 4), act1, slope1, grad2, PATCH_ROWS, "patch"
    )
    (grad1, keep, send, *small1), moved = under(outputs, *caption_grads, *moved3, *moved2)
    caption_grads, moved3, moved2 = moved[:4], moved[4:6], moved[6:]
    sum3 = sum_second(*part3, *moved3)
    whole3 = lax.psum(sum3, "z")
    part2 = sum_first(keep2, *moved2)
    moved = over_links(send_second(*part2))
    inner_quarter = lax.dynamic_slice(row(0, 5), (0, section * width), (1, width))
    inner_quarter = after(inner_quarter, grad1, sum3, *part2)
    outputs = shared_backward(
        caption_rows, caption_grads, info, weights.layer("g"), inner_quarter
    )
    (parts, keep0, send0, inner_grad, outer_grad), moved = under(outputs, *moved)
    parts = [parts[0]] + [over_section(parts[bits], bits) for bits in (1, 2, 3)]
    sum2 = sum_second(*part2, *moved)
    keep1 = added(keep, over_core(send))
    keep0 = added(keep0, over_core(send0))
    planes0 = Planes(keep0, plane, planes)
    planes0.take(*planes0.sends())
    moved = over_links(send_first(after(keep1, parts[1], parts[2], parts[3])))
    sent0 = planes0.sends()
    grad1 = after(grad1, planes0.value, keep1, sum2)
    outputs = attend_backward(
        x0,
        info,
        attend0,
        row(0, 0),
        row(0, 1),
        qkv0,
        mixed0,
        grad1,
        first=(y0, row(0, 3), [items_of(value) for value in parts]),
    )
    outputs, moved = under(outputs, *moved, whole3, *sent0)
    tokens_grad, keep, send, *small_first, gain_grad, shift_grad = outputs
    whole3 = moved[2]
    planes0.take(*moved[3:])
    part1 = sum_first(keep1, *moved[:2])
    keep_first = added(keep, over_core(send))
    sum1 = sum_second(*part1, *over_links(send_second(*part1)))
    planes0.take(*planes0.sends())
    whole1 = lax.psum(sum1, "z")
    moved = over_links(send_first(after(keep_first, sum1, planes0.value)))
    planes0.take(*planes0.sends(keep_first, sum1))
    part_first = sum_first(keep_first, *moved)
    moved = over_links(send_second(*part_first))
    last = sum_second(*part_first, *moved)
    inner_grad = lax.dynamic_update_slice(
        jnp.zeros((1, hidden), F32), inner_grad, (0, section * width)
    )
    small0 = [gain_grad, shift_grad, inner_grad, outer_grad]
    small = jnp.concatenate(small_first + small2 + small0 + small1 + small3, axis=1)
    small_rows = 8
    small = jnp.pad(small, ((0, 0), (0, small_rows * hidden - small.shape[1])))
    small = small.reshape(small_rows, hidden)
    small = small + over_core(small)
    small = small + over_section(small, 1)
    small = small + over_section(small, 2)
    planes_last = Planes(
        jnp.concatenate([last[0], sum2[0], small.astype(BF16)], axis=0), plane, planes
    )
    home_early = to_home({0: after(planes0.value, last), 3: after(whole3, last)})
    for turn in range(3):
        planes_last.take(*planes_last.sends())
    home_late = to_home({1: after(whole1, planes_last.value, *home_early[1:3])})
    planes_last.take(*planes_last.sends(whole1, *home_early[1:3]))
    eighth = last.shape[1]
    last = after(planes_last.value, home_early[3])
    home_attend = to_home({0: last[None, :eighth], 2: last[None, eighth : 2 * eighth]})
    small = planes_last.in_order(last[2 * eighth :].astype(F32))

    as_float = counts.astype(F32)
    one = jnp.ones((), F32)
    attend_scales = jnp.stack([as_float[2], one, as_float[2], one])
    expert_scales = jnp.stack([as_float[1], as_float[0], one, as_float[2]])

    def placed(pieces, scales):
        scale = lax.dynamic_index_in_dim(scales, section, 0).reshape(1, 1)
        pieces = jnp.stack(pieces)
        return finish(info, scale, pieces, over_core(pieces), planes)

    blank = jnp.zeros_like(whole1)
    inputs_whole, outputs_whole = placed(
        [
            by_section(section, {0: early, 1: late, 2: blank, 3: early})
            for early, late in zip(home_early, home_late)
        ],
        expert_scales,
    )
    blank = jnp.zeros_like(home_attend[0])
    attend_whole, output_whole = placed(
        [by_section(section, {0: got, 1: blank, 2: got, 3: blank}) for got in home_attend],
        attend_scales,
    )

    small = small.reshape(-1)
    attend_size, expert_size = 5 * width, 3 * width + hidden
    cuts = [attend_size, 2 * attend_size]
    cuts += [cuts[1] + expert_size, cuts[1] + 2 * expert_size, cuts[1] + 3 * expert_size]
    small = jnp.split(small, cuts)
    none_attend, none_expert = jnp.zeros_like(small[0]), jnp.zeros_like(small[2])
    attend_small = jnp.stack([small[0], none_attend, small[1], none_attend])
    expert_small = jnp.stack([small[2], small[3], none_expert, small[4]])
    attend_small = attend_small / attend_scales.reshape(-1, 1)
    expert_small = expert_small / expert_scales.reshape(-1, 1)
    attend_small = lax.dynamic_index_in_dim(attend_small, section, 0)
    expert_small = lax.dynamic_index_in_dim(expert_small, section, 0)
    return (
        layer_output[:, :positions],
        tokens_grad[:, :positions],
        attend_small[:, :width],
        attend_small[:, width : 2 * width],
        attend_whole,
        attend_small[:, 2 * width :],
        output_whole,
        expert_small[:, :width],
        expert_small[:, width : 2 * width],
        inputs_whole,
        expert_small[:, 2 * width : 2 * width + hidden],
        outputs_whole,
        expert_small[:, 2 * width + hidden :],
        counts,
    )


def solution(mesh):
    sections, groups = mesh.shape["section"], mesh.shape["dp"]
    split = Mesh(mesh.devices.reshape(sections, groups // 2, 2), ("section", "z", "core"))
    items = P(("section", "z", "core"), None, None)
    flat = P("section", None)
    matrix = P("section", None, None)
    placed = (
        items,
        P(("section", "z", "core")),
        flat,
        flat,
        matrix,
        flat,
        matrix,
        flat,
        flat,
        matrix,
        flat,
        matrix,
        flat,
        items,
    )
    return jax.shard_map(
        per_device,
        mesh=split,
        in_specs=placed,
        out_specs=(
            items,
            items,
            flat,
            flat,
            matrix,
            flat,
            matrix,
            flat,
            flat,
            matrix,
            flat,
            matrix,
            flat,
            P(),
        ),
        check_vma=False,
    )
```

```python
from functools import partial

import jax
import jax.numpy as jnp
from jax import lax
from jax.experimental import pallas as pl
from jax.experimental.pallas import tpu as pltpu
from jax.sharding import Mesh
from jax.sharding import PartitionSpec as P

HEADS = 12
HEAD_DIM = 64
PATCHES = 197
ROWS = 256
CAP_FIRST, CAP_ROWS = 192, 48
PATCH_ROWS = 208
PAIR = 2 * HEAD_DIM
SECTIONS = 4
PIECE_ROWS = 48
VMEM_BYTES = 58 * 1024 * 1024
F32 = jnp.float32
BF16 = jnp.bfloat16

PLAN_FOUR = (
    ({0: "a0", 1: "e0", 2: "c0", 3: "F"}, {0: "a1", 1: "e2", 2: "c0", 3: "F"}),
    ({0: "a1", 1: "e1", 2: "a1", 3: "e2"}, {0: "a0", 1: "a0", 2: "F", 3: "c0"}),
    ({0: "g3", 1: "e2", 2: "c1"}, {0: "e0", 1: "e3", 2: "c1"}),
    ({0: "g1", 1: "e3", 2: "e0", 3: "e3"}, {0: "e1", 1: "e1", 3: "c1"}),
    ({}, {0: "g2", 1: "g3"}),
)
PLAN_ANY = (
    ({0: "a0", 1: "e0", 2: "c0", 3: "f0"}, {0: "a1", 1: "e2", 2: "c0", 3: "f0"}),
    ({0: "a1", 1: "e1", 2: "a1", 3: "e2"}, {0: "a0", 1: "a0", 2: "c1", 3: "f1"}),
    ({0: "g3", 1: "e2", 2: "c1", 3: "f1"}, {0: "e0", 1: "e3", 2: "f0", 3: "f2"}),
    ({0: "g1", 1: "e3", 2: "e0", 3: "e3"}, {0: "e1", 1: "e1", 2: "f1", 3: "f3"}),
    ({0: "c1", 1: "f2", 3: "f2"}, {0: "g2", 1: "g3", 3: "c0"}),
    ({1: "f3", 3: "f3"}, {}),
)
EARLY_STEPS = 3
HOMES = {"a": 0, "c": 2, "e": 1, "f": 3, "F": 3, "g": 0}
ATTEND_BLOCKS = ((0, 1), (2, 3))
EXPERT_BLOCKS = ((0, 1), (4, 5), (2, 3), (6, 7))


def dot_plain(left, right):
    return jnp.dot(left, right, preferred_element_type=F32)


def dot_last(left, right):
    return lax.dot_general(left, right, (((1,), (1,)), ((), ())), preferred_element_type=F32)


def dot_first(left, right):
    return lax.dot_general(left, right, (((0,), (0,)), ((), ())), preferred_element_type=F32)


def column_sum(matrix):
    return jnp.sum(matrix.astype(F32), axis=0, keepdims=True)


def norm_parts(rows):
    centre = rows - jnp.mean(rows, axis=-1, keepdims=True)
    scale = lax.rsqrt(jnp.mean(centre * centre, axis=-1, keepdims=True) + 1e-06)
    return centre * scale, scale


def norm_back(normed_grad, unit, scale, gain):
    unit_grad = normed_grad * gain
    along = jnp.mean(unit_grad * unit, axis=-1, keepdims=True)
    return scale * (unit_grad - jnp.mean(unit_grad, axis=-1, keepdims=True) - unit * along)


def true_positions(length, first, count, axis, kind):
    shape = (count, 1) if axis == 0 else (1, count)
    position = first + lax.broadcasted_iota(jnp.int32, shape, axis)
    patch = position < PATCHES
    if kind == "patch":
        return patch
    caption = (position >= PATCHES) & (position - PATCHES < length)
    return caption if kind == "caption" else patch | caption


def head_masks():
    lane = lax.broadcasted_iota(jnp.int32, (1, PAIR), 1)
    even = (lane < HEAD_DIM).astype(F32).astype(BF16)
    odd = (lane >= HEAD_DIM).astype(F32).astype(BF16)
    return lane < HEAD_DIM, even, odd


def split_pair(pair, even, odd):
    return jnp.concatenate([pair * even, pair * odd], axis=0)


def start_weights(info, first, refs, plan, blocks, sems):
    half = blocks.shape[1] // 2
    section, core, plane = info[first], info[first + 1], info[first + 2]
    for at, at_plane, steps in plan:
        here = section == at
        if at_plane is not None:
            here = here & (plane == at_plane)

        @pl.when(here)
        def _(steps=steps):
            for block, source in steps:
                if source[0] == "own":
                    _, which, row, column = source
                    width = blocks.shape[2]
                    for part in range(2):
                        pltpu.make_async_copy(
                            refs[which].at[
                                pl.ds(row + part * half, half), pl.ds(column, width)
                            ],
                            blocks.at[block, pl.ds(part * half, half)],
                            sems.at[block],
                        ).start()
                else:
                    _, mine, theirs, index = source
                    pltpu.make_async_copy(
                        refs[mine].at[index],
                        blocks.at[block, pl.ds(pl.multiple_of(core * half, half), half)],
                        sems.at[block],
                    ).start()
                    pltpu.make_async_copy(
                        refs[theirs].at[index],
                        blocks.at[block, pl.ds(pl.multiple_of((1 - core) * half, half), half)],
                        sems.at[block],
                    ).start()


def wait_block(blocks, block, sems):
    pltpu.make_async_copy(blocks.at[block], blocks.at[block], sems.at[block]).wait()


def store_turned(target, turned, columns, section, core):
    half = target.shape[0] // 2
    for piece in range(16):
        path, owner = (piece >> 2) & 1, piece & 3
        away = owner ^ section
        place = ((away & 1) << 1) | (away >> 1) if path == 0 else away
        row = ((piece >> 3) ^ core) * half + (place >> 1) * (half // 2)
        row = row + path * (half // 4) + (place & 1) * PIECE_ROWS
        target[pl.ds(pl.multiple_of(row, 16), PIECE_ROWS), columns] = turned[
            piece * PIECE_ROWS : (piece + 1) * PIECE_ROWS
        ]


def put_travel(refs, which, columns, rows):
    rows = rows.astype(BF16)
    size = rows.shape[0] // 4
    for index, ref in enumerate(refs):
        ref[which, :, columns] = rows[index * size : (index + 1) * size]


def attend_forward_kernel(plan, weight_count, merge, info, *refs):
    weights, refs = refs[:weight_count], refs[weight_count:]
    if merge:
        x_ref, before_ref, part_ref, outer_ref, gain_ref, shift_ref, bias_ref = refs[:7]
        y_ref, qkv_ref, mixed_ref, joined_ref, blocks, sems, joined = refs[7:]
    else:
        x_ref, gain_ref, shift_ref, bias_ref, next_gain_ref, next_shift_ref = refs[:6]
        y_ref, qkv_ref, mixed_ref, caption_ref, blocks, sems = refs[6:]
    item = pl.program_id(0)
    items = pl.num_programs(0)
    length = info[item]
    width = x_ref.shape[-1]

    @pl.when(item == 0)
    def _():
        start_weights(info, items, weights, plan, blocks, sems)

    cap = slice(CAP_FIRST, CAP_FIRST + CAP_ROWS)
    if merge:
        joined[...] = x_ref[0].astype(F32)
        branch = part_ref[0].astype(F32) + outer_ref[...]
        is_true = true_positions(length, CAP_FIRST, CAP_ROWS, 0, "caption")
        captions = before_ref[0, cap] + jnp.where(is_true, branch, 0.0)
        position = CAP_FIRST + lax.broadcasted_iota(jnp.int32, (CAP_ROWS, 1), 0)
        captions = captions.astype(BF16).astype(F32)
        joined[cap] = jnp.where(position < PATCHES, joined[cap], captions)
        x = joined[...]
        joined_ref[0] = x.astype(BF16)
    else:
        x = x_ref[0].astype(F32)
    unit, _ = norm_parts(x)
    normed = (unit * gain_ref[...] + shift_ref[...]).astype(BF16)

    @pl.when(item == 0)
    def _():
        for block in range(4):
            wait_block(blocks, block, sems)

    queries = dot_plain(normed, blocks[0]) + bias_ref[:, :width]
    qkv_ref[0, :, :width] = (queries * HEAD_DIM ** (-0.5)).astype(BF16)
    qkv_ref[0, :, width : 2 * width] = dot_plain(normed, blocks[1]).astype(BF16)
    values = dot_plain(normed, blocks[2]) + bias_ref[:, width : 2 * width]
    qkv_ref[0, :, 2 * width :] = values.astype(BF16)
    key_true = true_positions(length, 0, ROWS, 1, "all")
    low_half, even, odd = head_masks()
    ones = jnp.ones((ROWS, PAIR), BF16)

    def scores_of(pair):
        at = pair * PAIR
        q2 = qkv_ref[0, :, at : at + PAIR]
        k2 = qkv_ref[0, :, width + at : width + at + PAIR]
        return dot_last(split_pair(q2, even, odd), k2)

    ahead = [scores_of(0), scores_of(1)]
    for pair in range(HEADS // 2):
        at = pair * PAIR
        scores = jnp.where(key_true, ahead.pop(0), -1e9)
        if pair + 2 < HEADS // 2:
            ahead.append(scores_of(pair + 2))
        weight = jnp.exp(scores - jnp.max(scores, axis=-1, keepdims=True)).astype(BF16)
        v2 = qkv_ref[0, :, 2 * width + at : 2 * width + at + PAIR]
        summed = dot_plain(weight, jnp.concatenate([v2, ones], axis=1))
        top = jnp.where(low_half, summed[:ROWS, :PAIR], summed[ROWS:, :PAIR])
        below = jnp.where(low_half, summed[:ROWS, PAIR:], summed[ROWS:, PAIR:])
        mixed_ref[0, :, at : at + PAIR] = (top / below).astype(BF16)
    branch = dot_plain(mixed_ref[0], blocks[3]) + bias_ref[:, 2 * width :]
    row_true = true_positions(length, 0, ROWS, 0, "all")
    y = x + jnp.where(row_true, branch, 0.0)
    y_ref[0] = y.astype(y_ref.dtype)
    if not merge:
        unit, _ = norm_parts(y[cap])
        caption_ref[0] = (unit * next_gain_ref[...] + next_shift_ref[...]).astype(BF16)


def attend_backward_kernel(plan, weight_count, first, info, *refs):
    weights, refs = refs[:weight_count], refs[weight_count:]
    x_ref, gain_ref, shift_ref, qkv_ref, mixed_ref, grad_ref = refs[:6]
    if first:
        after_ref, next_gain_ref, *parts = refs[6:12]
        refs = refs[12:]
    else:
        refs = refs[6:]
    out_ref, gain_grad_ref, shift_grad_ref, bias_grad_ref = refs[:4]
    travel_refs = refs[4:8]
    if first:
        next_gain_grad_ref, next_shift_grad_ref, joined = refs[8], refs[9], refs[-1]
    else:
        caption_ref = refs[8]
    blocks, sems, normed_turned, mixed_turned, branch_all, projected, mixed_grad = refs[
        10 if first else 9 :
    ][:7]
    item = pl.program_id(0)
    items = pl.num_programs(0)
    length = info[item]
    section, core = info[items], info[items + 1]
    width = x_ref.shape[-1]
    here = pl.ds(pl.multiple_of(item * ROWS, ROWS), ROWS)
    cap = slice(CAP_FIRST, CAP_FIRST + CAP_ROWS)

    @pl.when(item == 0)
    def _():
        start_weights(info, items, weights, plan, blocks, sems)

    def add_to(ref, part):
        @pl.when(item == 0)
        def _():
            ref[...] = part

        @pl.when(item > 0)
        def _():
            ref[...] += part

    x = x_ref[0].astype(F32)
    unit, scale = norm_parts(x)
    normed = (unit * gain_ref[...] + shift_ref[...]).astype(BF16)
    incoming = grad_ref[0].astype(F32)
    if first:
        after_unit, after_scale = norm_parts(after_ref[0, cap])
        caption_grad = parts[0][0].astype(F32)
        for part in parts[1:]:
            caption_grad = caption_grad + part[0].astype(F32)
        joined[...] = incoming
        joined[cap] += norm_back(caption_grad, after_unit, after_scale, next_gain_ref[...])
        incoming = joined[...]
        add_to(next_gain_grad_ref, jnp.sum(caption_grad * after_unit, axis=0, keepdims=True))
        add_to(next_shift_grad_ref, jnp.sum(caption_grad, axis=0, keepdims=True))
    row_true = true_positions(length, 0, ROWS, 0, "all")
    branch = jnp.where(row_true, incoming, 0.0).astype(BF16)
    branch_all[here, :] = branch
    store_turned(normed_turned, normed.T, here, section, core)
    store_turned(mixed_turned, mixed_ref[0].T, here, section, core)

    @pl.when(item == 0)
    def _():
        for block in range(4):
            wait_block(blocks, block, sems)

    mixed_grad[...] = dot_last(branch, blocks[3]).astype(BF16)
    key_true = true_positions(length, 0, ROWS, 0, "all")
    _, even, odd = head_masks()

    def products_of(pair):
        at = pair * PAIR
        q2 = split_pair(qkv_ref[0, :, at : at + PAIR], even, odd)
        k2 = qkv_ref[0, :, width + at : width + at + PAIR]
        v2 = qkv_ref[0, :, 2 * width + at : 2 * width + at + PAIR]
        g2 = split_pair(mixed_grad[:, at : at + PAIR], even, odd)
        return q2, k2, g2, dot_last(k2, q2), dot_last(v2, g2)

    ahead = [products_of(0)]
    for pair in range(HEADS // 2):
        at = pair * PAIR
        q2, k2, g2, scores, weight_grad = ahead.pop(0)
        if pair + 1 < HEADS // 2:
            ahead.append(products_of(pair + 1))
        scores = jnp.where(key_true, scores, -1e9)
        weight = jnp.exp(scores - jnp.max(scores, axis=0, keepdims=True))
        weight = weight * (1.0 / jnp.sum(weight, axis=0, keepdims=True))
        product = weight * weight_grad
        along = jnp.sum(product, axis=0, keepdims=True)
        score_grad = (product - weight * along).astype(BF16)
        values_grad = dot_plain(weight.astype(BF16), g2).astype(BF16)
        keys_grad = dot_plain(score_grad, q2).astype(BF16)
        k2_split = split_pair(k2, even, odd)
        stacked = jnp.concatenate([score_grad[:, :ROWS], score_grad[:, ROWS:]], axis=0)
        queries_grad = dot_first(stacked, k2_split).astype(BF16)
        queries_grad = (queries_grad.astype(F32) * HEAD_DIM ** (-0.5)).astype(BF16)
        projected[here, at : at + PAIR] = queries_grad
        projected[here, width + at : width + at + PAIR] = keys_grad
        projected[here, 2 * width + at : 2 * width + at + PAIR] = values_grad
    normed_grad = dot_last(projected[here, :width], blocks[0])
    normed_grad += dot_last(projected[here, width : 2 * width], blocks[1])
    normed_grad += dot_last(projected[here, 2 * width :], blocks[2])
    out = (incoming + norm_back(normed_grad, unit, scale, gain_ref[...])).astype(BF16)
    out_ref[0] = out
    if not first:
        is_true = true_positions(length, CAP_FIRST, CAP_ROWS, 0, "caption")
        caption_ref[0] = jnp.where(is_true, out[cap].astype(F32), 0.0).astype(BF16)
    add_to(gain_grad_ref, jnp.sum(normed_grad * unit, axis=0, keepdims=True))
    add_to(shift_grad_ref, jnp.sum(normed_grad, axis=0, keepdims=True))

    @pl.when(item == items - 1)
    def _():
        for block in range(4):
            columns = slice(block * width, (block + 1) * width)
            left = normed_turned if block < 3 else mixed_turned
            right = projected[:, columns] if block < 3 else branch_all[...]
            put_travel(travel_refs, 0, columns, dot_plain(left[...], right))
        bias_grad_ref[:, :width] = column_sum(projected[:, :width])
        bias_grad_ref[:, width : 2 * width] = column_sum(projected[:, 2 * width :])
        bias_grad_ref[:, 2 * width :] = column_sum(branch_all[...])


SHORT = pl.CostEstimate(flops=0, bytes_accessed=100_000, transcendentals=0)
ANYWHERE = pl.BlockSpec(memory_space=pl.ANY)


def whole_block(shape):
    return pl.BlockSpec(shape, lambda step, info: (0,) * len(shape))


def item_block(shape):
    return pl.BlockSpec((1,) + shape[1:], lambda step, info: (step,) + (0,) * (len(shape) - 1))


def blocks_scratch(count, width):
    return [pltpu.VMEM((count, width, width), BF16), pltpu.SemaphoreType.DMA((count,))]


def attend_forward(x, info, weights, gain, shift, bias, merge=None, following=None):
    arrays, plan = weights
    items, _, width = x.shape
    row = whole_block((1, width))
    bias_row = whole_block((1, 3 * width))
    caption_shape = (items, CAP_ROWS, width)
    if merge is not None:
        before, part, outer = merge
        operands = (x, before, part, outer, gain, shift, bias)
        specs = [item_block(x.shape), item_block(x.shape), item_block(caption_shape)]
        specs += [row, row, row, bias_row]
        last_shape, kind, scratch = x.shape, BF16, [pltpu.VMEM((ROWS, width), F32)]
    else:
        operands = (x, gain, shift, bias, *following)
        specs = [item_block(x.shape), row, row, bias_row, row, row]
        last_shape, kind, scratch = caption_shape, F32, []
    return pl.pallas_call(
        partial(attend_forward_kernel, plan, len(arrays), merge is not None),
        grid_spec=pltpu.PrefetchScalarGridSpec(
            num_scalar_prefetch=1,
            grid=(items,),
            in_specs=[ANYWHERE] * len(arrays) + specs,
            out_specs=[
                item_block(x.shape),
                item_block((items, ROWS, 3 * width)),
                item_block((items, ROWS, width)),
                item_block(last_shape),
            ],
            scratch_shapes=blocks_scratch(4, width) + scratch,
        ),
        out_shape=[
            jax.ShapeDtypeStruct(x.shape, kind),
            jax.ShapeDtypeStruct((items, ROWS, 3 * width), BF16),
            jax.ShapeDtypeStruct((items, ROWS, width), BF16),
            jax.ShapeDtypeStruct(last_shape, BF16),
        ],
        compiler_params=pltpu.CompilerParams(vmem_limit_bytes=VMEM_BYTES),
        cost_estimate=SHORT,
        name="attend_forward",
    )(info, *arrays, *operands)


def attend_backward(x, info, weights, gain, shift, qkv, mixed, incoming, first=None):
    arrays, plan = weights
    items, _, width = x.shape
    half = width // 2
    row = whole_block((1, width))
    caption_shape = (items, CAP_ROWS, width)
    operands = (x, gain, shift, qkv, mixed, incoming)
    specs = [item_block(x.shape), row, row, item_block(qkv.shape), item_block(mixed.shape)]
    specs += [item_block(incoming.shape)]
    outs = [
        (item_block(x.shape), x.shape, BF16),
        (row, (1, width), F32),
        (row, (1, width), F32),
        (whole_block((1, 3 * width)), (1, 3 * width), F32),
    ]
    outs += [(whole_block((1, half // 2, 4 * width)), (1, half // 2, 4 * width), BF16)] * 4
    scratch = []
    if first is not None:
        after, next_gain, parts = first
        operands += (after, next_gain, *parts)
        specs += [item_block(after.shape), row] + [item_block(caption_shape)] * 4
        outs += [(row, (1, width), F32)] * 2
        scratch = [pltpu.VMEM((ROWS, width), F32)]
    else:
        outs += [(item_block(caption_shape), caption_shape, BF16)]
    return pl.pallas_call(
        partial(attend_backward_kernel, plan, len(arrays), first is not None),
        grid_spec=pltpu.PrefetchScalarGridSpec(
            num_scalar_prefetch=1,
            grid=(items,),
            in_specs=[ANYWHERE] * len(arrays) + specs,
            out_specs=[spec for spec, _, _ in outs],
            scratch_shapes=blocks_scratch(4, width)
            + [
                pltpu.VMEM((width, items * ROWS), BF16),
                pltpu.VMEM((width, items * ROWS), BF16),
                pltpu.VMEM((items * ROWS, width), BF16),
                pltpu.VMEM((items * ROWS, 3 * width), BF16),
                pltpu.VMEM((ROWS, width), BF16),
            ]
            + scratch,
        ),
        out_shape=[jax.ShapeDtypeStruct(shape, kind) for _, shape, kind in outs],
        compiler_params=pltpu.CompilerParams(vmem_limit_bytes=VMEM_BYTES),
        cost_estimate=SHORT,
        name="attend_backward",
    )(info, *arrays, *operands)


def normal_parts(u):
    t = pl.reciprocal(1.0 + 0.23164190 * jnp.abs(u), approx=True)
    bell = jnp.exp2((u * -0.7213475204444817) * u)
    poly = t * (
        0.127414796
        + t * (-0.142248368 + t * (0.7107068705 + t * (-0.7265760135 + t * 0.5307027145)))
    )
    tail = poly * bell
    return jnp.where(u < 0, tail, 1.0 - tail), bell


def inner_forward(normed, matrix, bias):
    inner = dot_plain(normed, matrix) + bias
    cumulative, bell = normal_parts(inner)
    slope = cumulative + (inner * 0.3989422804014327) * bell
    return (inner * cumulative).astype(BF16), slope.astype(BF16)


def expert_forward_kernel(plan, weight_count, count, kind, info, *refs):
    weights, refs = refs[:weight_count], refs[weight_count:]
    x_ref, gain_ref, shift_ref, inner_ref, outer_ref = refs[:5]
    y_ref, act_ref, slope_ref, blocks, sems, normed, total = refs[5:]
    step = pl.program_id(0)
    items, _, width = x_ref.shape

    @pl.when(step == 0)
    def _():
        start_weights(info, items, weights, plan, blocks, sems)
        for item in range(items):
            x = x_ref[item, :count].astype(BF16).astype(F32)
            unit, _ = norm_parts(x)
            normed[item * count : (item + 1) * count] = (
                unit * gain_ref[...] + shift_ref[...]
            ).astype(BF16)

    wait_block(blocks, step, sems)
    wait_block(blocks, step + 4, sems)
    for at in range(0, width, 256):
        columns = slice(at, at + 256)
        act, slope = inner_forward(normed[...], blocks[step, :, columns], inner_ref[:, columns])
        act_ref[:, columns] = act
        slope_ref[:, columns] = slope
    part = dot_plain(act_ref[...], blocks[step + 4])

    @pl.when(step == 0)
    def _():
        total[...] = part

    @pl.when(step > 0)
    def _():
        total[...] += part

    @pl.when(step == pl.num_programs(0) - 1)
    def _():
        for item in range(items):
            row_true = true_positions(info[item], 0, count, 0, kind)
            branch = total[item * count : (item + 1) * count] + outer_ref[...]
            x = x_ref[item, :count].astype(BF16).astype(F32)
            y_ref[item, :count] = (x + jnp.where(row_true, branch, 0.0)).astype(BF16)
            if count < ROWS:
                y_ref[item, count:] = jnp.zeros((ROWS - count, width), BF16)


def expert_backward_kernel(plan, weight_count, count, kind, info, *refs):
    weights, refs = refs[:weight_count], refs[weight_count:]
    x_ref, gain_ref, shift_ref, act_ref, slope_ref, grad_ref = refs[:6]
    out_ref, gain_grad_ref, shift_grad_ref, inner_grad_ref, outer_grad_ref = refs[6:11]
    travel_refs = refs[11:15]
    blocks, sems, normed_turned, branch_turned, branch, inner_all, total = refs[15:]
    step = pl.program_id(0)
    items, _, width = x_ref.shape
    section, core = info[items], info[items + 1]

    @pl.when(step == 0)
    def _():
        start_weights(info, items, weights, plan, blocks, sems)
        outer = None
        for item in range(items):
            here = slice(item * count, (item + 1) * count)
            unit, _ = norm_parts(x_ref[item, :count].astype(BF16).astype(F32))
            normed = (unit * gain_ref[...] + shift_ref[...]).astype(BF16)
            row_true = true_positions(info[item], 0, count, 0, kind)
            incoming = grad_ref[item, :count].astype(F32)
            masked = jnp.where(row_true, incoming, 0.0).astype(BF16)
            branch[here] = masked
            store_turned(normed_turned, normed.T, here, section, core)
            store_turned(branch_turned, masked.T, here, section, core)
            term = column_sum(masked)
            outer = term if outer is None else outer + term
        outer_grad_ref[...] = outer

    wait_block(blocks, step, sems)
    wait_block(blocks, step + 4, sems)
    for at in range(0, width, 256):
        columns = slice(at, at + 256)
        act_grad = dot_last(branch[...], blocks[step + 4, columns])
        inner = (slope_ref[:, columns].astype(F32) * act_grad).astype(BF16)
        inner_all[:, columns] = inner
        inner_grad_ref[:, columns] = column_sum(inner)
        put_travel(travel_refs, 0, columns, dot_plain(normed_turned[...], inner))
        put_travel(travel_refs, 1, columns, dot_plain(branch_turned[...], act_ref[:, columns]))
    part = dot_last(inner_all[...], blocks[step])

    @pl.when(step == 0)
    def _():
        total[...] = part

    @pl.when(step > 0)
    def _():
        total[...] += part

    @pl.when(step == pl.num_programs(0) - 1)
    def _():
        gain_sum, shift_sum = None, None
        for item in range(items):
            unit, scale = norm_parts(x_ref[item, :count].astype(BF16).astype(F32))
            normed_grad = total[item * count : (item + 1) * count]
            gain_part = jnp.sum(normed_grad * unit, axis=0, keepdims=True)
            shift_part = jnp.sum(normed_grad, axis=0, keepdims=True)
            gain_sum = gain_part if gain_sum is None else gain_sum + gain_part
            shift_sum = shift_part if shift_sum is None else shift_sum + shift_part
            incoming = grad_ref[item, :count].astype(F32)
            hidden = incoming + norm_back(normed_grad, unit, scale, gain_ref[...])
            out_ref[item, :count] = hidden.astype(BF16)
            if count < ROWS:
                out_ref[item, count:] = grad_ref[item, count:]
        gain_grad_ref[...] = gain_sum
        shift_grad_ref[...] = shift_sum


def shared_forward_kernel(*refs):
    *rows_refs, inputs_ref, inner_ref, outputs_ref, part_ref, normed, total = refs
    count = rows_refs[0].shape[0]
    step = pl.program_id(0)

    @pl.when(step == 0)
    def _():
        for index, ref in enumerate(rows_refs):
            normed[index * count : (index + 1) * count] = ref[...]
        total[...] = jnp.zeros_like(total)

    act, _ = inner_forward(normed[...], inputs_ref[...], inner_ref[...])
    total[...] += dot_plain(act, outputs_ref[...])

    @pl.when(step == pl.num_programs(0) - 1)
    def _():
        for index in range(SECTIONS):
            part_ref[index] = total[index * count : (index + 1) * count].astype(BF16)


def shared_backward_kernel(plan, weight_count, info, *refs):
    weights, refs = refs[:weight_count], refs[weight_count:]
    rows_refs, grad_refs, inner_ref = refs[:4], refs[4:8], refs[8]
    part_ref, keep_ref, send_ref, inner_grad_ref, outer_grad_ref = refs[9:14]
    blocks, sems, normed, branch, matrix = refs[14:]
    count, width = rows_refs[0].shape
    half = width // 2
    first = info.shape[0] - 3
    core = info[first + 1]
    start_weights(info, first, weights, plan, blocks, sems)
    for index in range(SECTIONS):
        here = slice(index * count, (index + 1) * count)
        normed[here] = rows_refs[index][...]
        branch[here] = grad_refs[index][...]
    outer_grad_ref[...] = column_sum(grad_refs[0][...])
    wait_block(blocks, 0, sems)
    wait_block(blocks, 1, sems)
    part = None
    for at in range(0, width, 256):
        columns = slice(at, at + 256)
        act, slope = inner_forward(normed[...], blocks[0, :, columns], inner_ref[:, columns])
        act_grad = dot_last(branch[...], blocks[1, columns])
        inner = (slope.astype(F32) * act_grad).astype(BF16)
        inner_grad_ref[:, columns] = column_sum(inner)
        matrix[0, :, columns] = dot_first(normed[...], inner).astype(BF16)
        matrix[1, :, columns] = dot_first(branch[...], act).astype(BF16)
        term = dot_last(inner, blocks[0, :, columns])
        part = term if part is None else part + term
    for index in range(SECTIONS):
        part_ref[index] = part[index * count : (index + 1) * count].astype(BF16)
    quarter = half // 4
    for which in range(2):
        for group in range(4):
            columns = slice(group * width, (group + 1) * width)
            mine = pl.multiple_of(core * half, 16) + group * quarter
            other = pl.multiple_of((1 - core) * half, 16) + group * quarter
            keep_ref[which, :, columns] = matrix[which, pl.ds(pl.multiple_of(mine, 16), quarter)]
            send_ref[which, :, columns] = matrix[which, pl.ds(pl.multiple_of(other, 16), quarter)]


def chunk_columns(rows, width):
    return pl.BlockSpec((rows, width), lambda step, info: (0, step))


def expert_forward(x, info, weights, gain, shift, inner, outer, count, kind):
    arrays, plan = weights
    items, _, width = x.shape
    hidden = inner.shape[1]
    row = whole_block((1, width))
    return pl.pallas_call(
        partial(expert_forward_kernel, plan, len(arrays), count, kind),
        grid_spec=pltpu.PrefetchScalarGridSpec(
            num_scalar_prefetch=1,
            grid=(hidden // width,),
            in_specs=[ANYWHERE] * len(arrays)
            + [whole_block(x.shape), row, row, chunk_columns(1, width), row],
            out_specs=[
                whole_block((items, ROWS, width)),
                chunk_columns(items * count, width),
                chunk_columns(items * count, width),
            ],
            scratch_shapes=blocks_scratch(8, width)
            + [
                pltpu.VMEM((items * count, width), BF16),
                pltpu.VMEM((items * count, width), F32),
            ],
        ),
        out_shape=[
            jax.ShapeDtypeStruct((items, ROWS, width), BF16),
            jax.ShapeDtypeStruct((items * count, hidden), BF16),
            jax.ShapeDtypeStruct((items * count, hidden), BF16),
        ],
        compiler_params=pltpu.CompilerParams(vmem_limit_bytes=VMEM_BYTES),
        cost_estimate=SHORT,
        name="expert_forward_" + kind,
    )(info, *arrays, x, gain, shift, inner, outer)


def expert_backward(x, info, weights, gain, shift, act, slope, incoming, count, kind):
    arrays, plan = weights
    items, _, width = x.shape
    half = width // 2
    hidden = act.shape[1]
    row = whole_block((1, width))
    travel = pl.BlockSpec((2, half // 2, width), lambda step, info: (0, 0, step))
    return pl.pallas_call(
        partial(expert_backward_kernel, plan, len(arrays), count, kind),
        grid_spec=pltpu.PrefetchScalarGridSpec(
            num_scalar_prefetch=1,
            grid=(hidden // width,),
            in_specs=[ANYWHERE] * len(arrays)
            + [
                whole_block(x.shape),
                row,
                row,
                chunk_columns(items * count, width),
                chunk_columns(items * count, width),
                whole_block(incoming.shape),
            ],
            out_specs=[whole_block(incoming.shape), row, row, chunk_columns(1, width), row]
            + [travel] * 4,
            scratch_shapes=blocks_scratch(8, width)
            + [
                pltpu.VMEM((width, items * count), BF16),
                pltpu.VMEM((width, items * count), BF16),
                pltpu.VMEM((items * count, width), BF16),
                pltpu.VMEM((items * count, width), BF16),
                pltpu.VMEM((items * count, width), F32),
            ],
        ),
        out_shape=[
            jax.ShapeDtypeStruct(incoming.shape, BF16),
            jax.ShapeDtypeStruct((1, width), F32),
            jax.ShapeDtypeStruct((1, width), F32),
            jax.ShapeDtypeStruct((1, hidden), F32),
            jax.ShapeDtypeStruct((1, width), F32),
        ]
        + [jax.ShapeDtypeStruct((2, half // 2, hidden), BF16)] * 4,
        compiler_params=pltpu.CompilerParams(vmem_limit_bytes=VMEM_BYTES),
        cost_estimate=SHORT,
        name="expert_backward_" + kind,
    )(info, *arrays, x, gain, shift, act, slope, incoming)


IN_VMEM = pl.BlockSpec(memory_space=pltpu.VMEM)
IN_SMEM = pl.BlockSpec(memory_space=pltpu.SMEM)


def shared_forward(rows, inputs, inner, outputs):
    count, width = rows[0].shape
    total = SECTIONS * count
    hidden = inner.shape[1]
    return pl.pallas_call(
        shared_forward_kernel,
        grid=(hidden // width,),
        in_specs=[pl.BlockSpec(rows[0].shape, lambda step: (0, 0))] * 4
        + [
            pl.BlockSpec((width, width), lambda step: (0, step)),
            pl.BlockSpec((1, width), lambda step: (0, step)),
            pl.BlockSpec((width, width), lambda step: (step, 0)),
        ],
        out_specs=pl.BlockSpec((SECTIONS, count, width), lambda step: (0, 0, 0)),
        scratch_shapes=[pltpu.VMEM((total, width), BF16), pltpu.VMEM((total, width), F32)],
        out_shape=jax.ShapeDtypeStruct((SECTIONS, count, width), BF16),
        compiler_params=pltpu.CompilerParams(vmem_limit_bytes=VMEM_BYTES),
        cost_estimate=SHORT,
        name="shared_forward",
    )(*rows, inputs, inner, outputs)


def shared_backward(rows, grads, info, weights, inner):
    arrays, plan = weights
    count, width = rows[0].shape
    total = SECTIONS * count
    travel = (2, width // 8, 4 * width)
    return pl.pallas_call(
        partial(shared_backward_kernel, plan, len(arrays)),
        in_specs=[IN_SMEM] + [ANYWHERE] * len(arrays) + [IN_VMEM] * 9,
        out_specs=[IN_VMEM] * 5,
        scratch_shapes=blocks_scratch(2, width)
        + [
            pltpu.VMEM((total, width), BF16),
            pltpu.VMEM((total, width), BF16),
            pltpu.VMEM((2, width, width), BF16),
        ],
        out_shape=[
            jax.ShapeDtypeStruct((SECTIONS, count, width), BF16),
            jax.ShapeDtypeStruct(travel, BF16),
            jax.ShapeDtypeStruct(travel, BF16),
            jax.ShapeDtypeStruct((1, width), F32),
            jax.ShapeDtypeStruct((1, width), F32),
        ],
        compiler_params=pltpu.CompilerParams(vmem_limit_bytes=VMEM_BYTES),
        cost_estimate=SHORT,
        name="shared_backward",
    )(info, *arrays, *rows, *grads, inner)


def plane_turn(plane, planes):
    return ((plane & 1) << 1) | (plane >> 1) if planes == 4 else 0


def finish_kernel(planes, info, scale_ref, mine_ref, theirs_ref, *refs):
    step = pl.program_id(0)
    count = mine_ref.shape[1]
    placed = refs[-1]
    outs = refs[:-1]
    width = placed.shape[1]
    half = width // 2
    at = info.shape[0] - 3
    section, core = info[at], info[at + 1]
    turn = plane_turn(info[at + 2], planes)
    turned = turn if count == 1 else jnp.where(section == 1, turn, 0)
    scale = scale_ref[0, 0]
    columns = pl.ds(pl.multiple_of((step ^ turned) * width, width), width)

    def place(which):
        def by_rows():
            for side, ref in enumerate((mine_ref, theirs_ref)):
                for away in range(SECTIONS):
                    for path in range(2):
                        row = (core ^ side) * half + path * (half // 2)
                        row = row + (section ^ away) * PIECE_ROWS
                        placed[pl.ds(pl.multiple_of(row, 16), PIECE_ROWS), :] = ref[
                            away, which, path * PIECE_ROWS : (path + 1) * PIECE_ROWS, columns
                        ].astype(F32)

        def by_columns():
            for side, ref in enumerate((mine_ref, theirs_ref)):
                for group in range(4):
                    quarter = half // 4
                    row = (core ^ side) * half + group * quarter
                    placed[pl.ds(pl.multiple_of(row, 16), quarter), :] = ref[
                        step, which, :, group * width : (group + 1) * width
                    ].astype(F32)

        if count == 1:
            by_rows()
        else:
            pl.when(section != 0)(by_rows)
            pl.when(section == 0)(by_columns)

    place(0)
    if count == 1:

        @pl.when(step < 3)
        def _():
            outs[0][0] = placed[...] / scale

        @pl.when(step == 3)
        def _():
            outs[1][0] = placed[...] / scale

    else:
        outs[0][0] = placed[...] / scale
        place(1)
        outs[1][0] = (placed[...] / scale).T


def finish(info, scale, mine, theirs, planes):
    count, hidden = mine.shape[1], mine.shape[3]
    width = hidden // 4
    if count == 1:
        shapes = [(1, width, 3 * width), (1, width, width)]
        maps = [lambda step, info: (0, 0, jnp.minimum(step, 2)), lambda step, info: (0, 0, 0)]
    else:
        shapes = [(1, width, hidden), (1, hidden, width)]
        maps = [lambda step, info: (0, 0, step), lambda step, info: (0, step, 0)]
    return pl.pallas_call(
        partial(finish_kernel, planes),
        grid_spec=pltpu.PrefetchScalarGridSpec(
            num_scalar_prefetch=1,
            grid=(4,),
            in_specs=[IN_SMEM, whole_block(mine.shape), whole_block(mine.shape)],
            out_specs=[pl.BlockSpec((1, width, width), at) for at in maps],
            scratch_shapes=[pltpu.VMEM((width, width), F32)],
        ),
        out_shape=[jax.ShapeDtypeStruct(shape, F32) for shape in shapes],
        compiler_params=pltpu.CompilerParams(vmem_limit_bytes=VMEM_BYTES),
        cost_estimate=SHORT,
        name="finish",
    )(info, scale, mine, theirs)


def pack_kernel(count, plan, info, *refs):
    sources, outs, sems = refs[:count], refs[count:-1], refs[-1]
    first = info.shape[0] - 3
    section, core, plane = info[first], info[first + 1], info[first + 2]
    half = outs[0].shape[1]
    for index, (out, choices) in enumerate(zip(outs, plan)):
        for at, at_plane, parts in choices:
            here = section == at
            if at_plane is not None:
                here = here & (plane == at_plane)

            @pl.when(here)
            def _(index=index, out=out, parts=parts):
                for block, part in enumerate(parts):
                    if part[0] == "own":
                        _, which, row, column = part
                        rows = pl.ds(pl.multiple_of(row + core * half, half), half)
                        source = sources[which].at[rows, pl.ds(column, out.shape[2])]
                    else:
                        source = sources[part[1]].at[block]
                    pltpu.make_async_copy(source, out.at[block], sems.at[index, block]).start()

    for index, out in enumerate(outs):
        for block in range(2):
            pltpu.make_async_copy(out.at[block], out.at[block], sems.at[index, block]).wait()


def pack(info, sources, plan, shape):
    return pl.pallas_call(
        partial(pack_kernel, len(sources), plan),
        in_specs=[IN_SMEM] + [ANYWHERE] * len(sources),
        out_specs=[ANYWHERE] * len(plan),
        scratch_shapes=[pltpu.SemaphoreType.DMA((len(plan), 2))],
        out_shape=[jax.ShapeDtypeStruct(shape, BF16)] * len(plan),
        cost_estimate=SHORT,
        name="pack",
    )(info, *sources)


def over_section(value, bits, sources=range(SECTIONS)):
    return lax.ppermute(value, "section", [(at, at ^ bits) for at in sources])


def over_core(value):
    return lax.ppermute(value, "core", [(0, 1), (1, 0)])


def over_plane(value, pairs):
    return lax.ppermute(value, "z", pairs)


def added(left, right):
    return (left.astype(F32) + right.astype(F32)).astype(BF16)


def after(value, *earlier):
    return lax.optimization_barrier((value,) + earlier)[0]


def by_section(section, values):
    result, last = None, None
    for at in sorted(values):
        if result is None:
            result = values[at]
        elif values[at] is not last:
            result = jnp.where(section >= at, values[at], result)
        last = values[at]
    return result


def total(*values):
    result = values[0].astype(F32)
    for value in values[1:]:
        result = result + value.astype(F32)
    return result.astype(BF16)


class Sums:
    def __init__(self, travel):
        self.stay, self.move, self.other_stay, self.other_move = travel
        self.size = self.stay.shape[1] // 2

    def cross(self, *earlier):
        if earlier:
            self.other_move = after(self.other_move, *earlier)
            self.other_stay = after(self.other_stay, *earlier)
        self.got_move, self.got_stay = over_core(self.other_move), over_core(self.other_stay)

    def first_sends(self):
        size = self.size
        self.sent = [
            total(self.move[:, at : at + size], self.got_move[:, at : at + size])
            for at in (0, size)
        ]
        return self.sent

    def second_sends(self, from_x, from_y):
        size, half = self.size, self.size // 2
        self.first = from_x, from_y
        to_y = total(self.stay[:, half:size], self.got_stay[:, half:size], from_x[:, half:])
        to_x = total(
            self.stay[:, size + half :], self.got_stay[:, size + half :], from_y[:, half:]
        )
        self.sent = [to_x, to_y]
        return self.sent

    def whole(self, from_x, from_y):
        size, half = self.size, self.size // 2
        parts = []
        for at, first, second in ((0, self.first[0], from_y), (size, self.first[1], from_x)):
            here = slice(at, at + half)
            parts.append(total(self.stay[:, here], self.got_stay[:, here], first[:, :half], second))
        return jnp.concatenate(parts, axis=1)


def over_links(sends):
    return [over_section(sends[0], 1), over_section(sends[1], 2)]


class Planes:
    def __init__(self, value, plane, planes):
        self.value, self.plane, self.planes, self.turn = value, plane, planes, 0

    def sends(self, *earlier):
        value = after(self.value, *earlier) if earlier else self.value
        if self.planes != 4:
            return (value,)
        bits = (1, 2, 2, 1)[self.turn]
        if self.turn < 2:
            bit = (self.plane & 1, self.plane >> 1)[self.turn]
            size = value.shape[-1] // 2
            value = lax.dynamic_slice_in_dim(value, (1 - bit) * size, size, value.ndim - 1)
        return (over_plane(value, [(at, at ^ bits) for at in range(4)]),)

    def take(self, arrived):
        if self.planes != 4:
            self.value = lax.psum(arrived, "z") if self.turn == 3 else arrived
        elif self.turn < 2:
            bit = (self.plane & 1, self.plane >> 1)[self.turn]
            size = self.value.shape[-1] // 2
            keep = lax.dynamic_slice_in_dim(self.value, bit * size, size, self.value.ndim - 1)
            self.value = added(keep, arrived)
        else:
            self.value = jnp.concatenate([self.value, arrived], axis=-1)
        self.turn += 1

    def in_order(self, value):
        if self.planes != 4:
            return value
        size, turn = value.shape[-1] // 4, plane_turn(self.plane, 4)
        parts = [
            lax.dynamic_slice_in_dim(value, (at ^ turn) * size, size, value.ndim - 1)
            for at in range(4)
        ]
        return jnp.concatenate(parts, axis=-1)


class Weights:
    def __init__(self, own, info, planes):
        self.own, self.info = own, info
        self.four = planes == 4
        self.plan = PLAN_FOUR if self.four else PLAN_ANY
        self.half, self.width = own[1].shape[0] // 2, own[1].shape[1]
        self.mine, self.theirs, self.arrived = {}, {}, {}

    def place(self, layer, block):
        if layer in "ac":
            return (0, 0, block * self.width) if block < 3 else (1, 0, 0)
        if layer == "g":
            return (2, 0, block * self.width) if block < 4 else (3, (block - 4) * self.width, 0)
        return (2, 0, block * self.width) if block < 4 else (3, (block - 4) * self.width, 0)

    def choices(self, sends, sources):
        result = []
        for at in range(SECTIONS):
            name = sends.get(at)
            if name is not None and HOMES[name[0]] != at:
                key = self.arrived[at, name]
                if key not in sources:
                    sources[key] = len(self.own) + len(sources)
                result.append((at, None, [("arrived", sources[key])] * 2))
                continue
            for plane in range(4) if name == "F" else (None,):
                piece = ("f" + str(plane)) if name == "F" else name or "a0"
                layer, index = piece[0], int(piece[1])
                if layer in "ac":
                    blocks = ATTEND_BLOCKS[index]
                else:
                    blocks = (index, 4 + index) if layer == "g" else EXPERT_BLOCKS[index]
                parts = [("own",) + self.place(layer, block) for block in blocks]
                result.append((at, plane, parts))
        return result

    def packed(self, wanted, *earlier):
        sources = {}
        plan = [self.choices(sends, sources) for sends in wanted]
        info = after(self.info, *earlier) if earlier else self.info
        arrays = list(self.own) + [self.mine[key] for key in sources]
        return pack(info, arrays, plan, (2, self.half, self.width))

    def run_step(self, step, *earlier):
        links = [(link, sends) for link, sends in enumerate(self.plan[step]) if sends]
        payloads = self.packed([sends for _, sends in links], *earlier)
        for (link, sends), payload in zip(links, payloads):
            self.mine[step, link] = over_section(payload, link + 1, sorted(sends))
        for link, sends in links:
            for at, name in sends.items():
                self.arrived[at ^ (link + 1), name] = (step, link)
        return payloads

    def run_planes(self, step, *earlier):
        if not self.four:
            return ()
        if step == 1:
            self.mine["plane", 0] = self.packed([{at: "F" for at in range(SECTIONS)}], *earlier)[0]
            earlier = ()
        up, down = self.mine["plane", step - 1], self.mine["plane", 1 - step]
        if earlier:
            up, down = after(up, *earlier), after(down, *earlier)
        up = over_plane(up, [(at, at + 1) for at in range(step - 1, 3)])
        down = over_plane(down, [(at, at - 1) for at in range(4 - step, 0, -1)])
        self.mine["plane", step], self.mine["plane", -step] = up, down
        return up, down

    def hand_over(self, steps, *earlier):
        for key in [key for key in self.mine if key[0] in steps and key not in self.theirs]:
            mine = after(self.mine[key], *earlier) if earlier else self.mine[key]
            self.theirs[key] = over_core(mine)
        return [self.theirs[key] for key in self.theirs if key[0] in steps]

    def set_mine(self, keys, values):
        for key, value in zip(keys, values):
            self.mine[key] = value

    def layer(self, layer):
        arrays, places = list(self.own), {}

        def place(key):
            if key not in self.theirs:
                self.theirs[key] = over_core(self.mine[key])
            if key not in places:
                places[key] = len(arrays)
                arrays.extend([self.mine[key], self.theirs[key]])
            return places[key], places[key] + 1

        if layer in "ac":
            names = [(layer + str(index), ATTEND_BLOCKS[index]) for index in range(2)]
        else:
            names = [(layer + str(index), EXPERT_BLOCKS[index]) for index in range(4)]
        plan = []
        for at in range(SECTIONS):
            if layer == "g":
                names = [("g" + str(at), (0, 1))]
            if HOMES[layer] == at:
                steps = []
                for name, blocks in names:
                    for block in blocks:
                        source = block * 4 if layer == "g" else block
                        steps.append((block, ("own",) + self.place(layer, source)))
                plan.append((at, None, steps))
                continue
            by_plane = layer == "f" and self.four
            for plane in range(4) if by_plane else (None,):
                steps = []
                for index, (name, blocks) in enumerate(names):
                    key = ("plane", plane - index) if by_plane else self.arrived[at, name]
                    for which, block in enumerate(blocks):
                        steps.append((block, ("piece",) + place(key) + (which,)))
                plan.append((at, plane, steps))
        return arrays, plan


def per_device(
    tokens,
    caption_lengths,
    attend_gain,
    attend_shift,
    attend_inputs,
    attend_bias,
    attend_output,
    expert_gain,
    expert_shift,
    expert_inputs,
    expert_inner_bias,
    expert_outputs,
    expert_outer_bias,
    cotangent,
):
    section, core, plane = lax.axis_index("section"), lax.axis_index("core"), lax.axis_index("z")
    planes = lax.axis_size("z")
    items, positions, width = tokens.shape
    hidden = expert_inputs.shape[-1]
    info = [value.reshape(1).astype(jnp.int32) for value in (section, core, plane)]
    info = jnp.concatenate([caption_lengths] + info)
    weights = Weights(
        (attend_inputs[0], attend_output[0], expert_inputs[0], expert_outputs[0]), info, planes
    )

    def to_sections(value):
        return [value] + [over_section(value, bits) for bits in (1, 2, 3)]

    def items_of(part):
        return part.reshape(items, CAP_ROWS, width)

    def under(outputs, *arrivals):
        joined = lax.optimization_barrier(tuple(outputs) + arrivals)
        return joined[: len(outputs)], joined[len(outputs) :]

    weights.run_step(0)
    pad = ((0, 0), (0, ROWS - positions), (0, 0))
    x0 = jnp.pad(tokens, pad)
    last_grad = jnp.pad(cotangent, pad)
    rows = jnp.concatenate(
        [
            attend_gain,
            attend_shift,
            attend_bias,
            expert_gain,
            expert_shift,
            expert_inner_bias,
            expert_outer_bias,
            jnp.full((1, 128), jnp.sum(caption_lengths), F32),
        ],
        axis=1,
    )
    rows = jnp.concatenate(to_sections(rows), axis=0)
    language_count = jnp.sum(rows[:, -128:], axis=0, keepdims=True)
    language_count = language_count + over_core(language_count)
    if planes == 4:
        language_count = language_count + over_plane(language_count, [(at, at ^ 1) for at in range(4)])
        language_count = language_count + over_plane(language_count, [(at, at ^ 2) for at in range(4)])
    else:
        language_count = lax.psum(language_count, "z")
    language_count = language_count[0, 0].astype(jnp.int32)
    vision_count = PATCHES * items * SECTIONS * 2 * planes
    counts = jnp.stack(
        [jnp.full((), vision_count, jnp.int32), language_count, language_count + vision_count]
    )
    rows = [lax.dynamic_index_in_dim(rows, at ^ section, 0) for at in range(SECTIONS)]
    sizes = [width, width, 3 * width, width, width, hidden, width]
    ends = [sum(sizes[: at + 1]) for at in range(len(sizes))]

    def row(slot, which):
        return rows[slot][:, ends[which] - sizes[which] : ends[which]]

    used = [(0, 0), (0, 1), (0, 2), (0, 3), (0, 4), (0, 5), (1, 3), (1, 4), (1, 5), (1, 6)]
    used += [(0, 6), (2, 0), (2, 1), (2, 2), (3, 3), (3, 4), (3, 5), (3, 6)]
    kept = lax.optimization_barrier(tuple(row(*at) for at in used) + (x0, last_grad, counts))
    x0, last_grad, counts = kept[-3:]
    kept = dict(zip(used, kept))

    def row(slot, which):
        return kept[slot, which]

    weights.run_step(1)
    weights.hand_over((0,))
    sent = weights.run_step(2, *kept.values(), x0, last_grad, counts)
    weights.hand_over((1,), *sent)
    info = after(info, *weights.hand_over((0, 1)))
    attend0 = weights.layer("a")
    y0, qkv0, mixed0, caption_rows = attend_forward(
        x0, info, attend0, row(0, 0), row(0, 1), row(0, 2), following=(row(0, 3), row(0, 4))
    )
    caption_rows = to_sections(caption_rows.reshape(-1, width))
    weights.run_step(EARLY_STEPS, *caption_rows[1:], *weights.hand_over((2,), caption_rows[0]))
    planes_moved = weights.run_planes(1, *caption_rows[1:])
    late_keys = [key for key in weights.mine if key[0] == EARLY_STEPS]
    outputs = shared_forward(caption_rows, expert_inputs[0], expert_inner_bias, expert_outputs[0])
    if weights.four:
        late_keys += [("plane", 1), ("plane", -1)]
    (part,), moved = under([outputs], *[weights.mine[key] for key in late_keys])
    weights.set_mine(late_keys, moved)
    branch = {at: over_section(part[at], at, [0]) for at in range(1, SECTIONS)}
    branch[0] = part[0]
    weights.run_planes(2, part)
    expert1 = weights.layer("e")
    outputs = expert_forward(
        y0, info, expert1, row(1, 3), row(1, 4), row(1, 5), row(1, 6), PATCH_ROWS, "patch"
    )
    if weights.four:
        last_moved = [("plane", 2), ("plane", -2)]
    else:
        last_moved = []
        for step in range(EARLY_STEPS + 1, len(weights.plan)):
            weights.run_step(step, part)
    (x2, act1, slope1), moved = under(outputs, *[weights.mine[key] for key in last_moved])
    weights.set_mine(last_moved, moved)
    branch = items_of(by_section(section, branch))
    attend2 = weights.layer("c")
    weights.run_planes(3, x2)
    outputs = attend_forward(
        x2, info, attend2, row(2, 0), row(2, 1), row(2, 2), merge=(y0, branch, row(0, 6))
    )
    last_moved = [("plane", 3), ("plane", -3)] if weights.four else []
    (x3, qkv2, mixed2, x2), moved = under(outputs, *[weights.mine[key] for key in last_moved])
    weights.set_mine(last_moved, moved)
    expert3 = weights.layer("f")
    layer_output, act3, slope3 = expert_forward(
        x3, info, expert3, row(3, 3), row(3, 4), row(3, 5), row(3, 6), ROWS, "all"
    )

    def to_home(sums):
        got = [by_section(section, sums)]
        for bits in (1, 2, 3):
            sends = {at ^ bits: sums[at] for at in sums}
            got.append(over_section(by_section(section, sends), bits, sorted(sends)))
        return got

    last_moved = []
    if weights.four:
        weights.run_step(EARLY_STEPS + 1, x3)
        last_moved = [key for key in weights.mine if key[0] == EARLY_STEPS + 1]
    outputs = expert_backward(
        x3, info, expert3, row(3, 3), row(3, 4), act3, slope3, last_grad, ROWS, "all"
    )
    outputs, moved = under(outputs, *[weights.mine[key] for key in last_moved])
    weights.set_mine(last_moved, moved)
    handed = weights.hand_over((EARLY_STEPS + 1,)) if weights.four else []
    grad3, *small3 = outputs[:5]
    sums3 = Sums(outputs[5:])
    sums3.cross()
    moved = over_links(sums3.first_sends())
    grad3 = after(grad3, *sums3.sent)
    outputs = attend_backward(
        x2, info, attend2, row(2, 0), row(2, 1), qkv2, mixed2, grad3
    )
    outputs, moved = under(outputs, *moved, sums3.got_stay, *handed)
    grad2, *small2 = outputs[:4]
    sums2, caption_grad = Sums(outputs[4:8]), outputs[8]
    caption_grads = to_sections(caption_grad.reshape(-1, width))
    sums3.got_stay = moved[2]
    moved3 = over_links(sums3.second_sends(*moved[:2]))
    grad2 = after(grad2, *sums3.sent)
    outputs = expert_backward(
        y0, info, expert1, row(1, 3), row(1, 4), act1, slope1, grad2, PATCH_ROWS, "patch"
    )
    outputs, caption_grads = under(outputs, *caption_grads)
    grad1, *small1 = outputs[:5]
    sums2.cross(grad1)
    sums1 = Sums(outputs[5:])
    sums1.cross()
    inner_quarter = lax.dynamic_slice(row(0, 5), (0, section * width), (1, width))
    inner_quarter = after(inner_quarter, grad1)
    outputs = shared_backward(
        caption_rows, caption_grads, info, weights.layer("g"), inner_quarter
    )
    outputs, moved3 = under(outputs, *moved3)
    parts, keep0, send0, inner_grad, outer_grad = outputs
    parts = [parts[0]] + [over_section(parts[bits], bits) for bits in (1, 2, 3)]
    keep0 = added(keep0, over_core(send0))
    early = lax.psum(jnp.concatenate([sums3.whole(*moved3), keep0], axis=0), "z")
    sends = sums2.first_sends() + sums1.first_sends()
    sends = [after(value, *parts[1:]) for value in sends]
    moved2, moved1 = over_links(sends[:2]), over_links(sends[2:])
    grad1 = after(grad1, keep0, *sends)
    outputs = attend_backward(
        x0,
        info,
        attend0,
        row(0, 0),
        row(0, 1),
        qkv0,
        mixed0,
        grad1,
        first=(y0, row(0, 3), [items_of(value) for value in parts]),
    )
    outputs, moved2 = under(outputs, *moved2)
    tokens_grad, *small_first = outputs[:4]
    sums_first, gain_grad, shift_grad = Sums(outputs[4:8]), outputs[8], outputs[9]
    sums_first.cross()
    moved2 = over_links(sums2.second_sends(*moved2))
    moved1 = over_links(sums1.second_sends(*moved1))
    sends = [after(value, *sums1.sent) for value in sums_first.first_sends()]
    moved = over_links(sends)
    planes1 = Planes(sums1.whole(*moved1), plane, planes)
    planes1.take(*planes1.sends(*sends))
    sums_first.got_stay = after(sums_first.got_stay, planes1.value)
    moved = over_links(sums_first.second_sends(*moved))
    planes1.take(*planes1.sends(*sums_first.sent))
    last, sum2 = sums_first.whole(*moved), sums2.whole(*moved2)
    inner_grad = lax.dynamic_update_slice(
        jnp.zeros((1, hidden), F32), inner_grad, (0, section * width)
    )
    small0 = [gain_grad, shift_grad, inner_grad, outer_grad]
    small = jnp.concatenate(small_first + small2 + small0 + small1 + small3, axis=1)
    small_rows = 8
    small = jnp.pad(small, ((0, 0), (0, small_rows * hidden - small.shape[1])))
    small = small.reshape(small_rows, hidden)
    small = small + over_core(small)
    small = sum(to_sections(small))
    planes_last = Planes(
        jnp.concatenate([last[0], sum2[0], small.astype(BF16)], axis=0), plane, planes
    )
    planes_last.take(*planes_last.sends(planes1.value))
    planes1.take(*planes1.sends(planes_last.value))
    home_early = to_home({0: after(early[2:], planes1.value), 3: after(early[:2], planes1.value)})
    planes_last.take(*planes_last.sends(planes1.value))
    planes1.take(*planes1.sends(planes_last.value))
    home_late = to_home({1: after(planes1.value, *home_early[1:3])})
    planes_last.take(*planes_last.sends(planes1.value))
    planes_last.take(*planes_last.sends())
    eighth = last.shape[1]
    last = after(planes_last.value, home_early[3])
    home_attend = to_home({0: last[None, :eighth], 2: last[None, eighth : 2 * eighth]})
    small = planes_last.in_order(last[2 * eighth :].astype(F32))

    as_float = counts.astype(F32)
    one = jnp.ones((), F32)
    attend_scales = jnp.stack([as_float[2], one, as_float[2], one])
    expert_scales = jnp.stack([as_float[1], as_float[0], one, as_float[2]])

    def placed(pieces, scales):
        scale = lax.dynamic_index_in_dim(scales, section, 0).reshape(1, 1)
        pieces = jnp.stack(pieces)
        return finish(info, scale, pieces, over_core(pieces), planes)

    blank = jnp.zeros_like(home_late[0])
    inputs_whole, outputs_whole = placed(
        [
            by_section(section, {0: early, 1: late, 2: blank, 3: early})
            for early, late in zip(home_early, home_late)
        ],
        expert_scales,
    )
    blank = jnp.zeros_like(home_attend[0])
    attend_whole, output_whole = placed(
        [by_section(section, {0: got, 1: blank, 2: got, 3: blank}) for got in home_attend],
        attend_scales,
    )

    small = small.reshape(-1)
    attend_size, expert_size = 5 * width, 3 * width + hidden
    cuts = [attend_size, 2 * attend_size]
    cuts += [cuts[1] + expert_size, cuts[1] + 2 * expert_size, cuts[1] + 3 * expert_size]
    small = jnp.split(small, cuts)
    none_attend, none_expert = jnp.zeros_like(small[0]), jnp.zeros_like(small[2])
    attend_small = jnp.stack([small[0], none_attend, small[1], none_attend])
    expert_small = jnp.stack([small[2], small[3], none_expert, small[4]])
    attend_small = attend_small / attend_scales.reshape(-1, 1)
    expert_small = expert_small / expert_scales.reshape(-1, 1)
    attend_small = lax.dynamic_index_in_dim(attend_small, section, 0)
    expert_small = lax.dynamic_index_in_dim(expert_small, section, 0)
    return (
        layer_output[:, :positions],
        tokens_grad[:, :positions],
        attend_small[:, :width],
        attend_small[:, width : 2 * width],
        attend_whole,
        attend_small[:, 2 * width :],
        output_whole,
        expert_small[:, :width],
        expert_small[:, width : 2 * width],
        inputs_whole,
        expert_small[:, 2 * width : 2 * width + hidden],
        outputs_whole,
        expert_small[:, 2 * width + hidden :],
        counts,
    )


def solution(mesh):
    sections, groups = mesh.shape["section"], mesh.shape["dp"]
    split = Mesh(mesh.devices.reshape(sections, groups // 2, 2), ("section", "z", "core"))
    items = P(("section", "z", "core"), None, None)
    flat = P("section", None)
    matrix = P("section", None, None)
    placed = (
        items,
        P(("section", "z", "core")),
        flat,
        flat,
        matrix,
        flat,
        matrix,
        flat,
        flat,
        matrix,
        flat,
        matrix,
        flat,
        items,
    )
    return jax.shard_map(
        per_device,
        mesh=split,
        in_specs=placed,
        out_specs=(
            items,
            items,
            flat,
            flat,
            matrix,
            flat,
            matrix,
            flat,
            flat,
            matrix,
            flat,
            matrix,
            flat,
            P(),
        ),
        check_vma=False,
    )
```

```python
from functools import partial

import jax
import jax.numpy as jnp
from jax import lax
from jax.experimental import pallas as pl
from jax.experimental.pallas import tpu as pltpu
from jax.sharding import Mesh
from jax.sharding import PartitionSpec as P

HEADS = 12
HEAD_DIM = 64
PATCHES = 197
ROWS = 256
CAP_FIRST, CAP_ROWS = 192, 48
PATCH_ROWS = 208
PAIR = 2 * HEAD_DIM
SECTIONS = 4
PIECE_ROWS = 48
VMEM_BYTES = 58 * 1024 * 1024
F32 = jnp.float32
BF16 = jnp.bfloat16

PLAN_FOUR = (
    ({0: "a0", 1: "e0", 2: "c0", 3: "F"}, {0: "a1", 1: "e2", 2: "c0", 3: "F"}),
    ({0: "a1", 1: "e1", 2: "a1", 3: "e2"}, {0: "a0", 1: "a0", 2: "F", 3: "c0"}),
    ({0: "g3", 1: "e2", 2: "c1"}, {0: "e0", 1: "e3", 2: "c1"}),
    ({0: "g1", 1: "e3", 2: "e0", 3: "e3"}, {0: "e1", 1: "e1", 3: "c1"}),
    ({}, {0: "g2", 1: "g3"}),
)
PLAN_ANY = (
    ({0: "a0", 1: "e0", 2: "c0", 3: "f0"}, {0: "a1", 1: "e2", 2: "c0", 3: "f0"}),
    ({0: "a1", 1: "e1", 2: "a1", 3: "e2"}, {0: "a0", 1: "a0", 2: "c1", 3: "f1"}),
    ({0: "g3", 1: "e2", 2: "c1", 3: "f1"}, {0: "e0", 1: "e3", 2: "f0", 3: "f2"}),
    ({0: "g1", 1: "e3", 2: "e0", 3: "e3"}, {0: "e1", 1: "e1", 2: "f1", 3: "f3"}),
    ({0: "c1", 1: "f2", 3: "f2"}, {0: "g2", 1: "g3", 3: "c0"}),
    ({1: "f3", 3: "f3"}, {}),
)
EARLY_STEPS = 3
HOMES = {"a": 0, "c": 2, "e": 1, "f": 3, "F": 3, "g": 0}
ATTEND_BLOCKS = ((0, 1), (2, 3))
EXPERT_BLOCKS = ((0, 1), (4, 5), (2, 3), (6, 7))


def dot_plain(left, right):
    return jnp.dot(left, right, preferred_element_type=F32)


def dot_last(left, right):
    return lax.dot_general(left, right, (((1,), (1,)), ((), ())), preferred_element_type=F32)


def dot_first(left, right):
    return lax.dot_general(left, right, (((0,), (0,)), ((), ())), preferred_element_type=F32)


def column_sum(matrix):
    return jnp.sum(matrix.astype(F32), axis=0, keepdims=True)


def norm_parts(rows):
    centre = rows - jnp.mean(rows, axis=-1, keepdims=True)
    scale = lax.rsqrt(jnp.mean(centre * centre, axis=-1, keepdims=True) + 1e-06)
    return centre * scale, scale


def norm_back(normed_grad, unit, scale, gain):
    unit_grad = normed_grad * gain
    along = jnp.mean(unit_grad * unit, axis=-1, keepdims=True)
    return scale * (unit_grad - jnp.mean(unit_grad, axis=-1, keepdims=True) - unit * along)


def true_positions(length, first, count, axis, kind):
    shape = (count, 1) if axis == 0 else (1, count)
    position = first + lax.broadcasted_iota(jnp.int32, shape, axis)
    patch = position < PATCHES
    if kind == "patch":
        return patch
    caption = (position >= PATCHES) & (position - PATCHES < length)
    return caption if kind == "caption" else patch | caption


def head_masks():
    lane = lax.broadcasted_iota(jnp.int32, (1, PAIR), 1)
    even = (lane < HEAD_DIM).astype(F32).astype(BF16)
    odd = (lane >= HEAD_DIM).astype(F32).astype(BF16)
    return lane < HEAD_DIM, even, odd


def split_pair(pair, even, odd):
    return jnp.concatenate([pair * even, pair * odd], axis=0)


def start_weights(info, first, refs, plan, blocks, sems):
    half = blocks.shape[1] // 2
    section, core, plane = info[first], info[first + 1], info[first + 2]
    for at, at_plane, steps in plan:
        here = section == at
        if at_plane is not None:
            here = here & (plane == at_plane)

        @pl.when(here)
        def _(steps=steps):
            for block, source in steps:
                if source[0] == "own":
                    _, which, row, column = source
                    width = blocks.shape[2]
                    for part in range(2):
                        pltpu.make_async_copy(
                            refs[which].at[
                                pl.ds(row + part * half, half), pl.ds(column, width)
                            ],
                            blocks.at[block, pl.ds(part * half, half)],
                            sems.at[block],
                        ).start()
                else:
                    _, mine, theirs, index = source
                    pltpu.make_async_copy(
                        refs[mine].at[index],
                        blocks.at[block, pl.ds(pl.multiple_of(core * half, half), half)],
                        sems.at[block],
                    ).start()
                    pltpu.make_async_copy(
                        refs[theirs].at[index],
                        blocks.at[block, pl.ds(pl.multiple_of((1 - core) * half, half), half)],
                        sems.at[block],
                    ).start()


def wait_block(blocks, block, sems):
    pltpu.make_async_copy(blocks.at[block], blocks.at[block], sems.at[block]).wait()


def store_turned(target, turned, columns, section, core):
    half = target.shape[0] // 2
    for piece in range(16):
        path, owner = (piece >> 2) & 1, piece & 3
        away = owner ^ section
        place = ((away & 1) << 1) | (away >> 1) if path == 0 else away
        row = ((piece >> 3) ^ core) * half + (place >> 1) * (half // 2)
        row = row + path * (half // 4) + (place & 1) * PIECE_ROWS
        target[pl.ds(pl.multiple_of(row, 16), PIECE_ROWS), columns] = turned[
            piece * PIECE_ROWS : (piece + 1) * PIECE_ROWS
        ]


def put_travel(refs, which, columns, left, right):
    half = left.shape[0] // 2
    for side in range(2):
        rows = dot_plain(left[side * half : (side + 1) * half], right).astype(BF16)
        refs[2 * side][which, :, columns] = rows[: half // 2]
        refs[2 * side + 1][which, :, columns] = rows[half // 2 :]


def attend_forward_kernel(plan, weight_count, merge, info, *refs):
    weights, refs = refs[:weight_count], refs[weight_count:]
    if merge:
        x_ref, before_ref, part_ref, outer_ref, gain_ref, shift_ref, bias_ref = refs[:7]
        y_ref, qkv_ref, mixed_ref, joined_ref, blocks, sems, joined = refs[7:]
    else:
        x_ref, gain_ref, shift_ref, bias_ref, next_gain_ref, next_shift_ref = refs[:6]
        y_ref, qkv_ref, mixed_ref, caption_ref, blocks, sems = refs[6:]
    item = pl.program_id(0)
    items = pl.num_programs(0)
    length = info[item]
    width = x_ref.shape[-1]

    @pl.when(item == 0)
    def _():
        start_weights(info, items, weights, plan, blocks, sems)

    cap = slice(CAP_FIRST, CAP_FIRST + CAP_ROWS)
    if merge:
        joined[...] = x_ref[0].astype(F32)
        branch = part_ref[0].astype(F32) + outer_ref[...]
        is_true = true_positions(length, CAP_FIRST, CAP_ROWS, 0, "caption")
        captions = before_ref[0, cap] + jnp.where(is_true, branch, 0.0)
        position = CAP_FIRST + lax.broadcasted_iota(jnp.int32, (CAP_ROWS, 1), 0)
        captions = captions.astype(BF16).astype(F32)
        joined[cap] = jnp.where(position < PATCHES, joined[cap], captions)
        x = joined[...]
        joined_ref[0] = x.astype(BF16)
    else:
        x = x_ref[0].astype(F32)
    unit, _ = norm_parts(x)
    normed = (unit * gain_ref[...] + shift_ref[...]).astype(BF16)

    @pl.when(item == 0)
    def _():
        for block in range(4):
            wait_block(blocks, block, sems)

    queries = dot_plain(normed, blocks[0]) + bias_ref[:, :width]
    qkv_ref[0, :, :width] = (queries * HEAD_DIM ** (-0.5)).astype(BF16)
    qkv_ref[0, :, width : 2 * width] = dot_plain(normed, blocks[1]).astype(BF16)
    values = dot_plain(normed, blocks[2]) + bias_ref[:, width : 2 * width]
    qkv_ref[0, :, 2 * width :] = values.astype(BF16)
    key_true = true_positions(length, 0, ROWS, 1, "all")
    low_half, even, odd = head_masks()
    ones = jnp.ones((ROWS, PAIR), BF16)

    def scores_of(pair):
        at = pair * PAIR
        q2 = qkv_ref[0, :, at : at + PAIR]
        k2 = qkv_ref[0, :, width + at : width + at + PAIR]
        return dot_last(split_pair(q2, even, odd), k2)

    ahead = [scores_of(0), scores_of(1)]
    for pair in range(HEADS // 2):
        at = pair * PAIR
        scores = jnp.where(key_true, ahead.pop(0), -1e9)
        if pair + 2 < HEADS // 2:
            ahead.append(scores_of(pair + 2))
        weight = jnp.exp(scores - jnp.max(scores, axis=-1, keepdims=True)).astype(BF16)
        v2 = qkv_ref[0, :, 2 * width + at : 2 * width + at + PAIR]
        summed = dot_plain(weight, jnp.concatenate([v2, ones], axis=1))
        top = jnp.where(low_half, summed[:ROWS, :PAIR], summed[ROWS:, :PAIR])
        below = jnp.where(low_half, summed[:ROWS, PAIR:], summed[ROWS:, PAIR:])
        mixed_ref[0, :, at : at + PAIR] = (top / below).astype(BF16)
    branch = dot_plain(mixed_ref[0], blocks[3]) + bias_ref[:, 2 * width :]
    row_true = true_positions(length, 0, ROWS, 0, "all")
    y = x + jnp.where(row_true, branch, 0.0)
    y_ref[0] = y.astype(y_ref.dtype)
    if not merge:
        unit, _ = norm_parts(y[cap])
        caption_ref[0] = (unit * next_gain_ref[...] + next_shift_ref[...]).astype(BF16)


def attend_backward_kernel(plan, weight_count, first, info, *refs):
    weights, refs = refs[:weight_count], refs[weight_count:]
    x_ref, gain_ref, shift_ref, qkv_ref, mixed_ref, grad_ref = refs[:6]
    if first:
        after_ref, next_gain_ref, *parts = refs[6:12]
        refs = refs[12:]
    else:
        refs = refs[6:]
    out_ref, gain_grad_ref, shift_grad_ref, bias_grad_ref = refs[:4]
    travel_refs = refs[4:8]
    if first:
        next_gain_grad_ref, next_shift_grad_ref, joined = refs[8], refs[9], refs[-1]
    else:
        caption_ref = refs[8]
    blocks, sems, normed_turned, mixed_turned, branch_all, projected, mixed_grad = refs[
        10 if first else 9 :
    ][:7]
    item = pl.program_id(0)
    items = pl.num_programs(0)
    length = info[item]
    section, core = info[items], info[items + 1]
    width = x_ref.shape[-1]
    here = pl.ds(pl.multiple_of(item * ROWS, ROWS), ROWS)
    cap = slice(CAP_FIRST, CAP_FIRST + CAP_ROWS)

    @pl.when(item == 0)
    def _():
        start_weights(info, items, weights, plan, blocks, sems)

    def add_to(ref, part):
        @pl.when(item == 0)
        def _():
            ref[...] = part

        @pl.when(item > 0)
        def _():
            ref[...] += part

    x = x_ref[0].astype(F32)
    unit, scale = norm_parts(x)
    normed = (unit * gain_ref[...] + shift_ref[...]).astype(BF16)
    incoming = grad_ref[0].astype(F32)
    if first:
        after_unit, after_scale = norm_parts(after_ref[0, cap])
        caption_grad = parts[0][0].astype(F32)
        for part in parts[1:]:
            caption_grad = caption_grad + part[0].astype(F32)
        joined[...] = incoming
        joined[cap] += norm_back(caption_grad, after_unit, after_scale, next_gain_ref[...])
        incoming = joined[...]
        add_to(next_gain_grad_ref, jnp.sum(caption_grad * after_unit, axis=0, keepdims=True))
        add_to(next_shift_grad_ref, jnp.sum(caption_grad, axis=0, keepdims=True))
    row_true = true_positions(length, 0, ROWS, 0, "all")
    branch = jnp.where(row_true, incoming, 0.0).astype(BF16)
    branch_all[here, :] = branch
    store_turned(normed_turned, normed.T, here, section, core)
    store_turned(mixed_turned, mixed_ref[0].T, here, section, core)

    @pl.when(item == 0)
    def _():
        for block in range(4):
            wait_block(blocks, block, sems)

    mixed_grad[...] = dot_last(branch, blocks[3]).astype(BF16)
    key_true = true_positions(length, 0, ROWS, 0, "all")
    _, even, odd = head_masks()

    def products_of(pair):
        at = pair * PAIR
        q2 = split_pair(qkv_ref[0, :, at : at + PAIR], even, odd)
        k2 = qkv_ref[0, :, width + at : width + at + PAIR]
        v2 = qkv_ref[0, :, 2 * width + at : 2 * width + at + PAIR]
        g2 = split_pair(mixed_grad[:, at : at + PAIR], even, odd)
        return q2, k2, g2, dot_last(k2, q2), dot_last(v2, g2)

    ahead = [products_of(0)]
    for pair in range(HEADS // 2):
        at = pair * PAIR
        q2, k2, g2, scores, weight_grad = ahead.pop(0)
        if pair + 1 < HEADS // 2:
            ahead.append(products_of(pair + 1))
        scores = jnp.where(key_true, scores, -1e9)
        weight = jnp.exp(scores - jnp.max(scores, axis=0, keepdims=True))
        weight = weight * (1.0 / jnp.sum(weight, axis=0, keepdims=True))
        product = weight * weight_grad
        along = jnp.sum(product, axis=0, keepdims=True)
        score_grad = (product - weight * along).astype(BF16)
        values_grad = dot_plain(weight.astype(BF16), g2).astype(BF16)
        keys_grad = dot_plain(score_grad, q2).astype(BF16)
        k2_split = split_pair(k2, even, odd)
        stacked = jnp.concatenate([score_grad[:, :ROWS], score_grad[:, ROWS:]], axis=0)
        queries_grad = dot_first(stacked, k2_split).astype(BF16)
        queries_grad = (queries_grad.astype(F32) * HEAD_DIM ** (-0.5)).astype(BF16)
        projected[here, at : at + PAIR] = queries_grad
        projected[here, width + at : width + at + PAIR] = keys_grad
        projected[here, 2 * width + at : 2 * width + at + PAIR] = values_grad
    normed_grad = dot_last(projected[here, :width], blocks[0])
    normed_grad += dot_last(projected[here, width : 2 * width], blocks[1])
    normed_grad += dot_last(projected[here, 2 * width :], blocks[2])
    out = (incoming + norm_back(normed_grad, unit, scale, gain_ref[...])).astype(BF16)
    out_ref[0] = out
    if not first:
        is_true = true_positions(length, CAP_FIRST, CAP_ROWS, 0, "caption")
        caption_ref[0] = jnp.where(is_true, out[cap].astype(F32), 0.0).astype(BF16)
    add_to(gain_grad_ref, jnp.sum(normed_grad * unit, axis=0, keepdims=True))
    add_to(shift_grad_ref, jnp.sum(normed_grad, axis=0, keepdims=True))

    @pl.when(item == items - 1)
    def _():
        for block in range(4):
            columns = slice(block * width, (block + 1) * width)
            left = normed_turned if block < 3 else mixed_turned
            right = projected[:, columns] if block < 3 else branch_all[...]
            put_travel(travel_refs, 0, columns, left, right)
        bias_grad_ref[:, :width] = column_sum(projected[:, :width])
        bias_grad_ref[:, width : 2 * width] = column_sum(projected[:, 2 * width :])
        bias_grad_ref[:, 2 * width :] = column_sum(branch_all[...])


SHORT = pl.CostEstimate(flops=0, bytes_accessed=100_000, transcendentals=0)
LONG = pl.CostEstimate(flops=30_000_000_000, bytes_accessed=30_000_000, transcendentals=0)
ANYWHERE = pl.BlockSpec(memory_space=pl.ANY)


def whole_block(shape):
    return pl.BlockSpec(shape, lambda step, info: (0,) * len(shape))


def item_block(shape):
    return pl.BlockSpec((1,) + shape[1:], lambda step, info: (step,) + (0,) * (len(shape) - 1))


def blocks_scratch(count, width):
    return [pltpu.VMEM((count, width, width), BF16), pltpu.SemaphoreType.DMA((count,))]


def attend_forward(x, info, weights, gain, shift, bias, merge=None, following=None):
    arrays, plan = weights
    items, _, width = x.shape
    row = whole_block((1, width))
    bias_row = whole_block((1, 3 * width))
    caption_shape = (items, CAP_ROWS, width)
    if merge is not None:
        before, part, outer = merge
        operands = (x, before, part, outer, gain, shift, bias)
        specs = [item_block(x.shape), item_block(x.shape), item_block(caption_shape)]
        specs += [row, row, row, bias_row]
        last_shape, kind, scratch = x.shape, BF16, [pltpu.VMEM((ROWS, width), F32)]
    else:
        operands = (x, gain, shift, bias, *following)
        specs = [item_block(x.shape), row, row, bias_row, row, row]
        last_shape, kind, scratch = caption_shape, F32, []
    return pl.pallas_call(
        partial(attend_forward_kernel, plan, len(arrays), merge is not None),
        grid_spec=pltpu.PrefetchScalarGridSpec(
            num_scalar_prefetch=1,
            grid=(items,),
            in_specs=[ANYWHERE] * len(arrays) + specs,
            out_specs=[
                item_block(x.shape),
                item_block((items, ROWS, 3 * width)),
                item_block((items, ROWS, width)),
                item_block(last_shape),
            ],
            scratch_shapes=blocks_scratch(4, width) + scratch,
        ),
        out_shape=[
            jax.ShapeDtypeStruct(x.shape, kind),
            jax.ShapeDtypeStruct((items, ROWS, 3 * width), BF16),
            jax.ShapeDtypeStruct((items, ROWS, width), BF16),
            jax.ShapeDtypeStruct(last_shape, BF16),
        ],
        compiler_params=pltpu.CompilerParams(vmem_limit_bytes=VMEM_BYTES),
        cost_estimate=SHORT,
        name="attend_forward",
    )(info, *arrays, *operands)


def attend_backward(x, info, weights, gain, shift, qkv, mixed, incoming, first=None):
    arrays, plan = weights
    items, _, width = x.shape
    half = width // 2
    row = whole_block((1, width))
    caption_shape = (items, CAP_ROWS, width)
    operands = (x, gain, shift, qkv, mixed, incoming)
    specs = [item_block(x.shape), row, row, item_block(qkv.shape), item_block(mixed.shape)]
    specs += [item_block(incoming.shape)]
    outs = [
        (item_block(x.shape), x.shape, BF16),
        (row, (1, width), F32),
        (row, (1, width), F32),
        (whole_block((1, 3 * width)), (1, 3 * width), F32),
    ]
    outs += [(whole_block((1, half // 2, 4 * width)), (1, half // 2, 4 * width), BF16)] * 4
    scratch = []
    if first is not None:
        after, next_gain, parts = first
        operands += (after, next_gain, *parts)
        specs += [item_block(after.shape), row] + [item_block(caption_shape)] * 4
        outs += [(row, (1, width), F32)] * 2
        scratch = [pltpu.VMEM((ROWS, width), F32)]
    else:
        outs += [(item_block(caption_shape), caption_shape, BF16)]
    return pl.pallas_call(
        partial(attend_backward_kernel, plan, len(arrays), first is not None),
        grid_spec=pltpu.PrefetchScalarGridSpec(
            num_scalar_prefetch=1,
            grid=(items,),
            in_specs=[ANYWHERE] * len(arrays) + specs,
            out_specs=[spec for spec, _, _ in outs],
            scratch_shapes=blocks_scratch(4, width)
            + [
                pltpu.VMEM((width, items * ROWS), BF16),
                pltpu.VMEM((width, items * ROWS), BF16),
                pltpu.VMEM((items * ROWS, width), BF16),
                pltpu.VMEM((items * ROWS, 3 * width), BF16),
                pltpu.VMEM((ROWS, width), BF16),
            ]
            + scratch,
        ),
        out_shape=[jax.ShapeDtypeStruct(shape, kind) for _, shape, kind in outs],
        compiler_params=pltpu.CompilerParams(vmem_limit_bytes=VMEM_BYTES),
        cost_estimate=LONG,
        name="attend_backward",
    )(info, *arrays, *operands)


def normal_parts(u):
    t = pl.reciprocal(1.0 + 0.23164190 * jnp.abs(u), approx=True)
    bell = jnp.exp2((u * -0.7213475204444817) * u)
    poly = t * (
        0.127414796
        + t * (-0.142248368 + t * (0.7107068705 + t * (-0.7265760135 + t * 0.5307027145)))
    )
    tail = poly * bell
    return jnp.where(u < 0, tail, 1.0 - tail), bell


def inner_forward(normed, matrix, bias):
    inner = dot_plain(normed, matrix) + bias
    cumulative, bell = normal_parts(inner)
    slope = cumulative + (inner * 0.3989422804014327) * bell
    return (inner * cumulative).astype(BF16), slope.astype(BF16)


def expert_forward_kernel(plan, weight_count, count, kind, info, *refs):
    weights, refs = refs[:weight_count], refs[weight_count:]
    x_ref, gain_ref, shift_ref, inner_ref, outer_ref = refs[:5]
    y_ref, act_ref, slope_ref, blocks, sems, normed, total = refs[5:]
    step = pl.program_id(0)
    items, _, width = x_ref.shape

    @pl.when(step == 0)
    def _():
        start_weights(info, items, weights, plan, blocks, sems)
        for item in range(items):
            x = x_ref[item, :count].astype(BF16).astype(F32)
            unit, _ = norm_parts(x)
            normed[item * count : (item + 1) * count] = (
                unit * gain_ref[...] + shift_ref[...]
            ).astype(BF16)

    wait_block(blocks, step, sems)
    wait_block(blocks, step + 4, sems)
    for at in range(0, width, 256):
        columns = slice(at, at + 256)
        act, slope = inner_forward(normed[...], blocks[step, :, columns], inner_ref[:, columns])
        act_ref[:, columns] = act
        slope_ref[:, columns] = slope
    part = dot_plain(act_ref[...], blocks[step + 4])

    @pl.when(step == 0)
    def _():
        total[...] = part

    @pl.when(step > 0)
    def _():
        total[...] += part

    @pl.when(step == pl.num_programs(0) - 1)
    def _():
        for item in range(items):
            row_true = true_positions(info[item], 0, count, 0, kind)
            branch = total[item * count : (item + 1) * count] + outer_ref[...]
            x = x_ref[item, :count].astype(BF16).astype(F32)
            y_ref[item, :count] = (x + jnp.where(row_true, branch, 0.0)).astype(BF16)
            if count < ROWS:
                y_ref[item, count:] = jnp.zeros((ROWS - count, width), BF16)


def expert_backward_kernel(plan, weight_count, count, kind, info, *refs):
    weights, refs = refs[:weight_count], refs[weight_count:]
    x_ref, gain_ref, shift_ref, act_ref, slope_ref, grad_ref = refs[:6]
    out_ref, gain_grad_ref, shift_grad_ref, inner_grad_ref, outer_grad_ref = refs[6:11]
    travel_refs = refs[11:15]
    blocks, sems, normed_turned, branch_turned, branch, inner_all, total = refs[15:]
    step = pl.program_id(0)
    items, _, width = x_ref.shape
    section, core = info[items], info[items + 1]

    @pl.when(step == 0)
    def _():
        start_weights(info, items, weights, plan, blocks, sems)
        outer = None
        for item in range(items):
            here = slice(item * count, (item + 1) * count)
            unit, _ = norm_parts(x_ref[item, :count].astype(BF16).astype(F32))
            normed = (unit * gain_ref[...] + shift_ref[...]).astype(BF16)
            row_true = true_positions(info[item], 0, count, 0, kind)
            incoming = grad_ref[item, :count].astype(F32)
            masked = jnp.where(row_true, incoming, 0.0).astype(BF16)
            branch[here] = masked
            store_turned(normed_turned, normed.T, here, section, core)
            store_turned(branch_turned, masked.T, here, section, core)
            term = column_sum(masked)
            outer = term if outer is None else outer + term
        outer_grad_ref[...] = outer

    wait_block(blocks, step, sems)
    wait_block(blocks, step + 4, sems)
    for at in range(0, width, 256):
        columns = slice(at, at + 256)
        act_grad = dot_last(branch[...], blocks[step + 4, columns])
        inner = (slope_ref[:, columns].astype(F32) * act_grad).astype(BF16)
        inner_all[:, columns] = inner
        inner_grad_ref[:, columns] = column_sum(inner)
        put_travel(travel_refs, 0, columns, normed_turned, inner)
        put_travel(travel_refs, 1, columns, branch_turned, act_ref[:, columns])
    part = dot_last(inner_all[...], blocks[step])

    @pl.when(step == 0)
    def _():
        total[...] = part

    @pl.when(step > 0)
    def _():
        total[...] += part

    @pl.when(step == pl.num_programs(0) - 1)
    def _():
        gain_sum, shift_sum = None, None
        for item in range(items):
            unit, scale = norm_parts(x_ref[item, :count].astype(BF16).astype(F32))
            normed_grad = total[item * count : (item + 1) * count]
            gain_part = jnp.sum(normed_grad * unit, axis=0, keepdims=True)
            shift_part = jnp.sum(normed_grad, axis=0, keepdims=True)
            gain_sum = gain_part if gain_sum is None else gain_sum + gain_part
            shift_sum = shift_part if shift_sum is None else shift_sum + shift_part
            incoming = grad_ref[item, :count].astype(F32)
            hidden = incoming + norm_back(normed_grad, unit, scale, gain_ref[...])
            out_ref[item, :count] = hidden.astype(BF16)
            if count < ROWS:
                out_ref[item, count:] = grad_ref[item, count:]
        gain_grad_ref[...] = gain_sum
        shift_grad_ref[...] = shift_sum


def shared_forward_kernel(*refs):
    *rows_refs, inputs_ref, inner_ref, outputs_ref, part_ref, normed, total = refs
    count = rows_refs[0].shape[0]
    step = pl.program_id(0)

    @pl.when(step == 0)
    def _():
        for index, ref in enumerate(rows_refs):
            normed[index * count : (index + 1) * count] = ref[...]
        total[...] = jnp.zeros_like(total)

    act, _ = inner_forward(normed[...], inputs_ref[...], inner_ref[...])
    total[...] += dot_plain(act, outputs_ref[...])

    @pl.when(step == pl.num_programs(0) - 1)
    def _():
        for index in range(SECTIONS):
            part_ref[index] = total[index * count : (index + 1) * count].astype(BF16)


def shared_backward_kernel(plan, weight_count, info, *refs):
    weights, refs = refs[:weight_count], refs[weight_count:]
    rows_refs, grad_refs, inner_ref = refs[:4], refs[4:8], refs[8]
    part_ref, keep_ref, send_ref, inner_grad_ref, outer_grad_ref = refs[9:14]
    blocks, sems, normed, branch, matrix = refs[14:]
    count, width = rows_refs[0].shape
    half = width // 2
    first = info.shape[0] - 3
    core = info[first + 1]
    start_weights(info, first, weights, plan, blocks, sems)
    for index in range(SECTIONS):
        here = slice(index * count, (index + 1) * count)
        normed[here] = rows_refs[index][...]
        branch[here] = grad_refs[index][...]
    outer_grad_ref[...] = column_sum(grad_refs[0][...])
    wait_block(blocks, 0, sems)
    wait_block(blocks, 1, sems)
    part = None
    for at in range(0, width, 256):
        columns = slice(at, at + 256)
        act, slope = inner_forward(normed[...], blocks[0, :, columns], inner_ref[:, columns])
        act_grad = dot_last(branch[...], blocks[1, columns])
        inner = (slope.astype(F32) * act_grad).astype(BF16)
        inner_grad_ref[:, columns] = column_sum(inner)
        matrix[0, :, columns] = dot_first(normed[...], inner).astype(BF16)
        matrix[1, :, columns] = dot_first(branch[...], act).astype(BF16)
        term = dot_last(inner, blocks[0, :, columns])
        part = term if part is None else part + term
    for index in range(SECTIONS):
        part_ref[index] = part[index * count : (index + 1) * count].astype(BF16)
    quarter = half // 4
    for which in range(2):
        for group in range(4):
            columns = slice(group * width, (group + 1) * width)
            mine = pl.multiple_of(core * half, 16) + group * quarter
            other = pl.multiple_of((1 - core) * half, 16) + group * quarter
            keep_ref[which, :, columns] = matrix[which, pl.ds(pl.multiple_of(mine, 16), quarter)]
            send_ref[which, :, columns] = matrix[which, pl.ds(pl.multiple_of(other, 16), quarter)]


def chunk_columns(rows, width):
    return pl.BlockSpec((rows, width), lambda step, info: (0, step))


def expert_forward(x, info, weights, gain, shift, inner, outer, count, kind):
    arrays, plan = weights
    items, _, width = x.shape
    hidden = inner.shape[1]
    row = whole_block((1, width))
    return pl.pallas_call(
        partial(expert_forward_kernel, plan, len(arrays), count, kind),
        grid_spec=pltpu.PrefetchScalarGridSpec(
            num_scalar_prefetch=1,
            grid=(hidden // width,),
            in_specs=[ANYWHERE] * len(arrays)
            + [whole_block(x.shape), row, row, chunk_columns(1, width), row],
            out_specs=[
                whole_block((items, ROWS, width)),
                chunk_columns(items * count, width),
                chunk_columns(items * count, width),
            ],
            scratch_shapes=blocks_scratch(8, width)
            + [
                pltpu.VMEM((items * count, width), BF16),
                pltpu.VMEM((items * count, width), F32),
            ],
        ),
        out_shape=[
            jax.ShapeDtypeStruct((items, ROWS, width), BF16),
            jax.ShapeDtypeStruct((items * count, hidden), BF16),
            jax.ShapeDtypeStruct((items * count, hidden), BF16),
        ],
        compiler_params=pltpu.CompilerParams(vmem_limit_bytes=VMEM_BYTES),
        cost_estimate=SHORT,
        name="expert_forward_" + kind,
    )(info, *arrays, x, gain, shift, inner, outer)


def expert_backward(x, info, weights, gain, shift, act, slope, incoming, count, kind):
    arrays, plan = weights
    items, _, width = x.shape
    half = width // 2
    hidden = act.shape[1]
    row = whole_block((1, width))
    travel = pl.BlockSpec((2, half // 2, width), lambda step, info: (0, 0, step))
    return pl.pallas_call(
        partial(expert_backward_kernel, plan, len(arrays), count, kind),
        grid_spec=pltpu.PrefetchScalarGridSpec(
            num_scalar_prefetch=1,
            grid=(hidden // width,),
            in_specs=[ANYWHERE] * len(arrays)
            + [
                whole_block(x.shape),
                row,
                row,
                chunk_columns(items * count, width),
                chunk_columns(items * count, width),
                whole_block(incoming.shape),
            ],
            out_specs=[whole_block(incoming.shape), row, row, chunk_columns(1, width), row]
            + [travel] * 4,
            scratch_shapes=blocks_scratch(8, width)
            + [
                pltpu.VMEM((width, items * count), BF16),
                pltpu.VMEM((width, items * count), BF16),
                pltpu.VMEM((items * count, width), BF16),
                pltpu.VMEM((items * count, width), BF16),
                pltpu.VMEM((items * count, width), F32),
            ],
        ),
        out_shape=[
            jax.ShapeDtypeStruct(incoming.shape, BF16),
            jax.ShapeDtypeStruct((1, width), F32),
            jax.ShapeDtypeStruct((1, width), F32),
            jax.ShapeDtypeStruct((1, hidden), F32),
            jax.ShapeDtypeStruct((1, width), F32),
        ]
        + [jax.ShapeDtypeStruct((2, half // 2, hidden), BF16)] * 4,
        compiler_params=pltpu.CompilerParams(vmem_limit_bytes=VMEM_BYTES),
        cost_estimate=SHORT,
        name="expert_backward_" + kind,
    )(info, *arrays, x, gain, shift, act, slope, incoming)


IN_VMEM = pl.BlockSpec(memory_space=pltpu.VMEM)
IN_SMEM = pl.BlockSpec(memory_space=pltpu.SMEM)


def shared_forward(rows, inputs, inner, outputs):
    count, width = rows[0].shape
    total = SECTIONS * count
    hidden = inner.shape[1]
    return pl.pallas_call(
        shared_forward_kernel,
        grid=(hidden // width,),
        in_specs=[pl.BlockSpec(rows[0].shape, lambda step: (0, 0))] * 4
        + [
            pl.BlockSpec((width, width), lambda step: (0, step)),
            pl.BlockSpec((1, width), lambda step: (0, step)),
            pl.BlockSpec((width, width), lambda step: (step, 0)),
        ],
        out_specs=pl.BlockSpec((SECTIONS, count, width), lambda step: (0, 0, 0)),
        scratch_shapes=[pltpu.VMEM((total, width), BF16), pltpu.VMEM((total, width), F32)],
        out_shape=jax.ShapeDtypeStruct((SECTIONS, count, width), BF16),
        compiler_params=pltpu.CompilerParams(vmem_limit_bytes=VMEM_BYTES),
        cost_estimate=SHORT,
        name="shared_forward",
    )(*rows, inputs, inner, outputs)


def shared_backward(rows, grads, info, weights, inner):
    arrays, plan = weights
    count, width = rows[0].shape
    total = SECTIONS * count
    travel = (2, width // 8, 4 * width)
    return pl.pallas_call(
        partial(shared_backward_kernel, plan, len(arrays)),
        in_specs=[IN_SMEM] + [ANYWHERE] * len(arrays) + [IN_VMEM] * 9,
        out_specs=[IN_VMEM] * 5,
        scratch_shapes=blocks_scratch(2, width)
        + [
            pltpu.VMEM((total, width), BF16),
            pltpu.VMEM((total, width), BF16),
            pltpu.VMEM((2, width, width), BF16),
        ],
        out_shape=[
            jax.ShapeDtypeStruct((SECTIONS, count, width), BF16),
            jax.ShapeDtypeStruct(travel, BF16),
            jax.ShapeDtypeStruct(travel, BF16),
            jax.ShapeDtypeStruct((1, width), F32),
            jax.ShapeDtypeStruct((1, width), F32),
        ],
        compiler_params=pltpu.CompilerParams(vmem_limit_bytes=VMEM_BYTES),
        cost_estimate=SHORT,
        name="shared_backward",
    )(info, *arrays, *rows, *grads, inner)


def plane_turn(plane, planes):
    return ((plane & 1) << 1) | (plane >> 1) if planes == 4 else 0


def finish_kernel(planes, info, scale_ref, mine_ref, theirs_ref, *refs):
    step = pl.program_id(0)
    count = mine_ref.shape[1]
    placed = refs[-1]
    outs = refs[:-1]
    width = placed.shape[1]
    half = width // 2
    at = info.shape[0] - 3
    section, core = info[at], info[at + 1]
    turn = plane_turn(info[at + 2], planes)
    turned = turn if count == 1 else jnp.where(section == 1, turn, 0)
    scale = scale_ref[0, 0]
    columns = pl.ds(pl.multiple_of((step ^ turned) * width, width), width)

    def place(which):
        def by_rows():
            for side, ref in enumerate((mine_ref, theirs_ref)):
                for away in range(SECTIONS):
                    for path in range(2):
                        row = (core ^ side) * half + path * (half // 2)
                        row = row + (section ^ away) * PIECE_ROWS
                        placed[pl.ds(pl.multiple_of(row, 16), PIECE_ROWS), :] = ref[
                            away, which, path * PIECE_ROWS : (path + 1) * PIECE_ROWS, columns
                        ].astype(F32)

        def by_columns():
            for side, ref in enumerate((mine_ref, theirs_ref)):
                for group in range(4):
                    quarter = half // 4
                    row = (core ^ side) * half + group * quarter
                    placed[pl.ds(pl.multiple_of(row, 16), quarter), :] = ref[
                        step, which, :, group * width : (group + 1) * width
                    ].astype(F32)

        if count == 1:
            by_rows()
        else:
            pl.when(section != 0)(by_rows)
            pl.when(section == 0)(by_columns)

    place(0)
    if count == 1:

        @pl.when(step < 3)
        def _():
            outs[0][0] = placed[...] / scale

        @pl.when(step == 3)
        def _():
            outs[1][0] = placed[...] / scale

    else:
        outs[0][0] = placed[...] / scale
        place(1)
        outs[1][0] = (placed[...] / scale).T


def finish(info, scale, mine, theirs, planes):
    count, hidden = mine.shape[1], mine.shape[3]
    width = hidden // 4
    if count == 1:
        shapes = [(1, width, 3 * width), (1, width, width)]
        maps = [lambda step, info: (0, 0, jnp.minimum(step, 2)), lambda step, info: (0, 0, 0)]
    else:
        shapes = [(1, width, hidden), (1, hidden, width)]
        maps = [lambda step, info: (0, 0, step), lambda step, info: (0, step, 0)]
    return pl.pallas_call(
        partial(finish_kernel, planes),
        grid_spec=pltpu.PrefetchScalarGridSpec(
            num_scalar_prefetch=1,
            grid=(4,),
            in_specs=[IN_SMEM, whole_block(mine.shape), whole_block(mine.shape)],
            out_specs=[pl.BlockSpec((1, width, width), at) for at in maps],
            scratch_shapes=[pltpu.VMEM((width, width), F32)],
        ),
        out_shape=[jax.ShapeDtypeStruct(shape, F32) for shape in shapes],
        compiler_params=pltpu.CompilerParams(vmem_limit_bytes=VMEM_BYTES),
        cost_estimate=SHORT,
        name="finish",
    )(info, scale, mine, theirs)


def pack_kernel(count, plan, info, *refs):
    sources, outs, sems = refs[:count], refs[count:-1], refs[-1]
    first = info.shape[0] - 3
    section, core, plane = info[first], info[first + 1], info[first + 2]
    half = outs[0].shape[1]
    for index, (out, choices) in enumerate(zip(outs, plan)):
        for at, at_plane, parts in choices:
            here = section == at
            if at_plane is not None:
                here = here & (plane == at_plane)

            @pl.when(here)
            def _(index=index, out=out, parts=parts):
                for block, part in enumerate(parts):
                    if part[0] == "own":
                        _, which, row, column = part
                        rows = pl.ds(pl.multiple_of(row + core * half, half), half)
                        source = sources[which].at[rows, pl.ds(column, out.shape[2])]
                    else:
                        source = sources[part[1]].at[block]
                    pltpu.make_async_copy(source, out.at[block], sems.at[index, block]).start()

    for index, out in enumerate(outs):
        for block in range(2):
            pltpu.make_async_copy(out.at[block], out.at[block], sems.at[index, block]).wait()


def pack(info, sources, plan, shape):
    return pl.pallas_call(
        partial(pack_kernel, len(sources), plan),
        in_specs=[IN_SMEM] + [ANYWHERE] * len(sources),
        out_specs=[IN_VMEM] * len(plan),
        scratch_shapes=[pltpu.SemaphoreType.DMA((len(plan), 2))],
        out_shape=[jax.ShapeDtypeStruct(shape, BF16)] * len(plan),
        cost_estimate=SHORT,
        name="pack",
    )(info, *sources)


def over_section(value, bits, sources=range(SECTIONS)):
    return lax.ppermute(value, "section", [(at, at ^ bits) for at in sources])


def over_core(value):
    return lax.ppermute(value, "core", [(0, 1), (1, 0)])


def over_plane(value, pairs):
    return lax.ppermute(value, "z", pairs)


def added(left, right):
    return (left.astype(F32) + right.astype(F32)).astype(BF16)


def after(value, *earlier):
    return lax.optimization_barrier((value,) + earlier)[0]


def by_section(section, values):
    result, last = None, None
    for at in sorted(values):
        if result is None:
            result = values[at]
        elif values[at] is not last:
            result = jnp.where(section >= at, values[at], result)
        last = values[at]
    return result


def total(*values):
    result = values[0].astype(F32)
    for value in values[1:]:
        result = result + value.astype(F32)
    return result.astype(BF16)


class Sums:
    def __init__(self, travel):
        self.stay, self.move, self.other_stay, self.other_move = travel
        self.size = self.stay.shape[1] // 2

    def cross(self, *earlier):
        if earlier:
            self.other_move = after(self.other_move, *earlier)
            self.other_stay = after(self.other_stay, *earlier)
        self.got_move, self.got_stay = over_core(self.other_move), over_core(self.other_stay)

    def first_sends(self):
        size = self.size
        self.sent = [
            total(self.move[:, at : at + size], self.got_move[:, at : at + size])
            for at in (0, size)
        ]
        return self.sent

    def second_sends(self, from_x, from_y):
        size, half = self.size, self.size // 2
        self.first = from_x, from_y
        to_y = total(self.stay[:, half:size], self.got_stay[:, half:size], from_x[:, half:])
        to_x = total(
            self.stay[:, size + half :], self.got_stay[:, size + half :], from_y[:, half:]
        )
        self.sent = [to_x, to_y]
        return self.sent

    def whole(self, from_x, from_y):
        size, half = self.size, self.size // 2
        parts = []
        for at, first, second in ((0, self.first[0], from_y), (size, self.first[1], from_x)):
            here = slice(at, at + half)
            parts.append(total(self.stay[:, here], self.got_stay[:, here], first[:, :half], second))
        return jnp.concatenate(parts, axis=1)


def over_links(sends):
    return [over_section(sends[0], 1), over_section(sends[1], 2)]


class Planes:
    def __init__(self, value, plane, planes):
        self.value, self.plane, self.planes, self.turn = value, plane, planes, 0

    def sends(self, *earlier):
        value = after(self.value, *earlier) if earlier else self.value
        if self.planes != 4:
            return (value,)
        bits = (1, 2, 2, 1)[self.turn]
        if self.turn < 2:
            bit = (self.plane & 1, self.plane >> 1)[self.turn]
            size = value.shape[-1] // 2
            value = lax.dynamic_slice_in_dim(value, (1 - bit) * size, size, value.ndim - 1)
        return (over_plane(value, [(at, at ^ bits) for at in range(4)]),)

    def take(self, arrived):
        if self.planes != 4:
            self.value = lax.psum(arrived, "z") if self.turn == 3 else arrived
        elif self.turn < 2:
            bit = (self.plane & 1, self.plane >> 1)[self.turn]
            size = self.value.shape[-1] // 2
            keep = lax.dynamic_slice_in_dim(self.value, bit * size, size, self.value.ndim - 1)
            self.value = added(keep, arrived)
        else:
            self.value = jnp.concatenate([self.value, arrived], axis=-1)
        self.turn += 1

    def in_order(self, value):
        if self.planes != 4:
            return value
        size, turn = value.shape[-1] // 4, plane_turn(self.plane, 4)
        parts = [
            lax.dynamic_slice_in_dim(value, (at ^ turn) * size, size, value.ndim - 1)
            for at in range(4)
        ]
        return jnp.concatenate(parts, axis=-1)


class Weights:
    def __init__(self, own, info, planes):
        self.own, self.info = own, info
        self.four = planes == 4
        self.plan = PLAN_FOUR if self.four else PLAN_ANY
        self.half, self.width = own[1].shape[0] // 2, own[1].shape[1]
        self.mine, self.theirs, self.arrived = {}, {}, {}

    def place(self, layer, block):
        if layer in "ac":
            return (0, 0, block * self.width) if block < 3 else (1, 0, 0)
        if layer == "g":
            return (2, 0, block * self.width) if block < 4 else (3, (block - 4) * self.width, 0)
        return (2, 0, block * self.width) if block < 4 else (3, (block - 4) * self.width, 0)

    def choices(self, sends, sources):
        result = []
        for at in range(SECTIONS):
            name = sends.get(at)
            if name is not None and HOMES[name[0]] != at:
                key = self.arrived[at, name]
                if key not in sources:
                    sources[key] = len(self.own) + len(sources)
                result.append((at, None, [("arrived", sources[key])] * 2))
                continue
            for plane in range(4) if name == "F" else (None,):
                piece = ("f" + str(plane)) if name == "F" else name or "a0"
                layer, index = piece[0], int(piece[1])
                if layer in "ac":
                    blocks = ATTEND_BLOCKS[index]
                else:
                    blocks = (index, 4 + index) if layer == "g" else EXPERT_BLOCKS[index]
                parts = [("own",) + self.place(layer, block) for block in blocks]
                result.append((at, plane, parts))
        return result

    def packed(self, wanted, *earlier):
        sources = {}
        plan = [self.choices(sends, sources) for sends in wanted]
        info = after(self.info, *earlier) if earlier else self.info
        arrays = list(self.own) + [self.mine[key] for key in sources]
        return pack(info, arrays, plan, (2, self.half, self.width))

    def run_step(self, step, *earlier):
        links = [(link, sends) for link, sends in enumerate(self.plan[step]) if sends]
        payloads = self.packed([sends for _, sends in links], *earlier)
        for (link, sends), payload in zip(links, payloads):
            self.mine[step, link] = over_section(payload, link + 1, sorted(sends))
        for link, sends in links:
            for at, name in sends.items():
                self.arrived[at ^ (link + 1), name] = (step, link)
        return payloads

    def run_planes(self, step, *earlier):
        if not self.four:
            return ()
        if step == 1:
            self.mine["plane", 0] = self.packed([{at: "F" for at in range(SECTIONS)}], *earlier)[0]
            earlier = ()
        up, down = self.mine["plane", step - 1], self.mine["plane", 1 - step]
        if earlier:
            up, down = after(up, *earlier), after(down, *earlier)
        up = over_plane(up, [(at, at + 1) for at in range(step - 1, 3)])
        down = over_plane(down, [(at, at - 1) for at in range(4 - step, 0, -1)])
        self.mine["plane", step], self.mine["plane", -step] = up, down
        return up, down

    def hand_over(self, steps, *earlier):
        for key in [key for key in self.mine if key[0] in steps and key not in self.theirs]:
            mine = after(self.mine[key], *earlier) if earlier else self.mine[key]
            self.theirs[key] = over_core(mine)
        return [self.theirs[key] for key in self.theirs if key[0] in steps]

    def set_mine(self, keys, values):
        for key, value in zip(keys, values):
            self.mine[key] = value

    def layer(self, layer):
        arrays, places = list(self.own), {}

        def place(key):
            if key not in self.theirs:
                self.theirs[key] = over_core(self.mine[key])
            if key not in places:
                places[key] = len(arrays)
                arrays.extend([self.mine[key], self.theirs[key]])
            return places[key], places[key] + 1

        if layer in "ac":
            names = [(layer + str(index), ATTEND_BLOCKS[index]) for index in range(2)]
        else:
            names = [(layer + str(index), EXPERT_BLOCKS[index]) for index in range(4)]
        plan = []
        for at in range(SECTIONS):
            if layer == "g":
                names = [("g" + str(at), (0, 1))]
            if HOMES[layer] == at:
                steps = []
                for name, blocks in names:
                    for block in blocks:
                        source = block * 4 if layer == "g" else block
                        steps.append((block, ("own",) + self.place(layer, source)))
                plan.append((at, None, steps))
                continue
            by_plane = layer == "f" and self.four
            for plane in range(4) if by_plane else (None,):
                steps = []
                for index, (name, blocks) in enumerate(names):
                    key = ("plane", plane - index) if by_plane else self.arrived[at, name]
                    for which, block in enumerate(blocks):
                        steps.append((block, ("piece",) + place(key) + (which,)))
                plan.append((at, plane, steps))
        return arrays, plan


def per_device(
    tokens,
    caption_lengths,
    attend_gain,
    attend_shift,
    attend_inputs,
    attend_bias,
    attend_output,
    expert_gain,
    expert_shift,
    expert_inputs,
    expert_inner_bias,
    expert_outputs,
    expert_outer_bias,
    cotangent,
):
    section, core, plane = lax.axis_index("section"), lax.axis_index("core"), lax.axis_index("z")
    planes = lax.axis_size("z")
    items, positions, width = tokens.shape
    hidden = expert_inputs.shape[-1]
    info = [value.reshape(1).astype(jnp.int32) for value in (section, core, plane)]
    info = jnp.concatenate([caption_lengths] + info)
    weights = Weights(
        (attend_inputs[0], attend_output[0], expert_inputs[0], expert_outputs[0]), info, planes
    )

    def to_sections(value):
        return [value] + [over_section(value, bits) for bits in (1, 2, 3)]

    def items_of(part):
        return part.reshape(items, CAP_ROWS, width)

    def under(outputs, *arrivals):
        joined = lax.optimization_barrier(tuple(outputs) + arrivals)
        return joined[: len(outputs)], joined[len(outputs) :]

    weights.run_step(0)
    pad = ((0, 0), (0, ROWS - positions), (0, 0))
    x0 = jnp.pad(tokens, pad)
    last_grad = jnp.pad(cotangent, pad)
    rows = jnp.concatenate(
        [
            attend_gain,
            attend_shift,
            attend_bias,
            expert_gain,
            expert_shift,
            expert_inner_bias,
            expert_outer_bias,
            jnp.full((1, 128), jnp.sum(caption_lengths), F32),
        ],
        axis=1,
    )
    rows = jnp.concatenate(to_sections(rows), axis=0)
    language_count = jnp.sum(rows[:, -128:], axis=0, keepdims=True)
    language_count = language_count + over_core(language_count)
    if planes == 4:
        language_count = language_count + over_plane(language_count, [(at, at ^ 1) for at in range(4)])
        language_count = language_count + over_plane(language_count, [(at, at ^ 2) for at in range(4)])
    else:
        language_count = lax.psum(language_count, "z")
    language_count = language_count[0, 0].astype(jnp.int32)
    vision_count = PATCHES * items * SECTIONS * 2 * planes
    counts = jnp.stack(
        [jnp.full((), vision_count, jnp.int32), language_count, language_count + vision_count]
    )
    rows = [lax.dynamic_index_in_dim(rows, at ^ section, 0) for at in range(SECTIONS)]
    sizes = [width, width, 3 * width, width, width, hidden, width]
    ends = [sum(sizes[: at + 1]) for at in range(len(sizes))]

    def row(slot, which):
        return rows[slot][:, ends[which] - sizes[which] : ends[which]]

    used = [(0, 0), (0, 1), (0, 2), (0, 3), (0, 4), (0, 5), (1, 3), (1, 4), (1, 5), (1, 6)]
    used += [(0, 6), (2, 0), (2, 1), (2, 2), (3, 3), (3, 4), (3, 5), (3, 6)]
    kept = lax.optimization_barrier(tuple(row(*at) for at in used) + (x0, last_grad, counts))
    x0, last_grad, counts = kept[-3:]
    kept = dict(zip(used, kept))

    def row(slot, which):
        return kept[slot, which]

    weights.run_step(1)
    weights.hand_over((0,))
    sent = weights.run_step(2, *kept.values(), x0, last_grad, counts)
    weights.hand_over((1,), *sent)
    info = after(info, *weights.hand_over((0, 1)))
    attend0 = weights.layer("a")
    y0, qkv0, mixed0, caption_rows = attend_forward(
        x0, info, attend0, row(0, 0), row(0, 1), row(0, 2), following=(row(0, 3), row(0, 4))
    )
    caption_rows = to_sections(caption_rows.reshape(-1, width))
    weights.run_step(EARLY_STEPS, *caption_rows[1:], *weights.hand_over((2,), caption_rows[0]))
    planes_moved = weights.run_planes(1, *caption_rows[1:])
    late_keys = [key for key in weights.mine if key[0] == EARLY_STEPS]
    outputs = shared_forward(caption_rows, expert_inputs[0], expert_inner_bias, expert_outputs[0])
    if weights.four:
        late_keys += [("plane", 1), ("plane", -1)]
    (part,), moved = under([outputs], *[weights.mine[key] for key in late_keys])
    weights.set_mine(late_keys, moved)
    branch = {at: over_section(part[at], at, [0]) for at in range(1, SECTIONS)}
    branch[0] = part[0]
    weights.run_planes(2, part)
    expert1 = weights.layer("e")
    outputs = expert_forward(
        y0, info, expert1, row(1, 3), row(1, 4), row(1, 5), row(1, 6), PATCH_ROWS, "patch"
    )
    if weights.four:
        last_moved = [("plane", 2), ("plane", -2)]
    else:
        last_moved = []
        for step in range(EARLY_STEPS + 1, len(weights.plan)):
            weights.run_step(step, part)
    (x2, act1, slope1), moved = under(outputs, *[weights.mine[key] for key in last_moved])
    weights.set_mine(last_moved, moved)
    branch = items_of(by_section(section, branch))
    attend2 = weights.layer("c")
    weights.run_planes(3, x2)
    outputs = attend_forward(
        x2, info, attend2, row(2, 0), row(2, 1), row(2, 2), merge=(y0, branch, row(0, 6))
    )
    last_moved = [("plane", 3), ("plane", -3)] if weights.four else []
    (x3, qkv2, mixed2, x2), moved = under(outputs, *[weights.mine[key] for key in last_moved])
    weights.set_mine(last_moved, moved)
    expert3 = weights.layer("f")
    layer_output, act3, slope3 = expert_forward(
        x3, info, expert3, row(3, 3), row(3, 4), row(3, 5), row(3, 6), ROWS, "all"
    )

    def small_rows(values):
        flat = jnp.concatenate(values, axis=1)
        count = -(-flat.shape[1] // hidden)
        flat = jnp.pad(flat, ((0, 0), (0, count * hidden - flat.shape[1])))
        return flat.reshape(count, hidden)

    def to_home(sums):
        got = [by_section(section, sums)]
        for bits in (1, 2, 3):
            sends = {at ^ bits: sums[at] for at in sums}
            got.append(over_section(by_section(section, sends), bits, sorted(sends)))
        return got

    last_moved = []
    if weights.four:
        weights.run_step(EARLY_STEPS + 1, x3)
        last_moved = [key for key in weights.mine if key[0] == EARLY_STEPS + 1]
    outputs = expert_backward(
        x3, info, expert3, row(3, 3), row(3, 4), act3, slope3, last_grad, ROWS, "all"
    )
    outputs, moved = under(outputs, *[weights.mine[key] for key in last_moved])
    weights.set_mine(last_moved, moved)
    handed = weights.hand_over((EARLY_STEPS + 1,)) if weights.four else []
    grad3, *small3 = outputs[:5]
    sums3 = Sums(outputs[5:])
    sums3.cross()
    moved = over_links(sums3.first_sends())
    grad3 = after(grad3, *sums3.sent)
    outputs = attend_backward(
        x2, info, attend2, row(2, 0), row(2, 1), qkv2, mixed2, grad3
    )
    outputs, moved = under(outputs, *moved, sums3.got_stay, *handed)
    grad2, *small2 = outputs[:4]
    sums2, caption_grad = Sums(outputs[4:8]), outputs[8]
    caption_grads = to_sections(caption_grad.reshape(-1, width))
    sums3.got_stay = moved[2]
    moved3 = over_links(sums3.second_sends(*moved[:2]))
    grad2 = after(grad2, *sums3.sent)
    outputs = expert_backward(
        y0, info, expert1, row(1, 3), row(1, 4), act1, slope1, grad2, PATCH_ROWS, "patch"
    )
    outputs, caption_grads = under(outputs, *caption_grads)
    grad1, *small1 = outputs[:5]
    sums2.cross(grad1)
    sums1 = Sums(outputs[5:])
    sums1.cross()
    inner_quarter = lax.dynamic_slice(row(0, 5), (0, section * width), (1, width))
    inner_quarter = after(inner_quarter, grad1)
    outputs = shared_backward(
        caption_rows, caption_grads, info, weights.layer("g"), inner_quarter
    )
    outputs, moved3 = under(outputs, *moved3)
    parts, keep0, send0, inner_grad, outer_grad = outputs
    inner_grad = lax.dynamic_update_slice(
        jnp.zeros((1, hidden), F32), inner_grad, (0, section * width)
    )
    small_early = small_rows(small2 + small1 + small3 + [inner_grad, outer_grad])
    small_sent = small_early.astype(BF16).reshape(-1, width)
    got = [
        over_section(jnp.concatenate([parts[bits], small_sent], axis=0), bits) for bits in (1, 2, 3)
    ]
    caption_count = parts.shape[1]
    parts = [parts[0]] + [value[:caption_count] for value in got]
    small_early += sum(value[caption_count:].astype(F32) for value in got).reshape(-1, hidden)
    keep0 = added(keep0, over_core(send0))
    early = lax.psum(jnp.concatenate([sums3.whole(*moved3), keep0], axis=0), "z")
    sends = sums2.first_sends() + sums1.first_sends()
    sends = [after(value, *got) for value in sends]
    moved2, moved1 = over_links(sends[:2]), over_links(sends[2:])
    grad1 = after(grad1, keep0, *sends)
    outputs = attend_backward(
        x0,
        info,
        attend0,
        row(0, 0),
        row(0, 1),
        qkv0,
        mixed0,
        grad1,
        first=(y0, row(0, 3), [items_of(value) for value in parts]),
    )
    outputs, moved = under(outputs, *moved2, *moved1)
    moved2, moved1 = moved[:2], moved[2:]
    tokens_grad, *small_first = outputs[:4]
    sums_first, gain_grad, shift_grad = Sums(outputs[4:8]), outputs[8], outputs[9]
    sums_first.cross()
    moved1 = over_links(sums1.second_sends(*moved1))
    sends = [after(value, *sums1.sent) for value in sums_first.first_sends()]
    moved = over_links(sends)
    moved1 = [after(value, *sends) for value in moved1]
    planes1 = Planes(sums1.whole(*moved1), plane, planes)
    planes1.take(*planes1.sends(*sends))
    small_late = small_rows(small_first + [gain_grad, shift_grad])
    small_late = sum(to_sections(after(small_late, *moved)))
    sums2.second_sends(*moved2)
    sums_first.second_sends(*moved)
    sends = [jnp.concatenate(pair, axis=0) for pair in zip(sums_first.sent, sums2.sent)]
    moved = over_links(sends)
    planes1.take(*planes1.sends(*sends))
    last = sums_first.whole(*[value[:1] for value in moved])
    sum2 = sums2.whole(*[value[1:] for value in moved])
    small = jnp.concatenate([small_late, small_early], axis=0)
    small = (small + over_core(after(small, *sends))).astype(BF16)
    small_count = small.shape[0]
    planes_last = Planes(
        jnp.concatenate([last[0], sum2[0], small], axis=0), plane, planes
    )
    planes_last.take(*planes_last.sends(planes1.value))
    planes1.take(*planes1.sends(planes_last.value))
    home_early = to_home({0: after(early[2:], planes1.value), 3: after(early[:2], planes1.value)})
    planes_last.take(*planes_last.sends(planes1.value))
    planes1.take(*planes1.sends(planes_last.value))
    home_late = to_home({1: after(planes1.value, *home_early[1:3])})
    planes_last.take(*planes_last.sends(planes1.value))
    planes_last.take(*planes_last.sends())
    eighth = last.shape[1]
    last = after(planes_last.value, home_early[3])
    home_attend = to_home({0: last[None, :eighth], 2: last[None, eighth : 2 * eighth]})
    small = planes_last.in_order(last[2 * eighth :].astype(F32))

    as_float = counts.astype(F32)
    one = jnp.ones((), F32)
    attend_scales = jnp.stack([as_float[2], one, as_float[2], one])
    expert_scales = jnp.stack([as_float[1], as_float[0], one, as_float[2]])

    def placed(pieces, scales):
        scale = lax.dynamic_index_in_dim(scales, section, 0).reshape(1, 1)
        pieces = jnp.stack(pieces)
        return finish(info, scale, pieces, over_core(pieces), planes)

    blank = jnp.zeros_like(home_late[0])
    inputs_whole, outputs_whole = placed(
        [
            by_section(section, {0: early, 1: late, 2: blank, 3: early})
            for early, late in zip(home_early, home_late)
        ],
        expert_scales,
    )
    blank = jnp.zeros_like(home_attend[0])
    attend_whole, output_whole = placed(
        [by_section(section, {0: got, 1: blank, 2: got, 3: blank}) for got in home_attend],
        attend_scales,
    )

    late_rows = small_late.shape[0]
    late_small, early_small = small[:late_rows].reshape(-1), small[late_rows:].reshape(-1)
    attend_size, expert_size = 5 * width, 3 * width + hidden
    cuts = [attend_size, attend_size + expert_size, attend_size + 2 * expert_size]
    early_parts = jnp.split(early_small, cuts)
    first_attend = late_small[:attend_size]
    first_expert = jnp.concatenate(
        [late_small[attend_size : attend_size + 2 * width], early_parts[3][: hidden + width]]
    )
    none_attend, none_expert = jnp.zeros_like(first_attend), jnp.zeros_like(first_expert)
    attend_small = jnp.stack([first_attend, none_attend, early_parts[0], none_attend])
    expert_small = jnp.stack([first_expert, early_parts[1], none_expert, early_parts[2]])
    attend_small = attend_small / attend_scales.reshape(-1, 1)
    expert_small = expert_small / expert_scales.reshape(-1, 1)
    attend_small = lax.dynamic_index_in_dim(attend_small, section, 0)
    expert_small = lax.dynamic_index_in_dim(expert_small, section, 0)
    return (
        layer_output[:, :positions],
        tokens_grad[:, :positions],
        attend_small[:, :width],
        attend_small[:, width : 2 * width],
        attend_whole,
        attend_small[:, 2 * width :],
        output_whole,
        expert_small[:, :width],
        expert_small[:, width : 2 * width],
        inputs_whole,
        expert_small[:, 2 * width : 2 * width + hidden],
        outputs_whole,
        expert_small[:, 2 * width + hidden :],
        counts,
    )


def solution(mesh):
    sections, groups = mesh.shape["section"], mesh.shape["dp"]
    split = Mesh(mesh.devices.reshape(sections, groups // 2, 2), ("section", "z", "core"))
    items = P(("section", "z", "core"), None, None)
    flat = P("section", None)
    matrix = P("section", None, None)
    placed = (
        items,
        P(("section", "z", "core")),
        flat,
        flat,
        matrix,
        flat,
        matrix,
        flat,
        flat,
        matrix,
        flat,
        matrix,
        flat,
        items,
    )
    return jax.shard_map(
        per_device,
        mesh=split,
        in_specs=placed,
        out_specs=(
            items,
            items,
            flat,
            flat,
            matrix,
            flat,
            matrix,
            flat,
            flat,
            matrix,
            flat,
            matrix,
            flat,
            P(),
        ),
        check_vma=False,
    )
```

```python
from functools import partial

import jax
import jax.numpy as jnp
from jax import lax
from jax.experimental import pallas as pl
from jax.experimental.pallas import tpu as pltpu
from jax.sharding import Mesh
from jax.sharding import PartitionSpec as P

HEADS = 12
HEAD_DIM = 64
PATCHES = 197
ROWS = 256
CAP_FIRST, CAP_ROWS = 192, 48
PATCH_ROWS = 208
PAIR = 2 * HEAD_DIM
SECTIONS = 4
PIECE_ROWS = 48
VMEM_BYTES = 58 * 1024 * 1024
F32 = jnp.float32
BF16 = jnp.bfloat16

PLAN_FOUR = (
    ({0: "a0", 1: "e0", 2: "c0", 3: "F"}, {0: "a1", 1: "e2", 2: "c0", 3: "F"}),
    ({0: "a1", 1: "e1", 2: "a1", 3: "e2"}, {0: "a0", 1: "a0", 2: "F", 3: "c0"}),
    ({0: "g3", 1: "e2", 2: "c1"}, {0: "e0", 1: "e3", 2: "c1"}),
    ({0: "g1", 1: "e3", 2: "e0", 3: "e3"}, {0: "e1", 1: "e1", 3: "c1"}),
    ({}, {0: "g2", 1: "g3"}),
)
PLAN_ANY = (
    ({0: "a0", 1: "e0", 2: "c0", 3: "f0"}, {0: "a1", 1: "e2", 2: "c0", 3: "f0"}),
    ({0: "a1", 1: "e1", 2: "a1", 3: "e2"}, {0: "a0", 1: "a0", 2: "c1", 3: "f1"}),
    ({0: "g3", 1: "e2", 2: "c1", 3: "f1"}, {0: "e0", 1: "e3", 2: "f0", 3: "f2"}),
    ({0: "g1", 1: "e3", 2: "e0", 3: "e3"}, {0: "e1", 1: "e1", 2: "f1", 3: "f3"}),
    ({0: "c1", 1: "f2", 3: "f2"}, {0: "g2", 1: "g3", 3: "c0"}),
    ({1: "f3", 3: "f3"}, {}),
)
EARLY_STEPS = 3
HOMES = {"a": 0, "c": 2, "e": 1, "f": 3, "F": 3, "g": 0}
ATTEND_BLOCKS = ((0, 1), (2, 3))
EXPERT_BLOCKS = ((0, 1), (4, 5), (2, 3), (6, 7))


def dot_plain(left, right):
    return jnp.dot(left, right, preferred_element_type=F32)


def dot_last(left, right):
    return lax.dot_general(left, right, (((1,), (1,)), ((), ())), preferred_element_type=F32)


def dot_first(left, right):
    return lax.dot_general(left, right, (((0,), (0,)), ((), ())), preferred_element_type=F32)


def column_sum(matrix):
    return jnp.sum(matrix.astype(F32), axis=0, keepdims=True)


def norm_parts(rows):
    centre = rows - jnp.mean(rows, axis=-1, keepdims=True)
    scale = lax.rsqrt(jnp.mean(centre * centre, axis=-1, keepdims=True) + 1e-06)
    return centre * scale, scale


def norm_back(normed_grad, unit, scale, gain):
    unit_grad = normed_grad * gain
    along = jnp.mean(unit_grad * unit, axis=-1, keepdims=True)
    return scale * (unit_grad - jnp.mean(unit_grad, axis=-1, keepdims=True) - unit * along)


def true_positions(length, first, count, axis, kind):
    shape = (count, 1) if axis == 0 else (1, count)
    position = first + lax.broadcasted_iota(jnp.int32, shape, axis)
    patch = position < PATCHES
    if kind == "patch":
        return patch
    caption = (position >= PATCHES) & (position - PATCHES < length)
    return caption if kind == "caption" else patch | caption


def head_masks():
    lane = lax.broadcasted_iota(jnp.int32, (1, PAIR), 1)
    even = (lane < HEAD_DIM).astype(F32).astype(BF16)
    odd = (lane >= HEAD_DIM).astype(F32).astype(BF16)
    return lane < HEAD_DIM, even, odd


def split_pair(pair, even, odd):
    return jnp.concatenate([pair * even, pair * odd], axis=0)


def start_weights(info, first, refs, plan, blocks, sems):
    half = blocks.shape[1] // 2
    section, core, plane = info[first], info[first + 1], info[first + 2]
    for at, at_plane, steps in plan:
        here = section == at
        if at_plane is not None:
            here = here & (plane == at_plane)

        @pl.when(here)
        def _(steps=steps):
            for block, source in steps:
                if source[0] == "own":
                    _, which, row, column = source
                    width = blocks.shape[2]
                    for part in range(2):
                        pltpu.make_async_copy(
                            refs[which].at[
                                pl.ds(row + part * half, half), pl.ds(column, width)
                            ],
                            blocks.at[block, pl.ds(part * half, half)],
                            sems.at[block],
                        ).start()
                else:
                    _, mine, theirs, index = source
                    pltpu.make_async_copy(
                        refs[mine].at[index],
                        blocks.at[block, pl.ds(pl.multiple_of(core * half, half), half)],
                        sems.at[block],
                    ).start()
                    pltpu.make_async_copy(
                        refs[theirs].at[index],
                        blocks.at[block, pl.ds(pl.multiple_of((1 - core) * half, half), half)],
                        sems.at[block],
                    ).start()


def wait_block(blocks, block, sems):
    pltpu.make_async_copy(blocks.at[block], blocks.at[block], sems.at[block]).wait()


def store_turned(target, turned, columns, section, core):
    half = target.shape[0] // 2
    for piece in range(16):
        path, owner = (piece >> 2) & 1, piece & 3
        away = owner ^ section
        place = ((away & 1) << 1) | (away >> 1) if path == 0 else away
        row = ((piece >> 3) ^ core) * half + (place >> 1) * (half // 2)
        row = row + path * (half // 4) + (place & 1) * PIECE_ROWS
        target[pl.ds(pl.multiple_of(row, 16), PIECE_ROWS), columns] = turned[
            piece * PIECE_ROWS : (piece + 1) * PIECE_ROWS
        ]


def put_travel(refs, which, columns, left, right):
    half = left.shape[0] // 2
    for side in range(2):
        rows = dot_plain(left[side * half : (side + 1) * half], right).astype(BF16)
        refs[2 * side][which, :, columns] = rows[: half // 2]
        refs[2 * side + 1][which, :, columns] = rows[half // 2 :]


def attend_forward_kernel(plan, weight_count, merge, info, *refs):
    weights, refs = refs[:weight_count], refs[weight_count:]
    if merge:
        x_ref, before_ref, part_ref, outer_ref, gain_ref, shift_ref, bias_ref = refs[:7]
        y_ref, qkv_ref, mixed_ref, joined_ref, blocks, sems, joined = refs[7:]
    else:
        x_ref, gain_ref, shift_ref, bias_ref, next_gain_ref, next_shift_ref = refs[:6]
        y_ref, qkv_ref, mixed_ref, caption_ref, blocks, sems = refs[6:]
    item = pl.program_id(0)
    items = pl.num_programs(0)
    length = info[item]
    width = x_ref.shape[-1]

    @pl.when(item == 0)
    def _():
        start_weights(info, items, weights, plan, blocks, sems)

    cap = slice(CAP_FIRST, CAP_FIRST + CAP_ROWS)
    if merge:
        joined[...] = x_ref[0].astype(F32)
        branch = part_ref[0].astype(F32) + outer_ref[...]
        is_true = true_positions(length, CAP_FIRST, CAP_ROWS, 0, "caption")
        captions = before_ref[0, cap] + jnp.where(is_true, branch, 0.0)
        position = CAP_FIRST + lax.broadcasted_iota(jnp.int32, (CAP_ROWS, 1), 0)
        captions = captions.astype(BF16).astype(F32)
        joined[cap] = jnp.where(position < PATCHES, joined[cap], captions)
        x = joined[...]
        joined_ref[0] = x.astype(BF16)
    else:
        x = x_ref[0].astype(F32)
    unit, _ = norm_parts(x)
    normed = (unit * gain_ref[...] + shift_ref[...]).astype(BF16)

    @pl.when(item == 0)
    def _():
        for block in range(4):
            wait_block(blocks, block, sems)

    queries = dot_plain(normed, blocks[0]) + bias_ref[:, :width]
    qkv_ref[0, :, :width] = (queries * HEAD_DIM ** (-0.5)).astype(BF16)
    qkv_ref[0, :, width : 2 * width] = dot_plain(normed, blocks[1]).astype(BF16)
    values = dot_plain(normed, blocks[2]) + bias_ref[:, width : 2 * width]
    qkv_ref[0, :, 2 * width :] = values.astype(BF16)
    key_true = true_positions(length, 0, ROWS, 1, "all")
    low_half, even, odd = head_masks()
    ones = jnp.ones((ROWS, PAIR), BF16)

    def scores_of(pair):
        at = pair * PAIR
        q2 = qkv_ref[0, :, at : at + PAIR]
        k2 = qkv_ref[0, :, width + at : width + at + PAIR]
        return dot_last(split_pair(q2, even, odd), k2)

    ahead = [scores_of(0), scores_of(1)]
    for pair in range(HEADS // 2):
        at = pair * PAIR
        scores = jnp.where(key_true, ahead.pop(0), -1e9)
        if pair + 2 < HEADS // 2:
            ahead.append(scores_of(pair + 2))
        weight = jnp.exp(scores - jnp.max(scores, axis=-1, keepdims=True)).astype(BF16)
        v2 = qkv_ref[0, :, 2 * width + at : 2 * width + at + PAIR]
        summed = dot_plain(weight, jnp.concatenate([v2, ones], axis=1))
        top = jnp.where(low_half, summed[:ROWS, :PAIR], summed[ROWS:, :PAIR])
        below = jnp.where(low_half, summed[:ROWS, PAIR:], summed[ROWS:, PAIR:])
        mixed_ref[0, :, at : at + PAIR] = (top / below).astype(BF16)
    branch = dot_plain(mixed_ref[0], blocks[3]) + bias_ref[:, 2 * width :]
    row_true = true_positions(length, 0, ROWS, 0, "all")
    y = x + jnp.where(row_true, branch, 0.0)
    y_ref[0] = y.astype(y_ref.dtype)
    if not merge:
        unit, _ = norm_parts(y[cap])
        caption_ref[0] = (unit * next_gain_ref[...] + next_shift_ref[...]).astype(BF16)


def attend_backward_kernel(plan, weight_count, first, info, *refs):
    weights, refs = refs[:weight_count], refs[weight_count:]
    x_ref, gain_ref, shift_ref, qkv_ref, mixed_ref, grad_ref = refs[:6]
    if first:
        after_ref, next_gain_ref, *parts = refs[6:12]
        refs = refs[12:]
    else:
        refs = refs[6:]
    out_ref, gain_grad_ref, shift_grad_ref, bias_grad_ref = refs[:4]
    travel_refs = refs[4:8]
    if first:
        next_gain_grad_ref, next_shift_grad_ref, joined = refs[8], refs[9], refs[-1]
    else:
        caption_ref = refs[8]
    blocks, sems, normed_turned, mixed_turned, branch_all, projected, mixed_grad = refs[
        10 if first else 9 :
    ][:7]
    item = pl.program_id(0)
    items = pl.num_programs(0)
    length = info[item]
    section, core = info[items], info[items + 1]
    width = x_ref.shape[-1]
    here = pl.ds(pl.multiple_of(item * ROWS, ROWS), ROWS)
    cap = slice(CAP_FIRST, CAP_FIRST + CAP_ROWS)

    @pl.when(item == 0)
    def _():
        start_weights(info, items, weights, plan, blocks, sems)

    def add_to(ref, part):
        @pl.when(item == 0)
        def _():
            ref[...] = part

        @pl.when(item > 0)
        def _():
            ref[...] += part

    x = x_ref[0].astype(F32)
    unit, scale = norm_parts(x)
    normed = (unit * gain_ref[...] + shift_ref[...]).astype(BF16)
    incoming = grad_ref[0].astype(F32)
    if first:
        after_unit, after_scale = norm_parts(after_ref[0, cap])
        caption_grad = parts[0][...].astype(F32)
        for part in parts[1:]:
            caption_grad = caption_grad + part[...].astype(F32)
        joined[...] = incoming
        joined[cap] += norm_back(caption_grad, after_unit, after_scale, next_gain_ref[...])
        incoming = joined[...]
        add_to(next_gain_grad_ref, jnp.sum(caption_grad * after_unit, axis=0, keepdims=True))
        add_to(next_shift_grad_ref, jnp.sum(caption_grad, axis=0, keepdims=True))
    row_true = true_positions(length, 0, ROWS, 0, "all")
    branch = jnp.where(row_true, incoming, 0.0).astype(BF16)
    branch_all[here, :] = branch
    store_turned(normed_turned, normed.T, here, section, core)
    store_turned(mixed_turned, mixed_ref[0].T, here, section, core)

    @pl.when(item == 0)
    def _():
        for block in range(4):
            wait_block(blocks, block, sems)

    mixed_grad[...] = dot_last(branch, blocks[3]).astype(BF16)
    key_true = true_positions(length, 0, ROWS, 0, "all")
    _, even, odd = head_masks()

    def products_of(pair):
        at = pair * PAIR
        q2 = split_pair(qkv_ref[0, :, at : at + PAIR], even, odd)
        k2 = qkv_ref[0, :, width + at : width + at + PAIR]
        v2 = qkv_ref[0, :, 2 * width + at : 2 * width + at + PAIR]
        g2 = split_pair(mixed_grad[:, at : at + PAIR], even, odd)
        return q2, k2, g2, dot_last(k2, q2), dot_last(v2, g2)

    ahead = [products_of(0)]
    for pair in range(HEADS // 2):
        at = pair * PAIR
        q2, k2, g2, scores, weight_grad = ahead.pop(0)
        if pair + 1 < HEADS // 2:
            ahead.append(products_of(pair + 1))
        scores = jnp.where(key_true, scores, -1e9)
        weight = jnp.exp(scores - jnp.max(scores, axis=0, keepdims=True))
        weight = weight * (1.0 / jnp.sum(weight, axis=0, keepdims=True))
        product = weight * weight_grad
        along = jnp.sum(product, axis=0, keepdims=True)
        score_grad = (product - weight * along).astype(BF16)
        values_grad = dot_plain(weight.astype(BF16), g2).astype(BF16)
        keys_grad = dot_plain(score_grad, q2).astype(BF16)
        k2_split = split_pair(k2, even, odd)
        stacked = jnp.concatenate([score_grad[:, :ROWS], score_grad[:, ROWS:]], axis=0)
        queries_grad = dot_first(stacked, k2_split).astype(BF16)
        queries_grad = (queries_grad.astype(F32) * HEAD_DIM ** (-0.5)).astype(BF16)
        projected[here, at : at + PAIR] = queries_grad
        projected[here, width + at : width + at + PAIR] = keys_grad
        projected[here, 2 * width + at : 2 * width + at + PAIR] = values_grad
    normed_grad = dot_last(projected[here, :width], blocks[0])
    normed_grad += dot_last(projected[here, width : 2 * width], blocks[1])
    normed_grad += dot_last(projected[here, 2 * width :], blocks[2])
    out = (incoming + norm_back(normed_grad, unit, scale, gain_ref[...])).astype(BF16)
    out_ref[0] = out
    if not first:
        is_true = true_positions(length, CAP_FIRST, CAP_ROWS, 0, "caption")
        caption_ref[0] = jnp.where(is_true, out[cap].astype(F32), 0.0).astype(BF16)
    add_to(gain_grad_ref, jnp.sum(normed_grad * unit, axis=0, keepdims=True))
    add_to(shift_grad_ref, jnp.sum(normed_grad, axis=0, keepdims=True))

    @pl.when(item == items - 1)
    def _():
        for block in range(4):
            columns = slice(block * width, (block + 1) * width)
            left = normed_turned if block < 3 else mixed_turned
            right = projected[:, columns] if block < 3 else branch_all[...]
            put_travel(travel_refs, 0, columns, left, right)
        bias_grad_ref[:, :width] = column_sum(projected[:, :width])
        bias_grad_ref[:, width : 2 * width] = column_sum(projected[:, 2 * width :])
        bias_grad_ref[:, 2 * width :] = column_sum(branch_all[...])


SHORT = pl.CostEstimate(flops=0, bytes_accessed=100_000, transcendentals=0)
LONG = pl.CostEstimate(flops=30_000_000_000, bytes_accessed=30_000_000, transcendentals=0)
ANYWHERE = pl.BlockSpec(memory_space=pl.ANY)


def whole_block(shape):
    return pl.BlockSpec(shape, lambda step, info: (0,) * len(shape))


def item_block(shape):
    return pl.BlockSpec((1,) + shape[1:], lambda step, info: (step,) + (0,) * (len(shape) - 1))


def blocks_scratch(count, width):
    return [pltpu.VMEM((count, width, width), BF16), pltpu.SemaphoreType.DMA((count,))]


def attend_forward(x, info, weights, gain, shift, bias, merge=None, following=None):
    arrays, plan = weights
    items, _, width = x.shape
    row = whole_block((1, width))
    bias_row = whole_block((1, 3 * width))
    caption_shape = (items, CAP_ROWS, width)
    if merge is not None:
        before, part, outer = merge
        operands = (x, before, part, outer, gain, shift, bias)
        specs = [item_block(x.shape), item_block(x.shape), item_block(caption_shape)]
        specs += [row, row, row, bias_row]
        last_shape, kind, scratch = x.shape, BF16, [pltpu.VMEM((ROWS, width), F32)]
    else:
        operands = (x, gain, shift, bias, *following)
        specs = [item_block(x.shape), row, row, bias_row, row, row]
        last_shape, kind, scratch = caption_shape, F32, []
    return pl.pallas_call(
        partial(attend_forward_kernel, plan, len(arrays), merge is not None),
        grid_spec=pltpu.PrefetchScalarGridSpec(
            num_scalar_prefetch=1,
            grid=(items,),
            in_specs=[ANYWHERE] * len(arrays) + specs,
            out_specs=[
                item_block(x.shape),
                item_block((items, ROWS, 3 * width)),
                item_block((items, ROWS, width)),
                item_block(last_shape),
            ],
            scratch_shapes=blocks_scratch(4, width) + scratch,
        ),
        out_shape=[
            jax.ShapeDtypeStruct(x.shape, kind),
            jax.ShapeDtypeStruct((items, ROWS, 3 * width), BF16),
            jax.ShapeDtypeStruct((items, ROWS, width), BF16),
            jax.ShapeDtypeStruct(last_shape, BF16),
        ],
        compiler_params=pltpu.CompilerParams(vmem_limit_bytes=VMEM_BYTES),
        cost_estimate=SHORT,
        name="attend_forward",
    )(info, *arrays, *operands)


def attend_backward(x, info, weights, gain, shift, qkv, mixed, incoming, first=None):
    arrays, plan = weights
    items, _, width = x.shape
    half = width // 2
    row = whole_block((1, width))
    caption_shape = (items, CAP_ROWS, width)
    operands = (x, gain, shift, qkv, mixed, incoming)
    specs = [item_block(x.shape), row, row, item_block(qkv.shape), item_block(mixed.shape)]
    specs += [item_block(incoming.shape)]
    outs = [
        (item_block(x.shape), x.shape, BF16),
        (row, (1, width), F32),
        (row, (1, width), F32),
        (whole_block((1, 3 * width)), (1, 3 * width), F32),
    ]
    outs += [(whole_block((1, half // 2, 4 * width)), (1, half // 2, 4 * width), BF16)] * 4
    scratch = []
    if first is not None:
        after, next_gain, parts = first
        operands += (after, next_gain, *parts)
        caption_rows = pl.BlockSpec((CAP_ROWS, width), lambda step, info: (step, 0))
        specs += [item_block(after.shape), row] + [caption_rows] * 4
        outs += [(row, (1, width), F32)] * 2
        scratch = [pltpu.VMEM((ROWS, width), F32)]
    else:
        outs += [(item_block(caption_shape), caption_shape, BF16)]
    return pl.pallas_call(
        partial(attend_backward_kernel, plan, len(arrays), first is not None),
        grid_spec=pltpu.PrefetchScalarGridSpec(
            num_scalar_prefetch=1,
            grid=(items,),
            in_specs=[ANYWHERE] * len(arrays) + specs,
            out_specs=[spec for spec, _, _ in outs],
            scratch_shapes=blocks_scratch(4, width)
            + [
                pltpu.VMEM((width, items * ROWS), BF16),
                pltpu.VMEM((width, items * ROWS), BF16),
                pltpu.VMEM((items * ROWS, width), BF16),
                pltpu.VMEM((items * ROWS, 3 * width), BF16),
                pltpu.VMEM((ROWS, width), BF16),
            ]
            + scratch,
        ),
        out_shape=[jax.ShapeDtypeStruct(shape, kind) for _, shape, kind in outs],
        compiler_params=pltpu.CompilerParams(vmem_limit_bytes=VMEM_BYTES),
        cost_estimate=LONG,
        name="attend_backward",
    )(info, *arrays, *operands)


def normal_parts(u):
    t = pl.reciprocal(1.0 + 0.23164190 * jnp.abs(u), approx=True)
    bell = jnp.exp2((u * -0.7213475204444817) * u)
    poly = t * (
        0.127414796
        + t * (-0.142248368 + t * (0.7107068705 + t * (-0.7265760135 + t * 0.5307027145)))
    )
    tail = poly * bell
    return jnp.where(u < 0, tail, 1.0 - tail), bell


def inner_forward(normed, matrix, bias):
    inner = dot_plain(normed, matrix) + bias
    cumulative, bell = normal_parts(inner)
    slope = cumulative + (inner * 0.3989422804014327) * bell
    return (inner * cumulative).astype(BF16), slope.astype(BF16)


def expert_forward_kernel(plan, weight_count, count, kind, info, *refs):
    weights, refs = refs[:weight_count], refs[weight_count:]
    x_ref, gain_ref, shift_ref, inner_ref, outer_ref = refs[:5]
    y_ref, act_ref, slope_ref, blocks, sems, normed, total = refs[5:]
    step = pl.program_id(0)
    items, _, width = x_ref.shape

    @pl.when(step == 0)
    def _():
        start_weights(info, items, weights, plan, blocks, sems)
        for item in range(items):
            x = x_ref[item, :count].astype(BF16).astype(F32)
            unit, _ = norm_parts(x)
            normed[item * count : (item + 1) * count] = (
                unit * gain_ref[...] + shift_ref[...]
            ).astype(BF16)

    wait_block(blocks, step, sems)
    wait_block(blocks, step + 4, sems)
    for at in range(0, width, 256):
        columns = slice(at, at + 256)
        act, slope = inner_forward(normed[...], blocks[step, :, columns], inner_ref[:, columns])
        act_ref[:, columns] = act
        slope_ref[:, columns] = slope
    part = dot_plain(act_ref[...], blocks[step + 4])

    @pl.when(step == 0)
    def _():
        total[...] = part

    @pl.when(step > 0)
    def _():
        total[...] += part

    @pl.when(step == pl.num_programs(0) - 1)
    def _():
        for item in range(items):
            row_true = true_positions(info[item], 0, count, 0, kind)
            branch = total[item * count : (item + 1) * count] + outer_ref[...]
            x = x_ref[item, :count].astype(BF16).astype(F32)
            y_ref[item, :count] = (x + jnp.where(row_true, branch, 0.0)).astype(BF16)
            if count < ROWS:
                y_ref[item, count:] = jnp.zeros((ROWS - count, width), BF16)


def expert_backward_kernel(plan, weight_count, count, kind, info, *refs):
    weights, refs = refs[:weight_count], refs[weight_count:]
    x_ref, gain_ref, shift_ref, act_ref, slope_ref, grad_ref = refs[:6]
    out_ref, gain_grad_ref, shift_grad_ref, inner_grad_ref, outer_grad_ref = refs[6:11]
    travel_refs = refs[11:15]
    blocks, sems, normed_turned, branch_turned, branch, inner_all, total = refs[15:]
    step = pl.program_id(0)
    items, _, width = x_ref.shape
    section, core = info[items], info[items + 1]

    @pl.when(step == 0)
    def _():
        start_weights(info, items, weights, plan, blocks, sems)
        outer = None
        for item in range(items):
            here = slice(item * count, (item + 1) * count)
            unit, _ = norm_parts(x_ref[item, :count].astype(BF16).astype(F32))
            normed = (unit * gain_ref[...] + shift_ref[...]).astype(BF16)
            row_true = true_positions(info[item], 0, count, 0, kind)
            incoming = grad_ref[item, :count].astype(F32)
            masked = jnp.where(row_true, incoming, 0.0).astype(BF16)
            branch[here] = masked
            store_turned(normed_turned, normed.T, here, section, core)
            store_turned(branch_turned, masked.T, here, section, core)
            term = column_sum(masked)
            outer = term if outer is None else outer + term
        outer_grad_ref[...] = outer

    wait_block(blocks, step, sems)
    wait_block(blocks, step + 4, sems)
    for at in range(0, width, 256):
        columns = slice(at, at + 256)
        act_grad = dot_last(branch[...], blocks[step + 4, columns])
        inner = (slope_ref[:, columns].astype(F32) * act_grad).astype(BF16)
        inner_all[:, columns] = inner
        inner_grad_ref[:, columns] = column_sum(inner)
        put_travel(travel_refs, 0, columns, normed_turned, inner)
        put_travel(travel_refs, 1, columns, branch_turned, act_ref[:, columns])
    part = dot_last(inner_all[...], blocks[step])

    @pl.when(step == 0)
    def _():
        total[...] = part

    @pl.when(step > 0)
    def _():
        total[...] += part

    @pl.when(step == pl.num_programs(0) - 1)
    def _():
        gain_sum, shift_sum = None, None
        for item in range(items):
            unit, scale = norm_parts(x_ref[item, :count].astype(BF16).astype(F32))
            normed_grad = total[item * count : (item + 1) * count]
            gain_part = jnp.sum(normed_grad * unit, axis=0, keepdims=True)
            shift_part = jnp.sum(normed_grad, axis=0, keepdims=True)
            gain_sum = gain_part if gain_sum is None else gain_sum + gain_part
            shift_sum = shift_part if shift_sum is None else shift_sum + shift_part
            incoming = grad_ref[item, :count].astype(F32)
            hidden = incoming + norm_back(normed_grad, unit, scale, gain_ref[...])
            out_ref[item, :count] = hidden.astype(BF16)
            if count < ROWS:
                out_ref[item, count:] = grad_ref[item, count:]
        gain_grad_ref[...] = gain_sum
        shift_grad_ref[...] = shift_sum


def shared_forward_kernel(*refs):
    *rows_refs, inputs_ref, inner_ref, outputs_ref = refs[:7]
    *part_refs, normed, total = refs[7:]
    count = rows_refs[0].shape[0]
    step = pl.program_id(0)

    @pl.when(step == 0)
    def _():
        for index, ref in enumerate(rows_refs):
            normed[index * count : (index + 1) * count] = ref[...]
        total[...] = jnp.zeros_like(total)

    act, _ = inner_forward(normed[...], inputs_ref[...], inner_ref[...])
    total[...] += dot_plain(act, outputs_ref[...])

    @pl.when(step == pl.num_programs(0) - 1)
    def _():
        for index, ref in enumerate(part_refs):
            ref[...] = total[index * count : (index + 1) * count].astype(BF16)


def shared_backward_kernel(plan, weight_count, info, *refs):
    weights, refs = refs[:weight_count], refs[weight_count:]
    rows_refs, grad_refs, inner_ref = refs[:4], refs[4:8], refs[8]
    part_refs, (keep_ref, send_ref, inner_grad_ref, outer_grad_ref) = refs[9:13], refs[13:17]
    blocks, sems, normed, branch, matrix = refs[17:]
    count, width = rows_refs[0].shape
    half = width // 2
    first = info.shape[0] - 3
    core = info[first + 1]
    start_weights(info, first, weights, plan, blocks, sems)
    for index in range(SECTIONS):
        here = slice(index * count, (index + 1) * count)
        normed[here] = rows_refs[index][...]
        branch[here] = grad_refs[index][...]
    outer_grad_ref[...] = column_sum(grad_refs[0][...])
    wait_block(blocks, 0, sems)
    wait_block(blocks, 1, sems)
    part = None
    for at in range(0, width, 256):
        columns = slice(at, at + 256)
        act, slope = inner_forward(normed[...], blocks[0, :, columns], inner_ref[:, columns])
        act_grad = dot_last(branch[...], blocks[1, columns])
        inner = (slope.astype(F32) * act_grad).astype(BF16)
        inner_grad_ref[:, columns] = column_sum(inner)
        matrix[0, :, columns] = dot_first(normed[...], inner).astype(BF16)
        matrix[1, :, columns] = dot_first(branch[...], act).astype(BF16)
        term = dot_last(inner, blocks[0, :, columns])
        part = term if part is None else part + term
    for index, ref in enumerate(part_refs):
        ref[...] = part[index * count : (index + 1) * count].astype(BF16)
    quarter = half // 4
    for which in range(2):
        for group in range(4):
            columns = slice(group * width, (group + 1) * width)
            mine = pl.multiple_of(core * half, 16) + group * quarter
            other = pl.multiple_of((1 - core) * half, 16) + group * quarter
            keep_ref[which, :, columns] = matrix[which, pl.ds(pl.multiple_of(mine, 16), quarter)]
            send_ref[which, :, columns] = matrix[which, pl.ds(pl.multiple_of(other, 16), quarter)]


def chunk_columns(rows, width):
    return pl.BlockSpec((rows, width), lambda step, info: (0, step))


def expert_forward(x, info, weights, gain, shift, inner, outer, count, kind):
    arrays, plan = weights
    items, _, width = x.shape
    hidden = inner.shape[1]
    row = whole_block((1, width))
    return pl.pallas_call(
        partial(expert_forward_kernel, plan, len(arrays), count, kind),
        grid_spec=pltpu.PrefetchScalarGridSpec(
            num_scalar_prefetch=1,
            grid=(hidden // width,),
            in_specs=[ANYWHERE] * len(arrays)
            + [whole_block(x.shape), row, row, chunk_columns(1, width), row],
            out_specs=[
                whole_block((items, ROWS, width)),
                chunk_columns(items * count, width),
                chunk_columns(items * count, width),
            ],
            scratch_shapes=blocks_scratch(8, width)
            + [
                pltpu.VMEM((items * count, width), BF16),
                pltpu.VMEM((items * count, width), F32),
            ],
        ),
        out_shape=[
            jax.ShapeDtypeStruct((items, ROWS, width), BF16),
            jax.ShapeDtypeStruct((items * count, hidden), BF16),
            jax.ShapeDtypeStruct((items * count, hidden), BF16),
        ],
        compiler_params=pltpu.CompilerParams(vmem_limit_bytes=VMEM_BYTES),
        cost_estimate=SHORT,
        name="expert_forward_" + kind,
    )(info, *arrays, x, gain, shift, inner, outer)


def expert_backward(x, info, weights, gain, shift, act, slope, incoming, count, kind):
    arrays, plan = weights
    items, _, width = x.shape
    half = width // 2
    hidden = act.shape[1]
    row = whole_block((1, width))
    travel = pl.BlockSpec((2, half // 2, width), lambda step, info: (0, 0, step))
    return pl.pallas_call(
        partial(expert_backward_kernel, plan, len(arrays), count, kind),
        grid_spec=pltpu.PrefetchScalarGridSpec(
            num_scalar_prefetch=1,
            grid=(hidden // width,),
            in_specs=[ANYWHERE] * len(arrays)
            + [
                whole_block(x.shape),
                row,
                row,
                chunk_columns(items * count, width),
                chunk_columns(items * count, width),
                whole_block(incoming.shape),
            ],
            out_specs=[whole_block(incoming.shape), row, row, chunk_columns(1, width), row]
            + [travel] * 4,
            scratch_shapes=blocks_scratch(8, width)
            + [
                pltpu.VMEM((width, items * count), BF16),
                pltpu.VMEM((width, items * count), BF16),
                pltpu.VMEM((items * count, width), BF16),
                pltpu.VMEM((items * count, width), BF16),
                pltpu.VMEM((items * count, width), F32),
            ],
        ),
        out_shape=[
            jax.ShapeDtypeStruct(incoming.shape, BF16),
            jax.ShapeDtypeStruct((1, width), F32),
            jax.ShapeDtypeStruct((1, width), F32),
            jax.ShapeDtypeStruct((1, hidden), F32),
            jax.ShapeDtypeStruct((1, width), F32),
        ]
        + [jax.ShapeDtypeStruct((2, half // 2, hidden), BF16)] * 4,
        compiler_params=pltpu.CompilerParams(vmem_limit_bytes=VMEM_BYTES),
        cost_estimate=SHORT,
        name="expert_backward_" + kind,
    )(info, *arrays, x, gain, shift, act, slope, incoming)


IN_VMEM = pl.BlockSpec(memory_space=pltpu.VMEM)
IN_SMEM = pl.BlockSpec(memory_space=pltpu.SMEM)


def shared_forward(rows, inputs, inner, outputs):
    count, width = rows[0].shape
    total = SECTIONS * count
    hidden = inner.shape[1]
    return pl.pallas_call(
        shared_forward_kernel,
        grid=(hidden // width,),
        in_specs=[pl.BlockSpec(rows[0].shape, lambda step: (0, 0))] * 4
        + [
            pl.BlockSpec((width, width), lambda step: (0, step)),
            pl.BlockSpec((1, width), lambda step: (0, step)),
            pl.BlockSpec((width, width), lambda step: (step, 0)),
        ],
        out_specs=[pl.BlockSpec((count, width), lambda step: (0, 0))] * SECTIONS,
        scratch_shapes=[pltpu.VMEM((total, width), BF16), pltpu.VMEM((total, width), F32)],
        out_shape=[jax.ShapeDtypeStruct((count, width), BF16)] * SECTIONS,
        compiler_params=pltpu.CompilerParams(vmem_limit_bytes=VMEM_BYTES),
        cost_estimate=SHORT,
        name="shared_forward",
    )(*rows, inputs, inner, outputs)


def shared_backward(rows, grads, info, weights, inner):
    arrays, plan = weights
    count, width = rows[0].shape
    total = SECTIONS * count
    travel = (2, width // 8, 4 * width)
    return pl.pallas_call(
        partial(shared_backward_kernel, plan, len(arrays)),
        in_specs=[IN_SMEM] + [ANYWHERE] * len(arrays) + [IN_VMEM] * 9,
        out_specs=[IN_VMEM] * 8,
        scratch_shapes=blocks_scratch(2, width)
        + [
            pltpu.VMEM((total, width), BF16),
            pltpu.VMEM((total, width), BF16),
            pltpu.VMEM((2, width, width), BF16),
        ],
        out_shape=[
            *[jax.ShapeDtypeStruct((count, width), BF16)] * SECTIONS,
            jax.ShapeDtypeStruct(travel, BF16),
            jax.ShapeDtypeStruct(travel, BF16),
            jax.ShapeDtypeStruct((1, width), F32),
            jax.ShapeDtypeStruct((1, width), F32),
        ],
        compiler_params=pltpu.CompilerParams(vmem_limit_bytes=VMEM_BYTES),
        cost_estimate=SHORT,
        name="shared_backward",
    )(info, *arrays, *rows, *grads, inner)


def plane_turn(plane, planes):
    return ((plane & 1) << 1) | (plane >> 1) if planes == 4 else 0


def finish_kernel(planes, info, scale_ref, mine_ref, theirs_ref, *refs):
    step = pl.program_id(0)
    count = mine_ref.shape[1]
    placed = refs[-1]
    outs = refs[:-1]
    width = placed.shape[1]
    half = width // 2
    at = info.shape[0] - 3
    section, core = info[at], info[at + 1]
    turn = plane_turn(info[at + 2], planes)
    turned = turn if count == 1 else jnp.where(section == 1, turn, 0)
    scale = scale_ref[0, 0]
    columns = pl.ds(pl.multiple_of((step ^ turned) * width, width), width)

    def place(which):
        def by_rows():
            for side, ref in enumerate((mine_ref, theirs_ref)):
                for away in range(SECTIONS):
                    for path in range(2):
                        row = (core ^ side) * half + path * (half // 2)
                        row = row + (section ^ away) * PIECE_ROWS
                        placed[pl.ds(pl.multiple_of(row, 16), PIECE_ROWS), :] = ref[
                            away, which, path * PIECE_ROWS : (path + 1) * PIECE_ROWS, columns
                        ].astype(F32)

        def by_columns():
            for side, ref in enumerate((mine_ref, theirs_ref)):
                for group in range(4):
                    quarter = half // 4
                    row = (core ^ side) * half + group * quarter
                    placed[pl.ds(pl.multiple_of(row, 16), quarter), :] = ref[
                        step, which, :, group * width : (group + 1) * width
                    ].astype(F32)

        if count == 1:
            by_rows()
        else:
            pl.when(section != 0)(by_rows)
            pl.when(section == 0)(by_columns)

    place(0)
    if count == 1:

        @pl.when(step < 3)
        def _():
            outs[0][0] = placed[...] / scale

        @pl.when(step == 3)
        def _():
            outs[1][0] = placed[...] / scale

    else:
        outs[0][0] = placed[...] / scale
        place(1)
        outs[1][0] = (placed[...] / scale).T


def finish(info, scale, mine, theirs, planes):
    count, hidden = mine.shape[1], mine.shape[3]
    width = hidden // 4
    if count == 1:
        shapes = [(1, width, 3 * width), (1, width, width)]
        maps = [lambda step, info: (0, 0, jnp.minimum(step, 2)), lambda step, info: (0, 0, 0)]
    else:
        shapes = [(1, width, hidden), (1, hidden, width)]
        maps = [lambda step, info: (0, 0, step), lambda step, info: (0, step, 0)]
    return pl.pallas_call(
        partial(finish_kernel, planes),
        grid_spec=pltpu.PrefetchScalarGridSpec(
            num_scalar_prefetch=1,
            grid=(4,),
            in_specs=[IN_SMEM, whole_block(mine.shape), whole_block(mine.shape)],
            out_specs=[pl.BlockSpec((1, width, width), at) for at in maps],
            scratch_shapes=[pltpu.VMEM((width, width), F32)],
        ),
        out_shape=[jax.ShapeDtypeStruct(shape, F32) for shape in shapes],
        compiler_params=pltpu.CompilerParams(vmem_limit_bytes=VMEM_BYTES),
        cost_estimate=SHORT,
        name="finish",
    )(info, scale, mine, theirs)


def pack_kernel(count, plan, info, *refs):
    sources, outs, sems = refs[:count], refs[count:-1], refs[-1]
    first = info.shape[0] - 3
    section, core, plane = info[first], info[first + 1], info[first + 2]
    half = outs[0].shape[1]
    for index, (out, choices) in enumerate(zip(outs, plan)):
        for at, at_plane, parts in choices:
            here = section == at
            if at_plane is not None:
                here = here & (plane == at_plane)

            @pl.when(here)
            def _(index=index, out=out, parts=parts):
                for block, part in enumerate(parts):
                    if part[0] == "own":
                        _, which, row, column = part
                        rows = pl.ds(pl.multiple_of(row + core * half, half), half)
                        source = sources[which].at[rows, pl.ds(column, out.shape[2])]
                    else:
                        source = sources[part[1]].at[block]
                    pltpu.make_async_copy(source, out.at[block], sems.at[index, block]).start()

    for index, out in enumerate(outs):
        for block in range(2):
            pltpu.make_async_copy(out.at[block], out.at[block], sems.at[index, block]).wait()


def pack(info, sources, plan, shape):
    return pl.pallas_call(
        partial(pack_kernel, len(sources), plan),
        in_specs=[IN_SMEM] + [ANYWHERE] * len(sources),
        out_specs=[IN_VMEM] * len(plan),
        scratch_shapes=[pltpu.SemaphoreType.DMA((len(plan), 2))],
        out_shape=[jax.ShapeDtypeStruct(shape, BF16)] * len(plan),
        cost_estimate=SHORT,
        name="pack",
    )(info, *sources)


def over_section(value, bits, sources=range(SECTIONS)):
    return lax.ppermute(value, "section", [(at, at ^ bits) for at in sources])


def over_core(value):
    return lax.ppermute(value, "core", [(0, 1), (1, 0)])


def over_plane(value, pairs):
    return lax.ppermute(value, "z", pairs)


def added(left, right):
    return (left.astype(F32) + right.astype(F32)).astype(BF16)


def after(value, *earlier):
    return lax.optimization_barrier((value,) + earlier)[0]


def by_section(section, values):
    result, last = None, None
    for at in sorted(values):
        if result is None:
            result = values[at]
        elif values[at] is not last:
            result = jnp.where(section >= at, values[at], result)
        last = values[at]
    return result


def total(*values):
    result = values[0].astype(F32)
    for value in values[1:]:
        result = result + value.astype(F32)
    return result.astype(BF16)


class Sums:
    def __init__(self, travel):
        self.stay, self.move, self.other_stay, self.other_move = travel
        self.size = self.stay.shape[1] // 2

    def cross(self, *earlier):
        if earlier:
            self.other_move = after(self.other_move, *earlier)
            self.other_stay = after(self.other_stay, *earlier)
        self.got_move, self.got_stay = over_core(self.other_move), over_core(self.other_stay)

    def first_sends(self):
        size = self.size
        self.sent = [
            total(self.move[:, at : at + size], self.got_move[:, at : at + size])
            for at in (0, size)
        ]
        return self.sent

    def second_sends(self, from_x, from_y):
        size, half = self.size, self.size // 2
        self.first = from_x, from_y
        to_y = total(self.stay[:, half:size], self.got_stay[:, half:size], from_x[:, half:])
        to_x = total(
            self.stay[:, size + half :], self.got_stay[:, size + half :], from_y[:, half:]
        )
        self.sent = [to_x, to_y]
        return self.sent

    def whole(self, from_x, from_y):
        size, half = self.size, self.size // 2
        parts = []
        for at, first, second in ((0, self.first[0], from_y), (size, self.first[1], from_x)):
            here = slice(at, at + half)
            parts.append(total(self.stay[:, here], self.got_stay[:, here], first[:, :half], second))
        return jnp.concatenate(parts, axis=1)


def over_links(sends):
    return [over_section(sends[0], 1), over_section(sends[1], 2)]


class Planes:
    def __init__(self, value, plane, planes):
        self.value, self.plane, self.planes, self.turn = value, plane, planes, 0

    def sends(self, *earlier):
        value = after(self.value, *earlier) if earlier else self.value
        if self.planes != 4:
            return (value,)
        bits = (1, 2, 2, 1)[self.turn]
        if self.turn < 2:
            bit = (self.plane & 1, self.plane >> 1)[self.turn]
            size = value.shape[-1] // 2
            value = lax.dynamic_slice_in_dim(value, (1 - bit) * size, size, value.ndim - 1)
        return (over_plane(value, [(at, at ^ bits) for at in range(4)]),)

    def take(self, arrived):
        if self.planes != 4:
            self.value = lax.psum(arrived, "z") if self.turn == 3 else arrived
        elif self.turn < 2:
            bit = (self.plane & 1, self.plane >> 1)[self.turn]
            size = self.value.shape[-1] // 2
            keep = lax.dynamic_slice_in_dim(self.value, bit * size, size, self.value.ndim - 1)
            self.value = added(keep, arrived)
        else:
            self.value = jnp.concatenate([self.value, arrived], axis=-1)
        self.turn += 1

    def in_order(self, value):
        if self.planes != 4:
            return value
        size, turn = value.shape[-1] // 4, plane_turn(self.plane, 4)
        parts = [
            lax.dynamic_slice_in_dim(value, (at ^ turn) * size, size, value.ndim - 1)
            for at in range(4)
        ]
        return jnp.concatenate(parts, axis=-1)


class Weights:
    def __init__(self, own, info, planes):
        self.own, self.info = own, info
        self.four = planes == 4
        self.plan = PLAN_FOUR if self.four else PLAN_ANY
        self.half, self.width = own[1].shape[0] // 2, own[1].shape[1]
        self.mine, self.theirs, self.arrived = {}, {}, {}

    def place(self, layer, block):
        if layer in "ac":
            return (0, 0, block * self.width) if block < 3 else (1, 0, 0)
        if layer == "g":
            return (2, 0, block * self.width) if block < 4 else (3, (block - 4) * self.width, 0)
        return (2, 0, block * self.width) if block < 4 else (3, (block - 4) * self.width, 0)

    def choices(self, sends, sources):
        result = []
        for at in range(SECTIONS):
            name = sends.get(at)
            if name is not None and HOMES[name[0]] != at:
                key = self.arrived[at, name]
                if key not in sources:
                    sources[key] = len(self.own) + len(sources)
                result.append((at, None, [("arrived", sources[key])] * 2))
                continue
            for plane in range(4) if name == "F" else (None,):
                piece = ("f" + str(plane)) if name == "F" else name or "a0"
                layer, index = piece[0], int(piece[1])
                if layer in "ac":
                    blocks = ATTEND_BLOCKS[index]
                else:
                    blocks = (index, 4 + index) if layer == "g" else EXPERT_BLOCKS[index]
                parts = [("own",) + self.place(layer, block) for block in blocks]
                result.append((at, plane, parts))
        return result

    def packed(self, wanted, *earlier):
        sources = {}
        plan = [self.choices(sends, sources) for sends in wanted]
        info = after(self.info, *earlier) if earlier else self.info
        arrays = list(self.own) + [self.mine[key] for key in sources]
        return pack(info, arrays, plan, (2, self.half, self.width))

    def run_step(self, step, *earlier):
        links = [(link, sends) for link, sends in enumerate(self.plan[step]) if sends]
        payloads = self.packed([sends for _, sends in links], *earlier)
        for (link, sends), payload in zip(links, payloads):
            self.mine[step, link] = over_section(payload, link + 1, sorted(sends))
        for link, sends in links:
            for at, name in sends.items():
                self.arrived[at ^ (link + 1), name] = (step, link)
        return payloads

    def run_planes(self, step, *earlier):
        if not self.four:
            return ()
        if step == 1:
            self.mine["plane", 0] = self.packed([{at: "F" for at in range(SECTIONS)}], *earlier)[0]
            earlier = ()
        up, down = self.mine["plane", step - 1], self.mine["plane", 1 - step]
        if earlier:
            up, down = after(up, *earlier), after(down, *earlier)
        up = over_plane(up, [(at, at + 1) for at in range(step - 1, 3)])
        down = over_plane(down, [(at, at - 1) for at in range(4 - step, 0, -1)])
        self.mine["plane", step], self.mine["plane", -step] = up, down
        return up, down

    def hand_over(self, steps, *earlier):
        for key in [key for key in self.mine if key[0] in steps and key not in self.theirs]:
            mine = after(self.mine[key], *earlier) if earlier else self.mine[key]
            self.theirs[key] = over_core(mine)
        return [self.theirs[key] for key in self.theirs if key[0] in steps]

    def set_mine(self, keys, values):
        for key, value in zip(keys, values):
            self.mine[key] = value

    def layer(self, layer):
        arrays, places = list(self.own), {}

        def place(key):
            if key not in self.theirs:
                self.theirs[key] = over_core(self.mine[key])
            if key not in places:
                places[key] = len(arrays)
                arrays.extend([self.mine[key], self.theirs[key]])
            return places[key], places[key] + 1

        if layer in "ac":
            names = [(layer + str(index), ATTEND_BLOCKS[index]) for index in range(2)]
        else:
            names = [(layer + str(index), EXPERT_BLOCKS[index]) for index in range(4)]
        plan = []
        for at in range(SECTIONS):
            if layer == "g":
                names = [("g" + str(at), (0, 1))]
            if HOMES[layer] == at:
                steps = []
                for name, blocks in names:
                    for block in blocks:
                        source = block * 4 if layer == "g" else block
                        steps.append((block, ("own",) + self.place(layer, source)))
                plan.append((at, None, steps))
                continue
            by_plane = layer == "f" and self.four
            for plane in range(4) if by_plane else (None,):
                steps = []
                for index, (name, blocks) in enumerate(names):
                    key = ("plane", plane - index) if by_plane else self.arrived[at, name]
                    for which, block in enumerate(blocks):
                        steps.append((block, ("piece",) + place(key) + (which,)))
                plan.append((at, plane, steps))
        return arrays, plan


def per_device(
    tokens,
    caption_lengths,
    attend_gain,
    attend_shift,
    attend_inputs,
    attend_bias,
    attend_output,
    expert_gain,
    expert_shift,
    expert_inputs,
    expert_inner_bias,
    expert_outputs,
    expert_outer_bias,
    cotangent,
):
    section, core, plane = lax.axis_index("section"), lax.axis_index("core"), lax.axis_index("z")
    planes = lax.axis_size("z")
    items, positions, width = tokens.shape
    hidden = expert_inputs.shape[-1]
    info = [value.reshape(1).astype(jnp.int32) for value in (section, core, plane)]
    info = jnp.concatenate([caption_lengths] + info)
    weights = Weights(
        (attend_inputs[0], attend_output[0], expert_inputs[0], expert_outputs[0]), info, planes
    )

    def to_sections(value):
        return [value] + [over_section(value, bits) for bits in (1, 2, 3)]

    def items_of(part):
        return part.reshape(items, CAP_ROWS, width)

    def under(outputs, *arrivals):
        joined = lax.optimization_barrier(tuple(outputs) + arrivals)
        return joined[: len(outputs)], joined[len(outputs) :]

    weights.run_step(0)
    pad = ((0, 0), (0, ROWS - positions), (0, 0))
    x0 = jnp.pad(tokens, pad)
    last_grad = jnp.pad(cotangent, pad)
    rows = jnp.concatenate(
        [
            attend_gain,
            attend_shift,
            attend_bias,
            expert_gain,
            expert_shift,
            expert_inner_bias,
            expert_outer_bias,
            jnp.full((1, 128), jnp.sum(caption_lengths), F32),
        ],
        axis=1,
    )
    rows = jnp.concatenate(to_sections(rows), axis=0)
    language_count = jnp.sum(rows[:, -128:], axis=0, keepdims=True)
    language_count = language_count + over_core(language_count)
    if planes == 4:
        language_count = language_count + over_plane(language_count, [(at, at ^ 1) for at in range(4)])
        language_count = language_count + over_plane(language_count, [(at, at ^ 2) for at in range(4)])
    else:
        language_count = lax.psum(language_count, "z")
    language_count = language_count[0, 0].astype(jnp.int32)
    vision_count = PATCHES * items * SECTIONS * 2 * planes
    counts = jnp.stack(
        [jnp.full((), vision_count, jnp.int32), language_count, language_count + vision_count]
    )
    rows = [lax.dynamic_index_in_dim(rows, at ^ section, 0) for at in range(SECTIONS)]
    sizes = [width, width, 3 * width, width, width, hidden, width]
    ends = [sum(sizes[: at + 1]) for at in range(len(sizes))]

    def row(slot, which):
        return rows[slot][:, ends[which] - sizes[which] : ends[which]]

    used = [(0, 0), (0, 1), (0, 2), (0, 3), (0, 4), (0, 5), (1, 3), (1, 4), (1, 5), (1, 6)]
    used += [(0, 6), (2, 0), (2, 1), (2, 2), (3, 3), (3, 4), (3, 5), (3, 6)]
    kept = lax.optimization_barrier(tuple(row(*at) for at in used) + (x0, last_grad, counts))
    x0, last_grad, counts = kept[-3:]
    kept = dict(zip(used, kept))

    def row(slot, which):
        return kept[slot, which]

    weights.run_step(1)
    handed = weights.hand_over((0,))
    sent = weights.run_step(2, *kept.values(), x0, last_grad, counts, *handed)
    weights.hand_over((1,), *sent)
    info = after(info, *weights.hand_over((0, 1)))
    attend0 = weights.layer("a")
    y0, qkv0, mixed0, caption_rows = attend_forward(
        x0, info, attend0, row(0, 0), row(0, 1), row(0, 2), following=(row(0, 3), row(0, 4))
    )
    caption_rows = to_sections(caption_rows.reshape(-1, width))
    sent = weights.run_step(EARLY_STEPS, caption_rows[0])
    weights.hand_over((2,), *sent)
    weights.run_planes(1, *sent)
    late_keys = [key for key in weights.mine if key[0] == EARLY_STEPS]
    outputs = shared_forward(caption_rows, expert_inputs[0], expert_inner_bias, expert_outputs[0])
    if weights.four:
        late_keys += [("plane", 1), ("plane", -1)]
    part, moved = under(outputs, *[weights.mine[key] for key in late_keys])
    weights.set_mine(late_keys, moved)
    branch = {at: over_section(part[at], at, [0]) for at in range(1, SECTIONS)}
    branch[0] = part[0]
    weights.run_planes(2, *part)
    expert1 = weights.layer("e")
    outputs = expert_forward(
        y0, info, expert1, row(1, 3), row(1, 4), row(1, 5), row(1, 6), PATCH_ROWS, "patch"
    )
    if weights.four:
        last_moved = [("plane", 2), ("plane", -2)]
    else:
        last_moved = []
        for step in range(EARLY_STEPS + 1, len(weights.plan)):
            weights.run_step(step, *part)
    (x2, act1, slope1), moved = under(outputs, *[weights.mine[key] for key in last_moved])
    weights.set_mine(last_moved, moved)
    branch = items_of(by_section(section, branch))
    attend2 = weights.layer("c")
    weights.run_planes(3, x2)
    outputs = attend_forward(
        x2, info, attend2, row(2, 0), row(2, 1), row(2, 2), merge=(y0, branch, row(0, 6))
    )
    last_moved = [("plane", 3), ("plane", -3)] if weights.four else []
    (x3, qkv2, mixed2, x2), moved = under(outputs, *[weights.mine[key] for key in last_moved])
    weights.set_mine(last_moved, moved)
    expert3 = weights.layer("f")
    layer_output, act3, slope3 = expert_forward(
        x3, info, expert3, row(3, 3), row(3, 4), row(3, 5), row(3, 6), ROWS, "all"
    )

    def small_rows(values):
        flat = jnp.concatenate(values, axis=1)
        count = -(-flat.shape[1] // hidden)
        flat = jnp.pad(flat, ((0, 0), (0, count * hidden - flat.shape[1])))
        return flat.reshape(count, hidden)

    def to_home(sums):
        got = [by_section(section, sums)]
        for bits in (1, 2, 3):
            sends = {at ^ bits: sums[at] for at in sums}
            got.append(over_section(by_section(section, sends), bits, sorted(sends)))
        return got

    last_moved = []
    if weights.four:
        weights.run_step(EARLY_STEPS + 1, x3)
        last_moved = [key for key in weights.mine if key[0] == EARLY_STEPS + 1]
    outputs = expert_backward(
        x3, info, expert3, row(3, 3), row(3, 4), act3, slope3, last_grad, ROWS, "all"
    )
    outputs, moved = under(outputs, *[weights.mine[key] for key in last_moved])
    weights.set_mine(last_moved, moved)
    handed = weights.hand_over((EARLY_STEPS + 1,)) if weights.four else []
    grad3, *small3 = outputs[:5]
    sums3 = Sums(outputs[5:])
    sums3.cross()
    moved = over_links(sums3.first_sends())
    grad3 = after(grad3, *sums3.sent)
    outputs = attend_backward(
        x2, info, attend2, row(2, 0), row(2, 1), qkv2, mixed2, grad3
    )
    outputs, moved = under(outputs, *moved, sums3.got_stay, *handed)
    grad2, *small2 = outputs[:4]
    sums2, caption_grad = Sums(outputs[4:8]), outputs[8]
    caption_grads = to_sections(caption_grad.reshape(-1, width))
    sums3.got_stay = moved[2]
    moved3 = over_links(sums3.second_sends(*moved[:2]))
    grad2 = after(grad2, *sums3.sent)
    outputs = expert_backward(
        y0, info, expert1, row(1, 3), row(1, 4), act1, slope1, grad2, PATCH_ROWS, "patch"
    )
    outputs, caption_grads = under(outputs, *caption_grads)
    grad1, *small1 = outputs[:5]
    sums2.cross(grad1)
    sums1 = Sums(outputs[5:])
    sums1.cross()
    inner_quarter = lax.dynamic_slice(row(0, 5), (0, section * width), (1, width))
    sum3 = sums3.whole(*moved3)
    inner_quarter = after(inner_quarter, grad1, sum3)
    outputs = shared_backward(
        caption_rows, caption_grads, info, weights.layer("g"), inner_quarter
    )
    parts, (keep0, send0, inner_grad, outer_grad) = outputs[:4], outputs[4:]
    got = [over_section(parts[bits], bits) for bits in (1, 2, 3)]
    sends = [after(value, *parts) for value in sums1.first_sends()]
    moved1 = over_links(sends)
    keep0 = added(keep0, over_core(send0))
    early = lax.psum(jnp.concatenate([sum3, keep0], axis=0), "z")
    sends2 = [after(value, *sends) for value in sums2.first_sends()]
    moved2 = over_links(sends2)
    parts = [parts[0], *got]
    grad1 = after(grad1, keep0, *sends, *sends2)
    outputs = attend_backward(
        x0,
        info,
        attend0,
        row(0, 0),
        row(0, 1),
        qkv0,
        mixed0,
        grad1,
        first=(y0, row(0, 3), parts),
    )
    outputs, moved = under(outputs, *moved2, *moved1)
    moved2, moved1 = moved[:2], moved[2:]
    tokens_grad, *small_first = outputs[:4]
    sums_first, gain_grad, shift_grad = Sums(outputs[4:8]), outputs[8], outputs[9]
    sums_first.cross()
    moved1 = over_links(sums1.second_sends(*moved1))
    sends = [after(value, *sums1.sent) for value in sums_first.first_sends()]
    moved = over_links(sends)
    moved1 = [after(value, *sends) for value in moved1]
    sum1 = sums1.whole(*moved1)
    planes1 = Planes(sum1, plane, planes)
    planes1.take(*planes1.sends())
    inner_grad = lax.dynamic_update_slice(
        jnp.zeros((1, hidden), F32), inner_grad, (0, section * width)
    )
    small = small_rows(
        small_first + [gain_grad, shift_grad, inner_grad, outer_grad] + small2 + small1 + small3
    )
    small = sum(to_sections(after(small, *moved1, *sends)))
    sums2.second_sends(*moved2)
    sums_first.second_sends(*moved)
    sends = [jnp.concatenate(pair, axis=0) for pair in zip(sums_first.sent, sums2.sent)]
    moved = over_links(sends)
    last = sums_first.whole(*[value[:1] for value in moved])
    sum2 = sums2.whole(*[value[1:] for value in moved])
    small = (small + over_core(after(small, *sends))).astype(BF16)
    small_count = small.shape[0]
    planes_last = Planes(
        jnp.concatenate([last[0], sum2[0], small], axis=0), plane, planes
    )
    planes_last.take(*planes_last.sends())
    planes1.take(*planes1.sends())
    planes1.take(*planes1.sends())
    home_early = to_home({0: after(early[2:], planes_last.value), 3: after(early[:2], planes_last.value)})
    planes1.take(*planes1.sends())
    planes_last.take(*planes_last.sends())
    planes_last.take(*planes_last.sends())
    home_late = to_home({1: after(planes1.value, *home_early[1:3])})
    planes_last.take(*planes_last.sends())
    eighth = last.shape[1]
    last = after(planes_last.value, home_early[3])
    home_attend = to_home({0: last[None, :eighth], 2: last[None, eighth : 2 * eighth]})
    small = planes_last.in_order(last[2 * eighth :].astype(F32))

    as_float = counts.astype(F32)
    one = jnp.ones((), F32)
    attend_scales = jnp.stack([as_float[2], one, as_float[2], one])
    expert_scales = jnp.stack([as_float[1], as_float[0], one, as_float[2]])

    def placed(pieces, scales):
        scale = lax.dynamic_index_in_dim(scales, section, 0).reshape(1, 1)
        pieces = jnp.stack(pieces)
        return finish(info, scale, pieces, over_core(pieces), planes)

    blank = jnp.zeros_like(home_late[0])
    inputs_whole, outputs_whole = placed(
        [
            by_section(section, {0: early, 1: late, 2: blank, 3: early})
            for early, late in zip(home_early, home_late)
        ],
        expert_scales,
    )
    blank = jnp.zeros_like(home_attend[0])
    attend_whole, output_whole = placed(
        [by_section(section, {0: got, 1: blank, 2: got, 3: blank}) for got in home_attend],
        attend_scales,
    )

    attend_size, expert_size = 5 * width, 3 * width + hidden
    cuts = [attend_size, attend_size + expert_size]
    cuts += [cuts[1] + attend_size, cuts[1] + attend_size + expert_size]
    small = jnp.split(small.reshape(-1)[: cuts[3] + expert_size], cuts)
    none_attend, none_expert = jnp.zeros_like(small[0]), jnp.zeros_like(small[1])
    attend_small = jnp.stack([small[0], none_attend, small[2], none_attend])
    expert_small = jnp.stack([small[1], small[3], none_expert, small[4]])
    attend_small = attend_small / attend_scales.reshape(-1, 1)
    expert_small = expert_small / expert_scales.reshape(-1, 1)
    attend_small = lax.dynamic_index_in_dim(attend_small, section, 0)
    expert_small = lax.dynamic_index_in_dim(expert_small, section, 0)
    return (
        layer_output[:, :positions],
        tokens_grad[:, :positions],
        attend_small[:, :width],
        attend_small[:, width : 2 * width],
        attend_whole,
        attend_small[:, 2 * width :],
        output_whole,
        expert_small[:, :width],
        expert_small[:, width : 2 * width],
        inputs_whole,
        expert_small[:, 2 * width : 2 * width + hidden],
        outputs_whole,
        expert_small[:, 2 * width + hidden :],
        counts,
    )


def solution(mesh):
    sections, groups = mesh.shape["section"], mesh.shape["dp"]
    split = Mesh(mesh.devices.reshape(sections, groups // 2, 2), ("section", "z", "core"))
    items = P(("section", "z", "core"), None, None)
    flat = P("section", None)
    matrix = P("section", None, None)
    placed = (
        items,
        P(("section", "z", "core")),
        flat,
        flat,
        matrix,
        flat,
        matrix,
        flat,
        flat,
        matrix,
        flat,
        matrix,
        flat,
        items,
    )
    return jax.shard_map(
        per_device,
        mesh=split,
        in_specs=placed,
        out_specs=(
            items,
            items,
            flat,
            flat,
            matrix,
            flat,
            matrix,
            flat,
            flat,
            matrix,
            flat,
            matrix,
            flat,
            P(),
        ),
        check_vma=False,
    )
```

```python
from functools import partial

import jax
import jax.numpy as jnp
from jax import lax
from jax.experimental import pallas as pl
from jax.experimental.pallas import tpu as pltpu
from jax.sharding import Mesh
from jax.sharding import PartitionSpec as P

HEADS = 12
HEAD_DIM = 64
PATCHES = 197
ROWS = 256
CAP_FIRST, CAP_ROWS = 192, 48
PATCH_ROWS = 208
PAIR = 2 * HEAD_DIM
SECTIONS = 4
PIECE_ROWS = 48
VMEM_BYTES = 58 * 1024 * 1024
F32 = jnp.float32
BF16 = jnp.bfloat16

PLAN_FOUR = (
    ({0: "a0", 1: "e0", 2: "c0", 3: "F"}, {0: "a1", 1: "e2", 2: "c0", 3: "F"}),
    ({0: "a1", 1: "e1", 2: "a1", 3: "e2"}, {0: "a0", 1: "a0", 2: "F", 3: "c0"}),
    ({0: "g3", 1: "e2", 2: "c1"}, {0: "e0", 1: "e3", 2: "c1"}),
    ({0: "g1", 1: "e3", 2: "e0", 3: "e3"}, {0: "e1", 1: "e1", 3: "c1"}),
    ({}, {0: "g2", 1: "g3"}),
)
PLAN_ANY = (
    ({0: "a0", 1: "e0", 2: "c0", 3: "f0"}, {0: "a1", 1: "e2", 2: "c0", 3: "f0"}),
    ({0: "a1", 1: "e1", 2: "a1", 3: "e2"}, {0: "a0", 1: "a0", 2: "c1", 3: "f1"}),
    ({0: "g3", 1: "e2", 2: "c1", 3: "f1"}, {0: "e0", 1: "e3", 2: "f0", 3: "f2"}),
    ({0: "g1", 1: "e3", 2: "e0", 3: "e3"}, {0: "e1", 1: "e1", 2: "f1", 3: "f3"}),
    ({0: "c1", 1: "f2", 3: "f2"}, {0: "g2", 1: "g3", 3: "c0"}),
    ({1: "f3", 3: "f3"}, {}),
)
EARLY_STEPS = 3
HOMES = {"a": 0, "c": 2, "e": 1, "f": 3, "F": 3, "g": 0}
ATTEND_BLOCKS = ((0, 1), (2, 3))
EXPERT_BLOCKS = ((0, 1), (4, 5), (2, 3), (6, 7))


def dot_plain(left, right):
    return jnp.dot(left, right, preferred_element_type=F32)


def dot_last(left, right):
    return lax.dot_general(left, right, (((1,), (1,)), ((), ())), preferred_element_type=F32)


def dot_first(left, right):
    return lax.dot_general(left, right, (((0,), (0,)), ((), ())), preferred_element_type=F32)


def column_sum(matrix):
    return jnp.sum(matrix.astype(F32), axis=0, keepdims=True)


def norm_parts(rows):
    centre = rows - jnp.mean(rows, axis=-1, keepdims=True)
    scale = lax.rsqrt(jnp.mean(centre * centre, axis=-1, keepdims=True) + 1e-06)
    return centre * scale, scale


def norm_back(normed_grad, unit, scale, gain):
    unit_grad = normed_grad * gain
    along = jnp.mean(unit_grad * unit, axis=-1, keepdims=True)
    return scale * (unit_grad - jnp.mean(unit_grad, axis=-1, keepdims=True) - unit * along)


def true_positions(length, first, count, axis, kind):
    shape = (count, 1) if axis == 0 else (1, count)
    position = first + lax.broadcasted_iota(jnp.int32, shape, axis)
    patch = position < PATCHES
    if kind == "patch":
        return patch
    caption = (position >= PATCHES) & (position - PATCHES < length)
    return caption if kind == "caption" else patch | caption


def head_masks():
    lane = lax.broadcasted_iota(jnp.int32, (1, PAIR), 1)
    even = (lane < HEAD_DIM).astype(F32).astype(BF16)
    odd = (lane >= HEAD_DIM).astype(F32).astype(BF16)
    return lane < HEAD_DIM, even, odd


def split_pair(pair, even, odd):
    return jnp.concatenate([pair * even, pair * odd], axis=0)


def start_weights(info, first, refs, plan, blocks, sems):
    half = blocks.shape[1] // 2
    section, core, plane = info[first], info[first + 1], info[first + 2]
    for at, at_plane, steps in plan:
        here = section == at
        if at_plane is not None:
            here = here & (plane == at_plane)

        @pl.when(here)
        def _(steps=steps):
            for block, source in steps:
                if source[0] == "own":
                    _, which, row, column = source
                    width = blocks.shape[2]
                    for part in range(2):
                        pltpu.make_async_copy(
                            refs[which].at[
                                pl.ds(row + part * half, half), pl.ds(column, width)
                            ],
                            blocks.at[block, pl.ds(part * half, half)],
                            sems.at[block],
                        ).start()
                else:
                    _, mine, theirs, index = source
                    pltpu.make_async_copy(
                        refs[mine].at[index],
                        blocks.at[block, pl.ds(pl.multiple_of(core * half, half), half)],
                        sems.at[block],
                    ).start()
                    pltpu.make_async_copy(
                        refs[theirs].at[index],
                        blocks.at[block, pl.ds(pl.multiple_of((1 - core) * half, half), half)],
                        sems.at[block],
                    ).start()


def wait_block(blocks, block, sems):
    pltpu.make_async_copy(blocks.at[block], blocks.at[block], sems.at[block]).wait()


def store_turned(target, turned, columns, section, core):
    half = target.shape[0] // 2
    for piece in range(16):
        path, owner = (piece >> 2) & 1, piece & 3
        away = owner ^ section
        place = ((away & 1) << 1) | (away >> 1) if path == 0 else away
        row = ((piece >> 3) ^ core) * half + (place >> 1) * (half // 2)
        row = row + path * (half // 4) + (place & 1) * PIECE_ROWS
        target[pl.ds(pl.multiple_of(row, 16), PIECE_ROWS), columns] = turned[
            piece * PIECE_ROWS : (piece + 1) * PIECE_ROWS
        ]


def put_travel(refs, which, columns, left, right):
    half = left.shape[0] // 2
    for side in range(2):
        rows = dot_plain(left[side * half : (side + 1) * half], right).astype(BF16)
        refs[2 * side][which, :, columns] = rows[: half // 2]
        refs[2 * side + 1][which, :, columns] = rows[half // 2 :]


def attend_forward_kernel(plan, weight_count, merge, info, *refs):
    weights, refs = refs[:weight_count], refs[weight_count:]
    if merge:
        x_ref, before_ref, part_ref, outer_ref, gain_ref, shift_ref, bias_ref = refs[:7]
        y_ref, qkv_ref, mixed_ref, joined_ref, blocks, sems, joined = refs[7:]
    else:
        x_ref, gain_ref, shift_ref, bias_ref, next_gain_ref, next_shift_ref = refs[:6]
        y_ref, qkv_ref, mixed_ref, caption_ref, blocks, sems = refs[6:]
    item = pl.program_id(0)
    items = pl.num_programs(0)
    length = info[item]
    width = x_ref.shape[-1]

    @pl.when(item == 0)
    def _():
        start_weights(info, items, weights, plan, blocks, sems)

    cap = slice(CAP_FIRST, CAP_FIRST + CAP_ROWS)
    if merge:
        joined[...] = x_ref[0].astype(F32)
        branch = part_ref[0].astype(F32) + outer_ref[...]
        is_true = true_positions(length, CAP_FIRST, CAP_ROWS, 0, "caption")
        captions = before_ref[0, cap] + jnp.where(is_true, branch, 0.0)
        position = CAP_FIRST + lax.broadcasted_iota(jnp.int32, (CAP_ROWS, 1), 0)
        captions = captions.astype(BF16).astype(F32)
        joined[cap] = jnp.where(position < PATCHES, joined[cap], captions)
        x = joined[...]
        joined_ref[0] = x.astype(BF16)
    else:
        x = x_ref[0].astype(F32)
    unit, _ = norm_parts(x)
    normed = (unit * gain_ref[...] + shift_ref[...]).astype(BF16)

    @pl.when(item == 0)
    def _():
        for block in range(4):
            wait_block(blocks, block, sems)

    queries = dot_plain(normed, blocks[0]) + bias_ref[:, :width]
    qkv_ref[0, :, :width] = (queries * HEAD_DIM ** (-0.5)).astype(BF16)
    qkv_ref[0, :, width : 2 * width] = dot_plain(normed, blocks[1]).astype(BF16)
    values = dot_plain(normed, blocks[2]) + bias_ref[:, width : 2 * width]
    qkv_ref[0, :, 2 * width :] = values.astype(BF16)
    key_true = true_positions(length, 0, ROWS, 1, "all")
    low_half, even, odd = head_masks()
    ones = jnp.ones((ROWS, PAIR), BF16)

    def scores_of(pair):
        at = pair * PAIR
        q2 = qkv_ref[0, :, at : at + PAIR]
        k2 = qkv_ref[0, :, width + at : width + at + PAIR]
        return dot_last(split_pair(q2, even, odd), k2)

    ahead = [scores_of(0), scores_of(1)]
    for pair in range(HEADS // 2):
        at = pair * PAIR
        scores = jnp.where(key_true, ahead.pop(0), -1e9)
        if pair + 2 < HEADS // 2:
            ahead.append(scores_of(pair + 2))
        weight = jnp.exp(scores - jnp.max(scores, axis=-1, keepdims=True)).astype(BF16)
        v2 = qkv_ref[0, :, 2 * width + at : 2 * width + at + PAIR]
        summed = dot_plain(weight, jnp.concatenate([v2, ones], axis=1))
        top = jnp.where(low_half, summed[:ROWS, :PAIR], summed[ROWS:, :PAIR])
        below = jnp.where(low_half, summed[:ROWS, PAIR:], summed[ROWS:, PAIR:])
        mixed_ref[0, :, at : at + PAIR] = (top / below).astype(BF16)
    branch = dot_plain(mixed_ref[0], blocks[3]) + bias_ref[:, 2 * width :]
    row_true = true_positions(length, 0, ROWS, 0, "all")
    y = x + jnp.where(row_true, branch, 0.0)
    y_ref[0] = y.astype(y_ref.dtype)
    if not merge:
        unit, _ = norm_parts(y[cap])
        caption_ref[0] = (unit * next_gain_ref[...] + next_shift_ref[...]).astype(BF16)


def attend_backward_kernel(plan, weight_count, first, info, *refs):
    weights, refs = refs[:weight_count], refs[weight_count:]
    x_ref, gain_ref, shift_ref, qkv_ref, mixed_ref, grad_ref = refs[:6]
    if first:
        after_ref, next_gain_ref, *parts = refs[6:12]
        refs = refs[12:]
    else:
        refs = refs[6:]
    out_ref, gain_grad_ref, shift_grad_ref, bias_grad_ref = refs[:4]
    travel_refs = refs[4:8]
    if first:
        next_gain_grad_ref, next_shift_grad_ref, joined = refs[8], refs[9], refs[-1]
    else:
        caption_ref = refs[8]
    blocks, sems, normed_turned, mixed_turned, branch_all, projected, mixed_grad = refs[
        10 if first else 9 :
    ][:7]
    item = pl.program_id(0)
    items = pl.num_programs(0)
    length = info[item]
    section, core = info[items], info[items + 1]
    width = x_ref.shape[-1]
    here = pl.ds(pl.multiple_of(item * ROWS, ROWS), ROWS)
    cap = slice(CAP_FIRST, CAP_FIRST + CAP_ROWS)

    @pl.when(item == 0)
    def _():
        start_weights(info, items, weights, plan, blocks, sems)

    def add_to(ref, part):
        @pl.when(item == 0)
        def _():
            ref[...] = part

        @pl.when(item > 0)
        def _():
            ref[...] += part

    x = x_ref[0].astype(F32)
    unit, scale = norm_parts(x)
    normed = (unit * gain_ref[...] + shift_ref[...]).astype(BF16)
    incoming = grad_ref[0].astype(F32)
    if first:
        after_unit, after_scale = norm_parts(after_ref[0, cap])
        caption_grad = parts[0][...].astype(F32)
        for part in parts[1:]:
            caption_grad = caption_grad + part[...].astype(F32)
        joined[...] = incoming
        joined[cap] += norm_back(caption_grad, after_unit, after_scale, next_gain_ref[...])
        incoming = joined[...]
        add_to(next_gain_grad_ref, jnp.sum(caption_grad * after_unit, axis=0, keepdims=True))
        add_to(next_shift_grad_ref, jnp.sum(caption_grad, axis=0, keepdims=True))
    row_true = true_positions(length, 0, ROWS, 0, "all")
    branch = jnp.where(row_true, incoming, 0.0).astype(BF16)
    branch_all[here, :] = branch
    store_turned(normed_turned, normed.T, here, section, core)
    store_turned(mixed_turned, mixed_ref[0].T, here, section, core)

    @pl.when(item == 0)
    def _():
        for block in range(4):
            wait_block(blocks, block, sems)

    mixed_grad[...] = dot_last(branch, blocks[3]).astype(BF16)
    key_true = true_positions(length, 0, ROWS, 0, "all")
    _, even, odd = head_masks()

    def products_of(pair):
        at = pair * PAIR
        q2 = split_pair(qkv_ref[0, :, at : at + PAIR], even, odd)
        k2 = qkv_ref[0, :, width + at : width + at + PAIR]
        v2 = qkv_ref[0, :, 2 * width + at : 2 * width + at + PAIR]
        g2 = split_pair(mixed_grad[:, at : at + PAIR], even, odd)
        return q2, k2, g2, dot_last(k2, q2), dot_last(v2, g2)

    ahead = [products_of(0)]
    for pair in range(HEADS // 2):
        at = pair * PAIR
        q2, k2, g2, scores, weight_grad = ahead.pop(0)
        if pair + 1 < HEADS // 2:
            ahead.append(products_of(pair + 1))
        scores = jnp.where(key_true, scores, -1e9)
        weight = jnp.exp(scores - jnp.max(scores, axis=0, keepdims=True))
        weight = weight * (1.0 / jnp.sum(weight, axis=0, keepdims=True))
        product = weight * weight_grad
        along = jnp.sum(product, axis=0, keepdims=True)
        score_grad = (product - weight * along).astype(BF16)
        values_grad = dot_plain(weight.astype(BF16), g2).astype(BF16)
        keys_grad = dot_plain(score_grad, q2).astype(BF16)
        k2_split = split_pair(k2, even, odd)
        stacked = jnp.concatenate([score_grad[:, :ROWS], score_grad[:, ROWS:]], axis=0)
        queries_grad = dot_first(stacked, k2_split).astype(BF16)
        queries_grad = (queries_grad.astype(F32) * HEAD_DIM ** (-0.5)).astype(BF16)
        projected[here, at : at + PAIR] = queries_grad
        projected[here, width + at : width + at + PAIR] = keys_grad
        projected[here, 2 * width + at : 2 * width + at + PAIR] = values_grad
    normed_grad = dot_last(projected[here, :width], blocks[0])
    normed_grad += dot_last(projected[here, width : 2 * width], blocks[1])
    normed_grad += dot_last(projected[here, 2 * width :], blocks[2])
    out = (incoming + norm_back(normed_grad, unit, scale, gain_ref[...])).astype(BF16)
    out_ref[0] = out
    if not first:
        is_true = true_positions(length, CAP_FIRST, CAP_ROWS, 0, "caption")
        caption_ref[0] = jnp.where(is_true, out[cap].astype(F32), 0.0).astype(BF16)
    add_to(gain_grad_ref, jnp.sum(normed_grad * unit, axis=0, keepdims=True))
    add_to(shift_grad_ref, jnp.sum(normed_grad, axis=0, keepdims=True))

    @pl.when(item == items - 1)
    def _():
        for block in range(4):
            columns = slice(block * width, (block + 1) * width)
            left = normed_turned if block < 3 else mixed_turned
            right = projected[:, columns] if block < 3 else branch_all[...]
            put_travel(travel_refs, 0, columns, left, right)
        bias_grad_ref[:, :width] = column_sum(projected[:, :width])
        bias_grad_ref[:, width : 2 * width] = column_sum(projected[:, 2 * width :])
        bias_grad_ref[:, 2 * width :] = column_sum(branch_all[...])


SHORT = pl.CostEstimate(flops=0, bytes_accessed=100_000, transcendentals=0)
ANYWHERE = pl.BlockSpec(memory_space=pl.ANY)


def whole_block(shape):
    return pl.BlockSpec(shape, lambda step, info: (0,) * len(shape))


def item_block(shape):
    return pl.BlockSpec((1,) + shape[1:], lambda step, info: (step,) + (0,) * (len(shape) - 1))


def blocks_scratch(count, width):
    return [pltpu.VMEM((count, width, width), BF16), pltpu.SemaphoreType.DMA((count,))]


def attend_forward(x, info, weights, gain, shift, bias, merge=None, following=None):
    arrays, plan = weights
    items, _, width = x.shape
    row = whole_block((1, width))
    bias_row = whole_block((1, 3 * width))
    caption_shape = (items, CAP_ROWS, width)
    if merge is not None:
        before, part, outer = merge
        operands = (x, before, part, outer, gain, shift, bias)
        specs = [item_block(x.shape), item_block(x.shape), item_block(caption_shape)]
        specs += [row, row, row, bias_row]
        last_shape, kind, scratch = x.shape, BF16, [pltpu.VMEM((ROWS, width), F32)]
    else:
        operands = (x, gain, shift, bias, *following)
        specs = [item_block(x.shape), row, row, bias_row, row, row]
        last_shape, kind, scratch = caption_shape, F32, []
    return pl.pallas_call(
        partial(attend_forward_kernel, plan, len(arrays), merge is not None),
        grid_spec=pltpu.PrefetchScalarGridSpec(
            num_scalar_prefetch=1,
            grid=(items,),
            in_specs=[ANYWHERE] * len(arrays) + specs,
            out_specs=[
                item_block(x.shape),
                item_block((items, ROWS, 3 * width)),
                item_block((items, ROWS, width)),
                item_block(last_shape),
            ],
            scratch_shapes=blocks_scratch(4, width) + scratch,
        ),
        out_shape=[
            jax.ShapeDtypeStruct(x.shape, kind),
            jax.ShapeDtypeStruct((items, ROWS, 3 * width), BF16),
            jax.ShapeDtypeStruct((items, ROWS, width), BF16),
            jax.ShapeDtypeStruct(last_shape, BF16),
        ],
        compiler_params=pltpu.CompilerParams(vmem_limit_bytes=VMEM_BYTES),
        cost_estimate=SHORT,
        name="attend_forward",
    )(info, *arrays, *operands)


def attend_backward(x, info, weights, gain, shift, qkv, mixed, incoming, first=None):
    arrays, plan = weights
    items, _, width = x.shape
    half = width // 2
    row = whole_block((1, width))
    caption_shape = (items, CAP_ROWS, width)
    operands = (x, gain, shift, qkv, mixed, incoming)
    specs = [item_block(x.shape), row, row, item_block(qkv.shape), item_block(mixed.shape)]
    specs += [item_block(incoming.shape)]
    outs = [
        (item_block(x.shape), x.shape, BF16),
        (row, (1, width), F32),
        (row, (1, width), F32),
        (whole_block((1, 3 * width)), (1, 3 * width), F32),
    ]
    outs += [(whole_block((1, half // 2, 4 * width)), (1, half // 2, 4 * width), BF16)] * 4
    scratch = []
    if first is not None:
        after, next_gain, parts = first
        operands += (after, next_gain, *parts)
        caption_rows = pl.BlockSpec((CAP_ROWS, width), lambda step, info: (step, 0))
        specs += [item_block(after.shape), row] + [caption_rows] * 4
        outs += [(row, (1, width), F32)] * 2
        scratch = [pltpu.VMEM((ROWS, width), F32)]
    else:
        outs += [(item_block(caption_shape), caption_shape, BF16)]
    return pl.pallas_call(
        partial(attend_backward_kernel, plan, len(arrays), first is not None),
        grid_spec=pltpu.PrefetchScalarGridSpec(
            num_scalar_prefetch=1,
            grid=(items,),
            in_specs=[ANYWHERE] * len(arrays) + specs,
            out_specs=[spec for spec, _, _ in outs],
            scratch_shapes=blocks_scratch(4, width)
            + [
                pltpu.VMEM((width, items * ROWS), BF16),
                pltpu.VMEM((width, items * ROWS), BF16),
                pltpu.VMEM((items * ROWS, width), BF16),
                pltpu.VMEM((items * ROWS, 3 * width), BF16),
                pltpu.VMEM((ROWS, width), BF16),
            ]
            + scratch,
        ),
        out_shape=[jax.ShapeDtypeStruct(shape, kind) for _, shape, kind in outs],
        compiler_params=pltpu.CompilerParams(vmem_limit_bytes=VMEM_BYTES),
        cost_estimate=SHORT,
        name="attend_backward",
    )(info, *arrays, *operands)


def normal_parts(u):
    t = pl.reciprocal(1.0 + 0.23164190 * jnp.abs(u), approx=True)
    bell = jnp.exp2((u * -0.7213475204444817) * u)
    poly = t * (
        0.127414796
        + t * (-0.142248368 + t * (0.7107068705 + t * (-0.7265760135 + t * 0.5307027145)))
    )
    tail = poly * bell
    return jnp.where(u < 0, tail, 1.0 - tail), bell


def inner_forward(normed, matrix, bias):
    inner = dot_plain(normed, matrix) + bias
    cumulative, bell = normal_parts(inner)
    slope = cumulative + (inner * 0.3989422804014327) * bell
    return (inner * cumulative).astype(BF16), slope.astype(BF16)


def expert_forward_kernel(plan, weight_count, count, kind, info, *refs):
    weights, refs = refs[:weight_count], refs[weight_count:]
    x_ref, gain_ref, shift_ref, inner_ref, outer_ref = refs[:5]
    y_ref, act_ref, slope_ref, blocks, sems, normed, total = refs[5:]
    step = pl.program_id(0)
    items, _, width = x_ref.shape

    @pl.when(step == 0)
    def _():
        start_weights(info, items, weights, plan, blocks, sems)
        for item in range(items):
            x = x_ref[item, :count].astype(BF16).astype(F32)
            unit, _ = norm_parts(x)
            normed[item * count : (item + 1) * count] = (
                unit * gain_ref[...] + shift_ref[...]
            ).astype(BF16)

    wait_block(blocks, step, sems)
    wait_block(blocks, step + 4, sems)
    for at in range(0, width, 256):
        columns = slice(at, at + 256)
        act, slope = inner_forward(normed[...], blocks[step, :, columns], inner_ref[:, columns])
        act_ref[:, columns] = act
        slope_ref[:, columns] = slope
    part = dot_plain(act_ref[...], blocks[step + 4])

    @pl.when(step == 0)
    def _():
        total[...] = part

    @pl.when(step > 0)
    def _():
        total[...] += part

    @pl.when(step == pl.num_programs(0) - 1)
    def _():
        for item in range(items):
            row_true = true_positions(info[item], 0, count, 0, kind)
            branch = total[item * count : (item + 1) * count] + outer_ref[...]
            x = x_ref[item, :count].astype(BF16).astype(F32)
            y_ref[item, :count] = (x + jnp.where(row_true, branch, 0.0)).astype(BF16)
            if count < ROWS:
                y_ref[item, count:] = jnp.zeros((ROWS - count, width), BF16)


def expert_backward_kernel(plan, weight_count, count, kind, info, *refs):
    weights, refs = refs[:weight_count], refs[weight_count:]
    x_ref, gain_ref, shift_ref, act_ref, slope_ref, grad_ref = refs[:6]
    out_ref, gain_grad_ref, shift_grad_ref, inner_grad_ref, outer_grad_ref = refs[6:11]
    travel_refs = refs[11:15]
    blocks, sems, normed_turned, branch_turned, branch, inner_all, total = refs[15:]
    step = pl.program_id(0)
    items, _, width = x_ref.shape
    section, core = info[items], info[items + 1]

    @pl.when(step == 0)
    def _():
        start_weights(info, items, weights, plan, blocks, sems)
        outer = None
        for item in range(items):
            here = slice(item * count, (item + 1) * count)
            unit, _ = norm_parts(x_ref[item, :count].astype(BF16).astype(F32))
            normed = (unit * gain_ref[...] + shift_ref[...]).astype(BF16)
            row_true = true_positions(info[item], 0, count, 0, kind)
            incoming = grad_ref[item, :count].astype(F32)
            masked = jnp.where(row_true, incoming, 0.0).astype(BF16)
            branch[here] = masked
            store_turned(normed_turned, normed.T, here, section, core)
            store_turned(branch_turned, masked.T, here, section, core)
            term = column_sum(masked)
            outer = term if outer is None else outer + term
        outer_grad_ref[...] = outer

    wait_block(blocks, step, sems)
    wait_block(blocks, step + 4, sems)
    for at in range(0, width, 256):
        columns = slice(at, at + 256)
        act_grad = dot_last(branch[...], blocks[step + 4, columns])
        inner = (slope_ref[:, columns].astype(F32) * act_grad).astype(BF16)
        inner_all[:, columns] = inner
        inner_grad_ref[:, columns] = column_sum(inner)
        put_travel(travel_refs, 0, columns, normed_turned, inner)
        put_travel(travel_refs, 1, columns, branch_turned, act_ref[:, columns])
    part = dot_last(inner_all[...], blocks[step])

    @pl.when(step == 0)
    def _():
        total[...] = part

    @pl.when(step > 0)
    def _():
        total[...] += part

    @pl.when(step == pl.num_programs(0) - 1)
    def _():
        gain_sum, shift_sum = None, None
        for item in range(items):
            unit, scale = norm_parts(x_ref[item, :count].astype(BF16).astype(F32))
            normed_grad = total[item * count : (item + 1) * count]
            gain_part = jnp.sum(normed_grad * unit, axis=0, keepdims=True)
            shift_part = jnp.sum(normed_grad, axis=0, keepdims=True)
            gain_sum = gain_part if gain_sum is None else gain_sum + gain_part
            shift_sum = shift_part if shift_sum is None else shift_sum + shift_part
            incoming = grad_ref[item, :count].astype(F32)
            hidden = incoming + norm_back(normed_grad, unit, scale, gain_ref[...])
            out_ref[item, :count] = hidden.astype(BF16)
            if count < ROWS:
                out_ref[item, count:] = grad_ref[item, count:]
        gain_grad_ref[...] = gain_sum
        shift_grad_ref[...] = shift_sum


def shared_forward_kernel(*refs):
    *rows_refs, inputs_ref, inner_ref, outputs_ref = refs[:7]
    *part_refs, normed, total = refs[7:]
    count = rows_refs[0].shape[0]
    step = pl.program_id(0)

    @pl.when(step == 0)
    def _():
        for index, ref in enumerate(rows_refs):
            normed[index * count : (index + 1) * count] = ref[...]
        total[...] = jnp.zeros_like(total)

    act, _ = inner_forward(normed[...], inputs_ref[...], inner_ref[...])
    total[...] += dot_plain(act, outputs_ref[...])

    @pl.when(step == pl.num_programs(0) - 1)
    def _():
        for index, ref in enumerate(part_refs):
            ref[...] = total[index * count : (index + 1) * count].astype(BF16)


def shared_backward_kernel(plan, weight_count, info, *refs):
    weights, refs = refs[:weight_count], refs[weight_count:]
    rows_refs, grad_refs, inner_ref = refs[:4], refs[4:8], refs[8]
    part_refs, (keep_ref, send_ref, inner_grad_ref, outer_grad_ref) = refs[9:13], refs[13:17]
    blocks, sems, normed, branch, matrix = refs[17:]
    count, width = rows_refs[0].shape
    half = width // 2
    first = info.shape[0] - 3
    core = info[first + 1]
    start_weights(info, first, weights, plan, blocks, sems)
    for index in range(SECTIONS):
        here = slice(index * count, (index + 1) * count)
        normed[here] = rows_refs[index][...]
        branch[here] = grad_refs[index][...]
    outer_grad_ref[...] = column_sum(grad_refs[0][...])
    wait_block(blocks, 0, sems)
    wait_block(blocks, 1, sems)
    part = None
    for at in range(0, width, 256):
        columns = slice(at, at + 256)
        act, slope = inner_forward(normed[...], blocks[0, :, columns], inner_ref[:, columns])
        act_grad = dot_last(branch[...], blocks[1, columns])
        inner = (slope.astype(F32) * act_grad).astype(BF16)
        inner_grad_ref[:, columns] = column_sum(inner)
        matrix[0, :, columns] = dot_first(normed[...], inner).astype(BF16)
        matrix[1, :, columns] = dot_first(branch[...], act).astype(BF16)
        term = dot_last(inner, blocks[0, :, columns])
        part = term if part is None else part + term
    for index, ref in enumerate(part_refs):
        ref[...] = part[index * count : (index + 1) * count].astype(BF16)
    quarter = half // 4
    for which in range(2):
        for group in range(4):
            columns = slice(group * width, (group + 1) * width)
            mine = pl.multiple_of(core * half, 16) + group * quarter
            other = pl.multiple_of((1 - core) * half, 16) + group * quarter
            keep_ref[which, :, columns] = matrix[which, pl.ds(pl.multiple_of(mine, 16), quarter)]
            send_ref[which, :, columns] = matrix[which, pl.ds(pl.multiple_of(other, 16), quarter)]


def chunk_columns(rows, width):
    return pl.BlockSpec((rows, width), lambda step, info: (0, step))


def expert_forward(x, info, weights, gain, shift, inner, outer, count, kind):
    arrays, plan = weights
    items, _, width = x.shape
    hidden = inner.shape[1]
    row = whole_block((1, width))
    return pl.pallas_call(
        partial(expert_forward_kernel, plan, len(arrays), count, kind),
        grid_spec=pltpu.PrefetchScalarGridSpec(
            num_scalar_prefetch=1,
            grid=(hidden // width,),
            in_specs=[ANYWHERE] * len(arrays)
            + [whole_block(x.shape), row, row, chunk_columns(1, width), row],
            out_specs=[
                whole_block((items, ROWS, width)),
                chunk_columns(items * count, width),
                chunk_columns(items * count, width),
            ],
            scratch_shapes=blocks_scratch(8, width)
            + [
                pltpu.VMEM((items * count, width), BF16),
                pltpu.VMEM((items * count, width), F32),
            ],
        ),
        out_shape=[
            jax.ShapeDtypeStruct((items, ROWS, width), BF16),
            jax.ShapeDtypeStruct((items * count, hidden), BF16),
            jax.ShapeDtypeStruct((items * count, hidden), BF16),
        ],
        compiler_params=pltpu.CompilerParams(vmem_limit_bytes=VMEM_BYTES),
        cost_estimate=SHORT,
        name="expert_forward_" + kind,
    )(info, *arrays, x, gain, shift, inner, outer)


def expert_backward(x, info, weights, gain, shift, act, slope, incoming, count, kind):
    arrays, plan = weights
    items, _, width = x.shape
    half = width // 2
    hidden = act.shape[1]
    row = whole_block((1, width))
    travel = pl.BlockSpec((2, half // 2, width), lambda step, info: (0, 0, step))
    return pl.pallas_call(
        partial(expert_backward_kernel, plan, len(arrays), count, kind),
        grid_spec=pltpu.PrefetchScalarGridSpec(
            num_scalar_prefetch=1,
            grid=(hidden // width,),
            in_specs=[ANYWHERE] * len(arrays)
            + [
                whole_block(x.shape),
                row,
                row,
                chunk_columns(items * count, width),
                chunk_columns(items * count, width),
                whole_block(incoming.shape),
            ],
            out_specs=[whole_block(incoming.shape), row, row, chunk_columns(1, width), row]
            + [travel] * 4,
            scratch_shapes=blocks_scratch(8, width)
            + [
                pltpu.VMEM((width, items * count), BF16),
                pltpu.VMEM((width, items * count), BF16),
                pltpu.VMEM((items * count, width), BF16),
                pltpu.VMEM((items * count, width), BF16),
                pltpu.VMEM((items * count, width), F32),
            ],
        ),
        out_shape=[
            jax.ShapeDtypeStruct(incoming.shape, BF16),
            jax.ShapeDtypeStruct((1, width), F32),
            jax.ShapeDtypeStruct((1, width), F32),
            jax.ShapeDtypeStruct((1, hidden), F32),
            jax.ShapeDtypeStruct((1, width), F32),
        ]
        + [jax.ShapeDtypeStruct((2, half // 2, hidden), BF16)] * 4,
        compiler_params=pltpu.CompilerParams(vmem_limit_bytes=VMEM_BYTES),
        cost_estimate=SHORT,
        name="expert_backward_" + kind,
    )(info, *arrays, x, gain, shift, act, slope, incoming)


IN_VMEM = pl.BlockSpec(memory_space=pltpu.VMEM)
IN_SMEM = pl.BlockSpec(memory_space=pltpu.SMEM)


def shared_forward(rows, inputs, inner, outputs):
    count, width = rows[0].shape
    total = SECTIONS * count
    hidden = inner.shape[1]
    return pl.pallas_call(
        shared_forward_kernel,
        grid=(hidden // width,),
        in_specs=[pl.BlockSpec(rows[0].shape, lambda step: (0, 0))] * 4
        + [
            pl.BlockSpec((width, width), lambda step: (0, step)),
            pl.BlockSpec((1, width), lambda step: (0, step)),
            pl.BlockSpec((width, width), lambda step: (step, 0)),
        ],
        out_specs=[pl.BlockSpec((count, width), lambda step: (0, 0))] * SECTIONS,
        scratch_shapes=[pltpu.VMEM((total, width), BF16), pltpu.VMEM((total, width), F32)],
        out_shape=[jax.ShapeDtypeStruct((count, width), BF16)] * SECTIONS,
        compiler_params=pltpu.CompilerParams(vmem_limit_bytes=VMEM_BYTES),
        cost_estimate=SHORT,
        name="shared_forward",
    )(*rows, inputs, inner, outputs)


def shared_backward(rows, grads, info, weights, inner):
    arrays, plan = weights
    count, width = rows[0].shape
    total = SECTIONS * count
    travel = (2, width // 8, 4 * width)
    return pl.pallas_call(
        partial(shared_backward_kernel, plan, len(arrays)),
        in_specs=[IN_SMEM] + [ANYWHERE] * len(arrays) + [IN_VMEM] * 9,
        out_specs=[IN_VMEM] * 8,
        scratch_shapes=blocks_scratch(2, width)
        + [
            pltpu.VMEM((total, width), BF16),
            pltpu.VMEM((total, width), BF16),
            pltpu.VMEM((2, width, width), BF16),
        ],
        out_shape=[
            *[jax.ShapeDtypeStruct((count, width), BF16)] * SECTIONS,
            jax.ShapeDtypeStruct(travel, BF16),
            jax.ShapeDtypeStruct(travel, BF16),
            jax.ShapeDtypeStruct((1, width), F32),
            jax.ShapeDtypeStruct((1, width), F32),
        ],
        compiler_params=pltpu.CompilerParams(vmem_limit_bytes=VMEM_BYTES),
        cost_estimate=SHORT,
        name="shared_backward",
    )(info, *arrays, *rows, *grads, inner)


def plane_turn(plane, planes):
    return ((plane & 1) << 1) | (plane >> 1) if planes == 4 else 0


def finish_kernel(planes, info, scale_ref, mine_ref, theirs_ref, *refs):
    step = pl.program_id(0)
    count = mine_ref.shape[1]
    placed = refs[-1]
    outs = refs[:-1]
    width = placed.shape[1]
    half = width // 2
    at = info.shape[0] - 3
    section, core = info[at], info[at + 1]
    turn = plane_turn(info[at + 2], planes)
    turned = 0 if count == 1 else jnp.where(section == 1, turn, 0)
    scale = scale_ref[0, 0]
    columns = pl.ds(pl.multiple_of((step ^ turned) * width, width), width)

    def place(which):
        def by_rows():
            for side, ref in enumerate((mine_ref, theirs_ref)):
                for away in range(SECTIONS):
                    for path in range(2):
                        row = (core ^ side) * half + path * (half // 2)
                        row = row + (section ^ away) * PIECE_ROWS
                        placed[pl.ds(pl.multiple_of(row, 16), PIECE_ROWS), :] = ref[
                            away, which, path * PIECE_ROWS : (path + 1) * PIECE_ROWS, columns
                        ].astype(F32)

        def by_columns():
            for side, ref in enumerate((mine_ref, theirs_ref)):
                for group in range(4):
                    quarter = half // 4
                    row = (core ^ side) * half + group * quarter
                    placed[pl.ds(pl.multiple_of(row, 16), quarter), :] = ref[
                        step, which, :, group * width : (group + 1) * width
                    ].astype(F32)

        if count == 1:
            by_rows()
        else:
            pl.when(section != 0)(by_rows)
            pl.when(section == 0)(by_columns)

    place(0)
    if count == 1:

        @pl.when(step < 3)
        def _():
            outs[0][0] = placed[...] / scale

        @pl.when(step == 3)
        def _():
            outs[1][0] = placed[...] / scale

    else:
        outs[0][0] = placed[...] / scale
        place(1)
        outs[1][0] = (placed[...] / scale).T


def finish(info, scale, mine, theirs, planes):
    count, hidden = mine.shape[1], mine.shape[3]
    width = hidden // 4
    if count == 1:
        shapes = [(1, width, 3 * width), (1, width, width)]
        maps = [lambda step, info: (0, 0, jnp.minimum(step, 2)), lambda step, info: (0, 0, 0)]
    else:
        shapes = [(1, width, hidden), (1, hidden, width)]
        maps = [lambda step, info: (0, 0, step), lambda step, info: (0, step, 0)]
    return pl.pallas_call(
        partial(finish_kernel, planes),
        grid_spec=pltpu.PrefetchScalarGridSpec(
            num_scalar_prefetch=1,
            grid=(4,),
            in_specs=[IN_SMEM, whole_block(mine.shape), whole_block(mine.shape)],
            out_specs=[pl.BlockSpec((1, width, width), at) for at in maps],
            scratch_shapes=[pltpu.VMEM((width, width), F32)],
        ),
        out_shape=[jax.ShapeDtypeStruct(shape, F32) for shape in shapes],
        compiler_params=pltpu.CompilerParams(vmem_limit_bytes=VMEM_BYTES),
        cost_estimate=SHORT,
        name="finish",
    )(info, scale, mine, theirs)


def pack_kernel(count, plan, info, *refs):
    sources, outs, sems = refs[:count], refs[count:-1], refs[-1]
    first = info.shape[0] - 3
    section, core, plane = info[first], info[first + 1], info[first + 2]
    half = outs[0].shape[1]
    for index, (out, choices) in enumerate(zip(outs, plan)):
        for at, at_plane, parts in choices:
            here = section == at
            if at_plane is not None:
                here = here & (plane == at_plane)

            @pl.when(here)
            def _(index=index, out=out, parts=parts):
                for block, part in enumerate(parts):
                    if part[0] == "own":
                        _, which, row, column = part
                        rows = pl.ds(pl.multiple_of(row + core * half, half), half)
                        source = sources[which].at[rows, pl.ds(column, out.shape[2])]
                    else:
                        source = sources[part[1]].at[block]
                    pltpu.make_async_copy(source, out.at[block], sems.at[index, block]).start()

    for index, out in enumerate(outs):
        for block in range(2):
            pltpu.make_async_copy(out.at[block], out.at[block], sems.at[index, block]).wait()


def pack(info, sources, plan, shape):
    return pl.pallas_call(
        partial(pack_kernel, len(sources), plan),
        in_specs=[IN_SMEM] + [ANYWHERE] * len(sources),
        out_specs=[IN_VMEM] * len(plan),
        scratch_shapes=[pltpu.SemaphoreType.DMA((len(plan), 2))],
        out_shape=[jax.ShapeDtypeStruct(shape, BF16)] * len(plan),
        cost_estimate=SHORT,
        name="pack",
    )(info, *sources)


def over_section(value, bits, sources=range(SECTIONS)):
    return lax.ppermute(value, "section", [(at, at ^ bits) for at in sources])


def over_core(value):
    return lax.ppermute(value, "core", [(0, 1), (1, 0)])


def over_plane(value, pairs):
    return lax.ppermute(value, "z", pairs)


def added(left, right):
    return (left.astype(F32) + right.astype(F32)).astype(BF16)


def after(value, *earlier):
    return lax.optimization_barrier((value,) + earlier)[0]


def by_section(section, values):
    result, last = None, None
    for at in sorted(values):
        if result is None:
            result = values[at]
        elif values[at] is not last:
            result = jnp.where(section >= at, values[at], result)
        last = values[at]
    return result


def total(*values):
    result = values[0].astype(F32)
    for value in values[1:]:
        result = result + value.astype(F32)
    return result.astype(BF16)


class Sums:
    def __init__(self, travel):
        self.stay, self.move, self.other_stay, self.other_move = travel
        self.size = self.stay.shape[1] // 2

    def cross(self, *earlier):
        if earlier:
            self.other_move = after(self.other_move, *earlier)
            self.other_stay = after(self.other_stay, *earlier)
        self.got_move, self.got_stay = over_core(self.other_move), over_core(self.other_stay)

    def first_sends(self):
        size = self.size
        self.sent = [
            total(self.move[:, at : at + size], self.got_move[:, at : at + size])
            for at in (0, size)
        ]
        return self.sent

    def second_sends(self, from_x, from_y):
        size, half = self.size, self.size // 2
        self.first = from_x, from_y
        to_y = total(self.stay[:, half:size], self.got_stay[:, half:size], from_x[:, half:])
        to_x = total(
            self.stay[:, size + half :], self.got_stay[:, size + half :], from_y[:, half:]
        )
        self.sent = [to_x, to_y]
        return self.sent

    def whole(self, from_x, from_y):
        size, half = self.size, self.size // 2
        parts = []
        for at, first, second in ((0, self.first[0], from_y), (size, self.first[1], from_x)):
            here = slice(at, at + half)
            parts.append(total(self.stay[:, here], self.got_stay[:, here], first[:, :half], second))
        return jnp.concatenate(parts, axis=1)


def over_links(sends):
    return [over_section(sends[0], 1), over_section(sends[1], 2)]


class Planes:
    def __init__(self, value, plane, planes):
        self.value, self.plane, self.planes, self.turn = value, plane, planes, 0

    def sends(self, *earlier):
        value = after(self.value, *earlier) if earlier else self.value
        if self.planes != 4:
            return (value,)
        bits = (1, 2, 2, 1)[self.turn]
        if self.turn < 2:
            bit = (self.plane & 1, self.plane >> 1)[self.turn]
            size = value.shape[-1] // 2
            value = lax.dynamic_slice_in_dim(value, (1 - bit) * size, size, value.ndim - 1)
        return (over_plane(value, [(at, at ^ bits) for at in range(4)]),)

    def take(self, arrived):
        if self.planes != 4:
            self.value = lax.psum(arrived, "z") if self.turn == 3 else arrived
        elif self.turn < 2:
            bit = (self.plane & 1, self.plane >> 1)[self.turn]
            size = self.value.shape[-1] // 2
            keep = lax.dynamic_slice_in_dim(self.value, bit * size, size, self.value.ndim - 1)
            self.value = added(keep, arrived)
        else:
            self.value = jnp.concatenate([self.value, arrived], axis=-1)
        self.turn += 1

    def in_order(self, value):
        if self.planes != 4:
            return value
        size, turn = value.shape[-1] // 4, plane_turn(self.plane, 4)
        parts = [
            lax.dynamic_slice_in_dim(value, (at ^ turn) * size, size, value.ndim - 1)
            for at in range(4)
        ]
        return jnp.concatenate(parts, axis=-1)


class Weights:
    def __init__(self, own, info, planes):
        self.own, self.info = own, info
        self.four = planes == 4
        self.plan = PLAN_FOUR if self.four else PLAN_ANY
        self.half, self.width = own[1].shape[0] // 2, own[1].shape[1]
        self.mine, self.theirs, self.arrived = {}, {}, {}

    def place(self, layer, block):
        if layer in "ac":
            return (0, 0, block * self.width) if block < 3 else (1, 0, 0)
        if layer == "g":
            return (2, 0, block * self.width) if block < 4 else (3, (block - 4) * self.width, 0)
        return (2, 0, block * self.width) if block < 4 else (3, (block - 4) * self.width, 0)

    def choices(self, sends, sources):
        result = []
        for at in range(SECTIONS):
            name = sends.get(at)
            if name is not None and HOMES[name[0]] != at:
                key = self.arrived[at, name]
                if key not in sources:
                    sources[key] = len(self.own) + len(sources)
                result.append((at, None, [("arrived", sources[key])] * 2))
                continue
            for plane in range(4) if name == "F" else (None,):
                piece = ("f" + str(plane)) if name == "F" else name or "a0"
                layer, index = piece[0], int(piece[1])
                if layer in "ac":
                    blocks = ATTEND_BLOCKS[index]
                else:
                    blocks = (index, 4 + index) if layer == "g" else EXPERT_BLOCKS[index]
                parts = [("own",) + self.place(layer, block) for block in blocks]
                result.append((at, plane, parts))
        return result

    def packed(self, wanted, *earlier):
        sources = {}
        plan = [self.choices(sends, sources) for sends in wanted]
        info = after(self.info, *earlier) if earlier else self.info
        arrays = list(self.own) + [self.mine[key] for key in sources]
        return pack(info, arrays, plan, (2, self.half, self.width))

    def run_step(self, step, *earlier):
        links = [(link, sends) for link, sends in enumerate(self.plan[step]) if sends]
        payloads = self.packed([sends for _, sends in links], *earlier)
        for (link, sends), payload in zip(links, payloads):
            self.mine[step, link] = over_section(payload, link + 1, sorted(sends))
        for link, sends in links:
            for at, name in sends.items():
                self.arrived[at ^ (link + 1), name] = (step, link)
        return payloads

    def run_planes(self, step, *earlier):
        if not self.four:
            return ()
        if step == 1:
            self.mine["plane", 0] = self.packed([{at: "F" for at in range(SECTIONS)}], *earlier)[0]
            earlier = ()
        up, down = self.mine["plane", step - 1], self.mine["plane", 1 - step]
        if earlier:
            up, down = after(up, *earlier), after(down, *earlier)
        up = over_plane(up, [(at, at + 1) for at in range(step - 1, 3)])
        down = over_plane(down, [(at, at - 1) for at in range(4 - step, 0, -1)])
        self.mine["plane", step], self.mine["plane", -step] = up, down
        return up, down

    def hand_over(self, steps, *earlier):
        for key in [key for key in self.mine if key[0] in steps and key not in self.theirs]:
            mine = after(self.mine[key], *earlier) if earlier else self.mine[key]
            self.theirs[key] = over_core(mine)
        return [self.theirs[key] for key in self.theirs if key[0] in steps]

    def set_mine(self, keys, values):
        for key, value in zip(keys, values):
            self.mine[key] = value

    def layer(self, layer):
        arrays, places = list(self.own), {}

        def place(key):
            if key not in self.theirs:
                self.theirs[key] = over_core(self.mine[key])
            if key not in places:
                places[key] = len(arrays)
                arrays.extend([self.mine[key], self.theirs[key]])
            return places[key], places[key] + 1

        if layer in "ac":
            names = [(layer + str(index), ATTEND_BLOCKS[index]) for index in range(2)]
        else:
            names = [(layer + str(index), EXPERT_BLOCKS[index]) for index in range(4)]
        plan = []
        for at in range(SECTIONS):
            if layer == "g":
                names = [("g" + str(at), (0, 1))]
            if HOMES[layer] == at:
                steps = []
                for name, blocks in names:
                    for block in blocks:
                        source = block * 4 if layer == "g" else block
                        steps.append((block, ("own",) + self.place(layer, source)))
                plan.append((at, None, steps))
                continue
            by_plane = layer == "f" and self.four
            for plane in range(4) if by_plane else (None,):
                steps = []
                for index, (name, blocks) in enumerate(names):
                    key = ("plane", plane - index) if by_plane else self.arrived[at, name]
                    for which, block in enumerate(blocks):
                        steps.append((block, ("piece",) + place(key) + (which,)))
                plan.append((at, plane, steps))
        return arrays, plan


def per_device(
    tokens,
    caption_lengths,
    attend_gain,
    attend_shift,
    attend_inputs,
    attend_bias,
    attend_output,
    expert_gain,
    expert_shift,
    expert_inputs,
    expert_inner_bias,
    expert_outputs,
    expert_outer_bias,
    cotangent,
):
    section, core, plane = lax.axis_index("section"), lax.axis_index("core"), lax.axis_index("z")
    planes = lax.axis_size("z")
    items, positions, width = tokens.shape
    hidden = expert_inputs.shape[-1]
    info = [value.reshape(1).astype(jnp.int32) for value in (section, core, plane)]
    info = jnp.concatenate([caption_lengths] + info)
    weights = Weights(
        (attend_inputs[0], attend_output[0], expert_inputs[0], expert_outputs[0]), info, planes
    )

    def to_sections(value):
        return [value] + [over_section(value, bits) for bits in (1, 2, 3)]

    def items_of(part):
        return part.reshape(items, CAP_ROWS, width)

    def under(outputs, *arrivals):
        joined = lax.optimization_barrier(tuple(outputs) + arrivals)
        return joined[: len(outputs)], joined[len(outputs) :]

    weights.run_step(0)
    pad = ((0, 0), (0, ROWS - positions), (0, 0))
    x0 = jnp.pad(tokens, pad)
    last_grad = jnp.pad(cotangent, pad)
    rows = jnp.concatenate(
        [
            attend_gain,
            attend_shift,
            attend_bias,
            expert_gain,
            expert_shift,
            expert_inner_bias,
            expert_outer_bias,
            jnp.full((1, 128), jnp.sum(caption_lengths), F32),
        ],
        axis=1,
    )
    rows = jnp.concatenate(to_sections(rows), axis=0)
    language_count = jnp.sum(rows[:, -128:], axis=0, keepdims=True)
    language_count = language_count + over_core(language_count)
    if planes == 4:
        language_count = language_count + over_plane(language_count, [(at, at ^ 1) for at in range(4)])
        language_count = language_count + over_plane(language_count, [(at, at ^ 2) for at in range(4)])
    else:
        language_count = lax.psum(language_count, "z")
    language_count = language_count[0, 0].astype(jnp.int32)
    vision_count = PATCHES * items * SECTIONS * 2 * planes
    counts = jnp.stack(
        [jnp.full((), vision_count, jnp.int32), language_count, language_count + vision_count]
    )
    rows = [lax.dynamic_index_in_dim(rows, at ^ section, 0) for at in range(SECTIONS)]
    sizes = [width, width, 3 * width, width, width, hidden, width]
    ends = [sum(sizes[: at + 1]) for at in range(len(sizes))]

    def row(slot, which):
        return rows[slot][:, ends[which] - sizes[which] : ends[which]]

    used = [(0, 0), (0, 1), (0, 2), (0, 3), (0, 4), (0, 5), (1, 3), (1, 4), (1, 5), (1, 6)]
    used += [(0, 6), (2, 0), (2, 1), (2, 2), (3, 3), (3, 4), (3, 5), (3, 6)]
    kept = lax.optimization_barrier(tuple(row(*at) for at in used) + (x0, last_grad, counts))
    x0, last_grad, counts = kept[-3:]
    kept = dict(zip(used, kept))

    def row(slot, which):
        return kept[slot, which]

    weights.run_step(1)
    handed = weights.hand_over((0,))
    sent = weights.run_step(2, *kept.values(), x0, last_grad, counts, *handed)
    weights.hand_over((1,), *sent)
    planes_moved = weights.run_planes(1)
    info = after(info, *weights.hand_over((0, 1)), weights.mine.get(("plane", 0), counts))
    attend0 = weights.layer("a")
    outputs = attend_forward(
        x0, info, attend0, row(0, 0), row(0, 1), row(0, 2), following=(row(0, 3), row(0, 4))
    )
    outputs, planes_moved = under(outputs, *planes_moved)
    y0, qkv0, mixed0, caption_rows = outputs
    if weights.four:
        weights.set_mine([("plane", 1), ("plane", -1)], planes_moved)
    caption_rows = to_sections(caption_rows.reshape(-1, width))
    handed = weights.hand_over((2,), caption_rows[0])
    sent = weights.run_step(EARLY_STEPS, *caption_rows[1:], *handed)
    weights.run_planes(2, *sent)
    late_keys = [key for key in weights.mine if key[0] == EARLY_STEPS]
    outputs = shared_forward(caption_rows, expert_inputs[0], expert_inner_bias, expert_outputs[0])
    if weights.four:
        late_keys += [("plane", 2), ("plane", -2)]
    part, moved = under(outputs, *[weights.mine[key] for key in late_keys])
    weights.set_mine(late_keys, moved)
    branch = {at: over_section(part[at], at, [0]) for at in range(1, SECTIONS)}
    branch[0] = part[0]
    weights.run_planes(3, *part)
    expert1 = weights.layer("e")
    outputs = expert_forward(
        y0, info, expert1, row(1, 3), row(1, 4), row(1, 5), row(1, 6), PATCH_ROWS, "patch"
    )
    if weights.four:
        last_moved = [("plane", 3), ("plane", -3)]
    else:
        last_moved = []
        for step in range(EARLY_STEPS + 1, len(weights.plan)):
            weights.run_step(step, *part)
    (x2, act1, slope1), moved = under(outputs, *[weights.mine[key] for key in last_moved])
    weights.set_mine(last_moved, moved)
    branch = items_of(by_section(section, branch))
    attend2 = weights.layer("c")
    x3, qkv2, mixed2, x2 = attend_forward(
        x2, info, attend2, row(2, 0), row(2, 1), row(2, 2), merge=(y0, branch, row(0, 6))
    )
    expert3 = weights.layer("f")
    layer_output, act3, slope3 = expert_forward(
        x3, info, expert3, row(3, 3), row(3, 4), row(3, 5), row(3, 6), ROWS, "all"
    )

    def small_rows(values):
        flat = jnp.concatenate(values, axis=1)
        count = -(-flat.shape[1] // hidden)
        flat = jnp.pad(flat, ((0, 0), (0, count * hidden - flat.shape[1])))
        return flat.reshape(count, hidden)

    def to_home(sums):
        got = [by_section(section, sums)]
        for bits in (1, 2, 3):
            sends = {at ^ bits: sums[at] for at in sums}
            got.append(over_section(by_section(section, sends), bits, sorted(sends)))
        return got

    last_moved = []
    if weights.four:
        weights.run_step(EARLY_STEPS + 1, x3)
        last_moved = [key for key in weights.mine if key[0] == EARLY_STEPS + 1]
    outputs = expert_backward(
        x3, info, expert3, row(3, 3), row(3, 4), act3, slope3, last_grad, ROWS, "all"
    )
    outputs, moved = under(outputs, *[weights.mine[key] for key in last_moved])
    weights.set_mine(last_moved, moved)
    handed = weights.hand_over((EARLY_STEPS + 1,)) if weights.four else []
    grad3, *small3 = outputs[:5]
    sums3 = Sums(outputs[5:])
    sums3.cross()
    moved = over_links(sums3.first_sends())
    grad3 = after(grad3, *sums3.sent)
    outputs = attend_backward(
        x2, info, attend2, row(2, 0), row(2, 1), qkv2, mixed2, grad3
    )
    outputs, moved = under(outputs, *moved, sums3.got_stay, *handed)
    grad2, *small2 = outputs[:4]
    sums2, caption_grad = Sums(outputs[4:8]), outputs[8]
    caption_grads = to_sections(caption_grad.reshape(-1, width))
    sums3.got_stay = moved[2]
    sends = [after(value, *caption_grads[1:]) for value in sums3.second_sends(*moved[:2])]
    moved3 = over_links(sends)
    sums2.cross(caption_grads[3])
    inner_quarter = lax.dynamic_slice(row(0, 5), (0, section * width), (1, width))
    inner_quarter = after(inner_quarter, *sends)
    outputs = shared_backward(
        caption_rows, caption_grads, info, weights.layer("g"), inner_quarter
    )
    outputs, moved = under(outputs, *moved3, sums2.got_move, sums2.got_stay)
    moved3, sums2.got_move, sums2.got_stay = moved[:2], moved[2], moved[3]
    parts, (keep0, send0, inner_grad, outer_grad) = outputs[:4], outputs[4:]
    got = [over_section(parts[bits], bits) for bits in (1, 2, 3)]
    moved2 = over_links(sums2.first_sends())
    keep0 = added(keep0, over_core(send0))
    early = jnp.concatenate([sums3.whole(*moved3), keep0], axis=0)
    grad2, early = lax.optimization_barrier((after(grad2, *sums2.sent), early))
    early = lax.psum(early, "z")
    outputs = expert_backward(
        y0, info, expert1, row(1, 3), row(1, 4), act1, slope1, grad2, PATCH_ROWS, "patch"
    )
    outputs, moved = under(outputs, *got, *moved2)
    parts, moved2 = [parts[0], *moved[:3]], moved[3:]
    grad1, *small1 = outputs[:5]
    sums1 = Sums(outputs[5:])
    sums1.cross()
    moved2 = over_links(sums2.second_sends(*moved2))
    moved1 = over_links(sums1.first_sends())
    grad1 = after(grad1, *sums2.sent, *sums1.sent)
    outputs = attend_backward(
        x0,
        info,
        attend0,
        row(0, 0),
        row(0, 1),
        qkv0,
        mixed0,
        grad1,
        first=(y0, row(0, 3), parts),
    )
    outputs, moved = under(outputs, *moved1, *moved2, sums1.got_stay)
    moved1, moved2, sums1.got_stay = moved[:2], moved[2:4], moved[4]
    tokens_grad, *small_first = outputs[:4]
    sums_first, gain_grad, shift_grad = Sums(outputs[4:8]), outputs[8], outputs[9]
    sums_first.cross()
    inner_grad = lax.dynamic_update_slice(
        jnp.zeros((1, hidden), F32), inner_grad, (0, section * width)
    )
    small = small_rows(
        small_first + [gain_grad, shift_grad, inner_grad, outer_grad] + small2 + small1 + small3
    )
    small = added(small, over_core(small))
    to_x, to_y = sums_first.first_sends()
    to_x = jnp.concatenate([to_x[0], small], axis=0)
    sends = lax.optimization_barrier((*sums1.second_sends(*moved1), to_x, to_y))
    moved = over_links(sends[:2]) + over_links(sends[2:])
    moved = lax.optimization_barrier(tuple(moved))
    size = to_y.shape[1]
    small = added(small, moved[2][size:])
    planes1 = Planes(sums1.whole(*moved[:2]), plane, planes)
    to_x, to_y = sums_first.second_sends(moved[2][None, :size], moved[3])
    size = to_y.shape[1]
    to_y = jnp.concatenate([to_y[0], small], axis=0)
    to_x, to_y = lax.optimization_barrier((to_x, to_y))
    moved = lax.optimization_barrier((*over_links((to_x, to_y)), *planes1.sends(to_x, to_y)))
    planes1.take(moved[2])
    last = sums_first.whole(moved[0], moved[1][None, :size])
    small = added(small, moved[1][size:])
    small_count = small.shape[0]
    eighth = last.shape[1]
    last = jnp.concatenate([last[0], sums2.whole(*moved2)[0], small], axis=0)
    last = lax.psum(after(last, early), "z")
    home_early = to_home({0: after(early[2:], *moved), 3: after(early[:2], *moved)})
    planes1.take(*planes1.sends())
    planes1.take(*planes1.sends())
    planes1.take(*planes1.sends())
    home_late = to_home({1: after(planes1.value, *home_early[1:3])})
    home_attend = to_home({0: last[None, :eighth], 2: last[None, eighth : 2 * eighth]})
    small = last[2 * eighth :].astype(F32)

    as_float = counts.astype(F32)
    one = jnp.ones((), F32)
    attend_scales = jnp.stack([as_float[2], one, as_float[2], one])
    expert_scales = jnp.stack([as_float[1], as_float[0], one, as_float[2]])

    def placed(pieces, scales):
        scale = lax.dynamic_index_in_dim(scales, section, 0).reshape(1, 1)
        pieces = jnp.stack(pieces)
        return finish(info, scale, pieces, over_core(pieces), planes)

    blank = jnp.zeros_like(home_late[0])
    inputs_whole, outputs_whole = placed(
        [
            by_section(section, {0: early, 1: late, 2: blank, 3: early})
            for early, late in zip(home_early, home_late)
        ],
        expert_scales,
    )
    blank = jnp.zeros_like(home_attend[0])
    attend_whole, output_whole = placed(
        [by_section(section, {0: got, 1: blank, 2: got, 3: blank}) for got in home_attend],
        attend_scales,
    )

    attend_size, expert_size = 5 * width, 3 * width + hidden
    cuts = [attend_size, attend_size + expert_size]
    cuts += [cuts[1] + attend_size, cuts[1] + attend_size + expert_size]
    small = jnp.split(small.reshape(-1)[: cuts[3] + expert_size], cuts)
    none_attend, none_expert = jnp.zeros_like(small[0]), jnp.zeros_like(small[1])
    attend_small = jnp.stack([small[0], none_attend, small[2], none_attend])
    expert_small = jnp.stack([small[1], small[3], none_expert, small[4]])
    attend_small = attend_small / attend_scales.reshape(-1, 1)
    expert_small = expert_small / expert_scales.reshape(-1, 1)
    attend_small = lax.dynamic_index_in_dim(attend_small, section, 0)
    expert_small = lax.dynamic_index_in_dim(expert_small, section, 0)
    return (
        layer_output[:, :positions],
        tokens_grad[:, :positions],
        attend_small[:, :width],
        attend_small[:, width : 2 * width],
        attend_whole,
        attend_small[:, 2 * width :],
        output_whole,
        expert_small[:, :width],
        expert_small[:, width : 2 * width],
        inputs_whole,
        expert_small[:, 2 * width : 2 * width + hidden],
        outputs_whole,
        expert_small[:, 2 * width + hidden :],
        counts,
    )


def solution(mesh):
    sections, groups = mesh.shape["section"], mesh.shape["dp"]
    split = Mesh(mesh.devices.reshape(sections, groups // 2, 2), ("section", "z", "core"))
    items = P(("section", "z", "core"), None, None)
    flat = P("section", None)
    matrix = P("section", None, None)
    placed = (
        items,
        P(("section", "z", "core")),
        flat,
        flat,
        matrix,
        flat,
        matrix,
        flat,
        flat,
        matrix,
        flat,
        matrix,
        flat,
        items,
    )
    return jax.shard_map(
        per_device,
        mesh=split,
        in_specs=placed,
        out_specs=(
            items,
            items,
            flat,
            flat,
            matrix,
            flat,
            matrix,
            flat,
            flat,
            matrix,
            flat,
            matrix,
            flat,
            P(),
        ),
        check_vma=False,
    )
```

```python
from functools import partial

import jax
import jax.numpy as jnp
from jax import lax
from jax.experimental import pallas as pl
from jax.experimental.pallas import tpu as pltpu
from jax.sharding import Mesh
from jax.sharding import PartitionSpec as P

HEADS = 12
HEAD_DIM = 64
PATCHES = 197
ROWS = 256
CAP_FIRST, CAP_ROWS = 192, 48
PATCH_ROWS = 208
PAIR = 2 * HEAD_DIM
SECTIONS = 4
PIECE_ROWS = 48
VMEM_BYTES = 58 * 1024 * 1024
F32 = jnp.float32
BF16 = jnp.bfloat16

PLAN_FOUR = (
    ({0: "a0", 1: "e0", 2: "c0", 3: "F"}, {0: "a1", 1: "e2", 2: "c0", 3: "F"}),
    ({0: "a1", 1: "e1", 2: "a1", 3: "e2"}, {0: "a0", 1: "a0", 2: "F", 3: "c0"}),
    ({0: "g3", 1: "e2", 2: "c1"}, {0: "e0", 1: "e3", 2: "c1"}),
    ({0: "g1", 1: "e3", 2: "e0", 3: "e3"}, {0: "e1", 1: "e1", 3: "c1"}),
    ({}, {0: "g2", 1: "g3"}),
)
PLAN_ANY = (
    ({0: "a0", 1: "e0", 2: "c0", 3: "f0"}, {0: "a1", 1: "e2", 2: "c0", 3: "f0"}),
    ({0: "a1", 1: "e1", 2: "a1", 3: "e2"}, {0: "a0", 1: "a0", 2: "c1", 3: "f1"}),
    ({0: "g3", 1: "e2", 2: "c1", 3: "f1"}, {0: "e0", 1: "e3", 2: "f0", 3: "f2"}),
    ({0: "g1", 1: "e3", 2: "e0", 3: "e3"}, {0: "e1", 1: "e1", 2: "f1", 3: "f3"}),
    ({0: "c1", 1: "f2", 3: "f2"}, {0: "g2", 1: "g3", 3: "c0"}),
    ({1: "f3", 3: "f3"}, {}),
)
HOMES = {"a": 0, "c": 2, "e": 1, "f": 3, "F": 3, "g": 0}
ATTEND_BLOCKS = ((0, 1), (2, 3))
EXPERT_BLOCKS = ((0, 1), (4, 5), (2, 3), (6, 7))


def dot_plain(left, right):
    return jnp.dot(left, right, preferred_element_type=F32)


def dot_last(left, right):
    return lax.dot_general(left, right, (((1,), (1,)), ((), ())), preferred_element_type=F32)


def dot_first(left, right):
    return lax.dot_general(left, right, (((0,), (0,)), ((), ())), preferred_element_type=F32)


def column_sum(matrix):
    return jnp.sum(matrix.astype(F32), axis=0, keepdims=True)


def norm_parts(rows):
    centre = rows - jnp.mean(rows, axis=-1, keepdims=True)
    scale = lax.rsqrt(jnp.mean(centre * centre, axis=-1, keepdims=True) + 1e-06)
    return centre * scale, scale


def norm_back(normed_grad, unit, scale, gain):
    unit_grad = normed_grad * gain
    along = jnp.mean(unit_grad * unit, axis=-1, keepdims=True)
    return scale * (unit_grad - jnp.mean(unit_grad, axis=-1, keepdims=True) - unit * along)


def true_positions(length, first, count, axis, kind):
    shape = (count, 1) if axis == 0 else (1, count)
    position = first + lax.broadcasted_iota(jnp.int32, shape, axis)
    patch = position < PATCHES
    if kind == "patch":
        return patch
    caption = (position >= PATCHES) & (position - PATCHES < length)
    return caption if kind == "caption" else patch | caption


def head_masks():
    lane = lax.broadcasted_iota(jnp.int32, (1, PAIR), 1)
    even = (lane < HEAD_DIM).astype(F32).astype(BF16)
    odd = (lane >= HEAD_DIM).astype(F32).astype(BF16)
    return lane < HEAD_DIM, even, odd


def split_pair(pair, even, odd):
    return jnp.concatenate([pair * even, pair * odd], axis=0)


def start_weights(info, first, refs, plan, blocks, sems):
    half = blocks.shape[1] // 2
    section, core, plane = info[first], info[first + 1], info[first + 2]
    for at, at_plane, steps in plan:
        here = section == at
        if at_plane is not None:
            here = here & (plane == at_plane)

        @pl.when(here)
        def _(steps=steps):
            for block, source in steps:
                if source[0] == "own":
                    _, which, row, column = source
                    width = blocks.shape[2]
                    for part in range(2):
                        pltpu.make_async_copy(
                            refs[which].at[
                                pl.ds(row + part * half, half), pl.ds(column, width)
                            ],
                            blocks.at[block, pl.ds(part * half, half)],
                            sems.at[block],
                        ).start()
                else:
                    _, mine, theirs, index = source
                    pltpu.make_async_copy(
                        refs[mine].at[index],
                        blocks.at[block, pl.ds(pl.multiple_of(core * half, half), half)],
                        sems.at[block],
                    ).start()
                    pltpu.make_async_copy(
                        refs[theirs].at[index],
                        blocks.at[block, pl.ds(pl.multiple_of((1 - core) * half, half), half)],
                        sems.at[block],
                    ).start()


def wait_block(blocks, block, sems):
    pltpu.make_async_copy(blocks.at[block], blocks.at[block], sems.at[block]).wait()


def store_turned(target, turned, columns, section, core):
    half = target.shape[0] // 2
    for piece in range(16):
        path, owner = (piece >> 2) & 1, piece & 3
        away = owner ^ section
        place = ((away & 1) << 1) | (away >> 1) if path == 0 else away
        row = ((piece >> 3) ^ core) * half + (place >> 1) * (half // 2)
        row = row + path * (half // 4) + (place & 1) * PIECE_ROWS
        target[pl.ds(pl.multiple_of(row, 16), PIECE_ROWS), columns] = turned[
            piece * PIECE_ROWS : (piece + 1) * PIECE_ROWS
        ]


def put_travel(refs, which, columns, left, right):
    half = left.shape[0] // 2
    for side in range(2):
        rows = dot_plain(left[side * half : (side + 1) * half], right).astype(BF16)
        refs[2 * side][which, :, columns] = rows[: half // 2]
        refs[2 * side + 1][which, :, columns] = rows[half // 2 :]


def attend_forward_kernel(plan, weight_count, merge, info, *refs):
    weights, refs = refs[:weight_count], refs[weight_count:]
    if merge:
        x_ref, before_ref, part_ref, outer_ref, gain_ref, shift_ref, bias_ref = refs[:7]
        y_ref, qkv_ref, mixed_ref, joined_ref, blocks, sems, joined = refs[7:]
    else:
        x_ref, gain_ref, shift_ref, bias_ref, next_gain_ref, next_shift_ref = refs[:6]
        y_ref, qkv_ref, mixed_ref, caption_ref, blocks, sems = refs[6:]
    item = pl.program_id(0)
    items = pl.num_programs(0)
    length = info[item]
    width = x_ref.shape[-1]

    @pl.when(item == 0)
    def _():
        start_weights(info, items, weights, plan, blocks, sems)

    cap = slice(CAP_FIRST, CAP_FIRST + CAP_ROWS)
    if merge:
        joined[...] = x_ref[0].astype(F32)
        branch = part_ref[0].astype(F32) + outer_ref[...]
        is_true = true_positions(length, CAP_FIRST, CAP_ROWS, 0, "caption")
        captions = before_ref[0, cap] + jnp.where(is_true, branch, 0.0)
        position = CAP_FIRST + lax.broadcasted_iota(jnp.int32, (CAP_ROWS, 1), 0)
        captions = captions.astype(BF16).astype(F32)
        joined[cap] = jnp.where(position < PATCHES, joined[cap], captions)
        x = joined[...]
        joined_ref[0] = x.astype(BF16)
    else:
        x = x_ref[0].astype(F32)
    unit, _ = norm_parts(x)
    normed = (unit * gain_ref[...] + shift_ref[...]).astype(BF16)

    @pl.when(item == 0)
    def _():
        for block in range(4):
            wait_block(blocks, block, sems)

    queries = dot_plain(normed, blocks[0]) + bias_ref[:, :width]
    qkv_ref[0, :, :width] = (queries * HEAD_DIM ** (-0.5)).astype(BF16)
    qkv_ref[0, :, width : 2 * width] = dot_plain(normed, blocks[1]).astype(BF16)
    values = dot_plain(normed, blocks[2]) + bias_ref[:, width : 2 * width]
    qkv_ref[0, :, 2 * width :] = values.astype(BF16)
    key_true = true_positions(length, 0, ROWS, 1, "all")
    low_half, even, odd = head_masks()
    ones = jnp.ones((ROWS, PAIR), BF16)

    def scores_of(pair):
        at = pair * PAIR
        q2 = qkv_ref[0, :, at : at + PAIR]
        k2 = qkv_ref[0, :, width + at : width + at + PAIR]
        return dot_last(split_pair(q2, even, odd), k2)

    ahead = [scores_of(0), scores_of(1)]
    for pair in range(HEADS // 2):
        at = pair * PAIR
        scores = jnp.where(key_true, ahead.pop(0), -1e9)
        if pair + 2 < HEADS // 2:
            ahead.append(scores_of(pair + 2))
        weight = jnp.exp(scores - jnp.max(scores, axis=-1, keepdims=True)).astype(BF16)
        v2 = qkv_ref[0, :, 2 * width + at : 2 * width + at + PAIR]
        summed = dot_plain(weight, jnp.concatenate([v2, ones], axis=1))
        top = jnp.where(low_half, summed[:ROWS, :PAIR], summed[ROWS:, :PAIR])
        below = jnp.where(low_half, summed[:ROWS, PAIR:], summed[ROWS:, PAIR:])
        mixed_ref[0, :, at : at + PAIR] = (top / below).astype(BF16)
    branch = dot_plain(mixed_ref[0], blocks[3]) + bias_ref[:, 2 * width :]
    row_true = true_positions(length, 0, ROWS, 0, "all")
    y = x + jnp.where(row_true, branch, 0.0)
    y_ref[0] = y.astype(y_ref.dtype)
    if not merge:
        unit, _ = norm_parts(y[cap])
        caption_ref[0] = (unit * next_gain_ref[...] + next_shift_ref[...]).astype(BF16)


def attend_backward_kernel(plan, weight_count, first, info, *refs):
    weights, refs = refs[:weight_count], refs[weight_count:]
    x_ref, gain_ref, shift_ref, qkv_ref, mixed_ref, grad_ref = refs[:6]
    if first:
        after_ref, next_gain_ref, *parts = refs[6:12]
        refs = refs[12:]
    else:
        refs = refs[6:]
    out_ref, gain_grad_ref, shift_grad_ref, bias_grad_ref = refs[:4]
    travel_refs = refs[4:8]
    if first:
        next_gain_grad_ref, next_shift_grad_ref, joined = refs[8], refs[9], refs[-1]
    else:
        caption_ref = refs[8]
    blocks, sems, normed_turned, mixed_turned, branch_all, projected, mixed_grad = refs[
        10 if first else 9 :
    ][:7]
    item = pl.program_id(0)
    items = pl.num_programs(0)
    length = info[item]
    section, core = info[items], info[items + 1]
    width = x_ref.shape[-1]
    here = pl.ds(pl.multiple_of(item * ROWS, ROWS), ROWS)
    cap = slice(CAP_FIRST, CAP_FIRST + CAP_ROWS)

    @pl.when(item == 0)
    def _():
        start_weights(info, items, weights, plan, blocks, sems)

    def add_to(ref, part):
        @pl.when(item == 0)
        def _():
            ref[...] = part

        @pl.when(item > 0)
        def _():
            ref[...] += part

    x = x_ref[0].astype(F32)
    unit, scale = norm_parts(x)
    normed = (unit * gain_ref[...] + shift_ref[...]).astype(BF16)
    incoming = grad_ref[0].astype(F32)
    if first:
        after_unit, after_scale = norm_parts(after_ref[0, cap])
        caption_grad = parts[0][...].astype(F32)
        for part in parts[1:]:
            caption_grad = caption_grad + part[...].astype(F32)
        joined[...] = incoming
        joined[cap] += norm_back(caption_grad, after_unit, after_scale, next_gain_ref[...])
        incoming = joined[...]
        add_to(next_gain_grad_ref, jnp.sum(caption_grad * after_unit, axis=0, keepdims=True))
        add_to(next_shift_grad_ref, jnp.sum(caption_grad, axis=0, keepdims=True))
    row_true = true_positions(length, 0, ROWS, 0, "all")
    branch = jnp.where(row_true, incoming, 0.0).astype(BF16)
    branch_all[here, :] = branch
    store_turned(normed_turned, normed.T, here, section, core)
    store_turned(mixed_turned, mixed_ref[0].T, here, section, core)

    @pl.when(item == 0)
    def _():
        for block in range(4):
            wait_block(blocks, block, sems)

    mixed_grad[...] = dot_last(branch, blocks[3]).astype(BF16)
    key_true = true_positions(length, 0, ROWS, 0, "all")
    _, even, odd = head_masks()

    def products_of(pair):
        at = pair * PAIR
        q2 = split_pair(qkv_ref[0, :, at : at + PAIR], even, odd)
        k2 = qkv_ref[0, :, width + at : width + at + PAIR]
        v2 = qkv_ref[0, :, 2 * width + at : 2 * width + at + PAIR]
        g2 = split_pair(mixed_grad[:, at : at + PAIR], even, odd)
        return q2, k2, g2, dot_last(k2, q2), dot_last(v2, g2)

    ahead = [products_of(0)]
    for pair in range(HEADS // 2):
        at = pair * PAIR
        q2, k2, g2, scores, weight_grad = ahead.pop(0)
        if pair + 1 < HEADS // 2:
            ahead.append(products_of(pair + 1))
        scores = jnp.where(key_true, scores, -1e9)
        weight = jnp.exp(scores - jnp.max(scores, axis=0, keepdims=True))
        weight = weight * (1.0 / jnp.sum(weight, axis=0, keepdims=True))
        product = weight * weight_grad
        along = jnp.sum(product, axis=0, keepdims=True)
        score_grad = (product - weight * along).astype(BF16)
        values_grad = dot_plain(weight.astype(BF16), g2).astype(BF16)
        keys_grad = dot_plain(score_grad, q2).astype(BF16)
        k2_split = split_pair(k2, even, odd)
        stacked = jnp.concatenate([score_grad[:, :ROWS], score_grad[:, ROWS:]], axis=0)
        queries_grad = dot_first(stacked, k2_split).astype(BF16)
        queries_grad = (queries_grad.astype(F32) * HEAD_DIM ** (-0.5)).astype(BF16)
        projected[here, at : at + PAIR] = queries_grad
        projected[here, width + at : width + at + PAIR] = keys_grad
        projected[here, 2 * width + at : 2 * width + at + PAIR] = values_grad
    normed_grad = dot_last(projected[here, :width], blocks[0])
    normed_grad += dot_last(projected[here, width : 2 * width], blocks[1])
    normed_grad += dot_last(projected[here, 2 * width :], blocks[2])
    out = (incoming + norm_back(normed_grad, unit, scale, gain_ref[...])).astype(BF16)
    out_ref[0] = out
    if not first:
        is_true = true_positions(length, CAP_FIRST, CAP_ROWS, 0, "caption")
        caption_ref[0] = jnp.where(is_true, out[cap].astype(F32), 0.0).astype(BF16)
    add_to(gain_grad_ref, jnp.sum(normed_grad * unit, axis=0, keepdims=True))
    add_to(shift_grad_ref, jnp.sum(normed_grad, axis=0, keepdims=True))

    @pl.when(item == items - 1)
    def _():
        for block in range(4):
            columns = slice(block * width, (block + 1) * width)
            left = normed_turned if block < 3 else mixed_turned
            right = projected[:, columns] if block < 3 else branch_all[...]
            put_travel(travel_refs, 0, columns, left, right)
        bias_grad_ref[:, :width] = column_sum(projected[:, :width])
        bias_grad_ref[:, width : 2 * width] = column_sum(projected[:, 2 * width :])
        bias_grad_ref[:, 2 * width :] = column_sum(branch_all[...])


SHORT = pl.CostEstimate(flops=0, bytes_accessed=100_000, transcendentals=0)
LONG = pl.CostEstimate(flops=30_000_000_000, bytes_accessed=30_000_000, transcendentals=0)
ANYWHERE = pl.BlockSpec(memory_space=pl.ANY)


def whole_block(shape):
    return pl.BlockSpec(shape, lambda step, info: (0,) * len(shape))


def item_block(shape):
    return pl.BlockSpec((1,) + shape[1:], lambda step, info: (step,) + (0,) * (len(shape) - 1))


def blocks_scratch(count, width):
    return [pltpu.VMEM((count, width, width), BF16), pltpu.SemaphoreType.DMA((count,))]


def attend_forward(x, info, weights, gain, shift, bias, merge=None, following=None):
    arrays, plan = weights
    items, _, width = x.shape
    row = whole_block((1, width))
    bias_row = whole_block((1, 3 * width))
    caption_shape = (items, CAP_ROWS, width)
    if merge is not None:
        before, part, outer = merge
        operands = (x, before, part, outer, gain, shift, bias)
        specs = [item_block(x.shape), item_block(x.shape), item_block(caption_shape)]
        specs += [row, row, row, bias_row]
        last_shape, kind, scratch = x.shape, BF16, [pltpu.VMEM((ROWS, width), F32)]
    else:
        operands = (x, gain, shift, bias, *following)
        specs = [item_block(x.shape), row, row, bias_row, row, row]
        last_shape, kind, scratch = caption_shape, F32, []
    return pl.pallas_call(
        partial(attend_forward_kernel, plan, len(arrays), merge is not None),
        grid_spec=pltpu.PrefetchScalarGridSpec(
            num_scalar_prefetch=1,
            grid=(items,),
            in_specs=[ANYWHERE] * len(arrays) + specs,
            out_specs=[
                item_block(x.shape),
                item_block((items, ROWS, 3 * width)),
                item_block((items, ROWS, width)),
                item_block(last_shape),
            ],
            scratch_shapes=blocks_scratch(4, width) + scratch,
        ),
        out_shape=[
            jax.ShapeDtypeStruct(x.shape, kind),
            jax.ShapeDtypeStruct((items, ROWS, 3 * width), BF16),
            jax.ShapeDtypeStruct((items, ROWS, width), BF16),
            jax.ShapeDtypeStruct(last_shape, BF16),
        ],
        compiler_params=pltpu.CompilerParams(vmem_limit_bytes=VMEM_BYTES),
        cost_estimate=SHORT,
        name="attend_forward",
    )(info, *arrays, *operands)


def attend_backward(x, info, weights, gain, shift, qkv, mixed, incoming, first=None):
    arrays, plan = weights
    items, _, width = x.shape
    half = width // 2
    row = whole_block((1, width))
    caption_shape = (items, CAP_ROWS, width)
    operands = (x, gain, shift, qkv, mixed, incoming)
    specs = [item_block(x.shape), row, row, item_block(qkv.shape), item_block(mixed.shape)]
    specs += [item_block(incoming.shape)]
    outs = [
        (item_block(x.shape), x.shape, BF16),
        (row, (1, width), F32),
        (row, (1, width), F32),
        (whole_block((1, 3 * width)), (1, 3 * width), F32),
    ]
    outs += [(whole_block((1, half // 2, 4 * width)), (1, half // 2, 4 * width), BF16)] * 4
    scratch = []
    if first is not None:
        after, next_gain, parts = first
        operands += (after, next_gain, *parts)
        caption_rows = pl.BlockSpec((CAP_ROWS, width), lambda step, info: (step, 0))
        specs += [item_block(after.shape), row] + [caption_rows] * 4
        outs += [(row, (1, width), F32)] * 2
        scratch = [pltpu.VMEM((ROWS, width), F32)]
    else:
        outs += [(item_block(caption_shape), caption_shape, BF16)]
    return pl.pallas_call(
        partial(attend_backward_kernel, plan, len(arrays), first is not None),
        grid_spec=pltpu.PrefetchScalarGridSpec(
            num_scalar_prefetch=1,
            grid=(items,),
            in_specs=[ANYWHERE] * len(arrays) + specs,
            out_specs=[spec for spec, _, _ in outs],
            scratch_shapes=blocks_scratch(4, width)
            + [
                pltpu.VMEM((width, items * ROWS), BF16),
                pltpu.VMEM((width, items * ROWS), BF16),
                pltpu.VMEM((items * ROWS, width), BF16),
                pltpu.VMEM((items * ROWS, 3 * width), BF16),
                pltpu.VMEM((ROWS, width), BF16),
            ]
            + scratch,
        ),
        out_shape=[jax.ShapeDtypeStruct(shape, kind) for _, shape, kind in outs],
        compiler_params=pltpu.CompilerParams(vmem_limit_bytes=VMEM_BYTES),
        cost_estimate=LONG,
        name="attend_backward",
    )(info, *arrays, *operands)


def normal_parts(u):
    t = pl.reciprocal(1.0 + 0.23164190 * jnp.abs(u), approx=True)
    bell = jnp.exp2((u * -0.7213475204444817) * u)
    poly = t * (
        0.127414796
        + t * (-0.142248368 + t * (0.7107068705 + t * (-0.7265760135 + t * 0.5307027145)))
    )
    tail = poly * bell
    return jnp.where(u < 0, tail, 1.0 - tail), bell


def inner_forward(normed, matrix, bias):
    inner = dot_plain(normed, matrix) + bias
    cumulative, bell = normal_parts(inner)
    slope = cumulative + (inner * 0.3989422804014327) * bell
    return (inner * cumulative).astype(BF16), slope.astype(BF16)


def expert_forward_kernel(plan, weight_count, count, kind, info, *refs):
    weights, refs = refs[:weight_count], refs[weight_count:]
    x_ref, gain_ref, shift_ref, inner_ref, outer_ref = refs[:5]
    y_ref, act_ref, slope_ref, blocks, sems, normed, total = refs[5:]
    step = pl.program_id(0)
    items, _, width = x_ref.shape

    @pl.when(step == 0)
    def _():
        start_weights(info, items, weights, plan, blocks, sems)
        for item in range(items):
            x = x_ref[item, :count].astype(BF16).astype(F32)
            unit, _ = norm_parts(x)
            normed[item * count : (item + 1) * count] = (
                unit * gain_ref[...] + shift_ref[...]
            ).astype(BF16)

    wait_block(blocks, step, sems)
    wait_block(blocks, step + 4, sems)
    for at in range(0, width, 256):
        columns = slice(at, at + 256)
        act, slope = inner_forward(normed[...], blocks[step, :, columns], inner_ref[:, columns])
        act_ref[:, columns] = act
        slope_ref[:, columns] = slope
    part = dot_plain(act_ref[...], blocks[step + 4])

    @pl.when(step == 0)
    def _():
        total[...] = part

    @pl.when(step > 0)
    def _():
        total[...] += part

    @pl.when(step == pl.num_programs(0) - 1)
    def _():
        for item in range(items):
            row_true = true_positions(info[item], 0, count, 0, kind)
            branch = total[item * count : (item + 1) * count] + outer_ref[...]
            x = x_ref[item, :count].astype(BF16).astype(F32)
            y_ref[item, :count] = (x + jnp.where(row_true, branch, 0.0)).astype(BF16)
            if count < ROWS:
                y_ref[item, count:] = jnp.zeros((ROWS - count, width), BF16)


def expert_backward_kernel(plan, weight_count, count, kind, info, *refs):
    weights, refs = refs[:weight_count], refs[weight_count:]
    x_ref, gain_ref, shift_ref, act_ref, slope_ref, grad_ref = refs[:6]
    out_ref, gain_grad_ref, shift_grad_ref, inner_grad_ref, outer_grad_ref = refs[6:11]
    travel_refs = refs[11:15]
    blocks, sems, normed_turned, branch_turned, branch, inner_all, total = refs[15:]
    step = pl.program_id(0)
    items, _, width = x_ref.shape
    section, core = info[items], info[items + 1]

    @pl.when(step == 0)
    def _():
        start_weights(info, items, weights, plan, blocks, sems)
        outer = None
        for item in range(items):
            here = slice(item * count, (item + 1) * count)
            unit, _ = norm_parts(x_ref[item, :count].astype(BF16).astype(F32))
            normed = (unit * gain_ref[...] + shift_ref[...]).astype(BF16)
            row_true = true_positions(info[item], 0, count, 0, kind)
            incoming = grad_ref[item, :count].astype(F32)
            masked = jnp.where(row_true, incoming, 0.0).astype(BF16)
            branch[here] = masked
            store_turned(normed_turned, normed.T, here, section, core)
            store_turned(branch_turned, masked.T, here, section, core)
            term = column_sum(masked)
            outer = term if outer is None else outer + term
        outer_grad_ref[...] = outer

    wait_block(blocks, step, sems)
    wait_block(blocks, step + 4, sems)
    for at in range(0, width, 256):
        columns = slice(at, at + 256)
        act_grad = dot_last(branch[...], blocks[step + 4, columns])
        inner = (slope_ref[:, columns].astype(F32) * act_grad).astype(BF16)
        inner_all[:, columns] = inner
        inner_grad_ref[:, columns] = column_sum(inner)
        put_travel(travel_refs, 0, columns, normed_turned, inner)
        put_travel(travel_refs, 1, columns, branch_turned, act_ref[:, columns])
    part = dot_last(inner_all[...], blocks[step])

    @pl.when(step == 0)
    def _():
        total[...] = part

    @pl.when(step > 0)
    def _():
        total[...] += part

    @pl.when(step == pl.num_programs(0) - 1)
    def _():
        gain_sum, shift_sum = None, None
        for item in range(items):
            unit, scale = norm_parts(x_ref[item, :count].astype(BF16).astype(F32))
            normed_grad = total[item * count : (item + 1) * count]
            gain_part = jnp.sum(normed_grad * unit, axis=0, keepdims=True)
            shift_part = jnp.sum(normed_grad, axis=0, keepdims=True)
            gain_sum = gain_part if gain_sum is None else gain_sum + gain_part
            shift_sum = shift_part if shift_sum is None else shift_sum + shift_part
            incoming = grad_ref[item, :count].astype(F32)
            hidden = incoming + norm_back(normed_grad, unit, scale, gain_ref[...])
            out_ref[item, :count] = hidden.astype(BF16)
            if count < ROWS:
                out_ref[item, count:] = grad_ref[item, count:]
        gain_grad_ref[...] = gain_sum
        shift_grad_ref[...] = shift_sum


def shared_forward_kernel(*refs):
    *rows_refs, inputs_ref, inner_ref, outputs_ref = refs[:7]
    *part_refs, normed, total = refs[7:]
    count = rows_refs[0].shape[0]
    step = pl.program_id(0)

    @pl.when(step == 0)
    def _():
        for index, ref in enumerate(rows_refs):
            normed[index * count : (index + 1) * count] = ref[...]
        total[...] = jnp.zeros_like(total)

    act, _ = inner_forward(normed[...], inputs_ref[...], inner_ref[...])
    total[...] += dot_plain(act, outputs_ref[...])

    @pl.when(step == pl.num_programs(0) - 1)
    def _():
        for index, ref in enumerate(part_refs):
            ref[...] = total[index * count : (index + 1) * count].astype(BF16)


def shared_backward_kernel(plan, weight_count, info, *refs):
    weights, refs = refs[:weight_count], refs[weight_count:]
    rows_refs, grad_refs, inner_ref = refs[:4], refs[4:8], refs[8]
    part_refs, (keep_ref, send_ref, inner_grad_ref, outer_grad_ref) = refs[9:13], refs[13:17]
    blocks, sems, normed, branch, matrix = refs[17:]
    count, width = rows_refs[0].shape
    half = width // 2
    first = info.shape[0] - 3
    core = info[first + 1]
    start_weights(info, first, weights, plan, blocks, sems)
    for index in range(SECTIONS):
        here = slice(index * count, (index + 1) * count)
        normed[here] = rows_refs[index][...]
        branch[here] = grad_refs[index][...]
    outer_grad_ref[...] = column_sum(grad_refs[0][...])
    wait_block(blocks, 0, sems)
    wait_block(blocks, 1, sems)
    part = None
    for at in range(0, width, 256):
        columns = slice(at, at + 256)
        act, slope = inner_forward(normed[...], blocks[0, :, columns], inner_ref[:, columns])
        act_grad = dot_last(branch[...], blocks[1, columns])
        inner = (slope.astype(F32) * act_grad).astype(BF16)
        inner_grad_ref[:, columns] = column_sum(inner)
        matrix[0, :, columns] = dot_first(normed[...], inner).astype(BF16)
        matrix[1, :, columns] = dot_first(branch[...], act).astype(BF16)
        term = dot_last(inner, blocks[0, :, columns])
        part = term if part is None else part + term
    for index, ref in enumerate(part_refs):
        ref[...] = part[index * count : (index + 1) * count].astype(BF16)
    quarter = half // 4
    for which in range(2):
        for group in range(4):
            columns = slice(group * width, (group + 1) * width)
            mine = pl.multiple_of(core * half, 16) + group * quarter
            other = pl.multiple_of((1 - core) * half, 16) + group * quarter
            keep_ref[which, :, columns] = matrix[which, pl.ds(pl.multiple_of(mine, 16), quarter)]
            send_ref[which, :, columns] = matrix[which, pl.ds(pl.multiple_of(other, 16), quarter)]


def chunk_columns(rows, width):
    return pl.BlockSpec((rows, width), lambda step, info: (0, step))


def expert_forward(x, info, weights, gain, shift, inner, outer, count, kind):
    arrays, plan = weights
    items, _, width = x.shape
    hidden = inner.shape[1]
    row = whole_block((1, width))
    return pl.pallas_call(
        partial(expert_forward_kernel, plan, len(arrays), count, kind),
        grid_spec=pltpu.PrefetchScalarGridSpec(
            num_scalar_prefetch=1,
            grid=(hidden // width,),
            in_specs=[ANYWHERE] * len(arrays)
            + [whole_block(x.shape), row, row, chunk_columns(1, width), row],
            out_specs=[
                whole_block((items, ROWS, width)),
                chunk_columns(items * count, width),
                chunk_columns(items * count, width),
            ],
            scratch_shapes=blocks_scratch(8, width)
            + [
                pltpu.VMEM((items * count, width), BF16),
                pltpu.VMEM((items * count, width), F32),
            ],
        ),
        out_shape=[
            jax.ShapeDtypeStruct((items, ROWS, width), BF16),
            jax.ShapeDtypeStruct((items * count, hidden), BF16),
            jax.ShapeDtypeStruct((items * count, hidden), BF16),
        ],
        compiler_params=pltpu.CompilerParams(vmem_limit_bytes=VMEM_BYTES),
        cost_estimate=SHORT,
        name="expert_forward_" + kind,
    )(info, *arrays, x, gain, shift, inner, outer)


def expert_backward(x, info, weights, gain, shift, act, slope, incoming, count, kind):
    arrays, plan = weights
    items, _, width = x.shape
    half = width // 2
    hidden = act.shape[1]
    row = whole_block((1, width))
    travel = pl.BlockSpec((2, half // 2, width), lambda step, info: (0, 0, step))
    return pl.pallas_call(
        partial(expert_backward_kernel, plan, len(arrays), count, kind),
        grid_spec=pltpu.PrefetchScalarGridSpec(
            num_scalar_prefetch=1,
            grid=(hidden // width,),
            in_specs=[ANYWHERE] * len(arrays)
            + [
                whole_block(x.shape),
                row,
                row,
                chunk_columns(items * count, width),
                chunk_columns(items * count, width),
                whole_block(incoming.shape),
            ],
            out_specs=[whole_block(incoming.shape), row, row, chunk_columns(1, width), row]
            + [travel] * 4,
            scratch_shapes=blocks_scratch(8, width)
            + [
                pltpu.VMEM((width, items * count), BF16),
                pltpu.VMEM((width, items * count), BF16),
                pltpu.VMEM((items * count, width), BF16),
                pltpu.VMEM((items * count, width), BF16),
                pltpu.VMEM((items * count, width), F32),
            ],
        ),
        out_shape=[
            jax.ShapeDtypeStruct(incoming.shape, BF16),
            jax.ShapeDtypeStruct((1, width), F32),
            jax.ShapeDtypeStruct((1, width), F32),
            jax.ShapeDtypeStruct((1, hidden), F32),
            jax.ShapeDtypeStruct((1, width), F32),
        ]
        + [jax.ShapeDtypeStruct((2, half // 2, hidden), BF16)] * 4,
        compiler_params=pltpu.CompilerParams(vmem_limit_bytes=VMEM_BYTES),
        cost_estimate=SHORT,
        name="expert_backward_" + kind,
    )(info, *arrays, x, gain, shift, act, slope, incoming)


IN_VMEM = pl.BlockSpec(memory_space=pltpu.VMEM)
IN_SMEM = pl.BlockSpec(memory_space=pltpu.SMEM)


def shared_forward(rows, inputs, inner, outputs):
    count, width = rows[0].shape
    total = SECTIONS * count
    hidden = inner.shape[1]
    return pl.pallas_call(
        shared_forward_kernel,
        grid=(hidden // width,),
        in_specs=[pl.BlockSpec(rows[0].shape, lambda step: (0, 0))] * 4
        + [
            pl.BlockSpec((width, width), lambda step: (0, step)),
            pl.BlockSpec((1, width), lambda step: (0, step)),
            pl.BlockSpec((width, width), lambda step: (step, 0)),
        ],
        out_specs=[pl.BlockSpec((count, width), lambda step: (0, 0))] * SECTIONS,
        scratch_shapes=[pltpu.VMEM((total, width), BF16), pltpu.VMEM((total, width), F32)],
        out_shape=[jax.ShapeDtypeStruct((count, width), BF16)] * SECTIONS,
        compiler_params=pltpu.CompilerParams(vmem_limit_bytes=VMEM_BYTES),
        cost_estimate=SHORT,
        name="shared_forward",
    )(*rows, inputs, inner, outputs)


def shared_backward(rows, grads, info, weights, inner):
    arrays, plan = weights
    count, width = rows[0].shape
    total = SECTIONS * count
    travel = (2, width // 8, 4 * width)
    return pl.pallas_call(
        partial(shared_backward_kernel, plan, len(arrays)),
        in_specs=[IN_SMEM] + [ANYWHERE] * len(arrays) + [IN_VMEM] * 9,
        out_specs=[IN_VMEM] * 8,
        scratch_shapes=blocks_scratch(2, width)
        + [
            pltpu.VMEM((total, width), BF16),
            pltpu.VMEM((total, width), BF16),
            pltpu.VMEM((2, width, width), BF16),
        ],
        out_shape=[
            *[jax.ShapeDtypeStruct((count, width), BF16)] * SECTIONS,
            jax.ShapeDtypeStruct(travel, BF16),
            jax.ShapeDtypeStruct(travel, BF16),
            jax.ShapeDtypeStruct((1, width), F32),
            jax.ShapeDtypeStruct((1, width), F32),
        ],
        compiler_params=pltpu.CompilerParams(vmem_limit_bytes=VMEM_BYTES),
        cost_estimate=SHORT,
        name="shared_backward",
    )(info, *arrays, *rows, *grads, inner)


def plane_turn(plane, planes):
    return ((plane & 1) << 1) | (plane >> 1) if planes == 4 else 0


def finish_kernel(planes, info, scale_ref, mine_ref, theirs_ref, *refs):
    step = pl.program_id(0)
    count = mine_ref.shape[1]
    placed = refs[-1]
    outs = refs[:-1]
    width = placed.shape[1]
    half = width // 2
    at = info.shape[0] - 3
    section, core = info[at], info[at + 1]
    turn = plane_turn(info[at + 2], planes)
    turned = 0 if count == 1 else jnp.where(section == 1, turn, 0)
    scale = scale_ref[0, 0]
    columns = pl.ds(pl.multiple_of((step ^ turned) * width, width), width)

    def place(which):
        def by_rows():
            for side, ref in enumerate((mine_ref, theirs_ref)):
                for away in range(SECTIONS):
                    for path in range(2):
                        row = (core ^ side) * half + path * (half // 2)
                        row = row + (section ^ away) * PIECE_ROWS
                        placed[pl.ds(pl.multiple_of(row, 16), PIECE_ROWS), :] = ref[
                            away, which, path * PIECE_ROWS : (path + 1) * PIECE_ROWS, columns
                        ].astype(F32)

        def by_columns():
            for side, ref in enumerate((mine_ref, theirs_ref)):
                for group in range(4):
                    quarter = half // 4
                    row = (core ^ side) * half + group * quarter
                    placed[pl.ds(pl.multiple_of(row, 16), quarter), :] = ref[
                        step, which, :, group * width : (group + 1) * width
                    ].astype(F32)

        if count == 1:
            by_rows()
        else:
            pl.when(section != 0)(by_rows)
            pl.when(section == 0)(by_columns)

    place(0)
    if count == 1:

        @pl.when(step < 3)
        def _():
            outs[0][0] = placed[...] / scale

        @pl.when(step == 3)
        def _():
            outs[1][0] = placed[...] / scale

    else:
        outs[0][0] = placed[...] / scale
        place(1)
        outs[1][0] = (placed[...] / scale).T


def finish(info, scale, mine, theirs, planes):
    count, hidden = mine.shape[1], mine.shape[3]
    width = hidden // 4
    if count == 1:
        shapes = [(1, width, 3 * width), (1, width, width)]
        maps = [lambda step, info: (0, 0, jnp.minimum(step, 2)), lambda step, info: (0, 0, 0)]
    else:
        shapes = [(1, width, hidden), (1, hidden, width)]
        maps = [lambda step, info: (0, 0, step), lambda step, info: (0, step, 0)]
    return pl.pallas_call(
        partial(finish_kernel, planes),
        grid_spec=pltpu.PrefetchScalarGridSpec(
            num_scalar_prefetch=1,
            grid=(4,),
            in_specs=[IN_SMEM, whole_block(mine.shape), whole_block(mine.shape)],
            out_specs=[pl.BlockSpec((1, width, width), at) for at in maps],
            scratch_shapes=[pltpu.VMEM((width, width), F32)],
        ),
        out_shape=[jax.ShapeDtypeStruct(shape, F32) for shape in shapes],
        compiler_params=pltpu.CompilerParams(vmem_limit_bytes=VMEM_BYTES),
        cost_estimate=SHORT,
        name="finish",
    )(info, scale, mine, theirs)


def pack_kernel(count, plan, info, *refs):
    sources, outs, sems = refs[:count], refs[count:-1], refs[-1]
    first = info.shape[0] - 3
    section, core, plane = info[first], info[first + 1], info[first + 2]
    half = outs[0].shape[1]
    for index, (out, choices) in enumerate(zip(outs, plan)):
        for at, at_plane, parts in choices:
            here = section == at
            if at_plane is not None:
                here = here & (plane == at_plane)

            @pl.when(here)
            def _(index=index, out=out, parts=parts):
                for block, part in enumerate(parts):
                    if part[0] == "own":
                        _, which, row, column = part
                        rows = pl.ds(pl.multiple_of(row + core * half, half), half)
                        source = sources[which].at[rows, pl.ds(column, out.shape[2])]
                    else:
                        source = sources[part[1]].at[block]
                    pltpu.make_async_copy(source, out.at[block], sems.at[index, block]).start()

    for index, out in enumerate(outs):
        for block in range(2):
            pltpu.make_async_copy(out.at[block], out.at[block], sems.at[index, block]).wait()


def pack(info, sources, plan, shape):
    return pl.pallas_call(
        partial(pack_kernel, len(sources), plan),
        in_specs=[IN_SMEM] + [ANYWHERE] * len(sources),
        out_specs=[IN_VMEM] * len(plan),
        scratch_shapes=[pltpu.SemaphoreType.DMA((len(plan), 2))],
        out_shape=[jax.ShapeDtypeStruct(shape, BF16)] * len(plan),
        cost_estimate=SHORT,
        name="pack",
    )(info, *sources)


def over_section(value, bits, sources=range(SECTIONS)):
    return lax.ppermute(value, "section", [(at, at ^ bits) for at in sources])


def over_core(value):
    return lax.ppermute(value, "core", [(0, 1), (1, 0)])


def over_plane(value, pairs):
    return lax.ppermute(value, "z", pairs)


def added(left, right):
    return (left.astype(F32) + right.astype(F32)).astype(BF16)


def after(value, *earlier):
    return lax.optimization_barrier((value,) + earlier)[0]


def under(outputs, *arrivals):
    joined = lax.optimization_barrier(tuple(outputs) + arrivals)
    return list(joined[: len(outputs)]), list(joined[len(outputs) :])


def by_section(section, values):
    result, last = None, None
    for at in sorted(values):
        if result is None:
            result = values[at]
        elif values[at] is not last:
            result = jnp.where(section >= at, values[at], result)
        last = values[at]
    return result


def total(*values):
    result = values[0].astype(F32)
    for value in values[1:]:
        result = result + value.astype(F32)
    return result.astype(BF16)


class Sums:
    def __init__(self, travel):
        self.stay, self.move, self.other_stay, self.other_move = travel
        self.size = self.stay.shape[1] // 2

    def cross(self, *earlier):
        if earlier:
            self.other_move = after(self.other_move, *earlier)
            self.other_stay = after(self.other_stay, *earlier)
        self.got_move, self.got_stay = over_core(self.other_move), over_core(self.other_stay)

    def first_sends(self):
        size = self.size
        self.sent = [
            total(self.move[:, at : at + size], self.got_move[:, at : at + size])
            for at in (0, size)
        ]
        return self.sent

    def second_sends(self, from_x, from_y):
        size, half = self.size, self.size // 2
        self.first = from_x, from_y
        to_y = total(self.stay[:, half:size], self.got_stay[:, half:size], from_x[:, half:])
        to_x = total(
            self.stay[:, size + half :], self.got_stay[:, size + half :], from_y[:, half:]
        )
        self.sent = [to_x, to_y]
        return self.sent

    def whole(self, from_x, from_y):
        size, half = self.size, self.size // 2
        parts = []
        for at, first, second in ((0, self.first[0], from_y), (size, self.first[1], from_x)):
            here = slice(at, at + half)
            parts.append(total(self.stay[:, here], self.got_stay[:, here], first[:, :half], second))
        return jnp.concatenate(parts, axis=1)


def over_links(sends):
    return [over_section(sends[0], 1), over_section(sends[1], 2)]


class Planes:
    def __init__(self, value, plane, planes):
        self.value, self.plane, self.planes, self.turn = value, plane, planes, 0

    def sends(self, *earlier):
        value = after(self.value, *earlier) if earlier else self.value
        if self.planes != 4:
            return (value,)
        bits = (1, 2, 2, 1)[self.turn]
        if self.turn < 2:
            bit = (self.plane & 1, self.plane >> 1)[self.turn]
            size = value.shape[-1] // 2
            value = lax.dynamic_slice_in_dim(value, (1 - bit) * size, size, value.ndim - 1)
        return (over_plane(value, [(at, at ^ bits) for at in range(4)]),)

    def take(self, arrived):
        if self.planes != 4:
            self.value = lax.psum(arrived, "z") if self.turn == 3 else arrived
        elif self.turn < 2:
            bit = (self.plane & 1, self.plane >> 1)[self.turn]
            size = self.value.shape[-1] // 2
            keep = lax.dynamic_slice_in_dim(self.value, bit * size, size, self.value.ndim - 1)
            self.value = added(keep, arrived)
        else:
            self.value = jnp.concatenate([self.value, arrived], axis=-1)
        self.turn += 1

    def in_order(self, value):
        if self.planes != 4:
            return value
        size, turn = value.shape[-1] // 4, plane_turn(self.plane, 4)
        parts = [
            lax.dynamic_slice_in_dim(value, (at ^ turn) * size, size, value.ndim - 1)
            for at in range(4)
        ]
        return jnp.concatenate(parts, axis=-1)


class Weights:
    def __init__(self, own, info, planes):
        self.own, self.info = own, info
        self.four = planes == 4
        self.plan = PLAN_FOUR if self.four else PLAN_ANY
        self.half, self.width = own[1].shape[0] // 2, own[1].shape[1]
        self.mine, self.theirs, self.arrived = {}, {}, {}

    def place(self, layer, block):
        if layer in "ac":
            return (0, 0, block * self.width) if block < 3 else (1, 0, 0)
        if layer == "g":
            return (2, 0, block * self.width) if block < 4 else (3, (block - 4) * self.width, 0)
        return (2, 0, block * self.width) if block < 4 else (3, (block - 4) * self.width, 0)

    def choices(self, sends, sources):
        result = []
        for at in range(SECTIONS):
            name = sends.get(at)
            if name is not None and HOMES[name[0]] != at:
                key = self.arrived[at, name]
                if key not in sources:
                    sources[key] = len(self.own) + len(sources)
                result.append((at, None, [("arrived", sources[key])] * 2))
                continue
            for plane in range(4) if name == "F" else (None,):
                piece = ("f" + str(plane)) if name == "F" else name or "a0"
                layer, index = piece[0], int(piece[1])
                if layer in "ac":
                    blocks = ATTEND_BLOCKS[index]
                else:
                    blocks = (index, 4 + index) if layer == "g" else EXPERT_BLOCKS[index]
                parts = [("own",) + self.place(layer, block) for block in blocks]
                result.append((at, plane, parts))
        return result

    def packed(self, wanted):
        sources = {}
        plan = [self.choices(sends, sources) for sends in wanted]
        arrays = list(self.own) + [self.mine[key] for key in sources]
        return pack(self.info, arrays, plan, (2, self.half, self.width))

    def sends(self, step):
        if step == "F":
            return [{at: "F" for at in range(SECTIONS)}]
        return [sends for sends in self.plan[step] if sends]

    def payloads(self, *steps):
        wanted = [sends for step in steps for sends in self.sends(step)]
        return list(self.packed(wanted))

    def move(self, step, payloads):
        links = [(link, sends) for link, sends in enumerate(self.plan[step]) if sends]
        for (link, sends), payload in zip(links, payloads):
            self.mine[step, link] = over_section(payload, link + 1, sorted(sends))
            for at, name in sends.items():
                self.arrived[at ^ (link + 1), name] = (step, link)
        return [(step, link) for link, _ in links]

    def move_planes(self, step):
        up, down = self.mine["plane", step - 1], self.mine["plane", 1 - step]
        up = over_plane(up, [(at, at + 1) for at in range(step - 1, 3)])
        down = over_plane(down, [(at, at - 1) for at in range(4 - step, 0, -1)])
        self.mine["plane", step], self.mine["plane", -step] = up, down
        return [("plane", step), ("plane", -step)]

    def cross(self, keys):
        for key in keys:
            self.theirs[key] = over_core(self.mine[key])
        return keys

    def join(self, outputs, mine=(), theirs=()):
        values = [self.mine[key] for key in mine] + [self.theirs[key] for key in theirs]
        outputs, values = under(outputs, *values)
        for key, value in zip(mine, values):
            self.mine[key] = value
        for key, value in zip(theirs, values[len(mine) :]):
            self.theirs[key] = value
        return outputs

    def layer(self, layer):
        arrays, places = list(self.own), {}

        def place(key):
            if key not in places:
                places[key] = len(arrays)
                arrays.extend([self.mine[key], self.theirs[key]])
            return places[key], places[key] + 1

        if layer in "ac":
            names = [(layer + str(index), ATTEND_BLOCKS[index]) for index in range(2)]
        else:
            names = [(layer + str(index), EXPERT_BLOCKS[index]) for index in range(4)]
        plan = []
        for at in range(SECTIONS):
            if layer == "g":
                names = [("g" + str(at), (0, 1))]
            if HOMES[layer] == at:
                steps = []
                for name, blocks in names:
                    for block in blocks:
                        source = block * 4 if layer == "g" else block
                        steps.append((block, ("own",) + self.place(layer, source)))
                plan.append((at, None, steps))
                continue
            by_plane = layer == "f" and self.four
            for plane in range(4) if by_plane else (None,):
                steps = []
                for index, (name, blocks) in enumerate(names):
                    key = ("plane", plane - index) if by_plane else self.arrived[at, name]
                    for which, block in enumerate(blocks):
                        steps.append((block, ("piece",) + place(key) + (which,)))
                plan.append((at, plane, steps))
        return arrays, plan


def per_device(
    tokens,
    caption_lengths,
    attend_gain,
    attend_shift,
    attend_inputs,
    attend_bias,
    attend_output,
    expert_gain,
    expert_shift,
    expert_inputs,
    expert_inner_bias,
    expert_outputs,
    expert_outer_bias,
    cotangent,
):
    section, core, plane = lax.axis_index("section"), lax.axis_index("core"), lax.axis_index("z")
    planes = lax.axis_size("z")
    items, positions, width = tokens.shape
    hidden = expert_inputs.shape[-1]
    info = [value.reshape(1).astype(jnp.int32) for value in (section, core, plane)]
    info = jnp.concatenate([caption_lengths] + info)
    weights = Weights(
        (attend_inputs[0], attend_output[0], expert_inputs[0], expert_outputs[0]), info, planes
    )

    def to_sections(value):
        return [value] + [over_section(value, bits) for bits in (1, 2, 3)]

    def items_of(part):
        return part.reshape(items, CAP_ROWS, width)

    keys = weights.move(0, weights.payloads(0))
    pad = ((0, 0), (0, ROWS - positions), (0, 0))
    x0 = jnp.pad(tokens, pad)
    last_grad = jnp.pad(cotangent, pad)
    rows = jnp.concatenate(
        [
            attend_gain,
            attend_shift,
            attend_bias,
            expert_gain,
            expert_shift,
            expert_inner_bias,
            expert_outer_bias,
            jnp.full((1, 128), jnp.sum(caption_lengths), F32),
        ],
        axis=1,
    )
    rows = to_sections(rows)
    x0, last_grad, *rows = weights.join([x0, last_grad, *rows], keys)
    keys1 = weights.move(1, weights.payloads(1))
    rows = jnp.concatenate(rows, axis=0)
    language_count = jnp.sum(rows[:, -128:], axis=0, keepdims=True)
    rows = [lax.dynamic_index_in_dim(rows, at ^ section, 0) for at in range(SECTIONS)]
    sizes = [width, width, 3 * width, width, width, hidden, width]
    ends = [sum(sizes[: at + 1]) for at in range(len(sizes))]
    used = [(0, 0), (0, 1), (0, 2), (0, 3), (0, 4), (0, 5), (1, 3), (1, 4), (1, 5), (1, 6)]
    used += [(0, 6), (2, 0), (2, 1), (2, 2), (3, 3), (3, 4), (3, 5), (3, 6)]
    kept = [rows[slot][:, ends[which] - sizes[which] : ends[which]] for slot, which in used]
    language_count, *kept = weights.join([language_count, *kept], keys1)
    kept = dict(zip(used, kept))

    def row(slot, which):
        return kept[slot, which]

    crossed = weights.cross(keys + keys1)
    sends = weights.payloads(2, "F") if weights.four else weights.payloads(2)
    sends, (info, language_count) = under(sends, info, language_count)
    keys = weights.move(2, sends[:2])
    info, language_count = weights.join(
        [info, language_count + over_core(language_count)], theirs=crossed
    )
    if weights.four:
        weights.mine["plane", 0] = sends[2]
        keys += weights.move_planes(1)
    attend0 = weights.layer("a")
    outputs = attend_forward(
        x0, info, attend0, row(0, 0), row(0, 1), row(0, 2), following=(row(0, 3), row(0, 4))
    )
    y0, qkv0, mixed0, caption_rows = weights.join(outputs, keys)
    caption_rows = to_sections(caption_rows.reshape(-1, width))
    crossed = weights.cross([(2, 0), (2, 1)])
    sends = weights.payloads(3)
    if weights.four:
        language_count += over_plane(language_count, [(at, at ^ 1) for at in range(4)])
    *caption_rows, language_count = weights.join([*caption_rows, language_count], theirs=crossed)
    sends, caption_rows = under(sends, *caption_rows)
    keys = weights.move(3, sends)
    if weights.four:
        keys += weights.move_planes(2)
        language_count += over_plane(language_count, [(at, at ^ 2) for at in range(4)])
    else:
        language_count = lax.psum(language_count, "z")
    outputs = shared_forward(caption_rows, expert_inputs[0], expert_inner_bias, expert_outputs[0])
    *part, language_count = weights.join([*outputs, language_count], keys)
    language_count = language_count[0, 0].astype(jnp.int32)
    vision_count = PATCHES * items * SECTIONS * 2 * planes
    counts = jnp.stack(
        [jnp.full((), vision_count, jnp.int32), language_count, language_count + vision_count]
    )
    crossed = weights.cross([(3, 0), (3, 1)])
    branch = {at: over_section(part[at], at, [0]) for at in range(1, SECTIONS)}
    keys = weights.move_planes(3) if weights.four else []
    (y0,) = weights.join([y0], theirs=crossed)
    expert1 = weights.layer("e")
    outputs = expert_forward(
        y0, info, expert1, row(1, 3), row(1, 4), row(1, 5), row(1, 6), PATCH_ROWS, "patch"
    )
    outputs, moved = under(outputs, *branch.values())
    x2, act1, slope1 = weights.join(outputs, keys)
    branch = dict(zip(branch, moved))
    branch[0] = part[0]
    branch = items_of(by_section(section, branch))
    if weights.four:
        crossed = [("plane", step) for step in range(-3, 4)]
    else:
        for step in (4, 5):
            weights.move(step, weights.payloads(step))
        crossed = [(4, 0), (4, 1), (5, 0)]
    weights.cross(crossed)
    attend2 = weights.layer("c") if weights.four else None
    if not weights.four:
        (x2,) = weights.join([x2], theirs=crossed)
        attend2 = weights.layer("c")
    outputs = attend_forward(
        x2, info, attend2, row(2, 0), row(2, 1), row(2, 2), merge=(y0, branch, row(0, 6))
    )
    x3, qkv2, mixed2, x2 = weights.join(outputs, theirs=crossed)
    expert3 = weights.layer("f")
    layer_output, act3, slope3 = expert_forward(
        x3, info, expert3, row(3, 3), row(3, 4), row(3, 5), row(3, 6), ROWS, "all"
    )

    def small_rows(values):
        flat = jnp.concatenate(values, axis=1)
        count = -(-flat.shape[1] // hidden)
        flat = jnp.pad(flat, ((0, 0), (0, count * hidden - flat.shape[1])))
        return flat.reshape(count, hidden)

    def to_home(sums):
        got = [by_section(section, sums)]
        for bits in (1, 2, 3):
            sends = {at ^ bits: sums[at] for at in sums}
            got.append(over_section(by_section(section, sends), bits, sorted(sends)))
        return got

    keys = []
    if weights.four:
        sends, (layer_output, last_grad) = under(weights.payloads(4), layer_output, last_grad)
        keys = weights.move(4, sends)
    outputs = expert_backward(
        x3, info, expert3, row(3, 3), row(3, 4), act3, slope3, last_grad, ROWS, "all"
    )
    outputs = weights.join(outputs, keys)
    crossed = weights.cross(keys)
    grad3, *small3 = outputs[:5]
    sums3 = Sums(outputs[5:])
    sums3.cross()
    moved = over_links(sums3.first_sends())
    grad3 = after(grad3, *sums3.sent)
    outputs = attend_backward(
        x2, info, attend2, row(2, 0), row(2, 1), qkv2, mixed2, grad3
    )
    outputs, moved = under(outputs, *moved, sums3.got_stay)
    outputs = weights.join(outputs, theirs=crossed)
    grad2, *small2 = outputs[:4]
    sums2, caption_grad = Sums(outputs[4:8]), outputs[8]
    caption_grads = to_sections(caption_grad.reshape(-1, width))
    sums3.got_stay = moved[2]
    moved3 = over_links(sums3.second_sends(*moved[:2]))
    grad2 = after(grad2, *sums3.sent)
    outputs = expert_backward(
        y0, info, expert1, row(1, 3), row(1, 4), act1, slope1, grad2, PATCH_ROWS, "patch"
    )
    outputs, caption_grads = under(outputs, *caption_grads)
    grad1, *small1 = outputs[:5]
    sums2.cross(grad1)
    sums1 = Sums(outputs[5:])
    sums1.cross()
    inner_quarter = lax.dynamic_slice(row(0, 5), (0, section * width), (1, width))
    sum3 = sums3.whole(*moved3)
    inner_quarter = after(inner_quarter, grad1, sum3)
    outputs = shared_backward(
        caption_rows, caption_grads, info, weights.layer("g"), inner_quarter
    )
    parts, (keep0, send0, inner_grad, outer_grad) = outputs[:4], outputs[4:]
    got = [over_section(parts[bits], bits) for bits in (1, 2, 3)]
    sends = [after(value, *parts) for value in sums1.first_sends()]
    moved1 = over_links(sends)
    keep0 = added(keep0, over_core(send0))
    early = lax.psum(jnp.concatenate([sum3, keep0], axis=0), "z")
    sends2 = [after(value, *sends) for value in sums2.first_sends()]
    moved2 = over_links(sends2)
    parts = [parts[0], *got]
    grad1 = after(grad1, keep0, *sends, *sends2)
    outputs = attend_backward(
        x0,
        info,
        attend0,
        row(0, 0),
        row(0, 1),
        qkv0,
        mixed0,
        grad1,
        first=(y0, row(0, 3), parts),
    )
    outputs, moved = under(outputs, *moved2, *moved1)
    moved2, moved1 = moved[:2], moved[2:]
    tokens_grad, *small_first = outputs[:4]
    sums_first, gain_grad, shift_grad = Sums(outputs[4:8]), outputs[8], outputs[9]
    sums_first.cross()
    inner_grad = lax.dynamic_update_slice(
        jnp.zeros((1, hidden), F32), inner_grad, (0, section * width)
    )
    small = small_rows(
        small_first + [gain_grad, shift_grad, inner_grad, outer_grad] + small2 + small1 + small3
    )
    small = added(small, over_core(small))
    to_x, to_y = sums_first.first_sends()
    to_x = jnp.concatenate([to_x[0], small], axis=0)
    sends = lax.optimization_barrier((*sums1.second_sends(*moved1), to_x, to_y))
    moved1, moved = over_links(sends[:2]), over_links(sends[2:])
    planes1 = Planes(sums1.whole(*moved1), plane, planes)
    size = to_y.shape[1]
    small = added(small, moved[0][size:])
    to_x, to_y = sums_first.second_sends(moved[0][None, :size], moved[1])
    early_x, early_y = sums2.second_sends(*moved2)
    to_x = jnp.concatenate([to_x[0], early_x[0]], axis=0)
    to_y = jnp.concatenate([to_y[0], early_y[0], small], axis=0)
    to_x, to_y = lax.optimization_barrier((to_x, to_y))
    moved = [*over_links((to_x, to_y)), *planes1.sends()]
    moved = lax.optimization_barrier(tuple(moved))
    planes1.take(moved[2])
    size = early_x.shape[1]
    last = sums_first.whole(moved[0][None, :size], moved[1][None, :size])
    sum2 = sums2.whole(moved[0][None, size:], moved[1][None, size : 2 * size])
    small = added(small, moved[1][2 * size :])
    small_count = small.shape[0]
    eighth = last.shape[1]
    last = jnp.concatenate([last[0], sum2[0], small], axis=0)
    last = lax.psum(after(last, early), "z")
    planes1.take(*planes1.sends())
    home_early = to_home({0: after(early[2:], planes1.value), 3: after(early[:2], planes1.value)})
    planes1.take(*planes1.sends())
    planes1.take(*planes1.sends())
    home_late = to_home({1: after(planes1.value, *home_early[1:3])})
    home_attend = to_home({0: last[None, :eighth], 2: last[None, eighth : 2 * eighth]})
    small = last[2 * eighth :].astype(F32)

    as_float = counts.astype(F32)
    one = jnp.ones((), F32)
    attend_scales = jnp.stack([as_float[2], one, as_float[2], one])
    expert_scales = jnp.stack([as_float[1], as_float[0], one, as_float[2]])

    def placed(pieces, scales):
        scale = lax.dynamic_index_in_dim(scales, section, 0).reshape(1, 1)
        pieces = jnp.stack(pieces)
        return finish(info, scale, pieces, over_core(pieces), planes)

    blank = jnp.zeros_like(home_late[0])
    inputs_whole, outputs_whole = placed(
        [
            by_section(section, {0: early, 1: late, 2: blank, 3: early})
            for early, late in zip(home_early, home_late)
        ],
        expert_scales,
    )
    blank = jnp.zeros_like(home_attend[0])
    attend_whole, output_whole = placed(
        [by_section(section, {0: got, 1: blank, 2: got, 3: blank}) for got in home_attend],
        attend_scales,
    )

    attend_size, expert_size = 5 * width, 3 * width + hidden
    cuts = [attend_size, attend_size + expert_size]
    cuts += [cuts[1] + attend_size, cuts[1] + attend_size + expert_size]
    small = jnp.split(small.reshape(-1)[: cuts[3] + expert_size], cuts)
    none_attend, none_expert = jnp.zeros_like(small[0]), jnp.zeros_like(small[1])
    attend_small = jnp.stack([small[0], none_attend, small[2], none_attend])
    expert_small = jnp.stack([small[1], small[3], none_expert, small[4]])
    attend_small = attend_small / attend_scales.reshape(-1, 1)
    expert_small = expert_small / expert_scales.reshape(-1, 1)
    attend_small = lax.dynamic_index_in_dim(attend_small, section, 0)
    expert_small = lax.dynamic_index_in_dim(expert_small, section, 0)
    return (
        layer_output[:, :positions],
        tokens_grad[:, :positions],
        attend_small[:, :width],
        attend_small[:, width : 2 * width],
        attend_whole,
        attend_small[:, 2 * width :],
        output_whole,
        expert_small[:, :width],
        expert_small[:, width : 2 * width],
        inputs_whole,
        expert_small[:, 2 * width : 2 * width + hidden],
        outputs_whole,
        expert_small[:, 2 * width + hidden :],
        counts,
    )


def solution(mesh):
    sections, groups = mesh.shape["section"], mesh.shape["dp"]
    split = Mesh(mesh.devices.reshape(sections, groups // 2, 2), ("section", "z", "core"))
    items = P(("section", "z", "core"), None, None)
    flat = P("section", None)
    matrix = P("section", None, None)
    placed = (
        items,
        P(("section", "z", "core")),
        flat,
        flat,
        matrix,
        flat,
        matrix,
        flat,
        flat,
        matrix,
        flat,
        matrix,
        flat,
        items,
    )
    return jax.shard_map(
        per_device,
        mesh=split,
        in_specs=placed,
        out_specs=(
            items,
            items,
            flat,
            flat,
            matrix,
            flat,
            matrix,
            flat,
            flat,
            matrix,
            flat,
            matrix,
            flat,
            P(),
        ),
        check_vma=False,
    )
```

```python
from functools import partial

import jax
import jax.numpy as jnp
from jax import lax
from jax.experimental import pallas as pl
from jax.experimental.pallas import tpu as pltpu
from jax.sharding import Mesh
from jax.sharding import PartitionSpec as P

HEADS = 12
HEAD_DIM = 64
PATCHES = 197
ROWS = 256
CAP_FIRST, CAP_ROWS = 192, 48
PATCH_ROWS = 208
PAIR = 2 * HEAD_DIM
SECTIONS = 4
PIECE_ROWS = 48
VMEM_BYTES = 58 * 1024 * 1024
F32 = jnp.float32
BF16 = jnp.bfloat16

PLAN_FOUR = (
    ({0: "a0", 1: "e0", 2: "c0", 3: "F"}, {0: "a1", 1: "e2", 2: "c0", 3: "F"}),
    ({0: "a1", 1: "e1", 2: "a1", 3: "e2"}, {0: "a0", 1: "a0", 2: "F", 3: "c0"}),
    ({0: "g3", 1: "e2", 2: "c1"}, {0: "e0", 1: "e3", 2: "c1"}),
    ({0: "g1", 1: "e3", 2: "e0", 3: "e3"}, {0: "e1", 1: "e1", 3: "c1"}),
    ({}, {0: "g2", 1: "g3"}),
)
PLAN_ANY = (
    ({0: "a0", 1: "e0", 2: "c0", 3: "f0"}, {0: "a1", 1: "e2", 2: "c0", 3: "f0"}),
    ({0: "a1", 1: "e1", 2: "a1", 3: "e2"}, {0: "a0", 1: "a0", 2: "c1", 3: "f1"}),
    ({0: "g3", 1: "e2", 2: "c1", 3: "f1"}, {0: "e0", 1: "e3", 2: "f0", 3: "f2"}),
    ({0: "g1", 1: "e3", 2: "e0", 3: "e3"}, {0: "e1", 1: "e1", 2: "f1", 3: "f3"}),
    ({0: "c1", 1: "f2", 3: "f2"}, {0: "g2", 1: "g3", 3: "c0"}),
    ({1: "f3", 3: "f3"}, {}),
)
HOMES = {"a": 0, "c": 2, "e": 1, "f": 3, "F": 3, "g": 0}
ATTEND_BLOCKS = ((0, 1), (2, 3))
EXPERT_BLOCKS = ((0, 1), (4, 5), (2, 3), (6, 7))


def dot_plain(left, right):
    return jnp.dot(left, right, preferred_element_type=F32)


def dot_last(left, right):
    return lax.dot_general(left, right, (((1,), (1,)), ((), ())), preferred_element_type=F32)


def dot_first(left, right):
    return lax.dot_general(left, right, (((0,), (0,)), ((), ())), preferred_element_type=F32)


def column_sum(matrix):
    return jnp.sum(matrix.astype(F32), axis=0, keepdims=True)


def norm_parts(rows):
    centre = rows - jnp.mean(rows, axis=-1, keepdims=True)
    scale = lax.rsqrt(jnp.mean(centre * centre, axis=-1, keepdims=True) + 1e-06)
    return centre * scale, scale


def norm_back(normed_grad, unit, scale, gain):
    unit_grad = normed_grad * gain
    along = jnp.mean(unit_grad * unit, axis=-1, keepdims=True)
    return scale * (unit_grad - jnp.mean(unit_grad, axis=-1, keepdims=True) - unit * along)


def true_positions(length, first, count, axis, kind):
    shape = (count, 1) if axis == 0 else (1, count)
    position = first + lax.broadcasted_iota(jnp.int32, shape, axis)
    patch = position < PATCHES
    if kind == "patch":
        return patch
    caption = (position >= PATCHES) & (position - PATCHES < length)
    return caption if kind == "caption" else patch | caption


def head_masks():
    lane = lax.broadcasted_iota(jnp.int32, (1, PAIR), 1)
    even = (lane < HEAD_DIM).astype(F32).astype(BF16)
    odd = (lane >= HEAD_DIM).astype(F32).astype(BF16)
    return lane < HEAD_DIM, even, odd


def split_pair(pair, even, odd):
    return jnp.concatenate([pair * even, pair * odd], axis=0)


def start_weights(info, first, refs, plan, blocks, sems):
    half = blocks.shape[1] // 2
    section, core, plane = info[first], info[first + 1], info[first + 2]
    for at, at_plane, steps in plan:
        here = section == at
        if at_plane is not None:
            here = here & (plane == at_plane)

        @pl.when(here)
        def _(steps=steps):
            for block, source in steps:
                if source[0] == "own":
                    _, which, row, column = source
                    width = blocks.shape[2]
                    for part in range(2):
                        pltpu.make_async_copy(
                            refs[which].at[
                                pl.ds(row + part * half, half), pl.ds(column, width)
                            ],
                            blocks.at[block, pl.ds(part * half, half)],
                            sems.at[block],
                        ).start()
                else:
                    _, mine, theirs, index = source
                    pltpu.make_async_copy(
                        refs[mine].at[index],
                        blocks.at[block, pl.ds(pl.multiple_of(core * half, half), half)],
                        sems.at[block],
                    ).start()
                    pltpu.make_async_copy(
                        refs[theirs].at[index],
                        blocks.at[block, pl.ds(pl.multiple_of((1 - core) * half, half), half)],
                        sems.at[block],
                    ).start()


def wait_block(blocks, block, sems):
    pltpu.make_async_copy(blocks.at[block], blocks.at[block], sems.at[block]).wait()


def store_turned(target, turned, columns, section, core):
    half = target.shape[0] // 2
    for piece in range(16):
        path, owner = (piece >> 2) & 1, piece & 3
        away = owner ^ section
        place = ((away & 1) << 1) | (away >> 1) if path == 0 else away
        row = ((piece >> 3) ^ core) * half + (place >> 1) * (half // 2)
        row = row + path * (half // 4) + (place & 1) * PIECE_ROWS
        target[pl.ds(pl.multiple_of(row, 16), PIECE_ROWS), columns] = turned[
            piece * PIECE_ROWS : (piece + 1) * PIECE_ROWS
        ]


def put_travel(refs, which, columns, left, right):
    half = left.shape[0] // 2
    for side in range(2):
        rows = dot_plain(left[side * half : (side + 1) * half], right).astype(BF16)
        refs[2 * side][which, :, columns] = rows[: half // 2]
        refs[2 * side + 1][which, :, columns] = rows[half // 2 :]


def attend_forward_kernel(plan, weight_count, merge, info, *refs):
    weights, refs = refs[:weight_count], refs[weight_count:]
    if merge:
        x_ref, before_ref, part_ref, outer_ref, gain_ref, shift_ref, bias_ref = refs[:7]
        y_ref, qkv_ref, mixed_ref, joined_ref, blocks, sems, joined = refs[7:]
    else:
        x_ref, gain_ref, shift_ref, bias_ref, next_gain_ref, next_shift_ref = refs[:6]
        y_ref, qkv_ref, mixed_ref, caption_ref, blocks, sems = refs[6:]
    item = pl.program_id(0)
    items = pl.num_programs(0)
    length = info[item]
    width = x_ref.shape[-1]

    @pl.when(item == 0)
    def _():
        start_weights(info, items, weights, plan, blocks, sems)

    cap = slice(CAP_FIRST, CAP_FIRST + CAP_ROWS)
    if merge:
        joined[...] = x_ref[0].astype(F32)
        branch = part_ref[0].astype(F32) + outer_ref[...]
        is_true = true_positions(length, CAP_FIRST, CAP_ROWS, 0, "caption")
        captions = before_ref[0, cap] + jnp.where(is_true, branch, 0.0)
        position = CAP_FIRST + lax.broadcasted_iota(jnp.int32, (CAP_ROWS, 1), 0)
        captions = captions.astype(BF16).astype(F32)
        joined[cap] = jnp.where(position < PATCHES, joined[cap], captions)
        x = joined[...]
        joined_ref[0] = x.astype(BF16)
    else:
        x = x_ref[0].astype(F32)
    unit, _ = norm_parts(x)
    normed = (unit * gain_ref[...] + shift_ref[...]).astype(BF16)

    @pl.when(item == 0)
    def _():
        for block in range(4):
            wait_block(blocks, block, sems)

    queries = dot_plain(normed, blocks[0]) + bias_ref[:, :width]
    qkv_ref[0, :, :width] = (queries * HEAD_DIM ** (-0.5)).astype(BF16)
    qkv_ref[0, :, width : 2 * width] = dot_plain(normed, blocks[1]).astype(BF16)
    values = dot_plain(normed, blocks[2]) + bias_ref[:, width : 2 * width]
    qkv_ref[0, :, 2 * width :] = values.astype(BF16)
    key_true = true_positions(length, 0, ROWS, 1, "all")
    low_half, even, odd = head_masks()
    ones = jnp.ones((ROWS, PAIR), BF16)

    def scores_of(pair):
        at = pair * PAIR
        q2 = qkv_ref[0, :, at : at + PAIR]
        k2 = qkv_ref[0, :, width + at : width + at + PAIR]
        return dot_last(split_pair(q2, even, odd), k2)

    ahead = [scores_of(0), scores_of(1)]
    for pair in range(HEADS // 2):
        at = pair * PAIR
        scores = jnp.where(key_true, ahead.pop(0), -1e9)
        if pair + 2 < HEADS // 2:
            ahead.append(scores_of(pair + 2))
        weight = jnp.exp(scores - jnp.max(scores, axis=-1, keepdims=True)).astype(BF16)
        v2 = qkv_ref[0, :, 2 * width + at : 2 * width + at + PAIR]
        summed = dot_plain(weight, jnp.concatenate([v2, ones], axis=1))
        top = jnp.where(low_half, summed[:ROWS, :PAIR], summed[ROWS:, :PAIR])
        below = jnp.where(low_half, summed[:ROWS, PAIR:], summed[ROWS:, PAIR:])
        mixed_ref[0, :, at : at + PAIR] = (top / below).astype(BF16)
    branch = dot_plain(mixed_ref[0], blocks[3]) + bias_ref[:, 2 * width :]
    row_true = true_positions(length, 0, ROWS, 0, "all")
    y = x + jnp.where(row_true, branch, 0.0)
    y_ref[0] = y.astype(y_ref.dtype)
    if not merge:
        unit, _ = norm_parts(y[cap])
        caption_ref[0] = (unit * next_gain_ref[...] + next_shift_ref[...]).astype(BF16)


def attend_backward_kernel(plan, weight_count, first, info, *refs):
    weights, refs = refs[:weight_count], refs[weight_count:]
    x_ref, gain_ref, shift_ref, qkv_ref, mixed_ref, grad_ref = refs[:6]
    if first:
        after_ref, next_gain_ref, *parts = refs[6:12]
        refs = refs[12:]
    else:
        refs = refs[6:]
    out_ref, gain_grad_ref, shift_grad_ref, bias_grad_ref = refs[:4]
    travel_refs = refs[4:8]
    if first:
        next_gain_grad_ref, next_shift_grad_ref, joined = refs[8], refs[9], refs[-1]
    else:
        caption_ref = refs[8]
    blocks, sems, normed_turned, mixed_turned, branch_all, projected, mixed_grad = refs[
        10 if first else 9 :
    ][:7]
    item = pl.program_id(0)
    items = pl.num_programs(0)
    length = info[item]
    section, core = info[items], info[items + 1]
    width = x_ref.shape[-1]
    here = pl.ds(pl.multiple_of(item * ROWS, ROWS), ROWS)
    cap = slice(CAP_FIRST, CAP_FIRST + CAP_ROWS)

    @pl.when(item == 0)
    def _():
        start_weights(info, items, weights, plan, blocks, sems)

    def add_to(ref, part):
        @pl.when(item == 0)
        def _():
            ref[...] = part

        @pl.when(item > 0)
        def _():
            ref[...] += part

    x = x_ref[0].astype(F32)
    unit, scale = norm_parts(x)
    normed = (unit * gain_ref[...] + shift_ref[...]).astype(BF16)
    incoming = grad_ref[0].astype(F32)
    if first:
        after_unit, after_scale = norm_parts(after_ref[0, cap])
        caption_grad = parts[0][...].astype(F32)
        for part in parts[1:]:
            caption_grad = caption_grad + part[...].astype(F32)
        joined[...] = incoming
        joined[cap] += norm_back(caption_grad, after_unit, after_scale, next_gain_ref[...])
        incoming = joined[...]
        add_to(next_gain_grad_ref, jnp.sum(caption_grad * after_unit, axis=0, keepdims=True))
        add_to(next_shift_grad_ref, jnp.sum(caption_grad, axis=0, keepdims=True))
    row_true = true_positions(length, 0, ROWS, 0, "all")
    branch = jnp.where(row_true, incoming, 0.0).astype(BF16)
    branch_all[here, :] = branch
    store_turned(normed_turned, normed.T, here, section, core)
    store_turned(mixed_turned, mixed_ref[0].T, here, section, core)

    @pl.when(item == 0)
    def _():
        for block in range(4):
            wait_block(blocks, block, sems)

    mixed_grad[...] = dot_last(branch, blocks[3]).astype(BF16)
    key_true = true_positions(length, 0, ROWS, 0, "all")
    _, even, odd = head_masks()

    def products_of(pair):
        at = pair * PAIR
        q2 = split_pair(qkv_ref[0, :, at : at + PAIR], even, odd)
        k2 = qkv_ref[0, :, width + at : width + at + PAIR]
        v2 = qkv_ref[0, :, 2 * width + at : 2 * width + at + PAIR]
        g2 = split_pair(mixed_grad[:, at : at + PAIR], even, odd)
        return q2, k2, g2, dot_last(k2, q2), dot_last(v2, g2)

    ahead = [products_of(0)]
    for pair in range(HEADS // 2):
        at = pair * PAIR
        q2, k2, g2, scores, weight_grad = ahead.pop(0)
        if pair + 1 < HEADS // 2:
            ahead.append(products_of(pair + 1))
        scores = jnp.where(key_true, scores, -1e9)
        weight = jnp.exp(scores - jnp.max(scores, axis=0, keepdims=True))
        weight = weight * (1.0 / jnp.sum(weight, axis=0, keepdims=True))
        product = weight * weight_grad
        along = jnp.sum(product, axis=0, keepdims=True)
        score_grad = (product - weight * along).astype(BF16)
        values_grad = dot_plain(weight.astype(BF16), g2).astype(BF16)
        keys_grad = dot_plain(score_grad, q2).astype(BF16)
        k2_split = split_pair(k2, even, odd)
        stacked = jnp.concatenate([score_grad[:, :ROWS], score_grad[:, ROWS:]], axis=0)
        queries_grad = dot_first(stacked, k2_split).astype(BF16)
        queries_grad = (queries_grad.astype(F32) * HEAD_DIM ** (-0.5)).astype(BF16)
        projected[here, at : at + PAIR] = queries_grad
        projected[here, width + at : width + at + PAIR] = keys_grad
        projected[here, 2 * width + at : 2 * width + at + PAIR] = values_grad
    normed_grad = dot_last(projected[here, :width], blocks[0])
    normed_grad += dot_last(projected[here, width : 2 * width], blocks[1])
    normed_grad += dot_last(projected[here, 2 * width :], blocks[2])
    out = (incoming + norm_back(normed_grad, unit, scale, gain_ref[...])).astype(BF16)
    out_ref[0] = out
    if not first:
        is_true = true_positions(length, CAP_FIRST, CAP_ROWS, 0, "caption")
        caption_ref[0] = jnp.where(is_true, out[cap].astype(F32), 0.0).astype(BF16)
    add_to(gain_grad_ref, jnp.sum(normed_grad * unit, axis=0, keepdims=True))
    add_to(shift_grad_ref, jnp.sum(normed_grad, axis=0, keepdims=True))

    @pl.when(item == items - 1)
    def _():
        for block in range(4):
            columns = slice(block * width, (block + 1) * width)
            left = normed_turned if block < 3 else mixed_turned
            right = projected[:, columns] if block < 3 else branch_all[...]
            put_travel(travel_refs, 0, columns, left, right)
        bias_grad_ref[:, :width] = column_sum(projected[:, :width])
        bias_grad_ref[:, width : 2 * width] = column_sum(projected[:, 2 * width :])
        bias_grad_ref[:, 2 * width :] = column_sum(branch_all[...])


SHORT = pl.CostEstimate(flops=0, bytes_accessed=100_000, transcendentals=0)
LONG = pl.CostEstimate(flops=30_000_000_000, bytes_accessed=30_000_000, transcendentals=0)
ANYWHERE = pl.BlockSpec(memory_space=pl.ANY)


def whole_block(shape):
    return pl.BlockSpec(shape, lambda step, info: (0,) * len(shape))


def item_block(shape):
    return pl.BlockSpec((1,) + shape[1:], lambda step, info: (step,) + (0,) * (len(shape) - 1))


def blocks_scratch(count, width):
    return [pltpu.VMEM((count, width, width), BF16), pltpu.SemaphoreType.DMA((count,))]


def attend_forward(x, info, weights, gain, shift, bias, merge=None, following=None):
    arrays, plan = weights
    items, _, width = x.shape
    row = whole_block((1, width))
    bias_row = whole_block((1, 3 * width))
    caption_shape = (items, CAP_ROWS, width)
    if merge is not None:
        before, part, outer = merge
        operands = (x, before, part, outer, gain, shift, bias)
        specs = [item_block(x.shape), item_block(x.shape), item_block(caption_shape)]
        specs += [row, row, row, bias_row]
        last_shape, kind, scratch = x.shape, BF16, [pltpu.VMEM((ROWS, width), F32)]
    else:
        operands = (x, gain, shift, bias, *following)
        specs = [item_block(x.shape), row, row, bias_row, row, row]
        last_shape, kind, scratch = caption_shape, F32, []
    return pl.pallas_call(
        partial(attend_forward_kernel, plan, len(arrays), merge is not None),
        grid_spec=pltpu.PrefetchScalarGridSpec(
            num_scalar_prefetch=1,
            grid=(items,),
            in_specs=[ANYWHERE] * len(arrays) + specs,
            out_specs=[
                item_block(x.shape),
                item_block((items, ROWS, 3 * width)),
                item_block((items, ROWS, width)),
                item_block(last_shape),
            ],
            scratch_shapes=blocks_scratch(4, width) + scratch,
        ),
        out_shape=[
            jax.ShapeDtypeStruct(x.shape, kind),
            jax.ShapeDtypeStruct((items, ROWS, 3 * width), BF16),
            jax.ShapeDtypeStruct((items, ROWS, width), BF16),
            jax.ShapeDtypeStruct(last_shape, BF16),
        ],
        compiler_params=pltpu.CompilerParams(vmem_limit_bytes=VMEM_BYTES),
        cost_estimate=SHORT,
        name="attend_forward",
    )(info, *arrays, *operands)


def attend_backward(x, info, weights, gain, shift, qkv, mixed, incoming, first=None):
    arrays, plan = weights
    items, _, width = x.shape
    half = width // 2
    row = whole_block((1, width))
    caption_shape = (items, CAP_ROWS, width)
    operands = (x, gain, shift, qkv, mixed, incoming)
    specs = [item_block(x.shape), row, row, item_block(qkv.shape), item_block(mixed.shape)]
    specs += [item_block(incoming.shape)]
    outs = [
        (item_block(x.shape), x.shape, BF16),
        (row, (1, width), F32),
        (row, (1, width), F32),
        (whole_block((1, 3 * width)), (1, 3 * width), F32),
    ]
    outs += [(whole_block((1, half // 2, 4 * width)), (1, half // 2, 4 * width), BF16)] * 4
    scratch = []
    if first is not None:
        after, next_gain, parts = first
        operands += (after, next_gain, *parts)
        caption_rows = pl.BlockSpec((CAP_ROWS, width), lambda step, info: (step, 0))
        specs += [item_block(after.shape), row] + [caption_rows] * 4
        outs += [(row, (1, width), F32)] * 2
        scratch = [pltpu.VMEM((ROWS, width), F32)]
    else:
        outs += [(item_block(caption_shape), caption_shape, BF16)]
    return pl.pallas_call(
        partial(attend_backward_kernel, plan, len(arrays), first is not None),
        grid_spec=pltpu.PrefetchScalarGridSpec(
            num_scalar_prefetch=1,
            grid=(items,),
            in_specs=[ANYWHERE] * len(arrays) + specs,
            out_specs=[spec for spec, _, _ in outs],
            scratch_shapes=blocks_scratch(4, width)
            + [
                pltpu.VMEM((width, items * ROWS), BF16),
                pltpu.VMEM((width, items * ROWS), BF16),
                pltpu.VMEM((items * ROWS, width), BF16),
                pltpu.VMEM((items * ROWS, 3 * width), BF16),
                pltpu.VMEM((ROWS, width), BF16),
            ]
            + scratch,
        ),
        out_shape=[jax.ShapeDtypeStruct(shape, kind) for _, shape, kind in outs],
        compiler_params=pltpu.CompilerParams(vmem_limit_bytes=VMEM_BYTES),
        cost_estimate=LONG,
        name="attend_backward",
    )(info, *arrays, *operands)


def normal_parts(u):
    t = pl.reciprocal(1.0 + 0.23164190 * jnp.abs(u), approx=True)
    bell = jnp.exp2((u * -0.7213475204444817) * u)
    poly = t * (
        0.127414796
        + t * (-0.142248368 + t * (0.7107068705 + t * (-0.7265760135 + t * 0.5307027145)))
    )
    tail = poly * bell
    return jnp.where(u < 0, tail, 1.0 - tail), bell


def inner_forward(normed, matrix, bias):
    inner = dot_plain(normed, matrix) + bias
    cumulative, bell = normal_parts(inner)
    slope = cumulative + (inner * 0.3989422804014327) * bell
    return (inner * cumulative).astype(BF16), slope.astype(BF16)


def expert_forward_kernel(plan, weight_count, count, kind, info, *refs):
    weights, refs = refs[:weight_count], refs[weight_count:]
    x_ref, gain_ref, shift_ref, inner_ref, outer_ref = refs[:5]
    y_ref, act_ref, slope_ref, blocks, sems, normed, total = refs[5:]
    step = pl.program_id(0)
    items, _, width = x_ref.shape

    @pl.when(step == 0)
    def _():
        start_weights(info, items, weights, plan, blocks, sems)
        for item in range(items):
            x = x_ref[item, :count].astype(BF16).astype(F32)
            unit, _ = norm_parts(x)
            normed[item * count : (item + 1) * count] = (
                unit * gain_ref[...] + shift_ref[...]
            ).astype(BF16)

    wait_block(blocks, step, sems)
    wait_block(blocks, step + 4, sems)
    for at in range(0, width, 256):
        columns = slice(at, at + 256)
        act, slope = inner_forward(normed[...], blocks[step, :, columns], inner_ref[:, columns])
        act_ref[:, columns] = act
        slope_ref[:, columns] = slope
    part = dot_plain(act_ref[...], blocks[step + 4])

    @pl.when(step == 0)
    def _():
        total[...] = part

    @pl.when(step > 0)
    def _():
        total[...] += part

    @pl.when(step == pl.num_programs(0) - 1)
    def _():
        for item in range(items):
            row_true = true_positions(info[item], 0, count, 0, kind)
            branch = total[item * count : (item + 1) * count] + outer_ref[...]
            x = x_ref[item, :count].astype(BF16).astype(F32)
            y_ref[item, :count] = (x + jnp.where(row_true, branch, 0.0)).astype(BF16)
            if count < ROWS:
                y_ref[item, count:] = jnp.zeros((ROWS - count, width), BF16)


def expert_backward_kernel(plan, weight_count, count, kind, info, *refs):
    weights, refs = refs[:weight_count], refs[weight_count:]
    x_ref, gain_ref, shift_ref, act_ref, slope_ref, grad_ref = refs[:6]
    out_ref, gain_grad_ref, shift_grad_ref, inner_grad_ref, outer_grad_ref = refs[6:11]
    travel_refs = refs[11:15]
    blocks, sems, normed_turned, branch_turned, branch, inner_all, total = refs[15:]
    step = pl.program_id(0)
    items, _, width = x_ref.shape
    section, core = info[items], info[items + 1]

    @pl.when(step == 0)
    def _():
        start_weights(info, items, weights, plan, blocks, sems)
        outer = None
        for item in range(items):
            here = slice(item * count, (item + 1) * count)
            unit, _ = norm_parts(x_ref[item, :count].astype(BF16).astype(F32))
            normed = (unit * gain_ref[...] + shift_ref[...]).astype(BF16)
            row_true = true_positions(info[item], 0, count, 0, kind)
            incoming = grad_ref[item, :count].astype(F32)
            masked = jnp.where(row_true, incoming, 0.0).astype(BF16)
            branch[here] = masked
            store_turned(normed_turned, normed.T, here, section, core)
            store_turned(branch_turned, masked.T, here, section, core)
            term = column_sum(masked)
            outer = term if outer is None else outer + term
        outer_grad_ref[...] = outer

    wait_block(blocks, step, sems)
    wait_block(blocks, step + 4, sems)
    for at in range(0, width, 256):
        columns = slice(at, at + 256)
        act_grad = dot_last(branch[...], blocks[step + 4, columns])
        inner = (slope_ref[:, columns].astype(F32) * act_grad).astype(BF16)
        inner_all[:, columns] = inner
        inner_grad_ref[:, columns] = column_sum(inner)
        put_travel(travel_refs, 0, columns, normed_turned, inner)
        put_travel(travel_refs, 1, columns, branch_turned, act_ref[:, columns])
    part = dot_last(inner_all[...], blocks[step])

    @pl.when(step == 0)
    def _():
        total[...] = part

    @pl.when(step > 0)
    def _():
        total[...] += part

    @pl.when(step == pl.num_programs(0) - 1)
    def _():
        gain_sum, shift_sum = None, None
        for item in range(items):
            unit, scale = norm_parts(x_ref[item, :count].astype(BF16).astype(F32))
            normed_grad = total[item * count : (item + 1) * count]
            gain_part = jnp.sum(normed_grad * unit, axis=0, keepdims=True)
            shift_part = jnp.sum(normed_grad, axis=0, keepdims=True)
            gain_sum = gain_part if gain_sum is None else gain_sum + gain_part
            shift_sum = shift_part if shift_sum is None else shift_sum + shift_part
            incoming = grad_ref[item, :count].astype(F32)
            hidden = incoming + norm_back(normed_grad, unit, scale, gain_ref[...])
            out_ref[item, :count] = hidden.astype(BF16)
            if count < ROWS:
                out_ref[item, count:] = grad_ref[item, count:]
        gain_grad_ref[...] = gain_sum
        shift_grad_ref[...] = shift_sum


def shared_forward_kernel(*refs):
    *rows_refs, inputs_ref, inner_ref, outputs_ref = refs[:7]
    *part_refs, normed, total = refs[7:]
    count = rows_refs[0].shape[0]
    step = pl.program_id(0)

    @pl.when(step == 0)
    def _():
        for index, ref in enumerate(rows_refs):
            normed[index * count : (index + 1) * count] = ref[...]
        total[...] = jnp.zeros_like(total)

    act, _ = inner_forward(normed[...], inputs_ref[...], inner_ref[...])
    total[...] += dot_plain(act, outputs_ref[...])

    @pl.when(step == pl.num_programs(0) - 1)
    def _():
        for index, ref in enumerate(part_refs):
            ref[...] = total[index * count : (index + 1) * count].astype(BF16)


def shared_backward_kernel(plan, weight_count, info, *refs):
    weights, refs = refs[:weight_count], refs[weight_count:]
    rows_refs, grad_refs, inner_ref = refs[:4], refs[4:8], refs[8]
    part_refs, (keep_ref, send_ref, inner_grad_ref, outer_grad_ref) = refs[9:13], refs[13:17]
    blocks, sems, normed, branch, matrix = refs[17:]
    count, width = rows_refs[0].shape
    half = width // 2
    first = info.shape[0] - 3
    core = info[first + 1]
    start_weights(info, first, weights, plan, blocks, sems)
    for index in range(SECTIONS):
        here = slice(index * count, (index + 1) * count)
        normed[here] = rows_refs[index][...]
        branch[here] = grad_refs[index][...]
    outer_grad_ref[...] = column_sum(grad_refs[0][...])
    wait_block(blocks, 0, sems)
    wait_block(blocks, 1, sems)
    part = None
    for at in range(0, width, 256):
        columns = slice(at, at + 256)
        act, slope = inner_forward(normed[...], blocks[0, :, columns], inner_ref[:, columns])
        act_grad = dot_last(branch[...], blocks[1, columns])
        inner = (slope.astype(F32) * act_grad).astype(BF16)
        inner_grad_ref[:, columns] = column_sum(inner)
        matrix[0, :, columns] = dot_first(normed[...], inner).astype(BF16)
        matrix[1, :, columns] = dot_first(branch[...], act).astype(BF16)
        term = dot_last(inner, blocks[0, :, columns])
        part = term if part is None else part + term
    for index, ref in enumerate(part_refs):
        ref[...] = part[index * count : (index + 1) * count].astype(BF16)
    quarter = half // 4
    for which in range(2):
        for group in range(4):
            columns = slice(group * width, (group + 1) * width)
            mine = pl.multiple_of(core * half, 16) + group * quarter
            other = pl.multiple_of((1 - core) * half, 16) + group * quarter
            keep_ref[which, :, columns] = matrix[which, pl.ds(pl.multiple_of(mine, 16), quarter)]
            send_ref[which, :, columns] = matrix[which, pl.ds(pl.multiple_of(other, 16), quarter)]


def chunk_columns(rows, width):
    return pl.BlockSpec((rows, width), lambda step, info: (0, step))


def expert_forward(x, info, weights, gain, shift, inner, outer, count, kind):
    arrays, plan = weights
    items, _, width = x.shape
    hidden = inner.shape[1]
    row = whole_block((1, width))
    return pl.pallas_call(
        partial(expert_forward_kernel, plan, len(arrays), count, kind),
        grid_spec=pltpu.PrefetchScalarGridSpec(
            num_scalar_prefetch=1,
            grid=(hidden // width,),
            in_specs=[ANYWHERE] * len(arrays)
            + [whole_block(x.shape), row, row, chunk_columns(1, width), row],
            out_specs=[
                whole_block((items, ROWS, width)),
                chunk_columns(items * count, width),
                chunk_columns(items * count, width),
            ],
            scratch_shapes=blocks_scratch(8, width)
            + [
                pltpu.VMEM((items * count, width), BF16),
                pltpu.VMEM((items * count, width), F32),
            ],
        ),
        out_shape=[
            jax.ShapeDtypeStruct((items, ROWS, width), BF16),
            jax.ShapeDtypeStruct((items * count, hidden), BF16),
            jax.ShapeDtypeStruct((items * count, hidden), BF16),
        ],
        compiler_params=pltpu.CompilerParams(vmem_limit_bytes=VMEM_BYTES),
        cost_estimate=SHORT,
        name="expert_forward_" + kind,
    )(info, *arrays, x, gain, shift, inner, outer)


def expert_backward(x, info, weights, gain, shift, act, slope, incoming, count, kind):
    arrays, plan = weights
    items, _, width = x.shape
    half = width // 2
    hidden = act.shape[1]
    row = whole_block((1, width))
    travel = pl.BlockSpec((2, half // 2, width), lambda step, info: (0, 0, step))
    return pl.pallas_call(
        partial(expert_backward_kernel, plan, len(arrays), count, kind),
        grid_spec=pltpu.PrefetchScalarGridSpec(
            num_scalar_prefetch=1,
            grid=(hidden // width,),
            in_specs=[ANYWHERE] * len(arrays)
            + [
                whole_block(x.shape),
                row,
                row,
                chunk_columns(items * count, width),
                chunk_columns(items * count, width),
                whole_block(incoming.shape),
            ],
            out_specs=[whole_block(incoming.shape), row, row, chunk_columns(1, width), row]
            + [travel] * 4,
            scratch_shapes=blocks_scratch(8, width)
            + [
                pltpu.VMEM((width, items * count), BF16),
                pltpu.VMEM((width, items * count), BF16),
                pltpu.VMEM((items * count, width), BF16),
                pltpu.VMEM((items * count, width), BF16),
                pltpu.VMEM((items * count, width), F32),
            ],
        ),
        out_shape=[
            jax.ShapeDtypeStruct(incoming.shape, BF16),
            jax.ShapeDtypeStruct((1, width), F32),
            jax.ShapeDtypeStruct((1, width), F32),
            jax.ShapeDtypeStruct((1, hidden), F32),
            jax.ShapeDtypeStruct((1, width), F32),
        ]
        + [jax.ShapeDtypeStruct((2, half // 2, hidden), BF16)] * 4,
        compiler_params=pltpu.CompilerParams(vmem_limit_bytes=VMEM_BYTES),
        cost_estimate=SHORT,
        name="expert_backward_" + kind,
    )(info, *arrays, x, gain, shift, act, slope, incoming)


IN_VMEM = pl.BlockSpec(memory_space=pltpu.VMEM)
IN_SMEM = pl.BlockSpec(memory_space=pltpu.SMEM)


def shared_forward(rows, inputs, inner, outputs):
    count, width = rows[0].shape
    total = SECTIONS * count
    hidden = inner.shape[1]
    return pl.pallas_call(
        shared_forward_kernel,
        grid=(hidden // width,),
        in_specs=[pl.BlockSpec(rows[0].shape, lambda step: (0, 0))] * 4
        + [
            pl.BlockSpec((width, width), lambda step: (0, step)),
            pl.BlockSpec((1, width), lambda step: (0, step)),
            pl.BlockSpec((width, width), lambda step: (step, 0)),
        ],
        out_specs=[pl.BlockSpec((count, width), lambda step: (0, 0))] * SECTIONS,
        scratch_shapes=[pltpu.VMEM((total, width), BF16), pltpu.VMEM((total, width), F32)],
        out_shape=[jax.ShapeDtypeStruct((count, width), BF16)] * SECTIONS,
        compiler_params=pltpu.CompilerParams(vmem_limit_bytes=VMEM_BYTES),
        cost_estimate=SHORT,
        name="shared_forward",
    )(*rows, inputs, inner, outputs)


def shared_backward(rows, grads, info, weights, inner):
    arrays, plan = weights
    count, width = rows[0].shape
    total = SECTIONS * count
    travel = (2, width // 8, 4 * width)
    return pl.pallas_call(
        partial(shared_backward_kernel, plan, len(arrays)),
        in_specs=[IN_SMEM] + [ANYWHERE] * len(arrays) + [IN_VMEM] * 9,
        out_specs=[IN_VMEM] * 8,
        scratch_shapes=blocks_scratch(2, width)
        + [
            pltpu.VMEM((total, width), BF16),
            pltpu.VMEM((total, width), BF16),
            pltpu.VMEM((2, width, width), BF16),
        ],
        out_shape=[
            *[jax.ShapeDtypeStruct((count, width), BF16)] * SECTIONS,
            jax.ShapeDtypeStruct(travel, BF16),
            jax.ShapeDtypeStruct(travel, BF16),
            jax.ShapeDtypeStruct((1, width), F32),
            jax.ShapeDtypeStruct((1, width), F32),
        ],
        compiler_params=pltpu.CompilerParams(vmem_limit_bytes=VMEM_BYTES),
        cost_estimate=SHORT,
        name="shared_backward",
    )(info, *arrays, *rows, *grads, inner)


def plane_turn(plane, planes):
    return ((plane & 1) << 1) | (plane >> 1) if planes == 4 else 0


def finish_kernel(planes, info, scale_ref, mine_ref, theirs_ref, *refs):
    step = pl.program_id(0)
    count = mine_ref.shape[1]
    placed = refs[-1]
    outs = refs[:-1]
    width = placed.shape[1]
    half = width // 2
    at = info.shape[0] - 3
    section, core = info[at], info[at + 1]
    turn = plane_turn(info[at + 2], planes)
    turned = 0
    scale = scale_ref[0, 0]
    columns = pl.ds(pl.multiple_of((step ^ turned) * width, width), width)

    def place(which):
        def by_rows():
            for side, ref in enumerate((mine_ref, theirs_ref)):
                for away in range(SECTIONS):
                    for path in range(2):
                        row = (core ^ side) * half + path * (half // 2)
                        row = row + (section ^ away) * PIECE_ROWS
                        placed[pl.ds(pl.multiple_of(row, 16), PIECE_ROWS), :] = ref[
                            away, which, path * PIECE_ROWS : (path + 1) * PIECE_ROWS, columns
                        ].astype(F32)

        def by_columns():
            for side, ref in enumerate((mine_ref, theirs_ref)):
                for group in range(4):
                    quarter = half // 4
                    row = (core ^ side) * half + group * quarter
                    placed[pl.ds(pl.multiple_of(row, 16), quarter), :] = ref[
                        step, which, :, group * width : (group + 1) * width
                    ].astype(F32)

        if count == 1:
            by_rows()
        else:
            pl.when(section != 0)(by_rows)
            pl.when(section == 0)(by_columns)

    place(0)
    if count == 1:

        @pl.when(step < 3)
        def _():
            outs[0][0] = placed[...] / scale

        @pl.when(step == 3)
        def _():
            outs[1][0] = placed[...] / scale

    else:
        outs[0][0] = placed[...] / scale
        place(1)
        outs[1][0] = (placed[...] / scale).T


def finish(info, scale, mine, theirs, planes):
    count, hidden = mine.shape[1], mine.shape[3]
    width = hidden // 4
    if count == 1:
        shapes = [(1, width, 3 * width), (1, width, width)]
        maps = [lambda step, info: (0, 0, jnp.minimum(step, 2)), lambda step, info: (0, 0, 0)]
    else:
        shapes = [(1, width, hidden), (1, hidden, width)]
        maps = [lambda step, info: (0, 0, step), lambda step, info: (0, step, 0)]
    return pl.pallas_call(
        partial(finish_kernel, planes),
        grid_spec=pltpu.PrefetchScalarGridSpec(
            num_scalar_prefetch=1,
            grid=(4,),
            in_specs=[IN_SMEM, whole_block(mine.shape), whole_block(mine.shape)],
            out_specs=[pl.BlockSpec((1, width, width), at) for at in maps],
            scratch_shapes=[pltpu.VMEM((width, width), F32)],
        ),
        out_shape=[jax.ShapeDtypeStruct(shape, F32) for shape in shapes],
        compiler_params=pltpu.CompilerParams(vmem_limit_bytes=VMEM_BYTES),
        cost_estimate=SHORT,
        name="finish",
    )(info, scale, mine, theirs)


def pack_kernel(count, plan, info, *refs):
    sources, outs, sems = refs[:count], refs[count:-1], refs[-1]
    first = info.shape[0] - 3
    section, core, plane = info[first], info[first + 1], info[first + 2]
    half = outs[0].shape[1]
    for index, (out, choices) in enumerate(zip(outs, plan)):
        for at, at_plane, parts in choices:
            here = section == at
            if at_plane is not None:
                here = here & (plane == at_plane)

            @pl.when(here)
            def _(index=index, out=out, parts=parts):
                for block, part in enumerate(parts):
                    if part[0] == "own":
                        _, which, row, column = part
                        rows = pl.ds(pl.multiple_of(row + core * half, half), half)
                        source = sources[which].at[rows, pl.ds(column, out.shape[2])]
                    else:
                        source = sources[part[1]].at[block]
                    pltpu.make_async_copy(source, out.at[block], sems.at[index, block]).start()

    for index, out in enumerate(outs):
        for block in range(2):
            pltpu.make_async_copy(out.at[block], out.at[block], sems.at[index, block]).wait()


def pack(info, sources, plan, shape):
    return pl.pallas_call(
        partial(pack_kernel, len(sources), plan),
        in_specs=[IN_SMEM] + [ANYWHERE] * len(sources),
        out_specs=[IN_VMEM] * len(plan),
        scratch_shapes=[pltpu.SemaphoreType.DMA((len(plan), 2))],
        out_shape=[jax.ShapeDtypeStruct(shape, BF16)] * len(plan),
        cost_estimate=SHORT,
        name="pack",
    )(info, *sources)


def over_section(value, bits, sources=range(SECTIONS)):
    return lax.ppermute(value, "section", [(at, at ^ bits) for at in sources])


def over_core(value):
    return lax.ppermute(value, "core", [(0, 1), (1, 0)])


def over_plane(value, pairs):
    return lax.ppermute(value, "z", pairs)


def added(left, right):
    return (left.astype(F32) + right.astype(F32)).astype(BF16)


def after(value, *earlier):
    return lax.optimization_barrier((value,) + earlier)[0]


def under(outputs, *arrivals):
    joined = lax.optimization_barrier(tuple(outputs) + arrivals)
    return list(joined[: len(outputs)]), list(joined[len(outputs) :])


def by_section(section, values):
    result, last = None, None
    for at in sorted(values):
        if result is None:
            result = values[at]
        elif values[at] is not last:
            result = jnp.where(section >= at, values[at], result)
        last = values[at]
    return result


def total(*values):
    result = values[0].astype(F32)
    for value in values[1:]:
        result = result + value.astype(F32)
    return result.astype(BF16)


class Sums:
    def __init__(self, travel):
        self.stay, self.move, self.other_stay, self.other_move = travel
        self.size = self.stay.shape[1] // 2

    def cross(self, *earlier):
        if earlier:
            self.other_move = after(self.other_move, *earlier)
            self.other_stay = after(self.other_stay, *earlier)
        self.got_move, self.got_stay = over_core(self.other_move), over_core(self.other_stay)

    def first_sends(self):
        size = self.size
        self.sent = [
            total(self.move[:, at : at + size], self.got_move[:, at : at + size])
            for at in (0, size)
        ]
        return self.sent

    def second_sends(self, from_x, from_y):
        size, half = self.size, self.size // 2
        self.first = from_x, from_y
        to_y = total(self.stay[:, half:size], self.got_stay[:, half:size], from_x[:, half:])
        to_x = total(
            self.stay[:, size + half :], self.got_stay[:, size + half :], from_y[:, half:]
        )
        self.sent = [to_x, to_y]
        return self.sent

    def whole(self, from_x, from_y):
        size, half = self.size, self.size // 2
        parts = []
        for at, first, second in ((0, self.first[0], from_y), (size, self.first[1], from_x)):
            here = slice(at, at + half)
            parts.append(total(self.stay[:, here], self.got_stay[:, here], first[:, :half], second))
        return jnp.concatenate(parts, axis=1)


def over_links(sends):
    return [over_section(sends[0], 1), over_section(sends[1], 2)]


class Planes:
    def __init__(self, value, plane, planes):
        self.value, self.plane, self.planes, self.turn = value, plane, planes, 0

    def sends(self, *earlier):
        value = after(self.value, *earlier) if earlier else self.value
        if self.planes != 4:
            return (value,)
        bits = (1, 2, 2, 1)[self.turn]
        if self.turn < 2:
            bit = (self.plane & 1, self.plane >> 1)[self.turn]
            size = value.shape[-1] // 2
            value = lax.dynamic_slice_in_dim(value, (1 - bit) * size, size, value.ndim - 1)
        return (over_plane(value, [(at, at ^ bits) for at in range(4)]),)

    def take(self, arrived):
        if self.planes != 4:
            self.value = lax.psum(arrived, "z") if self.turn == 3 else arrived
        elif self.turn < 2:
            bit = (self.plane & 1, self.plane >> 1)[self.turn]
            size = self.value.shape[-1] // 2
            keep = lax.dynamic_slice_in_dim(self.value, bit * size, size, self.value.ndim - 1)
            self.value = added(keep, arrived)
        else:
            self.value = jnp.concatenate([self.value, arrived], axis=-1)
        self.turn += 1

    def in_order(self, value):
        if self.planes != 4:
            return value
        size, turn = value.shape[-1] // 4, plane_turn(self.plane, 4)
        parts = [
            lax.dynamic_slice_in_dim(value, (at ^ turn) * size, size, value.ndim - 1)
            for at in range(4)
        ]
        return jnp.concatenate(parts, axis=-1)


class Weights:
    def __init__(self, own, info, planes):
        self.own, self.info = own, info
        self.four = planes == 4
        self.plan = PLAN_FOUR if self.four else PLAN_ANY
        self.half, self.width = own[1].shape[0] // 2, own[1].shape[1]
        self.mine, self.theirs, self.arrived = {}, {}, {}

    def place(self, layer, block):
        if layer in "ac":
            return (0, 0, block * self.width) if block < 3 else (1, 0, 0)
        if layer == "g":
            return (2, 0, block * self.width) if block < 4 else (3, (block - 4) * self.width, 0)
        return (2, 0, block * self.width) if block < 4 else (3, (block - 4) * self.width, 0)

    def choices(self, sends, sources):
        result = []
        for at in range(SECTIONS):
            name = sends.get(at)
            if name is not None and HOMES[name[0]] != at:
                key = self.arrived[at, name]
                if key not in sources:
                    sources[key] = len(self.own) + len(sources)
                result.append((at, None, [("arrived", sources[key])] * 2))
                continue
            for plane in range(4) if name == "F" else (None,):
                piece = ("f" + str(plane)) if name == "F" else name or "a0"
                layer, index = piece[0], int(piece[1])
                if layer in "ac":
                    blocks = ATTEND_BLOCKS[index]
                else:
                    blocks = (index, 4 + index) if layer == "g" else EXPERT_BLOCKS[index]
                parts = [("own",) + self.place(layer, block) for block in blocks]
                result.append((at, plane, parts))
        return result

    def packed(self, wanted):
        sources = {}
        plan = [self.choices(sends, sources) for sends in wanted]
        arrays = list(self.own) + [self.mine[key] for key in sources]
        return pack(self.info, arrays, plan, (2, self.half, self.width))

    def sends(self, step):
        if step == "F":
            return [{at: "F" for at in range(SECTIONS)}]
        return [sends for sends in self.plan[step] if sends]

    def payloads(self, *steps):
        wanted = [sends for step in steps for sends in self.sends(step)]
        return list(self.packed(wanted))

    def move(self, step, payloads):
        links = [(link, sends) for link, sends in enumerate(self.plan[step]) if sends]
        for (link, sends), payload in zip(links, payloads):
            self.mine[step, link] = over_section(payload, link + 1, sorted(sends))
            for at, name in sends.items():
                self.arrived[at ^ (link + 1), name] = (step, link)
        return [(step, link) for link, _ in links]

    def move_planes(self, step):
        up, down = self.mine["plane", step - 1], self.mine["plane", 1 - step]
        up = over_plane(up, [(at, at + 1) for at in range(step - 1, 3)])
        down = over_plane(down, [(at, at - 1) for at in range(4 - step, 0, -1)])
        self.mine["plane", step], self.mine["plane", -step] = up, down
        return [("plane", step), ("plane", -step)]

    def cross(self, keys):
        for key in keys:
            self.theirs[key] = over_core(self.mine[key])
        return keys

    def join(self, outputs, mine=(), theirs=()):
        values = [self.mine[key] for key in mine] + [self.theirs[key] for key in theirs]
        outputs, values = under(outputs, *values)
        for key, value in zip(mine, values):
            self.mine[key] = value
        for key, value in zip(theirs, values[len(mine) :]):
            self.theirs[key] = value
        return outputs

    def layer(self, layer):
        arrays, places = list(self.own), {}

        def place(key):
            if key not in places:
                places[key] = len(arrays)
                arrays.extend([self.mine[key], self.theirs[key]])
            return places[key], places[key] + 1

        if layer in "ac":
            names = [(layer + str(index), ATTEND_BLOCKS[index]) for index in range(2)]
        else:
            names = [(layer + str(index), EXPERT_BLOCKS[index]) for index in range(4)]
        plan = []
        for at in range(SECTIONS):
            if layer == "g":
                names = [("g" + str(at), (0, 1))]
            if HOMES[layer] == at:
                steps = []
                for name, blocks in names:
                    for block in blocks:
                        source = block * 4 if layer == "g" else block
                        steps.append((block, ("own",) + self.place(layer, source)))
                plan.append((at, None, steps))
                continue
            by_plane = layer == "f" and self.four
            for plane in range(4) if by_plane else (None,):
                steps = []
                for index, (name, blocks) in enumerate(names):
                    key = ("plane", plane - index) if by_plane else self.arrived[at, name]
                    for which, block in enumerate(blocks):
                        steps.append((block, ("piece",) + place(key) + (which,)))
                plan.append((at, plane, steps))
        return arrays, plan


def per_device(
    tokens,
    caption_lengths,
    attend_gain,
    attend_shift,
    attend_inputs,
    attend_bias,
    attend_output,
    expert_gain,
    expert_shift,
    expert_inputs,
    expert_inner_bias,
    expert_outputs,
    expert_outer_bias,
    cotangent,
):
    section, core, plane = lax.axis_index("section"), lax.axis_index("core"), lax.axis_index("z")
    planes = lax.axis_size("z")
    items, positions, width = tokens.shape
    hidden = expert_inputs.shape[-1]
    info = [value.reshape(1).astype(jnp.int32) for value in (section, core, plane)]
    info = jnp.concatenate([caption_lengths] + info)
    weights = Weights(
        (attend_inputs[0], attend_output[0], expert_inputs[0], expert_outputs[0]), info, planes
    )

    def to_sections(value):
        return [value] + [over_section(value, bits) for bits in (1, 2, 3)]

    def items_of(part):
        return part.reshape(items, CAP_ROWS, width)

    pad = ((0, 0), (0, ROWS - positions), (0, 0))
    x0 = jnp.pad(tokens, pad)
    last_grad = jnp.pad(cotangent, pad)
    rows = jnp.concatenate(
        [
            attend_gain,
            attend_shift,
            attend_bias,
            expert_gain,
            expert_shift,
            expert_inner_bias,
            expert_outer_bias,
            jnp.full((1, 128), jnp.sum(caption_lengths), F32),
        ],
        axis=1,
    )
    rows = to_sections(rows)
    keys = weights.move(0, weights.payloads(0))
    x0, last_grad, *rows = weights.join([x0, last_grad, *rows], keys)
    keys1 = weights.move(1, weights.payloads(1))
    rows = jnp.concatenate(rows, axis=0)
    language_count = jnp.sum(rows[:, -128:], axis=0, keepdims=True)
    rows = [lax.dynamic_index_in_dim(rows, at ^ section, 0) for at in range(SECTIONS)]
    sizes = [width, width, 3 * width, width, width, hidden, width]
    ends = [sum(sizes[: at + 1]) for at in range(len(sizes))]
    used = [(0, 0), (0, 1), (0, 2), (0, 3), (0, 4), (0, 5), (1, 3), (1, 4), (1, 5), (1, 6)]
    used += [(0, 6), (2, 0), (2, 1), (2, 2), (3, 3), (3, 4), (3, 5), (3, 6)]
    kept = [rows[slot][:, ends[which] - sizes[which] : ends[which]] for slot, which in used]
    language_count, *kept = weights.join([language_count, *kept], keys1)
    kept = dict(zip(used, kept))

    def row(slot, which):
        return kept[slot, which]

    crossed = weights.cross(keys + keys1)
    sends = weights.payloads(2, "F") if weights.four else weights.payloads(2)
    sends, (info, language_count) = under(sends, info, language_count)
    keys = weights.move(2, sends[:2])
    info, language_count = weights.join(
        [info, language_count + over_core(language_count)], theirs=crossed
    )
    plane_keys = []
    if weights.four:
        weights.mine["plane", 0] = sends[2]
        plane_keys = weights.move_planes(1)
    attend0 = weights.layer("a")
    outputs = attend_forward(
        x0, info, attend0, row(0, 0), row(0, 1), row(0, 2), following=(row(0, 3), row(0, 4))
    )
    y0, qkv0, mixed0, caption_rows = weights.join(outputs, keys)
    caption_rows = to_sections(caption_rows.reshape(-1, width))
    sends, caption_rows[1:2] = under(weights.payloads(3), caption_rows[1])
    early_keys = keys
    keys = weights.move(3, sends)
    caption_rows = weights.join(caption_rows, plane_keys)
    if weights.four:
        keys += weights.move_planes(2)
    outputs = shared_forward(caption_rows, expert_inputs[0], expert_inner_bias, expert_outputs[0])
    part = weights.join(outputs, keys + early_keys)
    (y0,) = weights.join([y0], theirs=weights.cross(early_keys + [(3, 0), (3, 1)]))
    branch = {at: over_section(part[at], at, [0]) for at in range(1, SECTIONS)}
    keys = weights.move_planes(3) if weights.four else []
    expert1 = weights.layer("e")
    outputs = expert_forward(
        y0, info, expert1, row(1, 3), row(1, 4), row(1, 5), row(1, 6), PATCH_ROWS, "patch"
    )
    outputs, moved = under(outputs, *branch.values())
    x2, act1, slope1 = weights.join(outputs, keys)
    branch = dict(zip(branch, moved))
    branch[0] = part[0]
    branch = items_of(by_section(section, branch))
    if weights.four:
        crossed = [("plane", step) for step in range(-3, 4)]
    else:
        for step in (4, 5):
            weights.move(step, weights.payloads(step))
        crossed = [(4, 0), (4, 1), (5, 0)]
    weights.cross(crossed)
    attend2 = weights.layer("c") if weights.four else None
    if not weights.four:
        (x2,) = weights.join([x2], theirs=crossed)
        attend2 = weights.layer("c")
    outputs = attend_forward(
        x2, info, attend2, row(2, 0), row(2, 1), row(2, 2), merge=(y0, branch, row(0, 6))
    )
    if weights.four:
        language_count += over_plane(language_count, [(at, at ^ 1) for at in range(4)])
    x3, qkv2, mixed2, x2, language_count = weights.join([*outputs, language_count], theirs=crossed)
    if weights.four:
        language_count += over_plane(language_count, [(at, at ^ 2) for at in range(4)])
    else:
        language_count = lax.psum(language_count, "z")
    expert3 = weights.layer("f")
    outputs = expert_forward(
        x3, info, expert3, row(3, 3), row(3, 4), row(3, 5), row(3, 6), ROWS, "all"
    )
    layer_output, act3, slope3, language_count = under([*outputs, language_count])[0]
    language_count = language_count[0, 0].astype(jnp.int32)
    vision_count = PATCHES * items * SECTIONS * 2 * planes
    counts = jnp.stack(
        [jnp.full((), vision_count, jnp.int32), language_count, language_count + vision_count]
    )

    def small_rows(values):
        flat = jnp.concatenate(values, axis=1)
        count = -(-flat.shape[1] // hidden)
        flat = jnp.pad(flat, ((0, 0), (0, count * hidden - flat.shape[1])))
        return flat.reshape(count, hidden)

    def to_home(sums):
        got = [by_section(section, sums)]
        for bits in (1, 2, 3):
            sends = {at ^ bits: sums[at] for at in sums}
            got.append(over_section(by_section(section, sends), bits, sorted(sends)))
        return got

    keys = []
    if weights.four:
        sends, (layer_output, last_grad) = under(weights.payloads(4), layer_output, last_grad)
        keys = weights.move(4, sends)
    outputs = expert_backward(
        x3, info, expert3, row(3, 3), row(3, 4), act3, slope3, last_grad, ROWS, "all"
    )
    outputs = weights.join(outputs, keys)
    crossed = weights.cross(keys)
    grad3, *small3 = outputs[:5]
    sums3 = Sums(outputs[5:])
    sums3.cross()
    moved = over_links(sums3.first_sends())
    grad3 = after(grad3, *sums3.sent)
    outputs = attend_backward(
        x2, info, attend2, row(2, 0), row(2, 1), qkv2, mixed2, grad3
    )
    outputs, moved = under(outputs, *moved, sums3.got_stay)
    outputs = weights.join(outputs, theirs=crossed)
    grad2, *small2 = outputs[:4]
    sums2, caption_grad = Sums(outputs[4:8]), outputs[8]
    caption_grads = to_sections(caption_grad.reshape(-1, width))
    sums3.got_stay = moved[2]
    moved3 = over_links(sums3.second_sends(*moved[:2]))
    grad2 = after(grad2, *sums3.sent)
    outputs = expert_backward(
        y0, info, expert1, row(1, 3), row(1, 4), act1, slope1, grad2, PATCH_ROWS, "patch"
    )
    outputs, caption_grads = under(outputs, *caption_grads)
    grad1, *small1 = outputs[:5]
    sums2.cross(grad1)
    sums1 = Sums(outputs[5:])
    sums1.cross()
    inner_quarter = lax.dynamic_slice(row(0, 5), (0, section * width), (1, width))
    sum3 = sums3.whole(*moved3)
    inner_quarter = after(inner_quarter, grad1, sum3)
    outputs = shared_backward(
        caption_rows, caption_grads, info, weights.layer("g"), inner_quarter
    )
    parts, (keep0, send0, inner_grad, outer_grad) = outputs[:4], outputs[4:]
    got = [over_section(parts[bits], bits) for bits in (1, 2, 3)]
    sends = [after(value, *parts) for value in sums1.first_sends()]
    moved1 = over_links(sends)
    keep0 = added(keep0, over_core(send0))
    early = lax.psum(jnp.concatenate([sum3, keep0], axis=0), "z")
    sends2 = [after(value, *sends) for value in sums2.first_sends()]
    moved2 = over_links(sends2)
    parts = [parts[0], *got]
    grad1 = after(grad1, keep0, *sends, *sends2)
    outputs = attend_backward(
        x0,
        info,
        attend0,
        row(0, 0),
        row(0, 1),
        qkv0,
        mixed0,
        grad1,
        first=(y0, row(0, 3), parts),
    )
    outputs, moved = under(outputs, *moved2, *moved1)
    moved2, moved1 = moved[:2], moved[2:]
    tokens_grad, *small_first = outputs[:4]
    sums_first, gain_grad, shift_grad = Sums(outputs[4:8]), outputs[8], outputs[9]
    sums_first.cross()
    inner_grad = lax.dynamic_update_slice(
        jnp.zeros((1, hidden), F32), inner_grad, (0, section * width)
    )
    small = small_rows(
        small_first + [gain_grad, shift_grad, inner_grad, outer_grad] + small2 + small1 + small3
    )
    small = added(small, over_core(small))
    to_x, to_y = sums_first.first_sends()
    to_x = jnp.concatenate([to_x[0], small], axis=0)
    sends = lax.optimization_barrier((*sums1.second_sends(*moved1), to_x, to_y))
    moved1, moved = over_links(sends[:2]), over_links(sends[2:])
    sum1, early = lax.optimization_barrier((sums1.whole(*moved1), early))
    whole1 = lax.psum(sum1, "z")
    size = to_y.shape[1]
    small = added(small, moved[0][size:])
    to_x, to_y = sums_first.second_sends(moved[0][None, :size], moved[1])
    early_x, early_y = sums2.second_sends(*moved2)
    to_x = jnp.concatenate([to_x[0], early_x[0]], axis=0)
    to_y = jnp.concatenate([to_y[0], early_y[0], small], axis=0)
    to_x, to_y = lax.optimization_barrier((to_x, to_y))
    moved = over_links((to_x, to_y))
    size = early_x.shape[1]
    last = sums_first.whole(moved[0][None, :size], moved[1][None, :size])
    sum2 = sums2.whole(moved[0][None, size:], moved[1][None, size : 2 * size])
    small = added(small, moved[1][2 * size :])
    small_count = small.shape[0]
    eighth = last.shape[1]
    last = jnp.concatenate([last[0], sum2[0], small], axis=0)
    home_early = to_home({0: after(early[2:], last), 3: after(early[:2], last)})
    last, whole1, *home_early[1:3] = lax.optimization_barrier((last, whole1, *home_early[1:3]))
    last = lax.psum(last, "z")
    home_late = to_home({1: whole1})
    last, *home_early = lax.optimization_barrier((last, *home_early))
    home_attend = to_home({0: last[None, :eighth], 2: last[None, eighth : 2 * eighth]})
    small = last[2 * eighth :].astype(F32)

    as_float = counts.astype(F32)
    one = jnp.ones((), F32)
    attend_scales = jnp.stack([as_float[2], one, as_float[2], one])
    expert_scales = jnp.stack([as_float[1], as_float[0], one, as_float[2]])

    def placed(pieces, scales):
        scale = lax.dynamic_index_in_dim(scales, section, 0).reshape(1, 1)
        pieces = jnp.stack(pieces)
        return finish(info, scale, pieces, over_core(pieces), planes)

    blank = jnp.zeros_like(home_late[0])
    inputs_whole, outputs_whole = placed(
        [
            by_section(section, {0: early, 1: late, 2: blank, 3: early})
            for early, late in zip(home_early, home_late)
        ],
        expert_scales,
    )
    blank = jnp.zeros_like(home_attend[0])
    attend_whole, output_whole = placed(
        [by_section(section, {0: got, 1: blank, 2: got, 3: blank}) for got in home_attend],
        attend_scales,
    )

    attend_size, expert_size = 5 * width, 3 * width + hidden
    cuts = [attend_size, attend_size + expert_size]
    cuts += [cuts[1] + attend_size, cuts[1] + attend_size + expert_size]
    small = jnp.split(small.reshape(-1)[: cuts[3] + expert_size], cuts)
    none_attend, none_expert = jnp.zeros_like(small[0]), jnp.zeros_like(small[1])
    attend_small = jnp.stack([small[0], none_attend, small[2], none_attend])
    expert_small = jnp.stack([small[1], small[3], none_expert, small[4]])
    attend_small = attend_small / attend_scales.reshape(-1, 1)
    expert_small = expert_small / expert_scales.reshape(-1, 1)
    attend_small = lax.dynamic_index_in_dim(attend_small, section, 0)
    expert_small = lax.dynamic_index_in_dim(expert_small, section, 0)
    return (
        layer_output[:, :positions],
        tokens_grad[:, :positions],
        attend_small[:, :width],
        attend_small[:, width : 2 * width],
        attend_whole,
        attend_small[:, 2 * width :],
        output_whole,
        expert_small[:, :width],
        expert_small[:, width : 2 * width],
        inputs_whole,
        expert_small[:, 2 * width : 2 * width + hidden],
        outputs_whole,
        expert_small[:, 2 * width + hidden :],
        counts,
    )


def solution(mesh):
    sections, groups = mesh.shape["section"], mesh.shape["dp"]
    split = Mesh(mesh.devices.reshape(sections, groups // 2, 2), ("section", "z", "core"))
    items = P(("section", "z", "core"), None, None)
    flat = P("section", None)
    matrix = P("section", None, None)
    placed = (
        items,
        P(("section", "z", "core")),
        flat,
        flat,
        matrix,
        flat,
        matrix,
        flat,
        flat,
        matrix,
        flat,
        matrix,
        flat,
        items,
    )
    return jax.shard_map(
        per_device,
        mesh=split,
        in_specs=placed,
        out_specs=(
            items,
            items,
            flat,
            flat,
            matrix,
            flat,
            matrix,
            flat,
            flat,
            matrix,
            flat,
            matrix,
            flat,
            P(),
        ),
        check_vma=False,
    )
```

```python
from functools import partial

import jax
import jax.numpy as jnp
from jax import lax
from jax.experimental import pallas as pl
from jax.experimental.pallas import tpu as pltpu
from jax.sharding import Mesh
from jax.sharding import PartitionSpec as P

HEADS = 12
HEAD_DIM = 64
PATCHES = 197
ROWS = 256
CAP_FIRST, CAP_ROWS = 192, 48
PATCH_ROWS = 208
PAIR = 2 * HEAD_DIM
SECTIONS = 4
PIECE_ROWS = 48
VMEM_BYTES = 58 * 1024 * 1024
F32 = jnp.float32
BF16 = jnp.bfloat16

PLAN_FOUR = (
    ({0: "a0", 1: "e0", 2: "c0", 3: "F"}, {0: "a1", 1: "e2", 2: "c0", 3: "F"}),
    ({0: "a1", 1: "e1", 2: "a1", 3: "e2"}, {0: "a0", 1: "a0", 2: "F", 3: "c0"}),
    ({0: "g3", 1: "e2", 2: "c1"}, {0: "e0", 1: "e3", 2: "c1"}),
    ({0: "g1", 1: "e3", 2: "e0", 3: "e3"}, {0: "e1", 1: "e1", 3: "c1"}),
    ({}, {0: "g2", 1: "g3"}),
)
PLAN_ANY = (
    ({0: "a0", 1: "e0", 2: "c0", 3: "f0"}, {0: "a1", 1: "e2", 2: "c0", 3: "f0"}),
    ({0: "a1", 1: "e1", 2: "a1", 3: "e2"}, {0: "a0", 1: "a0", 2: "c1", 3: "f1"}),
    ({0: "g3", 1: "e2", 2: "c1", 3: "f1"}, {0: "e0", 1: "e3", 2: "f0", 3: "f2"}),
    ({0: "g1", 1: "e3", 2: "e0", 3: "e3"}, {0: "e1", 1: "e1", 2: "f1", 3: "f3"}),
    ({0: "c1", 1: "f2", 3: "f2"}, {0: "g2", 1: "g3", 3: "c0"}),
    ({1: "f3", 3: "f3"}, {}),
)
HOMES = {"a": 0, "c": 2, "e": 1, "f": 3, "F": 3, "g": 0}
ATTEND_BLOCKS = ((0, 1), (2, 3))
EXPERT_BLOCKS = ((0, 1), (4, 5), (2, 3), (6, 7))


def dot_plain(left, right):
    return jnp.dot(left, right, preferred_element_type=F32)


def dot_last(left, right):
    return lax.dot_general(left, right, (((1,), (1,)), ((), ())), preferred_element_type=F32)


def dot_first(left, right):
    return lax.dot_general(left, right, (((0,), (0,)), ((), ())), preferred_element_type=F32)


def column_sum(matrix):
    return jnp.sum(matrix.astype(F32), axis=0, keepdims=True)


def norm_parts(rows):
    centre = rows - jnp.mean(rows, axis=-1, keepdims=True)
    scale = lax.rsqrt(jnp.mean(centre * centre, axis=-1, keepdims=True) + 1e-06)
    return centre * scale, scale


def norm_back(normed_grad, unit, scale, gain):
    unit_grad = normed_grad * gain
    along = jnp.mean(unit_grad * unit, axis=-1, keepdims=True)
    return scale * (unit_grad - jnp.mean(unit_grad, axis=-1, keepdims=True) - unit * along)


def true_positions(length, first, count, axis, kind):
    shape = (count, 1) if axis == 0 else (1, count)
    position = first + lax.broadcasted_iota(jnp.int32, shape, axis)
    patch = position < PATCHES
    if kind == "patch":
        return patch
    caption = (position >= PATCHES) & (position - PATCHES < length)
    return caption if kind == "caption" else patch | caption


def head_masks():
    lane = lax.broadcasted_iota(jnp.int32, (1, PAIR), 1)
    even = (lane < HEAD_DIM).astype(F32).astype(BF16)
    odd = (lane >= HEAD_DIM).astype(F32).astype(BF16)
    return lane < HEAD_DIM, even, odd


def split_pair(pair, even, odd):
    return jnp.concatenate([pair * even, pair * odd], axis=0)


def start_weights(info, first, refs, plan, blocks, sems):
    half = blocks.shape[1] // 2
    section, core, plane = info[first], info[first + 1], info[first + 2]
    for at, at_plane, steps in plan:
        here = section == at
        if at_plane is not None:
            here = here & (plane == at_plane)

        @pl.when(here)
        def _(steps=steps):
            for block, source in steps:
                if source[0] == "own":
                    _, which, row, column = source
                    width = blocks.shape[2]
                    for part in range(2):
                        pltpu.make_async_copy(
                            refs[which].at[
                                pl.ds(row + part * half, half), pl.ds(column, width)
                            ],
                            blocks.at[block, pl.ds(part * half, half)],
                            sems.at[block],
                        ).start()
                else:
                    _, mine, theirs, index = source
                    pltpu.make_async_copy(
                        refs[mine].at[index],
                        blocks.at[block, pl.ds(pl.multiple_of(core * half, half), half)],
                        sems.at[block],
                    ).start()
                    pltpu.make_async_copy(
                        refs[theirs].at[index],
                        blocks.at[block, pl.ds(pl.multiple_of((1 - core) * half, half), half)],
                        sems.at[block],
                    ).start()


def wait_block(blocks, block, sems):
    pltpu.make_async_copy(blocks.at[block], blocks.at[block], sems.at[block]).wait()


def store_turned(target, turned, columns, section, core):
    half = target.shape[0] // 2
    for piece in range(16):
        path, owner = (piece >> 2) & 1, piece & 3
        away = owner ^ section
        place = ((away & 1) << 1) | (away >> 1) if path == 0 else away
        row = ((piece >> 3) ^ core) * half + (place >> 1) * (half // 2)
        row = row + path * (half // 4) + (place & 1) * PIECE_ROWS
        target[pl.ds(pl.multiple_of(row, 16), PIECE_ROWS), columns] = turned[
            piece * PIECE_ROWS : (piece + 1) * PIECE_ROWS
        ]


def put_travel(refs, which, columns, left, right):
    half = left.shape[0] // 2
    for side in range(2):
        rows = dot_plain(left[side * half : (side + 1) * half], right).astype(BF16)
        refs[2 * side][which, :, columns] = rows[: half // 2]
        refs[2 * side + 1][which, :, columns] = rows[half // 2 :]


def attend_forward_kernel(plan, weight_count, merge, info, *refs):
    weights, refs = refs[:weight_count], refs[weight_count:]
    if merge:
        x_ref, before_ref, part_ref, outer_ref, gain_ref, shift_ref, bias_ref = refs[:7]
        y_ref, qkv_ref, mixed_ref, joined_ref, blocks, sems, joined = refs[7:]
    else:
        x_ref, gain_ref, shift_ref, bias_ref, next_gain_ref, next_shift_ref = refs[:6]
        y_ref, qkv_ref, mixed_ref, caption_ref, blocks, sems = refs[6:]
    item = pl.program_id(0)
    items = pl.num_programs(0)
    length = info[item]
    width = x_ref.shape[-1]

    @pl.when(item == 0)
    def _():
        start_weights(info, items, weights, plan, blocks, sems)

    cap = slice(CAP_FIRST, CAP_FIRST + CAP_ROWS)
    if merge:
        joined[...] = x_ref[0].astype(F32)
        branch = part_ref[0].astype(F32) + outer_ref[...]
        is_true = true_positions(length, CAP_FIRST, CAP_ROWS, 0, "caption")
        captions = before_ref[0, cap] + jnp.where(is_true, branch, 0.0)
        position = CAP_FIRST + lax.broadcasted_iota(jnp.int32, (CAP_ROWS, 1), 0)
        captions = captions.astype(BF16).astype(F32)
        joined[cap] = jnp.where(position < PATCHES, joined[cap], captions)
        x = joined[...]
        joined_ref[0] = x.astype(BF16)
    else:
        x = x_ref[0].astype(F32)
    unit, _ = norm_parts(x)
    normed = (unit * gain_ref[...] + shift_ref[...]).astype(BF16)

    @pl.when(item == 0)
    def _():
        for block in range(4):
            wait_block(blocks, block, sems)

    queries = dot_plain(normed, blocks[0]) + bias_ref[:, :width]
    qkv_ref[0, :, :width] = (queries * HEAD_DIM ** (-0.5)).astype(BF16)
    qkv_ref[0, :, width : 2 * width] = dot_plain(normed, blocks[1]).astype(BF16)
    values = dot_plain(normed, blocks[2]) + bias_ref[:, width : 2 * width]
    qkv_ref[0, :, 2 * width :] = values.astype(BF16)
    key_true = true_positions(length, 0, ROWS, 1, "all")
    low_half, even, odd = head_masks()
    ones = jnp.ones((ROWS, PAIR), BF16)

    def scores_of(pair):
        at = pair * PAIR
        q2 = qkv_ref[0, :, at : at + PAIR]
        k2 = qkv_ref[0, :, width + at : width + at + PAIR]
        return dot_last(split_pair(q2, even, odd), k2)

    ahead = [scores_of(0), scores_of(1)]
    for pair in range(HEADS // 2):
        at = pair * PAIR
        scores = jnp.where(key_true, ahead.pop(0), -1e9)
        if pair + 2 < HEADS // 2:
            ahead.append(scores_of(pair + 2))
        weight = jnp.exp(scores - jnp.max(scores, axis=-1, keepdims=True)).astype(BF16)
        v2 = qkv_ref[0, :, 2 * width + at : 2 * width + at + PAIR]
        summed = dot_plain(weight, jnp.concatenate([v2, ones], axis=1))
        top = jnp.where(low_half, summed[:ROWS, :PAIR], summed[ROWS:, :PAIR])
        below = jnp.where(low_half, summed[:ROWS, PAIR:], summed[ROWS:, PAIR:])
        mixed_ref[0, :, at : at + PAIR] = (top / below).astype(BF16)
    branch = dot_plain(mixed_ref[0], blocks[3]) + bias_ref[:, 2 * width :]
    row_true = true_positions(length, 0, ROWS, 0, "all")
    y = x + jnp.where(row_true, branch, 0.0)
    y_ref[0] = y.astype(y_ref.dtype)
    if not merge:
        unit, _ = norm_parts(y[cap])
        caption_ref[0] = (unit * next_gain_ref[...] + next_shift_ref[...]).astype(BF16)


def attend_backward_kernel(plan, weight_count, first, info, *refs):
    weights, refs = refs[:weight_count], refs[weight_count:]
    x_ref, gain_ref, shift_ref, qkv_ref, mixed_ref, grad_ref = refs[:6]
    if first:
        after_ref, next_gain_ref, *parts = refs[6:12]
        refs = refs[12:]
    else:
        refs = refs[6:]
    out_ref, gain_grad_ref, shift_grad_ref, bias_grad_ref = refs[:4]
    travel_refs = refs[4:8]
    if first:
        next_gain_grad_ref, next_shift_grad_ref, joined = refs[8], refs[9], refs[-1]
    else:
        caption_ref = refs[8]
    blocks, sems, normed_turned, mixed_turned, branch_all, projected, mixed_grad = refs[
        10 if first else 9 :
    ][:7]
    item = pl.program_id(0)
    items = pl.num_programs(0)
    length = info[item]
    section, core = info[items], info[items + 1]
    width = x_ref.shape[-1]
    here = pl.ds(pl.multiple_of(item * ROWS, ROWS), ROWS)
    cap = slice(CAP_FIRST, CAP_FIRST + CAP_ROWS)

    @pl.when(item == 0)
    def _():
        start_weights(info, items, weights, plan, blocks, sems)

    def add_to(ref, part):
        @pl.when(item == 0)
        def _():
            ref[...] = part

        @pl.when(item > 0)
        def _():
            ref[...] += part

    x = x_ref[0].astype(F32)
    unit, scale = norm_parts(x)
    normed = (unit * gain_ref[...] + shift_ref[...]).astype(BF16)
    incoming = grad_ref[0].astype(F32)
    if first:
        after_unit, after_scale = norm_parts(after_ref[0, cap])
        caption_grad = parts[0][...].astype(F32)
        for part in parts[1:]:
            caption_grad = caption_grad + part[...].astype(F32)
        joined[...] = incoming
        joined[cap] += norm_back(caption_grad, after_unit, after_scale, next_gain_ref[...])
        incoming = joined[...]
        add_to(next_gain_grad_ref, jnp.sum(caption_grad * after_unit, axis=0, keepdims=True))
        add_to(next_shift_grad_ref, jnp.sum(caption_grad, axis=0, keepdims=True))
    row_true = true_positions(length, 0, ROWS, 0, "all")
    branch = jnp.where(row_true, incoming, 0.0).astype(BF16)
    branch_all[here, :] = branch
    store_turned(normed_turned, normed.T, here, section, core)
    store_turned(mixed_turned, mixed_ref[0].T, here, section, core)

    @pl.when(item == 0)
    def _():
        for block in range(4):
            wait_block(blocks, block, sems)

    mixed_grad[...] = dot_last(branch, blocks[3]).astype(BF16)
    key_true = true_positions(length, 0, ROWS, 0, "all")
    _, even, odd = head_masks()

    def products_of(pair):
        at = pair * PAIR
        q2 = split_pair(qkv_ref[0, :, at : at + PAIR], even, odd)
        k2 = qkv_ref[0, :, width + at : width + at + PAIR]
        v2 = qkv_ref[0, :, 2 * width + at : 2 * width + at + PAIR]
        g2 = split_pair(mixed_grad[:, at : at + PAIR], even, odd)
        return q2, k2, g2, dot_last(k2, q2), dot_last(v2, g2)

    ahead = [products_of(0)]
    for pair in range(HEADS // 2):
        at = pair * PAIR
        q2, k2, g2, scores, weight_grad = ahead.pop(0)
        if pair + 1 < HEADS // 2:
            ahead.append(products_of(pair + 1))
        scores = jnp.where(key_true, scores, -1e9)
        weight = jnp.exp(scores - jnp.max(scores, axis=0, keepdims=True))
        weight = weight * (1.0 / jnp.sum(weight, axis=0, keepdims=True))
        product = weight * weight_grad
        along = jnp.sum(product, axis=0, keepdims=True)
        score_grad = (product - weight * along).astype(BF16)
        values_grad = dot_plain(weight.astype(BF16), g2).astype(BF16)
        keys_grad = dot_plain(score_grad, q2).astype(BF16)
        k2_split = split_pair(k2, even, odd)
        stacked = jnp.concatenate([score_grad[:, :ROWS], score_grad[:, ROWS:]], axis=0)
        queries_grad = dot_first(stacked, k2_split).astype(BF16)
        queries_grad = (queries_grad.astype(F32) * HEAD_DIM ** (-0.5)).astype(BF16)
        projected[here, at : at + PAIR] = queries_grad
        projected[here, width + at : width + at + PAIR] = keys_grad
        projected[here, 2 * width + at : 2 * width + at + PAIR] = values_grad
    normed_grad = dot_last(projected[here, :width], blocks[0])
    normed_grad += dot_last(projected[here, width : 2 * width], blocks[1])
    normed_grad += dot_last(projected[here, 2 * width :], blocks[2])
    out = (incoming + norm_back(normed_grad, unit, scale, gain_ref[...])).astype(BF16)
    out_ref[0] = out
    if not first:
        is_true = true_positions(length, CAP_FIRST, CAP_ROWS, 0, "caption")
        caption_ref[0] = jnp.where(is_true, out[cap].astype(F32), 0.0).astype(BF16)
    add_to(gain_grad_ref, jnp.sum(normed_grad * unit, axis=0, keepdims=True))
    add_to(shift_grad_ref, jnp.sum(normed_grad, axis=0, keepdims=True))

    @pl.when(item == items - 1)
    def _():
        for block in range(4):
            columns = slice(block * width, (block + 1) * width)
            left = normed_turned if block < 3 else mixed_turned
            right = projected[:, columns] if block < 3 else branch_all[...]
            put_travel(travel_refs, 0, columns, left, right)
        bias_grad_ref[:, :width] = column_sum(projected[:, :width])
        bias_grad_ref[:, width : 2 * width] = column_sum(projected[:, 2 * width :])
        bias_grad_ref[:, 2 * width :] = column_sum(branch_all[...])


SHORT = pl.CostEstimate(flops=0, bytes_accessed=100_000, transcendentals=0)
LONG = pl.CostEstimate(flops=30_000_000_000, bytes_accessed=30_000_000, transcendentals=0)
ANYWHERE = pl.BlockSpec(memory_space=pl.ANY)


def whole_block(shape):
    return pl.BlockSpec(shape, lambda step, info: (0,) * len(shape))


def item_block(shape):
    return pl.BlockSpec((1,) + shape[1:], lambda step, info: (step,) + (0,) * (len(shape) - 1))


def blocks_scratch(count, width):
    return [pltpu.VMEM((count, width, width), BF16), pltpu.SemaphoreType.DMA((count,))]


def attend_forward(x, info, weights, gain, shift, bias, merge=None, following=None):
    arrays, plan = weights
    items, _, width = x.shape
    row = whole_block((1, width))
    bias_row = whole_block((1, 3 * width))
    caption_shape = (items, CAP_ROWS, width)
    if merge is not None:
        before, part, outer = merge
        operands = (x, before, part, outer, gain, shift, bias)
        specs = [item_block(x.shape), item_block(x.shape), item_block(caption_shape)]
        specs += [row, row, row, bias_row]
        last_shape, kind, scratch = x.shape, BF16, [pltpu.VMEM((ROWS, width), F32)]
    else:
        operands = (x, gain, shift, bias, *following)
        specs = [item_block(x.shape), row, row, bias_row, row, row]
        last_shape, kind, scratch = caption_shape, F32, []
    return pl.pallas_call(
        partial(attend_forward_kernel, plan, len(arrays), merge is not None),
        grid_spec=pltpu.PrefetchScalarGridSpec(
            num_scalar_prefetch=1,
            grid=(items,),
            in_specs=[ANYWHERE] * len(arrays) + specs,
            out_specs=[
                item_block(x.shape),
                item_block((items, ROWS, 3 * width)),
                item_block((items, ROWS, width)),
                item_block(last_shape),
            ],
            scratch_shapes=blocks_scratch(4, width) + scratch,
        ),
        out_shape=[
            jax.ShapeDtypeStruct(x.shape, kind),
            jax.ShapeDtypeStruct((items, ROWS, 3 * width), BF16),
            jax.ShapeDtypeStruct((items, ROWS, width), BF16),
            jax.ShapeDtypeStruct(last_shape, BF16),
        ],
        compiler_params=pltpu.CompilerParams(vmem_limit_bytes=VMEM_BYTES),
        cost_estimate=SHORT,
        name="attend_forward",
    )(info, *arrays, *operands)


def attend_backward(x, info, weights, gain, shift, qkv, mixed, incoming, first=None):
    arrays, plan = weights
    items, _, width = x.shape
    half = width // 2
    row = whole_block((1, width))
    caption_shape = (items, CAP_ROWS, width)
    operands = (x, gain, shift, qkv, mixed, incoming)
    specs = [item_block(x.shape), row, row, item_block(qkv.shape), item_block(mixed.shape)]
    specs += [item_block(incoming.shape)]
    outs = [
        (item_block(x.shape), x.shape, BF16),
        (row, (1, width), F32),
        (row, (1, width), F32),
        (whole_block((1, 3 * width)), (1, 3 * width), F32),
    ]
    outs += [(whole_block((1, half // 2, 4 * width)), (1, half // 2, 4 * width), BF16)] * 4
    scratch = []
    if first is not None:
        after, next_gain, parts = first
        operands += (after, next_gain, *parts)
        caption_rows = pl.BlockSpec((CAP_ROWS, width), lambda step, info: (step, 0))
        specs += [item_block(after.shape), row] + [caption_rows] * 4
        outs += [(row, (1, width), F32)] * 2
        scratch = [pltpu.VMEM((ROWS, width), F32)]
    else:
        outs += [(item_block(caption_shape), caption_shape, BF16)]
    return pl.pallas_call(
        partial(attend_backward_kernel, plan, len(arrays), first is not None),
        grid_spec=pltpu.PrefetchScalarGridSpec(
            num_scalar_prefetch=1,
            grid=(items,),
            in_specs=[ANYWHERE] * len(arrays) + specs,
            out_specs=[spec for spec, _, _ in outs],
            scratch_shapes=blocks_scratch(4, width)
            + [
                pltpu.VMEM((width, items * ROWS), BF16),
                pltpu.VMEM((width, items * ROWS), BF16),
                pltpu.VMEM((items * ROWS, width), BF16),
                pltpu.VMEM((items * ROWS, 3 * width), BF16),
                pltpu.VMEM((ROWS, width), BF16),
            ]
            + scratch,
        ),
        out_shape=[jax.ShapeDtypeStruct(shape, kind) for _, shape, kind in outs],
        compiler_params=pltpu.CompilerParams(vmem_limit_bytes=VMEM_BYTES),
        cost_estimate=LONG,
        name="attend_backward",
    )(info, *arrays, *operands)


def normal_parts(u):
    t = pl.reciprocal(1.0 + 0.23164190 * jnp.abs(u), approx=True)
    bell = jnp.exp2((u * -0.7213475204444817) * u)
    poly = t * (
        0.127414796
        + t * (-0.142248368 + t * (0.7107068705 + t * (-0.7265760135 + t * 0.5307027145)))
    )
    tail = poly * bell
    return jnp.where(u < 0, tail, 1.0 - tail), bell


def inner_forward(normed, matrix, bias):
    inner = dot_plain(normed, matrix) + bias
    cumulative, bell = normal_parts(inner)
    slope = cumulative + (inner * 0.3989422804014327) * bell
    return (inner * cumulative).astype(BF16), slope.astype(BF16)


def expert_forward_kernel(plan, weight_count, count, kind, info, *refs):
    weights, refs = refs[:weight_count], refs[weight_count:]
    x_ref, gain_ref, shift_ref, inner_ref, outer_ref = refs[:5]
    y_ref, act_ref, slope_ref, blocks, sems, normed, total = refs[5:]
    step = pl.program_id(0)
    items, _, width = x_ref.shape

    @pl.when(step == 0)
    def _():
        start_weights(info, items, weights, plan, blocks, sems)
        for item in range(items):
            x = x_ref[item, :count].astype(BF16).astype(F32)
            unit, _ = norm_parts(x)
            normed[item * count : (item + 1) * count] = (
                unit * gain_ref[...] + shift_ref[...]
            ).astype(BF16)

    wait_block(blocks, step, sems)
    wait_block(blocks, step + 4, sems)
    for at in range(0, width, 256):
        columns = slice(at, at + 256)
        act, slope = inner_forward(normed[...], blocks[step, :, columns], inner_ref[:, columns])
        act_ref[:, columns] = act
        slope_ref[:, columns] = slope
    part = dot_plain(act_ref[...], blocks[step + 4])

    @pl.when(step == 0)
    def _():
        total[...] = part

    @pl.when(step > 0)
    def _():
        total[...] += part

    @pl.when(step == pl.num_programs(0) - 1)
    def _():
        for item in range(items):
            row_true = true_positions(info[item], 0, count, 0, kind)
            branch = total[item * count : (item + 1) * count] + outer_ref[...]
            x = x_ref[item, :count].astype(BF16).astype(F32)
            y_ref[item, :count] = (x + jnp.where(row_true, branch, 0.0)).astype(BF16)
            if count < ROWS:
                y_ref[item, count:] = jnp.zeros((ROWS - count, width), BF16)


def expert_backward_kernel(plan, weight_count, count, kind, info, *refs):
    weights, refs = refs[:weight_count], refs[weight_count:]
    x_ref, gain_ref, shift_ref, act_ref, slope_ref, grad_ref = refs[:6]
    out_ref, gain_grad_ref, shift_grad_ref, inner_grad_ref, outer_grad_ref = refs[6:11]
    travel_refs = refs[11:15]
    blocks, sems, normed_turned, branch_turned, branch, inner_all, total = refs[15:]
    step = pl.program_id(0)
    items, _, width = x_ref.shape
    section, core = info[items], info[items + 1]

    @pl.when(step == 0)
    def _():
        start_weights(info, items, weights, plan, blocks, sems)
        outer = None
        for item in range(items):
            here = slice(item * count, (item + 1) * count)
            unit, _ = norm_parts(x_ref[item, :count].astype(BF16).astype(F32))
            normed = (unit * gain_ref[...] + shift_ref[...]).astype(BF16)
            row_true = true_positions(info[item], 0, count, 0, kind)
            incoming = grad_ref[item, :count].astype(F32)
            masked = jnp.where(row_true, incoming, 0.0).astype(BF16)
            branch[here] = masked
            store_turned(normed_turned, normed.T, here, section, core)
            store_turned(branch_turned, masked.T, here, section, core)
            term = column_sum(masked)
            outer = term if outer is None else outer + term
        outer_grad_ref[...] = outer

    wait_block(blocks, step, sems)
    wait_block(blocks, step + 4, sems)
    for at in range(0, width, 256):
        columns = slice(at, at + 256)
        act_grad = dot_last(branch[...], blocks[step + 4, columns])
        inner = (slope_ref[:, columns].astype(F32) * act_grad).astype(BF16)
        inner_all[:, columns] = inner
        inner_grad_ref[:, columns] = column_sum(inner)
        put_travel(travel_refs, 0, columns, normed_turned, inner)
        put_travel(travel_refs, 1, columns, branch_turned, act_ref[:, columns])
    part = dot_last(inner_all[...], blocks[step])

    @pl.when(step == 0)
    def _():
        total[...] = part

    @pl.when(step > 0)
    def _():
        total[...] += part

    @pl.when(step == pl.num_programs(0) - 1)
    def _():
        gain_sum, shift_sum = None, None
        for item in range(items):
            unit, scale = norm_parts(x_ref[item, :count].astype(BF16).astype(F32))
            normed_grad = total[item * count : (item + 1) * count]
            gain_part = jnp.sum(normed_grad * unit, axis=0, keepdims=True)
            shift_part = jnp.sum(normed_grad, axis=0, keepdims=True)
            gain_sum = gain_part if gain_sum is None else gain_sum + gain_part
            shift_sum = shift_part if shift_sum is None else shift_sum + shift_part
            incoming = grad_ref[item, :count].astype(F32)
            hidden = incoming + norm_back(normed_grad, unit, scale, gain_ref[...])
            out_ref[item, :count] = hidden.astype(BF16)
            if count < ROWS:
                out_ref[item, count:] = grad_ref[item, count:]
        gain_grad_ref[...] = gain_sum
        shift_grad_ref[...] = shift_sum


def shared_forward_kernel(*refs):
    *rows_refs, inputs_ref, inner_ref, outputs_ref = refs[:7]
    *part_refs, normed, total = refs[7:]
    count = rows_refs[0].shape[0]
    step = pl.program_id(0)

    @pl.when(step == 0)
    def _():
        for index, ref in enumerate(rows_refs):
            normed[index * count : (index + 1) * count] = ref[...]
        total[...] = jnp.zeros_like(total)

    act, _ = inner_forward(normed[...], inputs_ref[...], inner_ref[...])
    total[...] += dot_plain(act, outputs_ref[...])

    @pl.when(step == pl.num_programs(0) - 1)
    def _():
        for index, ref in enumerate(part_refs):
            ref[...] = total[index * count : (index + 1) * count].astype(BF16)


def shared_backward_kernel(plan, weight_count, info, *refs):
    weights, refs = refs[:weight_count], refs[weight_count:]
    rows_refs, grad_refs, inner_ref = refs[:4], refs[4:8], refs[8]
    part_refs, (keep_ref, send_ref, inner_grad_ref, outer_grad_ref) = refs[9:13], refs[13:17]
    blocks, sems, normed, branch, matrix = refs[17:]
    count, width = rows_refs[0].shape
    half = width // 2
    first = info.shape[0] - 3
    core = info[first + 1]
    start_weights(info, first, weights, plan, blocks, sems)
    for index in range(SECTIONS):
        here = slice(index * count, (index + 1) * count)
        normed[here] = rows_refs[index][...]
        branch[here] = grad_refs[index][...]
    outer_grad_ref[...] = column_sum(grad_refs[0][...])
    wait_block(blocks, 0, sems)
    wait_block(blocks, 1, sems)
    part = None
    for at in range(0, width, 256):
        columns = slice(at, at + 256)
        act, slope = inner_forward(normed[...], blocks[0, :, columns], inner_ref[:, columns])
        act_grad = dot_last(branch[...], blocks[1, columns])
        inner = (slope.astype(F32) * act_grad).astype(BF16)
        inner_grad_ref[:, columns] = column_sum(inner)
        matrix[0, :, columns] = dot_first(normed[...], inner).astype(BF16)
        matrix[1, :, columns] = dot_first(branch[...], act).astype(BF16)
        term = dot_last(inner, blocks[0, :, columns])
        part = term if part is None else part + term
    for index, ref in enumerate(part_refs):
        ref[...] = part[index * count : (index + 1) * count].astype(BF16)
    quarter = half // 4
    for which in range(2):
        for group in range(4):
            columns = slice(group * width, (group + 1) * width)
            mine = pl.multiple_of(core * half, 16) + group * quarter
            other = pl.multiple_of((1 - core) * half, 16) + group * quarter
            keep_ref[which, :, columns] = matrix[which, pl.ds(pl.multiple_of(mine, 16), quarter)]
            send_ref[which, :, columns] = matrix[which, pl.ds(pl.multiple_of(other, 16), quarter)]


def chunk_columns(rows, width):
    return pl.BlockSpec((rows, width), lambda step, info: (0, step))


def expert_forward(x, info, weights, gain, shift, inner, outer, count, kind):
    arrays, plan = weights
    items, _, width = x.shape
    hidden = inner.shape[1]
    row = whole_block((1, width))
    return pl.pallas_call(
        partial(expert_forward_kernel, plan, len(arrays), count, kind),
        grid_spec=pltpu.PrefetchScalarGridSpec(
            num_scalar_prefetch=1,
            grid=(hidden // width,),
            in_specs=[ANYWHERE] * len(arrays)
            + [whole_block(x.shape), row, row, chunk_columns(1, width), row],
            out_specs=[
                whole_block((items, ROWS, width)),
                chunk_columns(items * count, width),
                chunk_columns(items * count, width),
            ],
            scratch_shapes=blocks_scratch(8, width)
            + [
                pltpu.VMEM((items * count, width), BF16),
                pltpu.VMEM((items * count, width), F32),
            ],
        ),
        out_shape=[
            jax.ShapeDtypeStruct((items, ROWS, width), BF16),
            jax.ShapeDtypeStruct((items * count, hidden), BF16),
            jax.ShapeDtypeStruct((items * count, hidden), BF16),
        ],
        compiler_params=pltpu.CompilerParams(vmem_limit_bytes=VMEM_BYTES),
        cost_estimate=SHORT,
        name="expert_forward_" + kind,
    )(info, *arrays, x, gain, shift, inner, outer)


def expert_backward(x, info, weights, gain, shift, act, slope, incoming, count, kind):
    arrays, plan = weights
    items, _, width = x.shape
    half = width // 2
    hidden = act.shape[1]
    row = whole_block((1, width))
    travel = pl.BlockSpec((2, half // 2, width), lambda step, info: (0, 0, step))
    return pl.pallas_call(
        partial(expert_backward_kernel, plan, len(arrays), count, kind),
        grid_spec=pltpu.PrefetchScalarGridSpec(
            num_scalar_prefetch=1,
            grid=(hidden // width,),
            in_specs=[ANYWHERE] * len(arrays)
            + [
                whole_block(x.shape),
                row,
                row,
                chunk_columns(items * count, width),
                chunk_columns(items * count, width),
                whole_block(incoming.shape),
            ],
            out_specs=[whole_block(incoming.shape), row, row, chunk_columns(1, width), row]
            + [travel] * 4,
            scratch_shapes=blocks_scratch(8, width)
            + [
                pltpu.VMEM((width, items * count), BF16),
                pltpu.VMEM((width, items * count), BF16),
                pltpu.VMEM((items * count, width), BF16),
                pltpu.VMEM((items * count, width), BF16),
                pltpu.VMEM((items * count, width), F32),
            ],
        ),
        out_shape=[
            jax.ShapeDtypeStruct(incoming.shape, BF16),
            jax.ShapeDtypeStruct((1, width), F32),
            jax.ShapeDtypeStruct((1, width), F32),
            jax.ShapeDtypeStruct((1, hidden), F32),
            jax.ShapeDtypeStruct((1, width), F32),
        ]
        + [jax.ShapeDtypeStruct((2, half // 2, hidden), BF16)] * 4,
        compiler_params=pltpu.CompilerParams(vmem_limit_bytes=VMEM_BYTES),
        cost_estimate=SHORT,
        name="expert_backward_" + kind,
    )(info, *arrays, x, gain, shift, act, slope, incoming)


IN_VMEM = pl.BlockSpec(memory_space=pltpu.VMEM)
IN_SMEM = pl.BlockSpec(memory_space=pltpu.SMEM)


def shared_forward(rows, inputs, inner, outputs):
    count, width = rows[0].shape
    total = SECTIONS * count
    hidden = inner.shape[1]
    return pl.pallas_call(
        shared_forward_kernel,
        grid=(hidden // width,),
        in_specs=[pl.BlockSpec(rows[0].shape, lambda step: (0, 0))] * 4
        + [
            pl.BlockSpec((width, width), lambda step: (0, step)),
            pl.BlockSpec((1, width), lambda step: (0, step)),
            pl.BlockSpec((width, width), lambda step: (step, 0)),
        ],
        out_specs=[pl.BlockSpec((count, width), lambda step: (0, 0))] * SECTIONS,
        scratch_shapes=[pltpu.VMEM((total, width), BF16), pltpu.VMEM((total, width), F32)],
        out_shape=[jax.ShapeDtypeStruct((count, width), BF16)] * SECTIONS,
        compiler_params=pltpu.CompilerParams(vmem_limit_bytes=VMEM_BYTES),
        cost_estimate=SHORT,
        name="shared_forward",
    )(*rows, inputs, inner, outputs)


def shared_backward(rows, grads, info, weights, inner):
    arrays, plan = weights
    count, width = rows[0].shape
    total = SECTIONS * count
    travel = (2, width // 8, 4 * width)
    return pl.pallas_call(
        partial(shared_backward_kernel, plan, len(arrays)),
        in_specs=[IN_SMEM] + [ANYWHERE] * len(arrays) + [IN_VMEM] * 9,
        out_specs=[IN_VMEM] * 8,
        scratch_shapes=blocks_scratch(2, width)
        + [
            pltpu.VMEM((total, width), BF16),
            pltpu.VMEM((total, width), BF16),
            pltpu.VMEM((2, width, width), BF16),
        ],
        out_shape=[
            *[jax.ShapeDtypeStruct((count, width), BF16)] * SECTIONS,
            jax.ShapeDtypeStruct(travel, BF16),
            jax.ShapeDtypeStruct(travel, BF16),
            jax.ShapeDtypeStruct((1, width), F32),
            jax.ShapeDtypeStruct((1, width), F32),
        ],
        compiler_params=pltpu.CompilerParams(vmem_limit_bytes=VMEM_BYTES),
        cost_estimate=SHORT,
        name="shared_backward",
    )(info, *arrays, *rows, *grads, inner)


def plane_turn(plane, planes):
    return ((plane & 1) << 1) | (plane >> 1) if planes == 4 else 0


def finish_kernel(planes, info, scale_ref, mine_ref, theirs_ref, *refs):
    step = pl.program_id(0)
    count = mine_ref.shape[1]
    placed = refs[-1]
    outs = refs[:-1]
    width = placed.shape[1]
    half = width // 2
    at = info.shape[0] - 3
    section, core = info[at], info[at + 1]
    turn = plane_turn(info[at + 2], planes)
    turned = turn if count == 1 else 0
    scale = scale_ref[0, 0]
    columns = pl.ds(pl.multiple_of((step ^ turned) * width, width), width)

    def place(which):
        def by_rows():
            for side, ref in enumerate((mine_ref, theirs_ref)):
                for away in range(SECTIONS):
                    for path in range(2):
                        row = (core ^ side) * half + path * (half // 2)
                        row = row + (section ^ away) * PIECE_ROWS
                        placed[pl.ds(pl.multiple_of(row, 16), PIECE_ROWS), :] = ref[
                            away, which, path * PIECE_ROWS : (path + 1) * PIECE_ROWS, columns
                        ].astype(F32)

        def by_columns():
            for side, ref in enumerate((mine_ref, theirs_ref)):
                for group in range(4):
                    quarter = half // 4
                    row = (core ^ side) * half + group * quarter
                    column = pl.multiple_of((group ^ turn) * width, width)
                    placed[pl.ds(pl.multiple_of(row, 16), quarter), :] = ref[
                        step, which, :, pl.ds(column, width)
                    ].astype(F32)

        if count == 1:
            by_rows()
        else:
            pl.when(section != 0)(by_rows)
            pl.when(section == 0)(by_columns)

    place(0)
    if count == 1:

        @pl.when(step < 3)
        def _():
            outs[0][0] = placed[...] / scale

        @pl.when(step == 3)
        def _():
            outs[1][0] = placed[...] / scale

    else:
        outs[0][0] = placed[...] / scale
        place(1)
        outs[1][0] = (placed[...] / scale).T


def finish(info, scale, mine, theirs, planes):
    count, hidden = mine.shape[1], mine.shape[3]
    width = hidden // 4
    if count == 1:
        shapes = [(1, width, 3 * width), (1, width, width)]
        maps = [lambda step, info: (0, 0, jnp.minimum(step, 2)), lambda step, info: (0, 0, 0)]
    else:
        shapes = [(1, width, hidden), (1, hidden, width)]
        maps = [lambda step, info: (0, 0, step), lambda step, info: (0, step, 0)]
    return pl.pallas_call(
        partial(finish_kernel, planes),
        grid_spec=pltpu.PrefetchScalarGridSpec(
            num_scalar_prefetch=1,
            grid=(4,),
            in_specs=[IN_SMEM, whole_block(mine.shape), whole_block(mine.shape)],
            out_specs=[pl.BlockSpec((1, width, width), at) for at in maps],
            scratch_shapes=[pltpu.VMEM((width, width), F32)],
        ),
        out_shape=[jax.ShapeDtypeStruct(shape, F32) for shape in shapes],
        compiler_params=pltpu.CompilerParams(vmem_limit_bytes=VMEM_BYTES),
        cost_estimate=SHORT,
        name="finish",
    )(info, scale, mine, theirs)


def pack_kernel(count, plan, info, *refs):
    sources, outs, sems = refs[:count], refs[count:-1], refs[-1]
    first = info.shape[0] - 3
    section, core, plane = info[first], info[first + 1], info[first + 2]
    half = outs[0].shape[1]
    for index, (out, choices) in enumerate(zip(outs, plan)):
        for at, at_plane, parts in choices:
            here = section == at
            if at_plane is not None:
                here = here & (plane == at_plane)

            @pl.when(here)
            def _(index=index, out=out, parts=parts):
                for block, part in enumerate(parts):
                    if part[0] == "own":
                        _, which, row, column = part
                        rows = pl.ds(pl.multiple_of(row + core * half, half), half)
                        source = sources[which].at[rows, pl.ds(column, out.shape[2])]
                    else:
                        source = sources[part[1]].at[block]
                    pltpu.make_async_copy(source, out.at[block], sems.at[index, block]).start()

    for index, out in enumerate(outs):
        for block in range(2):
            pltpu.make_async_copy(out.at[block], out.at[block], sems.at[index, block]).wait()


def pack(info, sources, plan, shape):
    return pl.pallas_call(
        partial(pack_kernel, len(sources), plan),
        in_specs=[IN_SMEM] + [ANYWHERE] * len(sources),
        out_specs=[IN_VMEM] * len(plan),
        scratch_shapes=[pltpu.SemaphoreType.DMA((len(plan), 2))],
        out_shape=[jax.ShapeDtypeStruct(shape, BF16)] * len(plan),
        cost_estimate=SHORT,
        name="pack",
    )(info, *sources)


def over_section(value, bits, sources=range(SECTIONS)):
    return lax.ppermute(value, "section", [(at, at ^ bits) for at in sources])


def over_core(value):
    return lax.ppermute(value, "core", [(0, 1), (1, 0)])


def over_plane(value, pairs):
    return lax.ppermute(value, "z", pairs)


def added(left, right):
    return (left.astype(F32) + right.astype(F32)).astype(BF16)


def after(value, *earlier):
    return lax.optimization_barrier((value,) + earlier)[0]


def under(outputs, *arrivals):
    joined = lax.optimization_barrier(tuple(outputs) + arrivals)
    return list(joined[: len(outputs)]), list(joined[len(outputs) :])


def by_section(section, values):
    result, last = None, None
    for at in sorted(values):
        if result is None:
            result = values[at]
        elif values[at] is not last:
            result = jnp.where(section >= at, values[at], result)
        last = values[at]
    return result


def total(*values):
    result = values[0].astype(F32)
    for value in values[1:]:
        result = result + value.astype(F32)
    return result.astype(BF16)


class Sums:
    def __init__(self, travel):
        self.stay, self.move, self.other_stay, self.other_move = travel
        self.size = self.stay.shape[1] // 2

    def cross(self, *earlier):
        if earlier:
            self.other_move = after(self.other_move, *earlier)
            self.other_stay = after(self.other_stay, *earlier)
        self.got_move, self.got_stay = over_core(self.other_move), over_core(self.other_stay)

    def first_sends(self):
        size = self.size
        self.sent = [
            total(self.move[:, at : at + size], self.got_move[:, at : at + size])
            for at in (0, size)
        ]
        return self.sent

    def second_sends(self, from_x, from_y):
        size, half = self.size, self.size // 2
        self.first = from_x, from_y
        to_y = total(self.stay[:, half:size], self.got_stay[:, half:size], from_x[:, half:])
        to_x = total(
            self.stay[:, size + half :], self.got_stay[:, size + half :], from_y[:, half:]
        )
        self.sent = [to_x, to_y]
        return self.sent

    def whole(self, from_x, from_y):
        size, half = self.size, self.size // 2
        parts = []
        for at, first, second in ((0, self.first[0], from_y), (size, self.first[1], from_x)):
            here = slice(at, at + half)
            parts.append(total(self.stay[:, here], self.got_stay[:, here], first[:, :half], second))
        return jnp.concatenate(parts, axis=1)


def over_links(sends):
    return [over_section(sends[0], 1), over_section(sends[1], 2)]


class Planes:
    def __init__(self, value, plane, planes):
        self.value, self.plane, self.planes, self.turn = value, plane, planes, 0

    def sends(self, *earlier):
        value = after(self.value, *earlier) if earlier else self.value
        if self.planes != 4:
            return (value,)
        bits = (1, 2, 2, 1)[self.turn]
        if self.turn < 2:
            bit = (self.plane & 1, self.plane >> 1)[self.turn]
            size = value.shape[-1] // 2
            value = lax.dynamic_slice_in_dim(value, (1 - bit) * size, size, value.ndim - 1)
        return (over_plane(value, [(at, at ^ bits) for at in range(4)]),)

    def take(self, arrived):
        if self.planes != 4:
            self.value = lax.psum(arrived, "z") if self.turn == 3 else arrived
        elif self.turn < 2:
            bit = (self.plane & 1, self.plane >> 1)[self.turn]
            size = self.value.shape[-1] // 2
            keep = lax.dynamic_slice_in_dim(self.value, bit * size, size, self.value.ndim - 1)
            self.value = added(keep, arrived)
        else:
            self.value = jnp.concatenate([self.value, arrived], axis=-1)
        self.turn += 1

    def in_order(self, value):
        if self.planes != 4:
            return value
        size, turn = value.shape[-1] // 4, plane_turn(self.plane, 4)
        parts = [
            lax.dynamic_slice_in_dim(value, (at ^ turn) * size, size, value.ndim - 1)
            for at in range(4)
        ]
        return jnp.concatenate(parts, axis=-1)


class Weights:
    def __init__(self, own, info, planes):
        self.own, self.info = own, info
        self.four = planes == 4
        self.plan = PLAN_FOUR if self.four else PLAN_ANY
        self.half, self.width = own[1].shape[0] // 2, own[1].shape[1]
        self.mine, self.theirs, self.arrived = {}, {}, {}

    def place(self, layer, block):
        if layer in "ac":
            return (0, 0, block * self.width) if block < 3 else (1, 0, 0)
        if layer == "g":
            return (2, 0, block * self.width) if block < 4 else (3, (block - 4) * self.width, 0)
        return (2, 0, block * self.width) if block < 4 else (3, (block - 4) * self.width, 0)

    def choices(self, sends, sources):
        result = []
        for at in range(SECTIONS):
            name = sends.get(at)
            if name is not None and HOMES[name[0]] != at:
                key = self.arrived[at, name]
                if key not in sources:
                    sources[key] = len(self.own) + len(sources)
                result.append((at, None, [("arrived", sources[key])] * 2))
                continue
            for plane in range(4) if name == "F" else (None,):
                piece = ("f" + str(plane)) if name == "F" else name or "a0"
                layer, index = piece[0], int(piece[1])
                if layer in "ac":
                    blocks = ATTEND_BLOCKS[index]
                else:
                    blocks = (index, 4 + index) if layer == "g" else EXPERT_BLOCKS[index]
                parts = [("own",) + self.place(layer, block) for block in blocks]
                result.append((at, plane, parts))
        return result

    def packed(self, wanted):
        sources = {}
        plan = [self.choices(sends, sources) for sends in wanted]
        arrays = list(self.own) + [self.mine[key] for key in sources]
        return pack(self.info, arrays, plan, (2, self.half, self.width))

    def sends(self, step):
        if step == "F":
            return [{at: "F" for at in range(SECTIONS)}]
        return [sends for sends in self.plan[step] if sends]

    def payloads(self, *steps):
        wanted = [sends for step in steps for sends in self.sends(step)]
        return list(self.packed(wanted))

    def move(self, step, payloads):
        links = [(link, sends) for link, sends in enumerate(self.plan[step]) if sends]
        for (link, sends), payload in zip(links, payloads):
            self.mine[step, link] = over_section(payload, link + 1, sorted(sends))
            for at, name in sends.items():
                self.arrived[at ^ (link + 1), name] = (step, link)
        return [(step, link) for link, _ in links]

    def move_planes(self, step):
        up, down = self.mine["plane", step - 1], self.mine["plane", 1 - step]
        up = over_plane(up, [(at, at + 1) for at in range(step - 1, 3)])
        down = over_plane(down, [(at, at - 1) for at in range(4 - step, 0, -1)])
        self.mine["plane", step], self.mine["plane", -step] = up, down
        return [("plane", step), ("plane", -step)]

    def cross(self, keys):
        for key in keys:
            self.theirs[key] = over_core(self.mine[key])
        return keys

    def join(self, outputs, mine=(), theirs=()):
        values = [self.mine[key] for key in mine] + [self.theirs[key] for key in theirs]
        outputs, values = under(outputs, *values)
        for key, value in zip(mine, values):
            self.mine[key] = value
        for key, value in zip(theirs, values[len(mine) :]):
            self.theirs[key] = value
        return outputs

    def layer(self, layer):
        arrays, places = list(self.own), {}

        def place(key):
            if key not in places:
                places[key] = len(arrays)
                arrays.extend([self.mine[key], self.theirs[key]])
            return places[key], places[key] + 1

        if layer in "ac":
            names = [(layer + str(index), ATTEND_BLOCKS[index]) for index in range(2)]
        else:
            names = [(layer + str(index), EXPERT_BLOCKS[index]) for index in range(4)]
        plan = []
        for at in range(SECTIONS):
            if layer == "g":
                names = [("g" + str(at), (0, 1))]
            if HOMES[layer] == at:
                steps = []
                for name, blocks in names:
                    for block in blocks:
                        source = block * 4 if layer == "g" else block
                        steps.append((block, ("own",) + self.place(layer, source)))
                plan.append((at, None, steps))
                continue
            by_plane = layer == "f" and self.four
            for plane in range(4) if by_plane else (None,):
                steps = []
                for index, (name, blocks) in enumerate(names):
                    key = ("plane", plane - index) if by_plane else self.arrived[at, name]
                    for which, block in enumerate(blocks):
                        steps.append((block, ("piece",) + place(key) + (which,)))
                plan.append((at, plane, steps))
        return arrays, plan


def per_device(
    tokens,
    caption_lengths,
    attend_gain,
    attend_shift,
    attend_inputs,
    attend_bias,
    attend_output,
    expert_gain,
    expert_shift,
    expert_inputs,
    expert_inner_bias,
    expert_outputs,
    expert_outer_bias,
    cotangent,
):
    section, core, plane = lax.axis_index("section"), lax.axis_index("core"), lax.axis_index("z")
    planes = lax.axis_size("z")
    items, positions, width = tokens.shape
    hidden = expert_inputs.shape[-1]
    info = [value.reshape(1).astype(jnp.int32) for value in (section, core, plane)]
    info = jnp.concatenate([caption_lengths] + info)
    weights = Weights(
        (attend_inputs[0], attend_output[0], expert_inputs[0], expert_outputs[0]), info, planes
    )

    def to_sections(value):
        return [value] + [over_section(value, bits) for bits in (1, 2, 3)]

    def items_of(part):
        return part.reshape(items, CAP_ROWS, width)

    pad = ((0, 0), (0, ROWS - positions), (0, 0))
    x0 = jnp.pad(tokens, pad)
    last_grad = jnp.pad(cotangent, pad)
    rows = jnp.concatenate(
        [
            attend_gain,
            attend_shift,
            attend_bias,
            expert_gain,
            expert_shift,
            expert_inner_bias,
            expert_outer_bias,
            jnp.full((1, 128), jnp.sum(caption_lengths), F32),
        ],
        axis=1,
    )
    rows = to_sections(rows)
    keys = weights.move(0, weights.payloads(0))
    x0, last_grad, *rows = weights.join([x0, last_grad, *rows], keys)
    keys1 = weights.move(1, weights.payloads(1))
    rows = jnp.concatenate(rows, axis=0)
    language_count = jnp.sum(rows[:, -128:], axis=0, keepdims=True)
    rows = [lax.dynamic_index_in_dim(rows, at ^ section, 0) for at in range(SECTIONS)]
    sizes = [width, width, 3 * width, width, width, hidden, width]
    ends = [sum(sizes[: at + 1]) for at in range(len(sizes))]
    used = [(0, 0), (0, 1), (0, 2), (0, 3), (0, 4), (0, 5), (1, 3), (1, 4), (1, 5), (1, 6)]
    used += [(0, 6), (2, 0), (2, 1), (2, 2), (3, 3), (3, 4), (3, 5), (3, 6)]
    kept = [rows[slot][:, ends[which] - sizes[which] : ends[which]] for slot, which in used]
    language_count, *kept = weights.join([language_count, *kept], keys1)
    kept = dict(zip(used, kept))

    def row(slot, which):
        return kept[slot, which]

    crossed = weights.cross(keys + keys1)
    sends = weights.payloads(2, "F") if weights.four else weights.payloads(2)
    sends, (info, language_count) = under(sends, info, language_count)
    keys = weights.move(2, sends[:2])
    info, language_count = weights.join(
        [info, language_count + over_core(language_count)], theirs=crossed
    )
    plane_keys = []
    if weights.four:
        weights.mine["plane", 0] = sends[2]
        plane_keys = weights.move_planes(1)
    attend0 = weights.layer("a")
    outputs = attend_forward(
        x0, info, attend0, row(0, 0), row(0, 1), row(0, 2), following=(row(0, 3), row(0, 4))
    )
    y0, qkv0, mixed0, caption_rows = weights.join(outputs, keys)
    caption_rows = to_sections(caption_rows.reshape(-1, width))
    early_keys = keys
    sends, caption_rows[1:2] = under(weights.payloads(3), caption_rows[1])
    keys = weights.move(3, sends)
    caption_rows = weights.join(caption_rows, plane_keys)
    crossed = weights.cross(early_keys)
    outputs = shared_forward(caption_rows, expert_inputs[0], expert_inner_bias, expert_outputs[0])
    part = weights.join(outputs, keys, crossed)
    (y0,) = weights.join([y0], theirs=weights.cross(keys))
    branch = {at: over_section(part[at], at, [0]) for at in range(1, SECTIONS)}
    keys = weights.move_planes(2) if weights.four else []
    expert1 = weights.layer("e")
    outputs = expert_forward(
        y0, info, expert1, row(1, 3), row(1, 4), row(1, 5), row(1, 6), PATCH_ROWS, "patch"
    )
    outputs, moved = under(outputs, *branch.values())
    x2, act1, slope1 = weights.join(outputs, keys)
    branch = dict(zip(branch, moved))
    branch[0] = part[0]
    branch = items_of(by_section(section, branch))
    if weights.four:
        keys = weights.move_planes(3)
        crossed = [("plane", step) for step in range(-2, 3)]
    else:
        keys = []
        for step in (4, 5):
            weights.move(step, weights.payloads(step))
        crossed = [(4, 0), (4, 1), (5, 0)]
    weights.cross(crossed)
    if not weights.four:
        (x2,) = weights.join([x2], theirs=crossed)
    attend2 = weights.layer("c")
    outputs = attend_forward(
        x2, info, attend2, row(2, 0), row(2, 1), row(2, 2), merge=(y0, branch, row(0, 6))
    )
    if weights.four:
        language_count += over_plane(language_count, [(at, at ^ 1) for at in range(4)])
    x3, qkv2, mixed2, x2, language_count = weights.join(
        [*outputs, language_count], keys, [] if not weights.four else crossed
    )
    if weights.four:
        (x3,) = weights.join([x3], theirs=weights.cross(keys))
    if weights.four:
        language_count += over_plane(language_count, [(at, at ^ 2) for at in range(4)])
    else:
        language_count = lax.psum(language_count, "z")
    expert3 = weights.layer("f")
    outputs = expert_forward(
        x3, info, expert3, row(3, 3), row(3, 4), row(3, 5), row(3, 6), ROWS, "all"
    )
    layer_output, act3, slope3, language_count = under([*outputs, language_count])[0]
    language_count = language_count[0, 0].astype(jnp.int32)
    vision_count = PATCHES * items * SECTIONS * 2 * planes
    counts = jnp.stack(
        [jnp.full((), vision_count, jnp.int32), language_count, language_count + vision_count]
    )

    def together(sends):
        arrived = []
        for bits, parts in zip((1, 2), zip(*sends)):
            flat = [part.reshape(-1, hidden) for part in parts]
            moved = over_section(jnp.concatenate(flat, axis=0), bits)
            ends, at = [], 0
            for part, rows_of in zip(parts, flat):
                ends.append(moved[at : at + rows_of.shape[0]].reshape(part.shape))
                at += rows_of.shape[0]
            arrived.append(ends)
        return list(zip(*arrived))

    def small_rows(values):
        flat = jnp.concatenate(values, axis=1)
        count = -(-flat.shape[1] // hidden)
        flat = jnp.pad(flat, ((0, 0), (0, count * hidden - flat.shape[1])))
        return flat.reshape(count, hidden)

    def to_home(sums):
        got = [by_section(section, sums)]
        for bits in (1, 2, 3):
            sends = {at ^ bits: sums[at] for at in sums}
            got.append(over_section(by_section(section, sends), bits, sorted(sends)))
        return got

    keys = []
    if weights.four:
        sends, (layer_output, last_grad) = under(weights.payloads(4), layer_output, last_grad)
        keys = weights.move(4, sends)
    outputs = expert_backward(
        x3, info, expert3, row(3, 3), row(3, 4), act3, slope3, last_grad, ROWS, "all"
    )
    outputs = weights.join(outputs, keys)
    crossed = weights.cross(keys)
    grad3, *small3 = outputs[:5]
    sums3 = Sums(outputs[5:])
    sums3.cross()
    moved = over_links(sums3.first_sends())
    grad3 = after(grad3, *sums3.sent)
    outputs = attend_backward(
        x2, info, attend2, row(2, 0), row(2, 1), qkv2, mixed2, grad3
    )
    outputs, moved = under(outputs, *moved, sums3.got_stay)
    outputs = weights.join(outputs, theirs=crossed)
    grad2, *small2 = outputs[:4]
    sums2, caption_grad = Sums(outputs[4:8]), outputs[8]
    caption_grads = to_sections(caption_grad.reshape(-1, width))
    sums3.got_stay = moved[2]
    sums2.cross()
    moved3, moved2 = together([sums3.second_sends(*moved[:2]), sums2.first_sends()])
    grad2 = after(grad2, *sums3.sent, *sums2.sent)
    outputs = expert_backward(
        y0, info, expert1, row(1, 3), row(1, 4), act1, slope1, grad2, PATCH_ROWS, "patch"
    )
    outputs, moved = under(outputs, *caption_grads, *moved3, *moved2)
    caption_grads, moved3, moved2 = moved[:4], moved[4:6], moved[6:]
    grad1, *small1 = outputs[:5]
    sums1 = Sums(outputs[5:])
    sum3 = sums3.whole(*moved3)
    inner_quarter = lax.dynamic_slice(row(0, 5), (0, section * width), (1, width))
    inner_quarter = after(inner_quarter, grad1)
    outputs = shared_backward(
        caption_rows, caption_grads, info, weights.layer("g"), inner_quarter
    )
    parts, (keep0, send0, inner_grad, outer_grad) = outputs[:4], outputs[4:]
    got = [over_section(parts[bits], bits) for bits in (1, 2, 3)]
    planes0 = Planes(added(keep0, over_core(send0)), plane, planes)
    whole3 = lax.psum(sum3, "z")
    sums1.cross(parts[1])
    sends = [*sums1.first_sends(), *sums2.second_sends(*moved2)]
    *sends, got[0] = lax.optimization_barrier((*sends, got[0]))
    moved1, moved2 = over_links(sends[:2]), over_links(sends[2:])
    sent0 = planes0.sends(got[0])
    parts = [parts[0], *got]
    grad1 = after(grad1, *sends)
    outputs = attend_backward(
        x0,
        info,
        attend0,
        row(0, 0),
        row(0, 1),
        qkv0,
        mixed0,
        grad1,
        first=(y0, row(0, 3), parts),
    )
    outputs, moved = under(outputs, *moved1, *moved2, *sent0, sums1.got_stay, sums2.got_stay)
    moved1, moved2, sent0 = moved[:2], moved[2:4], moved[4:5]
    sums1.got_stay, sums2.got_stay = moved[5:]
    planes0.take(*sent0)
    tokens_grad, *small_first = outputs[:4]
    sums_first, gain_grad, shift_grad = Sums(outputs[4:8]), outputs[8], outputs[9]
    sums_first.cross()
    inner_grad = lax.dynamic_update_slice(
        jnp.zeros((1, hidden), F32), inner_grad, (0, section * width)
    )
    small = small_rows(
        small_first + [gain_grad, shift_grad, inner_grad, outer_grad] + small2 + small1 + small3
    )
    small = added(small, over_core(small))
    to_x, to_y = sums_first.first_sends()
    to_x, to_y = lax.optimization_barrier((jnp.concatenate([to_x[0], small], axis=0), to_y))
    moved = over_links((to_x, to_y))
    planes0.take(*planes0.sends(to_x, to_y))
    late = [after(value, to_x, to_y) for value in sums1.second_sends(*moved1)]
    size = to_y.shape[1]
    small = added(small, moved[0][size:])
    to_x, to_y = sums_first.second_sends(moved[0][None, :size], moved[1])
    to_y = jnp.concatenate([to_y, small[None]], axis=1)
    to_x, to_y, whole3, *late = lax.optimization_barrier((to_x, to_y, whole3, *late))
    moved, moved1 = over_links((to_x, to_y)), over_links(late)
    planes0.take(*planes0.sends(to_x, to_y))
    moved, moved1 = under(moved, *moved1)
    size = to_x.shape[1]
    last = sums_first.whole(moved[0], moved[1][:, :size])
    sum2 = sums2.whole(*moved2)
    small = added(small, moved[1][0, size:])
    small_count = small.shape[0]
    eighth = last.shape[1]
    planes_last = Planes(jnp.concatenate([last[0], sum2[0], small], axis=0), plane, planes)
    sum1, whole3 = lax.optimization_barrier((sums1.whole(*moved1), whole3))
    whole1 = lax.psum(sum1, "z")
    planes_last.take(*planes_last.sends())
    planes0.take(*planes0.sends(planes_last.value))
    home_early = to_home({0: planes0.value, 3: after(whole3, planes0.value)})
    planes_last.take(*planes_last.sends())
    planes_last.take(*planes_last.sends(*home_early[1:3]))
    planes_last.take(*planes_last.sends(home_early[3]))
    last, whole1 = lax.optimization_barrier((planes_last.value, whole1))
    home_late = to_home({1: whole1})
    home_attend = to_home({0: last[None, :eighth], 2: last[None, eighth : 2 * eighth]})
    small = planes_last.in_order(last[2 * eighth :].astype(F32))

    as_float = counts.astype(F32)
    one = jnp.ones((), F32)
    attend_scales = jnp.stack([as_float[2], one, as_float[2], one])
    expert_scales = jnp.stack([as_float[1], as_float[0], one, as_float[2]])

    def placed(pieces, scales):
        scale = lax.dynamic_index_in_dim(scales, section, 0).reshape(1, 1)
        pieces = jnp.stack(pieces)
        return finish(info, scale, pieces, over_core(pieces), planes)

    blank = jnp.zeros_like(home_late[0])
    inputs_whole, outputs_whole = placed(
        [
            by_section(section, {0: early, 1: late, 2: blank, 3: early})
            for early, late in zip(home_early, home_late)
        ],
        expert_scales,
    )
    blank = jnp.zeros_like(home_attend[0])
    attend_whole, output_whole = placed(
        [by_section(section, {0: got, 1: blank, 2: got, 3: blank}) for got in home_attend],
        attend_scales,
    )

    attend_size, expert_size = 5 * width, 3 * width + hidden
    cuts = [attend_size, attend_size + expert_size]
    cuts += [cuts[1] + attend_size, cuts[1] + attend_size + expert_size]
    small = jnp.split(small.reshape(-1)[: cuts[3] + expert_size], cuts)
    none_attend, none_expert = jnp.zeros_like(small[0]), jnp.zeros_like(small[1])
    attend_small = jnp.stack([small[0], none_attend, small[2], none_attend])
    expert_small = jnp.stack([small[1], small[3], none_expert, small[4]])
    attend_small = attend_small / attend_scales.reshape(-1, 1)
    expert_small = expert_small / expert_scales.reshape(-1, 1)
    attend_small = lax.dynamic_index_in_dim(attend_small, section, 0)
    expert_small = lax.dynamic_index_in_dim(expert_small, section, 0)
    return (
        layer_output[:, :positions],
        tokens_grad[:, :positions],
        attend_small[:, :width],
        attend_small[:, width : 2 * width],
        attend_whole,
        attend_small[:, 2 * width :],
        output_whole,
        expert_small[:, :width],
        expert_small[:, width : 2 * width],
        inputs_whole,
        expert_small[:, 2 * width : 2 * width + hidden],
        outputs_whole,
        expert_small[:, 2 * width + hidden :],
        counts,
    )


def solution(mesh):
    sections, groups = mesh.shape["section"], mesh.shape["dp"]
    split = Mesh(mesh.devices.reshape(sections, groups // 2, 2), ("section", "z", "core"))
    items = P(("section", "z", "core"), None, None)
    flat = P("section", None)
    matrix = P("section", None, None)
    placed = (
        items,
        P(("section", "z", "core")),
        flat,
        flat,
        matrix,
        flat,
        matrix,
        flat,
        flat,
        matrix,
        flat,
        matrix,
        flat,
        items,
    )
    return jax.shard_map(
        per_device,
        mesh=split,
        in_specs=placed,
        out_specs=(
            items,
            items,
            flat,
            flat,
            matrix,
            flat,
            matrix,
            flat,
            flat,
            matrix,
            flat,
            matrix,
            flat,
            P(),
        ),
        check_vma=False,
    )
```

```python
from functools import partial

import jax
import jax.numpy as jnp
from jax import lax
from jax.experimental import pallas as pl
from jax.experimental.pallas import tpu as pltpu
from jax.sharding import Mesh
from jax.sharding import PartitionSpec as P

HEADS = 12
HEAD_DIM = 64
PATCHES = 197
ROWS = 256
CAP_FIRST, CAP_ROWS = 192, 48
PATCH_ROWS = 208
PAIR = 2 * HEAD_DIM
SECTIONS = 4
PIECE_ROWS = 48
VMEM_BYTES = 58 * 1024 * 1024
F32 = jnp.float32
BF16 = jnp.bfloat16

PLAN_FOUR = (
    ({0: "a0", 1: "e0", 2: "c0", 3: "F"}, {0: "a1", 1: "e2", 2: "c0", 3: "F"}),
    ({0: "a1", 1: "e1", 2: "a1", 3: "e2"}, {0: "a0", 1: "a0", 2: "F", 3: "c0"}),
    ({0: "g3", 1: "e2", 2: "c1"}, {0: "e0", 1: "e3", 2: "c1"}),
    ({0: "g1", 1: "e3", 2: "e0", 3: "e3"}, {0: "e1", 1: "e1", 3: "c1"}),
    ({}, {0: "g2", 1: "g3"}),
)
PLAN_ANY = (
    ({0: "a0", 1: "e0", 2: "c0", 3: "f0"}, {0: "a1", 1: "e2", 2: "c0", 3: "f0"}),
    ({0: "a1", 1: "e1", 2: "a1", 3: "e2"}, {0: "a0", 1: "a0", 2: "c1", 3: "f1"}),
    ({0: "g3", 1: "e2", 2: "c1", 3: "f1"}, {0: "e0", 1: "e3", 2: "f0", 3: "f2"}),
    ({0: "g1", 1: "e3", 2: "e0", 3: "e3"}, {0: "e1", 1: "e1", 2: "f1", 3: "f3"}),
    ({0: "c1", 1: "f2", 3: "f2"}, {0: "g2", 1: "g3", 3: "c0"}),
    ({1: "f3", 3: "f3"}, {}),
)
HOMES = {"a": 0, "c": 2, "e": 1, "f": 3, "F": 3, "g": 0}
ATTEND_BLOCKS = ((0, 1), (2, 3))
EXPERT_BLOCKS = ((0, 1), (4, 5), (2, 3), (6, 7))


def dot_plain(left, right):
    return jnp.dot(left, right, preferred_element_type=F32)


def dot_last(left, right):
    return lax.dot_general(left, right, (((1,), (1,)), ((), ())), preferred_element_type=F32)


def dot_first(left, right):
    return lax.dot_general(left, right, (((0,), (0,)), ((), ())), preferred_element_type=F32)


def column_sum(matrix):
    return jnp.sum(matrix.astype(F32), axis=0, keepdims=True)


def norm_parts(rows):
    centre = rows - jnp.mean(rows, axis=-1, keepdims=True)
    scale = lax.rsqrt(jnp.mean(centre * centre, axis=-1, keepdims=True) + 1e-06)
    return centre * scale, scale


def norm_back(normed_grad, unit, scale, gain):
    unit_grad = normed_grad * gain
    along = jnp.mean(unit_grad * unit, axis=-1, keepdims=True)
    return scale * (unit_grad - jnp.mean(unit_grad, axis=-1, keepdims=True) - unit * along)


def true_positions(length, first, count, axis, kind):
    shape = (count, 1) if axis == 0 else (1, count)
    position = first + lax.broadcasted_iota(jnp.int32, shape, axis)
    patch = position < PATCHES
    if kind == "patch":
        return patch
    caption = (position >= PATCHES) & (position - PATCHES < length)
    return caption if kind == "caption" else patch | caption


def head_masks():
    lane = lax.broadcasted_iota(jnp.int32, (1, PAIR), 1)
    even = (lane < HEAD_DIM).astype(F32).astype(BF16)
    odd = (lane >= HEAD_DIM).astype(F32).astype(BF16)
    return lane < HEAD_DIM, even, odd


def split_pair(pair, even, odd):
    return jnp.concatenate([pair * even, pair * odd], axis=0)


def start_weights(info, first, refs, plan, blocks, sems):
    half = blocks.shape[1] // 2
    section, core, plane = info[first], info[first + 1], info[first + 2]
    for at, at_plane, steps in plan:
        here = section == at
        if at_plane is not None:
            here = here & (plane == at_plane)

        @pl.when(here)
        def _(steps=steps):
            for block, source in steps:
                if source[0] == "own":
                    _, which, row, column = source
                    width = blocks.shape[2]
                    for part in range(2):
                        pltpu.make_async_copy(
                            refs[which].at[
                                pl.ds(row + part * half, half), pl.ds(column, width)
                            ],
                            blocks.at[block, pl.ds(part * half, half)],
                            sems.at[block],
                        ).start()
                else:
                    _, mine, theirs, index = source
                    pltpu.make_async_copy(
                        refs[mine].at[index],
                        blocks.at[block, pl.ds(pl.multiple_of(core * half, half), half)],
                        sems.at[block],
                    ).start()
                    pltpu.make_async_copy(
                        refs[theirs].at[index],
                        blocks.at[block, pl.ds(pl.multiple_of((1 - core) * half, half), half)],
                        sems.at[block],
                    ).start()


def wait_block(blocks, block, sems):
    pltpu.make_async_copy(blocks.at[block], blocks.at[block], sems.at[block]).wait()


def store_turned(target, turned, columns, section, core):
    half = target.shape[0] // 2
    for piece in range(16):
        path, owner = (piece >> 2) & 1, piece & 3
        away = owner ^ section
        place = ((away & 1) << 1) | (away >> 1) if path == 0 else away
        row = ((piece >> 3) ^ core) * half + (place >> 1) * (half // 2)
        row = row + path * (half // 4) + (place & 1) * PIECE_ROWS
        target[pl.ds(pl.multiple_of(row, 16), PIECE_ROWS), columns] = turned[
            piece * PIECE_ROWS : (piece + 1) * PIECE_ROWS
        ]


def put_travel(refs, which, columns, left, right):
    half = left.shape[0] // 2
    for side in range(2):
        rows = dot_plain(left[side * half : (side + 1) * half], right).astype(BF16)
        refs[2 * side][which, :, columns] = rows[: half // 2]
        refs[2 * side + 1][which, :, columns] = rows[half // 2 :]


def attend_forward_kernel(plan, weight_count, merge, info, *refs):
    weights, refs = refs[:weight_count], refs[weight_count:]
    if merge:
        x_ref, before_ref, part_ref, outer_ref, gain_ref, shift_ref, bias_ref = refs[:7]
        y_ref, qkv_ref, mixed_ref, joined_ref, blocks, sems, joined = refs[7:]
    else:
        x_ref, gain_ref, shift_ref, bias_ref, next_gain_ref, next_shift_ref = refs[:6]
        y_ref, qkv_ref, mixed_ref, caption_ref, blocks, sems = refs[6:]
    item = pl.program_id(0)
    items = pl.num_programs(0)
    length = info[item]
    width = x_ref.shape[-1]

    @pl.when(item == 0)
    def _():
        start_weights(info, items, weights, plan, blocks, sems)

    cap = slice(CAP_FIRST, CAP_FIRST + CAP_ROWS)
    if merge:
        joined[...] = x_ref[0].astype(F32)
        branch = part_ref[0].astype(F32) + outer_ref[...]
        is_true = true_positions(length, CAP_FIRST, CAP_ROWS, 0, "caption")
        captions = before_ref[0, cap] + jnp.where(is_true, branch, 0.0)
        position = CAP_FIRST + lax.broadcasted_iota(jnp.int32, (CAP_ROWS, 1), 0)
        captions = captions.astype(BF16).astype(F32)
        joined[cap] = jnp.where(position < PATCHES, joined[cap], captions)
        x = joined[...]
        joined_ref[0] = x.astype(BF16)
    else:
        x = x_ref[0].astype(F32)
    unit, _ = norm_parts(x)
    normed = (unit * gain_ref[...] + shift_ref[...]).astype(BF16)

    @pl.when(item == 0)
    def _():
        for block in range(4):
            wait_block(blocks, block, sems)

    queries = dot_plain(normed, blocks[0]) + bias_ref[:, :width]
    qkv_ref[0, :, :width] = (queries * HEAD_DIM ** (-0.5)).astype(BF16)
    qkv_ref[0, :, width : 2 * width] = dot_plain(normed, blocks[1]).astype(BF16)
    values = dot_plain(normed, blocks[2]) + bias_ref[:, width : 2 * width]
    qkv_ref[0, :, 2 * width :] = values.astype(BF16)
    key_true = true_positions(length, 0, ROWS, 1, "all")
    low_half, even, odd = head_masks()
    ones = jnp.ones((ROWS, PAIR), BF16)

    def scores_of(pair):
        at = pair * PAIR
        q2 = qkv_ref[0, :, at : at + PAIR]
        k2 = qkv_ref[0, :, width + at : width + at + PAIR]
        return dot_last(split_pair(q2, even, odd), k2)

    ahead = [scores_of(0), scores_of(1)]
    for pair in range(HEADS // 2):
        at = pair * PAIR
        scores = jnp.where(key_true, ahead.pop(0), -1e9)
        if pair + 2 < HEADS // 2:
            ahead.append(scores_of(pair + 2))
        weight = jnp.exp(scores - jnp.max(scores, axis=-1, keepdims=True)).astype(BF16)
        v2 = qkv_ref[0, :, 2 * width + at : 2 * width + at + PAIR]
        summed = dot_plain(weight, jnp.concatenate([v2, ones], axis=1))
        top = jnp.where(low_half, summed[:ROWS, :PAIR], summed[ROWS:, :PAIR])
        below = jnp.where(low_half, summed[:ROWS, PAIR:], summed[ROWS:, PAIR:])
        mixed_ref[0, :, at : at + PAIR] = (top / below).astype(BF16)
    branch = dot_plain(mixed_ref[0], blocks[3]) + bias_ref[:, 2 * width :]
    row_true = true_positions(length, 0, ROWS, 0, "all")
    y = x + jnp.where(row_true, branch, 0.0)
    y_ref[0] = y.astype(y_ref.dtype)
    if not merge:
        unit, _ = norm_parts(y[cap])
        caption_ref[0] = (unit * next_gain_ref[...] + next_shift_ref[...]).astype(BF16)


def attend_backward_kernel(plan, weight_count, first, info, *refs):
    weights, refs = refs[:weight_count], refs[weight_count:]
    x_ref, gain_ref, shift_ref, qkv_ref, mixed_ref, grad_ref = refs[:6]
    if first:
        after_ref, next_gain_ref, *parts = refs[6:12]
        refs = refs[12:]
    else:
        refs = refs[6:]
    out_ref, gain_grad_ref, shift_grad_ref, bias_grad_ref = refs[:4]
    travel_refs = refs[4:8]
    if first:
        next_gain_grad_ref, next_shift_grad_ref, joined = refs[8], refs[9], refs[-1]
    else:
        caption_ref = refs[8]
    blocks, sems, normed_turned, mixed_turned, branch_all, projected, mixed_grad = refs[
        10 if first else 9 :
    ][:7]
    item = pl.program_id(0)
    items = pl.num_programs(0)
    length = info[item]
    section, core = info[items], info[items + 1]
    width = x_ref.shape[-1]
    here = pl.ds(pl.multiple_of(item * ROWS, ROWS), ROWS)
    cap = slice(CAP_FIRST, CAP_FIRST + CAP_ROWS)

    @pl.when(item == 0)
    def _():
        start_weights(info, items, weights, plan, blocks, sems)

    def add_to(ref, part):
        @pl.when(item == 0)
        def _():
            ref[...] = part

        @pl.when(item > 0)
        def _():
            ref[...] += part

    x = x_ref[0].astype(F32)
    unit, scale = norm_parts(x)
    normed = (unit * gain_ref[...] + shift_ref[...]).astype(BF16)
    incoming = grad_ref[0].astype(F32)
    if first:
        after_unit, after_scale = norm_parts(after_ref[0, cap])
        caption_grad = parts[0][...].astype(F32)
        for part in parts[1:]:
            caption_grad = caption_grad + part[...].astype(F32)
        joined[...] = incoming
        joined[cap] += norm_back(caption_grad, after_unit, after_scale, next_gain_ref[...])
        incoming = joined[...]
        add_to(next_gain_grad_ref, jnp.sum(caption_grad * after_unit, axis=0, keepdims=True))
        add_to(next_shift_grad_ref, jnp.sum(caption_grad, axis=0, keepdims=True))
    row_true = true_positions(length, 0, ROWS, 0, "all")
    branch = jnp.where(row_true, incoming, 0.0).astype(BF16)
    branch_all[here, :] = branch
    store_turned(normed_turned, normed.T, here, section, core)
    store_turned(mixed_turned, mixed_ref[0].T, here, section, core)

    @pl.when(item == 0)
    def _():
        for block in range(4):
            wait_block(blocks, block, sems)

    mixed_grad[...] = dot_last(branch, blocks[3]).astype(BF16)
    key_true = true_positions(length, 0, ROWS, 0, "all")
    _, even, odd = head_masks()

    def products_of(pair):
        at = pair * PAIR
        q2 = split_pair(qkv_ref[0, :, at : at + PAIR], even, odd)
        k2 = qkv_ref[0, :, width + at : width + at + PAIR]
        v2 = qkv_ref[0, :, 2 * width + at : 2 * width + at + PAIR]
        g2 = split_pair(mixed_grad[:, at : at + PAIR], even, odd)
        return q2, k2, g2, dot_last(k2, q2), dot_last(v2, g2)

    ahead = [products_of(0)]
    for pair in range(HEADS // 2):
        at = pair * PAIR
        q2, k2, g2, scores, weight_grad = ahead.pop(0)
        if pair + 1 < HEADS // 2:
            ahead.append(products_of(pair + 1))
        scores = jnp.where(key_true, scores, -1e9)
        weight = jnp.exp(scores - jnp.max(scores, axis=0, keepdims=True))
        weight = weight * (1.0 / jnp.sum(weight, axis=0, keepdims=True))
        product = weight * weight_grad
        along = jnp.sum(product, axis=0, keepdims=True)
        score_grad = (product - weight * along).astype(BF16)
        values_grad = dot_plain(weight.astype(BF16), g2).astype(BF16)
        keys_grad = dot_plain(score_grad, q2).astype(BF16)
        k2_split = split_pair(k2, even, odd)
        stacked = jnp.concatenate([score_grad[:, :ROWS], score_grad[:, ROWS:]], axis=0)
        queries_grad = dot_first(stacked, k2_split).astype(BF16)
        queries_grad = (queries_grad.astype(F32) * HEAD_DIM ** (-0.5)).astype(BF16)
        projected[here, at : at + PAIR] = queries_grad
        projected[here, width + at : width + at + PAIR] = keys_grad
        projected[here, 2 * width + at : 2 * width + at + PAIR] = values_grad
    normed_grad = dot_last(projected[here, :width], blocks[0])
    normed_grad += dot_last(projected[here, width : 2 * width], blocks[1])
    normed_grad += dot_last(projected[here, 2 * width :], blocks[2])
    out = (incoming + norm_back(normed_grad, unit, scale, gain_ref[...])).astype(BF16)
    out_ref[0] = out
    if not first:
        is_true = true_positions(length, CAP_FIRST, CAP_ROWS, 0, "caption")
        caption_ref[0] = jnp.where(is_true, out[cap].astype(F32), 0.0).astype(BF16)
    add_to(gain_grad_ref, jnp.sum(normed_grad * unit, axis=0, keepdims=True))
    add_to(shift_grad_ref, jnp.sum(normed_grad, axis=0, keepdims=True))

    @pl.when(item == items - 1)
    def _():
        for block in range(4):
            columns = slice(block * width, (block + 1) * width)
            left = normed_turned if block < 3 else mixed_turned
            right = projected[:, columns] if block < 3 else branch_all[...]
            put_travel(travel_refs, 0, columns, left, right)
        bias_grad_ref[:, :width] = column_sum(projected[:, :width])
        bias_grad_ref[:, width : 2 * width] = column_sum(projected[:, 2 * width :])
        bias_grad_ref[:, 2 * width :] = column_sum(branch_all[...])


SHORT = pl.CostEstimate(flops=0, bytes_accessed=100_000, transcendentals=0)
LONG = pl.CostEstimate(flops=30_000_000_000, bytes_accessed=30_000_000, transcendentals=0)
ANYWHERE = pl.BlockSpec(memory_space=pl.ANY)


def whole_block(shape):
    return pl.BlockSpec(shape, lambda step, info: (0,) * len(shape))


def item_block(shape):
    return pl.BlockSpec((1,) + shape[1:], lambda step, info: (step,) + (0,) * (len(shape) - 1))


def blocks_scratch(count, width):
    return [pltpu.VMEM((count, width, width), BF16), pltpu.SemaphoreType.DMA((count,))]


def attend_forward(x, info, weights, gain, shift, bias, merge=None, following=None):
    arrays, plan = weights
    items, _, width = x.shape
    row = whole_block((1, width))
    bias_row = whole_block((1, 3 * width))
    caption_shape = (items, CAP_ROWS, width)
    if merge is not None:
        before, part, outer = merge
        operands = (x, before, part, outer, gain, shift, bias)
        specs = [item_block(x.shape), item_block(x.shape), item_block(caption_shape)]
        specs += [row, row, row, bias_row]
        last_shape, kind, scratch = x.shape, BF16, [pltpu.VMEM((ROWS, width), F32)]
    else:
        operands = (x, gain, shift, bias, *following)
        specs = [item_block(x.shape), row, row, bias_row, row, row]
        last_shape, kind, scratch = caption_shape, F32, []
    return pl.pallas_call(
        partial(attend_forward_kernel, plan, len(arrays), merge is not None),
        grid_spec=pltpu.PrefetchScalarGridSpec(
            num_scalar_prefetch=1,
            grid=(items,),
            in_specs=[ANYWHERE] * len(arrays) + specs,
            out_specs=[
                item_block(x.shape),
                item_block((items, ROWS, 3 * width)),
                item_block((items, ROWS, width)),
                item_block(last_shape),
            ],
            scratch_shapes=blocks_scratch(4, width) + scratch,
        ),
        out_shape=[
            jax.ShapeDtypeStruct(x.shape, kind),
            jax.ShapeDtypeStruct((items, ROWS, 3 * width), BF16),
            jax.ShapeDtypeStruct((items, ROWS, width), BF16),
            jax.ShapeDtypeStruct(last_shape, BF16),
        ],
        compiler_params=pltpu.CompilerParams(vmem_limit_bytes=VMEM_BYTES),
        cost_estimate=SHORT,
        name="attend_forward",
    )(info, *arrays, *operands)


def attend_backward(x, info, weights, gain, shift, qkv, mixed, incoming, first=None):
    arrays, plan = weights
    items, _, width = x.shape
    half = width // 2
    row = whole_block((1, width))
    caption_shape = (items, CAP_ROWS, width)
    operands = (x, gain, shift, qkv, mixed, incoming)
    specs = [item_block(x.shape), row, row, item_block(qkv.shape), item_block(mixed.shape)]
    specs += [item_block(incoming.shape)]
    outs = [
        (item_block(x.shape), x.shape, BF16),
        (row, (1, width), F32),
        (row, (1, width), F32),
        (whole_block((1, 3 * width)), (1, 3 * width), F32),
    ]
    outs += [(whole_block((1, half // 2, 4 * width)), (1, half // 2, 4 * width), BF16)] * 4
    scratch = []
    if first is not None:
        after, next_gain, parts = first
        operands += (after, next_gain, *parts)
        caption_rows = pl.BlockSpec((CAP_ROWS, width), lambda step, info: (step, 0))
        specs += [item_block(after.shape), row] + [caption_rows] * 4
        outs += [(row, (1, width), F32)] * 2
        scratch = [pltpu.VMEM((ROWS, width), F32)]
    else:
        outs += [(item_block(caption_shape), caption_shape, BF16)]
    return pl.pallas_call(
        partial(attend_backward_kernel, plan, len(arrays), first is not None),
        grid_spec=pltpu.PrefetchScalarGridSpec(
            num_scalar_prefetch=1,
            grid=(items,),
            in_specs=[ANYWHERE] * len(arrays) + specs,
            out_specs=[spec for spec, _, _ in outs],
            scratch_shapes=blocks_scratch(4, width)
            + [
                pltpu.VMEM((width, items * ROWS), BF16),
                pltpu.VMEM((width, items * ROWS), BF16),
                pltpu.VMEM((items * ROWS, width), BF16),
                pltpu.VMEM((items * ROWS, 3 * width), BF16),
                pltpu.VMEM((ROWS, width), BF16),
            ]
            + scratch,
        ),
        out_shape=[jax.ShapeDtypeStruct(shape, kind) for _, shape, kind in outs],
        compiler_params=pltpu.CompilerParams(vmem_limit_bytes=VMEM_BYTES),
        cost_estimate=LONG,
        name="attend_backward",
    )(info, *arrays, *operands)


def normal_parts(u):
    t = pl.reciprocal(1.0 + 0.23164190 * jnp.abs(u), approx=True)
    bell = jnp.exp2((u * -0.7213475204444817) * u)
    poly = t * (
        0.127414796
        + t * (-0.142248368 + t * (0.7107068705 + t * (-0.7265760135 + t * 0.5307027145)))
    )
    tail = poly * bell
    return jnp.where(u < 0, tail, 1.0 - tail), bell


def inner_forward(normed, matrix, bias):
    inner = dot_plain(normed, matrix) + bias
    cumulative, bell = normal_parts(inner)
    slope = cumulative + (inner * 0.3989422804014327) * bell
    return (inner * cumulative).astype(BF16), slope.astype(BF16)


def expert_forward_kernel(plan, weight_count, count, kind, info, *refs):
    weights, refs = refs[:weight_count], refs[weight_count:]
    x_ref, gain_ref, shift_ref, inner_ref, outer_ref = refs[:5]
    y_ref, act_ref, slope_ref, blocks, sems, normed, total = refs[5:]
    step = pl.program_id(0)
    items, _, width = x_ref.shape

    @pl.when(step == 0)
    def _():
        start_weights(info, items, weights, plan, blocks, sems)
        for item in range(items):
            x = x_ref[item, :count].astype(BF16).astype(F32)
            unit, _ = norm_parts(x)
            normed[item * count : (item + 1) * count] = (
                unit * gain_ref[...] + shift_ref[...]
            ).astype(BF16)

    wait_block(blocks, step, sems)
    wait_block(blocks, step + 4, sems)
    for at in range(0, width, 256):
        columns = slice(at, at + 256)
        act, slope = inner_forward(normed[...], blocks[step, :, columns], inner_ref[:, columns])
        act_ref[:, columns] = act
        slope_ref[:, columns] = slope
    part = dot_plain(act_ref[...], blocks[step + 4])

    @pl.when(step == 0)
    def _():
        total[...] = part

    @pl.when(step > 0)
    def _():
        total[...] += part

    @pl.when(step == pl.num_programs(0) - 1)
    def _():
        for item in range(items):
            row_true = true_positions(info[item], 0, count, 0, kind)
            branch = total[item * count : (item + 1) * count] + outer_ref[...]
            x = x_ref[item, :count].astype(BF16).astype(F32)
            y_ref[item, :count] = (x + jnp.where(row_true, branch, 0.0)).astype(BF16)
            if count < ROWS:
                y_ref[item, count:] = jnp.zeros((ROWS - count, width), BF16)


def expert_backward_kernel(plan, weight_count, count, kind, info, *refs):
    weights, refs = refs[:weight_count], refs[weight_count:]
    x_ref, gain_ref, shift_ref, act_ref, slope_ref, grad_ref = refs[:6]
    out_ref, gain_grad_ref, shift_grad_ref, inner_grad_ref, outer_grad_ref = refs[6:11]
    travel_refs = refs[11:15]
    blocks, sems, normed_turned, branch_turned, branch, inner_all, total = refs[15:]
    step = pl.program_id(0)
    items, _, width = x_ref.shape
    section, core = info[items], info[items + 1]

    @pl.when(step == 0)
    def _():
        start_weights(info, items, weights, plan, blocks, sems)
        outer = None
        for item in range(items):
            here = slice(item * count, (item + 1) * count)
            unit, _ = norm_parts(x_ref[item, :count].astype(BF16).astype(F32))
            normed = (unit * gain_ref[...] + shift_ref[...]).astype(BF16)
            row_true = true_positions(info[item], 0, count, 0, kind)
            incoming = grad_ref[item, :count].astype(F32)
            masked = jnp.where(row_true, incoming, 0.0).astype(BF16)
            branch[here] = masked
            store_turned(normed_turned, normed.T, here, section, core)
            store_turned(branch_turned, masked.T, here, section, core)
            term = column_sum(masked)
            outer = term if outer is None else outer + term
        outer_grad_ref[...] = outer

    wait_block(blocks, step, sems)
    wait_block(blocks, step + 4, sems)
    for at in range(0, width, 256):
        columns = slice(at, at + 256)
        act_grad = dot_last(branch[...], blocks[step + 4, columns])
        inner = (slope_ref[:, columns].astype(F32) * act_grad).astype(BF16)
        inner_all[:, columns] = inner
        inner_grad_ref[:, columns] = column_sum(inner)
        put_travel(travel_refs, 0, columns, normed_turned, inner)
        put_travel(travel_refs, 1, columns, branch_turned, act_ref[:, columns])
    part = dot_last(inner_all[...], blocks[step])

    @pl.when(step == 0)
    def _():
        total[...] = part

    @pl.when(step > 0)
    def _():
        total[...] += part

    @pl.when(step == pl.num_programs(0) - 1)
    def _():
        gain_sum, shift_sum = None, None
        for item in range(items):
            unit, scale = norm_parts(x_ref[item, :count].astype(BF16).astype(F32))
            normed_grad = total[item * count : (item + 1) * count]
            gain_part = jnp.sum(normed_grad * unit, axis=0, keepdims=True)
            shift_part = jnp.sum(normed_grad, axis=0, keepdims=True)
            gain_sum = gain_part if gain_sum is None else gain_sum + gain_part
            shift_sum = shift_part if shift_sum is None else shift_sum + shift_part
            incoming = grad_ref[item, :count].astype(F32)
            hidden = incoming + norm_back(normed_grad, unit, scale, gain_ref[...])
            out_ref[item, :count] = hidden.astype(BF16)
            if count < ROWS:
                out_ref[item, count:] = grad_ref[item, count:]
        gain_grad_ref[...] = gain_sum
        shift_grad_ref[...] = shift_sum


def shared_forward_kernel(*refs):
    *rows_refs, inputs_ref, inner_ref, outputs_ref = refs[:7]
    *part_refs, normed, total = refs[7:]
    count = rows_refs[0].shape[0]
    step = pl.program_id(0)

    @pl.when(step == 0)
    def _():
        for index, ref in enumerate(rows_refs):
            normed[index * count : (index + 1) * count] = ref[...]
        total[...] = jnp.zeros_like(total)

    act, _ = inner_forward(normed[...], inputs_ref[...], inner_ref[...])
    total[...] += dot_plain(act, outputs_ref[...])

    @pl.when(step == pl.num_programs(0) - 1)
    def _():
        for index, ref in enumerate(part_refs):
            ref[...] = total[index * count : (index + 1) * count].astype(BF16)


def shared_backward_kernel(plan, weight_count, info, *refs):
    weights, refs = refs[:weight_count], refs[weight_count:]
    rows_refs, grad_refs, inner_ref = refs[:4], refs[4:8], refs[8]
    part_refs, (keep_ref, send_ref, inner_grad_ref, outer_grad_ref) = refs[9:13], refs[13:17]
    blocks, sems, normed, branch, matrix = refs[17:]
    count, width = rows_refs[0].shape
    half = width // 2
    first = info.shape[0] - 3
    core = info[first + 1]
    start_weights(info, first, weights, plan, blocks, sems)
    for index in range(SECTIONS):
        here = slice(index * count, (index + 1) * count)
        normed[here] = rows_refs[index][...]
        branch[here] = grad_refs[index][...]
    outer_grad_ref[...] = column_sum(grad_refs[0][...])
    wait_block(blocks, 0, sems)
    wait_block(blocks, 1, sems)
    part = None
    for at in range(0, width, 256):
        columns = slice(at, at + 256)
        act, slope = inner_forward(normed[...], blocks[0, :, columns], inner_ref[:, columns])
        act_grad = dot_last(branch[...], blocks[1, columns])
        inner = (slope.astype(F32) * act_grad).astype(BF16)
        inner_grad_ref[:, columns] = column_sum(inner)
        matrix[0, :, columns] = dot_first(normed[...], inner).astype(BF16)
        matrix[1, :, columns] = dot_first(branch[...], act).astype(BF16)
        term = dot_last(inner, blocks[0, :, columns])
        part = term if part is None else part + term
    for index, ref in enumerate(part_refs):
        ref[...] = part[index * count : (index + 1) * count].astype(BF16)
    quarter = half // 4
    for which in range(2):
        for group in range(4):
            columns = slice(group * width, (group + 1) * width)
            mine = pl.multiple_of(core * half, 16) + group * quarter
            other = pl.multiple_of((1 - core) * half, 16) + group * quarter
            keep_ref[which, :, columns] = matrix[which, pl.ds(pl.multiple_of(mine, 16), quarter)]
            send_ref[which, :, columns] = matrix[which, pl.ds(pl.multiple_of(other, 16), quarter)]


def chunk_columns(rows, width):
    return pl.BlockSpec((rows, width), lambda step, info: (0, step))


def expert_forward(x, info, weights, gain, shift, inner, outer, count, kind):
    arrays, plan = weights
    items, _, width = x.shape
    hidden = inner.shape[1]
    row = whole_block((1, width))
    return pl.pallas_call(
        partial(expert_forward_kernel, plan, len(arrays), count, kind),
        grid_spec=pltpu.PrefetchScalarGridSpec(
            num_scalar_prefetch=1,
            grid=(hidden // width,),
            in_specs=[ANYWHERE] * len(arrays)
            + [whole_block(x.shape), row, row, chunk_columns(1, width), row],
            out_specs=[
                whole_block((items, ROWS, width)),
                chunk_columns(items * count, width),
                chunk_columns(items * count, width),
            ],
            scratch_shapes=blocks_scratch(8, width)
            + [
                pltpu.VMEM((items * count, width), BF16),
                pltpu.VMEM((items * count, width), F32),
            ],
        ),
        out_shape=[
            jax.ShapeDtypeStruct((items, ROWS, width), BF16),
            jax.ShapeDtypeStruct((items * count, hidden), BF16),
            jax.ShapeDtypeStruct((items * count, hidden), BF16),
        ],
        compiler_params=pltpu.CompilerParams(vmem_limit_bytes=VMEM_BYTES),
        cost_estimate=SHORT,
        name="expert_forward_" + kind,
    )(info, *arrays, x, gain, shift, inner, outer)


def expert_backward(x, info, weights, gain, shift, act, slope, incoming, count, kind):
    arrays, plan = weights
    items, _, width = x.shape
    half = width // 2
    hidden = act.shape[1]
    row = whole_block((1, width))
    travel = pl.BlockSpec((2, half // 2, width), lambda step, info: (0, 0, step))
    return pl.pallas_call(
        partial(expert_backward_kernel, plan, len(arrays), count, kind),
        grid_spec=pltpu.PrefetchScalarGridSpec(
            num_scalar_prefetch=1,
            grid=(hidden // width,),
            in_specs=[ANYWHERE] * len(arrays)
            + [
                whole_block(x.shape),
                row,
                row,
                chunk_columns(items * count, width),
                chunk_columns(items * count, width),
                whole_block(incoming.shape),
            ],
            out_specs=[whole_block(incoming.shape), row, row, chunk_columns(1, width), row]
            + [travel] * 4,
            scratch_shapes=blocks_scratch(8, width)
            + [
                pltpu.VMEM((width, items * count), BF16),
                pltpu.VMEM((width, items * count), BF16),
                pltpu.VMEM((items * count, width), BF16),
                pltpu.VMEM((items * count, width), BF16),
                pltpu.VMEM((items * count, width), F32),
            ],
        ),
        out_shape=[
            jax.ShapeDtypeStruct(incoming.shape, BF16),
            jax.ShapeDtypeStruct((1, width), F32),
            jax.ShapeDtypeStruct((1, width), F32),
            jax.ShapeDtypeStruct((1, hidden), F32),
            jax.ShapeDtypeStruct((1, width), F32),
        ]
        + [jax.ShapeDtypeStruct((2, half // 2, hidden), BF16)] * 4,
        compiler_params=pltpu.CompilerParams(vmem_limit_bytes=VMEM_BYTES),
        cost_estimate=SHORT,
        name="expert_backward_" + kind,
    )(info, *arrays, x, gain, shift, act, slope, incoming)


IN_VMEM = pl.BlockSpec(memory_space=pltpu.VMEM)
IN_SMEM = pl.BlockSpec(memory_space=pltpu.SMEM)


def shared_forward(rows, inputs, inner, outputs):
    count, width = rows[0].shape
    total = SECTIONS * count
    hidden = inner.shape[1]
    return pl.pallas_call(
        shared_forward_kernel,
        grid=(hidden // width,),
        in_specs=[pl.BlockSpec(rows[0].shape, lambda step: (0, 0))] * 4
        + [
            pl.BlockSpec((width, width), lambda step: (0, step)),
            pl.BlockSpec((1, width), lambda step: (0, step)),
            pl.BlockSpec((width, width), lambda step: (step, 0)),
        ],
        out_specs=[pl.BlockSpec((count, width), lambda step: (0, 0))] * SECTIONS,
        scratch_shapes=[pltpu.VMEM((total, width), BF16), pltpu.VMEM((total, width), F32)],
        out_shape=[jax.ShapeDtypeStruct((count, width), BF16)] * SECTIONS,
        compiler_params=pltpu.CompilerParams(vmem_limit_bytes=VMEM_BYTES),
        cost_estimate=SHORT,
        name="shared_forward",
    )(*rows, inputs, inner, outputs)


def shared_backward(rows, grads, info, weights, inner):
    arrays, plan = weights
    count, width = rows[0].shape
    total = SECTIONS * count
    travel = (2, width // 8, 4 * width)
    return pl.pallas_call(
        partial(shared_backward_kernel, plan, len(arrays)),
        in_specs=[IN_SMEM] + [ANYWHERE] * len(arrays) + [IN_VMEM] * 9,
        out_specs=[IN_VMEM] * 8,
        scratch_shapes=blocks_scratch(2, width)
        + [
            pltpu.VMEM((total, width), BF16),
            pltpu.VMEM((total, width), BF16),
            pltpu.VMEM((2, width, width), BF16),
        ],
        out_shape=[
            *[jax.ShapeDtypeStruct((count, width), BF16)] * SECTIONS,
            jax.ShapeDtypeStruct(travel, BF16),
            jax.ShapeDtypeStruct(travel, BF16),
            jax.ShapeDtypeStruct((1, width), F32),
            jax.ShapeDtypeStruct((1, width), F32),
        ],
        compiler_params=pltpu.CompilerParams(vmem_limit_bytes=VMEM_BYTES),
        cost_estimate=SHORT,
        name="shared_backward",
    )(info, *arrays, *rows, *grads, inner)


def plane_turn(plane, planes):
    return ((plane & 1) << 1) | (plane >> 1) if planes == 4 else 0


def finish_kernel(planes, info, scale_ref, mine_ref, theirs_ref, *refs):
    step = pl.program_id(0)
    count = mine_ref.shape[1]
    placed = refs[-1]
    outs = refs[:-1]
    width = placed.shape[1]
    half = width // 2
    at = info.shape[0] - 3
    section, core = info[at], info[at + 1]
    turn = plane_turn(info[at + 2], planes)
    turned = turn if count == 1 else jnp.where(section == 1, turn, 0)
    scale = scale_ref[0, 0]
    columns = pl.ds(pl.multiple_of((step ^ turned) * width, width), width)

    def place(which):
        def by_rows():
            for side, ref in enumerate((mine_ref, theirs_ref)):
                for away in range(SECTIONS):
                    for path in range(2):
                        row = (core ^ side) * half + path * (half // 2)
                        row = row + (section ^ away) * PIECE_ROWS
                        placed[pl.ds(pl.multiple_of(row, 16), PIECE_ROWS), :] = ref[
                            away, which, path * PIECE_ROWS : (path + 1) * PIECE_ROWS, columns
                        ].astype(F32)

        def by_columns():
            for side, ref in enumerate((mine_ref, theirs_ref)):
                for group in range(4):
                    quarter = half // 4
                    row = (core ^ side) * half + group * quarter
                    placed[pl.ds(pl.multiple_of(row, 16), quarter), :] = ref[
                        step, which, :, group * width : (group + 1) * width
                    ].astype(F32)

        if count == 1:
            by_rows()
        else:
            pl.when(section != 0)(by_rows)
            pl.when(section == 0)(by_columns)

    place(0)
    if count == 1:

        @pl.when(step < 3)
        def _():
            outs[0][0] = placed[...] / scale

        @pl.when(step == 3)
        def _():
            outs[1][0] = placed[...] / scale

    else:
        outs[0][0] = placed[...] / scale
        place(1)
        outs[1][0] = (placed[...] / scale).T


def finish(info, scale, mine, theirs, planes):
    count, hidden = mine.shape[1], mine.shape[3]
    width = hidden // 4
    if count == 1:
        shapes = [(1, width, 3 * width), (1, width, width)]
        maps = [lambda step, info: (0, 0, jnp.minimum(step, 2)), lambda step, info: (0, 0, 0)]
    else:
        shapes = [(1, width, hidden), (1, hidden, width)]
        maps = [lambda step, info: (0, 0, step), lambda step, info: (0, step, 0)]
    return pl.pallas_call(
        partial(finish_kernel, planes),
        grid_spec=pltpu.PrefetchScalarGridSpec(
            num_scalar_prefetch=1,
            grid=(4,),
            in_specs=[IN_SMEM, whole_block(mine.shape), whole_block(mine.shape)],
            out_specs=[pl.BlockSpec((1, width, width), at) for at in maps],
            scratch_shapes=[pltpu.VMEM((width, width), F32)],
        ),
        out_shape=[jax.ShapeDtypeStruct(shape, F32) for shape in shapes],
        compiler_params=pltpu.CompilerParams(vmem_limit_bytes=VMEM_BYTES),
        cost_estimate=SHORT,
        name="finish",
    )(info, scale, mine, theirs)


def pack_kernel(count, plan, info, *refs):
    sources, outs, sems = refs[:count], refs[count:-1], refs[-1]
    first = info.shape[0] - 3
    section, core, plane = info[first], info[first + 1], info[first + 2]
    half = outs[0].shape[1]
    for index, (out, choices) in enumerate(zip(outs, plan)):
        for at, at_plane, parts in choices:
            here = section == at
            if at_plane is not None:
                here = here & (plane == at_plane)

            @pl.when(here)
            def _(index=index, out=out, parts=parts):
                for block, part in enumerate(parts):
                    if part[0] == "own":
                        _, which, row, column = part
                        rows = pl.ds(pl.multiple_of(row + core * half, half), half)
                        source = sources[which].at[rows, pl.ds(column, out.shape[2])]
                    else:
                        source = sources[part[1]].at[block]
                    pltpu.make_async_copy(source, out.at[block], sems.at[index, block]).start()

    for index, out in enumerate(outs):
        for block in range(2):
            pltpu.make_async_copy(out.at[block], out.at[block], sems.at[index, block]).wait()


def pack(info, sources, plan, shape):
    return pl.pallas_call(
        partial(pack_kernel, len(sources), plan),
        in_specs=[IN_SMEM] + [ANYWHERE] * len(sources),
        out_specs=[IN_VMEM] * len(plan),
        scratch_shapes=[pltpu.SemaphoreType.DMA((len(plan), 2))],
        out_shape=[jax.ShapeDtypeStruct(shape, BF16)] * len(plan),
        cost_estimate=SHORT,
        name="pack",
    )(info, *sources)


def over_section(value, bits, sources=range(SECTIONS)):
    return lax.ppermute(value, "section", [(at, at ^ bits) for at in sources])


def over_core(value):
    return lax.ppermute(value, "core", [(0, 1), (1, 0)])


def over_plane(value, pairs):
    return lax.ppermute(value, "z", pairs)


def added(left, right):
    return (left.astype(F32) + right.astype(F32)).astype(BF16)


def after(value, *earlier):
    return lax.optimization_barrier((value,) + earlier)[0]


def under(outputs, *arrivals):
    joined = lax.optimization_barrier(tuple(outputs) + arrivals)
    return list(joined[: len(outputs)]), list(joined[len(outputs) :])


def by_section(section, values):
    result, last = None, None
    for at in sorted(values):
        if result is None:
            result = values[at]
        elif values[at] is not last:
            result = jnp.where(section >= at, values[at], result)
        last = values[at]
    return result


def total(*values):
    result = values[0].astype(F32)
    for value in values[1:]:
        result = result + value.astype(F32)
    return result.astype(BF16)


class Sums:
    def __init__(self, travel):
        self.stay, self.move, self.other_stay, self.other_move = travel
        self.size = self.stay.shape[1] // 2

    def cross(self, *earlier):
        if earlier:
            self.other_move = after(self.other_move, *earlier)
            self.other_stay = after(self.other_stay, *earlier)
        self.got_move, self.got_stay = over_core(self.other_move), over_core(self.other_stay)

    def first_sends(self):
        size = self.size
        self.sent = [
            total(self.move[:, at : at + size], self.got_move[:, at : at + size])
            for at in (0, size)
        ]
        return self.sent

    def second_sends(self, from_x, from_y):
        size, half = self.size, self.size // 2
        self.first = from_x, from_y
        to_y = total(self.stay[:, half:size], self.got_stay[:, half:size], from_x[:, half:])
        to_x = total(
            self.stay[:, size + half :], self.got_stay[:, size + half :], from_y[:, half:]
        )
        self.sent = [to_x, to_y]
        return self.sent

    def whole(self, from_x, from_y):
        size, half = self.size, self.size // 2
        parts = []
        for at, first, second in ((0, self.first[0], from_y), (size, self.first[1], from_x)):
            here = slice(at, at + half)
            parts.append(total(self.stay[:, here], self.got_stay[:, here], first[:, :half], second))
        return jnp.concatenate(parts, axis=1)


def over_links(sends):
    return [over_section(sends[0], 1), over_section(sends[1], 2)]


class Planes:
    def __init__(self, value, plane, planes):
        self.value, self.plane, self.planes, self.turn = value, plane, planes, 0

    def sends(self, *earlier):
        value = after(self.value, *earlier) if earlier else self.value
        if self.planes != 4:
            return (value,)
        bits = (1, 2, 2, 1)[self.turn]
        if self.turn < 2:
            bit = (self.plane & 1, self.plane >> 1)[self.turn]
            size = value.shape[-1] // 2
            value = lax.dynamic_slice_in_dim(value, (1 - bit) * size, size, value.ndim - 1)
        return (over_plane(value, [(at, at ^ bits) for at in range(4)]),)

    def take(self, arrived):
        if self.planes != 4:
            self.value = lax.psum(arrived, "z") if self.turn == 3 else arrived
        elif self.turn < 2:
            bit = (self.plane & 1, self.plane >> 1)[self.turn]
            size = self.value.shape[-1] // 2
            keep = lax.dynamic_slice_in_dim(self.value, bit * size, size, self.value.ndim - 1)
            self.value = added(keep, arrived)
        else:
            self.value = jnp.concatenate([self.value, arrived], axis=-1)
        self.turn += 1

    def in_order(self, value):
        if self.planes != 4:
            return value
        size, turn = value.shape[-1] // 4, plane_turn(self.plane, 4)
        parts = [
            lax.dynamic_slice_in_dim(value, (at ^ turn) * size, size, value.ndim - 1)
            for at in range(4)
        ]
        return jnp.concatenate(parts, axis=-1)


class Weights:
    def __init__(self, own, info, planes):
        self.own, self.info = own, info
        self.four = planes == 4
        self.plan = PLAN_FOUR if self.four else PLAN_ANY
        self.half, self.width = own[1].shape[0] // 2, own[1].shape[1]
        self.mine, self.theirs, self.arrived = {}, {}, {}

    def place(self, layer, block):
        if layer in "ac":
            return (0, 0, block * self.width) if block < 3 else (1, 0, 0)
        if layer == "g":
            return (2, 0, block * self.width) if block < 4 else (3, (block - 4) * self.width, 0)
        return (2, 0, block * self.width) if block < 4 else (3, (block - 4) * self.width, 0)

    def choices(self, sends, sources):
        result = []
        for at in range(SECTIONS):
            name = sends.get(at)
            if name is not None and HOMES[name[0]] != at:
                key = self.arrived[at, name]
                if key not in sources:
                    sources[key] = len(self.own) + len(sources)
                result.append((at, None, [("arrived", sources[key])] * 2))
                continue
            for plane in range(4) if name == "F" else (None,):
                piece = ("f" + str(plane)) if name == "F" else name or "a0"
                layer, index = piece[0], int(piece[1])
                if layer in "ac":
                    blocks = ATTEND_BLOCKS[index]
                else:
                    blocks = (index, 4 + index) if layer == "g" else EXPERT_BLOCKS[index]
                parts = [("own",) + self.place(layer, block) for block in blocks]
                result.append((at, plane, parts))
        return result

    def packed(self, wanted):
        sources = {}
        plan = [self.choices(sends, sources) for sends in wanted]
        arrays = list(self.own) + [self.mine[key] for key in sources]
        return pack(self.info, arrays, plan, (2, self.half, self.width))

    def sends(self, step):
        if step == "F":
            return [{at: "F" for at in range(SECTIONS)}]
        return [sends for sends in self.plan[step] if sends]

    def payloads(self, *steps):
        wanted = [sends for step in steps for sends in self.sends(step)]
        return list(self.packed(wanted))

    def move(self, step, payloads):
        links = [(link, sends) for link, sends in enumerate(self.plan[step]) if sends]
        for (link, sends), payload in zip(links, payloads):
            self.mine[step, link] = over_section(payload, link + 1, sorted(sends))
            for at, name in sends.items():
                self.arrived[at ^ (link + 1), name] = (step, link)
        return [(step, link) for link, _ in links]

    def move_planes(self, step):
        up, down = self.mine["plane", step - 1], self.mine["plane", 1 - step]
        up = over_plane(up, [(at, at + 1) for at in range(step - 1, 3)])
        down = over_plane(down, [(at, at - 1) for at in range(4 - step, 0, -1)])
        self.mine["plane", step], self.mine["plane", -step] = up, down
        return [("plane", step), ("plane", -step)]

    def cross(self, keys):
        for key in keys:
            self.theirs[key] = over_core(self.mine[key])
        return keys

    def join(self, outputs, mine=(), theirs=()):
        values = [self.mine[key] for key in mine] + [self.theirs[key] for key in theirs]
        outputs, values = under(outputs, *values)
        for key, value in zip(mine, values):
            self.mine[key] = value
        for key, value in zip(theirs, values[len(mine) :]):
            self.theirs[key] = value
        return outputs

    def layer(self, layer):
        arrays, places = list(self.own), {}

        def place(key):
            if key not in places:
                places[key] = len(arrays)
                arrays.extend([self.mine[key], self.theirs[key]])
            return places[key], places[key] + 1

        if layer in "ac":
            names = [(layer + str(index), ATTEND_BLOCKS[index]) for index in range(2)]
        else:
            names = [(layer + str(index), EXPERT_BLOCKS[index]) for index in range(4)]
        plan = []
        for at in range(SECTIONS):
            if layer == "g":
                names = [("g" + str(at), (0, 1))]
            if HOMES[layer] == at:
                steps = []
                for name, blocks in names:
                    for block in blocks:
                        source = block * 4 if layer == "g" else block
                        steps.append((block, ("own",) + self.place(layer, source)))
                plan.append((at, None, steps))
                continue
            by_plane = layer == "f" and self.four
            for plane in range(4) if by_plane else (None,):
                steps = []
                for index, (name, blocks) in enumerate(names):
                    key = ("plane", plane - index) if by_plane else self.arrived[at, name]
                    for which, block in enumerate(blocks):
                        steps.append((block, ("piece",) + place(key) + (which,)))
                plan.append((at, plane, steps))
        return arrays, plan


def per_device(
    tokens,
    caption_lengths,
    attend_gain,
    attend_shift,
    attend_inputs,
    attend_bias,
    attend_output,
    expert_gain,
    expert_shift,
    expert_inputs,
    expert_inner_bias,
    expert_outputs,
    expert_outer_bias,
    cotangent,
):
    section, core, plane = lax.axis_index("section"), lax.axis_index("core"), lax.axis_index("z")
    planes = lax.axis_size("z")
    items, positions, width = tokens.shape
    hidden = expert_inputs.shape[-1]
    info = [value.reshape(1).astype(jnp.int32) for value in (section, core, plane)]
    info = jnp.concatenate([caption_lengths] + info)
    weights = Weights(
        (attend_inputs[0], attend_output[0], expert_inputs[0], expert_outputs[0]), info, planes
    )

    def to_sections(value):
        return [value] + [over_section(value, bits) for bits in (1, 2, 3)]

    def items_of(part):
        return part.reshape(items, CAP_ROWS, width)

    pad = ((0, 0), (0, ROWS - positions), (0, 0))
    x0 = jnp.pad(tokens, pad)
    last_grad = jnp.pad(cotangent, pad)
    rows = jnp.concatenate(
        [
            attend_gain,
            attend_shift,
            attend_bias,
            expert_gain,
            expert_shift,
            expert_inner_bias,
            expert_outer_bias,
            jnp.full((1, 128), jnp.sum(caption_lengths), F32),
        ],
        axis=1,
    )
    rows = to_sections(rows)
    keys = weights.move(0, weights.payloads(0))
    x0, last_grad, *rows = weights.join([x0, last_grad, *rows], keys)
    keys1 = weights.move(1, weights.payloads(1))
    rows = jnp.concatenate(rows, axis=0)
    language_count = jnp.sum(rows[:, -128:], axis=0, keepdims=True)
    rows = [lax.dynamic_index_in_dim(rows, at ^ section, 0) for at in range(SECTIONS)]
    sizes = [width, width, 3 * width, width, width, hidden, width]
    ends = [sum(sizes[: at + 1]) for at in range(len(sizes))]
    used = [(0, 0), (0, 1), (0, 2), (0, 3), (0, 4), (0, 5), (1, 3), (1, 4), (1, 5), (1, 6)]
    used += [(0, 6), (2, 0), (2, 1), (2, 2), (3, 3), (3, 4), (3, 5), (3, 6)]
    kept = [rows[slot][:, ends[which] - sizes[which] : ends[which]] for slot, which in used]
    language_count, *kept = weights.join([language_count, *kept], keys1)
    kept = dict(zip(used, kept))

    def row(slot, which):
        return kept[slot, which]

    crossed = weights.cross(keys + keys1)
    sends = weights.payloads(2, "F") if weights.four else weights.payloads(2)
    sends, (info, language_count) = under(sends, info, language_count)
    keys = weights.move(2, sends[:2])
    info, language_count = weights.join(
        [info, language_count + over_core(language_count)], theirs=crossed
    )
    plane_keys = []
    if weights.four:
        weights.mine["plane", 0] = sends[2]
        plane_keys = weights.move_planes(1)
    attend0 = weights.layer("a")
    outputs = attend_forward(
        x0, info, attend0, row(0, 0), row(0, 1), row(0, 2), following=(row(0, 3), row(0, 4))
    )
    y0, qkv0, mixed0, caption_rows = weights.join(outputs, keys)
    caption_rows = to_sections(caption_rows.reshape(-1, width))
    sends, caption_rows = under(weights.payloads(3), *weights.join(caption_rows, plane_keys))
    early_keys = keys
    keys = weights.move(3, sends)
    crossed = weights.cross(early_keys)
    plane_keys = weights.move_planes(2) if weights.four else []
    outputs = shared_forward(caption_rows, expert_inputs[0], expert_inner_bias, expert_outputs[0])
    part = weights.join(outputs, keys, crossed)
    (y0,) = weights.join([y0], plane_keys, weights.cross(keys))
    branch = {at: over_section(part[at], at, [0]) for at in range(1, SECTIONS)}
    keys = weights.move_planes(3) if weights.four else []
    expert1 = weights.layer("e")
    outputs = expert_forward(
        y0, info, expert1, row(1, 3), row(1, 4), row(1, 5), row(1, 6), PATCH_ROWS, "patch"
    )
    outputs, moved = under(outputs, *branch.values())
    if weights.four:
        keys += [("plane", step) for step in range(-2, 3)]
    x2, act1, slope1 = weights.join(outputs, keys)
    branch = dict(zip(branch, moved))
    branch[0] = part[0]
    branch = items_of(by_section(section, branch))
    if weights.four:
        crossed = [("plane", step) for step in range(-3, 4)]
    else:
        for step in (4, 5):
            weights.move(step, weights.payloads(step))
        crossed = [(4, 0), (4, 1), (5, 0)]
    weights.cross(crossed)
    attend2 = weights.layer("c") if weights.four else None
    if not weights.four:
        (x2,) = weights.join([x2], theirs=crossed)
        attend2 = weights.layer("c")
    outputs = attend_forward(
        x2, info, attend2, row(2, 0), row(2, 1), row(2, 2), merge=(y0, branch, row(0, 6))
    )
    if weights.four:
        language_count += over_plane(language_count, [(at, at ^ 1) for at in range(4)])
    x3, qkv2, mixed2, x2, language_count = weights.join([*outputs, language_count], theirs=crossed)
    if weights.four:
        language_count += over_plane(language_count, [(at, at ^ 2) for at in range(4)])
    else:
        language_count = lax.psum(language_count, "z")
    expert3 = weights.layer("f")
    outputs = expert_forward(
        x3, info, expert3, row(3, 3), row(3, 4), row(3, 5), row(3, 6), ROWS, "all"
    )
    layer_output, act3, slope3, language_count = under([*outputs, language_count])[0]
    language_count = language_count[0, 0].astype(jnp.int32)
    vision_count = PATCHES * items * SECTIONS * 2 * planes
    counts = jnp.stack(
        [jnp.full((), vision_count, jnp.int32), language_count, language_count + vision_count]
    )

    def small_rows(values):
        flat = jnp.concatenate(values, axis=1)
        count = -(-flat.shape[1] // hidden)
        flat = jnp.pad(flat, ((0, 0), (0, count * hidden - flat.shape[1])))
        return flat.reshape(count, hidden)

    def to_home(sums):
        got = [by_section(section, sums)]
        for bits in (1, 2, 3):
            sends = {at ^ bits: sums[at] for at in sums}
            got.append(over_section(by_section(section, sends), bits, sorted(sends)))
        return got

    keys = []
    if weights.four:
        sends, (layer_output, last_grad) = under(weights.payloads(4), layer_output, last_grad)
        keys = weights.move(4, sends)
    outputs = expert_backward(
        x3, info, expert3, row(3, 3), row(3, 4), act3, slope3, last_grad, ROWS, "all"
    )
    outputs = weights.join(outputs, keys)
    crossed = weights.cross(keys)
    grad3, *small3 = outputs[:5]
    sums3 = Sums(outputs[5:])
    sums3.cross()
    moved = over_links(sums3.first_sends())
    grad3 = after(grad3, *sums3.sent)
    outputs = attend_backward(
        x2, info, attend2, row(2, 0), row(2, 1), qkv2, mixed2, grad3
    )
    outputs, moved = under(outputs, *moved, sums3.got_stay)
    outputs = weights.join(outputs, theirs=crossed)
    grad2, *small2 = outputs[:4]
    sums2, caption_grad = Sums(outputs[4:8]), outputs[8]
    caption_grads = to_sections(caption_grad.reshape(-1, width))
    sums3.got_stay = moved[2]
    moved3 = over_links(sums3.second_sends(*moved[:2]))
    grad2 = after(grad2, *sums3.sent)
    outputs = expert_backward(
        y0, info, expert1, row(1, 3), row(1, 4), act1, slope1, grad2, PATCH_ROWS, "patch"
    )
    outputs, caption_grads = under(outputs, *caption_grads)
    grad1, *small1 = outputs[:5]
    sums2.cross(grad1)
    sums1 = Sums(outputs[5:])
    sums1.cross()
    inner_quarter = lax.dynamic_slice(row(0, 5), (0, section * width), (1, width))
    sum3 = sums3.whole(*moved3)
    inner_quarter = after(inner_quarter, grad1, sum3)
    outputs = shared_backward(
        caption_rows, caption_grads, info, weights.layer("g"), inner_quarter
    )
    parts, (keep0, send0, inner_grad, outer_grad) = outputs[:4], outputs[4:]
    got = [over_section(parts[bits], bits) for bits in (1, 2, 3)]
    sends = [after(value, *parts) for value in sums1.first_sends()]
    moved1 = over_links(sends)
    keep0 = added(keep0, over_core(send0))
    early = lax.psum(jnp.concatenate([sum3, keep0], axis=0), "z")
    sends2 = [after(value, *sends) for value in sums2.first_sends()]
    moved2 = over_links(sends2)
    parts = [parts[0], *got]
    grad1 = after(grad1, keep0, *sends, *sends2)
    outputs = attend_backward(
        x0,
        info,
        attend0,
        row(0, 0),
        row(0, 1),
        qkv0,
        mixed0,
        grad1,
        first=(y0, row(0, 3), parts),
    )
    outputs, moved = under(outputs, *moved2, *moved1)
    moved2, moved1 = moved[:2], moved[2:]
    tokens_grad, *small_first = outputs[:4]
    sums_first, gain_grad, shift_grad = Sums(outputs[4:8]), outputs[8], outputs[9]
    sums_first.cross()
    inner_grad = lax.dynamic_update_slice(
        jnp.zeros((1, hidden), F32), inner_grad, (0, section * width)
    )
    small = small_rows(
        small_first + [gain_grad, shift_grad, inner_grad, outer_grad] + small2 + small1 + small3
    )
    small = added(small, over_core(small))
    to_x, to_y = sums_first.first_sends()
    to_x = jnp.concatenate([to_x[0], small], axis=0)
    sends = lax.optimization_barrier((*sums1.second_sends(*moved1), to_x, to_y))
    moved1, moved = over_links(sends[:2]), over_links(sends[2:])
    planes1 = Planes(sums1.whole(*moved1), plane, planes)
    sent1 = planes1.sends()
    size = to_y.shape[1]
    small = added(small, moved[0][size:])
    to_x, to_y = sums_first.second_sends(moved[0][None, :size], moved[1])
    early_x, early_y = sums2.second_sends(*moved2)
    to_x = jnp.concatenate([to_x[0], early_x[0]], axis=0)
    to_y = jnp.concatenate([to_y[0], early_y[0], small], axis=0)
    to_x, to_y, early = lax.optimization_barrier((to_x, to_y, early))
    moved = lax.optimization_barrier(tuple(over_links((to_x, to_y))))
    size = early_x.shape[1]
    last = sums_first.whole(moved[0][None, :size], moved[1][None, :size])
    sum2 = sums2.whole(moved[0][None, size:], moved[1][None, size : 2 * size])
    small = added(small, moved[1][2 * size :])
    small_count = small.shape[0]
    eighth = last.shape[1]
    last = jnp.concatenate([last[0], sum2[0], small], axis=0)
    home_early = to_home({0: early[2:], 3: early[:2]})
    planes_last = Planes(last, plane, planes)
    planes1.take(*sent1)

    def turn_both(*earlier):
        sends = [*planes1.sends(*earlier), *planes_last.sends(*earlier)]
        sends = lax.optimization_barrier(tuple(sends))
        planes1.take(sends[0])
        planes_last.take(sends[1])

    turn_both()
    turn_both()
    turn_both(*home_early[1:])
    last, sum1 = lax.optimization_barrier((planes_last.value, planes1.value))
    home_late = to_home({1: sum1})
    planes_last.take(*planes_last.sends())
    last = planes_last.value
    home_attend = to_home({0: last[None, :eighth], 2: last[None, eighth : 2 * eighth]})
    small = planes_last.in_order(last[2 * eighth :].astype(F32))

    as_float = counts.astype(F32)
    one = jnp.ones((), F32)
    attend_scales = jnp.stack([as_float[2], one, as_float[2], one])
    expert_scales = jnp.stack([as_float[1], as_float[0], one, as_float[2]])

    def placed(pieces, scales):
        scale = lax.dynamic_index_in_dim(scales, section, 0).reshape(1, 1)
        pieces = jnp.stack(pieces)
        return finish(info, scale, pieces, over_core(pieces), planes)

    blank = jnp.zeros_like(home_late[0])
    inputs_whole, outputs_whole = placed(
        [
            by_section(section, {0: early, 1: late, 2: blank, 3: early})
            for early, late in zip(home_early, home_late)
        ],
        expert_scales,
    )
    blank = jnp.zeros_like(home_attend[0])
    attend_whole, output_whole = placed(
        [by_section(section, {0: got, 1: blank, 2: got, 3: blank}) for got in home_attend],
        attend_scales,
    )

    attend_size, expert_size = 5 * width, 3 * width + hidden
    cuts = [attend_size, attend_size + expert_size]
    cuts += [cuts[1] + attend_size, cuts[1] + attend_size + expert_size]
    small = jnp.split(small.reshape(-1)[: cuts[3] + expert_size], cuts)
    none_attend, none_expert = jnp.zeros_like(small[0]), jnp.zeros_like(small[1])
    attend_small = jnp.stack([small[0], none_attend, small[2], none_attend])
    expert_small = jnp.stack([small[1], small[3], none_expert, small[4]])
    attend_small = attend_small / attend_scales.reshape(-1, 1)
    expert_small = expert_small / expert_scales.reshape(-1, 1)
    attend_small = lax.dynamic_index_in_dim(attend_small, section, 0)
    expert_small = lax.dynamic_index_in_dim(expert_small, section, 0)
    return (
        layer_output[:, :positions],
        tokens_grad[:, :positions],
        attend_small[:, :width],
        attend_small[:, width : 2 * width],
        attend_whole,
        attend_small[:, 2 * width :],
        output_whole,
        expert_small[:, :width],
        expert_small[:, width : 2 * width],
        inputs_whole,
        expert_small[:, 2 * width : 2 * width + hidden],
        outputs_whole,
        expert_small[:, 2 * width + hidden :],
        counts,
    )


def solution(mesh):
    sections, groups = mesh.shape["section"], mesh.shape["dp"]
    split = Mesh(mesh.devices.reshape(sections, groups // 2, 2), ("section", "z", "core"))
    items = P(("section", "z", "core"), None, None)
    flat = P("section", None)
    matrix = P("section", None, None)
    placed = (
        items,
        P(("section", "z", "core")),
        flat,
        flat,
        matrix,
        flat,
        matrix,
        flat,
        flat,
        matrix,
        flat,
        matrix,
        flat,
        items,
    )
    return jax.shard_map(
        per_device,
        mesh=split,
        in_specs=placed,
        out_specs=(
            items,
            items,
            flat,
            flat,
            matrix,
            flat,
            matrix,
            flat,
            flat,
            matrix,
            flat,
            matrix,
            flat,
            P(),
        ),
        check_vma=False,
    )
```

```python
from functools import partial

import jax
import jax.numpy as jnp
from jax import lax
from jax.experimental import pallas as pl
from jax.experimental.pallas import tpu as pltpu
from jax.sharding import Mesh
from jax.sharding import PartitionSpec as P

HEADS = 12
HEAD_DIM = 64
PATCHES = 197
ROWS = 256
CAP_FIRST, CAP_ROWS = 192, 48
PATCH_ROWS = 208
PAIR = 2 * HEAD_DIM
SECTIONS = 4
PIECE_ROWS = 48
VMEM_BYTES = 58 * 1024 * 1024
F32 = jnp.float32
BF16 = jnp.bfloat16

PLAN_FOUR = (
    ({0: "a0", 1: "e0", 2: "c0", 3: "F"}, {0: "a1", 1: "e2", 2: "c0", 3: "F"}),
    ({0: "a1", 1: "e1", 2: "a1", 3: "e2"}, {0: "a0", 1: "a0", 2: "F", 3: "c0"}),
    ({0: "g3", 1: "e2", 2: "c1"}, {0: "e0", 1: "e3", 2: "c1"}),
    ({0: "g1", 1: "e3", 2: "e0", 3: "e3"}, {0: "e1", 1: "e1", 3: "c1"}),
    ({}, {0: "g2", 1: "g3"}),
)
PLAN_ANY = (
    ({0: "a0", 1: "e0", 2: "c0", 3: "f0"}, {0: "a1", 1: "e2", 2: "c0", 3: "f0"}),
    ({0: "a1", 1: "e1", 2: "a1", 3: "e2"}, {0: "a0", 1: "a0", 2: "c1", 3: "f1"}),
    ({0: "g3", 1: "e2", 2: "c1", 3: "f1"}, {0: "e0", 1: "e3", 2: "f0", 3: "f2"}),
    ({0: "g1", 1: "e3", 2: "e0", 3: "e3"}, {0: "e1", 1: "e1", 2: "f1", 3: "f3"}),
    ({0: "c1", 1: "f2", 3: "f2"}, {0: "g2", 1: "g3", 3: "c0"}),
    ({1: "f3", 3: "f3"}, {}),
)
HOMES = {"a": 0, "c": 2, "e": 1, "f": 3, "F": 3, "g": 0}
ATTEND_BLOCKS = ((0, 1), (2, 3))
EXPERT_BLOCKS = ((0, 1), (4, 5), (2, 3), (6, 7))


def dot_plain(left, right):
    return jnp.dot(left, right, preferred_element_type=F32)


def dot_last(left, right):
    return lax.dot_general(left, right, (((1,), (1,)), ((), ())), preferred_element_type=F32)


def dot_first(left, right):
    return lax.dot_general(left, right, (((0,), (0,)), ((), ())), preferred_element_type=F32)


def column_sum(matrix):
    return jnp.sum(matrix.astype(F32), axis=0, keepdims=True)


def norm_parts(rows):
    centre = rows - jnp.mean(rows, axis=-1, keepdims=True)
    scale = lax.rsqrt(jnp.mean(centre * centre, axis=-1, keepdims=True) + 1e-06)
    return centre * scale, scale


def norm_back(normed_grad, unit, scale, gain):
    unit_grad = normed_grad * gain
    along = jnp.mean(unit_grad * unit, axis=-1, keepdims=True)
    return scale * (unit_grad - jnp.mean(unit_grad, axis=-1, keepdims=True) - unit * along)


def true_positions(length, first, count, axis, kind):
    shape = (count, 1) if axis == 0 else (1, count)
    position = first + lax.broadcasted_iota(jnp.int32, shape, axis)
    patch = position < PATCHES
    if kind == "patch":
        return patch
    caption = (position >= PATCHES) & (position - PATCHES < length)
    return caption if kind == "caption" else patch | caption


def head_masks():
    lane = lax.broadcasted_iota(jnp.int32, (1, PAIR), 1)
    even = (lane < HEAD_DIM).astype(F32).astype(BF16)
    odd = (lane >= HEAD_DIM).astype(F32).astype(BF16)
    return lane < HEAD_DIM, even, odd


def split_pair(pair, even, odd):
    return jnp.concatenate([pair * even, pair * odd], axis=0)


def start_weights(info, first, refs, plan, blocks, sems):
    half = blocks.shape[1] // 2
    section, core, plane = info[first], info[first + 1], info[first + 2]
    for at, at_plane, steps in plan:
        here = section == at
        if at_plane is not None:
            here = here & (plane == at_plane)

        @pl.when(here)
        def _(steps=steps):
            for block, source in steps:
                if source[0] == "own":
                    _, which, row, column = source
                    width = blocks.shape[2]
                    for part in range(2):
                        pltpu.make_async_copy(
                            refs[which].at[
                                pl.ds(row + part * half, half), pl.ds(column, width)
                            ],
                            blocks.at[block, pl.ds(part * half, half)],
                            sems.at[block],
                        ).start()
                else:
                    _, mine, theirs, index = source
                    pltpu.make_async_copy(
                        refs[mine].at[index],
                        blocks.at[block, pl.ds(pl.multiple_of(core * half, half), half)],
                        sems.at[block],
                    ).start()
                    pltpu.make_async_copy(
                        refs[theirs].at[index],
                        blocks.at[block, pl.ds(pl.multiple_of((1 - core) * half, half), half)],
                        sems.at[block],
                    ).start()


def wait_block(blocks, block, sems):
    pltpu.make_async_copy(blocks.at[block], blocks.at[block], sems.at[block]).wait()


def store_turned(target, turned, columns, section, core):
    half = target.shape[0] // 2
    for piece in range(16):
        path, owner = (piece >> 2) & 1, piece & 3
        away = owner ^ section
        place = ((away & 1) << 1) | (away >> 1) if path == 0 else away
        row = ((piece >> 3) ^ core) * half + (place >> 1) * (half // 2)
        row = row + path * (half // 4) + (place & 1) * PIECE_ROWS
        target[pl.ds(pl.multiple_of(row, 16), PIECE_ROWS), columns] = turned[
            piece * PIECE_ROWS : (piece + 1) * PIECE_ROWS
        ]


def put_travel(refs, which, columns, left, right):
    half = left.shape[0] // 2
    for side in range(2):
        rows = dot_plain(left[side * half : (side + 1) * half], right).astype(BF16)
        refs[2 * side][which, :, columns] = rows[: half // 2]
        refs[2 * side + 1][which, :, columns] = rows[half // 2 :]


def attend_forward_kernel(plan, weight_count, merge, info, *refs):
    weights, refs = refs[:weight_count], refs[weight_count:]
    if merge:
        x_ref, before_ref, part_ref, outer_ref, gain_ref, shift_ref, bias_ref = refs[:7]
        y_ref, qkv_ref, mixed_ref, joined_ref, blocks, sems, joined = refs[7:]
    else:
        x_ref, gain_ref, shift_ref, bias_ref, next_gain_ref, next_shift_ref = refs[:6]
        y_ref, qkv_ref, mixed_ref, caption_ref, blocks, sems = refs[6:]
    item = pl.program_id(0)
    items = pl.num_programs(0)
    length = info[item]
    width = x_ref.shape[-1]

    @pl.when(item == 0)
    def _():
        start_weights(info, items, weights, plan, blocks, sems)

    cap = slice(CAP_FIRST, CAP_FIRST + CAP_ROWS)
    if merge:
        joined[...] = x_ref[0].astype(F32)
        branch = part_ref[0].astype(F32) + outer_ref[...]
        is_true = true_positions(length, CAP_FIRST, CAP_ROWS, 0, "caption")
        captions = before_ref[0, cap] + jnp.where(is_true, branch, 0.0)
        position = CAP_FIRST + lax.broadcasted_iota(jnp.int32, (CAP_ROWS, 1), 0)
        captions = captions.astype(BF16).astype(F32)
        joined[cap] = jnp.where(position < PATCHES, joined[cap], captions)
        x = joined[...]
        joined_ref[0] = x.astype(BF16)
    else:
        x = x_ref[0].astype(F32)
    unit, _ = norm_parts(x)
    normed = (unit * gain_ref[...] + shift_ref[...]).astype(BF16)

    @pl.when(item == 0)
    def _():
        for block in range(4):
            wait_block(blocks, block, sems)

    queries = dot_plain(normed, blocks[0]) + bias_ref[:, :width]
    qkv_ref[0, :, :width] = (queries * HEAD_DIM ** (-0.5)).astype(BF16)
    qkv_ref[0, :, width : 2 * width] = dot_plain(normed, blocks[1]).astype(BF16)
    values = dot_plain(normed, blocks[2]) + bias_ref[:, width : 2 * width]
    qkv_ref[0, :, 2 * width :] = values.astype(BF16)
    key_true = true_positions(length, 0, ROWS, 1, "all")
    low_half, even, odd = head_masks()
    ones = jnp.ones((ROWS, PAIR), BF16)

    def scores_of(pair):
        at = pair * PAIR
        q2 = qkv_ref[0, :, at : at + PAIR]
        k2 = qkv_ref[0, :, width + at : width + at + PAIR]
        return dot_last(split_pair(q2, even, odd), k2)

    ahead = [scores_of(0), scores_of(1)]
    for pair in range(HEADS // 2):
        at = pair * PAIR
        scores = jnp.where(key_true, ahead.pop(0), -1e9)
        if pair + 2 < HEADS // 2:
            ahead.append(scores_of(pair + 2))
        weight = jnp.exp(scores - jnp.max(scores, axis=-1, keepdims=True)).astype(BF16)
        v2 = qkv_ref[0, :, 2 * width + at : 2 * width + at + PAIR]
        summed = dot_plain(weight, jnp.concatenate([v2, ones], axis=1))
        top = jnp.where(low_half, summed[:ROWS, :PAIR], summed[ROWS:, :PAIR])
        below = jnp.where(low_half, summed[:ROWS, PAIR:], summed[ROWS:, PAIR:])
        mixed_ref[0, :, at : at + PAIR] = (top / below).astype(BF16)
    branch = dot_plain(mixed_ref[0], blocks[3]) + bias_ref[:, 2 * width :]
    row_true = true_positions(length, 0, ROWS, 0, "all")
    y = x + jnp.where(row_true, branch, 0.0)
    y_ref[0] = y.astype(y_ref.dtype)
    if not merge:
        unit, _ = norm_parts(y[cap])
        caption_ref[0] = (unit * next_gain_ref[...] + next_shift_ref[...]).astype(BF16)


def attend_backward_kernel(plan, weight_count, first, info, *refs):
    weights, refs = refs[:weight_count], refs[weight_count:]
    x_ref, gain_ref, shift_ref, qkv_ref, mixed_ref, grad_ref = refs[:6]
    if first:
        after_ref, next_gain_ref, *parts = refs[6:12]
        refs = refs[12:]
    else:
        refs = refs[6:]
    out_ref, gain_grad_ref, shift_grad_ref, bias_grad_ref = refs[:4]
    travel_refs = refs[4:8]
    if first:
        next_gain_grad_ref, next_shift_grad_ref, joined = refs[8], refs[9], refs[-1]
    else:
        caption_ref = refs[8]
    blocks, sems, normed_turned, mixed_turned, branch_all, projected, mixed_grad = refs[
        10 if first else 9 :
    ][:7]
    item = pl.program_id(0)
    items = pl.num_programs(0)
    length = info[item]
    section, core = info[items], info[items + 1]
    width = x_ref.shape[-1]
    here = pl.ds(pl.multiple_of(item * ROWS, ROWS), ROWS)
    cap = slice(CAP_FIRST, CAP_FIRST + CAP_ROWS)

    @pl.when(item == 0)
    def _():
        start_weights(info, items, weights, plan, blocks, sems)

    def add_to(ref, part):
        @pl.when(item == 0)
        def _():
            ref[...] = part

        @pl.when(item > 0)
        def _():
            ref[...] += part

    x = x_ref[0].astype(F32)
    unit, scale = norm_parts(x)
    normed = (unit * gain_ref[...] + shift_ref[...]).astype(BF16)
    incoming = grad_ref[0].astype(F32)
    if first:
        after_unit, after_scale = norm_parts(after_ref[0, cap])
        caption_grad = parts[0][...].astype(F32)
        for part in parts[1:]:
            caption_grad = caption_grad + part[...].astype(F32)
        joined[...] = incoming
        joined[cap] += norm_back(caption_grad, after_unit, after_scale, next_gain_ref[...])
        incoming = joined[...]
        add_to(next_gain_grad_ref, jnp.sum(caption_grad * after_unit, axis=0, keepdims=True))
        add_to(next_shift_grad_ref, jnp.sum(caption_grad, axis=0, keepdims=True))
    row_true = true_positions(length, 0, ROWS, 0, "all")
    branch = jnp.where(row_true, incoming, 0.0).astype(BF16)
    branch_all[here, :] = branch
    store_turned(normed_turned, normed.T, here, section, core)
    store_turned(mixed_turned, mixed_ref[0].T, here, section, core)

    @pl.when(item == 0)
    def _():
        for block in range(4):
            wait_block(blocks, block, sems)

    mixed_grad[...] = dot_last(branch, blocks[3]).astype(BF16)
    key_true = true_positions(length, 0, ROWS, 0, "all")
    _, even, odd = head_masks()

    def products_of(pair):
        at = pair * PAIR
        q2 = split_pair(qkv_ref[0, :, at : at + PAIR], even, odd)
        k2 = qkv_ref[0, :, width + at : width + at + PAIR]
        v2 = qkv_ref[0, :, 2 * width + at : 2 * width + at + PAIR]
        g2 = split_pair(mixed_grad[:, at : at + PAIR], even, odd)
        return q2, k2, g2, dot_last(k2, q2), dot_last(v2, g2)

    ahead = [products_of(0)]
    for pair in range(HEADS // 2):
        at = pair * PAIR
        q2, k2, g2, scores, weight_grad = ahead.pop(0)
        if pair + 1 < HEADS // 2:
            ahead.append(products_of(pair + 1))
        scores = jnp.where(key_true, scores, -1e9)
        weight = jnp.exp(scores - jnp.max(scores, axis=0, keepdims=True))
        weight = weight * (1.0 / jnp.sum(weight, axis=0, keepdims=True))
        product = weight * weight_grad
        along = jnp.sum(product, axis=0, keepdims=True)
        score_grad = (product - weight * along).astype(BF16)
        values_grad = dot_plain(weight.astype(BF16), g2).astype(BF16)
        keys_grad = dot_plain(score_grad, q2).astype(BF16)
        k2_split = split_pair(k2, even, odd)
        stacked = jnp.concatenate([score_grad[:, :ROWS], score_grad[:, ROWS:]], axis=0)
        queries_grad = dot_first(stacked, k2_split).astype(BF16)
        queries_grad = (queries_grad.astype(F32) * HEAD_DIM ** (-0.5)).astype(BF16)
        projected[here, at : at + PAIR] = queries_grad
        projected[here, width + at : width + at + PAIR] = keys_grad
        projected[here, 2 * width + at : 2 * width + at + PAIR] = values_grad
    normed_grad = dot_last(projected[here, :width], blocks[0])
    normed_grad += dot_last(projected[here, width : 2 * width], blocks[1])
    normed_grad += dot_last(projected[here, 2 * width :], blocks[2])
    out = (incoming + norm_back(normed_grad, unit, scale, gain_ref[...])).astype(BF16)
    out_ref[0] = out
    if not first:
        is_true = true_positions(length, CAP_FIRST, CAP_ROWS, 0, "caption")
        caption_ref[0] = jnp.where(is_true, out[cap].astype(F32), 0.0).astype(BF16)
    add_to(gain_grad_ref, jnp.sum(normed_grad * unit, axis=0, keepdims=True))
    add_to(shift_grad_ref, jnp.sum(normed_grad, axis=0, keepdims=True))

    @pl.when(item == items - 1)
    def _():
        for block in range(4):
            columns = slice(block * width, (block + 1) * width)
            left = normed_turned if block < 3 else mixed_turned
            right = projected[:, columns] if block < 3 else branch_all[...]
            put_travel(travel_refs, 0, columns, left, right)
        bias_grad_ref[:, :width] = column_sum(projected[:, :width])
        bias_grad_ref[:, width : 2 * width] = column_sum(projected[:, 2 * width :])
        bias_grad_ref[:, 2 * width :] = column_sum(branch_all[...])


SHORT = pl.CostEstimate(flops=0, bytes_accessed=100_000, transcendentals=0)
LONG = pl.CostEstimate(flops=30_000_000_000, bytes_accessed=30_000_000, transcendentals=0)
ANYWHERE = pl.BlockSpec(memory_space=pl.ANY)


def whole_block(shape):
    return pl.BlockSpec(shape, lambda step, info: (0,) * len(shape))


def item_block(shape):
    return pl.BlockSpec((1,) + shape[1:], lambda step, info: (step,) + (0,) * (len(shape) - 1))


def blocks_scratch(count, width):
    return [pltpu.VMEM((count, width, width), BF16), pltpu.SemaphoreType.DMA((count,))]


def attend_forward(x, info, weights, gain, shift, bias, merge=None, following=None):
    arrays, plan = weights
    items, _, width = x.shape
    row = whole_block((1, width))
    bias_row = whole_block((1, 3 * width))
    caption_shape = (items, CAP_ROWS, width)
    if merge is not None:
        before, part, outer = merge
        operands = (x, before, part, outer, gain, shift, bias)
        specs = [item_block(x.shape), item_block(x.shape), item_block(caption_shape)]
        specs += [row, row, row, bias_row]
        last_shape, kind, scratch = x.shape, BF16, [pltpu.VMEM((ROWS, width), F32)]
    else:
        operands = (x, gain, shift, bias, *following)
        specs = [item_block(x.shape), row, row, bias_row, row, row]
        last_shape, kind, scratch = caption_shape, F32, []
    return pl.pallas_call(
        partial(attend_forward_kernel, plan, len(arrays), merge is not None),
        grid_spec=pltpu.PrefetchScalarGridSpec(
            num_scalar_prefetch=1,
            grid=(items,),
            in_specs=[ANYWHERE] * len(arrays) + specs,
            out_specs=[
                item_block(x.shape),
                item_block((items, ROWS, 3 * width)),
                item_block((items, ROWS, width)),
                item_block(last_shape),
            ],
            scratch_shapes=blocks_scratch(4, width) + scratch,
        ),
        out_shape=[
            jax.ShapeDtypeStruct(x.shape, kind),
            jax.ShapeDtypeStruct((items, ROWS, 3 * width), BF16),
            jax.ShapeDtypeStruct((items, ROWS, width), BF16),
            jax.ShapeDtypeStruct(last_shape, BF16),
        ],
        compiler_params=pltpu.CompilerParams(vmem_limit_bytes=VMEM_BYTES),
        cost_estimate=SHORT,
        name="attend_forward",
    )(info, *arrays, *operands)


def attend_backward(x, info, weights, gain, shift, qkv, mixed, incoming, first=None):
    arrays, plan = weights
    items, _, width = x.shape
    half = width // 2
    row = whole_block((1, width))
    caption_shape = (items, CAP_ROWS, width)
    operands = (x, gain, shift, qkv, mixed, incoming)
    specs = [item_block(x.shape), row, row, item_block(qkv.shape), item_block(mixed.shape)]
    specs += [item_block(incoming.shape)]
    outs = [
        (item_block(x.shape), x.shape, BF16),
        (row, (1, width), F32),
        (row, (1, width), F32),
        (whole_block((1, 3 * width)), (1, 3 * width), F32),
    ]
    outs += [(whole_block((1, half // 2, 4 * width)), (1, half // 2, 4 * width), BF16)] * 4
    scratch = []
    if first is not None:
        after, next_gain, parts = first
        operands += (after, next_gain, *parts)
        caption_rows = pl.BlockSpec((CAP_ROWS, width), lambda step, info: (step, 0))
        specs += [item_block(after.shape), row] + [caption_rows] * 4
        outs += [(row, (1, width), F32)] * 2
        scratch = [pltpu.VMEM((ROWS, width), F32)]
    else:
        outs += [(item_block(caption_shape), caption_shape, BF16)]
    return pl.pallas_call(
        partial(attend_backward_kernel, plan, len(arrays), first is not None),
        grid_spec=pltpu.PrefetchScalarGridSpec(
            num_scalar_prefetch=1,
            grid=(items,),
            in_specs=[ANYWHERE] * len(arrays) + specs,
            out_specs=[spec for spec, _, _ in outs],
            scratch_shapes=blocks_scratch(4, width)
            + [
                pltpu.VMEM((width, items * ROWS), BF16),
                pltpu.VMEM((width, items * ROWS), BF16),
                pltpu.VMEM((items * ROWS, width), BF16),
                pltpu.VMEM((items * ROWS, 3 * width), BF16),
                pltpu.VMEM((ROWS, width), BF16),
            ]
            + scratch,
        ),
        out_shape=[jax.ShapeDtypeStruct(shape, kind) for _, shape, kind in outs],
        compiler_params=pltpu.CompilerParams(vmem_limit_bytes=VMEM_BYTES),
        cost_estimate=LONG,
        name="attend_backward",
    )(info, *arrays, *operands)


def normal_parts(u):
    t = pl.reciprocal(1.0 + 0.23164190 * jnp.abs(u), approx=True)
    bell = jnp.exp2((u * -0.7213475204444817) * u)
    poly = t * (
        0.127414796
        + t * (-0.142248368 + t * (0.7107068705 + t * (-0.7265760135 + t * 0.5307027145)))
    )
    tail = poly * bell
    return jnp.where(u < 0, tail, 1.0 - tail), bell


def inner_forward(normed, matrix, bias):
    inner = dot_plain(normed, matrix) + bias
    cumulative, bell = normal_parts(inner)
    slope = cumulative + (inner * 0.3989422804014327) * bell
    return (inner * cumulative).astype(BF16), slope.astype(BF16)


def expert_forward_kernel(plan, weight_count, count, kind, info, *refs):
    weights, refs = refs[:weight_count], refs[weight_count:]
    x_ref, gain_ref, shift_ref, inner_ref, outer_ref = refs[:5]
    y_ref, act_ref, slope_ref, blocks, sems, normed, total = refs[5:]
    step = pl.program_id(0)
    items, _, width = x_ref.shape

    @pl.when(step == 0)
    def _():
        start_weights(info, items, weights, plan, blocks, sems)
        for item in range(items):
            x = x_ref[item, :count].astype(BF16).astype(F32)
            unit, _ = norm_parts(x)
            normed[item * count : (item + 1) * count] = (
                unit * gain_ref[...] + shift_ref[...]
            ).astype(BF16)

    wait_block(blocks, step, sems)
    wait_block(blocks, step + 4, sems)
    for at in range(0, width, 256):
        columns = slice(at, at + 256)
        act, slope = inner_forward(normed[...], blocks[step, :, columns], inner_ref[:, columns])
        act_ref[:, columns] = act
        slope_ref[:, columns] = slope
    part = dot_plain(act_ref[...], blocks[step + 4])

    @pl.when(step == 0)
    def _():
        total[...] = part

    @pl.when(step > 0)
    def _():
        total[...] += part

    @pl.when(step == pl.num_programs(0) - 1)
    def _():
        for item in range(items):
            row_true = true_positions(info[item], 0, count, 0, kind)
            branch = total[item * count : (item + 1) * count] + outer_ref[...]
            x = x_ref[item, :count].astype(BF16).astype(F32)
            y_ref[item, :count] = (x + jnp.where(row_true, branch, 0.0)).astype(BF16)
            if count < ROWS:
                y_ref[item, count:] = jnp.zeros((ROWS - count, width), BF16)


def expert_backward_kernel(plan, weight_count, count, kind, info, *refs):
    weights, refs = refs[:weight_count], refs[weight_count:]
    x_ref, gain_ref, shift_ref, act_ref, slope_ref, grad_ref = refs[:6]
    out_ref, gain_grad_ref, shift_grad_ref, inner_grad_ref, outer_grad_ref = refs[6:11]
    travel_refs = refs[11:15]
    blocks, sems, normed_turned, branch_turned, branch, inner_all, total = refs[15:]
    step = pl.program_id(0)
    items, _, width = x_ref.shape
    section, core = info[items], info[items + 1]

    @pl.when(step == 0)
    def _():
        start_weights(info, items, weights, plan, blocks, sems)
        outer = None
        for item in range(items):
            here = slice(item * count, (item + 1) * count)
            unit, _ = norm_parts(x_ref[item, :count].astype(BF16).astype(F32))
            normed = (unit * gain_ref[...] + shift_ref[...]).astype(BF16)
            row_true = true_positions(info[item], 0, count, 0, kind)
            incoming = grad_ref[item, :count].astype(F32)
            masked = jnp.where(row_true, incoming, 0.0).astype(BF16)
            branch[here] = masked
            store_turned(normed_turned, normed.T, here, section, core)
            store_turned(branch_turned, masked.T, here, section, core)
            term = column_sum(masked)
            outer = term if outer is None else outer + term
        outer_grad_ref[...] = outer

    wait_block(blocks, step, sems)
    wait_block(blocks, step + 4, sems)
    for at in range(0, width, 256):
        columns = slice(at, at + 256)
        act_grad = dot_last(branch[...], blocks[step + 4, columns])
        inner = (slope_ref[:, columns].astype(F32) * act_grad).astype(BF16)
        inner_all[:, columns] = inner
        inner_grad_ref[:, columns] = column_sum(inner)
        put_travel(travel_refs, 0, columns, normed_turned, inner)
        put_travel(travel_refs, 1, columns, branch_turned, act_ref[:, columns])
    part = dot_last(inner_all[...], blocks[step])

    @pl.when(step == 0)
    def _():
        total[...] = part

    @pl.when(step > 0)
    def _():
        total[...] += part

    @pl.when(step == pl.num_programs(0) - 1)
    def _():
        gain_sum, shift_sum = None, None
        for item in range(items):
            unit, scale = norm_parts(x_ref[item, :count].astype(BF16).astype(F32))
            normed_grad = total[item * count : (item + 1) * count]
            gain_part = jnp.sum(normed_grad * unit, axis=0, keepdims=True)
            shift_part = jnp.sum(normed_grad, axis=0, keepdims=True)
            gain_sum = gain_part if gain_sum is None else gain_sum + gain_part
            shift_sum = shift_part if shift_sum is None else shift_sum + shift_part
            incoming = grad_ref[item, :count].astype(F32)
            hidden = incoming + norm_back(normed_grad, unit, scale, gain_ref[...])
            out_ref[item, :count] = hidden.astype(BF16)
            if count < ROWS:
                out_ref[item, count:] = grad_ref[item, count:]
        gain_grad_ref[...] = gain_sum
        shift_grad_ref[...] = shift_sum


def shared_forward_kernel(*refs):
    *rows_refs, inputs_ref, inner_ref, outputs_ref = refs[:7]
    *part_refs, normed, total = refs[7:]
    count = rows_refs[0].shape[0]
    step = pl.program_id(0)

    @pl.when(step == 0)
    def _():
        for index, ref in enumerate(rows_refs):
            normed[index * count : (index + 1) * count] = ref[...]
        total[...] = jnp.zeros_like(total)

    act, _ = inner_forward(normed[...], inputs_ref[...], inner_ref[...])
    total[...] += dot_plain(act, outputs_ref[...])

    @pl.when(step == pl.num_programs(0) - 1)
    def _():
        for index, ref in enumerate(part_refs):
            ref[...] = total[index * count : (index + 1) * count].astype(BF16)


def shared_backward_kernel(plan, weight_count, info, *refs):
    weights, refs = refs[:weight_count], refs[weight_count:]
    rows_refs, grad_refs, inner_ref = refs[:4], refs[4:8], refs[8]
    part_refs, (keep_ref, send_ref, inner_grad_ref, outer_grad_ref) = refs[9:13], refs[13:17]
    blocks, sems, normed, branch, matrix = refs[17:]
    count, width = rows_refs[0].shape
    half = width // 2
    first = info.shape[0] - 3
    core = info[first + 1]
    start_weights(info, first, weights, plan, blocks, sems)
    for index in range(SECTIONS):
        here = slice(index * count, (index + 1) * count)
        normed[here] = rows_refs[index][...]
        branch[here] = grad_refs[index][...]
    outer_grad_ref[...] = column_sum(grad_refs[0][...])
    wait_block(blocks, 0, sems)
    wait_block(blocks, 1, sems)
    part = None
    for at in range(0, width, 256):
        columns = slice(at, at + 256)
        act, slope = inner_forward(normed[...], blocks[0, :, columns], inner_ref[:, columns])
        act_grad = dot_last(branch[...], blocks[1, columns])
        inner = (slope.astype(F32) * act_grad).astype(BF16)
        inner_grad_ref[:, columns] = column_sum(inner)
        matrix[0, :, columns] = dot_first(normed[...], inner).astype(BF16)
        matrix[1, :, columns] = dot_first(branch[...], act).astype(BF16)
        term = dot_last(inner, blocks[0, :, columns])
        part = term if part is None else part + term
    for index, ref in enumerate(part_refs):
        ref[...] = part[index * count : (index + 1) * count].astype(BF16)
    quarter = half // 4
    for which in range(2):
        for group in range(4):
            columns = slice(group * width, (group + 1) * width)
            mine = pl.multiple_of(core * half, 16) + group * quarter
            other = pl.multiple_of((1 - core) * half, 16) + group * quarter
            keep_ref[which, :, columns] = matrix[which, pl.ds(pl.multiple_of(mine, 16), quarter)]
            send_ref[which, :, columns] = matrix[which, pl.ds(pl.multiple_of(other, 16), quarter)]


def chunk_columns(rows, width):
    return pl.BlockSpec((rows, width), lambda step, info: (0, step))


def expert_forward(x, info, weights, gain, shift, inner, outer, count, kind):
    arrays, plan = weights
    items, _, width = x.shape
    hidden = inner.shape[1]
    row = whole_block((1, width))
    return pl.pallas_call(
        partial(expert_forward_kernel, plan, len(arrays), count, kind),
        grid_spec=pltpu.PrefetchScalarGridSpec(
            num_scalar_prefetch=1,
            grid=(hidden // width,),
            in_specs=[ANYWHERE] * len(arrays)
            + [whole_block(x.shape), row, row, chunk_columns(1, width), row],
            out_specs=[
                whole_block((items, ROWS, width)),
                chunk_columns(items * count, width),
                chunk_columns(items * count, width),
            ],
            scratch_shapes=blocks_scratch(8, width)
            + [
                pltpu.VMEM((items * count, width), BF16),
                pltpu.VMEM((items * count, width), F32),
            ],
        ),
        out_shape=[
            jax.ShapeDtypeStruct((items, ROWS, width), BF16),
            jax.ShapeDtypeStruct((items * count, hidden), BF16),
            jax.ShapeDtypeStruct((items * count, hidden), BF16),
        ],
        compiler_params=pltpu.CompilerParams(vmem_limit_bytes=VMEM_BYTES),
        cost_estimate=SHORT,
        name="expert_forward_" + kind,
    )(info, *arrays, x, gain, shift, inner, outer)


def expert_backward(x, info, weights, gain, shift, act, slope, incoming, count, kind):
    arrays, plan = weights
    items, _, width = x.shape
    half = width // 2
    hidden = act.shape[1]
    row = whole_block((1, width))
    travel = pl.BlockSpec((2, half // 2, width), lambda step, info: (0, 0, step))
    return pl.pallas_call(
        partial(expert_backward_kernel, plan, len(arrays), count, kind),
        grid_spec=pltpu.PrefetchScalarGridSpec(
            num_scalar_prefetch=1,
            grid=(hidden // width,),
            in_specs=[ANYWHERE] * len(arrays)
            + [
                whole_block(x.shape),
                row,
                row,
                chunk_columns(items * count, width),
                chunk_columns(items * count, width),
                whole_block(incoming.shape),
            ],
            out_specs=[whole_block(incoming.shape), row, row, chunk_columns(1, width), row]
            + [travel] * 4,
            scratch_shapes=blocks_scratch(8, width)
            + [
                pltpu.VMEM((width, items * count), BF16),
                pltpu.VMEM((width, items * count), BF16),
                pltpu.VMEM((items * count, width), BF16),
                pltpu.VMEM((items * count, width), BF16),
                pltpu.VMEM((items * count, width), F32),
            ],
        ),
        out_shape=[
            jax.ShapeDtypeStruct(incoming.shape, BF16),
            jax.ShapeDtypeStruct((1, width), F32),
            jax.ShapeDtypeStruct((1, width), F32),
            jax.ShapeDtypeStruct((1, hidden), F32),
            jax.ShapeDtypeStruct((1, width), F32),
        ]
        + [jax.ShapeDtypeStruct((2, half // 2, hidden), BF16)] * 4,
        compiler_params=pltpu.CompilerParams(vmem_limit_bytes=VMEM_BYTES),
        cost_estimate=SHORT,
        name="expert_backward_" + kind,
    )(info, *arrays, x, gain, shift, act, slope, incoming)


IN_VMEM = pl.BlockSpec(memory_space=pltpu.VMEM)
IN_SMEM = pl.BlockSpec(memory_space=pltpu.SMEM)


def shared_forward(rows, inputs, inner, outputs):
    count, width = rows[0].shape
    total = SECTIONS * count
    hidden = inner.shape[1]
    return pl.pallas_call(
        shared_forward_kernel,
        grid=(hidden // width,),
        in_specs=[pl.BlockSpec(rows[0].shape, lambda step: (0, 0))] * 4
        + [
            pl.BlockSpec((width, width), lambda step: (0, step)),
            pl.BlockSpec((1, width), lambda step: (0, step)),
            pl.BlockSpec((width, width), lambda step: (step, 0)),
        ],
        out_specs=[pl.BlockSpec((count, width), lambda step: (0, 0))] * SECTIONS,
        scratch_shapes=[pltpu.VMEM((total, width), BF16), pltpu.VMEM((total, width), F32)],
        out_shape=[jax.ShapeDtypeStruct((count, width), BF16)] * SECTIONS,
        compiler_params=pltpu.CompilerParams(vmem_limit_bytes=VMEM_BYTES),
        cost_estimate=SHORT,
        name="shared_forward",
    )(*rows, inputs, inner, outputs)


def shared_backward(rows, grads, info, weights, inner):
    arrays, plan = weights
    count, width = rows[0].shape
    total = SECTIONS * count
    travel = (2, width // 8, 4 * width)
    return pl.pallas_call(
        partial(shared_backward_kernel, plan, len(arrays)),
        in_specs=[IN_SMEM] + [ANYWHERE] * len(arrays) + [IN_VMEM] * 9,
        out_specs=[IN_VMEM] * 8,
        scratch_shapes=blocks_scratch(2, width)
        + [
            pltpu.VMEM((total, width), BF16),
            pltpu.VMEM((total, width), BF16),
            pltpu.VMEM((2, width, width), BF16),
        ],
        out_shape=[
            *[jax.ShapeDtypeStruct((count, width), BF16)] * SECTIONS,
            jax.ShapeDtypeStruct(travel, BF16),
            jax.ShapeDtypeStruct(travel, BF16),
            jax.ShapeDtypeStruct((1, width), F32),
            jax.ShapeDtypeStruct((1, width), F32),
        ],
        compiler_params=pltpu.CompilerParams(vmem_limit_bytes=VMEM_BYTES),
        cost_estimate=SHORT,
        name="shared_backward",
    )(info, *arrays, *rows, *grads, inner)


def plane_turn(plane, planes):
    return ((plane & 1) << 1) | (plane >> 1) if planes == 4 else 0


def finish_kernel(planes, info, scale_ref, mine_ref, theirs_ref, *refs):
    step = pl.program_id(0)
    count = mine_ref.shape[1]
    placed = refs[-1]
    outs = refs[:-1]
    width = placed.shape[1]
    half = width // 2
    at = info.shape[0] - 3
    section, core = info[at], info[at + 1]
    turn = plane_turn(info[at + 2], planes)
    turned = turn if count == 1 else jnp.where(section == 1, turn, 0)
    scale = scale_ref[0, 0]
    columns = pl.ds(pl.multiple_of((step ^ turned) * width, width), width)

    def place(which):
        def by_rows():
            for side, ref in enumerate((mine_ref, theirs_ref)):
                for away in range(SECTIONS):
                    for path in range(2):
                        row = (core ^ side) * half + path * (half // 2)
                        row = row + (section ^ away) * PIECE_ROWS
                        placed[pl.ds(pl.multiple_of(row, 16), PIECE_ROWS), :] = ref[
                            away, which, path * PIECE_ROWS : (path + 1) * PIECE_ROWS, columns
                        ].astype(F32)

        def by_columns():
            for side, ref in enumerate((mine_ref, theirs_ref)):
                for group in range(4):
                    quarter = half // 4
                    row = (core ^ side) * half + group * quarter
                    placed[pl.ds(pl.multiple_of(row, 16), quarter), :] = ref[
                        step, which, :, group * width : (group + 1) * width
                    ].astype(F32)

        if count == 1:
            by_rows()
        else:
            pl.when(section != 0)(by_rows)
            pl.when(section == 0)(by_columns)

    place(0)
    if count == 1:

        @pl.when(step < 3)
        def _():
            outs[0][0] = placed[...] / scale

        @pl.when(step == 3)
        def _():
            outs[1][0] = placed[...] / scale

    else:
        outs[0][0] = placed[...] / scale
        place(1)
        outs[1][0] = (placed[...] / scale).T


def finish(info, scale, mine, theirs, planes):
    count, hidden = mine.shape[1], mine.shape[3]
    width = hidden // 4
    if count == 1:
        shapes = [(1, width, 3 * width), (1, width, width)]
        maps = [lambda step, info: (0, 0, jnp.minimum(step, 2)), lambda step, info: (0, 0, 0)]
    else:
        shapes = [(1, width, hidden), (1, hidden, width)]
        maps = [lambda step, info: (0, 0, step), lambda step, info: (0, step, 0)]
    return pl.pallas_call(
        partial(finish_kernel, planes),
        grid_spec=pltpu.PrefetchScalarGridSpec(
            num_scalar_prefetch=1,
            grid=(4,),
            in_specs=[IN_SMEM, whole_block(mine.shape), whole_block(mine.shape)],
            out_specs=[pl.BlockSpec((1, width, width), at) for at in maps],
            scratch_shapes=[pltpu.VMEM((width, width), F32)],
        ),
        out_shape=[jax.ShapeDtypeStruct(shape, F32) for shape in shapes],
        compiler_params=pltpu.CompilerParams(vmem_limit_bytes=VMEM_BYTES),
        cost_estimate=SHORT,
        name="finish",
    )(info, scale, mine, theirs)


def pack_kernel(count, plan, info, *refs):
    sources, outs, sems = refs[:count], refs[count:-1], refs[-1]
    first = info.shape[0] - 3
    section, core, plane = info[first], info[first + 1], info[first + 2]
    half = outs[0].shape[1]
    for index, (out, choices) in enumerate(zip(outs, plan)):
        for at, at_plane, parts in choices:
            here = section == at
            if at_plane is not None:
                here = here & (plane == at_plane)

            @pl.when(here)
            def _(index=index, out=out, parts=parts):
                for block, part in enumerate(parts):
                    if part[0] == "own":
                        _, which, row, column = part
                        rows = pl.ds(pl.multiple_of(row + core * half, half), half)
                        source = sources[which].at[rows, pl.ds(column, out.shape[2])]
                    else:
                        source = sources[part[1]].at[block]
                    pltpu.make_async_copy(source, out.at[block], sems.at[index, block]).start()

    for index, out in enumerate(outs):
        for block in range(2):
            pltpu.make_async_copy(out.at[block], out.at[block], sems.at[index, block]).wait()


def pack(info, sources, plan, shape):
    return pl.pallas_call(
        partial(pack_kernel, len(sources), plan),
        in_specs=[IN_SMEM] + [ANYWHERE] * len(sources),
        out_specs=[IN_VMEM] * len(plan),
        scratch_shapes=[pltpu.SemaphoreType.DMA((len(plan), 2))],
        out_shape=[jax.ShapeDtypeStruct(shape, BF16)] * len(plan),
        cost_estimate=SHORT,
        name="pack",
    )(info, *sources)


def over_section(value, bits, sources=range(SECTIONS)):
    return lax.ppermute(value, "section", [(at, at ^ bits) for at in sources])


def over_core(value):
    return lax.ppermute(value, "core", [(0, 1), (1, 0)])


def over_plane(value, pairs):
    return lax.ppermute(value, "z", pairs)


def added(left, right):
    return (left.astype(F32) + right.astype(F32)).astype(BF16)


def after(value, *earlier):
    return lax.optimization_barrier((value,) + earlier)[0]


def under(outputs, *arrivals):
    joined = lax.optimization_barrier(tuple(outputs) + arrivals)
    return list(joined[: len(outputs)]), list(joined[len(outputs) :])


def by_section(section, values):
    result, last = None, None
    for at in sorted(values):
        if result is None:
            result = values[at]
        elif values[at] is not last:
            result = jnp.where(section >= at, values[at], result)
        last = values[at]
    return result


def total(*values):
    result = values[0].astype(F32)
    for value in values[1:]:
        result = result + value.astype(F32)
    return result.astype(BF16)


class Sums:
    def __init__(self, travel):
        self.stay, self.move, self.other_stay, self.other_move = travel
        self.size = self.stay.shape[1] // 2

    def cross(self, *earlier):
        if earlier:
            self.other_move = after(self.other_move, *earlier)
            self.other_stay = after(self.other_stay, *earlier)
        self.got_move, self.got_stay = over_core(self.other_move), over_core(self.other_stay)

    def first_sends(self):
        size = self.size
        self.sent = [
            total(self.move[:, at : at + size], self.got_move[:, at : at + size])
            for at in (0, size)
        ]
        return self.sent

    def second_sends(self, from_x, from_y):
        size, half = self.size, self.size // 2
        self.first = from_x, from_y
        to_y = total(self.stay[:, half:size], self.got_stay[:, half:size], from_x[:, half:])
        to_x = total(
            self.stay[:, size + half :], self.got_stay[:, size + half :], from_y[:, half:]
        )
        self.sent = [to_x, to_y]
        return self.sent

    def whole(self, from_x, from_y):
        size, half = self.size, self.size // 2
        parts = []
        for at, first, second in ((0, self.first[0], from_y), (size, self.first[1], from_x)):
            here = slice(at, at + half)
            parts.append(total(self.stay[:, here], self.got_stay[:, here], first[:, :half], second))
        return jnp.concatenate(parts, axis=1)


def over_links(sends):
    return [over_section(sends[0], 1), over_section(sends[1], 2)]


class Planes:
    def __init__(self, value, plane, planes):
        self.value, self.plane, self.planes, self.turn = value, plane, planes, 0

    def sends(self, *earlier):
        value = after(self.value, *earlier) if earlier else self.value
        if self.planes != 4:
            return (value,)
        bits = (1, 2, 2, 1)[self.turn]
        if self.turn < 2:
            bit = (self.plane & 1, self.plane >> 1)[self.turn]
            size = value.shape[-1] // 2
            value = lax.dynamic_slice_in_dim(value, (1 - bit) * size, size, value.ndim - 1)
        return (over_plane(value, [(at, at ^ bits) for at in range(4)]),)

    def take(self, arrived):
        if self.planes != 4:
            self.value = lax.psum(arrived, "z") if self.turn == 3 else arrived
        elif self.turn < 2:
            bit = (self.plane & 1, self.plane >> 1)[self.turn]
            size = self.value.shape[-1] // 2
            keep = lax.dynamic_slice_in_dim(self.value, bit * size, size, self.value.ndim - 1)
            self.value = added(keep, arrived)
        else:
            self.value = jnp.concatenate([self.value, arrived], axis=-1)
        self.turn += 1

    def in_order(self, value):
        if self.planes != 4:
            return value
        size, turn = value.shape[-1] // 4, plane_turn(self.plane, 4)
        parts = [
            lax.dynamic_slice_in_dim(value, (at ^ turn) * size, size, value.ndim - 1)
            for at in range(4)
        ]
        return jnp.concatenate(parts, axis=-1)


class Weights:
    def __init__(self, own, info, planes):
        self.own, self.info = own, info
        self.four = planes == 4
        self.plan = PLAN_FOUR if self.four else PLAN_ANY
        self.half, self.width = own[1].shape[0] // 2, own[1].shape[1]
        self.mine, self.theirs, self.arrived = {}, {}, {}

    def place(self, layer, block):
        if layer in "ac":
            return (0, 0, block * self.width) if block < 3 else (1, 0, 0)
        if layer == "g":
            return (2, 0, block * self.width) if block < 4 else (3, (block - 4) * self.width, 0)
        return (2, 0, block * self.width) if block < 4 else (3, (block - 4) * self.width, 0)

    def choices(self, sends, sources):
        result = []
        for at in range(SECTIONS):
            name = sends.get(at)
            if name is not None and HOMES[name[0]] != at:
                key = self.arrived[at, name]
                if key not in sources:
                    sources[key] = len(self.own) + len(sources)
                result.append((at, None, [("arrived", sources[key])] * 2))
                continue
            for plane in range(4) if name == "F" else (None,):
                piece = ("f" + str(plane)) if name == "F" else name or "a0"
                layer, index = piece[0], int(piece[1])
                if layer in "ac":
                    blocks = ATTEND_BLOCKS[index]
                else:
                    blocks = (index, 4 + index) if layer == "g" else EXPERT_BLOCKS[index]
                parts = [("own",) + self.place(layer, block) for block in blocks]
                result.append((at, plane, parts))
        return result

    def packed(self, wanted):
        sources = {}
        plan = [self.choices(sends, sources) for sends in wanted]
        arrays = list(self.own) + [self.mine[key] for key in sources]
        return pack(self.info, arrays, plan, (2, self.half, self.width))

    def sends(self, step):
        if step == "F":
            return [{at: "F" for at in range(SECTIONS)}]
        return [sends for sends in self.plan[step] if sends]

    def payloads(self, *steps):
        wanted = [sends for step in steps for sends in self.sends(step)]
        return list(self.packed(wanted))

    def move(self, step, payloads):
        links = [(link, sends) for link, sends in enumerate(self.plan[step]) if sends]
        for (link, sends), payload in zip(links, payloads):
            self.mine[step, link] = over_section(payload, link + 1, sorted(sends))
            for at, name in sends.items():
                self.arrived[at ^ (link + 1), name] = (step, link)
        return [(step, link) for link, _ in links]

    def move_planes(self, step):
        up, down = self.mine["plane", step - 1], self.mine["plane", 1 - step]
        up = over_plane(up, [(at, at + 1) for at in range(step - 1, 3)])
        down = over_plane(down, [(at, at - 1) for at in range(4 - step, 0, -1)])
        self.mine["plane", step], self.mine["plane", -step] = up, down
        return [("plane", step), ("plane", -step)]

    def cross(self, keys):
        for key in keys:
            self.theirs[key] = over_core(self.mine[key])
        return keys

    def join(self, outputs, mine=(), theirs=()):
        values = [self.mine[key] for key in mine] + [self.theirs[key] for key in theirs]
        outputs, values = under(outputs, *values)
        for key, value in zip(mine, values):
            self.mine[key] = value
        for key, value in zip(theirs, values[len(mine) :]):
            self.theirs[key] = value
        return outputs

    def layer(self, layer):
        arrays, places = list(self.own), {}

        def place(key):
            if key not in places:
                places[key] = len(arrays)
                arrays.extend([self.mine[key], self.theirs[key]])
            return places[key], places[key] + 1

        if layer in "ac":
            names = [(layer + str(index), ATTEND_BLOCKS[index]) for index in range(2)]
        else:
            names = [(layer + str(index), EXPERT_BLOCKS[index]) for index in range(4)]
        plan = []
        for at in range(SECTIONS):
            if layer == "g":
                names = [("g" + str(at), (0, 1))]
            if HOMES[layer] == at:
                steps = []
                for name, blocks in names:
                    for block in blocks:
                        source = block * 4 if layer == "g" else block
                        steps.append((block, ("own",) + self.place(layer, source)))
                plan.append((at, None, steps))
                continue
            by_plane = layer == "f" and self.four
            for plane in range(4) if by_plane else (None,):
                steps = []
                for index, (name, blocks) in enumerate(names):
                    key = ("plane", plane - index) if by_plane else self.arrived[at, name]
                    for which, block in enumerate(blocks):
                        steps.append((block, ("piece",) + place(key) + (which,)))
                plan.append((at, plane, steps))
        return arrays, plan


def per_device(
    tokens,
    caption_lengths,
    attend_gain,
    attend_shift,
    attend_inputs,
    attend_bias,
    attend_output,
    expert_gain,
    expert_shift,
    expert_inputs,
    expert_inner_bias,
    expert_outputs,
    expert_outer_bias,
    cotangent,
):
    section, core, plane = lax.axis_index("section"), lax.axis_index("core"), lax.axis_index("z")
    planes = lax.axis_size("z")
    items, positions, width = tokens.shape
    hidden = expert_inputs.shape[-1]
    info = [value.reshape(1).astype(jnp.int32) for value in (section, core, plane)]
    info = jnp.concatenate([caption_lengths] + info)
    weights = Weights(
        (attend_inputs[0], attend_output[0], expert_inputs[0], expert_outputs[0]), info, planes
    )

    def to_sections(value):
        return [value] + [over_section(value, bits) for bits in (1, 2, 3)]

    def items_of(part):
        return part.reshape(items, CAP_ROWS, width)

    keys = weights.move(0, weights.payloads(0))
    pad = ((0, 0), (0, ROWS - positions), (0, 0))
    x0 = jnp.pad(tokens, pad)
    last_grad = jnp.pad(cotangent, pad)
    rows = jnp.concatenate(
        [
            attend_gain,
            attend_shift,
            attend_bias,
            expert_gain,
            expert_shift,
            expert_inner_bias,
            expert_outer_bias,
            jnp.full((1, 128), jnp.sum(caption_lengths), F32),
        ],
        axis=1,
    )
    rows = to_sections(rows)
    x0, last_grad, *rows = weights.join([x0, last_grad, *rows], keys)
    keys1 = weights.move(1, weights.payloads(1))
    rows = jnp.concatenate(rows, axis=0)
    language_count = jnp.sum(rows[:, -128:], axis=0, keepdims=True)
    rows = [lax.dynamic_index_in_dim(rows, at ^ section, 0) for at in range(SECTIONS)]
    sizes = [width, width, 3 * width, width, width, hidden, width]
    ends = [sum(sizes[: at + 1]) for at in range(len(sizes))]
    used = [(0, 0), (0, 1), (0, 2), (0, 3), (0, 4), (0, 5), (1, 3), (1, 4), (1, 5), (1, 6)]
    used += [(0, 6), (2, 0), (2, 1), (2, 2), (3, 3), (3, 4), (3, 5), (3, 6)]
    kept = [rows[slot][:, ends[which] - sizes[which] : ends[which]] for slot, which in used]
    language_count, *kept = weights.join([language_count, *kept], keys1)
    kept = dict(zip(used, kept))

    def row(slot, which):
        return kept[slot, which]

    crossed = weights.cross(keys + keys1)
    sends = weights.payloads(2, "F") if weights.four else weights.payloads(2)
    sends, (info, language_count) = under(sends, info, language_count)
    keys = weights.move(2, sends[:2])
    info, language_count = weights.join(
        [info, language_count + over_core(language_count)], theirs=crossed
    )
    if weights.four:
        weights.mine["plane", 0] = sends[2]
        keys += weights.move_planes(1)
    attend0 = weights.layer("a")
    outputs = attend_forward(
        x0, info, attend0, row(0, 0), row(0, 1), row(0, 2), following=(row(0, 3), row(0, 4))
    )
    y0, qkv0, mixed0, caption_rows = weights.join(outputs, keys)
    caption_rows = to_sections(caption_rows.reshape(-1, width))
    crossed = weights.cross([(2, 0), (2, 1)])
    sends = weights.payloads(3, 4) if weights.four else weights.payloads(3)
    if weights.four:
        language_count += over_plane(language_count, [(at, at ^ 1) for at in range(4)])
    *caption_rows, language_count = weights.join([*caption_rows, language_count], theirs=crossed)
    sends, caption_rows = under(sends, *caption_rows)
    keys, sends = weights.move(3, sends), sends[2:]
    if weights.four:
        keys += weights.move_planes(2)
        language_count += over_plane(language_count, [(at, at ^ 2) for at in range(4)])
    else:
        language_count = lax.psum(language_count, "z")
    outputs = shared_forward(caption_rows, expert_inputs[0], expert_inner_bias, expert_outputs[0])
    *part, language_count = weights.join([*outputs, language_count], keys)
    language_count = language_count[0, 0].astype(jnp.int32)
    vision_count = PATCHES * items * SECTIONS * 2 * planes
    counts = jnp.stack(
        [jnp.full((), vision_count, jnp.int32), language_count, language_count + vision_count]
    )
    crossed = weights.cross([(3, 0), (3, 1)])
    branch = {at: over_section(part[at], at, [0]) for at in range(1, SECTIONS)}
    keys = weights.move_planes(3) if weights.four else []
    (y0,) = weights.join([y0], theirs=crossed)
    expert1 = weights.layer("e")
    outputs = expert_forward(
        y0, info, expert1, row(1, 3), row(1, 4), row(1, 5), row(1, 6), PATCH_ROWS, "patch"
    )
    outputs, moved = under(outputs, *branch.values())
    x2, act1, slope1 = weights.join(outputs, keys)
    branch = dict(zip(branch, moved))
    branch[0] = part[0]
    branch = items_of(by_section(section, branch))
    if weights.four:
        crossed = [("plane", step) for step in range(-3, 4)]
    else:
        for step in (4, 5):
            weights.move(step, weights.payloads(step))
        crossed = [(4, 0), (4, 1), (5, 0)]
    weights.cross(crossed)
    attend2 = weights.layer("c") if weights.four else None
    if not weights.four:
        (x2,) = weights.join([x2], theirs=crossed)
        attend2 = weights.layer("c")
    outputs = attend_forward(
        x2, info, attend2, row(2, 0), row(2, 1), row(2, 2), merge=(y0, branch, row(0, 6))
    )
    x3, qkv2, mixed2, x2 = weights.join(outputs, theirs=crossed)
    expert3 = weights.layer("f")
    layer_output, act3, slope3 = expert_forward(
        x3, info, expert3, row(3, 3), row(3, 4), row(3, 5), row(3, 6), ROWS, "all"
    )

    def small_rows(values):
        flat = jnp.concatenate(values, axis=1)
        count = -(-flat.shape[1] // hidden)
        flat = jnp.pad(flat, ((0, 0), (0, count * hidden - flat.shape[1])))
        return flat.reshape(count, hidden)

    def to_home(sums):
        got = [by_section(section, sums)]
        for bits in (1, 2, 3):
            sends = {at ^ bits: sums[at] for at in sums}
            got.append(over_section(by_section(section, sends), bits, sorted(sends)))
        return got

    keys = []
    if weights.four:
        sends, (layer_output, last_grad) = under(sends, layer_output, last_grad)
        keys = weights.move(4, sends)
    outputs = expert_backward(
        x3, info, expert3, row(3, 3), row(3, 4), act3, slope3, last_grad, ROWS, "all"
    )
    outputs = weights.join(outputs, keys)
    crossed = weights.cross(keys)
    grad3, *small3 = outputs[:5]
    sums3 = Sums(outputs[5:])
    sums3.cross()
    moved = over_links(sums3.first_sends())
    grad3 = after(grad3, *sums3.sent)
    outputs = attend_backward(
        x2, info, attend2, row(2, 0), row(2, 1), qkv2, mixed2, grad3
    )
    outputs, moved = under(outputs, *moved, sums3.got_stay)
    outputs = weights.join(outputs, theirs=crossed)
    grad2, *small2 = outputs[:4]
    sums2, caption_grad = Sums(outputs[4:8]), outputs[8]
    caption_grads = to_sections(caption_grad.reshape(-1, width))
    sums3.got_stay = moved[2]
    moved3 = over_links(sums3.second_sends(*moved[:2]))
    grad2 = after(grad2, *sums3.sent)
    outputs = expert_backward(
        y0, info, expert1, row(1, 3), row(1, 4), act1, slope1, grad2, PATCH_ROWS, "patch"
    )
    outputs, caption_grads = under(outputs, *caption_grads)
    grad1, *small1 = outputs[:5]
    sums2.cross(grad1)
    sums1 = Sums(outputs[5:])
    sums1.cross()
    inner_quarter = lax.dynamic_slice(row(0, 5), (0, section * width), (1, width))
    sum3 = sums3.whole(*moved3)
    inner_quarter = after(inner_quarter, grad1, sum3)
    outputs = shared_backward(
        caption_rows, caption_grads, info, weights.layer("g"), inner_quarter
    )
    parts, (keep0, send0, inner_grad, outer_grad) = outputs[:4], outputs[4:]
    got = [over_section(parts[bits], bits) for bits in (1, 2, 3)]
    sends = [after(value, *parts) for value in sums1.first_sends()]
    moved1 = over_links(sends)
    keep0 = added(keep0, over_core(send0))
    early = lax.psum(jnp.concatenate([sum3, keep0], axis=0), "z")
    sends2 = [after(value, *sends) for value in sums2.first_sends()]
    moved2 = over_links(sends2)
    parts = [parts[0], *got]
    grad1 = after(grad1, keep0, *sends, *sends2)
    outputs = attend_backward(
        x0,
        info,
        attend0,
        row(0, 0),
        row(0, 1),
        qkv0,
        mixed0,
        grad1,
        first=(y0, row(0, 3), parts),
    )
    outputs, moved = under(outputs, *moved2, *moved1)
    moved2, moved1 = moved[:2], moved[2:]
    tokens_grad, *small_first = outputs[:4]
    sums_first, gain_grad, shift_grad = Sums(outputs[4:8]), outputs[8], outputs[9]
    sums_first.cross()
    inner_grad = lax.dynamic_update_slice(
        jnp.zeros((1, hidden), F32), inner_grad, (0, section * width)
    )
    small = small_rows(
        small_first + [gain_grad, shift_grad, inner_grad, outer_grad] + small2 + small1 + small3
    )
    small = added(small, over_core(small))
    to_x, to_y = sums_first.first_sends()
    to_x = jnp.concatenate([to_x[0], small], axis=0)
    sends = lax.optimization_barrier((*sums1.second_sends(*moved1), to_x, to_y))
    moved1, moved = over_links(sends[:2]), over_links(sends[2:])
    sum1, early = lax.optimization_barrier((sums1.whole(*moved1), early))
    planes1 = Planes(sum1, plane, planes)
    size = to_y.shape[1]
    small = added(small, moved[0][size:])
    to_x, to_y = sums_first.second_sends(moved[0][None, :size], moved[1])
    early_x, early_y = sums2.second_sends(*moved2)
    to_x = jnp.concatenate([to_x[0], early_x[0]], axis=0)
    to_y = jnp.concatenate([to_y[0], early_y[0], small], axis=0)
    to_x, to_y = lax.optimization_barrier((to_x, to_y))
    sent1 = planes1.sends()
    moved = lax.optimization_barrier(tuple(over_links((to_x, to_y))))
    size = early_x.shape[1]
    last = sums_first.whole(moved[0][None, :size], moved[1][None, :size])
    sum2 = sums2.whole(moved[0][None, size:], moved[1][None, size : 2 * size])
    small = added(small, moved[1][2 * size :])
    small_count = small.shape[0]
    eighth = last.shape[1]
    last = jnp.concatenate([last[0], sum2[0], small], axis=0)
    planes_last = Planes(last, plane, planes)
    home_early = to_home({0: after(early[2:], *moved), 3: after(early[:2], *moved)})
    planes_last.take(*planes_last.sends())
    planes1.take(*sent1)
    planes1.take(*planes1.sends())
    planes1.take(*planes1.sends())
    planes1.take(*planes1.sends())
    planes_last.take(*planes_last.sends())
    planes_last.take(*planes_last.sends())
    home_late = to_home({1: after(planes1.value, *home_early[1:])})
    planes_last.take(*planes_last.sends())
    last = planes_last.value
    home_attend = to_home({0: last[None, :eighth], 2: last[None, eighth : 2 * eighth]})
    small = planes_last.in_order(last[2 * eighth :].astype(F32))

    as_float = counts.astype(F32)
    one = jnp.ones((), F32)
    attend_scales = jnp.stack([as_float[2], one, as_float[2], one])
    expert_scales = jnp.stack([as_float[1], as_float[0], one, as_float[2]])

    def placed(pieces, scales):
        scale = lax.dynamic_index_in_dim(scales, section, 0).reshape(1, 1)
        pieces = jnp.stack(pieces)
        return finish(info, scale, pieces, over_core(pieces), planes)

    blank = jnp.zeros_like(home_late[0])
    inputs_whole, outputs_whole = placed(
        [
            by_section(section, {0: early, 1: late, 2: blank, 3: early})
            for early, late in zip(home_early, home_late)
        ],
        expert_scales,
    )
    blank = jnp.zeros_like(home_attend[0])
    attend_whole, output_whole = placed(
        [by_section(section, {0: got, 1: blank, 2: got, 3: blank}) for got in home_attend],
        attend_scales,
    )

    attend_size, expert_size = 5 * width, 3 * width + hidden
    cuts = [attend_size, attend_size + expert_size]
    cuts += [cuts[1] + attend_size, cuts[1] + attend_size + expert_size]
    small = jnp.split(small.reshape(-1)[: cuts[3] + expert_size], cuts)
    none_attend, none_expert = jnp.zeros_like(small[0]), jnp.zeros_like(small[1])
    attend_small = jnp.stack([small[0], none_attend, small[2], none_attend])
    expert_small = jnp.stack([small[1], small[3], none_expert, small[4]])
    attend_small = attend_small / attend_scales.reshape(-1, 1)
    expert_small = expert_small / expert_scales.reshape(-1, 1)
    attend_small = lax.dynamic_index_in_dim(attend_small, section, 0)
    expert_small = lax.dynamic_index_in_dim(expert_small, section, 0)
    return (
        layer_output[:, :positions],
        tokens_grad[:, :positions],
        attend_small[:, :width],
        attend_small[:, width : 2 * width],
        attend_whole,
        attend_small[:, 2 * width :],
        output_whole,
        expert_small[:, :width],
        expert_small[:, width : 2 * width],
        inputs_whole,
        expert_small[:, 2 * width : 2 * width + hidden],
        outputs_whole,
        expert_small[:, 2 * width + hidden :],
        counts,
    )


def solution(mesh):
    sections, groups = mesh.shape["section"], mesh.shape["dp"]
    split = Mesh(mesh.devices.reshape(sections, groups // 2, 2), ("section", "z", "core"))
    items = P(("section", "z", "core"), None, None)
    flat = P("section", None)
    matrix = P("section", None, None)
    placed = (
        items,
        P(("section", "z", "core")),
        flat,
        flat,
        matrix,
        flat,
        matrix,
        flat,
        flat,
        matrix,
        flat,
        matrix,
        flat,
        items,
    )
    return jax.shard_map(
        per_device,
        mesh=split,
        in_specs=placed,
        out_specs=(
            items,
            items,
            flat,
            flat,
            matrix,
            flat,
            matrix,
            flat,
            flat,
            matrix,
            flat,
            matrix,
            flat,
            P(),
        ),
        check_vma=False,
    )
```

```python
from functools import partial

import jax
import jax.numpy as jnp
from jax import lax
from jax.experimental import pallas as pl
from jax.experimental.pallas import tpu as pltpu
from jax.sharding import Mesh
from jax.sharding import PartitionSpec as P

HEADS = 12
HEAD_DIM = 64
PATCHES = 197
ROWS = 256
CAP_FIRST, CAP_ROWS = 192, 48
PATCH_ROWS = 208
PAIR = 2 * HEAD_DIM
SECTIONS = 4
PIECE_ROWS = 48
VMEM_BYTES = 58 * 1024 * 1024
F32 = jnp.float32
BF16 = jnp.bfloat16

PLAN_FOUR = (
    ({0: "a0", 1: "e0", 2: "c0", 3: "F"}, {0: "a1", 1: "e2", 2: "c0", 3: "F"}),
    ({0: "a1", 1: "e1", 2: "a1", 3: "e2"}, {0: "a0", 1: "a0", 2: "F", 3: "c0"}),
    ({0: "g3", 1: "e2", 2: "c1"}, {0: "e0", 1: "e3", 2: "c1"}),
    ({0: "g1", 1: "e3", 2: "e0", 3: "e3"}, {0: "e1", 1: "e1", 3: "c1"}),
    ({}, {0: "g2", 1: "g3"}),
)
PLAN_ANY = (
    ({0: "a0", 1: "e0", 2: "c0", 3: "f0"}, {0: "a1", 1: "e2", 2: "c0", 3: "f0"}),
    ({0: "a1", 1: "e1", 2: "a1", 3: "e2"}, {0: "a0", 1: "a0", 2: "c1", 3: "f1"}),
    ({0: "g3", 1: "e2", 2: "c1", 3: "f1"}, {0: "e0", 1: "e3", 2: "f0", 3: "f2"}),
    ({0: "g1", 1: "e3", 2: "e0", 3: "e3"}, {0: "e1", 1: "e1", 2: "f1", 3: "f3"}),
    ({0: "c1", 1: "f2", 3: "f2"}, {0: "g2", 1: "g3", 3: "c0"}),
    ({1: "f3", 3: "f3"}, {}),
)
HOMES = {"a": 0, "c": 2, "e": 1, "f": 3, "F": 3, "g": 0}
ATTEND_BLOCKS = ((0, 1), (2, 3))
EXPERT_BLOCKS = ((0, 1), (4, 5), (2, 3), (6, 7))


def dot_plain(left, right):
    return jnp.dot(left, right, preferred_element_type=F32)


def dot_last(left, right):
    return lax.dot_general(left, right, (((1,), (1,)), ((), ())), preferred_element_type=F32)


def dot_first(left, right):
    return lax.dot_general(left, right, (((0,), (0,)), ((), ())), preferred_element_type=F32)


def column_sum(matrix):
    return jnp.sum(matrix.astype(F32), axis=0, keepdims=True)


def norm_parts(rows):
    centre = rows - jnp.mean(rows, axis=-1, keepdims=True)
    scale = lax.rsqrt(jnp.mean(centre * centre, axis=-1, keepdims=True) + 1e-06)
    return centre * scale, scale


def norm_back(normed_grad, unit, scale, gain):
    unit_grad = normed_grad * gain
    along = jnp.mean(unit_grad * unit, axis=-1, keepdims=True)
    return scale * (unit_grad - jnp.mean(unit_grad, axis=-1, keepdims=True) - unit * along)


def true_positions(length, first, count, axis, kind):
    shape = (count, 1) if axis == 0 else (1, count)
    position = first + lax.broadcasted_iota(jnp.int32, shape, axis)
    patch = position < PATCHES
    if kind == "patch":
        return patch
    caption = (position >= PATCHES) & (position - PATCHES < length)
    return caption if kind == "caption" else patch | caption


def head_masks():
    lane = lax.broadcasted_iota(jnp.int32, (1, PAIR), 1)
    even = (lane < HEAD_DIM).astype(F32).astype(BF16)
    odd = (lane >= HEAD_DIM).astype(F32).astype(BF16)
    return lane < HEAD_DIM, even, odd


def split_pair(pair, even, odd):
    return jnp.concatenate([pair * even, pair * odd], axis=0)


def start_weights(info, first, refs, plan, blocks, sems):
    half = blocks.shape[1] // 2
    section, core, plane = info[first], info[first + 1], info[first + 2]
    for at, at_plane, steps in plan:
        here = section == at
        if at_plane is not None:
            here = here & (plane == at_plane)

        @pl.when(here)
        def _(steps=steps):
            for block, source in steps:
                if source[0] == "own":
                    _, which, row, column = source
                    width = blocks.shape[2]
                    for part in range(2):
                        pltpu.make_async_copy(
                            refs[which].at[
                                pl.ds(row + part * half, half), pl.ds(column, width)
                            ],
                            blocks.at[block, pl.ds(part * half, half)],
                            sems.at[block],
                        ).start()
                else:
                    _, mine, theirs, index = source
                    pltpu.make_async_copy(
                        refs[mine].at[index],
                        blocks.at[block, pl.ds(pl.multiple_of(core * half, half), half)],
                        sems.at[block],
                    ).start()
                    pltpu.make_async_copy(
                        refs[theirs].at[index],
                        blocks.at[block, pl.ds(pl.multiple_of((1 - core) * half, half), half)],
                        sems.at[block],
                    ).start()


def wait_block(blocks, block, sems):
    pltpu.make_async_copy(blocks.at[block], blocks.at[block], sems.at[block]).wait()


def store_turned(target, turned, columns, section, core):
    half = target.shape[0] // 2
    for piece in range(16):
        path, owner = (piece >> 2) & 1, piece & 3
        away = owner ^ section
        place = ((away & 1) << 1) | (away >> 1) if path == 0 else away
        row = ((piece >> 3) ^ core) * half + (place >> 1) * (half // 2)
        row = row + path * (half // 4) + (place & 1) * PIECE_ROWS
        target[pl.ds(pl.multiple_of(row, 16), PIECE_ROWS), columns] = turned[
            piece * PIECE_ROWS : (piece + 1) * PIECE_ROWS
        ]


def put_travel(refs, which, columns, left, right):
    half = left.shape[0] // 2
    for side in range(2):
        rows = dot_plain(left[side * half : (side + 1) * half], right).astype(BF16)
        refs[2 * side][which, :, columns] = rows[: half // 2]
        refs[2 * side + 1][which, :, columns] = rows[half // 2 :]


def attend_forward_kernel(plan, weight_count, merge, info, *refs):
    weights, refs = refs[:weight_count], refs[weight_count:]
    if merge:
        x_ref, before_ref, part_ref, outer_ref, gain_ref, shift_ref, bias_ref = refs[:7]
        y_ref, qkv_ref, mixed_ref, joined_ref, blocks, sems, joined = refs[7:]
    else:
        x_ref, gain_ref, shift_ref, bias_ref, next_gain_ref, next_shift_ref = refs[:6]
        y_ref, qkv_ref, mixed_ref, caption_ref, blocks, sems = refs[6:]
    item = pl.program_id(0)
    items = pl.num_programs(0)
    length = info[item]
    width = x_ref.shape[-1]

    @pl.when(item == 0)
    def _():
        start_weights(info, items, weights, plan, blocks, sems)

    cap = slice(CAP_FIRST, CAP_FIRST + CAP_ROWS)
    if merge:
        joined[...] = x_ref[0].astype(F32)
        branch = part_ref[0].astype(F32) + outer_ref[...]
        is_true = true_positions(length, CAP_FIRST, CAP_ROWS, 0, "caption")
        captions = before_ref[0, cap] + jnp.where(is_true, branch, 0.0)
        position = CAP_FIRST + lax.broadcasted_iota(jnp.int32, (CAP_ROWS, 1), 0)
        captions = captions.astype(BF16).astype(F32)
        joined[cap] = jnp.where(position < PATCHES, joined[cap], captions)
        x = joined[...]
        joined_ref[0] = x.astype(BF16)
    else:
        x = x_ref[0].astype(F32)
    unit, _ = norm_parts(x)
    normed = (unit * gain_ref[...] + shift_ref[...]).astype(BF16)

    @pl.when(item == 0)
    def _():
        for block in range(4):
            wait_block(blocks, block, sems)

    queries = dot_plain(normed, blocks[0]) + bias_ref[:, :width]
    qkv_ref[0, :, :width] = (queries * HEAD_DIM ** (-0.5)).astype(BF16)
    qkv_ref[0, :, width : 2 * width] = dot_plain(normed, blocks[1]).astype(BF16)
    values = dot_plain(normed, blocks[2]) + bias_ref[:, width : 2 * width]
    qkv_ref[0, :, 2 * width :] = values.astype(BF16)
    key_true = true_positions(length, 0, ROWS, 1, "all")
    low_half, even, odd = head_masks()
    ones = jnp.ones((ROWS, PAIR), BF16)

    def scores_of(pair):
        at = pair * PAIR
        q2 = qkv_ref[0, :, at : at + PAIR]
        k2 = qkv_ref[0, :, width + at : width + at + PAIR]
        return dot_last(split_pair(q2, even, odd), k2)

    ahead = [scores_of(0), scores_of(1)]
    for pair in range(HEADS // 2):
        at = pair * PAIR
        scores = jnp.where(key_true, ahead.pop(0), -1e9)
        if pair + 2 < HEADS // 2:
            ahead.append(scores_of(pair + 2))
        weight = jnp.exp(scores - jnp.max(scores, axis=-1, keepdims=True)).astype(BF16)
        v2 = qkv_ref[0, :, 2 * width + at : 2 * width + at + PAIR]
        summed = dot_plain(weight, jnp.concatenate([v2, ones], axis=1))
        top = jnp.where(low_half, summed[:ROWS, :PAIR], summed[ROWS:, :PAIR])
        below = jnp.where(low_half, summed[:ROWS, PAIR:], summed[ROWS:, PAIR:])
        mixed_ref[0, :, at : at + PAIR] = (top / below).astype(BF16)
    branch = dot_plain(mixed_ref[0], blocks[3]) + bias_ref[:, 2 * width :]
    row_true = true_positions(length, 0, ROWS, 0, "all")
    y = x + jnp.where(row_true, branch, 0.0)
    y_ref[0] = y.astype(y_ref.dtype)
    if not merge:
        unit, _ = norm_parts(y[cap])
        caption_ref[0] = (unit * next_gain_ref[...] + next_shift_ref[...]).astype(BF16)


def attend_backward_kernel(plan, weight_count, first, info, *refs):
    weights, refs = refs[:weight_count], refs[weight_count:]
    x_ref, gain_ref, shift_ref, qkv_ref, mixed_ref, grad_ref = refs[:6]
    if first:
        after_ref, next_gain_ref, *parts = refs[6:12]
        refs = refs[12:]
    else:
        refs = refs[6:]
    out_ref, gain_grad_ref, shift_grad_ref, bias_grad_ref = refs[:4]
    travel_refs = refs[4:8]
    if first:
        next_gain_grad_ref, next_shift_grad_ref, joined = refs[8], refs[9], refs[-1]
    else:
        caption_ref = refs[8]
    blocks, sems, normed_turned, mixed_turned, branch_all, projected, mixed_grad = refs[
        10 if first else 9 :
    ][:7]
    item = pl.program_id(0)
    items = pl.num_programs(0)
    length = info[item]
    section, core = info[items], info[items + 1]
    width = x_ref.shape[-1]
    here = pl.ds(pl.multiple_of(item * ROWS, ROWS), ROWS)
    cap = slice(CAP_FIRST, CAP_FIRST + CAP_ROWS)

    @pl.when(item == 0)
    def _():
        start_weights(info, items, weights, plan, blocks, sems)

    def add_to(ref, part):
        @pl.when(item == 0)
        def _():
            ref[...] = part

        @pl.when(item > 0)
        def _():
            ref[...] += part

    x = x_ref[0].astype(F32)
    unit, scale = norm_parts(x)
    normed = (unit * gain_ref[...] + shift_ref[...]).astype(BF16)
    incoming = grad_ref[0].astype(F32)
    if first:
        after_unit, after_scale = norm_parts(after_ref[0, cap])
        caption_grad = parts[0][...].astype(F32)
        for part in parts[1:]:
            caption_grad = caption_grad + part[...].astype(F32)
        joined[...] = incoming
        joined[cap] += norm_back(caption_grad, after_unit, after_scale, next_gain_ref[...])
        incoming = joined[...]
        add_to(next_gain_grad_ref, jnp.sum(caption_grad * after_unit, axis=0, keepdims=True))
        add_to(next_shift_grad_ref, jnp.sum(caption_grad, axis=0, keepdims=True))
    row_true = true_positions(length, 0, ROWS, 0, "all")
    branch = jnp.where(row_true, incoming, 0.0).astype(BF16)
    branch_all[here, :] = branch
    store_turned(normed_turned, normed.T, here, section, core)
    store_turned(mixed_turned, mixed_ref[0].T, here, section, core)

    @pl.when(item == 0)
    def _():
        for block in range(4):
            wait_block(blocks, block, sems)

    mixed_grad[...] = dot_last(branch, blocks[3]).astype(BF16)
    key_true = true_positions(length, 0, ROWS, 0, "all")
    _, even, odd = head_masks()

    def products_of(pair):
        at = pair * PAIR
        q2 = split_pair(qkv_ref[0, :, at : at + PAIR], even, odd)
        k2 = qkv_ref[0, :, width + at : width + at + PAIR]
        v2 = qkv_ref[0, :, 2 * width + at : 2 * width + at + PAIR]
        g2 = split_pair(mixed_grad[:, at : at + PAIR], even, odd)
        return q2, k2, g2, dot_last(k2, q2), dot_last(v2, g2)

    ahead = [products_of(0)]
    for pair in range(HEADS // 2):
        at = pair * PAIR
        q2, k2, g2, scores, weight_grad = ahead.pop(0)
        if pair + 1 < HEADS // 2:
            ahead.append(products_of(pair + 1))
        scores = jnp.where(key_true, scores, -1e9)
        weight = jnp.exp(scores - jnp.max(scores, axis=0, keepdims=True))
        weight = weight * (1.0 / jnp.sum(weight, axis=0, keepdims=True))
        product = weight * weight_grad
        along = jnp.sum(product, axis=0, keepdims=True)
        score_grad = (product - weight * along).astype(BF16)
        values_grad = dot_plain(weight.astype(BF16), g2).astype(BF16)
        keys_grad = dot_plain(score_grad, q2).astype(BF16)
        k2_split = split_pair(k2, even, odd)
        stacked = jnp.concatenate([score_grad[:, :ROWS], score_grad[:, ROWS:]], axis=0)
        queries_grad = dot_first(stacked, k2_split).astype(BF16)
        queries_grad = (queries_grad.astype(F32) * HEAD_DIM ** (-0.5)).astype(BF16)
        projected[here, at : at + PAIR] = queries_grad
        projected[here, width + at : width + at + PAIR] = keys_grad
        projected[here, 2 * width + at : 2 * width + at + PAIR] = values_grad
    normed_grad = dot_last(projected[here, :width], blocks[0])
    normed_grad += dot_last(projected[here, width : 2 * width], blocks[1])
    normed_grad += dot_last(projected[here, 2 * width :], blocks[2])
    out = (incoming + norm_back(normed_grad, unit, scale, gain_ref[...])).astype(BF16)
    out_ref[0] = out
    if not first:
        is_true = true_positions(length, CAP_FIRST, CAP_ROWS, 0, "caption")
        caption_ref[0] = jnp.where(is_true, out[cap].astype(F32), 0.0).astype(BF16)
    add_to(gain_grad_ref, jnp.sum(normed_grad * unit, axis=0, keepdims=True))
    add_to(shift_grad_ref, jnp.sum(normed_grad, axis=0, keepdims=True))

    @pl.when(item == items - 1)
    def _():
        for block in range(4):
            columns = slice(block * width, (block + 1) * width)
            left = normed_turned if block < 3 else mixed_turned
            right = projected[:, columns] if block < 3 else branch_all[...]
            put_travel(travel_refs, 0, columns, left, right)
        bias_grad_ref[:, :width] = column_sum(projected[:, :width])
        bias_grad_ref[:, width : 2 * width] = column_sum(projected[:, 2 * width :])
        bias_grad_ref[:, 2 * width :] = column_sum(branch_all[...])


SHORT = pl.CostEstimate(flops=0, bytes_accessed=100_000, transcendentals=0)
LONG = pl.CostEstimate(flops=30_000_000_000, bytes_accessed=30_000_000, transcendentals=0)
ANYWHERE = pl.BlockSpec(memory_space=pl.ANY)


def whole_block(shape):
    return pl.BlockSpec(shape, lambda step, info: (0,) * len(shape))


def item_block(shape):
    return pl.BlockSpec((1,) + shape[1:], lambda step, info: (step,) + (0,) * (len(shape) - 1))


def blocks_scratch(count, width):
    return [pltpu.VMEM((count, width, width), BF16), pltpu.SemaphoreType.DMA((count,))]


def attend_forward(x, info, weights, gain, shift, bias, merge=None, following=None):
    arrays, plan = weights
    items, _, width = x.shape
    row = whole_block((1, width))
    bias_row = whole_block((1, 3 * width))
    caption_shape = (items, CAP_ROWS, width)
    if merge is not None:
        before, part, outer = merge
        operands = (x, before, part, outer, gain, shift, bias)
        specs = [item_block(x.shape), item_block(x.shape), item_block(caption_shape)]
        specs += [row, row, row, bias_row]
        last_shape, kind, scratch = x.shape, BF16, [pltpu.VMEM((ROWS, width), F32)]
    else:
        operands = (x, gain, shift, bias, *following)
        specs = [item_block(x.shape), row, row, bias_row, row, row]
        last_shape, kind, scratch = caption_shape, F32, []
    return pl.pallas_call(
        partial(attend_forward_kernel, plan, len(arrays), merge is not None),
        grid_spec=pltpu.PrefetchScalarGridSpec(
            num_scalar_prefetch=1,
            grid=(items,),
            in_specs=[ANYWHERE] * len(arrays) + specs,
            out_specs=[
                item_block(x.shape),
                item_block((items, ROWS, 3 * width)),
                item_block((items, ROWS, width)),
                item_block(last_shape),
            ],
            scratch_shapes=blocks_scratch(4, width) + scratch,
        ),
        out_shape=[
            jax.ShapeDtypeStruct(x.shape, kind),
            jax.ShapeDtypeStruct((items, ROWS, 3 * width), BF16),
            jax.ShapeDtypeStruct((items, ROWS, width), BF16),
            jax.ShapeDtypeStruct(last_shape, BF16),
        ],
        compiler_params=pltpu.CompilerParams(vmem_limit_bytes=VMEM_BYTES),
        cost_estimate=SHORT,
        name="attend_forward",
    )(info, *arrays, *operands)


def attend_backward(x, info, weights, gain, shift, qkv, mixed, incoming, first=None):
    arrays, plan = weights
    items, _, width = x.shape
    half = width // 2
    row = whole_block((1, width))
    caption_shape = (items, CAP_ROWS, width)
    operands = (x, gain, shift, qkv, mixed, incoming)
    specs = [item_block(x.shape), row, row, item_block(qkv.shape), item_block(mixed.shape)]
    specs += [item_block(incoming.shape)]
    outs = [
        (item_block(x.shape), x.shape, BF16),
        (row, (1, width), F32),
        (row, (1, width), F32),
        (whole_block((1, 3 * width)), (1, 3 * width), F32),
    ]
    outs += [(whole_block((1, half // 2, 4 * width)), (1, half // 2, 4 * width), BF16)] * 4
    scratch = []
    if first is not None:
        after, next_gain, parts = first
        operands += (after, next_gain, *parts)
        caption_rows = pl.BlockSpec((CAP_ROWS, width), lambda step, info: (step, 0))
        specs += [item_block(after.shape), row] + [caption_rows] * 4
        outs += [(row, (1, width), F32)] * 2
        scratch = [pltpu.VMEM((ROWS, width), F32)]
    else:
        outs += [(item_block(caption_shape), caption_shape, BF16)]
    return pl.pallas_call(
        partial(attend_backward_kernel, plan, len(arrays), first is not None),
        grid_spec=pltpu.PrefetchScalarGridSpec(
            num_scalar_prefetch=1,
            grid=(items,),
            in_specs=[ANYWHERE] * len(arrays) + specs,
            out_specs=[spec for spec, _, _ in outs],
            scratch_shapes=blocks_scratch(4, width)
            + [
                pltpu.VMEM((width, items * ROWS), BF16),
                pltpu.VMEM((width, items * ROWS), BF16),
                pltpu.VMEM((items * ROWS, width), BF16),
                pltpu.VMEM((items * ROWS, 3 * width), BF16),
                pltpu.VMEM((ROWS, width), BF16),
            ]
            + scratch,
        ),
        out_shape=[jax.ShapeDtypeStruct(shape, kind) for _, shape, kind in outs],
        compiler_params=pltpu.CompilerParams(vmem_limit_bytes=VMEM_BYTES),
        cost_estimate=LONG,
        name="attend_backward",
    )(info, *arrays, *operands)


def normal_parts(u):
    t = pl.reciprocal(1.0 + 0.23164190 * jnp.abs(u), approx=True)
    bell = jnp.exp2((u * -0.7213475204444817) * u)
    poly = t * (
        0.127414796
        + t * (-0.142248368 + t * (0.7107068705 + t * (-0.7265760135 + t * 0.5307027145)))
    )
    tail = poly * bell
    return jnp.where(u < 0, tail, 1.0 - tail), bell


def inner_forward(normed, matrix, bias):
    inner = dot_plain(normed, matrix) + bias
    cumulative, bell = normal_parts(inner)
    slope = cumulative + (inner * 0.3989422804014327) * bell
    return (inner * cumulative).astype(BF16), slope.astype(BF16)


def expert_forward_kernel(plan, weight_count, count, kind, info, *refs):
    weights, refs = refs[:weight_count], refs[weight_count:]
    x_ref, gain_ref, shift_ref, inner_ref, outer_ref = refs[:5]
    y_ref, act_ref, slope_ref, blocks, sems, normed, total = refs[5:]
    step = pl.program_id(0)
    items, _, width = x_ref.shape
    used = items * count

    @pl.when(step == 0)
    def _():
        start_weights(info, items, weights, plan, blocks, sems)
        for item in range(items):
            x = x_ref[item, :count].astype(BF16).astype(F32)
            unit, _ = norm_parts(x)
            normed[item * count : (item + 1) * count] = (
                unit * gain_ref[...] + shift_ref[...]
            ).astype(BF16)

    wait_block(blocks, step, sems)
    wait_block(blocks, step + 4, sems)
    for at in range(0, width, 256):
        columns = slice(at, at + 256)
        act, slope = inner_forward(normed[...], blocks[step, :, columns], inner_ref[:, columns])
        act_ref[:used, columns] = act
        slope_ref[:, columns] = slope
    if used < act_ref.shape[0]:
        act_ref[used:] = jnp.zeros((act_ref.shape[0] - used, width), BF16)
    part = dot_plain(act_ref[:used], blocks[step + 4])

    @pl.when(step == 0)
    def _():
        total[...] = part

    @pl.when(step > 0)
    def _():
        total[...] += part

    @pl.when(step == pl.num_programs(0) - 1)
    def _():
        for item in range(items):
            row_true = true_positions(info[item], 0, count, 0, kind)
            branch = total[item * count : (item + 1) * count] + outer_ref[...]
            x = x_ref[item, :count].astype(BF16).astype(F32)
            y_ref[item, :count] = (x + jnp.where(row_true, branch, 0.0)).astype(BF16)
            if count < ROWS:
                y_ref[item, count:] = jnp.zeros((ROWS - count, width), BF16)


def expert_backward_kernel(plan, weight_count, count, kind, info, *refs):
    weights, refs = refs[:weight_count], refs[weight_count:]
    x_ref, gain_ref, shift_ref, act_ref, slope_ref, grad_ref = refs[:6]
    out_ref, gain_grad_ref, shift_grad_ref, inner_grad_ref, outer_grad_ref = refs[6:11]
    travel_refs = refs[11:15]
    blocks, sems, normed_turned, branch_turned, branch, inner_all, total = refs[15:]
    step = pl.program_id(0)
    items, _, width = x_ref.shape
    section, core = info[items], info[items + 1]

    @pl.when(step == 0)
    def _():
        start_weights(info, items, weights, plan, blocks, sems)
        outer = None
        for item in range(items):
            here = slice(item * count, (item + 1) * count)
            unit, _ = norm_parts(x_ref[item, :count].astype(BF16).astype(F32))
            normed = (unit * gain_ref[...] + shift_ref[...]).astype(BF16)
            row_true = true_positions(info[item], 0, count, 0, kind)
            incoming = grad_ref[item, :count].astype(F32)
            masked = jnp.where(row_true, incoming, 0.0).astype(BF16)
            branch[here] = masked
            store_turned(normed_turned, normed.T, here, section, core)
            store_turned(branch_turned, masked.T, here, section, core)
            term = column_sum(masked)
            outer = term if outer is None else outer + term
        outer_grad_ref[...] = outer

    wait_block(blocks, step, sems)
    wait_block(blocks, step + 4, sems)
    for at in range(0, width, 256):
        columns = slice(at, at + 256)
        act_grad = dot_last(branch[...], blocks[step + 4, columns])
        inner = (slope_ref[:, columns].astype(F32) * act_grad).astype(BF16)
        inner_all[:, columns] = inner
        inner_grad_ref[:, columns] = column_sum(inner)
        put_travel(travel_refs, 0, columns, normed_turned, inner)
        put_travel(travel_refs, 1, columns, branch_turned, act_ref[:, columns])
    part = dot_last(inner_all[...], blocks[step])

    @pl.when(step == 0)
    def _():
        total[...] = part

    @pl.when(step > 0)
    def _():
        total[...] += part

    @pl.when(step == pl.num_programs(0) - 1)
    def _():
        gain_sum, shift_sum = None, None
        for item in range(items):
            unit, scale = norm_parts(x_ref[item, :count].astype(BF16).astype(F32))
            normed_grad = total[item * count : (item + 1) * count]
            gain_part = jnp.sum(normed_grad * unit, axis=0, keepdims=True)
            shift_part = jnp.sum(normed_grad, axis=0, keepdims=True)
            gain_sum = gain_part if gain_sum is None else gain_sum + gain_part
            shift_sum = shift_part if shift_sum is None else shift_sum + shift_part
            incoming = grad_ref[item, :count].astype(F32)
            hidden = incoming + norm_back(normed_grad, unit, scale, gain_ref[...])
            out_ref[item, :count] = hidden.astype(BF16)
            if count < ROWS:
                out_ref[item, count:] = grad_ref[item, count:]
        gain_grad_ref[...] = gain_sum
        shift_grad_ref[...] = shift_sum


def expert_back_kernel(plan, weight_count, count, kind, info, *refs):
    weights, refs = refs[:weight_count], refs[weight_count:]
    x_ref, gain_ref, shift_ref, slope_ref, grad_ref = refs[:5]
    out_ref, gain_grad_ref, shift_grad_ref, inner_grad_ref, outer_grad_ref = refs[5:10]
    inner_ref, normed_turned_ref, branch_turned_ref = refs[10:13]
    blocks, sems, normed, branch, total = refs[13:]
    step = pl.program_id(0)
    items, _, width = x_ref.shape
    section, core = info[items], info[items + 1]
    used, rows = items * count, normed.shape[0]

    @pl.when(step == 0)
    def _():
        start_weights(info, items, weights, plan, blocks, sems)
        outer = None
        for item in range(items):
            here = slice(item * count, (item + 1) * count)
            unit, _ = norm_parts(x_ref[item, :count].astype(BF16).astype(F32))
            normed[here] = (unit * gain_ref[...] + shift_ref[...]).astype(BF16)
            row_true = true_positions(info[item], 0, count, 0, kind)
            incoming = grad_ref[item, :count].astype(F32)
            masked = jnp.where(row_true, incoming, 0.0).astype(BF16)
            branch[here] = masked
            term = column_sum(masked)
            outer = term if outer is None else outer + term
        outer_grad_ref[...] = outer
        normed[used:] = jnp.zeros((rows - used, width), BF16)
        branch[used:] = jnp.zeros((rows - used, width), BF16)
        store_turned(normed_turned_ref, normed[...].T, slice(0, rows), section, core)
        store_turned(branch_turned_ref, branch[...].T, slice(0, rows), section, core)

    wait_block(blocks, step, sems)
    wait_block(blocks, step + 4, sems)
    for at in range(0, width, 256):
        columns = slice(at, at + 256)
        act_grad = dot_last(branch[:used], blocks[step + 4, columns])
        inner = (slope_ref[:, columns].astype(F32) * act_grad).astype(BF16)
        inner_ref[:used, columns] = inner
        inner_ref[used:, columns] = jnp.zeros((rows - used, 256), BF16)
        inner_grad_ref[:, columns] = column_sum(inner)
    part = dot_last(inner_ref[:used], blocks[step])

    @pl.when(step == 0)
    def _():
        total[...] = part

    @pl.when(step > 0)
    def _():
        total[...] += part

    @pl.when(step == pl.num_programs(0) - 1)
    def _():
        gain_sum, shift_sum = None, None
        for item in range(items):
            unit, scale = norm_parts(x_ref[item, :count].astype(BF16).astype(F32))
            normed_grad = total[item * count : (item + 1) * count]
            gain_part = jnp.sum(normed_grad * unit, axis=0, keepdims=True)
            shift_part = jnp.sum(normed_grad, axis=0, keepdims=True)
            gain_sum = gain_part if gain_sum is None else gain_sum + gain_part
            shift_sum = shift_part if shift_sum is None else shift_sum + shift_part
            incoming = grad_ref[item, :count].astype(F32)
            hidden = incoming + norm_back(normed_grad, unit, scale, gain_ref[...])
            out_ref[item, :count] = hidden.astype(BF16)
            if count < ROWS:
                out_ref[item, count:] = grad_ref[item, count:]
        gain_grad_ref[...] = gain_sum
        shift_grad_ref[...] = shift_sum


def expert_weights_kernel(normed_turned_ref, branch_turned_ref, inner_ref, act_ref, *travel_refs):
    width = inner_ref.shape[1]
    for at in range(0, width, 256):
        columns = slice(at, at + 256)
        put_travel(travel_refs, 0, columns, normed_turned_ref, inner_ref[:, columns])
        put_travel(travel_refs, 1, columns, branch_turned_ref, act_ref[:, columns])


def shared_forward_kernel(*refs):
    *rows_refs, inputs_ref, inner_ref, outputs_ref = refs[:7]
    *part_refs, normed, total = refs[7:]
    count = rows_refs[0].shape[0]
    step = pl.program_id(0)

    @pl.when(step == 0)
    def _():
        for index, ref in enumerate(rows_refs):
            normed[index * count : (index + 1) * count] = ref[...]
        total[...] = jnp.zeros_like(total)

    act, _ = inner_forward(normed[...], inputs_ref[...], inner_ref[...])
    total[...] += dot_plain(act, outputs_ref[...])

    @pl.when(step == pl.num_programs(0) - 1)
    def _():
        for index, ref in enumerate(part_refs):
            ref[...] = total[index * count : (index + 1) * count].astype(BF16)


def shared_backward_kernel(plan, weight_count, info, *refs):
    weights, refs = refs[:weight_count], refs[weight_count:]
    rows_refs, grad_refs, inner_ref = refs[:4], refs[4:8], refs[8]
    part_refs, (keep_ref, send_ref, inner_grad_ref, outer_grad_ref) = refs[9:13], refs[13:17]
    blocks, sems, normed, branch, matrix = refs[17:]
    count, width = rows_refs[0].shape
    half = width // 2
    first = info.shape[0] - 3
    core = info[first + 1]
    start_weights(info, first, weights, plan, blocks, sems)
    for index in range(SECTIONS):
        here = slice(index * count, (index + 1) * count)
        normed[here] = rows_refs[index][...]
        branch[here] = grad_refs[index][...]
    outer_grad_ref[...] = column_sum(grad_refs[0][...])
    wait_block(blocks, 0, sems)
    wait_block(blocks, 1, sems)
    part = None
    for at in range(0, width, 256):
        columns = slice(at, at + 256)
        act, slope = inner_forward(normed[...], blocks[0, :, columns], inner_ref[:, columns])
        act_grad = dot_last(branch[...], blocks[1, columns])
        inner = (slope.astype(F32) * act_grad).astype(BF16)
        inner_grad_ref[:, columns] = column_sum(inner)
        matrix[0, :, columns] = dot_first(normed[...], inner).astype(BF16)
        matrix[1, :, columns] = dot_first(branch[...], act).astype(BF16)
        term = dot_last(inner, blocks[0, :, columns])
        part = term if part is None else part + term
    for index, ref in enumerate(part_refs):
        ref[...] = part[index * count : (index + 1) * count].astype(BF16)
    quarter = half // 4
    for which in range(2):
        for group in range(4):
            columns = slice(group * width, (group + 1) * width)
            mine = pl.multiple_of(core * half, 16) + group * quarter
            other = pl.multiple_of((1 - core) * half, 16) + group * quarter
            keep_ref[which, :, columns] = matrix[which, pl.ds(pl.multiple_of(mine, 16), quarter)]
            send_ref[which, :, columns] = matrix[which, pl.ds(pl.multiple_of(other, 16), quarter)]


def chunk_columns(rows, width):
    return pl.BlockSpec((rows, width), lambda step, info: (0, step))


def expert_forward(x, info, weights, gain, shift, inner, outer, count, kind):
    arrays, plan = weights
    items, _, width = x.shape
    hidden = inner.shape[1]
    rows = -(-items * count // 128) * 128
    row = whole_block((1, width))
    return pl.pallas_call(
        partial(expert_forward_kernel, plan, len(arrays), count, kind),
        grid_spec=pltpu.PrefetchScalarGridSpec(
            num_scalar_prefetch=1,
            grid=(hidden // width,),
            in_specs=[ANYWHERE] * len(arrays)
            + [whole_block(x.shape), row, row, chunk_columns(1, width), row],
            out_specs=[
                whole_block((items, ROWS, width)),
                chunk_columns(rows, width),
                chunk_columns(items * count, width),
            ],
            scratch_shapes=blocks_scratch(8, width)
            + [
                pltpu.VMEM((items * count, width), BF16),
                pltpu.VMEM((items * count, width), F32),
            ],
        ),
        out_shape=[
            jax.ShapeDtypeStruct((items, ROWS, width), BF16),
            jax.ShapeDtypeStruct((rows, hidden), BF16),
            jax.ShapeDtypeStruct((items * count, hidden), BF16),
        ],
        compiler_params=pltpu.CompilerParams(vmem_limit_bytes=VMEM_BYTES),
        cost_estimate=SHORT,
        name="expert_forward_" + kind,
    )(info, *arrays, x, gain, shift, inner, outer)


def expert_backward(x, info, weights, gain, shift, act, slope, incoming, count, kind):
    arrays, plan = weights
    items, _, width = x.shape
    half = width // 2
    hidden = act.shape[1]
    row = whole_block((1, width))
    travel = pl.BlockSpec((2, half // 2, width), lambda step, info: (0, 0, step))
    return pl.pallas_call(
        partial(expert_backward_kernel, plan, len(arrays), count, kind),
        grid_spec=pltpu.PrefetchScalarGridSpec(
            num_scalar_prefetch=1,
            grid=(hidden // width,),
            in_specs=[ANYWHERE] * len(arrays)
            + [
                whole_block(x.shape),
                row,
                row,
                chunk_columns(items * count, width),
                chunk_columns(items * count, width),
                whole_block(incoming.shape),
            ],
            out_specs=[whole_block(incoming.shape), row, row, chunk_columns(1, width), row]
            + [travel] * 4,
            scratch_shapes=blocks_scratch(8, width)
            + [
                pltpu.VMEM((width, items * count), BF16),
                pltpu.VMEM((width, items * count), BF16),
                pltpu.VMEM((items * count, width), BF16),
                pltpu.VMEM((items * count, width), BF16),
                pltpu.VMEM((items * count, width), F32),
            ],
        ),
        out_shape=[
            jax.ShapeDtypeStruct(incoming.shape, BF16),
            jax.ShapeDtypeStruct((1, width), F32),
            jax.ShapeDtypeStruct((1, width), F32),
            jax.ShapeDtypeStruct((1, hidden), F32),
            jax.ShapeDtypeStruct((1, width), F32),
        ]
        + [jax.ShapeDtypeStruct((2, half // 2, hidden), BF16)] * 4,
        compiler_params=pltpu.CompilerParams(vmem_limit_bytes=VMEM_BYTES),
        cost_estimate=SHORT,
        name="expert_backward_" + kind,
    )(info, *arrays, x, gain, shift, act, slope, incoming)


def expert_back(x, info, weights, gain, shift, slope, incoming, count, kind):
    arrays, plan = weights
    items, _, width = x.shape
    hidden = slope.shape[1]
    used = items * count
    rows = -(-used // 128) * 128
    row = whole_block((1, width))
    turned = whole_block((width, rows))
    return pl.pallas_call(
        partial(expert_back_kernel, plan, len(arrays), count, kind),
        grid_spec=pltpu.PrefetchScalarGridSpec(
            num_scalar_prefetch=1,
            grid=(hidden // width,),
            in_specs=[ANYWHERE] * len(arrays)
            + [
                whole_block(x.shape),
                row,
                row,
                chunk_columns(used, width),
                whole_block(incoming.shape),
            ],
            out_specs=[whole_block(incoming.shape), row, row, chunk_columns(1, width), row]
            + [chunk_columns(rows, width), turned, turned],
            scratch_shapes=blocks_scratch(8, width)
            + [
                pltpu.VMEM((rows, width), BF16),
                pltpu.VMEM((rows, width), BF16),
                pltpu.VMEM((used, width), F32),
            ],
        ),
        out_shape=[
            jax.ShapeDtypeStruct(incoming.shape, BF16),
            jax.ShapeDtypeStruct((1, width), F32),
            jax.ShapeDtypeStruct((1, width), F32),
            jax.ShapeDtypeStruct((1, hidden), F32),
            jax.ShapeDtypeStruct((1, width), F32),
            jax.ShapeDtypeStruct((rows, hidden), BF16),
            jax.ShapeDtypeStruct((width, rows), BF16),
            jax.ShapeDtypeStruct((width, rows), BF16),
        ],
        compiler_params=pltpu.CompilerParams(vmem_limit_bytes=VMEM_BYTES),
        cost_estimate=SHORT,
        name="expert_back_" + kind,
    )(info, *arrays, x, gain, shift, slope, incoming)


def expert_weights(normed_turned, branch_turned, inner, act):
    width, rows = normed_turned.shape
    hidden = inner.shape[1]
    turned = pl.BlockSpec((width, rows), lambda step: (0, 0))
    columns = pl.BlockSpec((rows, width), lambda step: (0, step))
    travel = pl.BlockSpec((2, width // 4, width), lambda step: (0, 0, step))
    return pl.pallas_call(
        expert_weights_kernel,
        grid=(hidden // width,),
        in_specs=[turned, turned, columns, columns],
        out_specs=[travel] * 4,
        out_shape=[jax.ShapeDtypeStruct((2, width // 4, hidden), BF16)] * 4,
        compiler_params=pltpu.CompilerParams(vmem_limit_bytes=VMEM_BYTES),
        cost_estimate=SHORT,
        name="expert_weights",
    )(normed_turned, branch_turned, inner, act)


IN_VMEM = pl.BlockSpec(memory_space=pltpu.VMEM)
IN_SMEM = pl.BlockSpec(memory_space=pltpu.SMEM)


def shared_forward(rows, inputs, inner, outputs):
    count, width = rows[0].shape
    total = SECTIONS * count
    hidden = inner.shape[1]
    return pl.pallas_call(
        shared_forward_kernel,
        grid=(hidden // width,),
        in_specs=[pl.BlockSpec(rows[0].shape, lambda step: (0, 0))] * 4
        + [
            pl.BlockSpec((width, width), lambda step: (0, step)),
            pl.BlockSpec((1, width), lambda step: (0, step)),
            pl.BlockSpec((width, width), lambda step: (step, 0)),
        ],
        out_specs=[pl.BlockSpec((count, width), lambda step: (0, 0))] * SECTIONS,
        scratch_shapes=[pltpu.VMEM((total, width), BF16), pltpu.VMEM((total, width), F32)],
        out_shape=[jax.ShapeDtypeStruct((count, width), BF16)] * SECTIONS,
        compiler_params=pltpu.CompilerParams(vmem_limit_bytes=VMEM_BYTES),
        cost_estimate=SHORT,
        name="shared_forward",
    )(*rows, inputs, inner, outputs)


def shared_backward(rows, grads, info, weights, inner):
    arrays, plan = weights
    count, width = rows[0].shape
    total = SECTIONS * count
    travel = (2, width // 8, 4 * width)
    return pl.pallas_call(
        partial(shared_backward_kernel, plan, len(arrays)),
        in_specs=[IN_SMEM] + [ANYWHERE] * len(arrays) + [IN_VMEM] * 9,
        out_specs=[IN_VMEM] * 8,
        scratch_shapes=blocks_scratch(2, width)
        + [
            pltpu.VMEM((total, width), BF16),
            pltpu.VMEM((total, width), BF16),
            pltpu.VMEM((2, width, width), BF16),
        ],
        out_shape=[
            *[jax.ShapeDtypeStruct((count, width), BF16)] * SECTIONS,
            jax.ShapeDtypeStruct(travel, BF16),
            jax.ShapeDtypeStruct(travel, BF16),
            jax.ShapeDtypeStruct((1, width), F32),
            jax.ShapeDtypeStruct((1, width), F32),
        ],
        compiler_params=pltpu.CompilerParams(vmem_limit_bytes=VMEM_BYTES),
        cost_estimate=SHORT,
        name="shared_backward",
    )(info, *arrays, *rows, *grads, inner)


def plane_turn(plane, planes):
    return ((plane & 1) << 1) | (plane >> 1) if planes == 4 else 0


def finish_kernel(planes, info, scale_ref, mine_ref, theirs_ref, *refs):
    step = pl.program_id(0)
    count = mine_ref.shape[1]
    placed = refs[-1]
    outs = refs[:-1]
    width = placed.shape[1]
    half = width // 2
    at = info.shape[0] - 3
    section, core = info[at], info[at + 1]
    turn = plane_turn(info[at + 2], planes)
    turned = turn if count == 1 else jnp.where(section == 1, turn, 0)
    scale = scale_ref[0, 0]
    columns = pl.ds(pl.multiple_of((step ^ turned) * width, width), width)

    def place(which):
        def by_rows():
            for side, ref in enumerate((mine_ref, theirs_ref)):
                for away in range(SECTIONS):
                    for path in range(2):
                        row = (core ^ side) * half + path * (half // 2)
                        row = row + (section ^ away) * PIECE_ROWS
                        placed[pl.ds(pl.multiple_of(row, 16), PIECE_ROWS), :] = ref[
                            away, which, path * PIECE_ROWS : (path + 1) * PIECE_ROWS, columns
                        ].astype(F32)

        def by_columns():
            for side, ref in enumerate((mine_ref, theirs_ref)):
                for group in range(4):
                    quarter = half // 4
                    row = (core ^ side) * half + group * quarter
                    placed[pl.ds(pl.multiple_of(row, 16), quarter), :] = ref[
                        step, which, :, group * width : (group + 1) * width
                    ].astype(F32)

        if count == 1:
            by_rows()
        else:
            pl.when(section != 0)(by_rows)
            pl.when(section == 0)(by_columns)

    place(0)
    if count == 1:

        @pl.when(step < 3)
        def _():
            outs[0][0] = placed[...] / scale

        @pl.when(step == 3)
        def _():
            outs[1][0] = placed[...] / scale

    else:
        outs[0][0] = placed[...] / scale
        place(1)
        outs[1][0] = (placed[...] / scale).T


def finish(info, scale, mine, theirs, planes):
    count, hidden = mine.shape[1], mine.shape[3]
    width = hidden // 4
    if count == 1:
        shapes = [(1, width, 3 * width), (1, width, width)]
        maps = [lambda step, info: (0, 0, jnp.minimum(step, 2)), lambda step, info: (0, 0, 0)]
    else:
        shapes = [(1, width, hidden), (1, hidden, width)]
        maps = [lambda step, info: (0, 0, step), lambda step, info: (0, step, 0)]
    return pl.pallas_call(
        partial(finish_kernel, planes),
        grid_spec=pltpu.PrefetchScalarGridSpec(
            num_scalar_prefetch=1,
            grid=(4,),
            in_specs=[IN_SMEM, whole_block(mine.shape), whole_block(mine.shape)],
            out_specs=[pl.BlockSpec((1, width, width), at) for at in maps],
            scratch_shapes=[pltpu.VMEM((width, width), F32)],
        ),
        out_shape=[jax.ShapeDtypeStruct(shape, F32) for shape in shapes],
        compiler_params=pltpu.CompilerParams(vmem_limit_bytes=VMEM_BYTES),
        cost_estimate=SHORT,
        name="finish",
    )(info, scale, mine, theirs)


def pack_kernel(count, plan, info, *refs):
    sources, outs, sems = refs[:count], refs[count:-1], refs[-1]
    first = info.shape[0] - 3
    section, core, plane = info[first], info[first + 1], info[first + 2]
    half = outs[0].shape[1]
    for index, (out, choices) in enumerate(zip(outs, plan)):
        for at, at_plane, parts in choices:
            here = section == at
            if at_plane is not None:
                here = here & (plane == at_plane)

            @pl.when(here)
            def _(index=index, out=out, parts=parts):
                for block, part in enumerate(parts):
                    if part[0] == "own":
                        _, which, row, column = part
                        rows = pl.ds(pl.multiple_of(row + core * half, half), half)
                        source = sources[which].at[rows, pl.ds(column, out.shape[2])]
                    else:
                        source = sources[part[1]].at[block]
                    pltpu.make_async_copy(source, out.at[block], sems.at[index, block]).start()

    for index, out in enumerate(outs):
        for block in range(2):
            pltpu.make_async_copy(out.at[block], out.at[block], sems.at[index, block]).wait()


def pack(info, sources, plan, shape):
    return pl.pallas_call(
        partial(pack_kernel, len(sources), plan),
        in_specs=[IN_SMEM] + [ANYWHERE] * len(sources),
        out_specs=[IN_VMEM] * len(plan),
        scratch_shapes=[pltpu.SemaphoreType.DMA((len(plan), 2))],
        out_shape=[jax.ShapeDtypeStruct(shape, BF16)] * len(plan),
        cost_estimate=SHORT,
        name="pack",
    )(info, *sources)


def over_section(value, bits, sources=range(SECTIONS)):
    return lax.ppermute(value, "section", [(at, at ^ bits) for at in sources])


def over_core(value):
    return lax.ppermute(value, "core", [(0, 1), (1, 0)])


def over_plane(value, pairs):
    return lax.ppermute(value, "z", pairs)


def added(left, right):
    return (left.astype(F32) + right.astype(F32)).astype(BF16)


def after(value, *earlier):
    return lax.optimization_barrier((value,) + earlier)[0]


def under(outputs, *arrivals):
    joined = lax.optimization_barrier(tuple(outputs) + arrivals)
    return list(joined[: len(outputs)]), list(joined[len(outputs) :])


def by_section(section, values):
    result, last = None, None
    for at in sorted(values):
        if result is None:
            result = values[at]
        elif values[at] is not last:
            result = jnp.where(section >= at, values[at], result)
        last = values[at]
    return result


def total(*values):
    result = values[0].astype(F32)
    for value in values[1:]:
        result = result + value.astype(F32)
    return result.astype(BF16)


class Sums:
    def __init__(self, travel):
        self.stay, self.move, self.other_stay, self.other_move = travel
        self.size = self.stay.shape[1] // 2

    def cross(self, *earlier):
        if earlier:
            self.other_move = after(self.other_move, *earlier)
            self.other_stay = after(self.other_stay, *earlier)
        self.got_move, self.got_stay = over_core(self.other_move), over_core(self.other_stay)

    def first_sends(self):
        size = self.size
        self.sent = [
            total(self.move[:, at : at + size], self.got_move[:, at : at + size])
            for at in (0, size)
        ]
        return self.sent

    def second_sends(self, from_x, from_y):
        size, half = self.size, self.size // 2
        self.first = from_x, from_y
        to_y = total(self.stay[:, half:size], self.got_stay[:, half:size], from_x[:, half:])
        to_x = total(
            self.stay[:, size + half :], self.got_stay[:, size + half :], from_y[:, half:]
        )
        self.sent = [to_x, to_y]
        return self.sent

    def whole(self, from_x, from_y):
        size, half = self.size, self.size // 2
        parts = []
        for at, first, second in ((0, self.first[0], from_y), (size, self.first[1], from_x)):
            here = slice(at, at + half)
            parts.append(total(self.stay[:, here], self.got_stay[:, here], first[:, :half], second))
        return jnp.concatenate(parts, axis=1)


def over_links(sends):
    return [over_section(sends[0], 1), over_section(sends[1], 2)]


class Planes:
    def __init__(self, value, plane, planes):
        self.value, self.plane, self.planes, self.turn = value, plane, planes, 0

    def sends(self, *earlier):
        value = after(self.value, *earlier) if earlier else self.value
        if self.planes != 4:
            return (value,)
        bits = (1, 2, 2, 1)[self.turn]
        if self.turn < 2:
            bit = (self.plane & 1, self.plane >> 1)[self.turn]
            size = value.shape[-1] // 2
            value = lax.dynamic_slice_in_dim(value, (1 - bit) * size, size, value.ndim - 1)
        return (over_plane(value, [(at, at ^ bits) for at in range(4)]),)

    def take(self, arrived):
        if self.planes != 4:
            self.value = lax.psum(arrived, "z") if self.turn == 3 else arrived
        elif self.turn < 2:
            bit = (self.plane & 1, self.plane >> 1)[self.turn]
            size = self.value.shape[-1] // 2
            keep = lax.dynamic_slice_in_dim(self.value, bit * size, size, self.value.ndim - 1)
            self.value = added(keep, arrived)
        else:
            self.value = jnp.concatenate([self.value, arrived], axis=-1)
        self.turn += 1

    def in_order(self, value):
        if self.planes != 4:
            return value
        size, turn = value.shape[-1] // 4, plane_turn(self.plane, 4)
        parts = [
            lax.dynamic_slice_in_dim(value, (at ^ turn) * size, size, value.ndim - 1)
            for at in range(4)
        ]
        return jnp.concatenate(parts, axis=-1)


class Weights:
    def __init__(self, own, info, planes):
        self.own, self.info = own, info
        self.four = planes == 4
        self.plan = PLAN_FOUR if self.four else PLAN_ANY
        self.half, self.width = own[1].shape[0] // 2, own[1].shape[1]
        self.mine, self.theirs, self.arrived = {}, {}, {}

    def place(self, layer, block):
        if layer in "ac":
            return (0, 0, block * self.width) if block < 3 else (1, 0, 0)
        if layer == "g":
            return (2, 0, block * self.width) if block < 4 else (3, (block - 4) * self.width, 0)
        return (2, 0, block * self.width) if block < 4 else (3, (block - 4) * self.width, 0)

    def choices(self, sends, sources):
        result = []
        for at in range(SECTIONS):
            name = sends.get(at)
            if name is not None and HOMES[name[0]] != at:
                key = self.arrived[at, name]
                if key not in sources:
                    sources[key] = len(self.own) + len(sources)
                result.append((at, None, [("arrived", sources[key])] * 2))
                continue
            for plane in range(4) if name == "F" else (None,):
                piece = ("f" + str(plane)) if name == "F" else name or "a0"
                layer, index = piece[0], int(piece[1])
                if layer in "ac":
                    blocks = ATTEND_BLOCKS[index]
                else:
                    blocks = (index, 4 + index) if layer == "g" else EXPERT_BLOCKS[index]
                parts = [("own",) + self.place(layer, block) for block in blocks]
                result.append((at, plane, parts))
        return result

    def packed(self, wanted):
        sources = {}
        plan = [self.choices(sends, sources) for sends in wanted]
        arrays = list(self.own) + [self.mine[key] for key in sources]
        return pack(self.info, arrays, plan, (2, self.half, self.width))

    def sends(self, step):
        if step == "F":
            return [{at: "F" for at in range(SECTIONS)}]
        return [sends for sends in self.plan[step] if sends]

    def payloads(self, *steps):
        wanted = [sends for step in steps for sends in self.sends(step)]
        return list(self.packed(wanted))

    def move(self, step, payloads):
        links = [(link, sends) for link, sends in enumerate(self.plan[step]) if sends]
        for (link, sends), payload in zip(links, payloads):
            self.mine[step, link] = over_section(payload, link + 1, sorted(sends))
            for at, name in sends.items():
                self.arrived[at ^ (link + 1), name] = (step, link)
        return [(step, link) for link, _ in links]

    def move_planes(self, step):
        up, down = self.mine["plane", step - 1], self.mine["plane", 1 - step]
        up = over_plane(up, [(at, at + 1) for at in range(step - 1, 3)])
        down = over_plane(down, [(at, at - 1) for at in range(4 - step, 0, -1)])
        self.mine["plane", step], self.mine["plane", -step] = up, down
        return [("plane", step), ("plane", -step)]

    def cross(self, keys):
        for key in keys:
            self.theirs[key] = over_core(self.mine[key])
        return keys

    def join(self, outputs, mine=(), theirs=()):
        values = [self.mine[key] for key in mine] + [self.theirs[key] for key in theirs]
        outputs, values = under(outputs, *values)
        for key, value in zip(mine, values):
            self.mine[key] = value
        for key, value in zip(theirs, values[len(mine) :]):
            self.theirs[key] = value
        return outputs

    def layer(self, layer):
        arrays, places = list(self.own), {}

        def place(key):
            if key not in places:
                places[key] = len(arrays)
                arrays.extend([self.mine[key], self.theirs[key]])
            return places[key], places[key] + 1

        if layer in "ac":
            names = [(layer + str(index), ATTEND_BLOCKS[index]) for index in range(2)]
        else:
            names = [(layer + str(index), EXPERT_BLOCKS[index]) for index in range(4)]
        plan = []
        for at in range(SECTIONS):
            if layer == "g":
                names = [("g" + str(at), (0, 1))]
            if HOMES[layer] == at:
                steps = []
                for name, blocks in names:
                    for block in blocks:
                        source = block * 4 if layer == "g" else block
                        steps.append((block, ("own",) + self.place(layer, source)))
                plan.append((at, None, steps))
                continue
            by_plane = layer == "f" and self.four
            for plane in range(4) if by_plane else (None,):
                steps = []
                for index, (name, blocks) in enumerate(names):
                    key = ("plane", plane - index) if by_plane else self.arrived[at, name]
                    for which, block in enumerate(blocks):
                        steps.append((block, ("piece",) + place(key) + (which,)))
                plan.append((at, plane, steps))
        return arrays, plan


def per_device(
    tokens,
    caption_lengths,
    attend_gain,
    attend_shift,
    attend_inputs,
    attend_bias,
    attend_output,
    expert_gain,
    expert_shift,
    expert_inputs,
    expert_inner_bias,
    expert_outputs,
    expert_outer_bias,
    cotangent,
):
    section, core, plane = lax.axis_index("section"), lax.axis_index("core"), lax.axis_index("z")
    planes = lax.axis_size("z")
    items, positions, width = tokens.shape
    hidden = expert_inputs.shape[-1]
    info = [value.reshape(1).astype(jnp.int32) for value in (section, core, plane)]
    info = jnp.concatenate([caption_lengths] + info)
    weights = Weights(
        (attend_inputs[0], attend_output[0], expert_inputs[0], expert_outputs[0]), info, planes
    )

    def to_sections(value):
        return [value] + [over_section(value, bits) for bits in (1, 2, 3)]

    def items_of(part):
        return part.reshape(items, CAP_ROWS, width)

    keys = weights.move(0, weights.payloads(0))
    pad = ((0, 0), (0, ROWS - positions), (0, 0))
    x0 = jnp.pad(tokens, pad)
    last_grad = jnp.pad(cotangent, pad)
    rows = jnp.concatenate(
        [
            attend_gain,
            attend_shift,
            attend_bias,
            expert_gain,
            expert_shift,
            expert_inner_bias,
            expert_outer_bias,
            jnp.full((1, 128), jnp.sum(caption_lengths), F32),
        ],
        axis=1,
    )
    rows = to_sections(rows)
    x0, last_grad, *rows = weights.join([x0, last_grad, *rows], keys)
    keys1 = weights.move(1, weights.payloads(1))
    rows = jnp.concatenate(rows, axis=0)
    language_count = jnp.sum(rows[:, -128:], axis=0, keepdims=True)
    rows = [lax.dynamic_index_in_dim(rows, at ^ section, 0) for at in range(SECTIONS)]
    sizes = [width, width, 3 * width, width, width, hidden, width]
    ends = [sum(sizes[: at + 1]) for at in range(len(sizes))]
    used = [(0, 0), (0, 1), (0, 2), (0, 3), (0, 4), (0, 5), (1, 3), (1, 4), (1, 5), (1, 6)]
    used += [(0, 6), (2, 0), (2, 1), (2, 2), (3, 3), (3, 4), (3, 5), (3, 6)]
    kept = [rows[slot][:, ends[which] - sizes[which] : ends[which]] for slot, which in used]
    language_count, *kept = weights.join([language_count, *kept], keys1)
    kept = dict(zip(used, kept))

    def row(slot, which):
        return kept[slot, which]

    crossed = weights.cross(keys + keys1)
    sends = weights.payloads(2, "F") if weights.four else weights.payloads(2)
    sends, (info, language_count) = under(sends, info, language_count)
    keys = weights.move(2, sends[:2])
    info, language_count = weights.join(
        [info, language_count + over_core(language_count)], theirs=crossed
    )
    plane_keys = []
    if weights.four:
        weights.mine["plane", 0] = sends[2]
        plane_keys = weights.move_planes(1)
    attend0 = weights.layer("a")
    outputs = attend_forward(
        x0, info, attend0, row(0, 0), row(0, 1), row(0, 2), following=(row(0, 3), row(0, 4))
    )
    y0, qkv0, mixed0, caption_rows = weights.join(outputs, keys)
    caption_rows = to_sections(caption_rows.reshape(-1, width))
    sends = weights.payloads(3, 4) if weights.four else weights.payloads(3)
    caption_rows = weights.join(caption_rows, plane_keys)
    sends, caption_rows = under(sends, *caption_rows)
    early_keys = keys
    keys, sends = weights.move(3, sends[:2]), sends[2:]
    crossed = weights.cross(early_keys)
    if weights.four:
        keys += weights.move_planes(2)
    outputs = shared_forward(caption_rows, expert_inputs[0], expert_inner_bias, expert_outputs[0])
    part = weights.join(outputs, keys, crossed)
    (y0,) = weights.join([y0], theirs=weights.cross([(3, 0), (3, 1)]))
    branch = {at: over_section(part[at], at, [0]) for at in range(1, SECTIONS)}
    keys = weights.move_planes(3) if weights.four else []
    expert1 = weights.layer("e")
    outputs = expert_forward(
        y0, info, expert1, row(1, 3), row(1, 4), row(1, 5), row(1, 6), PATCH_ROWS, "patch"
    )
    outputs, moved = under(outputs, *branch.values())
    if weights.four:
        keys += [("plane", step) for step in range(-2, 3)]
    x2, act1, slope1 = weights.join(outputs, keys)
    branch = dict(zip(branch, moved))
    branch[0] = part[0]
    branch = items_of(by_section(section, branch))
    if weights.four:
        crossed = [("plane", step) for step in range(-3, 4)]
    else:
        for step in (4, 5):
            weights.move(step, weights.payloads(step))
        crossed = [(4, 0), (4, 1), (5, 0)]
    weights.cross(crossed)
    attend2 = weights.layer("c") if weights.four else None
    if not weights.four:
        (x2,) = weights.join([x2], theirs=crossed)
        attend2 = weights.layer("c")
    outputs = attend_forward(
        x2, info, attend2, row(2, 0), row(2, 1), row(2, 2), merge=(y0, branch, row(0, 6))
    )
    if weights.four:
        language_count += over_plane(language_count, [(at, at ^ 1) for at in range(4)])
    x3, qkv2, mixed2, x2, language_count = weights.join([*outputs, language_count], theirs=crossed)
    if weights.four:
        language_count += over_plane(language_count, [(at, at ^ 2) for at in range(4)])
    else:
        language_count = lax.psum(language_count, "z")
    expert3 = weights.layer("f")
    outputs = expert_forward(
        x3, info, expert3, row(3, 3), row(3, 4), row(3, 5), row(3, 6), ROWS, "all"
    )
    layer_output, act3, slope3, language_count = under([*outputs, language_count])[0]
    language_count = language_count[0, 0].astype(jnp.int32)
    vision_count = PATCHES * items * SECTIONS * 2 * planes
    counts = jnp.stack(
        [jnp.full((), vision_count, jnp.int32), language_count, language_count + vision_count]
    )

    def small_rows(values):
        flat = jnp.concatenate(values, axis=1)
        count = -(-flat.shape[1] // hidden)
        flat = jnp.pad(flat, ((0, 0), (0, count * hidden - flat.shape[1])))
        return flat.reshape(count, hidden)

    def to_home(sums):
        got = [by_section(section, sums)]
        for bits in (1, 2, 3):
            sends = {at ^ bits: sums[at] for at in sums}
            got.append(over_section(by_section(section, sends), bits, sorted(sends)))
        return got

    keys = []
    if weights.four:
        sends, (layer_output, last_grad) = under(sends, layer_output, last_grad)
        keys = weights.move(4, sends)
    outputs = expert_backward(
        x3, info, expert3, row(3, 3), row(3, 4), act3, slope3, last_grad, ROWS, "all"
    )
    outputs = weights.join(outputs, keys)
    crossed = weights.cross(keys)
    grad3, *small3 = outputs[:5]
    sums3 = Sums(outputs[5:])
    sums3.cross()
    moved = over_links(sums3.first_sends())
    grad3 = after(grad3, *sums3.sent)
    outputs = attend_backward(
        x2, info, attend2, row(2, 0), row(2, 1), qkv2, mixed2, grad3
    )
    outputs, moved = under(outputs, *moved, sums3.got_stay)
    outputs = weights.join(outputs, theirs=crossed)
    grad2, *small2 = outputs[:4]
    sums2, caption_grad = Sums(outputs[4:8]), outputs[8]
    caption_grads = to_sections(caption_grad.reshape(-1, width))
    sums3.got_stay = moved[2]
    sends3 = sums3.second_sends(*moved[:2])
    grad2, *sends3 = lax.optimization_barrier((grad2, *sends3))
    outputs = expert_back(
        y0, info, expert1, row(1, 3), row(1, 4), slope1, grad2, PATCH_ROWS, "patch"
    )
    outputs, caption_grads = under(outputs, *caption_grads)
    grad1, *small1 = outputs[:5]
    inner1, *turned1 = outputs[5:]
    inner_quarter = lax.dynamic_slice(row(0, 5), (0, section * width), (1, width))
    grad1, *sends3 = lax.optimization_barrier((grad1, *sends3))
    moved3 = over_links(sends3)
    inner_quarter = after(inner_quarter, grad1)
    outputs = shared_backward(
        caption_rows, caption_grads, info, weights.layer("g"), inner_quarter
    )
    outputs, moved3 = under(outputs, *moved3)
    parts, (keep0, send0, inner_grad, outer_grad) = outputs[:4], outputs[4:]
    got = [over_section(parts[bits], bits) for bits in (1, 2, 3)]
    keep0 = added(keep0, over_core(send0))
    early = jnp.concatenate([sums3.whole(*moved3), keep0], axis=0)
    early, inner1 = lax.optimization_barrier((early, inner1))
    early = lax.psum(early, "z")
    outputs = expert_weights(*turned1, inner1, act1)
    outputs, got = under(outputs, *got)
    sums1 = Sums(outputs)
    sums1.cross()
    sums2.cross(outputs[0])
    sends, sends2 = sums1.first_sends(), sums2.first_sends()
    grad1, *sends = lax.optimization_barrier((grad1, *sends, *sends2))
    moved1, moved2 = over_links(sends[:2]), over_links(sends[2:])
    parts = [parts[0], *got]
    outputs = attend_backward(
        x0,
        info,
        attend0,
        row(0, 0),
        row(0, 1),
        qkv0,
        mixed0,
        grad1,
        first=(y0, row(0, 3), parts),
    )
    outputs, moved = under(outputs, *moved2, *moved1)
    moved2, moved1 = moved[:2], moved[2:]
    tokens_grad, *small_first = outputs[:4]
    sums_first, gain_grad, shift_grad = Sums(outputs[4:8]), outputs[8], outputs[9]
    sums_first.cross()
    inner_grad = lax.dynamic_update_slice(
        jnp.zeros((1, hidden), F32), inner_grad, (0, section * width)
    )
    small = small_rows(
        small_first + [gain_grad, shift_grad, inner_grad, outer_grad] + small2 + small1 + small3
    )
    small = added(small, over_core(small))
    to_x, to_y = sums_first.first_sends()
    to_x = jnp.concatenate([to_x[0], small], axis=0)
    sends = lax.optimization_barrier((*sums1.second_sends(*moved1), to_x, to_y))
    moved1, moved = over_links(sends[:2]), over_links(sends[2:])
    sum1, early = lax.optimization_barrier((sums1.whole(*moved1), early))
    planes1 = Planes(sum1, plane, planes)
    size = to_y.shape[1]
    small = added(small, moved[0][size:])
    to_x, to_y = sums_first.second_sends(moved[0][None, :size], moved[1])
    early_x, early_y = sums2.second_sends(*moved2)
    to_x = jnp.concatenate([to_x[0], early_x[0]], axis=0)
    to_y = jnp.concatenate([to_y[0], early_y[0], small], axis=0)
    to_x, to_y = lax.optimization_barrier((to_x, to_y))
    sent1 = planes1.sends()
    moved = lax.optimization_barrier(tuple(over_links((to_x, to_y))))
    size = early_x.shape[1]
    last = sums_first.whole(moved[0][None, :size], moved[1][None, :size])
    sum2 = sums2.whole(moved[0][None, size:], moved[1][None, size : 2 * size])
    small = added(small, moved[1][2 * size :])
    small_count = small.shape[0]
    eighth = last.shape[1]
    last = jnp.concatenate([last[0], sum2[0], small], axis=0)
    planes_last = Planes(last, plane, planes)
    home_early = to_home({0: after(early[2:], *moved), 3: after(early[:2], *moved)})
    planes_last.take(*planes_last.sends())
    planes1.take(*sent1)
    planes1.take(*planes1.sends())
    planes1.take(*planes1.sends(*home_early[1:3]))
    planes_last.take(*planes_last.sends())
    planes1.take(*planes1.sends(home_early[3]))
    planes_last.take(*planes_last.sends())
    home_late = to_home({1: after(planes1.value, *home_early[1:])})
    planes_last.take(*planes_last.sends())
    last = planes_last.value
    home_attend = to_home({0: last[None, :eighth], 2: last[None, eighth : 2 * eighth]})
    small = planes_last.in_order(last[2 * eighth :].astype(F32))

    as_float = counts.astype(F32)
    one = jnp.ones((), F32)
    attend_scales = jnp.stack([as_float[2], one, as_float[2], one])
    expert_scales = jnp.stack([as_float[1], as_float[0], one, as_float[2]])

    def placed(pieces, scales):
        scale = lax.dynamic_index_in_dim(scales, section, 0).reshape(1, 1)
        pieces = jnp.stack(pieces)
        return finish(info, scale, pieces, over_core(pieces), planes)

    blank = jnp.zeros_like(home_late[0])
    inputs_whole, outputs_whole = placed(
        [
            by_section(section, {0: early, 1: late, 2: blank, 3: early})
            for early, late in zip(home_early, home_late)
        ],
        expert_scales,
    )
    blank = jnp.zeros_like(home_attend[0])
    attend_whole, output_whole = placed(
        [by_section(section, {0: got, 1: blank, 2: got, 3: blank}) for got in home_attend],
        attend_scales,
    )

    attend_size, expert_size = 5 * width, 3 * width + hidden
    cuts = [attend_size, attend_size + expert_size]
    cuts += [cuts[1] + attend_size, cuts[1] + attend_size + expert_size]
    small = jnp.split(small.reshape(-1)[: cuts[3] + expert_size], cuts)
    none_attend, none_expert = jnp.zeros_like(small[0]), jnp.zeros_like(small[1])
    attend_small = jnp.stack([small[0], none_attend, small[2], none_attend])
    expert_small = jnp.stack([small[1], small[3], none_expert, small[4]])
    attend_small = attend_small / attend_scales.reshape(-1, 1)
    expert_small = expert_small / expert_scales.reshape(-1, 1)
    attend_small = lax.dynamic_index_in_dim(attend_small, section, 0)
    expert_small = lax.dynamic_index_in_dim(expert_small, section, 0)
    return (
        layer_output[:, :positions],
        tokens_grad[:, :positions],
        attend_small[:, :width],
        attend_small[:, width : 2 * width],
        attend_whole,
        attend_small[:, 2 * width :],
        output_whole,
        expert_small[:, :width],
        expert_small[:, width : 2 * width],
        inputs_whole,
        expert_small[:, 2 * width : 2 * width + hidden],
        outputs_whole,
        expert_small[:, 2 * width + hidden :],
        counts,
    )


def solution(mesh):
    sections, groups = mesh.shape["section"], mesh.shape["dp"]
    split = Mesh(mesh.devices.reshape(sections, groups // 2, 2), ("section", "z", "core"))
    items = P(("section", "z", "core"), None, None)
    flat = P("section", None)
    matrix = P("section", None, None)
    placed = (
        items,
        P(("section", "z", "core")),
        flat,
        flat,
        matrix,
        flat,
        matrix,
        flat,
        flat,
        matrix,
        flat,
        matrix,
        flat,
        items,
    )
    return jax.shard_map(
        per_device,
        mesh=split,
        in_specs=placed,
        out_specs=(
            items,
            items,
            flat,
            flat,
            matrix,
            flat,
            matrix,
            flat,
            flat,
            matrix,
            flat,
            matrix,
            flat,
            P(),
        ),
        check_vma=False,
    )
```

```python
from functools import partial

import jax
import jax.numpy as jnp
from jax import lax
from jax.experimental import pallas as pl
from jax.experimental.pallas import tpu as pltpu
from jax.sharding import Mesh
from jax.sharding import PartitionSpec as P

HEADS = 12
HEAD_DIM = 64
PATCHES = 197
ROWS = 256
CAP_FIRST, CAP_ROWS = 192, 48
PATCH_ROWS = 208
PAIR = 2 * HEAD_DIM
SECTIONS = 4
PIECE_ROWS = 48
VMEM_BYTES = 58 * 1024 * 1024
F32 = jnp.float32
BF16 = jnp.bfloat16

PLAN_FOUR = (
    ({0: "a0", 1: "e0", 2: "c0", 3: "F"}, {0: "a1", 1: "e2", 2: "c0", 3: "F"}),
    ({0: "a1", 1: "e1", 2: "a1", 3: "e2"}, {0: "a0", 1: "a0", 2: "F", 3: "c0"}),
    ({0: "g3", 1: "e2", 2: "c1"}, {0: "e0", 1: "e3", 2: "c1"}),
    ({0: "g1", 1: "e3", 2: "e0", 3: "e3"}, {0: "e1", 1: "e1", 3: "c1"}),
    ({}, {0: "g2", 1: "g3"}),
)
PLAN_ANY = (
    ({0: "a0", 1: "e0", 2: "c0", 3: "f0"}, {0: "a1", 1: "e2", 2: "c0", 3: "f0"}),
    ({0: "a1", 1: "e1", 2: "a1", 3: "e2"}, {0: "a0", 1: "a0", 2: "c1", 3: "f1"}),
    ({0: "g3", 1: "e2", 2: "c1", 3: "f1"}, {0: "e0", 1: "e3", 2: "f0", 3: "f2"}),
    ({0: "g1", 1: "e3", 2: "e0", 3: "e3"}, {0: "e1", 1: "e1", 2: "f1", 3: "f3"}),
    ({0: "c1", 1: "f2", 3: "f2"}, {0: "g2", 1: "g3", 3: "c0"}),
    ({1: "f3", 3: "f3"}, {}),
)
HOMES = {"a": 0, "c": 2, "e": 1, "f": 3, "F": 3, "g": 0}
ATTEND_BLOCKS = ((0, 1), (2, 3))
EXPERT_BLOCKS = ((0, 1), (4, 5), (2, 3), (6, 7))


def dot_plain(left, right):
    return jnp.dot(left, right, preferred_element_type=F32)


def dot_last(left, right):
    return lax.dot_general(left, right, (((1,), (1,)), ((), ())), preferred_element_type=F32)


def dot_first(left, right):
    return lax.dot_general(left, right, (((0,), (0,)), ((), ())), preferred_element_type=F32)


def column_sum(matrix):
    return jnp.sum(matrix.astype(F32), axis=0, keepdims=True)


def norm_parts(rows):
    centre = rows - jnp.mean(rows, axis=-1, keepdims=True)
    scale = lax.rsqrt(jnp.mean(centre * centre, axis=-1, keepdims=True) + 1e-06)
    return centre * scale, scale


def norm_back(normed_grad, unit, scale, gain):
    unit_grad = normed_grad * gain
    along = jnp.mean(unit_grad * unit, axis=-1, keepdims=True)
    return scale * (unit_grad - jnp.mean(unit_grad, axis=-1, keepdims=True) - unit * along)


def true_positions(length, first, count, axis, kind):
    shape = (count, 1) if axis == 0 else (1, count)
    position = first + lax.broadcasted_iota(jnp.int32, shape, axis)
    patch = position < PATCHES
    if kind == "patch":
        return patch
    caption = (position >= PATCHES) & (position - PATCHES < length)
    return caption if kind == "caption" else patch | caption


def head_masks():
    lane = lax.broadcasted_iota(jnp.int32, (1, PAIR), 1)
    even = (lane < HEAD_DIM).astype(F32).astype(BF16)
    odd = (lane >= HEAD_DIM).astype(F32).astype(BF16)
    return lane < HEAD_DIM, even, odd


def split_pair(pair, even, odd):
    return jnp.concatenate([pair * even, pair * odd], axis=0)


def start_weights(info, first, refs, plan, blocks, sems):
    half = blocks.shape[1] // 2
    section, core, plane = info[first], info[first + 1], info[first + 2]
    for at, at_plane, steps in plan:
        here = section == at
        if at_plane is not None:
            here = here & (plane == at_plane)

        @pl.when(here)
        def _(steps=steps):
            for block, source in steps:
                if source[0] == "own":
                    _, which, row, column = source
                    width = blocks.shape[2]
                    for part in range(2):
                        pltpu.make_async_copy(
                            refs[which].at[
                                pl.ds(row + part * half, half), pl.ds(column, width)
                            ],
                            blocks.at[block, pl.ds(part * half, half)],
                            sems.at[block],
                        ).start()
                else:
                    _, mine, theirs, index = source
                    pltpu.make_async_copy(
                        refs[mine].at[index],
                        blocks.at[block, pl.ds(pl.multiple_of(core * half, half), half)],
                        sems.at[block],
                    ).start()
                    pltpu.make_async_copy(
                        refs[theirs].at[index],
                        blocks.at[block, pl.ds(pl.multiple_of((1 - core) * half, half), half)],
                        sems.at[block],
                    ).start()


def wait_block(blocks, block, sems):
    pltpu.make_async_copy(blocks.at[block], blocks.at[block], sems.at[block]).wait()


def store_turned(target, turned, columns, section, core):
    half = target.shape[0] // 2
    for piece in range(16):
        path, owner = (piece >> 2) & 1, piece & 3
        away = owner ^ section
        place = ((away & 1) << 1) | (away >> 1) if path == 0 else away
        row = ((piece >> 3) ^ core) * half + (place >> 1) * (half // 2)
        row = row + path * (half // 4) + (place & 1) * PIECE_ROWS
        target[pl.ds(pl.multiple_of(row, 16), PIECE_ROWS), columns] = turned[
            piece * PIECE_ROWS : (piece + 1) * PIECE_ROWS
        ]


def put_travel(refs, which, columns, left, right):
    half = left.shape[0] // 2
    for side in range(2):
        rows = dot_plain(left[side * half : (side + 1) * half], right).astype(BF16)
        refs[2 * side][which, :, columns] = rows[: half // 2]
        refs[2 * side + 1][which, :, columns] = rows[half // 2 :]


def attend_forward_kernel(plan, weight_count, merge, info, *refs):
    weights, refs = refs[:weight_count], refs[weight_count:]
    if merge:
        x_ref, before_ref, part_ref, outer_ref, gain_ref, shift_ref, bias_ref = refs[:7]
        y_ref, qkv_ref, mixed_ref, joined_ref, blocks, sems, joined = refs[7:]
    else:
        x_ref, gain_ref, shift_ref, bias_ref, next_gain_ref, next_shift_ref = refs[:6]
        y_ref, qkv_ref, mixed_ref, caption_ref, blocks, sems = refs[6:]
    item = pl.program_id(0)
    items = pl.num_programs(0)
    length = info[item]
    width = x_ref.shape[-1]

    @pl.when(item == 0)
    def _():
        start_weights(info, items, weights, plan, blocks, sems)

    cap = slice(CAP_FIRST, CAP_FIRST + CAP_ROWS)
    if merge:
        joined[...] = x_ref[0].astype(F32)
        branch = part_ref[0].astype(F32) + outer_ref[...]
        is_true = true_positions(length, CAP_FIRST, CAP_ROWS, 0, "caption")
        captions = before_ref[0, cap] + jnp.where(is_true, branch, 0.0)
        position = CAP_FIRST + lax.broadcasted_iota(jnp.int32, (CAP_ROWS, 1), 0)
        captions = captions.astype(BF16).astype(F32)
        joined[cap] = jnp.where(position < PATCHES, joined[cap], captions)
        x = joined[...]
        joined_ref[0] = x.astype(BF16)
    else:
        x = x_ref[0].astype(F32)
    unit, _ = norm_parts(x)
    normed = (unit * gain_ref[...] + shift_ref[...]).astype(BF16)

    @pl.when(item == 0)
    def _():
        for block in range(4):
            wait_block(blocks, block, sems)

    queries = dot_plain(normed, blocks[0]) + bias_ref[:, :width]
    qkv_ref[0, :, :width] = (queries * HEAD_DIM ** (-0.5)).astype(BF16)
    qkv_ref[0, :, width : 2 * width] = dot_plain(normed, blocks[1]).astype(BF16)
    values = dot_plain(normed, blocks[2]) + bias_ref[:, width : 2 * width]
    qkv_ref[0, :, 2 * width :] = values.astype(BF16)
    key_true = true_positions(length, 0, ROWS, 1, "all")
    low_half, even, odd = head_masks()
    ones = jnp.ones((ROWS, PAIR), BF16)

    def scores_of(pair):
        at = pair * PAIR
        q2 = qkv_ref[0, :, at : at + PAIR]
        k2 = qkv_ref[0, :, width + at : width + at + PAIR]
        return dot_last(split_pair(q2, even, odd), k2)

    ahead = [scores_of(0), scores_of(1)]
    for pair in range(HEADS // 2):
        at = pair * PAIR
        scores = jnp.where(key_true, ahead.pop(0), -1e9)
        if pair + 2 < HEADS // 2:
            ahead.append(scores_of(pair + 2))
        weight = jnp.exp(scores - jnp.max(scores, axis=-1, keepdims=True)).astype(BF16)
        v2 = qkv_ref[0, :, 2 * width + at : 2 * width + at + PAIR]
        summed = dot_plain(weight, jnp.concatenate([v2, ones], axis=1))
        top = jnp.where(low_half, summed[:ROWS, :PAIR], summed[ROWS:, :PAIR])
        below = jnp.where(low_half, summed[:ROWS, PAIR:], summed[ROWS:, PAIR:])
        mixed_ref[0, :, at : at + PAIR] = (top / below).astype(BF16)
    branch = dot_plain(mixed_ref[0], blocks[3]) + bias_ref[:, 2 * width :]
    row_true = true_positions(length, 0, ROWS, 0, "all")
    y = x + jnp.where(row_true, branch, 0.0)
    y_ref[0] = y.astype(y_ref.dtype)
    if not merge:
        unit, _ = norm_parts(y[cap])
        caption_ref[0] = (unit * next_gain_ref[...] + next_shift_ref[...]).astype(BF16)


def attend_backward_kernel(plan, weight_count, first, info, *refs):
    weights, refs = refs[:weight_count], refs[weight_count:]
    x_ref, gain_ref, shift_ref, qkv_ref, mixed_ref, grad_ref = refs[:6]
    if first:
        after_ref, next_gain_ref, *parts = refs[6:12]
        refs = refs[12:]
    else:
        refs = refs[6:]
    out_ref, gain_grad_ref, shift_grad_ref, bias_grad_ref = refs[:4]
    travel_refs = refs[4:8]
    if first:
        next_gain_grad_ref, next_shift_grad_ref, joined = refs[8], refs[9], refs[-1]
    else:
        caption_ref = refs[8]
    blocks, sems, normed_turned, mixed_turned, branch_all, projected, mixed_grad = refs[
        10 if first else 9 :
    ][:7]
    item = pl.program_id(0)
    items = pl.num_programs(0)
    length = info[item]
    section, core = info[items], info[items + 1]
    width = x_ref.shape[-1]
    here = pl.ds(pl.multiple_of(item * ROWS, ROWS), ROWS)
    cap = slice(CAP_FIRST, CAP_FIRST + CAP_ROWS)

    @pl.when(item == 0)
    def _():
        start_weights(info, items, weights, plan, blocks, sems)

    def add_to(ref, part):
        @pl.when(item == 0)
        def _():
            ref[...] = part

        @pl.when(item > 0)
        def _():
            ref[...] += part

    x = x_ref[0].astype(F32)
    unit, scale = norm_parts(x)
    normed = (unit * gain_ref[...] + shift_ref[...]).astype(BF16)
    incoming = grad_ref[0].astype(F32)
    if first:
        after_unit, after_scale = norm_parts(after_ref[0, cap])
        caption_grad = parts[0][...].astype(F32)
        for part in parts[1:]:
            caption_grad = caption_grad + part[...].astype(F32)
        joined[...] = incoming
        joined[cap] += norm_back(caption_grad, after_unit, after_scale, next_gain_ref[...])
        incoming = joined[...]
        add_to(next_gain_grad_ref, jnp.sum(caption_grad * after_unit, axis=0, keepdims=True))
        add_to(next_shift_grad_ref, jnp.sum(caption_grad, axis=0, keepdims=True))
    row_true = true_positions(length, 0, ROWS, 0, "all")
    branch = jnp.where(row_true, incoming, 0.0).astype(BF16)
    branch_all[here, :] = branch
    store_turned(normed_turned, normed.T, here, section, core)
    store_turned(mixed_turned, mixed_ref[0].T, here, section, core)

    @pl.when(item == 0)
    def _():
        for block in range(4):
            wait_block(blocks, block, sems)

    mixed_grad[...] = dot_last(branch, blocks[3]).astype(BF16)
    key_true = true_positions(length, 0, ROWS, 0, "all")
    _, even, odd = head_masks()

    def products_of(pair):
        at = pair * PAIR
        q2 = split_pair(qkv_ref[0, :, at : at + PAIR], even, odd)
        k2 = qkv_ref[0, :, width + at : width + at + PAIR]
        v2 = qkv_ref[0, :, 2 * width + at : 2 * width + at + PAIR]
        g2 = split_pair(mixed_grad[:, at : at + PAIR], even, odd)
        return q2, k2, g2, dot_last(k2, q2), dot_last(v2, g2)

    ahead = [products_of(0)]
    for pair in range(HEADS // 2):
        at = pair * PAIR
        q2, k2, g2, scores, weight_grad = ahead.pop(0)
        if pair + 1 < HEADS // 2:
            ahead.append(products_of(pair + 1))
        scores = jnp.where(key_true, scores, -1e9)
        weight = jnp.exp(scores - jnp.max(scores, axis=0, keepdims=True))
        weight = weight * (1.0 / jnp.sum(weight, axis=0, keepdims=True))
        product = weight * weight_grad
        along = jnp.sum(product, axis=0, keepdims=True)
        score_grad = (product - weight * along).astype(BF16)
        values_grad = dot_plain(weight.astype(BF16), g2).astype(BF16)
        keys_grad = dot_plain(score_grad, q2).astype(BF16)
        k2_split = split_pair(k2, even, odd)
        stacked = jnp.concatenate([score_grad[:, :ROWS], score_grad[:, ROWS:]], axis=0)
        queries_grad = dot_first(stacked, k2_split).astype(BF16)
        queries_grad = (queries_grad.astype(F32) * HEAD_DIM ** (-0.5)).astype(BF16)
        projected[here, at : at + PAIR] = queries_grad
        projected[here, width + at : width + at + PAIR] = keys_grad
        projected[here, 2 * width + at : 2 * width + at + PAIR] = values_grad
    normed_grad = dot_last(projected[here, :width], blocks[0])
    normed_grad += dot_last(projected[here, width : 2 * width], blocks[1])
    normed_grad += dot_last(projected[here, 2 * width :], blocks[2])
    out = (incoming + norm_back(normed_grad, unit, scale, gain_ref[...])).astype(BF16)
    out_ref[0] = out
    if not first:
        is_true = true_positions(length, CAP_FIRST, CAP_ROWS, 0, "caption")
        caption_ref[0] = jnp.where(is_true, out[cap].astype(F32), 0.0).astype(BF16)
    add_to(gain_grad_ref, jnp.sum(normed_grad * unit, axis=0, keepdims=True))
    add_to(shift_grad_ref, jnp.sum(normed_grad, axis=0, keepdims=True))

    @pl.when(item == items - 1)
    def _():
        for block in range(4):
            columns = slice(block * width, (block + 1) * width)
            left = normed_turned if block < 3 else mixed_turned
            right = projected[:, columns] if block < 3 else branch_all[...]
            put_travel(travel_refs, 0, columns, left, right)
        bias_grad_ref[:, :width] = column_sum(projected[:, :width])
        bias_grad_ref[:, width : 2 * width] = column_sum(projected[:, 2 * width :])
        bias_grad_ref[:, 2 * width :] = column_sum(branch_all[...])


SHORT = pl.CostEstimate(flops=0, bytes_accessed=100_000, transcendentals=0)
LONG = pl.CostEstimate(flops=30_000_000_000, bytes_accessed=30_000_000, transcendentals=0)
ANYWHERE = pl.BlockSpec(memory_space=pl.ANY)


def whole_block(shape):
    return pl.BlockSpec(shape, lambda step, info: (0,) * len(shape))


def item_block(shape):
    return pl.BlockSpec((1,) + shape[1:], lambda step, info: (step,) + (0,) * (len(shape) - 1))


def blocks_scratch(count, width):
    return [pltpu.VMEM((count, width, width), BF16), pltpu.SemaphoreType.DMA((count,))]


def attend_forward(x, info, weights, gain, shift, bias, merge=None, following=None):
    arrays, plan = weights
    items, _, width = x.shape
    row = whole_block((1, width))
    bias_row = whole_block((1, 3 * width))
    caption_shape = (items, CAP_ROWS, width)
    if merge is not None:
        before, part, outer = merge
        operands = (x, before, part, outer, gain, shift, bias)
        specs = [item_block(x.shape), item_block(x.shape), item_block(caption_shape)]
        specs += [row, row, row, bias_row]
        last_shape, kind, scratch = x.shape, BF16, [pltpu.VMEM((ROWS, width), F32)]
    else:
        operands = (x, gain, shift, bias, *following)
        specs = [item_block(x.shape), row, row, bias_row, row, row]
        last_shape, kind, scratch = caption_shape, F32, []
    return pl.pallas_call(
        partial(attend_forward_kernel, plan, len(arrays), merge is not None),
        grid_spec=pltpu.PrefetchScalarGridSpec(
            num_scalar_prefetch=1,
            grid=(items,),
            in_specs=[ANYWHERE] * len(arrays) + specs,
            out_specs=[
                item_block(x.shape),
                item_block((items, ROWS, 3 * width)),
                item_block((items, ROWS, width)),
                item_block(last_shape),
            ],
            scratch_shapes=blocks_scratch(4, width) + scratch,
        ),
        out_shape=[
            jax.ShapeDtypeStruct(x.shape, kind),
            jax.ShapeDtypeStruct((items, ROWS, 3 * width), BF16),
            jax.ShapeDtypeStruct((items, ROWS, width), BF16),
            jax.ShapeDtypeStruct(last_shape, BF16),
        ],
        compiler_params=pltpu.CompilerParams(vmem_limit_bytes=VMEM_BYTES),
        cost_estimate=SHORT,
        name="attend_forward",
    )(info, *arrays, *operands)


def attend_backward(x, info, weights, gain, shift, qkv, mixed, incoming, first=None):
    arrays, plan = weights
    items, _, width = x.shape
    half = width // 2
    row = whole_block((1, width))
    caption_shape = (items, CAP_ROWS, width)
    operands = (x, gain, shift, qkv, mixed, incoming)
    specs = [item_block(x.shape), row, row, item_block(qkv.shape), item_block(mixed.shape)]
    specs += [item_block(incoming.shape)]
    outs = [
        (item_block(x.shape), x.shape, BF16),
        (row, (1, width), F32),
        (row, (1, width), F32),
        (whole_block((1, 3 * width)), (1, 3 * width), F32),
    ]
    outs += [(whole_block((1, half // 2, 4 * width)), (1, half // 2, 4 * width), BF16)] * 4
    scratch = []
    if first is not None:
        after, next_gain, parts = first
        operands += (after, next_gain, *parts)
        caption_rows = pl.BlockSpec((CAP_ROWS, width), lambda step, info: (step, 0))
        specs += [item_block(after.shape), row] + [caption_rows] * 4
        outs += [(row, (1, width), F32)] * 2
        scratch = [pltpu.VMEM((ROWS, width), F32)]
    else:
        outs += [(item_block(caption_shape), caption_shape, BF16)]
    return pl.pallas_call(
        partial(attend_backward_kernel, plan, len(arrays), first is not None),
        grid_spec=pltpu.PrefetchScalarGridSpec(
            num_scalar_prefetch=1,
            grid=(items,),
            in_specs=[ANYWHERE] * len(arrays) + specs,
            out_specs=[spec for spec, _, _ in outs],
            scratch_shapes=blocks_scratch(4, width)
            + [
                pltpu.VMEM((width, items * ROWS), BF16),
                pltpu.VMEM((width, items * ROWS), BF16),
                pltpu.VMEM((items * ROWS, width), BF16),
                pltpu.VMEM((items * ROWS, 3 * width), BF16),
                pltpu.VMEM((ROWS, width), BF16),
            ]
            + scratch,
        ),
        out_shape=[jax.ShapeDtypeStruct(shape, kind) for _, shape, kind in outs],
        compiler_params=pltpu.CompilerParams(vmem_limit_bytes=VMEM_BYTES),
        cost_estimate=LONG,
        name="attend_backward",
    )(info, *arrays, *operands)


def normal_parts(u):
    t = pl.reciprocal(1.0 + 0.23164190 * jnp.abs(u), approx=True)
    bell = jnp.exp2((u * -0.7213475204444817) * u)
    poly = t * (
        0.127414796
        + t * (-0.142248368 + t * (0.7107068705 + t * (-0.7265760135 + t * 0.5307027145)))
    )
    tail = poly * bell
    return jnp.where(u < 0, tail, 1.0 - tail), bell


def inner_forward(normed, matrix, bias):
    inner = dot_plain(normed, matrix) + bias
    cumulative, bell = normal_parts(inner)
    slope = cumulative + (inner * 0.3989422804014327) * bell
    return (inner * cumulative).astype(BF16), slope.astype(BF16)


def expert_forward_kernel(plan, weight_count, count, kind, info, *refs):
    weights, refs = refs[:weight_count], refs[weight_count:]
    x_ref, gain_ref, shift_ref, inner_ref, outer_ref = refs[:5]
    y_ref, act_ref, slope_ref, blocks, sems, normed, total = refs[5:]
    step = pl.program_id(0)
    items, _, width = x_ref.shape

    @pl.when(step == 0)
    def _():
        start_weights(info, items, weights, plan, blocks, sems)
        for item in range(items):
            x = x_ref[item, :count].astype(BF16).astype(F32)
            unit, _ = norm_parts(x)
            normed[item * count : (item + 1) * count] = (
                unit * gain_ref[...] + shift_ref[...]
            ).astype(BF16)

    wait_block(blocks, step, sems)
    wait_block(blocks, step + 4, sems)
    for at in range(0, width, 256):
        columns = slice(at, at + 256)
        act, slope = inner_forward(normed[...], blocks[step, :, columns], inner_ref[:, columns])
        act_ref[:, columns] = act
        slope_ref[:, columns] = slope
    part = dot_plain(act_ref[...], blocks[step + 4])

    @pl.when(step == 0)
    def _():
        total[...] = part

    @pl.when(step > 0)
    def _():
        total[...] += part

    @pl.when(step == pl.num_programs(0) - 1)
    def _():
        for item in range(items):
            row_true = true_positions(info[item], 0, count, 0, kind)
            branch = total[item * count : (item + 1) * count] + outer_ref[...]
            x = x_ref[item, :count].astype(BF16).astype(F32)
            y_ref[item, :count] = (x + jnp.where(row_true, branch, 0.0)).astype(BF16)
            if count < ROWS:
                y_ref[item, count:] = jnp.zeros((ROWS - count, width), BF16)


def expert_backward_kernel(plan, weight_count, count, kind, info, *refs):
    weights, refs = refs[:weight_count], refs[weight_count:]
    x_ref, gain_ref, shift_ref, act_ref, slope_ref, grad_ref = refs[:6]
    out_ref, gain_grad_ref, shift_grad_ref, inner_grad_ref, outer_grad_ref = refs[6:11]
    travel_refs = refs[11:15]
    blocks, sems, normed_turned, branch_turned, branch, inner_all, total = refs[15:]
    step = pl.program_id(0)
    items, _, width = x_ref.shape
    section, core = info[items], info[items + 1]

    @pl.when(step == 0)
    def _():
        start_weights(info, items, weights, plan, blocks, sems)
        outer = None
        for item in range(items):
            here = slice(item * count, (item + 1) * count)
            unit, _ = norm_parts(x_ref[item, :count].astype(BF16).astype(F32))
            normed = (unit * gain_ref[...] + shift_ref[...]).astype(BF16)
            row_true = true_positions(info[item], 0, count, 0, kind)
            incoming = grad_ref[item, :count].astype(F32)
            masked = jnp.where(row_true, incoming, 0.0).astype(BF16)
            branch[here] = masked
            store_turned(normed_turned, normed.T, here, section, core)
            store_turned(branch_turned, masked.T, here, section, core)
            term = column_sum(masked)
            outer = term if outer is None else outer + term
        outer_grad_ref[...] = outer

    wait_block(blocks, step, sems)
    wait_block(blocks, step + 4, sems)
    for at in range(0, width, 256):
        columns = slice(at, at + 256)
        act_grad = dot_last(branch[...], blocks[step + 4, columns])
        inner = (slope_ref[:, columns].astype(F32) * act_grad).astype(BF16)
        inner_all[:, columns] = inner
        inner_grad_ref[:, columns] = column_sum(inner)
        put_travel(travel_refs, 0, columns, normed_turned, inner)
        put_travel(travel_refs, 1, columns, branch_turned, act_ref[:, columns])
    part = dot_last(inner_all[...], blocks[step])

    @pl.when(step == 0)
    def _():
        total[...] = part

    @pl.when(step > 0)
    def _():
        total[...] += part

    @pl.when(step == pl.num_programs(0) - 1)
    def _():
        gain_sum, shift_sum = None, None
        for item in range(items):
            unit, scale = norm_parts(x_ref[item, :count].astype(BF16).astype(F32))
            normed_grad = total[item * count : (item + 1) * count]
            gain_part = jnp.sum(normed_grad * unit, axis=0, keepdims=True)
            shift_part = jnp.sum(normed_grad, axis=0, keepdims=True)
            gain_sum = gain_part if gain_sum is None else gain_sum + gain_part
            shift_sum = shift_part if shift_sum is None else shift_sum + shift_part
            incoming = grad_ref[item, :count].astype(F32)
            hidden = incoming + norm_back(normed_grad, unit, scale, gain_ref[...])
            out_ref[item, :count] = hidden.astype(BF16)
            if count < ROWS:
                out_ref[item, count:] = grad_ref[item, count:]
        gain_grad_ref[...] = gain_sum
        shift_grad_ref[...] = shift_sum


def shared_forward_kernel(*refs):
    *rows_refs, inputs_ref, inner_ref, outputs_ref = refs[:7]
    *part_refs, normed, total = refs[7:]
    count = rows_refs[0].shape[0]
    step = pl.program_id(0)

    @pl.when(step == 0)
    def _():
        for index, ref in enumerate(rows_refs):
            normed[index * count : (index + 1) * count] = ref[...]
        total[...] = jnp.zeros_like(total)

    act, _ = inner_forward(normed[...], inputs_ref[...], inner_ref[...])
    total[...] += dot_plain(act, outputs_ref[...])

    @pl.when(step == pl.num_programs(0) - 1)
    def _():
        for index, ref in enumerate(part_refs):
            ref[...] = total[index * count : (index + 1) * count].astype(BF16)


def shared_backward_kernel(plan, weight_count, info, *refs):
    weights, refs = refs[:weight_count], refs[weight_count:]
    rows_refs, grad_refs, inner_ref = refs[:4], refs[4:8], refs[8]
    part_refs, (keep_ref, send_ref, inner_grad_ref, outer_grad_ref) = refs[9:13], refs[13:17]
    blocks, sems, normed, branch, matrix = refs[17:]
    count, width = rows_refs[0].shape
    half = width // 2
    first = info.shape[0] - 3
    core = info[first + 1]
    start_weights(info, first, weights, plan, blocks, sems)
    for index in range(SECTIONS):
        here = slice(index * count, (index + 1) * count)
        normed[here] = rows_refs[index][...]
        branch[here] = grad_refs[index][...]
    outer_grad_ref[...] = column_sum(grad_refs[0][...])
    wait_block(blocks, 0, sems)
    wait_block(blocks, 1, sems)
    part = None
    for at in range(0, width, 256):
        columns = slice(at, at + 256)
        act, slope = inner_forward(normed[...], blocks[0, :, columns], inner_ref[:, columns])
        act_grad = dot_last(branch[...], blocks[1, columns])
        inner = (slope.astype(F32) * act_grad).astype(BF16)
        inner_grad_ref[:, columns] = column_sum(inner)
        matrix[0, :, columns] = dot_first(normed[...], inner).astype(BF16)
        matrix[1, :, columns] = dot_first(branch[...], act).astype(BF16)
        term = dot_last(inner, blocks[0, :, columns])
        part = term if part is None else part + term
    for index, ref in enumerate(part_refs):
        ref[...] = part[index * count : (index + 1) * count].astype(BF16)
    quarter = half // 4
    for which in range(2):
        for group in range(4):
            columns = slice(group * width, (group + 1) * width)
            mine = pl.multiple_of(core * half, 16) + group * quarter
            other = pl.multiple_of((1 - core) * half, 16) + group * quarter
            keep_ref[which, :, columns] = matrix[which, pl.ds(pl.multiple_of(mine, 16), quarter)]
            send_ref[which, :, columns] = matrix[which, pl.ds(pl.multiple_of(other, 16), quarter)]


def chunk_columns(rows, width):
    return pl.BlockSpec((rows, width), lambda step, info: (0, step))


def expert_forward(x, info, weights, gain, shift, inner, outer, count, kind):
    arrays, plan = weights
    items, _, width = x.shape
    hidden = inner.shape[1]
    row = whole_block((1, width))
    return pl.pallas_call(
        partial(expert_forward_kernel, plan, len(arrays), count, kind),
        grid_spec=pltpu.PrefetchScalarGridSpec(
            num_scalar_prefetch=1,
            grid=(hidden // width,),
            in_specs=[ANYWHERE] * len(arrays)
            + [whole_block(x.shape), row, row, chunk_columns(1, width), row],
            out_specs=[
                whole_block((items, ROWS, width)),
                chunk_columns(items * count, width),
                chunk_columns(items * count, width),
            ],
            scratch_shapes=blocks_scratch(8, width)
            + [
                pltpu.VMEM((items * count, width), BF16),
                pltpu.VMEM((items * count, width), F32),
            ],
        ),
        out_shape=[
            jax.ShapeDtypeStruct((items, ROWS, width), BF16),
            jax.ShapeDtypeStruct((items * count, hidden), BF16),
            jax.ShapeDtypeStruct((items * count, hidden), BF16),
        ],
        compiler_params=pltpu.CompilerParams(vmem_limit_bytes=VMEM_BYTES),
        cost_estimate=SHORT,
        name="expert_forward_" + kind,
    )(info, *arrays, x, gain, shift, inner, outer)


def expert_backward(x, info, weights, gain, shift, act, slope, incoming, count, kind):
    arrays, plan = weights
    items, _, width = x.shape
    half = width // 2
    hidden = act.shape[1]
    row = whole_block((1, width))
    travel = pl.BlockSpec((2, half // 2, width), lambda step, info: (0, 0, step))
    return pl.pallas_call(
        partial(expert_backward_kernel, plan, len(arrays), count, kind),
        grid_spec=pltpu.PrefetchScalarGridSpec(
            num_scalar_prefetch=1,
            grid=(hidden // width,),
            in_specs=[ANYWHERE] * len(arrays)
            + [
                whole_block(x.shape),
                row,
                row,
                chunk_columns(items * count, width),
                chunk_columns(items * count, width),
                whole_block(incoming.shape),
            ],
            out_specs=[whole_block(incoming.shape), row, row, chunk_columns(1, width), row]
            + [travel] * 4,
            scratch_shapes=blocks_scratch(8, width)
            + [
                pltpu.VMEM((width, items * count), BF16),
                pltpu.VMEM((width, items * count), BF16),
                pltpu.VMEM((items * count, width), BF16),
                pltpu.VMEM((items * count, width), BF16),
                pltpu.VMEM((items * count, width), F32),
            ],
        ),
        out_shape=[
            jax.ShapeDtypeStruct(incoming.shape, BF16),
            jax.ShapeDtypeStruct((1, width), F32),
            jax.ShapeDtypeStruct((1, width), F32),
            jax.ShapeDtypeStruct((1, hidden), F32),
            jax.ShapeDtypeStruct((1, width), F32),
        ]
        + [jax.ShapeDtypeStruct((2, half // 2, hidden), BF16)] * 4,
        compiler_params=pltpu.CompilerParams(vmem_limit_bytes=VMEM_BYTES),
        cost_estimate=SHORT,
        name="expert_backward_" + kind,
    )(info, *arrays, x, gain, shift, act, slope, incoming)


IN_VMEM = pl.BlockSpec(memory_space=pltpu.VMEM)
IN_SMEM = pl.BlockSpec(memory_space=pltpu.SMEM)


def shared_forward(rows, inputs, inner, outputs):
    count, width = rows[0].shape
    total = SECTIONS * count
    hidden = inner.shape[1]
    return pl.pallas_call(
        shared_forward_kernel,
        grid=(hidden // width,),
        in_specs=[pl.BlockSpec(rows[0].shape, lambda step: (0, 0))] * 4
        + [
            pl.BlockSpec((width, width), lambda step: (0, step)),
            pl.BlockSpec((1, width), lambda step: (0, step)),
            pl.BlockSpec((width, width), lambda step: (step, 0)),
        ],
        out_specs=[pl.BlockSpec((count, width), lambda step: (0, 0))] * SECTIONS,
        scratch_shapes=[pltpu.VMEM((total, width), BF16), pltpu.VMEM((total, width), F32)],
        out_shape=[jax.ShapeDtypeStruct((count, width), BF16)] * SECTIONS,
        compiler_params=pltpu.CompilerParams(vmem_limit_bytes=VMEM_BYTES),
        cost_estimate=SHORT,
        name="shared_forward",
    )(*rows, inputs, inner, outputs)


def shared_backward(rows, grads, info, weights, inner):
    arrays, plan = weights
    count, width = rows[0].shape
    total = SECTIONS * count
    travel = (2, width // 8, 4 * width)
    return pl.pallas_call(
        partial(shared_backward_kernel, plan, len(arrays)),
        in_specs=[IN_SMEM] + [ANYWHERE] * len(arrays) + [IN_VMEM] * 9,
        out_specs=[IN_VMEM] * 8,
        scratch_shapes=blocks_scratch(2, width)
        + [
            pltpu.VMEM((total, width), BF16),
            pltpu.VMEM((total, width), BF16),
            pltpu.VMEM((2, width, width), BF16),
        ],
        out_shape=[
            *[jax.ShapeDtypeStruct((count, width), BF16)] * SECTIONS,
            jax.ShapeDtypeStruct(travel, BF16),
            jax.ShapeDtypeStruct(travel, BF16),
            jax.ShapeDtypeStruct((1, width), F32),
            jax.ShapeDtypeStruct((1, width), F32),
        ],
        compiler_params=pltpu.CompilerParams(vmem_limit_bytes=VMEM_BYTES),
        cost_estimate=SHORT,
        name="shared_backward",
    )(info, *arrays, *rows, *grads, inner)


def plane_turn(plane, planes):
    return ((plane & 1) << 1) | (plane >> 1) if planes == 4 else 0


def finish_kernel(planes, info, scale_ref, *refs):
    step = pl.program_id(0)
    mine, theirs, outs, placed = refs[:4], refs[4:8], refs[8:-1], refs[-1]
    count = mine[0].shape[0]
    width = placed.shape[1]
    half = width // 2
    at = info.shape[0] - 3
    section, core = info[at], info[at + 1]
    turn = plane_turn(info[at + 2], planes)
    turned = turn if count == 1 else jnp.where(section == 1, turn, 0)
    scale = scale_ref[0, 0]
    columns = pl.ds(pl.multiple_of((step ^ turned) * width, width), width)

    def place(which):
        def by_rows():
            for side, pieces in enumerate((mine, theirs)):
                for away, ref in enumerate(pieces):
                    for path in range(2):
                        row = (core ^ side) * half + path * (half // 2)
                        row = row + (section ^ away) * PIECE_ROWS
                        placed[pl.ds(pl.multiple_of(row, 16), PIECE_ROWS), :] = ref[
                            which, path * PIECE_ROWS : (path + 1) * PIECE_ROWS, columns
                        ].astype(F32)

        def by_columns():
            for side, pieces in enumerate((mine, theirs)):
                for away, ref in enumerate(pieces):

                    @pl.when(step == away)
                    def _(side=side, ref=ref):
                        for group in range(4):
                            quarter = half // 4
                            row = (core ^ side) * half + group * quarter
                            placed[pl.ds(pl.multiple_of(row, 16), quarter), :] = ref[
                                which, :, group * width : (group + 1) * width
                            ].astype(F32)

        if count == 1:
            by_rows()
        else:
            pl.when(section != 0)(by_rows)
            pl.when(section == 0)(by_columns)

    place(0)
    if count == 1:

        @pl.when(step < 3)
        def _():
            outs[0][0] = placed[...] / scale

        @pl.when(step == 3)
        def _():
            outs[1][0] = placed[...] / scale

    else:
        outs[0][0] = placed[...] / scale
        place(1)
        outs[1][0] = (placed[...] / scale).T


def finish(info, scale, mine, theirs, planes):
    count, _, hidden = mine[0].shape
    width = hidden // 4
    if count == 1:
        shapes = [(1, width, 3 * width), (1, width, width)]
        maps = [lambda step, info: (0, 0, jnp.minimum(step, 2)), lambda step, info: (0, 0, 0)]
    else:
        shapes = [(1, width, hidden), (1, hidden, width)]
        maps = [lambda step, info: (0, 0, step), lambda step, info: (0, step, 0)]
    return pl.pallas_call(
        partial(finish_kernel, planes),
        grid_spec=pltpu.PrefetchScalarGridSpec(
            num_scalar_prefetch=1,
            grid=(4,),
            in_specs=[IN_SMEM] + [whole_block(mine[0].shape)] * 8,
            out_specs=[pl.BlockSpec((1, width, width), at) for at in maps],
            scratch_shapes=[pltpu.VMEM((width, width), F32)],
        ),
        out_shape=[jax.ShapeDtypeStruct(shape, F32) for shape in shapes],
        compiler_params=pltpu.CompilerParams(vmem_limit_bytes=VMEM_BYTES),
        cost_estimate=SHORT,
        name="finish",
    )(info, scale, *mine, *theirs)


def pack_kernel(count, plan, info, *refs):
    sources, outs, sems = refs[:count], refs[count:-1], refs[-1]
    first = info.shape[0] - 3
    section, core, plane = info[first], info[first + 1], info[first + 2]
    half = outs[0].shape[1]
    for index, (out, choices) in enumerate(zip(outs, plan)):
        for at, at_plane, parts in choices:
            here = section == at
            if at_plane is not None:
                here = here & (plane == at_plane)

            @pl.when(here)
            def _(index=index, out=out, parts=parts):
                for block, part in enumerate(parts):
                    if part[0] == "own":
                        _, which, row, column = part
                        rows = pl.ds(pl.multiple_of(row + core * half, half), half)
                        source = sources[which].at[rows, pl.ds(column, out.shape[2])]
                    else:
                        source = sources[part[1]].at[block]
                    pltpu.make_async_copy(source, out.at[block], sems.at[index, block]).start()

    for index, out in enumerate(outs):
        for block in range(2):
            pltpu.make_async_copy(out.at[block], out.at[block], sems.at[index, block]).wait()


def pack(info, sources, plan, shape):
    return pl.pallas_call(
        partial(pack_kernel, len(sources), plan),
        in_specs=[IN_SMEM] + [ANYWHERE] * len(sources),
        out_specs=[IN_VMEM] * len(plan),
        scratch_shapes=[pltpu.SemaphoreType.DMA((len(plan), 2))],
        out_shape=[jax.ShapeDtypeStruct(shape, BF16)] * len(plan),
        cost_estimate=SHORT,
        name="pack",
    )(info, *sources)


def over_section(value, bits, sources=range(SECTIONS)):
    return lax.ppermute(value, "section", [(at, at ^ bits) for at in sources])


def over_core(value):
    return lax.ppermute(value, "core", [(0, 1), (1, 0)])


def over_plane(value, pairs):
    return lax.ppermute(value, "z", pairs)


def added(left, right):
    return (left.astype(F32) + right.astype(F32)).astype(BF16)


def after(value, *earlier):
    return lax.optimization_barrier((value,) + earlier)[0]


def under(outputs, *arrivals):
    joined = lax.optimization_barrier(tuple(outputs) + arrivals)
    return list(joined[: len(outputs)]), list(joined[len(outputs) :])


def by_section(section, values):
    result, last = None, None
    for at in sorted(values):
        if result is None:
            result = values[at]
        elif values[at] is not last:
            result = jnp.where(section >= at, values[at], result)
        last = values[at]
    return result


def total(*values):
    result = values[0].astype(F32)
    for value in values[1:]:
        result = result + value.astype(F32)
    return result.astype(BF16)


class Sums:
    def __init__(self, travel):
        self.stay, self.move, self.other_stay, self.other_move = travel
        self.size = self.stay.shape[1] // 2

    def cross(self, *earlier):
        if earlier:
            self.other_move = after(self.other_move, *earlier)
            self.other_stay = after(self.other_stay, *earlier)
        self.got_move, self.got_stay = over_core(self.other_move), over_core(self.other_stay)

    def first_sends(self):
        size = self.size
        self.sent = [
            total(self.move[:, at : at + size], self.got_move[:, at : at + size])
            for at in (0, size)
        ]
        return self.sent

    def second_sends(self, from_x, from_y):
        size, half = self.size, self.size // 2
        self.first = from_x, from_y
        to_y = total(self.stay[:, half:size], self.got_stay[:, half:size], from_x[:, half:])
        to_x = total(
            self.stay[:, size + half :], self.got_stay[:, size + half :], from_y[:, half:]
        )
        self.sent = [to_x, to_y]
        return self.sent

    def whole(self, from_x, from_y):
        size, half = self.size, self.size // 2
        parts = []
        for at, first, second in ((0, self.first[0], from_y), (size, self.first[1], from_x)):
            here = slice(at, at + half)
            parts.append(total(self.stay[:, here], self.got_stay[:, here], first[:, :half], second))
        return jnp.concatenate(parts, axis=1)


def over_links(sends):
    return [over_section(sends[0], 1), over_section(sends[1], 2)]


class Planes:
    def __init__(self, value, plane, planes):
        self.value, self.plane, self.planes, self.turn = value, plane, planes, 0

    def sends(self, *earlier):
        value = after(self.value, *earlier) if earlier else self.value
        if self.planes != 4:
            return (value,)
        bits = (1, 2, 2, 1)[self.turn]
        if self.turn < 2:
            bit = (self.plane & 1, self.plane >> 1)[self.turn]
            size = value.shape[-1] // 2
            value = lax.dynamic_slice_in_dim(value, (1 - bit) * size, size, value.ndim - 1)
        return (over_plane(value, [(at, at ^ bits) for at in range(4)]),)

    def take(self, arrived):
        if self.planes != 4:
            self.value = lax.psum(arrived, "z") if self.turn == 3 else arrived
        elif self.turn < 2:
            bit = (self.plane & 1, self.plane >> 1)[self.turn]
            size = self.value.shape[-1] // 2
            keep = lax.dynamic_slice_in_dim(self.value, bit * size, size, self.value.ndim - 1)
            self.value = added(keep, arrived)
        else:
            self.value = jnp.concatenate([self.value, arrived], axis=-1)
        self.turn += 1

    def in_order(self, value):
        if self.planes != 4:
            return value
        size, turn = value.shape[-1] // 4, plane_turn(self.plane, 4)
        parts = [
            lax.dynamic_slice_in_dim(value, (at ^ turn) * size, size, value.ndim - 1)
            for at in range(4)
        ]
        return jnp.concatenate(parts, axis=-1)


class Weights:
    def __init__(self, own, info, planes):
        self.own, self.info = own, info
        self.four = planes == 4
        self.plan = PLAN_FOUR if self.four else PLAN_ANY
        self.half, self.width = own[1].shape[0] // 2, own[1].shape[1]
        self.mine, self.theirs, self.arrived = {}, {}, {}

    def place(self, layer, block):
        if layer in "ac":
            return (0, 0, block * self.width) if block < 3 else (1, 0, 0)
        if layer == "g":
            return (2, 0, block * self.width) if block < 4 else (3, (block - 4) * self.width, 0)
        return (2, 0, block * self.width) if block < 4 else (3, (block - 4) * self.width, 0)

    def choices(self, sends, sources):
        result = []
        for at in range(SECTIONS):
            name = sends.get(at)
            if name is not None and HOMES[name[0]] != at:
                key = self.arrived[at, name]
                if key not in sources:
                    sources[key] = len(self.own) + len(sources)
                result.append((at, None, [("arrived", sources[key])] * 2))
                continue
            for plane in range(4) if name == "F" else (None,):
                piece = ("f" + str(plane)) if name == "F" else name or "a0"
                layer, index = piece[0], int(piece[1])
                if layer in "ac":
                    blocks = ATTEND_BLOCKS[index]
                else:
                    blocks = (index, 4 + index) if layer == "g" else EXPERT_BLOCKS[index]
                parts = [("own",) + self.place(layer, block) for block in blocks]
                result.append((at, plane, parts))
        return result

    def packed(self, wanted):
        sources = {}
        plan = [self.choices(sends, sources) for sends in wanted]
        arrays = list(self.own) + [self.mine[key] for key in sources]
        return pack(self.info, arrays, plan, (2, self.half, self.width))

    def sends(self, step):
        if step == "F":
            return [{at: "F" for at in range(SECTIONS)}]
        return [sends for sends in self.plan[step] if sends]

    def payloads(self, *steps):
        wanted = [sends for step in steps for sends in self.sends(step)]
        return list(self.packed(wanted))

    def move(self, step, payloads):
        links = [(link, sends) for link, sends in enumerate(self.plan[step]) if sends]
        for (link, sends), payload in zip(links, payloads):
            self.mine[step, link] = over_section(payload, link + 1, sorted(sends))
            for at, name in sends.items():
                self.arrived[at ^ (link + 1), name] = (step, link)
        return [(step, link) for link, _ in links]

    def move_planes(self, step):
        up, down = self.mine["plane", step - 1], self.mine["plane", 1 - step]
        up = over_plane(up, [(at, at + 1) for at in range(step - 1, 3)])
        down = over_plane(down, [(at, at - 1) for at in range(4 - step, 0, -1)])
        self.mine["plane", step], self.mine["plane", -step] = up, down
        return [("plane", step), ("plane", -step)]

    def cross(self, keys):
        for key in keys:
            self.theirs[key] = over_core(self.mine[key])
        return keys

    def join(self, outputs, mine=(), theirs=()):
        values = [self.mine[key] for key in mine] + [self.theirs[key] for key in theirs]
        outputs, values = under(outputs, *values)
        for key, value in zip(mine, values):
            self.mine[key] = value
        for key, value in zip(theirs, values[len(mine) :]):
            self.theirs[key] = value
        return outputs

    def layer(self, layer):
        arrays, places = list(self.own), {}

        def place(key):
            if key not in places:
                places[key] = len(arrays)
                arrays.extend([self.mine[key], self.theirs[key]])
            return places[key], places[key] + 1

        if layer in "ac":
            names = [(layer + str(index), ATTEND_BLOCKS[index]) for index in range(2)]
        else:
            names = [(layer + str(index), EXPERT_BLOCKS[index]) for index in range(4)]
        plan = []
        for at in range(SECTIONS):
            if layer == "g":
                names = [("g" + str(at), (0, 1))]
            if HOMES[layer] == at:
                steps = []
                for name, blocks in names:
                    for block in blocks:
                        source = block * 4 if layer == "g" else block
                        steps.append((block, ("own",) + self.place(layer, source)))
                plan.append((at, None, steps))
                continue
            by_plane = layer == "f" and self.four
            for plane in range(4) if by_plane else (None,):
                steps = []
                for index, (name, blocks) in enumerate(names):
                    key = ("plane", plane - index) if by_plane else self.arrived[at, name]
                    for which, block in enumerate(blocks):
                        steps.append((block, ("piece",) + place(key) + (which,)))
                plan.append((at, plane, steps))
        return arrays, plan


def per_device(
    tokens,
    caption_lengths,
    attend_gain,
    attend_shift,
    attend_inputs,
    attend_bias,
    attend_output,
    expert_gain,
    expert_shift,
    expert_inputs,
    expert_inner_bias,
    expert_outputs,
    expert_outer_bias,
    cotangent,
):
    section, core, plane = lax.axis_index("section"), lax.axis_index("core"), lax.axis_index("z")
    planes = lax.axis_size("z")
    items, positions, width = tokens.shape
    hidden = expert_inputs.shape[-1]
    info = [value.reshape(1).astype(jnp.int32) for value in (section, core, plane)]
    info = jnp.concatenate([caption_lengths] + info)
    weights = Weights(
        (attend_inputs[0], attend_output[0], expert_inputs[0], expert_outputs[0]), info, planes
    )

    def to_sections(value):
        return [value] + [over_section(value, bits) for bits in (1, 2, 3)]

    def items_of(part):
        return part.reshape(items, CAP_ROWS, width)

    keys = weights.move(0, weights.payloads(0))
    pad = ((0, 0), (0, ROWS - positions), (0, 0))
    x0 = jnp.pad(tokens, pad)
    last_grad = jnp.pad(cotangent, pad)
    rows = jnp.concatenate(
        [
            attend_gain,
            attend_shift,
            attend_bias,
            expert_gain,
            expert_shift,
            expert_inner_bias,
            expert_outer_bias,
            jnp.full((1, 128), jnp.sum(caption_lengths), F32),
        ],
        axis=1,
    )
    rows = to_sections(rows)
    x0, last_grad, *rows = weights.join([x0, last_grad, *rows], keys)
    keys1 = weights.move(1, weights.payloads(1))
    rows = jnp.concatenate(rows, axis=0)
    language_count = jnp.sum(rows[:, -128:], axis=0, keepdims=True)
    rows = [lax.dynamic_index_in_dim(rows, at ^ section, 0) for at in range(SECTIONS)]
    sizes = [width, width, 3 * width, width, width, hidden, width]
    ends = [sum(sizes[: at + 1]) for at in range(len(sizes))]
    used = [(0, 0), (0, 1), (0, 2), (0, 3), (0, 4), (0, 5), (1, 3), (1, 4), (1, 5), (1, 6)]
    used += [(0, 6), (2, 0), (2, 1), (2, 2), (3, 3), (3, 4), (3, 5), (3, 6)]
    kept = [rows[slot][:, ends[which] - sizes[which] : ends[which]] for slot, which in used]
    language_count, *kept = weights.join([language_count, *kept], keys1)
    kept = dict(zip(used, kept))

    def row(slot, which):
        return kept[slot, which]

    crossed = weights.cross(keys + keys1)
    sends = weights.payloads(2, "F") if weights.four else weights.payloads(2)
    sends, (info, language_count) = under(sends, info, language_count)
    keys = weights.move(2, sends[:2])
    info, language_count = weights.join(
        [info, language_count + over_core(language_count)], theirs=crossed
    )
    plane_keys = []
    if weights.four:
        weights.mine["plane", 0] = sends[2]
        plane_keys = weights.move_planes(1)
    attend0 = weights.layer("a")
    outputs = attend_forward(
        x0, info, attend0, row(0, 0), row(0, 1), row(0, 2), following=(row(0, 3), row(0, 4))
    )
    y0, qkv0, mixed0, caption_rows = weights.join(outputs, keys)
    caption_rows = to_sections(caption_rows.reshape(-1, width))
    sends = weights.payloads(3, 4) if weights.four else weights.payloads(3)
    caption_rows = weights.join(caption_rows, plane_keys)
    sends, caption_rows = under(sends, *caption_rows)
    early_keys = keys
    keys, sends = weights.move(3, sends[:2]), sends[2:]
    crossed = weights.cross(early_keys)
    if weights.four:
        keys += weights.move_planes(2)
    outputs = shared_forward(caption_rows, expert_inputs[0], expert_inner_bias, expert_outputs[0])
    part = weights.join(outputs, keys, crossed)
    (y0,) = weights.join([y0], theirs=weights.cross([(3, 0), (3, 1)]))
    branch = {at: over_section(part[at], at, [0]) for at in range(1, SECTIONS)}
    keys = weights.move_planes(3) if weights.four else []
    expert1 = weights.layer("e")
    outputs = expert_forward(
        y0, info, expert1, row(1, 3), row(1, 4), row(1, 5), row(1, 6), PATCH_ROWS, "patch"
    )
    outputs, moved = under(outputs, *branch.values())
    if weights.four:
        keys += [("plane", step) for step in range(-2, 3)]
    x2, act1, slope1 = weights.join(outputs, keys)
    branch = dict(zip(branch, moved))
    branch[0] = part[0]
    branch = items_of(by_section(section, branch))
    if weights.four:
        crossed = [("plane", step) for step in range(-3, 4)]
    else:
        for step in (4, 5):
            weights.move(step, weights.payloads(step))
        crossed = [(4, 0), (4, 1), (5, 0)]
    weights.cross(crossed)
    attend2 = weights.layer("c") if weights.four else None
    if not weights.four:
        (x2,) = weights.join([x2], theirs=crossed)
        attend2 = weights.layer("c")
    outputs = attend_forward(
        x2, info, attend2, row(2, 0), row(2, 1), row(2, 2), merge=(y0, branch, row(0, 6))
    )
    if weights.four:
        language_count += over_plane(language_count, [(at, at ^ 1) for at in range(4)])
    x3, qkv2, mixed2, x2, language_count = weights.join([*outputs, language_count], theirs=crossed)
    if weights.four:
        language_count += over_plane(language_count, [(at, at ^ 2) for at in range(4)])
    else:
        language_count = lax.psum(language_count, "z")
    expert3 = weights.layer("f")
    outputs = expert_forward(
        x3, info, expert3, row(3, 3), row(3, 4), row(3, 5), row(3, 6), ROWS, "all"
    )
    layer_output, act3, slope3, language_count = under([*outputs, language_count])[0]
    language_count = language_count[0, 0].astype(jnp.int32)
    vision_count = PATCHES * items * SECTIONS * 2 * planes
    counts = jnp.stack(
        [jnp.full((), vision_count, jnp.int32), language_count, language_count + vision_count]
    )

    def small_rows(values):
        flat = jnp.concatenate(values, axis=1)
        count = -(-flat.shape[1] // hidden)
        flat = jnp.pad(flat, ((0, 0), (0, count * hidden - flat.shape[1])))
        return flat.reshape(count, hidden)

    def to_home(sums):
        got = [by_section(section, sums)]
        for bits in (1, 2, 3):
            sends = {at ^ bits: sums[at] for at in sums}
            got.append(over_section(by_section(section, sends), bits, sorted(sends)))
        return got

    keys = []
    if weights.four:
        sends, (layer_output, last_grad) = under(sends, layer_output, last_grad)
        keys = weights.move(4, sends)
    outputs = expert_backward(
        x3, info, expert3, row(3, 3), row(3, 4), act3, slope3, last_grad, ROWS, "all"
    )
    outputs = weights.join(outputs, keys)
    crossed = weights.cross(keys)
    grad3, *small3 = outputs[:5]
    sums3 = Sums(outputs[5:])
    sums3.cross()
    moved = over_links(sums3.first_sends())
    grad3 = after(grad3, *sums3.sent)
    outputs = attend_backward(
        x2, info, attend2, row(2, 0), row(2, 1), qkv2, mixed2, grad3
    )
    outputs, moved = under(outputs, *moved, sums3.got_stay)
    outputs = weights.join(outputs, theirs=crossed)
    grad2, *small2 = outputs[:4]
    sums2, caption_grad = Sums(outputs[4:8]), outputs[8]
    caption_grads = to_sections(caption_grad.reshape(-1, width))
    sums3.got_stay = moved[2]
    moved3 = over_links(sums3.second_sends(*moved[:2]))
    grad2 = after(grad2, *sums3.sent)
    outputs = expert_backward(
        y0, info, expert1, row(1, 3), row(1, 4), act1, slope1, grad2, PATCH_ROWS, "patch"
    )
    outputs, caption_grads = under(outputs, *caption_grads)
    grad1, *small1 = outputs[:5]
    sums2.cross(grad1)
    sums1 = Sums(outputs[5:])
    sums1.cross()
    inner_quarter = lax.dynamic_slice(row(0, 5), (0, section * width), (1, width))
    sum3 = sums3.whole(*moved3)
    inner_quarter = after(inner_quarter, grad1, sum3)
    outputs = shared_backward(
        caption_rows, caption_grads, info, weights.layer("g"), inner_quarter
    )
    parts, (keep0, send0, inner_grad, outer_grad) = outputs[:4], outputs[4:]
    got = [over_section(parts[bits], bits) for bits in (1, 2, 3)]
    sends = [after(value, *parts) for value in sums1.first_sends()]
    moved1 = over_links(sends)
    keep0 = added(keep0, over_core(send0))
    early = lax.psum(jnp.concatenate([sum3, keep0], axis=0), "z")
    sends2 = [after(value, *sends) for value in sums2.first_sends()]
    moved2 = over_links(sends2)
    parts = [parts[0], *got]
    grad1 = after(grad1, keep0, *sends, *sends2)
    outputs = attend_backward(
        x0,
        info,
        attend0,
        row(0, 0),
        row(0, 1),
        qkv0,
        mixed0,
        grad1,
        first=(y0, row(0, 3), parts),
    )
    outputs, moved = under(outputs, *moved2, *moved1)
    moved2, moved1 = moved[:2], moved[2:]
    tokens_grad, *small_first = outputs[:4]
    sums_first, gain_grad, shift_grad = Sums(outputs[4:8]), outputs[8], outputs[9]
    sums_first.cross()
    inner_grad = lax.dynamic_update_slice(
        jnp.zeros((1, hidden), F32), inner_grad, (0, section * width)
    )
    small = small_rows(
        small_first + [gain_grad, shift_grad, inner_grad, outer_grad] + small2 + small1 + small3
    )
    small = added(small, over_core(small))
    to_x, to_y = sums_first.first_sends()
    to_x = jnp.concatenate([to_x[0], small], axis=0)
    sends = lax.optimization_barrier((*sums1.second_sends(*moved1), to_x, to_y))
    moved1, moved = over_links(sends[:2]), over_links(sends[2:])
    sum1, early = lax.optimization_barrier((sums1.whole(*moved1), early))
    planes1 = Planes(sum1, plane, planes)
    size = to_y.shape[1]
    small = added(small, moved[0][size:])
    to_x, to_y = sums_first.second_sends(moved[0][None, :size], moved[1])
    early_x, early_y = sums2.second_sends(*moved2)
    to_x = jnp.concatenate([to_x[0], early_x[0]], axis=0)
    to_y = jnp.concatenate([to_y[0], early_y[0], small], axis=0)
    to_x, to_y = lax.optimization_barrier((to_x, to_y))
    sent1 = planes1.sends()
    moved = lax.optimization_barrier(tuple(over_links((to_x, to_y))))
    size = early_x.shape[1]
    last = sums_first.whole(moved[0][None, :size], moved[1][None, :size])
    sum2 = sums2.whole(moved[0][None, size:], moved[1][None, size : 2 * size])
    small = added(small, moved[1][2 * size :])
    small_count = small.shape[0]
    eighth = last.shape[1]
    last = jnp.concatenate([last[0], sum2[0], small], axis=0)
    planes_last = Planes(last, plane, planes)
    home_early = to_home({0: after(early[2:], *moved), 3: after(early[:2], *moved)})
    planes_last.take(*planes_last.sends())
    planes1.take(*sent1)
    planes1.take(*planes1.sends())
    planes1.take(*planes1.sends())
    planes1.take(*planes1.sends())
    planes_last.take(*planes_last.sends(*home_early[1:3]))
    planes_last.take(*planes_last.sends(home_early[3]))
    home_late = to_home({1: after(planes1.value, *home_early[1:])})
    planes_last.take(*planes_last.sends())
    last = planes_last.value
    home_attend = to_home({0: last[None, :eighth], 2: last[None, eighth : 2 * eighth]})
    small = planes_last.in_order(last[2 * eighth :].astype(F32))

    as_float = counts.astype(F32)
    one = jnp.ones((), F32)
    attend_scales = jnp.stack([as_float[2], one, as_float[2], one])
    expert_scales = jnp.stack([as_float[1], as_float[0], one, as_float[2]])

    def placed(pieces, scales):
        scale = lax.dynamic_index_in_dim(scales, section, 0).reshape(1, 1)
        return finish(info, scale, pieces, [over_core(piece) for piece in pieces], planes)

    blank = jnp.zeros_like(home_late[0])
    inputs_whole, outputs_whole = placed(
        [
            after(by_section(section, {0: early, 1: late, 2: blank, 3: early}), *home_attend[1:])
            for early, late in zip(home_early, home_late)
        ],
        expert_scales,
    )
    blank = jnp.zeros_like(home_attend[0])
    attend_whole, output_whole = placed(
        [by_section(section, {0: got, 1: blank, 2: got, 3: blank}) for got in home_attend],
        attend_scales,
    )

    attend_size, expert_size = 5 * width, 3 * width + hidden
    cuts = [attend_size, attend_size + expert_size]
    cuts += [cuts[1] + attend_size, cuts[1] + attend_size + expert_size]
    small = jnp.split(small.reshape(-1)[: cuts[3] + expert_size], cuts)
    none_attend, none_expert = jnp.zeros_like(small[0]), jnp.zeros_like(small[1])
    attend_small = jnp.stack([small[0], none_attend, small[2], none_attend])
    expert_small = jnp.stack([small[1], small[3], none_expert, small[4]])
    attend_small = attend_small / attend_scales.reshape(-1, 1)
    expert_small = expert_small / expert_scales.reshape(-1, 1)
    attend_small = lax.dynamic_index_in_dim(attend_small, section, 0)
    expert_small = lax.dynamic_index_in_dim(expert_small, section, 0)
    return (
        layer_output[:, :positions],
        tokens_grad[:, :positions],
        attend_small[:, :width],
        attend_small[:, width : 2 * width],
        attend_whole,
        attend_small[:, 2 * width :],
        output_whole,
        expert_small[:, :width],
        expert_small[:, width : 2 * width],
        inputs_whole,
        expert_small[:, 2 * width : 2 * width + hidden],
        outputs_whole,
        expert_small[:, 2 * width + hidden :],
        counts,
    )


def solution(mesh):
    sections, groups = mesh.shape["section"], mesh.shape["dp"]
    split = Mesh(mesh.devices.reshape(sections, groups // 2, 2), ("section", "z", "core"))
    items = P(("section", "z", "core"), None, None)
    flat = P("section", None)
    matrix = P("section", None, None)
    placed = (
        items,
        P(("section", "z", "core")),
        flat,
        flat,
        matrix,
        flat,
        matrix,
        flat,
        flat,
        matrix,
        flat,
        matrix,
        flat,
        items,
    )
    return jax.shard_map(
        per_device,
        mesh=split,
        in_specs=placed,
        out_specs=(
            items,
            items,
            flat,
            flat,
            matrix,
            flat,
            matrix,
            flat,
            flat,
            matrix,
            flat,
            matrix,
            flat,
            P(),
        ),
        check_vma=False,
    )
```

```python
from functools import partial

import jax
import jax.numpy as jnp
from jax import lax
from jax.experimental import pallas as pl
from jax.experimental.pallas import tpu as pltpu
from jax.sharding import Mesh
from jax.sharding import PartitionSpec as P

HEADS = 12
HEAD_DIM = 64
PATCHES = 197
ROWS = 256
CAP_FIRST, CAP_ROWS = 192, 48
PATCH_ROWS = 208
PAIR = 2 * HEAD_DIM
SECTIONS = 4
PIECE_ROWS = 48
VMEM_BYTES = 58 * 1024 * 1024
F32 = jnp.float32
BF16 = jnp.bfloat16

PLAN_FOUR = (
    ({0: "a0", 1: "e0", 2: "c0", 3: "F"}, {0: "a1", 1: "e2", 2: "c0", 3: "F"}),
    ({0: "a1", 1: "e1", 2: "a1", 3: "e2"}, {0: "a0", 1: "a0", 2: "F", 3: "c0"}),
    ({0: "g3", 1: "e2", 2: "c1"}, {0: "e0", 1: "e3", 2: "c1"}),
    ({0: "g1", 1: "e3", 2: "e0", 3: "e3"}, {0: "e1", 1: "e1", 3: "c1"}),
    ({}, {0: "g2", 1: "g3"}),
)
PLAN_ANY = (
    ({0: "a0", 1: "e0", 2: "c0", 3: "f0"}, {0: "a1", 1: "e2", 2: "c0", 3: "f0"}),
    ({0: "a1", 1: "e1", 2: "a1", 3: "e2"}, {0: "a0", 1: "a0", 2: "c1", 3: "f1"}),
    ({0: "g3", 1: "e2", 2: "c1", 3: "f1"}, {0: "e0", 1: "e3", 2: "f0", 3: "f2"}),
    ({0: "g1", 1: "e3", 2: "e0", 3: "e3"}, {0: "e1", 1: "e1", 2: "f1", 3: "f3"}),
    ({0: "c1", 1: "f2", 3: "f2"}, {0: "g2", 1: "g3", 3: "c0"}),
    ({1: "f3", 3: "f3"}, {}),
)
HOMES = {"a": 0, "c": 2, "e": 1, "f": 3, "F": 3, "g": 0}
ATTEND_BLOCKS = ((0, 1), (2, 3))
EXPERT_BLOCKS = ((0, 1), (4, 5), (2, 3), (6, 7))


def dot_plain(left, right):
    return jnp.dot(left, right, preferred_element_type=F32)


def dot_last(left, right):
    return lax.dot_general(left, right, (((1,), (1,)), ((), ())), preferred_element_type=F32)


def dot_first(left, right):
    return lax.dot_general(left, right, (((0,), (0,)), ((), ())), preferred_element_type=F32)


def column_sum(matrix):
    return jnp.sum(matrix.astype(F32), axis=0, keepdims=True)


def norm_parts(rows):
    centre = rows - jnp.mean(rows, axis=-1, keepdims=True)
    scale = lax.rsqrt(jnp.mean(centre * centre, axis=-1, keepdims=True) + 1e-06)
    return centre * scale, scale


def norm_back(normed_grad, unit, scale, gain):
    unit_grad = normed_grad * gain
    along = jnp.mean(unit_grad * unit, axis=-1, keepdims=True)
    return scale * (unit_grad - jnp.mean(unit_grad, axis=-1, keepdims=True) - unit * along)


def true_positions(length, first, count, axis, kind):
    shape = (count, 1) if axis == 0 else (1, count)
    position = first + lax.broadcasted_iota(jnp.int32, shape, axis)
    patch = position < PATCHES
    if kind == "patch":
        return patch
    caption = (position >= PATCHES) & (position - PATCHES < length)
    return caption if kind == "caption" else patch | caption


def head_masks():
    lane = lax.broadcasted_iota(jnp.int32, (1, PAIR), 1)
    even = (lane < HEAD_DIM).astype(F32).astype(BF16)
    odd = (lane >= HEAD_DIM).astype(F32).astype(BF16)
    return lane < HEAD_DIM, even, odd


def split_pair(pair, even, odd):
    return jnp.concatenate([pair * even, pair * odd], axis=0)


def start_weights(info, first, refs, plan, blocks, sems):
    half = blocks.shape[1] // 2
    section, core, plane = info[first], info[first + 1], info[first + 2]
    for at, at_plane, steps in plan:
        here = section == at
        if at_plane is not None:
            here = here & (plane == at_plane)

        @pl.when(here)
        def _(steps=steps):
            for block, source in steps:
                if source[0] == "own":
                    _, which, row, column = source
                    width = blocks.shape[2]
                    for part in range(2):
                        pltpu.make_async_copy(
                            refs[which].at[
                                pl.ds(row + part * half, half), pl.ds(column, width)
                            ],
                            blocks.at[block, pl.ds(part * half, half)],
                            sems.at[block],
                        ).start()
                else:
                    _, mine, theirs, index = source
                    pltpu.make_async_copy(
                        refs[mine].at[index],
                        blocks.at[block, pl.ds(pl.multiple_of(core * half, half), half)],
                        sems.at[block],
                    ).start()
                    pltpu.make_async_copy(
                        refs[theirs].at[index],
                        blocks.at[block, pl.ds(pl.multiple_of((1 - core) * half, half), half)],
                        sems.at[block],
                    ).start()


def wait_block(blocks, block, sems):
    pltpu.make_async_copy(blocks.at[block], blocks.at[block], sems.at[block]).wait()


def store_turned(target, turned, columns, section, core):
    half = target.shape[0] // 2
    for piece in range(16):
        path, owner = (piece >> 2) & 1, piece & 3
        away = owner ^ section
        place = ((away & 1) << 1) | (away >> 1) if path == 0 else away
        row = ((piece >> 3) ^ core) * half + (place >> 1) * (half // 2)
        row = row + path * (half // 4) + (place & 1) * PIECE_ROWS
        target[pl.ds(pl.multiple_of(row, 16), PIECE_ROWS), columns] = turned[
            piece * PIECE_ROWS : (piece + 1) * PIECE_ROWS
        ]


def put_travel(refs, which, columns, left, right):
    half = left.shape[0] // 2
    for side in range(2):
        rows = dot_plain(left[side * half : (side + 1) * half], right).astype(BF16)
        refs[2 * side][which, :, columns] = rows[: half // 2]
        refs[2 * side + 1][which, :, columns] = rows[half // 2 :]


def attend_forward_kernel(plan, weight_count, merge, info, *refs):
    weights, refs = refs[:weight_count], refs[weight_count:]
    if merge:
        x_ref, before_ref, part_ref, outer_ref, gain_ref, shift_ref, bias_ref = refs[:7]
        y_ref, qkv_ref, mixed_ref, joined_ref, blocks, sems, joined = refs[7:]
    else:
        x_ref, gain_ref, shift_ref, bias_ref, next_gain_ref, next_shift_ref = refs[:6]
        y_ref, qkv_ref, mixed_ref, caption_ref, blocks, sems = refs[6:]
    item = pl.program_id(0)
    items = pl.num_programs(0)
    length = info[item]
    width = x_ref.shape[-1]

    @pl.when(item == 0)
    def _():
        start_weights(info, items, weights, plan, blocks, sems)

    cap = slice(CAP_FIRST, CAP_FIRST + CAP_ROWS)
    if merge:
        joined[...] = x_ref[0].astype(F32)
        branch = part_ref[0].astype(F32) + outer_ref[...]
        is_true = true_positions(length, CAP_FIRST, CAP_ROWS, 0, "caption")
        captions = before_ref[0, cap] + jnp.where(is_true, branch, 0.0)
        position = CAP_FIRST + lax.broadcasted_iota(jnp.int32, (CAP_ROWS, 1), 0)
        captions = captions.astype(BF16).astype(F32)
        joined[cap] = jnp.where(position < PATCHES, joined[cap], captions)
        x = joined[...]
        joined_ref[0] = x.astype(BF16)
    else:
        x = x_ref[0].astype(F32)
    unit, _ = norm_parts(x)
    normed = (unit * gain_ref[...] + shift_ref[...]).astype(BF16)

    @pl.when(item == 0)
    def _():
        for block in range(4):
            wait_block(blocks, block, sems)

    queries = dot_plain(normed, blocks[0]) + bias_ref[:, :width]
    qkv_ref[0, :, :width] = (queries * HEAD_DIM ** (-0.5)).astype(BF16)
    qkv_ref[0, :, width : 2 * width] = dot_plain(normed, blocks[1]).astype(BF16)
    values = dot_plain(normed, blocks[2]) + bias_ref[:, width : 2 * width]
    qkv_ref[0, :, 2 * width :] = values.astype(BF16)
    key_true = true_positions(length, 0, ROWS, 1, "all")
    low_half, even, odd = head_masks()
    ones = jnp.ones((ROWS, PAIR), BF16)

    def scores_of(pair):
        at = pair * PAIR
        q2 = qkv_ref[0, :, at : at + PAIR]
        k2 = qkv_ref[0, :, width + at : width + at + PAIR]
        return dot_last(split_pair(q2, even, odd), k2)

    ahead = [scores_of(0), scores_of(1)]
    for pair in range(HEADS // 2):
        at = pair * PAIR
        scores = jnp.where(key_true, ahead.pop(0), -1e9)
        if pair + 2 < HEADS // 2:
            ahead.append(scores_of(pair + 2))
        weight = jnp.exp(scores - jnp.max(scores, axis=-1, keepdims=True)).astype(BF16)
        v2 = qkv_ref[0, :, 2 * width + at : 2 * width + at + PAIR]
        summed = dot_plain(weight, jnp.concatenate([v2, ones], axis=1))
        top = jnp.where(low_half, summed[:ROWS, :PAIR], summed[ROWS:, :PAIR])
        below = jnp.where(low_half, summed[:ROWS, PAIR:], summed[ROWS:, PAIR:])
        mixed_ref[0, :, at : at + PAIR] = (top / below).astype(BF16)
    branch = dot_plain(mixed_ref[0], blocks[3]) + bias_ref[:, 2 * width :]
    row_true = true_positions(length, 0, ROWS, 0, "all")
    y = x + jnp.where(row_true, branch, 0.0)
    y_ref[0] = y.astype(y_ref.dtype)
    if not merge:
        unit, _ = norm_parts(y[cap])
        caption_ref[0] = (unit * next_gain_ref[...] + next_shift_ref[...]).astype(BF16)


def attend_backward_kernel(plan, weight_count, first, info, *refs):
    weights, refs = refs[:weight_count], refs[weight_count:]
    x_ref, gain_ref, shift_ref, qkv_ref, mixed_ref, grad_ref = refs[:6]
    if first:
        after_ref, next_gain_ref, *parts = refs[6:12]
        refs = refs[12:]
    else:
        refs = refs[6:]
    out_ref, gain_grad_ref, shift_grad_ref, bias_grad_ref = refs[:4]
    travel_refs = refs[4:8]
    if first:
        next_gain_grad_ref, next_shift_grad_ref, joined = refs[8], refs[9], refs[-1]
    else:
        caption_ref = refs[8]
    blocks, sems, normed_turned, mixed_turned, branch_all, projected, mixed_grad = refs[
        10 if first else 9 :
    ][:7]
    item = pl.program_id(0)
    items = pl.num_programs(0)
    length = info[item]
    section, core = info[items], info[items + 1]
    width = x_ref.shape[-1]
    here = pl.ds(pl.multiple_of(item * ROWS, ROWS), ROWS)
    cap = slice(CAP_FIRST, CAP_FIRST + CAP_ROWS)

    @pl.when(item == 0)
    def _():
        start_weights(info, items, weights, plan, blocks, sems)

    def add_to(ref, part):
        @pl.when(item == 0)
        def _():
            ref[...] = part

        @pl.when(item > 0)
        def _():
            ref[...] += part

    x = x_ref[0].astype(F32)
    unit, scale = norm_parts(x)
    normed = (unit * gain_ref[...] + shift_ref[...]).astype(BF16)
    incoming = grad_ref[0].astype(F32)
    if first:
        after_unit, after_scale = norm_parts(after_ref[0, cap])
        caption_grad = parts[0][...].astype(F32)
        for part in parts[1:]:
            caption_grad = caption_grad + part[...].astype(F32)
        joined[...] = incoming
        joined[cap] += norm_back(caption_grad, after_unit, after_scale, next_gain_ref[...])
        incoming = joined[...]
        add_to(next_gain_grad_ref, jnp.sum(caption_grad * after_unit, axis=0, keepdims=True))
        add_to(next_shift_grad_ref, jnp.sum(caption_grad, axis=0, keepdims=True))
    row_true = true_positions(length, 0, ROWS, 0, "all")
    branch = jnp.where(row_true, incoming, 0.0).astype(BF16)
    branch_all[here, :] = branch
    store_turned(normed_turned, normed.T, here, section, core)
    store_turned(mixed_turned, mixed_ref[0].T, here, section, core)

    @pl.when(item == 0)
    def _():
        for block in range(4):
            wait_block(blocks, block, sems)

    mixed_grad[...] = dot_last(branch, blocks[3]).astype(BF16)
    key_true = true_positions(length, 0, ROWS, 0, "all")
    _, even, odd = head_masks()

    def products_of(pair):
        at = pair * PAIR
        q2 = split_pair(qkv_ref[0, :, at : at + PAIR], even, odd)
        k2 = qkv_ref[0, :, width + at : width + at + PAIR]
        v2 = qkv_ref[0, :, 2 * width + at : 2 * width + at + PAIR]
        g2 = split_pair(mixed_grad[:, at : at + PAIR], even, odd)
        return q2, k2, g2, dot_last(k2, q2), dot_last(v2, g2)

    ahead = [products_of(0)]
    for pair in range(HEADS // 2):
        at = pair * PAIR
        q2, k2, g2, scores, weight_grad = ahead.pop(0)
        if pair + 1 < HEADS // 2:
            ahead.append(products_of(pair + 1))
        scores = jnp.where(key_true, scores, -1e9)
        weight = jnp.exp(scores - jnp.max(scores, axis=0, keepdims=True))
        weight = weight * (1.0 / jnp.sum(weight, axis=0, keepdims=True))
        product = weight * weight_grad
        along = jnp.sum(product, axis=0, keepdims=True)
        score_grad = (product - weight * along).astype(BF16)
        values_grad = dot_plain(weight.astype(BF16), g2).astype(BF16)
        keys_grad = dot_plain(score_grad, q2).astype(BF16)
        k2_split = split_pair(k2, even, odd)
        stacked = jnp.concatenate([score_grad[:, :ROWS], score_grad[:, ROWS:]], axis=0)
        queries_grad = dot_first(stacked, k2_split).astype(BF16)
        queries_grad = (queries_grad.astype(F32) * HEAD_DIM ** (-0.5)).astype(BF16)
        projected[here, at : at + PAIR] = queries_grad
        projected[here, width + at : width + at + PAIR] = keys_grad
        projected[here, 2 * width + at : 2 * width + at + PAIR] = values_grad
    normed_grad = dot_last(projected[here, :width], blocks[0])
    normed_grad += dot_last(projected[here, width : 2 * width], blocks[1])
    normed_grad += dot_last(projected[here, 2 * width :], blocks[2])
    out = (incoming + norm_back(normed_grad, unit, scale, gain_ref[...])).astype(BF16)
    out_ref[0] = out
    if not first:
        is_true = true_positions(length, CAP_FIRST, CAP_ROWS, 0, "caption")
        caption_ref[0] = jnp.where(is_true, out[cap].astype(F32), 0.0).astype(BF16)
    add_to(gain_grad_ref, jnp.sum(normed_grad * unit, axis=0, keepdims=True))
    add_to(shift_grad_ref, jnp.sum(normed_grad, axis=0, keepdims=True))

    @pl.when(item == items - 1)
    def _():
        for block in range(4):
            columns = slice(block * width, (block + 1) * width)
            left = normed_turned if block < 3 else mixed_turned
            right = projected[:, columns] if block < 3 else branch_all[...]
            put_travel(travel_refs, 0, columns, left, right)
        bias_grad_ref[:, :width] = column_sum(projected[:, :width])
        bias_grad_ref[:, width : 2 * width] = column_sum(projected[:, 2 * width :])
        bias_grad_ref[:, 2 * width :] = column_sum(branch_all[...])


SHORT = pl.CostEstimate(flops=0, bytes_accessed=100_000, transcendentals=0)
LONG = pl.CostEstimate(flops=30_000_000_000, bytes_accessed=30_000_000, transcendentals=0)
ANYWHERE = pl.BlockSpec(memory_space=pl.ANY)


def whole_block(shape):
    return pl.BlockSpec(shape, lambda step, info: (0,) * len(shape))


def item_block(shape):
    return pl.BlockSpec((1,) + shape[1:], lambda step, info: (step,) + (0,) * (len(shape) - 1))


def blocks_scratch(count, width):
    return [pltpu.VMEM((count, width, width), BF16), pltpu.SemaphoreType.DMA((count,))]


def attend_forward(x, info, weights, gain, shift, bias, merge=None, following=None):
    arrays, plan = weights
    items, _, width = x.shape
    row = whole_block((1, width))
    bias_row = whole_block((1, 3 * width))
    caption_shape = (items, CAP_ROWS, width)
    if merge is not None:
        before, part, outer = merge
        operands = (x, before, part, outer, gain, shift, bias)
        specs = [item_block(x.shape), item_block(x.shape), item_block(caption_shape)]
        specs += [row, row, row, bias_row]
        last_shape, kind, scratch = x.shape, BF16, [pltpu.VMEM((ROWS, width), F32)]
    else:
        operands = (x, gain, shift, bias, *following)
        specs = [item_block(x.shape), row, row, bias_row, row, row]
        last_shape, kind, scratch = caption_shape, F32, []
    return pl.pallas_call(
        partial(attend_forward_kernel, plan, len(arrays), merge is not None),
        grid_spec=pltpu.PrefetchScalarGridSpec(
            num_scalar_prefetch=1,
            grid=(items,),
            in_specs=[ANYWHERE] * len(arrays) + specs,
            out_specs=[
                item_block(x.shape),
                item_block((items, ROWS, 3 * width)),
                item_block((items, ROWS, width)),
                item_block(last_shape),
            ],
            scratch_shapes=blocks_scratch(4, width) + scratch,
        ),
        out_shape=[
            jax.ShapeDtypeStruct(x.shape, kind),
            jax.ShapeDtypeStruct((items, ROWS, 3 * width), BF16),
            jax.ShapeDtypeStruct((items, ROWS, width), BF16),
            jax.ShapeDtypeStruct(last_shape, BF16),
        ],
        compiler_params=pltpu.CompilerParams(vmem_limit_bytes=VMEM_BYTES),
        cost_estimate=SHORT,
        name="attend_forward",
    )(info, *arrays, *operands)


def attend_backward(x, info, weights, gain, shift, qkv, mixed, incoming, first=None):
    arrays, plan = weights
    items, _, width = x.shape
    half = width // 2
    row = whole_block((1, width))
    caption_shape = (items, CAP_ROWS, width)
    operands = (x, gain, shift, qkv, mixed, incoming)
    specs = [item_block(x.shape), row, row, item_block(qkv.shape), item_block(mixed.shape)]
    specs += [item_block(incoming.shape)]
    outs = [
        (item_block(x.shape), x.shape, BF16),
        (row, (1, width), F32),
        (row, (1, width), F32),
        (whole_block((1, 3 * width)), (1, 3 * width), F32),
    ]
    outs += [(whole_block((1, half // 2, 4 * width)), (1, half // 2, 4 * width), BF16)] * 4
    scratch = []
    if first is not None:
        after, next_gain, parts = first
        operands += (after, next_gain, *parts)
        caption_rows = pl.BlockSpec((CAP_ROWS, width), lambda step, info: (step, 0))
        specs += [item_block(after.shape), row] + [caption_rows] * 4
        outs += [(row, (1, width), F32)] * 2
        scratch = [pltpu.VMEM((ROWS, width), F32)]
    else:
        outs += [(item_block(caption_shape), caption_shape, BF16)]
    return pl.pallas_call(
        partial(attend_backward_kernel, plan, len(arrays), first is not None),
        grid_spec=pltpu.PrefetchScalarGridSpec(
            num_scalar_prefetch=1,
            grid=(items,),
            in_specs=[ANYWHERE] * len(arrays) + specs,
            out_specs=[spec for spec, _, _ in outs],
            scratch_shapes=blocks_scratch(4, width)
            + [
                pltpu.VMEM((width, items * ROWS), BF16),
                pltpu.VMEM((width, items * ROWS), BF16),
                pltpu.VMEM((items * ROWS, width), BF16),
                pltpu.VMEM((items * ROWS, 3 * width), BF16),
                pltpu.VMEM((ROWS, width), BF16),
            ]
            + scratch,
        ),
        out_shape=[jax.ShapeDtypeStruct(shape, kind) for _, shape, kind in outs],
        compiler_params=pltpu.CompilerParams(vmem_limit_bytes=VMEM_BYTES),
        cost_estimate=LONG,
        name="attend_backward",
    )(info, *arrays, *operands)


def normal_parts(u):
    t = pl.reciprocal(1.0 + 0.23164190 * jnp.abs(u), approx=True)
    bell = jnp.exp2((u * -0.7213475204444817) * u)
    poly = t * (
        0.127414796
        + t * (-0.142248368 + t * (0.7107068705 + t * (-0.7265760135 + t * 0.5307027145)))
    )
    tail = poly * bell
    return jnp.where(u < 0, tail, 1.0 - tail), bell


def inner_forward(normed, matrix, bias):
    inner = dot_plain(normed, matrix) + bias
    cumulative, bell = normal_parts(inner)
    slope = cumulative + (inner * 0.3989422804014327) * bell
    return (inner * cumulative).astype(BF16), slope.astype(BF16)


def expert_forward_kernel(plan, weight_count, count, kind, info, *refs):
    weights, refs = refs[:weight_count], refs[weight_count:]
    x_ref, gain_ref, shift_ref, inner_ref, outer_ref = refs[:5]
    y_ref, act_ref, slope_ref, blocks, sems, normed, total = refs[5:]
    step = pl.program_id(0)
    items, _, width = x_ref.shape

    @pl.when(step == 0)
    def _():
        start_weights(info, items, weights, plan, blocks, sems)
        for item in range(items):
            x = x_ref[item, :count].astype(BF16).astype(F32)
            unit, _ = norm_parts(x)
            normed[item * count : (item + 1) * count] = (
                unit * gain_ref[...] + shift_ref[...]
            ).astype(BF16)

    wait_block(blocks, step, sems)
    wait_block(blocks, step + 4, sems)
    for at in range(0, width, 256):
        columns = slice(at, at + 256)
        act, slope = inner_forward(normed[...], blocks[step, :, columns], inner_ref[:, columns])
        act_ref[:, columns] = act
        slope_ref[:, columns] = slope
    part = dot_plain(act_ref[...], blocks[step + 4])

    @pl.when(step == 0)
    def _():
        total[...] = part

    @pl.when(step > 0)
    def _():
        total[...] += part

    @pl.when(step == pl.num_programs(0) - 1)
    def _():
        for item in range(items):
            row_true = true_positions(info[item], 0, count, 0, kind)
            branch = total[item * count : (item + 1) * count] + outer_ref[...]
            x = x_ref[item, :count].astype(BF16).astype(F32)
            y_ref[item, :count] = (x + jnp.where(row_true, branch, 0.0)).astype(BF16)
            if count < ROWS:
                y_ref[item, count:] = jnp.zeros((ROWS - count, width), BF16)


def expert_backward_kernel(plan, weight_count, count, kind, info, *refs):
    weights, refs = refs[:weight_count], refs[weight_count:]
    x_ref, gain_ref, shift_ref, act_ref, slope_ref, grad_ref = refs[:6]
    out_ref, gain_grad_ref, shift_grad_ref, inner_grad_ref, outer_grad_ref = refs[6:11]
    travel_refs = refs[11:15]
    blocks, sems, normed_turned, branch_turned, branch, inner_all, total = refs[15:]
    step = pl.program_id(0)
    items, _, width = x_ref.shape
    section, core = info[items], info[items + 1]

    @pl.when(step == 0)
    def _():
        start_weights(info, items, weights, plan, blocks, sems)
        outer = None
        for item in range(items):
            here = slice(item * count, (item + 1) * count)
            unit, _ = norm_parts(x_ref[item, :count].astype(BF16).astype(F32))
            normed = (unit * gain_ref[...] + shift_ref[...]).astype(BF16)
            row_true = true_positions(info[item], 0, count, 0, kind)
            incoming = grad_ref[item, :count].astype(F32)
            masked = jnp.where(row_true, incoming, 0.0).astype(BF16)
            branch[here] = masked
            store_turned(normed_turned, normed.T, here, section, core)
            store_turned(branch_turned, masked.T, here, section, core)
            term = column_sum(masked)
            outer = term if outer is None else outer + term
        outer_grad_ref[...] = outer

    wait_block(blocks, step, sems)
    wait_block(blocks, step + 4, sems)
    for at in range(0, width, 256):
        columns = slice(at, at + 256)
        act_grad = dot_last(branch[...], blocks[step + 4, columns])
        inner = (slope_ref[:, columns].astype(F32) * act_grad).astype(BF16)
        inner_all[:, columns] = inner
        inner_grad_ref[:, columns] = column_sum(inner)
        put_travel(travel_refs, 0, columns, normed_turned, inner)
        put_travel(travel_refs, 1, columns, branch_turned, act_ref[:, columns])
    part = dot_last(inner_all[...], blocks[step])

    @pl.when(step == 0)
    def _():
        total[...] = part

    @pl.when(step > 0)
    def _():
        total[...] += part

    @pl.when(step == pl.num_programs(0) - 1)
    def _():
        gain_sum, shift_sum = None, None
        for item in range(items):
            unit, scale = norm_parts(x_ref[item, :count].astype(BF16).astype(F32))
            normed_grad = total[item * count : (item + 1) * count]
            gain_part = jnp.sum(normed_grad * unit, axis=0, keepdims=True)
            shift_part = jnp.sum(normed_grad, axis=0, keepdims=True)
            gain_sum = gain_part if gain_sum is None else gain_sum + gain_part
            shift_sum = shift_part if shift_sum is None else shift_sum + shift_part
            incoming = grad_ref[item, :count].astype(F32)
            hidden = incoming + norm_back(normed_grad, unit, scale, gain_ref[...])
            out_ref[item, :count] = hidden.astype(BF16)
            if count < ROWS:
                out_ref[item, count:] = grad_ref[item, count:]
        gain_grad_ref[...] = gain_sum
        shift_grad_ref[...] = shift_sum


def shared_forward_kernel(*refs):
    *rows_refs, inputs_ref, inner_ref, outputs_ref = refs[:7]
    *part_refs, normed, total = refs[7:]
    count = rows_refs[0].shape[0]
    step = pl.program_id(0)

    @pl.when(step == 0)
    def _():
        for index, ref in enumerate(rows_refs):
            normed[index * count : (index + 1) * count] = ref[...]
        total[...] = jnp.zeros_like(total)

    act, _ = inner_forward(normed[...], inputs_ref[...], inner_ref[...])
    total[...] += dot_plain(act, outputs_ref[...])

    @pl.when(step == pl.num_programs(0) - 1)
    def _():
        for index, ref in enumerate(part_refs):
            ref[...] = total[index * count : (index + 1) * count].astype(BF16)


def shared_backward_kernel(plan, weight_count, info, *refs):
    weights, refs = refs[:weight_count], refs[weight_count:]
    rows_refs, grad_refs, inner_ref = refs[:4], refs[4:8], refs[8]
    part_refs, (keep_ref, send_ref, inner_grad_ref, outer_grad_ref) = refs[9:13], refs[13:17]
    blocks, sems, normed, branch, matrix = refs[17:]
    count, width = rows_refs[0].shape
    half = width // 2
    first = info.shape[0] - 3
    core = info[first + 1]
    start_weights(info, first, weights, plan, blocks, sems)
    for index in range(SECTIONS):
        here = slice(index * count, (index + 1) * count)
        normed[here] = rows_refs[index][...]
        branch[here] = grad_refs[index][...]
    outer_grad_ref[...] = column_sum(grad_refs[0][...])
    wait_block(blocks, 0, sems)
    wait_block(blocks, 1, sems)
    part = None
    for at in range(0, width, 256):
        columns = slice(at, at + 256)
        act, slope = inner_forward(normed[...], blocks[0, :, columns], inner_ref[:, columns])
        act_grad = dot_last(branch[...], blocks[1, columns])
        inner = (slope.astype(F32) * act_grad).astype(BF16)
        inner_grad_ref[:, columns] = column_sum(inner)
        matrix[0, :, columns] = dot_first(normed[...], inner).astype(BF16)
        matrix[1, :, columns] = dot_first(branch[...], act).astype(BF16)
        term = dot_last(inner, blocks[0, :, columns])
        part = term if part is None else part + term
    for index, ref in enumerate(part_refs):
        ref[...] = part[index * count : (index + 1) * count].astype(BF16)
    quarter = half // 4
    for which in range(2):
        for group in range(4):
            columns = slice(group * width, (group + 1) * width)
            mine = pl.multiple_of(core * half, 16) + group * quarter
            other = pl.multiple_of((1 - core) * half, 16) + group * quarter
            keep_ref[which, :, columns] = matrix[which, pl.ds(pl.multiple_of(mine, 16), quarter)]
            send_ref[which, :, columns] = matrix[which, pl.ds(pl.multiple_of(other, 16), quarter)]


def chunk_columns(rows, width):
    return pl.BlockSpec((rows, width), lambda step, info: (0, step))


def expert_forward(x, info, weights, gain, shift, inner, outer, count, kind):
    arrays, plan = weights
    items, _, width = x.shape
    hidden = inner.shape[1]
    row = whole_block((1, width))
    return pl.pallas_call(
        partial(expert_forward_kernel, plan, len(arrays), count, kind),
        grid_spec=pltpu.PrefetchScalarGridSpec(
            num_scalar_prefetch=1,
            grid=(hidden // width,),
            in_specs=[ANYWHERE] * len(arrays)
            + [whole_block(x.shape), row, row, chunk_columns(1, width), row],
            out_specs=[
                whole_block((items, ROWS, width)),
                chunk_columns(items * count, width),
                chunk_columns(items * count, width),
            ],
            scratch_shapes=blocks_scratch(8, width)
            + [
                pltpu.VMEM((items * count, width), BF16),
                pltpu.VMEM((items * count, width), F32),
            ],
        ),
        out_shape=[
            jax.ShapeDtypeStruct((items, ROWS, width), BF16),
            jax.ShapeDtypeStruct((items * count, hidden), BF16),
            jax.ShapeDtypeStruct((items * count, hidden), BF16),
        ],
        compiler_params=pltpu.CompilerParams(vmem_limit_bytes=VMEM_BYTES),
        cost_estimate=SHORT,
        name="expert_forward_" + kind,
    )(info, *arrays, x, gain, shift, inner, outer)


def expert_backward(x, info, weights, gain, shift, act, slope, incoming, count, kind):
    arrays, plan = weights
    items, _, width = x.shape
    half = width // 2
    hidden = act.shape[1]
    row = whole_block((1, width))
    travel = pl.BlockSpec((2, half // 2, width), lambda step, info: (0, 0, step))
    return pl.pallas_call(
        partial(expert_backward_kernel, plan, len(arrays), count, kind),
        grid_spec=pltpu.PrefetchScalarGridSpec(
            num_scalar_prefetch=1,
            grid=(hidden // width,),
            in_specs=[ANYWHERE] * len(arrays)
            + [
                whole_block(x.shape),
                row,
                row,
                chunk_columns(items * count, width),
                chunk_columns(items * count, width),
                whole_block(incoming.shape),
            ],
            out_specs=[whole_block(incoming.shape), row, row, chunk_columns(1, width), row]
            + [travel] * 4,
            scratch_shapes=blocks_scratch(8, width)
            + [
                pltpu.VMEM((width, items * count), BF16),
                pltpu.VMEM((width, items * count), BF16),
                pltpu.VMEM((items * count, width), BF16),
                pltpu.VMEM((items * count, width), BF16),
                pltpu.VMEM((items * count, width), F32),
            ],
        ),
        out_shape=[
            jax.ShapeDtypeStruct(incoming.shape, BF16),
            jax.ShapeDtypeStruct((1, width), F32),
            jax.ShapeDtypeStruct((1, width), F32),
            jax.ShapeDtypeStruct((1, hidden), F32),
            jax.ShapeDtypeStruct((1, width), F32),
        ]
        + [jax.ShapeDtypeStruct((2, half // 2, hidden), BF16)] * 4,
        compiler_params=pltpu.CompilerParams(vmem_limit_bytes=VMEM_BYTES),
        cost_estimate=SHORT,
        name="expert_backward_" + kind,
    )(info, *arrays, x, gain, shift, act, slope, incoming)


IN_VMEM = pl.BlockSpec(memory_space=pltpu.VMEM)
IN_SMEM = pl.BlockSpec(memory_space=pltpu.SMEM)


def shared_forward(rows, inputs, inner, outputs):
    count, width = rows[0].shape
    total = SECTIONS * count
    hidden = inner.shape[1]
    return pl.pallas_call(
        shared_forward_kernel,
        grid=(hidden // width,),
        in_specs=[pl.BlockSpec(rows[0].shape, lambda step: (0, 0))] * 4
        + [
            pl.BlockSpec((width, width), lambda step: (0, step)),
            pl.BlockSpec((1, width), lambda step: (0, step)),
            pl.BlockSpec((width, width), lambda step: (step, 0)),
        ],
        out_specs=[pl.BlockSpec((count, width), lambda step: (0, 0))] * SECTIONS,
        scratch_shapes=[pltpu.VMEM((total, width), BF16), pltpu.VMEM((total, width), F32)],
        out_shape=[jax.ShapeDtypeStruct((count, width), BF16)] * SECTIONS,
        compiler_params=pltpu.CompilerParams(vmem_limit_bytes=VMEM_BYTES),
        cost_estimate=SHORT,
        name="shared_forward",
    )(*rows, inputs, inner, outputs)


def shared_backward(rows, grads, info, weights, inner):
    arrays, plan = weights
    count, width = rows[0].shape
    total = SECTIONS * count
    travel = (2, width // 8, 4 * width)
    return pl.pallas_call(
        partial(shared_backward_kernel, plan, len(arrays)),
        in_specs=[IN_SMEM] + [ANYWHERE] * len(arrays) + [IN_VMEM] * 9,
        out_specs=[IN_VMEM] * 8,
        scratch_shapes=blocks_scratch(2, width)
        + [
            pltpu.VMEM((total, width), BF16),
            pltpu.VMEM((total, width), BF16),
            pltpu.VMEM((2, width, width), BF16),
        ],
        out_shape=[
            *[jax.ShapeDtypeStruct((count, width), BF16)] * SECTIONS,
            jax.ShapeDtypeStruct(travel, BF16),
            jax.ShapeDtypeStruct(travel, BF16),
            jax.ShapeDtypeStruct((1, width), F32),
            jax.ShapeDtypeStruct((1, width), F32),
        ],
        compiler_params=pltpu.CompilerParams(vmem_limit_bytes=VMEM_BYTES),
        cost_estimate=SHORT,
        name="shared_backward",
    )(info, *arrays, *rows, *grads, inner)


def plane_turn(plane, planes):
    return ((plane & 1) << 1) | (plane >> 1) if planes == 4 else 0


def finish_kernel(planes, info, scale_ref, *refs):
    step = pl.program_id(0)
    mine, theirs, outs, placed = refs[:4], refs[4:8], refs[8:-1], refs[-1]
    count = mine[0].shape[0]
    width = placed.shape[1]
    half = width // 2
    at = info.shape[0] - 3
    section, core = info[at], info[at + 1]
    turn = plane_turn(info[at + 2], planes)
    turned = turn if count == 1 else jnp.where(section == 1, turn, 0)
    scale = scale_ref[0, 0]
    columns = pl.ds(pl.multiple_of((step ^ turned) * width, width), width)

    def place(which):
        def by_rows():
            for side, pieces in enumerate((mine, theirs)):
                for away, ref in enumerate(pieces):
                    for path in range(2):
                        row = (core ^ side) * half + path * (half // 2)
                        row = row + (section ^ away) * PIECE_ROWS
                        placed[pl.ds(pl.multiple_of(row, 16), PIECE_ROWS), :] = ref[
                            which, path * PIECE_ROWS : (path + 1) * PIECE_ROWS, columns
                        ].astype(F32)

        def by_columns():
            for side, pieces in enumerate((mine, theirs)):
                for away, ref in enumerate(pieces):

                    @pl.when(step == away)
                    def _(side=side, ref=ref):
                        for group in range(4):
                            quarter = half // 4
                            row = (core ^ side) * half + group * quarter
                            placed[pl.ds(pl.multiple_of(row, 16), quarter), :] = ref[
                                which, :, group * width : (group + 1) * width
                            ].astype(F32)

        if count == 1:
            by_rows()
        else:
            pl.when(section != 0)(by_rows)
            pl.when(section == 0)(by_columns)

    place(0)
    if count == 1:

        @pl.when(step < 3)
        def _():
            outs[0][0] = placed[...] / scale

        @pl.when(step == 3)
        def _():
            outs[1][0] = placed[...] / scale

    else:
        outs[0][0] = placed[...] / scale
        place(1)
        outs[1][0] = (placed[...] / scale).T


def finish(info, scale, mine, theirs, planes):
    count, _, hidden = mine[0].shape
    width = hidden // 4
    if count == 1:
        shapes = [(1, width, 3 * width), (1, width, width)]
        maps = [lambda step, info: (0, 0, jnp.minimum(step, 2)), lambda step, info: (0, 0, 0)]
    else:
        shapes = [(1, width, hidden), (1, hidden, width)]
        maps = [lambda step, info: (0, 0, step), lambda step, info: (0, step, 0)]
    return pl.pallas_call(
        partial(finish_kernel, planes),
        grid_spec=pltpu.PrefetchScalarGridSpec(
            num_scalar_prefetch=1,
            grid=(4,),
            in_specs=[IN_SMEM] + [whole_block(mine[0].shape)] * 8,
            out_specs=[pl.BlockSpec((1, width, width), at) for at in maps],
            scratch_shapes=[pltpu.VMEM((width, width), F32)],
        ),
        out_shape=[jax.ShapeDtypeStruct(shape, F32) for shape in shapes],
        compiler_params=pltpu.CompilerParams(vmem_limit_bytes=VMEM_BYTES),
        cost_estimate=SHORT,
        name="finish",
    )(info, scale, *mine, *theirs)


def pack_kernel(count, plan, info, *refs):
    sources, outs, sems = refs[:count], refs[count:-1], refs[-1]
    first = info.shape[0] - 3
    section, core, plane = info[first], info[first + 1], info[first + 2]
    half = outs[0].shape[1]
    for index, (out, choices) in enumerate(zip(outs, plan)):
        for at, at_plane, parts in choices:
            here = section == at
            if at_plane is not None:
                here = here & (plane == at_plane)

            @pl.when(here)
            def _(index=index, out=out, parts=parts):
                for block, part in enumerate(parts):
                    if part[0] == "own":
                        _, which, row, column = part
                        rows = pl.ds(pl.multiple_of(row + core * half, half), half)
                        source = sources[which].at[rows, pl.ds(column, out.shape[2])]
                    else:
                        source = sources[part[1]].at[block]
                    pltpu.make_async_copy(source, out.at[block], sems.at[index, block]).start()

    for index, out in enumerate(outs):
        for block in range(2):
            pltpu.make_async_copy(out.at[block], out.at[block], sems.at[index, block]).wait()


def pack(info, sources, plan, shape):
    return pl.pallas_call(
        partial(pack_kernel, len(sources), plan),
        in_specs=[IN_SMEM] + [ANYWHERE] * len(sources),
        out_specs=[IN_VMEM] * len(plan),
        scratch_shapes=[pltpu.SemaphoreType.DMA((len(plan), 2))],
        out_shape=[jax.ShapeDtypeStruct(shape, BF16)] * len(plan),
        cost_estimate=SHORT,
        name="pack",
    )(info, *sources)


def over_section(value, bits, sources=range(SECTIONS)):
    return lax.ppermute(value, "section", [(at, at ^ bits) for at in sources])


def over_core(value):
    return lax.ppermute(value, "core", [(0, 1), (1, 0)])


def over_plane(value, pairs):
    return lax.ppermute(value, "z", pairs)


def added(left, right):
    return (left.astype(F32) + right.astype(F32)).astype(BF16)


def after(value, *earlier):
    return lax.optimization_barrier((value,) + earlier)[0]


def under(outputs, *arrivals):
    joined = lax.optimization_barrier(tuple(outputs) + arrivals)
    return list(joined[: len(outputs)]), list(joined[len(outputs) :])


def by_section(section, values):
    result, last = None, None
    for at in sorted(values):
        if result is None:
            result = values[at]
        elif values[at] is not last:
            result = jnp.where(section >= at, values[at], result)
        last = values[at]
    return result


def total(*values):
    result = values[0].astype(F32)
    for value in values[1:]:
        result = result + value.astype(F32)
    return result.astype(BF16)


class Sums:
    def __init__(self, travel):
        self.stay, self.move, self.other_stay, self.other_move = travel
        self.size = self.stay.shape[1] // 2

    def cross(self, *earlier):
        if earlier:
            self.other_move = after(self.other_move, *earlier)
            self.other_stay = after(self.other_stay, *earlier)
        self.got_move, self.got_stay = over_core(self.other_move), over_core(self.other_stay)

    def first_sends(self):
        size = self.size
        self.sent = [
            total(self.move[:, at : at + size], self.got_move[:, at : at + size])
            for at in (0, size)
        ]
        return self.sent

    def second_sends(self, from_x, from_y):
        size, half = self.size, self.size // 2
        self.first = from_x, from_y
        to_y = total(self.stay[:, half:size], self.got_stay[:, half:size], from_x[:, half:])
        to_x = total(
            self.stay[:, size + half :], self.got_stay[:, size + half :], from_y[:, half:]
        )
        self.sent = [to_x, to_y]
        return self.sent

    def whole(self, from_x, from_y):
        size, half = self.size, self.size // 2
        parts = []
        for at, first, second in ((0, self.first[0], from_y), (size, self.first[1], from_x)):
            here = slice(at, at + half)
            parts.append(total(self.stay[:, here], self.got_stay[:, here], first[:, :half], second))
        return jnp.concatenate(parts, axis=1)


def over_links(sends):
    return [over_section(sends[0], 1), over_section(sends[1], 2)]


class Planes:
    def __init__(self, value, plane, planes):
        self.value, self.plane, self.planes, self.turn = value, plane, planes, 0

    def sends(self, *earlier):
        value = after(self.value, *earlier) if earlier else self.value
        if self.planes != 4:
            return (value,)
        bits = (1, 2, 2, 1)[self.turn]
        if self.turn < 2:
            bit = (self.plane & 1, self.plane >> 1)[self.turn]
            size = value.shape[-1] // 2
            value = lax.dynamic_slice_in_dim(value, (1 - bit) * size, size, value.ndim - 1)
        return (over_plane(value, [(at, at ^ bits) for at in range(4)]),)

    def take(self, arrived):
        if self.planes != 4:
            self.value = lax.psum(arrived, "z") if self.turn == 3 else arrived
        elif self.turn < 2:
            bit = (self.plane & 1, self.plane >> 1)[self.turn]
            size = self.value.shape[-1] // 2
            keep = lax.dynamic_slice_in_dim(self.value, bit * size, size, self.value.ndim - 1)
            self.value = added(keep, arrived)
        else:
            self.value = jnp.concatenate([self.value, arrived], axis=-1)
        self.turn += 1

    def in_order(self, value):
        if self.planes != 4:
            return value
        size, turn = value.shape[-1] // 4, plane_turn(self.plane, 4)
        parts = [
            lax.dynamic_slice_in_dim(value, (at ^ turn) * size, size, value.ndim - 1)
            for at in range(4)
        ]
        return jnp.concatenate(parts, axis=-1)


class Weights:
    def __init__(self, own, info, planes):
        self.own, self.info = own, info
        self.four = planes == 4
        self.plan = PLAN_FOUR if self.four else PLAN_ANY
        self.half, self.width = own[1].shape[0] // 2, own[1].shape[1]
        self.mine, self.theirs, self.arrived = {}, {}, {}

    def place(self, layer, block):
        if layer in "ac":
            return (0, 0, block * self.width) if block < 3 else (1, 0, 0)
        if layer == "g":
            return (2, 0, block * self.width) if block < 4 else (3, (block - 4) * self.width, 0)
        return (2, 0, block * self.width) if block < 4 else (3, (block - 4) * self.width, 0)

    def choices(self, sends, sources):
        result = []
        for at in range(SECTIONS):
            name = sends.get(at)
            if name is not None and HOMES[name[0]] != at:
                key = self.arrived[at, name]
                if key not in sources:
                    sources[key] = len(self.own) + len(sources)
                result.append((at, None, [("arrived", sources[key])] * 2))
                continue
            for plane in range(4) if name == "F" else (None,):
                piece = ("f" + str(plane)) if name == "F" else name or "a0"
                layer, index = piece[0], int(piece[1])
                if layer in "ac":
                    blocks = ATTEND_BLOCKS[index]
                else:
                    blocks = (index, 4 + index) if layer == "g" else EXPERT_BLOCKS[index]
                parts = [("own",) + self.place(layer, block) for block in blocks]
                result.append((at, plane, parts))
        return result

    def packed(self, wanted):
        sources = {}
        plan = [self.choices(sends, sources) for sends in wanted]
        arrays = list(self.own) + [self.mine[key] for key in sources]
        return pack(self.info, arrays, plan, (2, self.half, self.width))

    def sends(self, step):
        if step == "F":
            return [{at: "F" for at in range(SECTIONS)}]
        return [sends for sends in self.plan[step] if sends]

    def payloads(self, *steps):
        wanted = [sends for step in steps for sends in self.sends(step)]
        return list(self.packed(wanted))

    def move(self, step, payloads):
        links = [(link, sends) for link, sends in enumerate(self.plan[step]) if sends]
        for (link, sends), payload in zip(links, payloads):
            self.mine[step, link] = over_section(payload, link + 1, sorted(sends))
            for at, name in sends.items():
                self.arrived[at ^ (link + 1), name] = (step, link)
        return [(step, link) for link, _ in links]

    def move_planes(self, step):
        up, down = self.mine["plane", step - 1], self.mine["plane", 1 - step]
        up = over_plane(up, [(at, at + 1) for at in range(step - 1, 3)])
        down = over_plane(down, [(at, at - 1) for at in range(4 - step, 0, -1)])
        self.mine["plane", step], self.mine["plane", -step] = up, down
        return [("plane", step), ("plane", -step)]

    def cross(self, keys):
        for key in keys:
            self.theirs[key] = over_core(self.mine[key])
        return keys

    def join(self, outputs, mine=(), theirs=()):
        values = [self.mine[key] for key in mine] + [self.theirs[key] for key in theirs]
        outputs, values = under(outputs, *values)
        for key, value in zip(mine, values):
            self.mine[key] = value
        for key, value in zip(theirs, values[len(mine) :]):
            self.theirs[key] = value
        return outputs

    def layer(self, layer):
        arrays, places = list(self.own), {}

        def place(key):
            if key not in places:
                places[key] = len(arrays)
                arrays.extend([self.mine[key], self.theirs[key]])
            return places[key], places[key] + 1

        if layer in "ac":
            names = [(layer + str(index), ATTEND_BLOCKS[index]) for index in range(2)]
        else:
            names = [(layer + str(index), EXPERT_BLOCKS[index]) for index in range(4)]
        plan = []
        for at in range(SECTIONS):
            if layer == "g":
                names = [("g" + str(at), (0, 1))]
            if HOMES[layer] == at:
                steps = []
                for name, blocks in names:
                    for block in blocks:
                        source = block * 4 if layer == "g" else block
                        steps.append((block, ("own",) + self.place(layer, source)))
                plan.append((at, None, steps))
                continue
            by_plane = layer == "f" and self.four
            for plane in range(4) if by_plane else (None,):
                steps = []
                for index, (name, blocks) in enumerate(names):
                    key = ("plane", plane - index) if by_plane else self.arrived[at, name]
                    for which, block in enumerate(blocks):
                        steps.append((block, ("piece",) + place(key) + (which,)))
                plan.append((at, plane, steps))
        return arrays, plan


def per_device(
    tokens,
    caption_lengths,
    attend_gain,
    attend_shift,
    attend_inputs,
    attend_bias,
    attend_output,
    expert_gain,
    expert_shift,
    expert_inputs,
    expert_inner_bias,
    expert_outputs,
    expert_outer_bias,
    cotangent,
):
    section, core, plane = lax.axis_index("section"), lax.axis_index("core"), lax.axis_index("z")
    planes = lax.axis_size("z")
    items, positions, width = tokens.shape
    hidden = expert_inputs.shape[-1]
    info = [value.reshape(1).astype(jnp.int32) for value in (section, core, plane)]
    info = jnp.concatenate([caption_lengths] + info)
    weights = Weights(
        (attend_inputs[0], attend_output[0], expert_inputs[0], expert_outputs[0]), info, planes
    )

    def to_sections(value):
        return [value] + [over_section(value, bits) for bits in (1, 2, 3)]

    def items_of(part):
        return part.reshape(items, CAP_ROWS, width)

    keys = weights.move(0, weights.payloads(0))
    pad = ((0, 0), (0, ROWS - positions), (0, 0))
    x0 = jnp.pad(tokens, pad)
    last_grad = jnp.pad(cotangent, pad)
    rows = jnp.concatenate(
        [
            attend_gain,
            attend_shift,
            attend_bias,
            expert_gain,
            expert_shift,
            expert_inner_bias,
            expert_outer_bias,
            jnp.full((1, 128), jnp.sum(caption_lengths), F32),
        ],
        axis=1,
    )
    rows = to_sections(rows)
    x0, last_grad, *rows = weights.join([x0, last_grad, *rows], keys)
    keys1 = weights.move(1, weights.payloads(1))
    rows = jnp.concatenate(rows, axis=0)
    language_count = jnp.sum(rows[:, -128:], axis=0, keepdims=True)
    rows = [lax.dynamic_index_in_dim(rows, at ^ section, 0) for at in range(SECTIONS)]
    sizes = [width, width, 3 * width, width, width, hidden, width]
    ends = [sum(sizes[: at + 1]) for at in range(len(sizes))]
    used = [(0, 0), (0, 1), (0, 2), (0, 3), (0, 4), (0, 5), (1, 3), (1, 4), (1, 5), (1, 6)]
    used += [(0, 6), (2, 0), (2, 1), (2, 2), (3, 3), (3, 4), (3, 5), (3, 6)]
    kept = [rows[slot][:, ends[which] - sizes[which] : ends[which]] for slot, which in used]
    language_count, *kept = weights.join([language_count, *kept], keys1)
    kept = dict(zip(used, kept))

    def row(slot, which):
        return kept[slot, which]

    crossed = weights.cross(keys + keys1)
    sends = weights.payloads(2, "F") if weights.four else weights.payloads(2)
    sends, (info, language_count) = under(sends, info, language_count)
    keys = weights.move(2, sends[:2])
    info, language_count = weights.join(
        [info, language_count + over_core(language_count)], theirs=crossed
    )
    plane_keys = []
    if weights.four:
        weights.mine["plane", 0] = sends[2]
        plane_keys = weights.move_planes(1)
    attend0 = weights.layer("a")
    outputs = attend_forward(
        x0, info, attend0, row(0, 0), row(0, 1), row(0, 2), following=(row(0, 3), row(0, 4))
    )
    y0, qkv0, mixed0, caption_rows = weights.join(outputs, keys)
    caption_rows = to_sections(caption_rows.reshape(-1, width))
    sends = weights.payloads(3, 4) if weights.four else weights.payloads(3)
    caption_rows = weights.join(caption_rows, plane_keys)
    sends, caption_rows = under(sends, *caption_rows)
    early_keys = keys
    keys, sends = weights.move(3, sends[:2]), sends[2:]
    crossed = weights.cross(early_keys)
    if weights.four:
        keys += weights.move_planes(2)
    outputs = shared_forward(caption_rows, expert_inputs[0], expert_inner_bias, expert_outputs[0])
    part = weights.join(outputs, keys, crossed)
    (y0,) = weights.join([y0], theirs=weights.cross([(3, 0), (3, 1)]))
    branch = {at: over_section(part[at], at, [0]) for at in range(1, SECTIONS)}
    keys = weights.move_planes(3) if weights.four else []
    expert1 = weights.layer("e")
    outputs = expert_forward(
        y0, info, expert1, row(1, 3), row(1, 4), row(1, 5), row(1, 6), PATCH_ROWS, "patch"
    )
    outputs, moved = under(outputs, *branch.values())
    if weights.four:
        keys += [("plane", step) for step in range(-2, 3)]
    x2, act1, slope1 = weights.join(outputs, keys)
    branch = dict(zip(branch, moved))
    branch[0] = part[0]
    branch = items_of(by_section(section, branch))
    if weights.four:
        crossed = [("plane", step) for step in range(-3, 4)]
    else:
        for step in (4, 5):
            weights.move(step, weights.payloads(step))
        crossed = [(4, 0), (4, 1), (5, 0)]
    weights.cross(crossed)
    attend2 = weights.layer("c") if weights.four else None
    if not weights.four:
        (x2,) = weights.join([x2], theirs=crossed)
        attend2 = weights.layer("c")
    outputs = attend_forward(
        x2, info, attend2, row(2, 0), row(2, 1), row(2, 2), merge=(y0, branch, row(0, 6))
    )
    if weights.four:
        language_count += over_plane(language_count, [(at, at ^ 1) for at in range(4)])
    x3, qkv2, mixed2, x2, language_count = weights.join([*outputs, language_count], theirs=crossed)
    if weights.four:
        language_count += over_plane(language_count, [(at, at ^ 2) for at in range(4)])
    else:
        language_count = lax.psum(language_count, "z")
    expert3 = weights.layer("f")
    outputs = expert_forward(
        x3, info, expert3, row(3, 3), row(3, 4), row(3, 5), row(3, 6), ROWS, "all"
    )
    layer_output, act3, slope3, language_count = under([*outputs, language_count])[0]
    language_count = language_count[0, 0].astype(jnp.int32)
    vision_count = PATCHES * items * SECTIONS * 2 * planes
    counts = jnp.stack(
        [jnp.full((), vision_count, jnp.int32), language_count, language_count + vision_count]
    )

    def small_rows(values):
        flat = jnp.concatenate(values, axis=1)
        count = -(-flat.shape[1] // hidden)
        flat = jnp.pad(flat, ((0, 0), (0, count * hidden - flat.shape[1])))
        return flat.reshape(count, hidden)

    def to_home(sums):
        got = [by_section(section, sums)]
        for bits in (1, 2, 3):
            sends = {at ^ bits: sums[at] for at in sums}
            got.append(over_section(by_section(section, sends), bits, sorted(sends)))
        return got

    keys = []
    if weights.four:
        sends, (layer_output, last_grad) = under(sends, layer_output, last_grad)
        keys = weights.move(4, sends)
    outputs = expert_backward(
        x3, info, expert3, row(3, 3), row(3, 4), act3, slope3, last_grad, ROWS, "all"
    )
    outputs = weights.join(outputs, keys)
    crossed = weights.cross(keys)
    grad3, *small3 = outputs[:5]
    sums3 = Sums(outputs[5:])
    sums3.cross()
    moved = over_links(sums3.first_sends())
    grad3 = after(grad3, *sums3.sent)
    outputs = attend_backward(
        x2, info, attend2, row(2, 0), row(2, 1), qkv2, mixed2, grad3
    )
    outputs, moved = under(outputs, *moved, sums3.got_stay)
    outputs = weights.join(outputs, theirs=crossed)
    grad2, *small2 = outputs[:4]
    sums2, caption_grad = Sums(outputs[4:8]), outputs[8]
    caption_grads = to_sections(caption_grad.reshape(-1, width))
    sums3.got_stay = moved[2]
    moved3 = over_links(sums3.second_sends(*moved[:2]))
    grad2 = after(grad2, *sums3.sent)
    outputs = expert_backward(
        y0, info, expert1, row(1, 3), row(1, 4), act1, slope1, grad2, PATCH_ROWS, "patch"
    )
    outputs, caption_grads = under(outputs, *caption_grads)
    grad1, *small1 = outputs[:5]
    sums2.cross(grad1)
    sums1 = Sums(outputs[5:])
    sums1.cross()
    inner_quarter = lax.dynamic_slice(row(0, 5), (0, section * width), (1, width))
    sum3 = sums3.whole(*moved3)
    inner_quarter = after(inner_quarter, grad1, sum3)
    outputs = shared_backward(
        caption_rows, caption_grads, info, weights.layer("g"), inner_quarter
    )
    parts, (keep0, send0, inner_grad, outer_grad) = outputs[:4], outputs[4:]
    got = [over_section(parts[bits], bits) for bits in (1, 2, 3)]
    sends = [after(value, *parts) for value in sums1.first_sends()]
    moved1 = over_links(sends)
    keep0 = added(keep0, over_core(send0))
    early = lax.psum(jnp.concatenate([sum3, keep0], axis=0), "z")
    sends2 = [after(value, *sends) for value in sums2.first_sends()]
    moved2 = over_links(sends2)
    parts = [parts[0], *got]
    grad1 = after(grad1, keep0, *sends, *sends2)
    outputs = attend_backward(
        x0,
        info,
        attend0,
        row(0, 0),
        row(0, 1),
        qkv0,
        mixed0,
        grad1,
        first=(y0, row(0, 3), parts),
    )
    outputs, moved = under(outputs, *moved2, *moved1)
    moved2, moved1 = moved[:2], moved[2:]
    tokens_grad, *small_first = outputs[:4]
    sums_first, gain_grad, shift_grad = Sums(outputs[4:8]), outputs[8], outputs[9]
    sums_first.cross()
    inner_grad = lax.dynamic_update_slice(
        jnp.zeros((1, hidden), F32), inner_grad, (0, section * width)
    )
    small = small_rows(
        small_first + [gain_grad, shift_grad, inner_grad, outer_grad] + small2 + small1 + small3
    )
    small = added(small, over_core(small))
    to_x, to_y = sums_first.first_sends()
    to_x = jnp.concatenate([to_x[0], small], axis=0)
    sends = lax.optimization_barrier((*sums1.second_sends(*moved1), to_x, to_y))
    moved1, moved = over_links(sends[:2]), over_links(sends[2:])
    sum1, early = lax.optimization_barrier((sums1.whole(*moved1), early))
    planes1 = Planes(sum1, plane, planes)
    size = to_y.shape[1]
    small = added(small, moved[0][size:])
    to_x, to_y = sums_first.second_sends(moved[0][None, :size], moved[1])
    early_x, early_y = sums2.second_sends(*moved2)
    to_x = jnp.concatenate([to_x[0], early_x[0]], axis=0)
    to_y = jnp.concatenate([to_y[0], early_y[0], small], axis=0)
    to_x, to_y = lax.optimization_barrier((to_x, to_y))
    sent1 = planes1.sends()
    moved = lax.optimization_barrier(tuple(over_links((to_x, to_y))))
    size = early_x.shape[1]
    last = sums_first.whole(moved[0][None, :size], moved[1][None, :size])
    sum2 = sums2.whole(moved[0][None, size:], moved[1][None, size : 2 * size])
    small = added(small, moved[1][2 * size :])
    small_count = small.shape[0]
    eighth = last.shape[1]
    last = jnp.concatenate([last[0], sum2[0], small], axis=0)
    planes_last = Planes(last, plane, planes)
    home_early = to_home({0: after(early[2:], *moved), 3: after(early[:2], *moved)})
    planes_last.take(*planes_last.sends())
    planes1.take(*sent1)
    planes1.take(*planes1.sends())
    planes1.take(*planes1.sends())
    planes1.take(*planes1.sends())
    planes_last.take(*planes_last.sends())
    planes_last.take(*planes_last.sends())
    home_late = to_home({1: after(planes1.value, *home_early[1:3])})
    planes_last.take(*planes_last.sends())
    last = planes_last.value
    home_attend = to_home({0: last[None, :eighth], 2: last[None, eighth : 2 * eighth]})
    small = planes_last.in_order(last[2 * eighth :].astype(F32))

    as_float = counts.astype(F32)
    one = jnp.ones((), F32)
    attend_scales = jnp.stack([as_float[2], one, as_float[2], one])
    expert_scales = jnp.stack([as_float[1], as_float[0], one, as_float[2]])

    def placed(pieces, scales):
        scale = lax.dynamic_index_in_dim(scales, section, 0).reshape(1, 1)
        return finish(info, scale, pieces, [over_core(piece) for piece in pieces], planes)

    blank = jnp.zeros_like(home_late[0])
    inputs_whole, outputs_whole = placed(
        [
            after(by_section(section, {0: early, 1: late, 2: blank, 3: early}), *home_attend[1:])
            for early, late in zip(home_early, home_late)
        ],
        expert_scales,
    )
    blank = jnp.zeros_like(home_attend[0])
    attend_whole, output_whole = placed(
        [by_section(section, {0: got, 1: blank, 2: got, 3: blank}) for got in home_attend],
        attend_scales,
    )

    attend_size, expert_size = 5 * width, 3 * width + hidden
    cuts = [attend_size, attend_size + expert_size]
    cuts += [cuts[1] + attend_size, cuts[1] + attend_size + expert_size]
    small = jnp.split(small.reshape(-1)[: cuts[3] + expert_size], cuts)
    none_attend, none_expert = jnp.zeros_like(small[0]), jnp.zeros_like(small[1])
    attend_small = jnp.stack([small[0], none_attend, small[2], none_attend])
    expert_small = jnp.stack([small[1], small[3], none_expert, small[4]])
    attend_small = attend_small / attend_scales.reshape(-1, 1)
    expert_small = expert_small / expert_scales.reshape(-1, 1)
    attend_small = lax.dynamic_index_in_dim(attend_small, section, 0)
    expert_small = lax.dynamic_index_in_dim(expert_small, section, 0)
    return (
        layer_output[:, :positions],
        tokens_grad[:, :positions],
        attend_small[:, :width],
        attend_small[:, width : 2 * width],
        attend_whole,
        attend_small[:, 2 * width :],
        output_whole,
        expert_small[:, :width],
        expert_small[:, width : 2 * width],
        inputs_whole,
        expert_small[:, 2 * width : 2 * width + hidden],
        outputs_whole,
        expert_small[:, 2 * width + hidden :],
        counts,
    )


def solution(mesh):
    sections, groups = mesh.shape["section"], mesh.shape["dp"]
    split = Mesh(mesh.devices.reshape(sections, groups // 2, 2), ("section", "z", "core"))
    items = P(("section", "z", "core"), None, None)
    flat = P("section", None)
    matrix = P("section", None, None)
    placed = (
        items,
        P(("section", "z", "core")),
        flat,
        flat,
        matrix,
        flat,
        matrix,
        flat,
        flat,
        matrix,
        flat,
        matrix,
        flat,
        items,
    )
    return jax.shard_map(
        per_device,
        mesh=split,
        in_specs=placed,
        out_specs=(
            items,
            items,
            flat,
            flat,
            matrix,
            flat,
            matrix,
            flat,
            flat,
            matrix,
            flat,
            matrix,
            flat,
            P(),
        ),
        check_vma=False,
    )
```

```python
from functools import partial

import jax
import jax.numpy as jnp
from jax import lax
from jax.experimental import pallas as pl
from jax.experimental.pallas import tpu as pltpu
from jax.sharding import Mesh
from jax.sharding import PartitionSpec as P

HEADS = 12
HEAD_DIM = 64
PATCHES = 197
ROWS = 256
CAP_FIRST, CAP_ROWS = 192, 48
PATCH_ROWS = 208
PAIR = 2 * HEAD_DIM
SECTIONS = 4
PIECE_ROWS = 48
VMEM_BYTES = 58 * 1024 * 1024
F32 = jnp.float32
BF16 = jnp.bfloat16

PLAN_FOUR = (
    ({0: "a0", 1: "e0", 2: "c0", 3: "F"}, {0: "a1", 1: "e2", 2: "c0", 3: "F"}),
    ({0: "a1", 1: "e1", 2: "a1", 3: "e2"}, {0: "a0", 1: "a0", 2: "F", 3: "c0"}),
    ({0: "g3", 1: "e2", 2: "c1"}, {0: "e0", 1: "e3", 2: "c1"}),
    ({0: "g1", 1: "e3", 2: "e0", 3: "e3"}, {0: "e1", 1: "e1", 3: "c1"}),
    ({}, {0: "g2", 1: "g3"}),
)
PLAN_ANY = (
    ({0: "a0", 1: "e0", 2: "c0", 3: "f0"}, {0: "a1", 1: "e2", 2: "c0", 3: "f0"}),
    ({0: "a1", 1: "e1", 2: "a1", 3: "e2"}, {0: "a0", 1: "a0", 2: "c1", 3: "f1"}),
    ({0: "g3", 1: "e2", 2: "c1", 3: "f1"}, {0: "e0", 1: "e3", 2: "f0", 3: "f2"}),
    ({0: "g1", 1: "e3", 2: "e0", 3: "e3"}, {0: "e1", 1: "e1", 2: "f1", 3: "f3"}),
    ({0: "c1", 1: "f2", 3: "f2"}, {0: "g2", 1: "g3", 3: "c0"}),
    ({1: "f3", 3: "f3"}, {}),
)
HOMES = {"a": 0, "c": 2, "e": 1, "f": 3, "F": 3, "g": 0}
ATTEND_BLOCKS = ((0, 1), (2, 3))
EXPERT_BLOCKS = ((0, 1), (4, 5), (2, 3), (6, 7))


def dot_plain(left, right):
    return jnp.dot(left, right, preferred_element_type=F32)


def dot_last(left, right):
    return lax.dot_general(left, right, (((1,), (1,)), ((), ())), preferred_element_type=F32)


def dot_first(left, right):
    return lax.dot_general(left, right, (((0,), (0,)), ((), ())), preferred_element_type=F32)


def column_sum(matrix):
    return jnp.sum(matrix.astype(F32), axis=0, keepdims=True)


def norm_parts(rows):
    centre = rows - jnp.mean(rows, axis=-1, keepdims=True)
    scale = lax.rsqrt(jnp.mean(centre * centre, axis=-1, keepdims=True) + 1e-06)
    return centre * scale, scale


def norm_back(normed_grad, unit, scale, gain):
    unit_grad = normed_grad * gain
    along = jnp.mean(unit_grad * unit, axis=-1, keepdims=True)
    return scale * (unit_grad - jnp.mean(unit_grad, axis=-1, keepdims=True) - unit * along)


def true_positions(length, first, count, axis, kind):
    shape = (count, 1) if axis == 0 else (1, count)
    position = first + lax.broadcasted_iota(jnp.int32, shape, axis)
    patch = position < PATCHES
    if kind == "patch":
        return patch
    caption = (position >= PATCHES) & (position - PATCHES < length)
    return caption if kind == "caption" else patch | caption


def head_masks():
    lane = lax.broadcasted_iota(jnp.int32, (1, PAIR), 1)
    even = (lane < HEAD_DIM).astype(F32).astype(BF16)
    odd = (lane >= HEAD_DIM).astype(F32).astype(BF16)
    return lane < HEAD_DIM, even, odd


def split_pair(pair, even, odd):
    return jnp.concatenate([pair * even, pair * odd], axis=0)


def start_weights(info, first, refs, plan, blocks, sems):
    half = blocks.shape[1] // 2
    section, core, plane = info[first], info[first + 1], info[first + 2]
    for at, at_plane, steps in plan:
        here = section == at
        if at_plane is not None:
            here = here & (plane == at_plane)

        @pl.when(here)
        def _(steps=steps):
            for block, source in steps:
                if source[0] == "own":
                    _, which, row, column = source
                    width = blocks.shape[2]
                    for part in range(2):
                        pltpu.make_async_copy(
                            refs[which].at[
                                pl.ds(row + part * half, half), pl.ds(column, width)
                            ],
                            blocks.at[block, pl.ds(part * half, half)],
                            sems.at[block],
                        ).start()
                else:
                    _, mine, theirs, index = source
                    pltpu.make_async_copy(
                        refs[mine].at[index],
                        blocks.at[block, pl.ds(pl.multiple_of(core * half, half), half)],
                        sems.at[block],
                    ).start()
                    pltpu.make_async_copy(
                        refs[theirs].at[index],
                        blocks.at[block, pl.ds(pl.multiple_of((1 - core) * half, half), half)],
                        sems.at[block],
                    ).start()


def wait_block(blocks, block, sems):
    pltpu.make_async_copy(blocks.at[block], blocks.at[block], sems.at[block]).wait()


def store_turned(target, turned, columns, section, core):
    half = target.shape[0] // 2
    for piece in range(16):
        path, owner = (piece >> 2) & 1, piece & 3
        away = owner ^ section
        place = ((away & 1) << 1) | (away >> 1) if path == 0 else away
        row = ((piece >> 3) ^ core) * half + (place >> 1) * (half // 2)
        row = row + path * (half // 4) + (place & 1) * PIECE_ROWS
        target[pl.ds(pl.multiple_of(row, 16), PIECE_ROWS), columns] = turned[
            piece * PIECE_ROWS : (piece + 1) * PIECE_ROWS
        ]


def put_travel(refs, which, columns, left, right):
    half = left.shape[0] // 2
    for side in range(2):
        rows = dot_plain(left[side * half : (side + 1) * half], right).astype(BF16)
        refs[2 * side][which, :, columns] = rows[: half // 2]
        refs[2 * side + 1][which, :, columns] = rows[half // 2 :]


def attend_forward_kernel(plan, weight_count, merge, info, *refs):
    weights, refs = refs[:weight_count], refs[weight_count:]
    if merge:
        x_ref, before_ref, part_ref, outer_ref, gain_ref, shift_ref, bias_ref = refs[:7]
        y_ref, qkv_ref, mixed_ref, joined_ref, blocks, sems, joined = refs[7:]
    else:
        x_ref, gain_ref, shift_ref, bias_ref, next_gain_ref, next_shift_ref = refs[:6]
        y_ref, qkv_ref, mixed_ref, caption_ref, blocks, sems = refs[6:]
    item = pl.program_id(0)
    items = pl.num_programs(0)
    length = info[item]
    width = x_ref.shape[-1]

    @pl.when(item == 0)
    def _():
        start_weights(info, items, weights, plan, blocks, sems)

    cap = slice(CAP_FIRST, CAP_FIRST + CAP_ROWS)
    if merge:
        joined[...] = x_ref[0].astype(F32)
        branch = part_ref[0].astype(F32) + outer_ref[...]
        is_true = true_positions(length, CAP_FIRST, CAP_ROWS, 0, "caption")
        captions = before_ref[0, cap] + jnp.where(is_true, branch, 0.0)
        position = CAP_FIRST + lax.broadcasted_iota(jnp.int32, (CAP_ROWS, 1), 0)
        captions = captions.astype(BF16).astype(F32)
        joined[cap] = jnp.where(position < PATCHES, joined[cap], captions)
        x = joined[...]
        joined_ref[0] = x.astype(BF16)
    else:
        x = x_ref[0].astype(F32)
    unit, _ = norm_parts(x)
    normed = (unit * gain_ref[...] + shift_ref[...]).astype(BF16)

    @pl.when(item == 0)
    def _():
        for block in range(4):
            wait_block(blocks, block, sems)

    queries = dot_plain(normed, blocks[0]) + bias_ref[:, :width]
    qkv_ref[0, :, :width] = (queries * HEAD_DIM ** (-0.5)).astype(BF16)
    qkv_ref[0, :, width : 2 * width] = dot_plain(normed, blocks[1]).astype(BF16)
    values = dot_plain(normed, blocks[2]) + bias_ref[:, width : 2 * width]
    qkv_ref[0, :, 2 * width :] = values.astype(BF16)
    key_true = true_positions(length, 0, ROWS, 1, "all")
    low_half, even, odd = head_masks()
    ones = jnp.ones((ROWS, PAIR), BF16)

    def scores_of(pair):
        at = pair * PAIR
        q2 = qkv_ref[0, :, at : at + PAIR]
        k2 = qkv_ref[0, :, width + at : width + at + PAIR]
        return dot_last(split_pair(q2, even, odd), k2)

    ahead = [scores_of(0), scores_of(1)]
    for pair in range(HEADS // 2):
        at = pair * PAIR
        scores = jnp.where(key_true, ahead.pop(0), -1e9)
        if pair + 2 < HEADS // 2:
            ahead.append(scores_of(pair + 2))
        weight = jnp.exp(scores - jnp.max(scores, axis=-1, keepdims=True)).astype(BF16)
        v2 = qkv_ref[0, :, 2 * width + at : 2 * width + at + PAIR]
        summed = dot_plain(weight, jnp.concatenate([v2, ones], axis=1))
        top = jnp.where(low_half, summed[:ROWS, :PAIR], summed[ROWS:, :PAIR])
        below = jnp.where(low_half, summed[:ROWS, PAIR:], summed[ROWS:, PAIR:])
        mixed_ref[0, :, at : at + PAIR] = (top / below).astype(BF16)
    branch = dot_plain(mixed_ref[0], blocks[3]) + bias_ref[:, 2 * width :]
    row_true = true_positions(length, 0, ROWS, 0, "all")
    y = x + jnp.where(row_true, branch, 0.0)
    y_ref[0] = y.astype(y_ref.dtype)
    if not merge:
        unit, _ = norm_parts(y[cap])
        caption_ref[0] = (unit * next_gain_ref[...] + next_shift_ref[...]).astype(BF16)


def attend_backward_kernel(plan, weight_count, first, info, *refs):
    weights, refs = refs[:weight_count], refs[weight_count:]
    x_ref, gain_ref, shift_ref, qkv_ref, mixed_ref, grad_ref = refs[:6]
    if first:
        after_ref, next_gain_ref, *parts = refs[6:12]
        refs = refs[12:]
    else:
        refs = refs[6:]
    out_ref, gain_grad_ref, shift_grad_ref, bias_grad_ref = refs[:4]
    travel_refs = refs[4:8]
    if first:
        next_gain_grad_ref, next_shift_grad_ref, joined = refs[8], refs[9], refs[-1]
    else:
        caption_ref = refs[8]
    blocks, sems, normed_turned, mixed_turned, branch_all, projected, mixed_grad = refs[
        10 if first else 9 :
    ][:7]
    item = pl.program_id(0)
    items = pl.num_programs(0)
    length = info[item]
    section, core = info[items], info[items + 1]
    width = x_ref.shape[-1]
    here = pl.ds(pl.multiple_of(item * ROWS, ROWS), ROWS)
    cap = slice(CAP_FIRST, CAP_FIRST + CAP_ROWS)

    @pl.when(item == 0)
    def _():
        start_weights(info, items, weights, plan, blocks, sems)

    def add_to(ref, part):
        @pl.when(item == 0)
        def _():
            ref[...] = part

        @pl.when(item > 0)
        def _():
            ref[...] += part

    x = x_ref[0].astype(F32)
    unit, scale = norm_parts(x)
    normed = (unit * gain_ref[...] + shift_ref[...]).astype(BF16)
    incoming = grad_ref[0].astype(F32)
    if first:
        after_unit, after_scale = norm_parts(after_ref[0, cap])
        caption_grad = parts[0][...].astype(F32)
        for part in parts[1:]:
            caption_grad = caption_grad + part[...].astype(F32)
        joined[...] = incoming
        joined[cap] += norm_back(caption_grad, after_unit, after_scale, next_gain_ref[...])
        incoming = joined[...]
        add_to(next_gain_grad_ref, jnp.sum(caption_grad * after_unit, axis=0, keepdims=True))
        add_to(next_shift_grad_ref, jnp.sum(caption_grad, axis=0, keepdims=True))
    row_true = true_positions(length, 0, ROWS, 0, "all")
    branch = jnp.where(row_true, incoming, 0.0).astype(BF16)
    branch_all[here, :] = branch
    store_turned(normed_turned, normed.T, here, section, core)
    store_turned(mixed_turned, mixed_ref[0].T, here, section, core)

    @pl.when(item == 0)
    def _():
        for block in range(4):
            wait_block(blocks, block, sems)

    mixed_grad[...] = dot_last(branch, blocks[3]).astype(BF16)
    key_true = true_positions(length, 0, ROWS, 0, "all")
    _, even, odd = head_masks()

    def products_of(pair):
        at = pair * PAIR
        q2 = split_pair(qkv_ref[0, :, at : at + PAIR], even, odd)
        k2 = qkv_ref[0, :, width + at : width + at + PAIR]
        v2 = qkv_ref[0, :, 2 * width + at : 2 * width + at + PAIR]
        g2 = split_pair(mixed_grad[:, at : at + PAIR], even, odd)
        return q2, k2, g2, dot_last(k2, q2), dot_last(v2, g2)

    ahead = [products_of(0)]
    for pair in range(HEADS // 2):
        at = pair * PAIR
        q2, k2, g2, scores, weight_grad = ahead.pop(0)
        if pair + 1 < HEADS // 2:
            ahead.append(products_of(pair + 1))
        scores = jnp.where(key_true, scores, -1e9)
        weight = jnp.exp(scores - jnp.max(scores, axis=0, keepdims=True))
        weight = weight * (1.0 / jnp.sum(weight, axis=0, keepdims=True))
        product = weight * weight_grad
        along = jnp.sum(product, axis=0, keepdims=True)
        score_grad = (product - weight * along).astype(BF16)
        values_grad = dot_plain(weight.astype(BF16), g2).astype(BF16)
        keys_grad = dot_plain(score_grad, q2).astype(BF16)
        k2_split = split_pair(k2, even, odd)
        stacked = jnp.concatenate([score_grad[:, :ROWS], score_grad[:, ROWS:]], axis=0)
        queries_grad = dot_first(stacked, k2_split).astype(BF16)
        queries_grad = (queries_grad.astype(F32) * HEAD_DIM ** (-0.5)).astype(BF16)
        projected[here, at : at + PAIR] = queries_grad
        projected[here, width + at : width + at + PAIR] = keys_grad
        projected[here, 2 * width + at : 2 * width + at + PAIR] = values_grad
    normed_grad = dot_last(projected[here, :width], blocks[0])
    normed_grad += dot_last(projected[here, width : 2 * width], blocks[1])
    normed_grad += dot_last(projected[here, 2 * width :], blocks[2])
    out = (incoming + norm_back(normed_grad, unit, scale, gain_ref[...])).astype(BF16)
    out_ref[0] = out
    if not first:
        is_true = true_positions(length, CAP_FIRST, CAP_ROWS, 0, "caption")
        caption_ref[0] = jnp.where(is_true, out[cap].astype(F32), 0.0).astype(BF16)
    add_to(gain_grad_ref, jnp.sum(normed_grad * unit, axis=0, keepdims=True))
    add_to(shift_grad_ref, jnp.sum(normed_grad, axis=0, keepdims=True))

    @pl.when(item == items - 1)
    def _():
        for block in range(4):
            columns = slice(block * width, (block + 1) * width)
            left = normed_turned if block < 3 else mixed_turned
            right = projected[:, columns] if block < 3 else branch_all[...]
            put_travel(travel_refs, 0, columns, left, right)
        bias_grad_ref[:, :width] = column_sum(projected[:, :width])
        bias_grad_ref[:, width : 2 * width] = column_sum(projected[:, 2 * width :])
        bias_grad_ref[:, 2 * width :] = column_sum(branch_all[...])


SHORT = pl.CostEstimate(flops=0, bytes_accessed=100_000, transcendentals=0)
LONG = pl.CostEstimate(flops=30_000_000_000, bytes_accessed=30_000_000, transcendentals=0)
ANYWHERE = pl.BlockSpec(memory_space=pl.ANY)


def whole_block(shape):
    return pl.BlockSpec(shape, lambda step, info: (0,) * len(shape))


def item_block(shape):
    return pl.BlockSpec((1,) + shape[1:], lambda step, info: (step,) + (0,) * (len(shape) - 1))


def blocks_scratch(count, width):
    return [pltpu.VMEM((count, width, width), BF16), pltpu.SemaphoreType.DMA((count,))]


def attend_forward(x, info, weights, gain, shift, bias, merge=None, following=None):
    arrays, plan = weights
    items, _, width = x.shape
    row = whole_block((1, width))
    bias_row = whole_block((1, 3 * width))
    caption_shape = (items, CAP_ROWS, width)
    if merge is not None:
        before, part, outer = merge
        operands = (x, before, part, outer, gain, shift, bias)
        specs = [item_block(x.shape), item_block(x.shape), item_block(caption_shape)]
        specs += [row, row, row, bias_row]
        last_shape, kind, scratch = x.shape, BF16, [pltpu.VMEM((ROWS, width), F32)]
    else:
        operands = (x, gain, shift, bias, *following)
        specs = [item_block(x.shape), row, row, bias_row, row, row]
        last_shape, kind, scratch = caption_shape, F32, []
    return pl.pallas_call(
        partial(attend_forward_kernel, plan, len(arrays), merge is not None),
        grid_spec=pltpu.PrefetchScalarGridSpec(
            num_scalar_prefetch=1,
            grid=(items,),
            in_specs=[ANYWHERE] * len(arrays) + specs,
            out_specs=[
                item_block(x.shape),
                item_block((items, ROWS, 3 * width)),
                item_block((items, ROWS, width)),
                item_block(last_shape),
            ],
            scratch_shapes=blocks_scratch(4, width) + scratch,
        ),
        out_shape=[
            jax.ShapeDtypeStruct(x.shape, kind),
            jax.ShapeDtypeStruct((items, ROWS, 3 * width), BF16),
            jax.ShapeDtypeStruct((items, ROWS, width), BF16),
            jax.ShapeDtypeStruct(last_shape, BF16),
        ],
        compiler_params=pltpu.CompilerParams(vmem_limit_bytes=VMEM_BYTES),
        cost_estimate=SHORT,
        name="attend_forward",
    )(info, *arrays, *operands)


def attend_backward(x, info, weights, gain, shift, qkv, mixed, incoming, first=None):
    arrays, plan = weights
    items, _, width = x.shape
    half = width // 2
    row = whole_block((1, width))
    caption_shape = (items, CAP_ROWS, width)
    operands = (x, gain, shift, qkv, mixed, incoming)
    specs = [item_block(x.shape), row, row, item_block(qkv.shape), item_block(mixed.shape)]
    specs += [item_block(incoming.shape)]
    outs = [
        (item_block(x.shape), x.shape, BF16),
        (row, (1, width), F32),
        (row, (1, width), F32),
        (whole_block((1, 3 * width)), (1, 3 * width), F32),
    ]
    outs += [(whole_block((1, half // 2, 4 * width)), (1, half // 2, 4 * width), BF16)] * 4
    scratch = []
    if first is not None:
        after, next_gain, parts = first
        operands += (after, next_gain, *parts)
        caption_rows = pl.BlockSpec((CAP_ROWS, width), lambda step, info: (step, 0))
        specs += [item_block(after.shape), row] + [caption_rows] * 4
        outs += [(row, (1, width), F32)] * 2
        scratch = [pltpu.VMEM((ROWS, width), F32)]
    else:
        outs += [(item_block(caption_shape), caption_shape, BF16)]
    return pl.pallas_call(
        partial(attend_backward_kernel, plan, len(arrays), first is not None),
        grid_spec=pltpu.PrefetchScalarGridSpec(
            num_scalar_prefetch=1,
            grid=(items,),
            in_specs=[ANYWHERE] * len(arrays) + specs,
            out_specs=[spec for spec, _, _ in outs],
            scratch_shapes=blocks_scratch(4, width)
            + [
                pltpu.VMEM((width, items * ROWS), BF16),
                pltpu.VMEM((width, items * ROWS), BF16),
                pltpu.VMEM((items * ROWS, width), BF16),
                pltpu.VMEM((items * ROWS, 3 * width), BF16),
                pltpu.VMEM((ROWS, width), BF16),
            ]
            + scratch,
        ),
        out_shape=[jax.ShapeDtypeStruct(shape, kind) for _, shape, kind in outs],
        compiler_params=pltpu.CompilerParams(vmem_limit_bytes=VMEM_BYTES),
        cost_estimate=LONG,
        name="attend_backward",
    )(info, *arrays, *operands)


def normal_parts(u):
    t = pl.reciprocal(1.0 + 0.23164190 * jnp.abs(u), approx=True)
    bell = jnp.exp2((u * -0.7213475204444817) * u)
    poly = t * (
        0.127414796
        + t * (-0.142248368 + t * (0.7107068705 + t * (-0.7265760135 + t * 0.5307027145)))
    )
    tail = poly * bell
    return jnp.where(u < 0, tail, 1.0 - tail), bell


def inner_forward(normed, matrix, bias):
    inner = dot_plain(normed, matrix) + bias
    cumulative, bell = normal_parts(inner)
    slope = cumulative + (inner * 0.3989422804014327) * bell
    return (inner * cumulative).astype(BF16), slope.astype(BF16)


def expert_forward_kernel(plan, weight_count, count, kind, info, *refs):
    weights, refs = refs[:weight_count], refs[weight_count:]
    x_ref, gain_ref, shift_ref, inner_ref, outer_ref = refs[:5]
    y_ref, act_ref, slope_ref, blocks, sems, normed, total = refs[5:]
    step = pl.program_id(0)
    items, _, width = x_ref.shape

    @pl.when(step == 0)
    def _():
        start_weights(info, items, weights, plan, blocks, sems)
        for item in range(items):
            x = x_ref[item, :count].astype(BF16).astype(F32)
            unit, _ = norm_parts(x)
            normed[item * count : (item + 1) * count] = (
                unit * gain_ref[...] + shift_ref[...]
            ).astype(BF16)

    wait_block(blocks, step, sems)
    wait_block(blocks, step + 4, sems)
    for at in range(0, width, 256):
        columns = slice(at, at + 256)
        act, slope = inner_forward(normed[...], blocks[step, :, columns], inner_ref[:, columns])
        act_ref[:, columns] = act
        slope_ref[:, columns] = slope
    part = dot_plain(act_ref[...], blocks[step + 4])

    @pl.when(step == 0)
    def _():
        total[...] = part

    @pl.when(step > 0)
    def _():
        total[...] += part

    @pl.when(step == pl.num_programs(0) - 1)
    def _():
        for item in range(items):
            row_true = true_positions(info[item], 0, count, 0, kind)
            branch = total[item * count : (item + 1) * count] + outer_ref[...]
            x = x_ref[item, :count].astype(BF16).astype(F32)
            y_ref[item, :count] = (x + jnp.where(row_true, branch, 0.0)).astype(BF16)
            if count < ROWS:
                y_ref[item, count:] = jnp.zeros((ROWS - count, width), BF16)


def expert_backward_kernel(plan, weight_count, count, kind, info, *refs):
    weights, refs = refs[:weight_count], refs[weight_count:]
    x_ref, gain_ref, shift_ref, act_ref, slope_ref, grad_ref = refs[:6]
    out_ref, gain_grad_ref, shift_grad_ref, inner_grad_ref, outer_grad_ref = refs[6:11]
    travel_refs = refs[11:15]
    blocks, sems, normed_turned, branch_turned, branch, inner_all, total = refs[15:]
    step = pl.program_id(0)
    items, _, width = x_ref.shape
    section, core = info[items], info[items + 1]

    @pl.when(step == 0)
    def _():
        start_weights(info, items, weights, plan, blocks, sems)
        outer = None
        for item in range(items):
            here = slice(item * count, (item + 1) * count)
            unit, _ = norm_parts(x_ref[item, :count].astype(BF16).astype(F32))
            normed = (unit * gain_ref[...] + shift_ref[...]).astype(BF16)
            row_true = true_positions(info[item], 0, count, 0, kind)
            incoming = grad_ref[item, :count].astype(F32)
            masked = jnp.where(row_true, incoming, 0.0).astype(BF16)
            branch[here] = masked
            store_turned(normed_turned, normed.T, here, section, core)
            store_turned(branch_turned, masked.T, here, section, core)
            term = column_sum(masked)
            outer = term if outer is None else outer + term
        outer_grad_ref[...] = outer

    wait_block(blocks, step, sems)
    wait_block(blocks, step + 4, sems)
    for at in range(0, width, 256):
        columns = slice(at, at + 256)
        act_grad = dot_last(branch[...], blocks[step + 4, columns])
        inner = (slope_ref[:, columns].astype(F32) * act_grad).astype(BF16)
        inner_all[:, columns] = inner
        inner_grad_ref[:, columns] = column_sum(inner)
        put_travel(travel_refs, 0, columns, normed_turned, inner)
        put_travel(travel_refs, 1, columns, branch_turned, act_ref[:, columns])
    part = dot_last(inner_all[...], blocks[step])

    @pl.when(step == 0)
    def _():
        total[...] = part

    @pl.when(step > 0)
    def _():
        total[...] += part

    @pl.when(step == pl.num_programs(0) - 1)
    def _():
        gain_sum, shift_sum = None, None
        for item in range(items):
            unit, scale = norm_parts(x_ref[item, :count].astype(BF16).astype(F32))
            normed_grad = total[item * count : (item + 1) * count]
            gain_part = jnp.sum(normed_grad * unit, axis=0, keepdims=True)
            shift_part = jnp.sum(normed_grad, axis=0, keepdims=True)
            gain_sum = gain_part if gain_sum is None else gain_sum + gain_part
            shift_sum = shift_part if shift_sum is None else shift_sum + shift_part
            incoming = grad_ref[item, :count].astype(F32)
            hidden = incoming + norm_back(normed_grad, unit, scale, gain_ref[...])
            out_ref[item, :count] = hidden.astype(BF16)
            if count < ROWS:
                out_ref[item, count:] = grad_ref[item, count:]
        gain_grad_ref[...] = gain_sum
        shift_grad_ref[...] = shift_sum


def shared_forward_kernel(*refs):
    *rows_refs, inputs_ref, inner_ref, outputs_ref = refs[:7]
    *part_refs, normed, total = refs[7:]
    count = rows_refs[0].shape[0]
    step = pl.program_id(0)

    @pl.when(step == 0)
    def _():
        for index, ref in enumerate(rows_refs):
            normed[index * count : (index + 1) * count] = ref[...]
        total[...] = jnp.zeros_like(total)

    act, _ = inner_forward(normed[...], inputs_ref[...], inner_ref[...])
    total[...] += dot_plain(act, outputs_ref[...])

    @pl.when(step == pl.num_programs(0) - 1)
    def _():
        for index, ref in enumerate(part_refs):
            ref[...] = total[index * count : (index + 1) * count].astype(BF16)


def shared_backward_kernel(plan, weight_count, info, *refs):
    weights, refs = refs[:weight_count], refs[weight_count:]
    rows_refs, grad_refs, inner_ref = refs[:4], refs[4:8], refs[8]
    part_refs, (keep_ref, send_ref, inner_grad_ref, outer_grad_ref) = refs[9:13], refs[13:17]
    blocks, sems, normed, branch, matrix = refs[17:]
    count, width = rows_refs[0].shape
    half = width // 2
    first = info.shape[0] - 3
    core = info[first + 1]
    start_weights(info, first, weights, plan, blocks, sems)
    for index in range(SECTIONS):
        here = slice(index * count, (index + 1) * count)
        normed[here] = rows_refs[index][...]
        branch[here] = grad_refs[index][...]
    outer_grad_ref[...] = column_sum(grad_refs[0][...])
    wait_block(blocks, 0, sems)
    wait_block(blocks, 1, sems)
    part = None
    for at in range(0, width, 256):
        columns = slice(at, at + 256)
        act, slope = inner_forward(normed[...], blocks[0, :, columns], inner_ref[:, columns])
        act_grad = dot_last(branch[...], blocks[1, columns])
        inner = (slope.astype(F32) * act_grad).astype(BF16)
        inner_grad_ref[:, columns] = column_sum(inner)
        matrix[0, :, columns] = dot_first(normed[...], inner).astype(BF16)
        matrix[1, :, columns] = dot_first(branch[...], act).astype(BF16)
        term = dot_last(inner, blocks[0, :, columns])
        part = term if part is None else part + term
    for index, ref in enumerate(part_refs):
        ref[...] = part[index * count : (index + 1) * count].astype(BF16)
    quarter = half // 4
    for which in range(2):
        for group in range(4):
            columns = slice(group * width, (group + 1) * width)
            mine = pl.multiple_of(core * half, 16) + group * quarter
            other = pl.multiple_of((1 - core) * half, 16) + group * quarter
            keep_ref[which, :, columns] = matrix[which, pl.ds(pl.multiple_of(mine, 16), quarter)]
            send_ref[which, :, columns] = matrix[which, pl.ds(pl.multiple_of(other, 16), quarter)]


def chunk_columns(rows, width):
    return pl.BlockSpec((rows, width), lambda step, info: (0, step))


def expert_forward(x, info, weights, gain, shift, inner, outer, count, kind):
    arrays, plan = weights
    items, _, width = x.shape
    hidden = inner.shape[1]
    row = whole_block((1, width))
    return pl.pallas_call(
        partial(expert_forward_kernel, plan, len(arrays), count, kind),
        grid_spec=pltpu.PrefetchScalarGridSpec(
            num_scalar_prefetch=1,
            grid=(hidden // width,),
            in_specs=[ANYWHERE] * len(arrays)
            + [whole_block(x.shape), row, row, chunk_columns(1, width), row],
            out_specs=[
                whole_block((items, ROWS, width)),
                chunk_columns(items * count, width),
                chunk_columns(items * count, width),
            ],
            scratch_shapes=blocks_scratch(8, width)
            + [
                pltpu.VMEM((items * count, width), BF16),
                pltpu.VMEM((items * count, width), F32),
            ],
        ),
        out_shape=[
            jax.ShapeDtypeStruct((items, ROWS, width), BF16),
            jax.ShapeDtypeStruct((items * count, hidden), BF16),
            jax.ShapeDtypeStruct((items * count, hidden), BF16),
        ],
        compiler_params=pltpu.CompilerParams(vmem_limit_bytes=VMEM_BYTES),
        cost_estimate=SHORT,
        name="expert_forward_" + kind,
    )(info, *arrays, x, gain, shift, inner, outer)


def expert_backward(x, info, weights, gain, shift, act, slope, incoming, count, kind):
    arrays, plan = weights
    items, _, width = x.shape
    half = width // 2
    hidden = act.shape[1]
    row = whole_block((1, width))
    travel = pl.BlockSpec((2, half // 2, width), lambda step, info: (0, 0, step))
    return pl.pallas_call(
        partial(expert_backward_kernel, plan, len(arrays), count, kind),
        grid_spec=pltpu.PrefetchScalarGridSpec(
            num_scalar_prefetch=1,
            grid=(hidden // width,),
            in_specs=[ANYWHERE] * len(arrays)
            + [
                whole_block(x.shape),
                row,
                row,
                chunk_columns(items * count, width),
                chunk_columns(items * count, width),
                whole_block(incoming.shape),
            ],
            out_specs=[whole_block(incoming.shape), row, row, chunk_columns(1, width), row]
            + [travel] * 4,
            scratch_shapes=blocks_scratch(8, width)
            + [
                pltpu.VMEM((width, items * count), BF16),
                pltpu.VMEM((width, items * count), BF16),
                pltpu.VMEM((items * count, width), BF16),
                pltpu.VMEM((items * count, width), BF16),
                pltpu.VMEM((items * count, width), F32),
            ],
        ),
        out_shape=[
            jax.ShapeDtypeStruct(incoming.shape, BF16),
            jax.ShapeDtypeStruct((1, width), F32),
            jax.ShapeDtypeStruct((1, width), F32),
            jax.ShapeDtypeStruct((1, hidden), F32),
            jax.ShapeDtypeStruct((1, width), F32),
        ]
        + [jax.ShapeDtypeStruct((2, half // 2, hidden), BF16)] * 4,
        compiler_params=pltpu.CompilerParams(vmem_limit_bytes=VMEM_BYTES),
        cost_estimate=SHORT,
        name="expert_backward_" + kind,
    )(info, *arrays, x, gain, shift, act, slope, incoming)


IN_VMEM = pl.BlockSpec(memory_space=pltpu.VMEM)
IN_SMEM = pl.BlockSpec(memory_space=pltpu.SMEM)


def shared_forward(rows, inputs, inner, outputs):
    count, width = rows[0].shape
    total = SECTIONS * count
    hidden = inner.shape[1]
    return pl.pallas_call(
        shared_forward_kernel,
        grid=(hidden // width,),
        in_specs=[pl.BlockSpec(rows[0].shape, lambda step: (0, 0))] * 4
        + [
            pl.BlockSpec((width, width), lambda step: (0, step)),
            pl.BlockSpec((1, width), lambda step: (0, step)),
            pl.BlockSpec((width, width), lambda step: (step, 0)),
        ],
        out_specs=[pl.BlockSpec((count, width), lambda step: (0, 0))] * SECTIONS,
        scratch_shapes=[pltpu.VMEM((total, width), BF16), pltpu.VMEM((total, width), F32)],
        out_shape=[jax.ShapeDtypeStruct((count, width), BF16)] * SECTIONS,
        compiler_params=pltpu.CompilerParams(vmem_limit_bytes=VMEM_BYTES),
        cost_estimate=SHORT,
        name="shared_forward",
    )(*rows, inputs, inner, outputs)


def shared_backward(rows, grads, info, weights, inner):
    arrays, plan = weights
    count, width = rows[0].shape
    total = SECTIONS * count
    travel = (2, width // 8, 4 * width)
    return pl.pallas_call(
        partial(shared_backward_kernel, plan, len(arrays)),
        in_specs=[IN_SMEM] + [ANYWHERE] * len(arrays) + [IN_VMEM] * 9,
        out_specs=[IN_VMEM] * 8,
        scratch_shapes=blocks_scratch(2, width)
        + [
            pltpu.VMEM((total, width), BF16),
            pltpu.VMEM((total, width), BF16),
            pltpu.VMEM((2, width, width), BF16),
        ],
        out_shape=[
            *[jax.ShapeDtypeStruct((count, width), BF16)] * SECTIONS,
            jax.ShapeDtypeStruct(travel, BF16),
            jax.ShapeDtypeStruct(travel, BF16),
            jax.ShapeDtypeStruct((1, width), F32),
            jax.ShapeDtypeStruct((1, width), F32),
        ],
        compiler_params=pltpu.CompilerParams(vmem_limit_bytes=VMEM_BYTES),
        cost_estimate=SHORT,
        name="shared_backward",
    )(info, *arrays, *rows, *grads, inner)


def plane_turn(plane, planes):
    return ((plane & 1) << 1) | (plane >> 1) if planes == 4 else 0


def finish_kernel(planes, info, scale_ref, *refs):
    step = pl.program_id(0)
    mine, theirs, outs, placed = refs[:4], refs[4:8], refs[8:-1], refs[-1]
    count = mine[0].shape[0]
    width = placed.shape[1]
    half = width // 2
    at = info.shape[0] - 3
    section, core = info[at], info[at + 1]
    turn = plane_turn(info[at + 2], planes)
    turned = turn if count == 1 else jnp.where(section == 1, turn, 0)
    scale = scale_ref[0, 0]
    columns = pl.ds(pl.multiple_of((step ^ turned) * width, width), width)

    def place(which):
        def by_rows():
            for side, pieces in enumerate((mine, theirs)):
                for away, ref in enumerate(pieces):
                    for path in range(2):
                        row = (core ^ side) * half + path * (half // 2)
                        row = row + (section ^ away) * PIECE_ROWS
                        placed[pl.ds(pl.multiple_of(row, 16), PIECE_ROWS), :] = ref[
                            which, path * PIECE_ROWS : (path + 1) * PIECE_ROWS, columns
                        ].astype(F32)

        def by_columns():
            for side, pieces in enumerate((mine, theirs)):
                for away, ref in enumerate(pieces):

                    @pl.when(step == away)
                    def _(side=side, ref=ref):
                        for group in range(4):
                            quarter = half // 4
                            row = (core ^ side) * half + group * quarter
                            column = pl.multiple_of((group ^ turn) * width, width)
                            placed[pl.ds(pl.multiple_of(row, 16), quarter), :] = ref[
                                which, :, pl.ds(column, width)
                            ].astype(F32)

        if count == 1:
            by_rows()
        else:
            pl.when(section != 0)(by_rows)
            pl.when(section == 0)(by_columns)

    place(0)
    if count == 1:

        @pl.when(step < 3)
        def _():
            outs[0][0] = placed[...] / scale

        @pl.when(step == 3)
        def _():
            outs[1][0] = placed[...] / scale

    else:
        outs[0][0] = placed[...] / scale
        place(1)
        outs[1][0] = (placed[...] / scale).T


def finish(info, scale, mine, theirs, planes):
    count, _, hidden = mine[0].shape
    width = hidden // 4
    if count == 1:
        shapes = [(1, width, 3 * width), (1, width, width)]
        maps = [lambda step, info: (0, 0, jnp.minimum(step, 2)), lambda step, info: (0, 0, 0)]
    else:
        shapes = [(1, width, hidden), (1, hidden, width)]
        maps = [lambda step, info: (0, 0, step), lambda step, info: (0, step, 0)]
    return pl.pallas_call(
        partial(finish_kernel, planes),
        grid_spec=pltpu.PrefetchScalarGridSpec(
            num_scalar_prefetch=1,
            grid=(4,),
            in_specs=[IN_SMEM] + [whole_block(mine[0].shape)] * 8,
            out_specs=[pl.BlockSpec((1, width, width), at) for at in maps],
            scratch_shapes=[pltpu.VMEM((width, width), F32)],
        ),
        out_shape=[jax.ShapeDtypeStruct(shape, F32) for shape in shapes],
        compiler_params=pltpu.CompilerParams(vmem_limit_bytes=VMEM_BYTES),
        cost_estimate=SHORT,
        name="finish",
    )(info, scale, *mine, *theirs)


def pack_kernel(count, plan, info, *refs):
    sources, outs, sems = refs[:count], refs[count:-1], refs[-1]
    first = info.shape[0] - 3
    section, core, plane = info[first], info[first + 1], info[first + 2]
    half = outs[0].shape[1]
    for index, (out, choices) in enumerate(zip(outs, plan)):
        for at, at_plane, parts in choices:
            here = section == at
            if at_plane is not None:
                here = here & (plane == at_plane)

            @pl.when(here)
            def _(index=index, out=out, parts=parts):
                for block, part in enumerate(parts):
                    if part[0] == "own":
                        _, which, row, column = part
                        rows = pl.ds(pl.multiple_of(row + core * half, half), half)
                        source = sources[which].at[rows, pl.ds(column, out.shape[2])]
                    else:
                        source = sources[part[1]].at[block]
                    pltpu.make_async_copy(source, out.at[block], sems.at[index, block]).start()

    for index, out in enumerate(outs):
        for block in range(2):
            pltpu.make_async_copy(out.at[block], out.at[block], sems.at[index, block]).wait()


def pack(info, sources, plan, shape):
    return pl.pallas_call(
        partial(pack_kernel, len(sources), plan),
        in_specs=[IN_SMEM] + [ANYWHERE] * len(sources),
        out_specs=[IN_VMEM] * len(plan),
        scratch_shapes=[pltpu.SemaphoreType.DMA((len(plan), 2))],
        out_shape=[jax.ShapeDtypeStruct(shape, BF16)] * len(plan),
        cost_estimate=SHORT,
        name="pack",
    )(info, *sources)


def over_section(value, bits, sources=range(SECTIONS)):
    return lax.ppermute(value, "section", [(at, at ^ bits) for at in sources])


def over_core(value):
    return lax.ppermute(value, "core", [(0, 1), (1, 0)])


def over_plane(value, pairs):
    return lax.ppermute(value, "z", pairs)


def added(left, right):
    return (left.astype(F32) + right.astype(F32)).astype(BF16)


def after(value, *earlier):
    return lax.optimization_barrier((value,) + earlier)[0]


def under(outputs, *arrivals):
    joined = lax.optimization_barrier(tuple(outputs) + arrivals)
    return list(joined[: len(outputs)]), list(joined[len(outputs) :])


def by_section(section, values):
    result, last = None, None
    for at in sorted(values):
        if result is None:
            result = values[at]
        elif values[at] is not last:
            result = jnp.where(section >= at, values[at], result)
        last = values[at]
    return result


def total(*values):
    result = values[0].astype(F32)
    for value in values[1:]:
        result = result + value.astype(F32)
    return result.astype(BF16)


class Sums:
    def __init__(self, travel):
        self.stay, self.move, self.other_stay, self.other_move = travel
        self.size = self.stay.shape[1] // 2

    def cross(self, *earlier):
        if earlier:
            self.other_move = after(self.other_move, *earlier)
            self.other_stay = after(self.other_stay, *earlier)
        self.got_move, self.got_stay = over_core(self.other_move), over_core(self.other_stay)

    def first_sends(self):
        size = self.size
        self.sent = [
            total(self.move[:, at : at + size], self.got_move[:, at : at + size])
            for at in (0, size)
        ]
        return self.sent

    def second_sends(self, from_x, from_y):
        size, half = self.size, self.size // 2
        self.first = from_x, from_y
        to_y = total(self.stay[:, half:size], self.got_stay[:, half:size], from_x[:, half:])
        to_x = total(
            self.stay[:, size + half :], self.got_stay[:, size + half :], from_y[:, half:]
        )
        self.sent = [to_x, to_y]
        return self.sent

    def whole(self, from_x, from_y):
        size, half = self.size, self.size // 2
        parts = []
        for at, first, second in ((0, self.first[0], from_y), (size, self.first[1], from_x)):
            here = slice(at, at + half)
            parts.append(total(self.stay[:, here], self.got_stay[:, here], first[:, :half], second))
        return jnp.concatenate(parts, axis=1)


def over_links(sends):
    return [over_section(sends[0], 1), over_section(sends[1], 2)]


class Planes:
    def __init__(self, value, plane, planes):
        self.value, self.plane, self.planes, self.turn = value, plane, planes, 0

    def sends(self, *earlier):
        value = after(self.value, *earlier) if earlier else self.value
        if self.planes != 4:
            return (value,)
        bits = (1, 2, 2, 1)[self.turn]
        if self.turn < 2:
            bit = (self.plane & 1, self.plane >> 1)[self.turn]
            size = value.shape[-1] // 2
            value = lax.dynamic_slice_in_dim(value, (1 - bit) * size, size, value.ndim - 1)
        return (over_plane(value, [(at, at ^ bits) for at in range(4)]),)

    def take(self, arrived):
        if self.planes != 4:
            self.value = lax.psum(arrived, "z") if self.turn == 3 else arrived
        elif self.turn < 2:
            bit = (self.plane & 1, self.plane >> 1)[self.turn]
            size = self.value.shape[-1] // 2
            keep = lax.dynamic_slice_in_dim(self.value, bit * size, size, self.value.ndim - 1)
            self.value = added(keep, arrived)
        else:
            self.value = jnp.concatenate([self.value, arrived], axis=-1)
        self.turn += 1

    def in_order(self, value):
        if self.planes != 4:
            return value
        size, turn = value.shape[-1] // 4, plane_turn(self.plane, 4)
        parts = [
            lax.dynamic_slice_in_dim(value, (at ^ turn) * size, size, value.ndim - 1)
            for at in range(4)
        ]
        return jnp.concatenate(parts, axis=-1)


class Weights:
    def __init__(self, own, info, planes):
        self.own, self.info = own, info
        self.four = planes == 4
        self.plan = PLAN_FOUR if self.four else PLAN_ANY
        self.half, self.width = own[1].shape[0] // 2, own[1].shape[1]
        self.mine, self.theirs, self.arrived = {}, {}, {}

    def place(self, layer, block):
        if layer in "ac":
            return (0, 0, block * self.width) if block < 3 else (1, 0, 0)
        if layer == "g":
            return (2, 0, block * self.width) if block < 4 else (3, (block - 4) * self.width, 0)
        return (2, 0, block * self.width) if block < 4 else (3, (block - 4) * self.width, 0)

    def choices(self, sends, sources):
        result = []
        for at in range(SECTIONS):
            name = sends.get(at)
            if name is not None and HOMES[name[0]] != at:
                key = self.arrived[at, name]
                if key not in sources:
                    sources[key] = len(self.own) + len(sources)
                result.append((at, None, [("arrived", sources[key])] * 2))
                continue
            for plane in range(4) if name == "F" else (None,):
                piece = ("f" + str(plane)) if name == "F" else name or "a0"
                layer, index = piece[0], int(piece[1])
                if layer in "ac":
                    blocks = ATTEND_BLOCKS[index]
                else:
                    blocks = (index, 4 + index) if layer == "g" else EXPERT_BLOCKS[index]
                parts = [("own",) + self.place(layer, block) for block in blocks]
                result.append((at, plane, parts))
        return result

    def packed(self, wanted):
        sources = {}
        plan = [self.choices(sends, sources) for sends in wanted]
        arrays = list(self.own) + [self.mine[key] for key in sources]
        return pack(self.info, arrays, plan, (2, self.half, self.width))

    def sends(self, step):
        if step == "F":
            return [{at: "F" for at in range(SECTIONS)}]
        return [sends for sends in self.plan[step] if sends]

    def payloads(self, *steps):
        wanted = [sends for step in steps for sends in self.sends(step)]
        return list(self.packed(wanted))

    def move(self, step, payloads):
        links = [(link, sends) for link, sends in enumerate(self.plan[step]) if sends]
        for (link, sends), payload in zip(links, payloads):
            self.mine[step, link] = over_section(payload, link + 1, sorted(sends))
            for at, name in sends.items():
                self.arrived[at ^ (link + 1), name] = (step, link)
        return [(step, link) for link, _ in links]

    def move_planes(self, step):
        up, down = self.mine["plane", step - 1], self.mine["plane", 1 - step]
        up = over_plane(up, [(at, at + 1) for at in range(step - 1, 3)])
        down = over_plane(down, [(at, at - 1) for at in range(4 - step, 0, -1)])
        self.mine["plane", step], self.mine["plane", -step] = up, down
        return [("plane", step), ("plane", -step)]

    def cross(self, keys):
        for key in keys:
            self.theirs[key] = over_core(self.mine[key])
        return keys

    def join(self, outputs, mine=(), theirs=()):
        values = [self.mine[key] for key in mine] + [self.theirs[key] for key in theirs]
        outputs, values = under(outputs, *values)
        for key, value in zip(mine, values):
            self.mine[key] = value
        for key, value in zip(theirs, values[len(mine) :]):
            self.theirs[key] = value
        return outputs

    def layer(self, layer):
        arrays, places = list(self.own), {}

        def place(key):
            if key not in places:
                places[key] = len(arrays)
                arrays.extend([self.mine[key], self.theirs[key]])
            return places[key], places[key] + 1

        if layer in "ac":
            names = [(layer + str(index), ATTEND_BLOCKS[index]) for index in range(2)]
        else:
            names = [(layer + str(index), EXPERT_BLOCKS[index]) for index in range(4)]
        plan = []
        for at in range(SECTIONS):
            if layer == "g":
                names = [("g" + str(at), (0, 1))]
            if HOMES[layer] == at:
                steps = []
                for name, blocks in names:
                    for block in blocks:
                        source = block * 4 if layer == "g" else block
                        steps.append((block, ("own",) + self.place(layer, source)))
                plan.append((at, None, steps))
                continue
            by_plane = layer == "f" and self.four
            for plane in range(4) if by_plane else (None,):
                steps = []
                for index, (name, blocks) in enumerate(names):
                    key = ("plane", plane - index) if by_plane else self.arrived[at, name]
                    for which, block in enumerate(blocks):
                        steps.append((block, ("piece",) + place(key) + (which,)))
                plan.append((at, plane, steps))
        return arrays, plan


def per_device(
    tokens,
    caption_lengths,
    attend_gain,
    attend_shift,
    attend_inputs,
    attend_bias,
    attend_output,
    expert_gain,
    expert_shift,
    expert_inputs,
    expert_inner_bias,
    expert_outputs,
    expert_outer_bias,
    cotangent,
):
    section, core, plane = lax.axis_index("section"), lax.axis_index("core"), lax.axis_index("z")
    planes = lax.axis_size("z")
    items, positions, width = tokens.shape
    hidden = expert_inputs.shape[-1]
    info = [value.reshape(1).astype(jnp.int32) for value in (section, core, plane)]
    info = jnp.concatenate([caption_lengths] + info)
    weights = Weights(
        (attend_inputs[0], attend_output[0], expert_inputs[0], expert_outputs[0]), info, planes
    )

    def to_sections(value):
        return [value] + [over_section(value, bits) for bits in (1, 2, 3)]

    def items_of(part):
        return part.reshape(items, CAP_ROWS, width)

    keys = weights.move(0, weights.payloads(0))
    pad = ((0, 0), (0, ROWS - positions), (0, 0))
    x0 = jnp.pad(tokens, pad)
    last_grad = jnp.pad(cotangent, pad)
    rows = jnp.concatenate(
        [
            attend_gain,
            attend_shift,
            attend_bias,
            expert_gain,
            expert_shift,
            expert_inner_bias,
            expert_outer_bias,
            jnp.full((1, 128), jnp.sum(caption_lengths), F32),
        ],
        axis=1,
    )
    rows = to_sections(rows)
    x0, last_grad, *rows = weights.join([x0, last_grad, *rows], keys)
    keys1 = weights.move(1, weights.payloads(1))
    rows = jnp.concatenate(rows, axis=0)
    language_count = jnp.sum(rows[:, -128:], axis=0, keepdims=True)
    rows = [lax.dynamic_index_in_dim(rows, at ^ section, 0) for at in range(SECTIONS)]
    sizes = [width, width, 3 * width, width, width, hidden, width]
    ends = [sum(sizes[: at + 1]) for at in range(len(sizes))]
    used = [(0, 0), (0, 1), (0, 2), (0, 3), (0, 4), (0, 5), (1, 3), (1, 4), (1, 5), (1, 6)]
    used += [(0, 6), (2, 0), (2, 1), (2, 2), (3, 3), (3, 4), (3, 5), (3, 6)]
    kept = [rows[slot][:, ends[which] - sizes[which] : ends[which]] for slot, which in used]
    language_count, *kept = weights.join([language_count, *kept], keys1)
    kept = dict(zip(used, kept))

    def row(slot, which):
        return kept[slot, which]

    crossed = weights.cross(keys + keys1)
    sends = weights.payloads(2, "F") if weights.four else weights.payloads(2)
    sends, (info, language_count) = under(sends, info, language_count)
    keys = weights.move(2, sends[:2])
    info, language_count = weights.join(
        [info, language_count + over_core(language_count)], theirs=crossed
    )
    plane_keys = []
    if weights.four:
        weights.mine["plane", 0] = sends[2]
        plane_keys = weights.move_planes(1)
    attend0 = weights.layer("a")
    outputs = attend_forward(
        x0, info, attend0, row(0, 0), row(0, 1), row(0, 2), following=(row(0, 3), row(0, 4))
    )
    y0, qkv0, mixed0, caption_rows = weights.join(outputs, keys)
    caption_rows = to_sections(caption_rows.reshape(-1, width))
    sends = weights.payloads(3, 4) if weights.four else weights.payloads(3)
    caption_rows = weights.join(caption_rows, plane_keys)
    sends, caption_rows = under(sends, *caption_rows)
    early_keys = keys
    keys, sends = weights.move(3, sends[:2]), sends[2:]
    crossed = weights.cross(early_keys)
    if weights.four:
        keys += weights.move_planes(2)
    outputs = shared_forward(caption_rows, expert_inputs[0], expert_inner_bias, expert_outputs[0])
    part = weights.join(outputs, keys, crossed)
    (y0,) = weights.join([y0], theirs=weights.cross([(3, 0), (3, 1)]))
    branch = {at: over_section(part[at], at, [0]) for at in range(1, SECTIONS)}
    keys = weights.move_planes(3) if weights.four else []
    expert1 = weights.layer("e")
    outputs = expert_forward(
        y0, info, expert1, row(1, 3), row(1, 4), row(1, 5), row(1, 6), PATCH_ROWS, "patch"
    )
    outputs, moved = under(outputs, *branch.values())
    if weights.four:
        keys += [("plane", step) for step in range(-2, 3)]
    x2, act1, slope1 = weights.join(outputs, keys)
    branch = dict(zip(branch, moved))
    branch[0] = part[0]
    branch = items_of(by_section(section, branch))
    if weights.four:
        crossed = [("plane", step) for step in range(-3, 4)]
    else:
        for step in (4, 5):
            weights.move(step, weights.payloads(step))
        crossed = [(4, 0), (4, 1), (5, 0)]
    weights.cross(crossed)
    attend2 = weights.layer("c") if weights.four else None
    if not weights.four:
        (x2,) = weights.join([x2], theirs=crossed)
        attend2 = weights.layer("c")
    outputs = attend_forward(
        x2, info, attend2, row(2, 0), row(2, 1), row(2, 2), merge=(y0, branch, row(0, 6))
    )
    if weights.four:
        language_count += over_plane(language_count, [(at, at ^ 1) for at in range(4)])
    x3, qkv2, mixed2, x2, language_count = weights.join([*outputs, language_count], theirs=crossed)
    if weights.four:
        language_count += over_plane(language_count, [(at, at ^ 2) for at in range(4)])
    else:
        language_count = lax.psum(language_count, "z")
    expert3 = weights.layer("f")
    outputs = expert_forward(
        x3, info, expert3, row(3, 3), row(3, 4), row(3, 5), row(3, 6), ROWS, "all"
    )
    layer_output, act3, slope3, language_count = under([*outputs, language_count])[0]
    language_count = language_count[0, 0].astype(jnp.int32)
    vision_count = PATCHES * items * SECTIONS * 2 * planes
    counts = jnp.stack(
        [jnp.full((), vision_count, jnp.int32), language_count, language_count + vision_count]
    )

    def small_rows(values):
        flat = jnp.concatenate(values, axis=1)
        count = -(-flat.shape[1] // hidden)
        flat = jnp.pad(flat, ((0, 0), (0, count * hidden - flat.shape[1])))
        return flat.reshape(count, hidden)

    def to_home(sums):
        got = [by_section(section, sums)]
        for bits in (1, 2, 3):
            sends = {at ^ bits: sums[at] for at in sums}
            got.append(over_section(by_section(section, sends), bits, sorted(sends)))
        return got

    keys = []
    if weights.four:
        sends, (layer_output, last_grad) = under(sends, layer_output, last_grad)
        keys = weights.move(4, sends)
    outputs = expert_backward(
        x3, info, expert3, row(3, 3), row(3, 4), act3, slope3, last_grad, ROWS, "all"
    )
    outputs = weights.join(outputs, keys)
    crossed = weights.cross(keys)
    grad3, *small3 = outputs[:5]
    sums3 = Sums(outputs[5:])
    sums3.cross()
    moved = over_links(sums3.first_sends())
    grad3 = after(grad3, *sums3.sent)
    outputs = attend_backward(
        x2, info, attend2, row(2, 0), row(2, 1), qkv2, mixed2, grad3
    )
    outputs, moved = under(outputs, *moved, sums3.got_stay)
    outputs = weights.join(outputs, theirs=crossed)
    grad2, *small2 = outputs[:4]
    sums2, caption_grad = Sums(outputs[4:8]), outputs[8]
    caption_grads = to_sections(caption_grad.reshape(-1, width))
    sums3.got_stay = moved[2]
    moved3 = over_links(sums3.second_sends(*moved[:2]))
    grad2 = after(grad2, *sums3.sent)
    outputs = expert_backward(
        y0, info, expert1, row(1, 3), row(1, 4), act1, slope1, grad2, PATCH_ROWS, "patch"
    )
    outputs, caption_grads = under(outputs, *caption_grads)
    grad1, *small1 = outputs[:5]
    sums2.cross(grad1)
    sums1 = Sums(outputs[5:])
    sums1.cross()
    inner_quarter = lax.dynamic_slice(row(0, 5), (0, section * width), (1, width))
    sum3 = sums3.whole(*moved3)
    inner_quarter = after(inner_quarter, grad1, sum3)
    outputs = shared_backward(
        caption_rows, caption_grads, info, weights.layer("g"), inner_quarter
    )
    parts, (keep0, send0, inner_grad, outer_grad) = outputs[:4], outputs[4:]
    got = [over_section(parts[bits], bits) for bits in (1, 2, 3)]
    sends = [after(value, *parts) for value in sums1.first_sends()]
    moved1 = over_links(sends)
    keep0 = added(keep0, over_core(send0))
    early = lax.psum(sum3, "z")
    inner_grad = lax.dynamic_update_slice(
        jnp.zeros((1, hidden), F32), inner_grad, (0, section * width)
    )
    small_early = small_rows([inner_grad, outer_grad] + small2 + small1 + small3)
    sends2 = [after(value, *sends) for value in sums2.first_sends()]
    moved2 = over_links(sends2)
    planes0 = Planes(keep0, plane, planes)
    sent0 = planes0.sends(*sends2)
    parts = [parts[0], *got]
    grad1, sums1.got_stay, sums2.got_stay = lax.optimization_barrier(
        (after(grad1, keep0, small_early, *sends, *sends2), sums1.got_stay, sums2.got_stay)
    )
    outputs = attend_backward(
        x0,
        info,
        attend0,
        row(0, 0),
        row(0, 1),
        qkv0,
        mixed0,
        grad1,
        first=(y0, row(0, 3), parts),
    )
    outputs, moved = under(outputs, *moved2, *moved1, *sent0)
    moved2, moved1 = moved[:2], moved[2:4]
    planes0.take(*moved[4:])
    tokens_grad, *small_first = outputs[:4]
    sums_first, gain_grad, shift_grad = Sums(outputs[4:8]), outputs[8], outputs[9]
    sums_first.cross()
    small_late = small_rows(small_first + [gain_grad, shift_grad])
    small = jnp.concatenate([small_late, small_early], axis=0)
    small = added(small, over_core(small))
    to_x, to_y = sums_first.first_sends()
    to_x = jnp.concatenate([to_x[0], small], axis=0)
    sends = lax.optimization_barrier((*sums1.second_sends(*moved1), to_x, to_y))
    moved1, moved = over_links(sends[:2]), over_links(sends[2:])
    sent0 = planes0.sends(*sends[2:])
    sum1, early = lax.optimization_barrier((sums1.whole(*moved1), early))
    planes1 = Planes(sum1, plane, planes)
    size = to_y.shape[1]
    moved, sent0 = under(moved, *sent0)
    planes0.take(*sent0)
    small = added(small, moved[0][size:])
    to_x, to_y = sums_first.second_sends(moved[0][None, :size], moved[1])
    early_x, early_y = sums2.second_sends(*moved2)
    to_x = jnp.concatenate([to_x[0], early_x[0]], axis=0)
    to_y = jnp.concatenate([to_y[0], early_y[0], small], axis=0)
    to_x, to_y = lax.optimization_barrier((to_x, to_y))
    sent1 = planes1.sends()
    sent0 = planes0.sends(to_x, to_y)
    moved = lax.optimization_barrier(tuple(over_links((to_x, to_y))))
    size = early_x.shape[1]
    last = sums_first.whole(moved[0][None, :size], moved[1][None, :size])
    sum2 = sums2.whole(moved[0][None, size:], moved[1][None, size : 2 * size])
    small = added(small, moved[1][2 * size :])
    small_count = small.shape[0]
    eighth = last.shape[1]
    last = jnp.concatenate([last[0], sum2[0], small], axis=0)
    planes_last = Planes(last, plane, planes)
    planes1.take(*sent1)
    planes0.take(*sent0)
    planes_last.take(*planes_last.sends())
    planes0.take(*planes0.sends(*moved))
    home_early = to_home({0: planes0.value, 3: after(early, planes0.value)})
    planes1.take(*planes1.sends())
    planes1.take(*planes1.sends())
    planes1.take(*planes1.sends())
    planes_last.take(*planes_last.sends())
    planes_last.take(*planes_last.sends())
    home_late = to_home({1: after(planes1.value, *home_early[1:3])})
    planes_last.take(*planes_last.sends())
    last = planes_last.value
    home_attend = to_home({0: last[None, :eighth], 2: last[None, eighth : 2 * eighth]})
    small = planes_last.in_order(last[2 * eighth :].astype(F32))

    as_float = counts.astype(F32)
    one = jnp.ones((), F32)
    attend_scales = jnp.stack([as_float[2], one, as_float[2], one])
    expert_scales = jnp.stack([as_float[1], as_float[0], one, as_float[2]])

    def placed(pieces, scales):
        scale = lax.dynamic_index_in_dim(scales, section, 0).reshape(1, 1)
        return finish(info, scale, pieces, [over_core(piece) for piece in pieces], planes)

    blank = jnp.zeros_like(home_late[0])
    inputs_whole, outputs_whole = placed(
        [
            after(by_section(section, {0: early, 1: late, 2: blank, 3: early}), *home_attend[1:])
            for early, late in zip(home_early, home_late)
        ],
        expert_scales,
    )
    blank = jnp.zeros_like(home_attend[0])
    attend_whole, output_whole = placed(
        [by_section(section, {0: got, 1: blank, 2: got, 3: blank}) for got in home_attend],
        attend_scales,
    )

    attend_size, expert_size = 5 * width, 3 * width + hidden
    late_rows = small_late.shape[0]
    late_small, early_small = small[:late_rows].reshape(-1), small[late_rows:].reshape(-1)
    cuts = [hidden + width, hidden + width + attend_size]
    cuts += [cuts[1] + expert_size, cuts[1] + 2 * expert_size]
    early_small = jnp.split(early_small, cuts)
    first_expert = late_small[attend_size : attend_size + 2 * width]
    small = [late_small[:attend_size], jnp.concatenate([first_expert, early_small[0]])]
    small += early_small[1:4]
    none_attend, none_expert = jnp.zeros_like(small[0]), jnp.zeros_like(small[1])
    attend_small = jnp.stack([small[0], none_attend, small[2], none_attend])
    expert_small = jnp.stack([small[1], small[3], none_expert, small[4]])
    attend_small = attend_small / attend_scales.reshape(-1, 1)
    expert_small = expert_small / expert_scales.reshape(-1, 1)
    attend_small = lax.dynamic_index_in_dim(attend_small, section, 0)
    expert_small = lax.dynamic_index_in_dim(expert_small, section, 0)
    return (
        layer_output[:, :positions],
        tokens_grad[:, :positions],
        attend_small[:, :width],
        attend_small[:, width : 2 * width],
        attend_whole,
        attend_small[:, 2 * width :],
        output_whole,
        expert_small[:, :width],
        expert_small[:, width : 2 * width],
        inputs_whole,
        expert_small[:, 2 * width : 2 * width + hidden],
        outputs_whole,
        expert_small[:, 2 * width + hidden :],
        counts,
    )


def solution(mesh):
    sections, groups = mesh.shape["section"], mesh.shape["dp"]
    split = Mesh(mesh.devices.reshape(sections, groups // 2, 2), ("section", "z", "core"))
    items = P(("section", "z", "core"), None, None)
    flat = P("section", None)
    matrix = P("section", None, None)
    placed = (
        items,
        P(("section", "z", "core")),
        flat,
        flat,
        matrix,
        flat,
        matrix,
        flat,
        flat,
        matrix,
        flat,
        matrix,
        flat,
        items,
    )
    return jax.shard_map(
        per_device,
        mesh=split,
        in_specs=placed,
        out_specs=(
            items,
            items,
            flat,
            flat,
            matrix,
            flat,
            matrix,
            flat,
            flat,
            matrix,
            flat,
            matrix,
            flat,
            P(),
        ),
        check_vma=False,
    )
```

```python
from functools import partial

import jax
import jax.numpy as jnp
from jax import lax
from jax.experimental import pallas as pl
from jax.experimental.pallas import tpu as pltpu
from jax.sharding import Mesh
from jax.sharding import PartitionSpec as P

HEADS = 12
HEAD_DIM = 64
PATCHES = 197
ROWS = 256
CAP_FIRST, CAP_ROWS = 192, 48
PATCH_ROWS = 208
PAIR = 2 * HEAD_DIM
SECTIONS = 4
PIECE_ROWS = 48
VMEM_BYTES = 58 * 1024 * 1024
F32 = jnp.float32
BF16 = jnp.bfloat16

PLAN_FOUR = (
    ({0: "a0", 1: "e0", 2: "c0", 3: "F"}, {0: "a1", 1: "e2", 2: "c0", 3: "F"}),
    ({0: "a1", 1: "e1", 2: "a1", 3: "e2"}, {0: "a0", 1: "a0", 2: "F", 3: "c0"}),
    ({0: "g3", 1: "e2", 2: "c1"}, {0: "e0", 1: "e3", 2: "c1"}),
    ({0: "g1", 1: "e3", 2: "e0", 3: "e3"}, {0: "e1", 1: "e1", 3: "c1"}),
    ({}, {0: "g2", 1: "g3"}),
)
PLAN_ANY = (
    ({0: "a0", 1: "e0", 2: "c0", 3: "f0"}, {0: "a1", 1: "e2", 2: "c0", 3: "f0"}),
    ({0: "a1", 1: "e1", 2: "a1", 3: "e2"}, {0: "a0", 1: "a0", 2: "c1", 3: "f1"}),
    ({0: "g3", 1: "e2", 2: "c1", 3: "f1"}, {0: "e0", 1: "e3", 2: "f0", 3: "f2"}),
    ({0: "g1", 1: "e3", 2: "e0", 3: "e3"}, {0: "e1", 1: "e1", 2: "f1", 3: "f3"}),
    ({0: "c1", 1: "f2", 3: "f2"}, {0: "g2", 1: "g3", 3: "c0"}),
    ({1: "f3", 3: "f3"}, {}),
)
HOMES = {"a": 0, "c": 2, "e": 1, "f": 3, "F": 3, "g": 0}
ATTEND_BLOCKS = ((0, 1), (2, 3))
EXPERT_BLOCKS = ((0, 1), (4, 5), (2, 3), (6, 7))


def dot_plain(left, right):
    return jnp.dot(left, right, preferred_element_type=F32)


def dot_last(left, right):
    return lax.dot_general(left, right, (((1,), (1,)), ((), ())), preferred_element_type=F32)


def dot_first(left, right):
    return lax.dot_general(left, right, (((0,), (0,)), ((), ())), preferred_element_type=F32)


def column_sum(matrix):
    return jnp.sum(matrix.astype(F32), axis=0, keepdims=True)


def norm_parts(rows):
    centre = rows - jnp.mean(rows, axis=-1, keepdims=True)
    scale = lax.rsqrt(jnp.mean(centre * centre, axis=-1, keepdims=True) + 1e-06)
    return centre * scale, scale


def norm_back(normed_grad, unit, scale, gain):
    unit_grad = normed_grad * gain
    along = jnp.mean(unit_grad * unit, axis=-1, keepdims=True)
    return scale * (unit_grad - jnp.mean(unit_grad, axis=-1, keepdims=True) - unit * along)


def true_positions(length, first, count, axis, kind):
    shape = (count, 1) if axis == 0 else (1, count)
    position = first + lax.broadcasted_iota(jnp.int32, shape, axis)
    patch = position < PATCHES
    if kind == "patch":
        return patch
    caption = (position >= PATCHES) & (position - PATCHES < length)
    return caption if kind == "caption" else patch | caption


def head_masks():
    lane = lax.broadcasted_iota(jnp.int32, (1, PAIR), 1)
    even = (lane < HEAD_DIM).astype(F32).astype(BF16)
    odd = (lane >= HEAD_DIM).astype(F32).astype(BF16)
    return lane < HEAD_DIM, even, odd


def split_pair(pair, even, odd):
    return jnp.concatenate([pair * even, pair * odd], axis=0)


def start_weights(info, first, refs, plan, blocks, sems):
    half = blocks.shape[1] // 2
    section, core, plane = info[first], info[first + 1], info[first + 2]
    for at, at_plane, steps in plan:
        here = section == at
        if at_plane is not None:
            here = here & (plane == at_plane)

        @pl.when(here)
        def _(steps=steps):
            for block, source in steps:
                if source[0] == "own":
                    _, which, row, column = source
                    width = blocks.shape[2]
                    for part in range(2):
                        pltpu.make_async_copy(
                            refs[which].at[
                                pl.ds(row + part * half, half), pl.ds(column, width)
                            ],
                            blocks.at[block, pl.ds(part * half, half)],
                            sems.at[block],
                        ).start()
                else:
                    _, mine, theirs, index = source
                    pltpu.make_async_copy(
                        refs[mine].at[index],
                        blocks.at[block, pl.ds(pl.multiple_of(core * half, half), half)],
                        sems.at[block],
                    ).start()
                    pltpu.make_async_copy(
                        refs[theirs].at[index],
                        blocks.at[block, pl.ds(pl.multiple_of((1 - core) * half, half), half)],
                        sems.at[block],
                    ).start()


def wait_block(blocks, block, sems):
    pltpu.make_async_copy(blocks.at[block], blocks.at[block], sems.at[block]).wait()


def store_turned(target, turned, columns, section, core):
    half = target.shape[0] // 2
    for piece in range(16):
        path, owner = (piece >> 2) & 1, piece & 3
        away = owner ^ section
        place = ((away & 1) << 1) | (away >> 1) if path == 0 else away
        row = ((piece >> 3) ^ core) * half + (place >> 1) * (half // 2)
        row = row + path * (half // 4) + (place & 1) * PIECE_ROWS
        target[pl.ds(pl.multiple_of(row, 16), PIECE_ROWS), columns] = turned[
            piece * PIECE_ROWS : (piece + 1) * PIECE_ROWS
        ]


def put_travel(refs, which, columns, left, right):
    half = left.shape[0] // 2
    for side in range(2):
        rows = dot_plain(left[side * half : (side + 1) * half], right).astype(BF16)
        refs[2 * side][which, :, columns] = rows[: half // 2]
        refs[2 * side + 1][which, :, columns] = rows[half // 2 :]


def attend_forward_kernel(plan, weight_count, merge, info, *refs):
    weights, refs = refs[:weight_count], refs[weight_count:]
    if merge:
        x_ref, before_ref, part_ref, outer_ref, gain_ref, shift_ref, bias_ref = refs[:7]
        y_ref, qkv_ref, mixed_ref, joined_ref, blocks, sems, joined = refs[7:]
    else:
        x_ref, gain_ref, shift_ref, bias_ref, next_gain_ref, next_shift_ref = refs[:6]
        y_ref, qkv_ref, mixed_ref, caption_ref, blocks, sems = refs[6:]
    item = pl.program_id(0)
    items = pl.num_programs(0)
    length = info[item]
    width = x_ref.shape[-1]

    @pl.when(item == 0)
    def _():
        start_weights(info, items, weights, plan, blocks, sems)

    cap = slice(CAP_FIRST, CAP_FIRST + CAP_ROWS)
    if merge:
        joined[...] = x_ref[0].astype(F32)
        branch = part_ref[0].astype(F32) + outer_ref[...]
        is_true = true_positions(length, CAP_FIRST, CAP_ROWS, 0, "caption")
        captions = before_ref[0, cap] + jnp.where(is_true, branch, 0.0)
        position = CAP_FIRST + lax.broadcasted_iota(jnp.int32, (CAP_ROWS, 1), 0)
        captions = captions.astype(BF16).astype(F32)
        joined[cap] = jnp.where(position < PATCHES, joined[cap], captions)
        x = joined[...]
        joined_ref[0] = x.astype(BF16)
    else:
        x = x_ref[0].astype(F32)
    unit, _ = norm_parts(x)
    normed = (unit * gain_ref[...] + shift_ref[...]).astype(BF16)

    @pl.when(item == 0)
    def _():
        for block in range(4):
            wait_block(blocks, block, sems)

    queries = dot_plain(normed, blocks[0]) + bias_ref[:, :width]
    qkv_ref[0, :, :width] = (queries * HEAD_DIM ** (-0.5)).astype(BF16)
    qkv_ref[0, :, width : 2 * width] = dot_plain(normed, blocks[1]).astype(BF16)
    values = dot_plain(normed, blocks[2]) + bias_ref[:, width : 2 * width]
    qkv_ref[0, :, 2 * width :] = values.astype(BF16)
    key_true = true_positions(length, 0, ROWS, 1, "all")
    low_half, even, odd = head_masks()
    ones = jnp.ones((ROWS, PAIR), BF16)

    def scores_of(pair):
        at = pair * PAIR
        q2 = qkv_ref[0, :, at : at + PAIR]
        k2 = qkv_ref[0, :, width + at : width + at + PAIR]
        return dot_last(split_pair(q2, even, odd), k2)

    ahead = [scores_of(0), scores_of(1)]
    for pair in range(HEADS // 2):
        at = pair * PAIR
        scores = jnp.where(key_true, ahead.pop(0), -1e9)
        if pair + 2 < HEADS // 2:
            ahead.append(scores_of(pair + 2))
        weight = jnp.exp(scores - jnp.max(scores, axis=-1, keepdims=True)).astype(BF16)
        v2 = qkv_ref[0, :, 2 * width + at : 2 * width + at + PAIR]
        summed = dot_plain(weight, jnp.concatenate([v2, ones], axis=1))
        top = jnp.where(low_half, summed[:ROWS, :PAIR], summed[ROWS:, :PAIR])
        below = jnp.where(low_half, summed[:ROWS, PAIR:], summed[ROWS:, PAIR:])
        mixed_ref[0, :, at : at + PAIR] = (top / below).astype(BF16)
    branch = dot_plain(mixed_ref[0], blocks[3]) + bias_ref[:, 2 * width :]
    row_true = true_positions(length, 0, ROWS, 0, "all")
    y = x + jnp.where(row_true, branch, 0.0)
    y_ref[0] = y.astype(y_ref.dtype)
    if not merge:
        unit, _ = norm_parts(y[cap])
        caption_ref[0] = (unit * next_gain_ref[...] + next_shift_ref[...]).astype(BF16)


def attend_backward_kernel(plan, weight_count, first, info, *refs):
    weights, refs = refs[:weight_count], refs[weight_count:]
    x_ref, gain_ref, shift_ref, qkv_ref, mixed_ref, grad_ref = refs[:6]
    if first:
        after_ref, next_gain_ref, *parts = refs[6:12]
        refs = refs[12:]
    else:
        refs = refs[6:]
    out_ref, gain_grad_ref, shift_grad_ref, bias_grad_ref = refs[:4]
    travel_refs = refs[4:8]
    if first:
        next_gain_grad_ref, next_shift_grad_ref, joined = refs[8], refs[9], refs[-1]
    else:
        caption_ref = refs[8]
    blocks, sems, normed_turned, mixed_turned, branch_all, projected, mixed_grad = refs[
        10 if first else 9 :
    ][:7]
    item = pl.program_id(0)
    items = pl.num_programs(0)
    length = info[item]
    section, core = info[items], info[items + 1]
    width = x_ref.shape[-1]
    here = pl.ds(pl.multiple_of(item * ROWS, ROWS), ROWS)
    cap = slice(CAP_FIRST, CAP_FIRST + CAP_ROWS)

    @pl.when(item == 0)
    def _():
        start_weights(info, items, weights, plan, blocks, sems)

    def add_to(ref, part):
        @pl.when(item == 0)
        def _():
            ref[...] = part

        @pl.when(item > 0)
        def _():
            ref[...] += part

    x = x_ref[0].astype(F32)
    unit, scale = norm_parts(x)
    normed = (unit * gain_ref[...] + shift_ref[...]).astype(BF16)
    incoming = grad_ref[0].astype(F32)
    if first:
        after_unit, after_scale = norm_parts(after_ref[0, cap])
        caption_grad = parts[0][...].astype(F32)
        for part in parts[1:]:
            caption_grad = caption_grad + part[...].astype(F32)
        joined[...] = incoming
        joined[cap] += norm_back(caption_grad, after_unit, after_scale, next_gain_ref[...])
        incoming = joined[...]
        add_to(next_gain_grad_ref, jnp.sum(caption_grad * after_unit, axis=0, keepdims=True))
        add_to(next_shift_grad_ref, jnp.sum(caption_grad, axis=0, keepdims=True))
    row_true = true_positions(length, 0, ROWS, 0, "all")
    branch = jnp.where(row_true, incoming, 0.0).astype(BF16)
    branch_all[here, :] = branch
    store_turned(normed_turned, normed.T, here, section, core)
    store_turned(mixed_turned, mixed_ref[0].T, here, section, core)

    @pl.when(item == 0)
    def _():
        for block in range(4):
            wait_block(blocks, block, sems)

    mixed_grad[...] = dot_last(branch, blocks[3]).astype(BF16)
    key_true = true_positions(length, 0, ROWS, 0, "all")
    _, even, odd = head_masks()

    def products_of(pair):
        at = pair * PAIR
        q2 = split_pair(qkv_ref[0, :, at : at + PAIR], even, odd)
        k2 = qkv_ref[0, :, width + at : width + at + PAIR]
        v2 = qkv_ref[0, :, 2 * width + at : 2 * width + at + PAIR]
        g2 = split_pair(mixed_grad[:, at : at + PAIR], even, odd)
        return q2, k2, g2, dot_last(k2, q2), dot_last(v2, g2)

    ahead = [products_of(0)]
    for pair in range(HEADS // 2):
        at = pair * PAIR
        q2, k2, g2, scores, weight_grad = ahead.pop(0)
        if pair + 1 < HEADS // 2:
            ahead.append(products_of(pair + 1))
        scores = jnp.where(key_true, scores, -1e9)
        weight = jnp.exp(scores - jnp.max(scores, axis=0, keepdims=True))
        weight = weight * (1.0 / jnp.sum(weight, axis=0, keepdims=True))
        product = weight * weight_grad
        along = jnp.sum(product, axis=0, keepdims=True)
        score_grad = (product - weight * along).astype(BF16)
        values_grad = dot_plain(weight.astype(BF16), g2).astype(BF16)
        keys_grad = dot_plain(score_grad, q2).astype(BF16)
        k2_split = split_pair(k2, even, odd)
        stacked = jnp.concatenate([score_grad[:, :ROWS], score_grad[:, ROWS:]], axis=0)
        queries_grad = dot_first(stacked, k2_split).astype(BF16)
        queries_grad = (queries_grad.astype(F32) * HEAD_DIM ** (-0.5)).astype(BF16)
        projected[here, at : at + PAIR] = queries_grad
        projected[here, width + at : width + at + PAIR] = keys_grad
        projected[here, 2 * width + at : 2 * width + at + PAIR] = values_grad
    normed_grad = dot_last(projected[here, :width], blocks[0])
    normed_grad += dot_last(projected[here, width : 2 * width], blocks[1])
    normed_grad += dot_last(projected[here, 2 * width :], blocks[2])
    out = (incoming + norm_back(normed_grad, unit, scale, gain_ref[...])).astype(BF16)
    out_ref[0] = out
    if not first:
        is_true = true_positions(length, CAP_FIRST, CAP_ROWS, 0, "caption")
        caption_ref[0] = jnp.where(is_true, out[cap].astype(F32), 0.0).astype(BF16)
    add_to(gain_grad_ref, jnp.sum(normed_grad * unit, axis=0, keepdims=True))
    add_to(shift_grad_ref, jnp.sum(normed_grad, axis=0, keepdims=True))

    @pl.when(item == items - 1)
    def _():
        for block in range(4):
            columns = slice(block * width, (block + 1) * width)
            left = normed_turned if block < 3 else mixed_turned
            right = projected[:, columns] if block < 3 else branch_all[...]
            put_travel(travel_refs, 0, columns, left, right)
        bias_grad_ref[:, :width] = column_sum(projected[:, :width])
        bias_grad_ref[:, width : 2 * width] = column_sum(projected[:, 2 * width :])
        bias_grad_ref[:, 2 * width :] = column_sum(branch_all[...])


SHORT = pl.CostEstimate(flops=0, bytes_accessed=100_000, transcendentals=0)
LONG = pl.CostEstimate(flops=30_000_000_000, bytes_accessed=30_000_000, transcendentals=0)
ANYWHERE = pl.BlockSpec(memory_space=pl.ANY)


def whole_block(shape):
    return pl.BlockSpec(shape, lambda step, info: (0,) * len(shape))


def item_block(shape):
    return pl.BlockSpec((1,) + shape[1:], lambda step, info: (step,) + (0,) * (len(shape) - 1))


def blocks_scratch(count, width):
    return [pltpu.VMEM((count, width, width), BF16), pltpu.SemaphoreType.DMA((count,))]


def attend_forward(x, info, weights, gain, shift, bias, merge=None, following=None):
    arrays, plan = weights
    items, _, width = x.shape
    row = whole_block((1, width))
    bias_row = whole_block((1, 3 * width))
    caption_shape = (items, CAP_ROWS, width)
    if merge is not None:
        before, part, outer = merge
        operands = (x, before, part, outer, gain, shift, bias)
        specs = [item_block(x.shape), item_block(x.shape), item_block(caption_shape)]
        specs += [row, row, row, bias_row]
        last_shape, kind, scratch = x.shape, BF16, [pltpu.VMEM((ROWS, width), F32)]
    else:
        operands = (x, gain, shift, bias, *following)
        specs = [item_block(x.shape), row, row, bias_row, row, row]
        last_shape, kind, scratch = caption_shape, F32, []
    return pl.pallas_call(
        partial(attend_forward_kernel, plan, len(arrays), merge is not None),
        grid_spec=pltpu.PrefetchScalarGridSpec(
            num_scalar_prefetch=1,
            grid=(items,),
            in_specs=[ANYWHERE] * len(arrays) + specs,
            out_specs=[
                item_block(x.shape),
                item_block((items, ROWS, 3 * width)),
                item_block((items, ROWS, width)),
                item_block(last_shape),
            ],
            scratch_shapes=blocks_scratch(4, width) + scratch,
        ),
        out_shape=[
            jax.ShapeDtypeStruct(x.shape, kind),
            jax.ShapeDtypeStruct((items, ROWS, 3 * width), BF16),
            jax.ShapeDtypeStruct((items, ROWS, width), BF16),
            jax.ShapeDtypeStruct(last_shape, BF16),
        ],
        compiler_params=pltpu.CompilerParams(vmem_limit_bytes=VMEM_BYTES),
        cost_estimate=SHORT,
        name="attend_forward",
    )(info, *arrays, *operands)


def attend_backward(x, info, weights, gain, shift, qkv, mixed, incoming, first=None):
    arrays, plan = weights
    items, _, width = x.shape
    half = width // 2
    row = whole_block((1, width))
    caption_shape = (items, CAP_ROWS, width)
    operands = (x, gain, shift, qkv, mixed, incoming)
    specs = [item_block(x.shape), row, row, item_block(qkv.shape), item_block(mixed.shape)]
    specs += [item_block(incoming.shape)]
    outs = [
        (item_block(x.shape), x.shape, BF16),
        (row, (1, width), F32),
        (row, (1, width), F32),
        (whole_block((1, 3 * width)), (1, 3 * width), F32),
    ]
    outs += [(whole_block((1, half // 2, 4 * width)), (1, half // 2, 4 * width), BF16)] * 4
    scratch = []
    if first is not None:
        after, next_gain, parts = first
        operands += (after, next_gain, *parts)
        caption_rows = pl.BlockSpec((CAP_ROWS, width), lambda step, info: (step, 0))
        specs += [item_block(after.shape), row] + [caption_rows] * 4
        outs += [(row, (1, width), F32)] * 2
        scratch = [pltpu.VMEM((ROWS, width), F32)]
    else:
        outs += [(item_block(caption_shape), caption_shape, BF16)]
    return pl.pallas_call(
        partial(attend_backward_kernel, plan, len(arrays), first is not None),
        grid_spec=pltpu.PrefetchScalarGridSpec(
            num_scalar_prefetch=1,
            grid=(items,),
            in_specs=[ANYWHERE] * len(arrays) + specs,
            out_specs=[spec for spec, _, _ in outs],
            scratch_shapes=blocks_scratch(4, width)
            + [
                pltpu.VMEM((width, items * ROWS), BF16),
                pltpu.VMEM((width, items * ROWS), BF16),
                pltpu.VMEM((items * ROWS, width), BF16),
                pltpu.VMEM((items * ROWS, 3 * width), BF16),
                pltpu.VMEM((ROWS, width), BF16),
            ]
            + scratch,
        ),
        out_shape=[jax.ShapeDtypeStruct(shape, kind) for _, shape, kind in outs],
        compiler_params=pltpu.CompilerParams(vmem_limit_bytes=VMEM_BYTES),
        cost_estimate=LONG,
        name="attend_backward",
    )(info, *arrays, *operands)


def normal_parts(u):
    t = pl.reciprocal(1.0 + 0.23164190 * jnp.abs(u), approx=True)
    bell = jnp.exp2((u * -0.7213475204444817) * u)
    poly = t * (
        0.127414796
        + t * (-0.142248368 + t * (0.7107068705 + t * (-0.7265760135 + t * 0.5307027145)))
    )
    tail = poly * bell
    return jnp.where(u < 0, tail, 1.0 - tail), bell


def inner_forward(normed, matrix, bias):
    inner = dot_plain(normed, matrix) + bias
    cumulative, bell = normal_parts(inner)
    slope = cumulative + (inner * 0.3989422804014327) * bell
    return (inner * cumulative).astype(BF16), slope.astype(BF16)


def expert_forward_kernel(plan, weight_count, count, kind, info, *refs):
    weights, refs = refs[:weight_count], refs[weight_count:]
    x_ref, gain_ref, shift_ref, inner_ref, outer_ref = refs[:5]
    y_ref, act_ref, slope_ref, blocks, sems, normed, total = refs[5:]
    step = pl.program_id(0)
    items, _, width = x_ref.shape

    @pl.when(step == 0)
    def _():
        start_weights(info, items, weights, plan, blocks, sems)
        for item in range(items):
            x = x_ref[item, :count].astype(BF16).astype(F32)
            unit, _ = norm_parts(x)
            normed[item * count : (item + 1) * count] = (
                unit * gain_ref[...] + shift_ref[...]
            ).astype(BF16)

    wait_block(blocks, step, sems)
    wait_block(blocks, step + 4, sems)
    for at in range(0, width, 256):
        columns = slice(at, at + 256)
        act, slope = inner_forward(normed[...], blocks[step, :, columns], inner_ref[:, columns])
        act_ref[:, columns] = act
        slope_ref[:, columns] = slope
    part = dot_plain(act_ref[...], blocks[step + 4])

    @pl.when(step == 0)
    def _():
        total[...] = part

    @pl.when(step > 0)
    def _():
        total[...] += part

    @pl.when(step == pl.num_programs(0) - 1)
    def _():
        for item in range(items):
            row_true = true_positions(info[item], 0, count, 0, kind)
            branch = total[item * count : (item + 1) * count] + outer_ref[...]
            x = x_ref[item, :count].astype(BF16).astype(F32)
            y_ref[item, :count] = (x + jnp.where(row_true, branch, 0.0)).astype(BF16)
            if count < ROWS:
                y_ref[item, count:] = jnp.zeros((ROWS - count, width), BF16)


def expert_backward_kernel(plan, weight_count, count, kind, info, *refs):
    weights, refs = refs[:weight_count], refs[weight_count:]
    x_ref, gain_ref, shift_ref, act_ref, slope_ref, grad_ref = refs[:6]
    out_ref, gain_grad_ref, shift_grad_ref, inner_grad_ref, outer_grad_ref = refs[6:11]
    travel_refs = refs[11:15]
    blocks, sems, normed_turned, branch_turned, branch, inner_all, total = refs[15:]
    step = pl.program_id(0)
    items, _, width = x_ref.shape
    section, core = info[items], info[items + 1]

    @pl.when(step == 0)
    def _():
        start_weights(info, items, weights, plan, blocks, sems)
        outer = None
        for item in range(items):
            here = slice(item * count, (item + 1) * count)
            unit, _ = norm_parts(x_ref[item, :count].astype(BF16).astype(F32))
            normed = (unit * gain_ref[...] + shift_ref[...]).astype(BF16)
            row_true = true_positions(info[item], 0, count, 0, kind)
            incoming = grad_ref[item, :count].astype(F32)
            masked = jnp.where(row_true, incoming, 0.0).astype(BF16)
            branch[here] = masked
            store_turned(normed_turned, normed.T, here, section, core)
            store_turned(branch_turned, masked.T, here, section, core)
            term = column_sum(masked)
            outer = term if outer is None else outer + term
        outer_grad_ref[...] = outer

    wait_block(blocks, step, sems)
    wait_block(blocks, step + 4, sems)
    for at in range(0, width, 256):
        columns = slice(at, at + 256)
        act_grad = dot_last(branch[...], blocks[step + 4, columns])
        inner = (slope_ref[:, columns].astype(F32) * act_grad).astype(BF16)
        inner_all[:, columns] = inner
        inner_grad_ref[:, columns] = column_sum(inner)
        put_travel(travel_refs, 0, columns, normed_turned, inner)
        put_travel(travel_refs, 1, columns, branch_turned, act_ref[:, columns])
    part = dot_last(inner_all[...], blocks[step])

    @pl.when(step == 0)
    def _():
        total[...] = part

    @pl.when(step > 0)
    def _():
        total[...] += part

    @pl.when(step == pl.num_programs(0) - 1)
    def _():
        gain_sum, shift_sum = None, None
        for item in range(items):
            unit, scale = norm_parts(x_ref[item, :count].astype(BF16).astype(F32))
            normed_grad = total[item * count : (item + 1) * count]
            gain_part = jnp.sum(normed_grad * unit, axis=0, keepdims=True)
            shift_part = jnp.sum(normed_grad, axis=0, keepdims=True)
            gain_sum = gain_part if gain_sum is None else gain_sum + gain_part
            shift_sum = shift_part if shift_sum is None else shift_sum + shift_part
            incoming = grad_ref[item, :count].astype(F32)
            hidden = incoming + norm_back(normed_grad, unit, scale, gain_ref[...])
            out_ref[item, :count] = hidden.astype(BF16)
            if count < ROWS:
                out_ref[item, count:] = grad_ref[item, count:]
        gain_grad_ref[...] = gain_sum
        shift_grad_ref[...] = shift_sum


def shared_forward_kernel(*refs):
    *rows_refs, inputs_ref, inner_ref, outputs_ref = refs[:7]
    *part_refs, normed, total = refs[7:]
    count = rows_refs[0].shape[0]
    step = pl.program_id(0)

    @pl.when(step == 0)
    def _():
        for index, ref in enumerate(rows_refs):
            normed[index * count : (index + 1) * count] = ref[...]
        total[...] = jnp.zeros_like(total)

    act, _ = inner_forward(normed[...], inputs_ref[...], inner_ref[...])
    total[...] += dot_plain(act, outputs_ref[...])

    @pl.when(step == pl.num_programs(0) - 1)
    def _():
        for index, ref in enumerate(part_refs):
            ref[...] = total[index * count : (index + 1) * count].astype(BF16)


def shared_backward_kernel(plan, weight_count, info, *refs):
    weights, refs = refs[:weight_count], refs[weight_count:]
    rows_refs, grad_refs, inner_ref = refs[:4], refs[4:8], refs[8]
    part_refs, (keep_ref, send_ref, inner_grad_ref, outer_grad_ref) = refs[9:13], refs[13:17]
    blocks, sems, normed, branch, matrix = refs[17:]
    count, width = rows_refs[0].shape
    half = width // 2
    first = info.shape[0] - 3
    core = info[first + 1]
    start_weights(info, first, weights, plan, blocks, sems)
    for index in range(SECTIONS):
        here = slice(index * count, (index + 1) * count)
        normed[here] = rows_refs[index][...]
        branch[here] = grad_refs[index][...]
    outer_grad_ref[...] = column_sum(grad_refs[0][...])
    wait_block(blocks, 0, sems)
    wait_block(blocks, 1, sems)
    part = None
    for at in range(0, width, 256):
        columns = slice(at, at + 256)
        act, slope = inner_forward(normed[...], blocks[0, :, columns], inner_ref[:, columns])
        act_grad = dot_last(branch[...], blocks[1, columns])
        inner = (slope.astype(F32) * act_grad).astype(BF16)
        inner_grad_ref[:, columns] = column_sum(inner)
        matrix[0, :, columns] = dot_first(normed[...], inner).astype(BF16)
        matrix[1, :, columns] = dot_first(branch[...], act).astype(BF16)
        term = dot_last(inner, blocks[0, :, columns])
        part = term if part is None else part + term
    for index, ref in enumerate(part_refs):
        ref[...] = part[index * count : (index + 1) * count].astype(BF16)
    quarter = half // 4
    for which in range(2):
        for group in range(4):
            columns = slice(group * width, (group + 1) * width)
            mine = pl.multiple_of(core * half, 16) + group * quarter
            other = pl.multiple_of((1 - core) * half, 16) + group * quarter
            keep_ref[which, :, columns] = matrix[which, pl.ds(pl.multiple_of(mine, 16), quarter)]
            send_ref[which, :, columns] = matrix[which, pl.ds(pl.multiple_of(other, 16), quarter)]


def chunk_columns(rows, width):
    return pl.BlockSpec((rows, width), lambda step, info: (0, step))


def expert_forward(x, info, weights, gain, shift, inner, outer, count, kind):
    arrays, plan = weights
    items, _, width = x.shape
    hidden = inner.shape[1]
    row = whole_block((1, width))
    return pl.pallas_call(
        partial(expert_forward_kernel, plan, len(arrays), count, kind),
        grid_spec=pltpu.PrefetchScalarGridSpec(
            num_scalar_prefetch=1,
            grid=(hidden // width,),
            in_specs=[ANYWHERE] * len(arrays)
            + [whole_block(x.shape), row, row, chunk_columns(1, width), row],
            out_specs=[
                whole_block((items, ROWS, width)),
                chunk_columns(items * count, width),
                chunk_columns(items * count, width),
            ],
            scratch_shapes=blocks_scratch(8, width)
            + [
                pltpu.VMEM((items * count, width), BF16),
                pltpu.VMEM((items * count, width), F32),
            ],
        ),
        out_shape=[
            jax.ShapeDtypeStruct((items, ROWS, width), BF16),
            jax.ShapeDtypeStruct((items * count, hidden), BF16),
            jax.ShapeDtypeStruct((items * count, hidden), BF16),
        ],
        compiler_params=pltpu.CompilerParams(vmem_limit_bytes=VMEM_BYTES),
        cost_estimate=SHORT,
        name="expert_forward_" + kind,
    )(info, *arrays, x, gain, shift, inner, outer)


def expert_backward(x, info, weights, gain, shift, act, slope, incoming, count, kind):
    arrays, plan = weights
    items, _, width = x.shape
    half = width // 2
    hidden = act.shape[1]
    row = whole_block((1, width))
    travel = pl.BlockSpec((2, half // 2, width), lambda step, info: (0, 0, step))
    return pl.pallas_call(
        partial(expert_backward_kernel, plan, len(arrays), count, kind),
        grid_spec=pltpu.PrefetchScalarGridSpec(
            num_scalar_prefetch=1,
            grid=(hidden // width,),
            in_specs=[ANYWHERE] * len(arrays)
            + [
                whole_block(x.shape),
                row,
                row,
                chunk_columns(items * count, width),
                chunk_columns(items * count, width),
                whole_block(incoming.shape),
            ],
            out_specs=[whole_block(incoming.shape), row, row, chunk_columns(1, width), row]
            + [travel] * 4,
            scratch_shapes=blocks_scratch(8, width)
            + [
                pltpu.VMEM((width, items * count), BF16),
                pltpu.VMEM((width, items * count), BF16),
                pltpu.VMEM((items * count, width), BF16),
                pltpu.VMEM((items * count, width), BF16),
                pltpu.VMEM((items * count, width), F32),
            ],
        ),
        out_shape=[
            jax.ShapeDtypeStruct(incoming.shape, BF16),
            jax.ShapeDtypeStruct((1, width), F32),
            jax.ShapeDtypeStruct((1, width), F32),
            jax.ShapeDtypeStruct((1, hidden), F32),
            jax.ShapeDtypeStruct((1, width), F32),
        ]
        + [jax.ShapeDtypeStruct((2, half // 2, hidden), BF16)] * 4,
        compiler_params=pltpu.CompilerParams(vmem_limit_bytes=VMEM_BYTES),
        cost_estimate=SHORT,
        name="expert_backward_" + kind,
    )(info, *arrays, x, gain, shift, act, slope, incoming)


IN_VMEM = pl.BlockSpec(memory_space=pltpu.VMEM)
IN_SMEM = pl.BlockSpec(memory_space=pltpu.SMEM)


def shared_forward(rows, inputs, inner, outputs):
    count, width = rows[0].shape
    total = SECTIONS * count
    hidden = inner.shape[1]
    return pl.pallas_call(
        shared_forward_kernel,
        grid=(hidden // width,),
        in_specs=[pl.BlockSpec(rows[0].shape, lambda step: (0, 0))] * 4
        + [
            pl.BlockSpec((width, width), lambda step: (0, step)),
            pl.BlockSpec((1, width), lambda step: (0, step)),
            pl.BlockSpec((width, width), lambda step: (step, 0)),
        ],
        out_specs=[pl.BlockSpec((count, width), lambda step: (0, 0))] * SECTIONS,
        scratch_shapes=[pltpu.VMEM((total, width), BF16), pltpu.VMEM((total, width), F32)],
        out_shape=[jax.ShapeDtypeStruct((count, width), BF16)] * SECTIONS,
        compiler_params=pltpu.CompilerParams(vmem_limit_bytes=VMEM_BYTES),
        cost_estimate=SHORT,
        name="shared_forward",
    )(*rows, inputs, inner, outputs)


def shared_backward(rows, grads, info, weights, inner):
    arrays, plan = weights
    count, width = rows[0].shape
    total = SECTIONS * count
    travel = (2, width // 8, 4 * width)
    return pl.pallas_call(
        partial(shared_backward_kernel, plan, len(arrays)),
        in_specs=[IN_SMEM] + [ANYWHERE] * len(arrays) + [IN_VMEM] * 9,
        out_specs=[IN_VMEM] * 8,
        scratch_shapes=blocks_scratch(2, width)
        + [
            pltpu.VMEM((total, width), BF16),
            pltpu.VMEM((total, width), BF16),
            pltpu.VMEM((2, width, width), BF16),
        ],
        out_shape=[
            *[jax.ShapeDtypeStruct((count, width), BF16)] * SECTIONS,
            jax.ShapeDtypeStruct(travel, BF16),
            jax.ShapeDtypeStruct(travel, BF16),
            jax.ShapeDtypeStruct((1, width), F32),
            jax.ShapeDtypeStruct((1, width), F32),
        ],
        compiler_params=pltpu.CompilerParams(vmem_limit_bytes=VMEM_BYTES),
        cost_estimate=SHORT,
        name="shared_backward",
    )(info, *arrays, *rows, *grads, inner)


def plane_turn(plane, planes):
    return ((plane & 1) << 1) | (plane >> 1) if planes == 4 else 0


def finish_kernel(planes, info, scale_ref, *refs):
    step = pl.program_id(0)
    mine, theirs, outs, placed = refs[:4], refs[4:8], refs[8:-1], refs[-1]
    count = mine[0].shape[0]
    width = placed.shape[1]
    half = width // 2
    at = info.shape[0] - 3
    section, core = info[at], info[at + 1]
    turn = plane_turn(info[at + 2], planes)
    turned = turn if count == 1 else jnp.where(section == 1, turn, 0)
    scale = scale_ref[0, 0]
    columns = pl.ds(pl.multiple_of((step ^ turned) * width, width), width)

    def place(which):
        def by_rows():
            for side, pieces in enumerate((mine, theirs)):
                for away, ref in enumerate(pieces):
                    for path in range(2):
                        row = (core ^ side) * half + path * (half // 2)
                        row = row + (section ^ away) * PIECE_ROWS
                        placed[pl.ds(pl.multiple_of(row, 16), PIECE_ROWS), :] = ref[
                            which, path * PIECE_ROWS : (path + 1) * PIECE_ROWS, columns
                        ].astype(F32)

        def by_columns():
            for side, pieces in enumerate((mine, theirs)):
                for away, ref in enumerate(pieces):

                    @pl.when(step == away)
                    def _(side=side, ref=ref):
                        for group in range(4):
                            quarter = half // 4
                            row = (core ^ side) * half + group * quarter
                            placed[pl.ds(pl.multiple_of(row, 16), quarter), :] = ref[
                                which, :, group * width : (group + 1) * width
                            ].astype(F32)

        if count == 1:
            by_rows()
        else:
            pl.when(section != 0)(by_rows)
            pl.when(section == 0)(by_columns)

    place(0)
    if count == 1:

        @pl.when(step < 3)
        def _():
            outs[0][0] = placed[...] / scale

        @pl.when(step == 3)
        def _():
            outs[1][0] = placed[...] / scale

    else:
        outs[0][0] = placed[...] / scale
        place(1)
        outs[1][0] = (placed[...] / scale).T


def finish(info, scale, mine, theirs, planes):
    count, _, hidden = mine[0].shape
    width = hidden // 4
    if count == 1:
        shapes = [(1, width, 3 * width), (1, width, width)]
        maps = [lambda step, info: (0, 0, jnp.minimum(step, 2)), lambda step, info: (0, 0, 0)]
    else:
        shapes = [(1, width, hidden), (1, hidden, width)]
        maps = [lambda step, info: (0, 0, step), lambda step, info: (0, step, 0)]
    return pl.pallas_call(
        partial(finish_kernel, planes),
        grid_spec=pltpu.PrefetchScalarGridSpec(
            num_scalar_prefetch=1,
            grid=(4,),
            in_specs=[IN_SMEM] + [whole_block(mine[0].shape)] * 8,
            out_specs=[pl.BlockSpec((1, width, width), at) for at in maps],
            scratch_shapes=[pltpu.VMEM((width, width), F32)],
        ),
        out_shape=[jax.ShapeDtypeStruct(shape, F32) for shape in shapes],
        compiler_params=pltpu.CompilerParams(vmem_limit_bytes=VMEM_BYTES),
        cost_estimate=SHORT,
        name="finish",
    )(info, scale, *mine, *theirs)


def pack_kernel(count, plan, info, *refs):
    sources, outs, sems = refs[:count], refs[count:-1], refs[-1]
    first = info.shape[0] - 3
    section, core, plane = info[first], info[first + 1], info[first + 2]
    half = outs[0].shape[1]
    for index, (out, choices) in enumerate(zip(outs, plan)):
        for at, at_plane, parts in choices:
            here = section == at
            if at_plane is not None:
                here = here & (plane == at_plane)

            @pl.when(here)
            def _(index=index, out=out, parts=parts):
                for block, part in enumerate(parts):
                    if part[0] == "own":
                        _, which, row, column = part
                        rows = pl.ds(pl.multiple_of(row + core * half, half), half)
                        source = sources[which].at[rows, pl.ds(column, out.shape[2])]
                    else:
                        source = sources[part[1]].at[block]
                    pltpu.make_async_copy(source, out.at[block], sems.at[index, block]).start()

    for index, out in enumerate(outs):
        for block in range(2):
            pltpu.make_async_copy(out.at[block], out.at[block], sems.at[index, block]).wait()


def pack(info, sources, plan, shape):
    return pl.pallas_call(
        partial(pack_kernel, len(sources), plan),
        in_specs=[IN_SMEM] + [ANYWHERE] * len(sources),
        out_specs=[IN_VMEM] * len(plan),
        scratch_shapes=[pltpu.SemaphoreType.DMA((len(plan), 2))],
        out_shape=[jax.ShapeDtypeStruct(shape, BF16)] * len(plan),
        cost_estimate=SHORT,
        name="pack",
    )(info, *sources)


def over_section(value, bits, sources=range(SECTIONS)):
    return lax.ppermute(value, "section", [(at, at ^ bits) for at in sources])


def over_core(value):
    return lax.ppermute(value, "core", [(0, 1), (1, 0)])


def over_plane(value, pairs):
    return lax.ppermute(value, "z", pairs)


def added(left, right):
    return (left.astype(F32) + right.astype(F32)).astype(BF16)


def after(value, *earlier):
    return lax.optimization_barrier((value,) + earlier)[0]


def under(outputs, *arrivals):
    joined = lax.optimization_barrier(tuple(outputs) + arrivals)
    return list(joined[: len(outputs)]), list(joined[len(outputs) :])


def by_section(section, values):
    result, last = None, None
    for at in sorted(values):
        if result is None:
            result = values[at]
        elif values[at] is not last:
            result = jnp.where(section >= at, values[at], result)
        last = values[at]
    return result


def total(*values):
    result = values[0].astype(F32)
    for value in values[1:]:
        result = result + value.astype(F32)
    return result.astype(BF16)


class Sums:
    def __init__(self, travel):
        self.stay, self.move, self.other_stay, self.other_move = travel
        self.size = self.stay.shape[1] // 2

    def cross(self, *earlier):
        if earlier:
            self.other_move = after(self.other_move, *earlier)
            self.other_stay = after(self.other_stay, *earlier)
        self.got_move, self.got_stay = over_core(self.other_move), over_core(self.other_stay)

    def first_sends(self):
        size = self.size
        self.sent = [
            total(self.move[:, at : at + size], self.got_move[:, at : at + size])
            for at in (0, size)
        ]
        return self.sent

    def second_sends(self, from_x, from_y):
        size, half = self.size, self.size // 2
        self.first = from_x, from_y
        to_y = total(self.stay[:, half:size], self.got_stay[:, half:size], from_x[:, half:])
        to_x = total(
            self.stay[:, size + half :], self.got_stay[:, size + half :], from_y[:, half:]
        )
        self.sent = [to_x, to_y]
        return self.sent

    def whole(self, from_x, from_y):
        size, half = self.size, self.size // 2
        parts = []
        for at, first, second in ((0, self.first[0], from_y), (size, self.first[1], from_x)):
            here = slice(at, at + half)
            parts.append(total(self.stay[:, here], self.got_stay[:, here], first[:, :half], second))
        return jnp.concatenate(parts, axis=1)


def over_links(sends):
    return [over_section(sends[0], 1), over_section(sends[1], 2)]


class Planes:
    def __init__(self, value, plane, planes):
        self.value, self.plane, self.planes, self.turn = value, plane, planes, 0

    def sends(self, *earlier):
        value = after(self.value, *earlier) if earlier else self.value
        if self.planes != 4:
            return (value,)
        bits = (1, 2, 2, 1)[self.turn]
        if self.turn < 2:
            bit = (self.plane & 1, self.plane >> 1)[self.turn]
            size = value.shape[-1] // 2
            value = lax.dynamic_slice_in_dim(value, (1 - bit) * size, size, value.ndim - 1)
        return (over_plane(value, [(at, at ^ bits) for at in range(4)]),)

    def take(self, arrived):
        if self.planes != 4:
            self.value = lax.psum(arrived, "z") if self.turn == 3 else arrived
        elif self.turn < 2:
            bit = (self.plane & 1, self.plane >> 1)[self.turn]
            size = self.value.shape[-1] // 2
            keep = lax.dynamic_slice_in_dim(self.value, bit * size, size, self.value.ndim - 1)
            self.value = added(keep, arrived)
        else:
            self.value = jnp.concatenate([self.value, arrived], axis=-1)
        self.turn += 1

    def in_order(self, value):
        if self.planes != 4:
            return value
        size, turn = value.shape[-1] // 4, plane_turn(self.plane, 4)
        parts = [
            lax.dynamic_slice_in_dim(value, (at ^ turn) * size, size, value.ndim - 1)
            for at in range(4)
        ]
        return jnp.concatenate(parts, axis=-1)


class Weights:
    def __init__(self, own, info, planes):
        self.own, self.info = own, info
        self.four = planes == 4
        self.plan = PLAN_FOUR if self.four else PLAN_ANY
        self.half, self.width = own[1].shape[0] // 2, own[1].shape[1]
        self.mine, self.theirs, self.arrived = {}, {}, {}

    def place(self, layer, block):
        if layer in "ac":
            return (0, 0, block * self.width) if block < 3 else (1, 0, 0)
        if layer == "g":
            return (2, 0, block * self.width) if block < 4 else (3, (block - 4) * self.width, 0)
        return (2, 0, block * self.width) if block < 4 else (3, (block - 4) * self.width, 0)

    def choices(self, sends, sources):
        result = []
        for at in range(SECTIONS):
            name = sends.get(at)
            if name is not None and HOMES[name[0]] != at:
                key = self.arrived[at, name]
                if key not in sources:
                    sources[key] = len(self.own) + len(sources)
                result.append((at, None, [("arrived", sources[key])] * 2))
                continue
            for plane in range(4) if name == "F" else (None,):
                piece = ("f" + str(plane)) if name == "F" else name or "a0"
                layer, index = piece[0], int(piece[1])
                if layer in "ac":
                    blocks = ATTEND_BLOCKS[index]
                else:
                    blocks = (index, 4 + index) if layer == "g" else EXPERT_BLOCKS[index]
                parts = [("own",) + self.place(layer, block) for block in blocks]
                result.append((at, plane, parts))
        return result

    def packed(self, wanted):
        sources = {}
        plan = [self.choices(sends, sources) for sends in wanted]
        arrays = list(self.own) + [self.mine[key] for key in sources]
        return pack(self.info, arrays, plan, (2, self.half, self.width))

    def sends(self, step):
        if step == "F":
            return [{at: "F" for at in range(SECTIONS)}]
        return [sends for sends in self.plan[step] if sends]

    def payloads(self, *steps):
        wanted = [sends for step in steps for sends in self.sends(step)]
        return list(self.packed(wanted))

    def move(self, step, payloads):
        links = [(link, sends) for link, sends in enumerate(self.plan[step]) if sends]
        for (link, sends), payload in zip(links, payloads):
            self.mine[step, link] = over_section(payload, link + 1, sorted(sends))
            for at, name in sends.items():
                self.arrived[at ^ (link + 1), name] = (step, link)
        return [(step, link) for link, _ in links]

    def move_planes(self, step):
        up, down = self.mine["plane", step - 1], self.mine["plane", 1 - step]
        up = over_plane(up, [(at, at + 1) for at in range(step - 1, 3)])
        down = over_plane(down, [(at, at - 1) for at in range(4 - step, 0, -1)])
        self.mine["plane", step], self.mine["plane", -step] = up, down
        return [("plane", step), ("plane", -step)]

    def cross(self, keys):
        for key in keys:
            self.theirs[key] = over_core(self.mine[key])
        return keys

    def join(self, outputs, mine=(), theirs=()):
        values = [self.mine[key] for key in mine] + [self.theirs[key] for key in theirs]
        outputs, values = under(outputs, *values)
        for key, value in zip(mine, values):
            self.mine[key] = value
        for key, value in zip(theirs, values[len(mine) :]):
            self.theirs[key] = value
        return outputs

    def layer(self, layer):
        arrays, places = list(self.own), {}

        def place(key):
            if key not in places:
                places[key] = len(arrays)
                arrays.extend([self.mine[key], self.theirs[key]])
            return places[key], places[key] + 1

        if layer in "ac":
            names = [(layer + str(index), ATTEND_BLOCKS[index]) for index in range(2)]
        else:
            names = [(layer + str(index), EXPERT_BLOCKS[index]) for index in range(4)]
        plan = []
        for at in range(SECTIONS):
            if layer == "g":
                names = [("g" + str(at), (0, 1))]
            if HOMES[layer] == at:
                steps = []
                for name, blocks in names:
                    for block in blocks:
                        source = block * 4 if layer == "g" else block
                        steps.append((block, ("own",) + self.place(layer, source)))
                plan.append((at, None, steps))
                continue
            by_plane = layer == "f" and self.four
            for plane in range(4) if by_plane else (None,):
                steps = []
                for index, (name, blocks) in enumerate(names):
                    key = ("plane", plane - index) if by_plane else self.arrived[at, name]
                    for which, block in enumerate(blocks):
                        steps.append((block, ("piece",) + place(key) + (which,)))
                plan.append((at, plane, steps))
        return arrays, plan


def per_device(
    tokens,
    caption_lengths,
    attend_gain,
    attend_shift,
    attend_inputs,
    attend_bias,
    attend_output,
    expert_gain,
    expert_shift,
    expert_inputs,
    expert_inner_bias,
    expert_outputs,
    expert_outer_bias,
    cotangent,
):
    section, core, plane = lax.axis_index("section"), lax.axis_index("core"), lax.axis_index("z")
    planes = lax.axis_size("z")
    items, positions, width = tokens.shape
    hidden = expert_inputs.shape[-1]
    info = [value.reshape(1).astype(jnp.int32) for value in (section, core, plane)]
    info = jnp.concatenate([caption_lengths] + info)
    weights = Weights(
        (attend_inputs[0], attend_output[0], expert_inputs[0], expert_outputs[0]), info, planes
    )

    def to_sections(value):
        return [value] + [over_section(value, bits) for bits in (1, 2, 3)]

    def items_of(part):
        return part.reshape(items, CAP_ROWS, width)

    keys = weights.move(0, weights.payloads(0))
    pad = ((0, 0), (0, ROWS - positions), (0, 0))
    x0 = jnp.pad(tokens, pad)
    last_grad = jnp.pad(cotangent, pad)
    rows = jnp.concatenate(
        [
            attend_gain,
            attend_shift,
            attend_bias,
            expert_gain,
            expert_shift,
            expert_inner_bias,
            expert_outer_bias,
            jnp.full((1, 128), jnp.sum(caption_lengths), F32),
        ],
        axis=1,
    )
    rows = to_sections(rows)
    x0, last_grad, *rows = weights.join([x0, last_grad, *rows], keys)
    keys1 = weights.move(1, weights.payloads(1))
    rows = jnp.concatenate(rows, axis=0)
    language_count = jnp.sum(rows[:, -128:], axis=0, keepdims=True)
    rows = [lax.dynamic_index_in_dim(rows, at ^ section, 0) for at in range(SECTIONS)]
    sizes = [width, width, 3 * width, width, width, hidden, width]
    ends = [sum(sizes[: at + 1]) for at in range(len(sizes))]
    used = [(0, 0), (0, 1), (0, 2), (0, 3), (0, 4), (0, 5), (1, 3), (1, 4), (1, 5), (1, 6)]
    used += [(0, 6), (2, 0), (2, 1), (2, 2), (3, 3), (3, 4), (3, 5), (3, 6)]
    kept = [rows[slot][:, ends[which] - sizes[which] : ends[which]] for slot, which in used]
    language_count, *kept = weights.join([language_count, *kept], keys1)
    kept = dict(zip(used, kept))

    def row(slot, which):
        return kept[slot, which]

    crossed = weights.cross(keys + keys1)
    sends = weights.payloads(2, "F") if weights.four else weights.payloads(2)
    sends, (info, language_count) = under(sends, info, language_count)
    keys = weights.move(2, sends[:2])
    info, language_count = weights.join(
        [info, language_count + over_core(language_count)], theirs=crossed
    )
    plane_keys = []
    if weights.four:
        weights.mine["plane", 0] = sends[2]
        plane_keys = weights.move_planes(1)
    attend0 = weights.layer("a")
    outputs = attend_forward(
        x0, info, attend0, row(0, 0), row(0, 1), row(0, 2), following=(row(0, 3), row(0, 4))
    )
    y0, qkv0, mixed0, caption_rows = weights.join(outputs, keys)
    caption_rows = to_sections(caption_rows.reshape(-1, width))
    sends = weights.payloads(3, 4) if weights.four else weights.payloads(3)
    caption_rows = weights.join(caption_rows, plane_keys)
    sends, caption_rows = under(sends, *caption_rows)
    early_keys = keys
    keys, sends = weights.move(3, sends[:2]), sends[2:]
    crossed = weights.cross(early_keys)
    if weights.four:
        keys += weights.move_planes(2)
    outputs = shared_forward(caption_rows, expert_inputs[0], expert_inner_bias, expert_outputs[0])
    part = weights.join(outputs, keys, crossed)
    (y0,) = weights.join([y0], theirs=weights.cross([(3, 0), (3, 1)]))
    branch = {at: over_section(part[at], at, [0]) for at in range(1, SECTIONS)}
    keys = weights.move_planes(3) if weights.four else []
    expert1 = weights.layer("e")
    outputs = expert_forward(
        y0, info, expert1, row(1, 3), row(1, 4), row(1, 5), row(1, 6), PATCH_ROWS, "patch"
    )
    outputs, moved = under(outputs, *branch.values())
    if weights.four:
        keys += [("plane", step) for step in range(-2, 3)]
    x2, act1, slope1 = weights.join(outputs, keys)
    branch = dict(zip(branch, moved))
    branch[0] = part[0]
    branch = items_of(by_section(section, branch))
    if weights.four:
        crossed = [("plane", step) for step in range(-3, 4)]
    else:
        for step in (4, 5):
            weights.move(step, weights.payloads(step))
        crossed = [(4, 0), (4, 1), (5, 0)]
    weights.cross(crossed)
    attend2 = weights.layer("c") if weights.four else None
    if not weights.four:
        (x2,) = weights.join([x2], theirs=crossed)
        attend2 = weights.layer("c")
    outputs = attend_forward(
        x2, info, attend2, row(2, 0), row(2, 1), row(2, 2), merge=(y0, branch, row(0, 6))
    )
    if weights.four:
        language_count += over_plane(language_count, [(at, at ^ 1) for at in range(4)])
    x3, qkv2, mixed2, x2, language_count = weights.join([*outputs, language_count], theirs=crossed)
    if weights.four:
        language_count += over_plane(language_count, [(at, at ^ 2) for at in range(4)])
    else:
        language_count = lax.psum(language_count, "z")
    expert3 = weights.layer("f")
    outputs = expert_forward(
        x3, info, expert3, row(3, 3), row(3, 4), row(3, 5), row(3, 6), ROWS, "all"
    )
    layer_output, act3, slope3, language_count = under([*outputs, language_count])[0]
    language_count = language_count[0, 0].astype(jnp.int32)
    vision_count = PATCHES * items * SECTIONS * 2 * planes
    counts = jnp.stack(
        [jnp.full((), vision_count, jnp.int32), language_count, language_count + vision_count]
    )

    def small_rows(values):
        flat = jnp.concatenate(values, axis=1)
        count = -(-flat.shape[1] // hidden)
        flat = jnp.pad(flat, ((0, 0), (0, count * hidden - flat.shape[1])))
        return flat.reshape(count, hidden)

    def to_home(sums):
        got = [by_section(section, sums)]
        for bits in (1, 2, 3):
            sends = {at ^ bits: sums[at] for at in sums}
            got.append(over_section(by_section(section, sends), bits, sorted(sends)))
        return got

    keys = []
    if weights.four:
        sends, (layer_output, last_grad) = under(sends, layer_output, last_grad)
        keys = weights.move(4, sends)
    outputs = expert_backward(
        x3, info, expert3, row(3, 3), row(3, 4), act3, slope3, last_grad, ROWS, "all"
    )
    outputs = weights.join(outputs, keys)
    crossed = weights.cross(keys)
    grad3, *small3 = outputs[:5]
    sums3 = Sums(outputs[5:])
    sums3.cross()
    moved = over_links(sums3.first_sends())
    grad3 = after(grad3, *sums3.sent)
    outputs = attend_backward(
        x2, info, attend2, row(2, 0), row(2, 1), qkv2, mixed2, grad3
    )
    outputs, moved = under(outputs, *moved, sums3.got_stay)
    outputs = weights.join(outputs, theirs=crossed)
    grad2, *small2 = outputs[:4]
    sums2, caption_grad = Sums(outputs[4:8]), outputs[8]
    caption_grads = to_sections(caption_grad.reshape(-1, width))
    sums3.got_stay = moved[2]
    moved3 = over_links(sums3.second_sends(*moved[:2]))
    grad2 = after(grad2, *sums3.sent)
    outputs = expert_backward(
        y0, info, expert1, row(1, 3), row(1, 4), act1, slope1, grad2, PATCH_ROWS, "patch"
    )
    outputs, caption_grads = under(outputs, *caption_grads)
    grad1, *small1 = outputs[:5]
    sums2.cross(grad1)
    sums1 = Sums(outputs[5:])
    sums1.cross()
    inner_quarter = lax.dynamic_slice(row(0, 5), (0, section * width), (1, width))
    sum3 = sums3.whole(*moved3)
    inner_quarter = after(inner_quarter, grad1, sum3)
    outputs = shared_backward(
        caption_rows, caption_grads, info, weights.layer("g"), inner_quarter
    )
    parts, (keep0, send0, inner_grad, outer_grad) = outputs[:4], outputs[4:]
    got = [over_section(parts[bits], bits) for bits in (1, 2, 3)]
    sends = [after(value, *parts) for value in sums1.first_sends()]
    moved1 = over_links(sends)
    keep0 = added(keep0, over_core(send0))
    early = lax.psum(jnp.concatenate([sum3, keep0], axis=0), "z")
    sends2 = [after(value, *sends) for value in sums2.first_sends()]
    moved2 = over_links(sends2)
    parts = [parts[0], *got]
    grad1 = after(grad1, keep0, *sends, *sends2)
    outputs = attend_backward(
        x0,
        info,
        attend0,
        row(0, 0),
        row(0, 1),
        qkv0,
        mixed0,
        grad1,
        first=(y0, row(0, 3), parts),
    )
    outputs, moved = under(outputs, *moved2, *moved1)
    moved2, moved1 = moved[:2], moved[2:]
    tokens_grad, *small_first = outputs[:4]
    sums_first, gain_grad, shift_grad = Sums(outputs[4:8]), outputs[8], outputs[9]
    sums_first.cross()
    inner_grad = lax.dynamic_update_slice(
        jnp.zeros((1, hidden), F32), inner_grad, (0, section * width)
    )
    small = small_rows(
        small_first + [gain_grad, shift_grad, inner_grad, outer_grad] + small2 + small1 + small3
    )
    small = added(small, over_core(small))
    to_x, to_y = sums_first.first_sends()
    to_x = jnp.concatenate([to_x[0], small], axis=0)
    sends = lax.optimization_barrier((*sums1.second_sends(*moved1), to_x, to_y))
    moved1, moved = over_links(sends[:2]), over_links(sends[2:])
    sum1, early = lax.optimization_barrier((sums1.whole(*moved1), early))
    planes1 = Planes(sum1, plane, planes)
    size = to_y.shape[1]
    small = added(small, moved[0][size:])
    to_x, to_y = sums_first.second_sends(moved[0][None, :size], moved[1])
    early_x, early_y = sums2.second_sends(*moved2)
    to_x = jnp.concatenate([to_x[0], early_x[0]], axis=0)
    to_y = jnp.concatenate([to_y[0], early_y[0], small], axis=0)
    to_x, to_y = lax.optimization_barrier((to_x, to_y))
    sent1 = planes1.sends()
    moved = lax.optimization_barrier(tuple(over_links((to_x, to_y))))
    size = early_x.shape[1]
    last = sums_first.whole(moved[0][None, :size], moved[1][None, :size])
    sum2 = sums2.whole(moved[0][None, size:], moved[1][None, size : 2 * size])
    small = added(small, moved[1][2 * size :])
    small_count = small.shape[0]
    eighth = last.shape[1]
    last = jnp.concatenate([last[0], sum2[0], small], axis=0)
    planes_last = Planes(last, plane, planes)
    home_early = to_home({0: after(early[2:], *moved), 3: after(early[:2], *moved)})
    planes_last.take(*planes_last.sends())
    planes1.take(*sent1)
    planes1.take(*planes1.sends())
    planes1.take(*planes1.sends())
    planes1.take(*planes1.sends())
    planes_last.take(*planes_last.sends())
    planes_last.take(*planes_last.sends())
    home_late = to_home({1: after(planes1.value, *home_early[1:3])})
    planes_last.take(*planes_last.sends())
    last = planes_last.value
    home_attend = to_home({0: last[None, :eighth], 2: last[None, eighth : 2 * eighth]})
    small = planes_last.in_order(last[2 * eighth :].astype(F32))

    as_float = counts.astype(F32)
    one = jnp.ones((), F32)
    attend_scales = jnp.stack([as_float[2], one, as_float[2], one])
    expert_scales = jnp.stack([as_float[1], as_float[0], one, as_float[2]])

    def placed(pieces, scales, *earlier):
        scale = lax.dynamic_index_in_dim(scales, section, 0).reshape(1, 1)
        theirs = []
        for piece in pieces:
            theirs.append(over_core(after(piece, theirs[-1]) if theirs else piece))
        if earlier:
            scale = after(scale, *earlier)
        return finish(info, scale, pieces, theirs, planes)

    blank = jnp.zeros_like(home_late[0])
    inputs_whole, outputs_whole = placed(
        [
            by_section(section, {0: early, 1: late, 2: blank, 3: early})
            for early, late in zip(home_early, home_late)
        ],
        expert_scales,
    )
    blank = jnp.zeros_like(home_attend[0])
    attend_whole, output_whole = placed(
        [by_section(section, {0: got, 1: blank, 2: got, 3: blank}) for got in home_attend],
        attend_scales,
        inputs_whole,
    )

    attend_size, expert_size = 5 * width, 3 * width + hidden
    cuts = [attend_size, attend_size + expert_size]
    cuts += [cuts[1] + attend_size, cuts[1] + attend_size + expert_size]
    small = jnp.split(small.reshape(-1)[: cuts[3] + expert_size], cuts)
    none_attend, none_expert = jnp.zeros_like(small[0]), jnp.zeros_like(small[1])
    attend_small = jnp.stack([small[0], none_attend, small[2], none_attend])
    expert_small = jnp.stack([small[1], small[3], none_expert, small[4]])
    attend_small = attend_small / attend_scales.reshape(-1, 1)
    expert_small = expert_small / expert_scales.reshape(-1, 1)
    attend_small = lax.dynamic_index_in_dim(attend_small, section, 0)
    expert_small = lax.dynamic_index_in_dim(expert_small, section, 0)
    return (
        layer_output[:, :positions],
        tokens_grad[:, :positions],
        attend_small[:, :width],
        attend_small[:, width : 2 * width],
        attend_whole,
        attend_small[:, 2 * width :],
        output_whole,
        expert_small[:, :width],
        expert_small[:, width : 2 * width],
        inputs_whole,
        expert_small[:, 2 * width : 2 * width + hidden],
        outputs_whole,
        expert_small[:, 2 * width + hidden :],
        counts,
    )


def solution(mesh):
    sections, groups = mesh.shape["section"], mesh.shape["dp"]
    split = Mesh(mesh.devices.reshape(sections, groups // 2, 2), ("section", "z", "core"))
    items = P(("section", "z", "core"), None, None)
    flat = P("section", None)
    matrix = P("section", None, None)
    placed = (
        items,
        P(("section", "z", "core")),
        flat,
        flat,
        matrix,
        flat,
        matrix,
        flat,
        flat,
        matrix,
        flat,
        matrix,
        flat,
        items,
    )
    return jax.shard_map(
        per_device,
        mesh=split,
        in_specs=placed,
        out_specs=(
            items,
            items,
            flat,
            flat,
            matrix,
            flat,
            matrix,
            flat,
            flat,
            matrix,
            flat,
            matrix,
            flat,
            P(),
        ),
        check_vma=False,
    )
```

```python
from functools import partial

import jax
import jax.numpy as jnp
from jax import lax
from jax.experimental import pallas as pl
from jax.experimental.pallas import tpu as pltpu
from jax.sharding import Mesh
from jax.sharding import PartitionSpec as P

HEADS = 12
HEAD_DIM = 64
PATCHES = 197
ROWS = 256
CAP_FIRST, CAP_ROWS = 192, 48
PATCH_ROWS = 208
PAIR = 2 * HEAD_DIM
SECTIONS = 4
PIECE_ROWS = 48
VMEM_BYTES = 58 * 1024 * 1024
F32 = jnp.float32
BF16 = jnp.bfloat16

PLAN_FOUR = (
    ({0: "a0", 1: "e0", 2: "c0", 3: "F"}, {0: "a1", 1: "e2", 2: "c0", 3: "F"}),
    ({0: "a1", 1: "e1", 2: "a1", 3: "e2"}, {0: "a0", 1: "a0", 2: "F", 3: "c0"}),
    ({0: "g3", 1: "e2", 2: "c1"}, {0: "e0", 1: "e3", 2: "c1"}),
    ({0: "g1", 1: "e3", 2: "e0", 3: "e3"}, {0: "e1", 1: "e1", 3: "c1"}),
    ({}, {0: "g2", 1: "g3"}),
)
PLAN_ANY = (
    ({0: "a0", 1: "e0", 2: "c0", 3: "f0"}, {0: "a1", 1: "e2", 2: "c0", 3: "f0"}),
    ({0: "a1", 1: "e1", 2: "a1", 3: "e2"}, {0: "a0", 1: "a0", 2: "c1", 3: "f1"}),
    ({0: "g3", 1: "e2", 2: "c1", 3: "f1"}, {0: "e0", 1: "e3", 2: "f0", 3: "f2"}),
    ({0: "g1", 1: "e3", 2: "e0", 3: "e3"}, {0: "e1", 1: "e1", 2: "f1", 3: "f3"}),
    ({0: "c1", 1: "f2", 3: "f2"}, {0: "g2", 1: "g3", 3: "c0"}),
    ({1: "f3", 3: "f3"}, {}),
)
HOMES = {"a": 0, "c": 2, "e": 1, "f": 3, "F": 3, "g": 0}
ATTEND_BLOCKS = ((0, 1), (2, 3))
EXPERT_BLOCKS = ((0, 1), (4, 5), (2, 3), (6, 7))


def dot_plain(left, right):
    return jnp.dot(left, right, preferred_element_type=F32)


def dot_last(left, right):
    return lax.dot_general(left, right, (((1,), (1,)), ((), ())), preferred_element_type=F32)


def dot_first(left, right):
    return lax.dot_general(left, right, (((0,), (0,)), ((), ())), preferred_element_type=F32)


def column_sum(matrix):
    return jnp.sum(matrix.astype(F32), axis=0, keepdims=True)


def norm_parts(rows):
    centre = rows - jnp.mean(rows, axis=-1, keepdims=True)
    scale = lax.rsqrt(jnp.mean(centre * centre, axis=-1, keepdims=True) + 1e-06)
    return centre * scale, scale


def norm_back(normed_grad, unit, scale, gain):
    unit_grad = normed_grad * gain
    along = jnp.mean(unit_grad * unit, axis=-1, keepdims=True)
    return scale * (unit_grad - jnp.mean(unit_grad, axis=-1, keepdims=True) - unit * along)


def true_positions(length, first, count, axis, kind):
    shape = (count, 1) if axis == 0 else (1, count)
    position = first + lax.broadcasted_iota(jnp.int32, shape, axis)
    patch = position < PATCHES
    if kind == "patch":
        return patch
    caption = (position >= PATCHES) & (position - PATCHES < length)
    return caption if kind == "caption" else patch | caption


def head_masks():
    lane = lax.broadcasted_iota(jnp.int32, (1, PAIR), 1)
    even = (lane < HEAD_DIM).astype(F32).astype(BF16)
    odd = (lane >= HEAD_DIM).astype(F32).astype(BF16)
    return lane < HEAD_DIM, even, odd


def split_pair(pair, even, odd):
    return jnp.concatenate([pair * even, pair * odd], axis=0)


def start_weights(info, first, refs, plan, blocks, sems):
    half = blocks.shape[1] // 2
    section, core, plane = info[first], info[first + 1], info[first + 2]
    for at, at_plane, steps in plan:
        here = section == at
        if at_plane is not None:
            here = here & (plane == at_plane)

        @pl.when(here)
        def _(steps=steps):
            for block, source in steps:
                if source[0] == "own":
                    _, which, row, column = source
                    width = blocks.shape[2]
                    for part in range(2):
                        pltpu.make_async_copy(
                            refs[which].at[
                                pl.ds(row + part * half, half), pl.ds(column, width)
                            ],
                            blocks.at[block, pl.ds(part * half, half)],
                            sems.at[block],
                        ).start()
                else:
                    _, mine, theirs, index = source
                    pltpu.make_async_copy(
                        refs[mine].at[index],
                        blocks.at[block, pl.ds(pl.multiple_of(core * half, half), half)],
                        sems.at[block],
                    ).start()
                    pltpu.make_async_copy(
                        refs[theirs].at[index],
                        blocks.at[block, pl.ds(pl.multiple_of((1 - core) * half, half), half)],
                        sems.at[block],
                    ).start()


def wait_block(blocks, block, sems):
    pltpu.make_async_copy(blocks.at[block], blocks.at[block], sems.at[block]).wait()


def store_turned(target, turned, columns, section, core):
    half = target.shape[0] // 2
    for piece in range(16):
        path, owner = (piece >> 2) & 1, piece & 3
        away = owner ^ section
        place = ((away & 1) << 1) | (away >> 1) if path == 0 else away
        row = ((piece >> 3) ^ core) * half + (place >> 1) * (half // 2)
        row = row + path * (half // 4) + (place & 1) * PIECE_ROWS
        target[pl.ds(pl.multiple_of(row, 16), PIECE_ROWS), columns] = turned[
            piece * PIECE_ROWS : (piece + 1) * PIECE_ROWS
        ]


def put_travel(refs, which, columns, left, right):
    half = left.shape[0] // 2
    for side in range(2):
        rows = dot_plain(left[side * half : (side + 1) * half], right).astype(BF16)
        refs[2 * side][which, :, columns] = rows[: half // 2]
        refs[2 * side + 1][which, :, columns] = rows[half // 2 :]


def attend_forward_kernel(plan, weight_count, merge, info, *refs):
    weights, refs = refs[:weight_count], refs[weight_count:]
    if merge:
        x_ref, before_ref, part_ref, outer_ref, gain_ref, shift_ref, bias_ref = refs[:7]
        y_ref, qkv_ref, mixed_ref, joined_ref, blocks, sems, joined = refs[7:]
    else:
        x_ref, gain_ref, shift_ref, bias_ref, next_gain_ref, next_shift_ref = refs[:6]
        y_ref, qkv_ref, mixed_ref, caption_ref, blocks, sems = refs[6:]
    item = pl.program_id(0)
    items = pl.num_programs(0)
    length = info[item]
    width = x_ref.shape[-1]

    @pl.when(item == 0)
    def _():
        start_weights(info, items, weights, plan, blocks, sems)

    cap = slice(CAP_FIRST, CAP_FIRST + CAP_ROWS)
    if merge:
        joined[...] = x_ref[0].astype(F32)
        branch = part_ref[0].astype(F32) + outer_ref[...]
        is_true = true_positions(length, CAP_FIRST, CAP_ROWS, 0, "caption")
        captions = before_ref[0, cap] + jnp.where(is_true, branch, 0.0)
        position = CAP_FIRST + lax.broadcasted_iota(jnp.int32, (CAP_ROWS, 1), 0)
        captions = captions.astype(BF16).astype(F32)
        joined[cap] = jnp.where(position < PATCHES, joined[cap], captions)
        x = joined[...]
        joined_ref[0] = x.astype(BF16)
    else:
        x = x_ref[0].astype(F32)
    unit, _ = norm_parts(x)
    normed = (unit * gain_ref[...] + shift_ref[...]).astype(BF16)

    @pl.when(item == 0)
    def _():
        for block in range(4):
            wait_block(blocks, block, sems)

    queries = dot_plain(normed, blocks[0]) + bias_ref[:, :width]
    qkv_ref[0, :, :width] = (queries * HEAD_DIM ** (-0.5)).astype(BF16)
    qkv_ref[0, :, width : 2 * width] = dot_plain(normed, blocks[1]).astype(BF16)
    values = dot_plain(normed, blocks[2]) + bias_ref[:, width : 2 * width]
    qkv_ref[0, :, 2 * width :] = values.astype(BF16)
    key_true = true_positions(length, 0, ROWS, 1, "all")
    low_half, even, odd = head_masks()
    ones = jnp.ones((ROWS, PAIR), BF16)

    def scores_of(pair):
        at = pair * PAIR
        q2 = qkv_ref[0, :, at : at + PAIR]
        k2 = qkv_ref[0, :, width + at : width + at + PAIR]
        return dot_last(split_pair(q2, even, odd), k2)

    ahead = [scores_of(0), scores_of(1)]
    for pair in range(HEADS // 2):
        at = pair * PAIR
        scores = jnp.where(key_true, ahead.pop(0), -1e9)
        if pair + 2 < HEADS // 2:
            ahead.append(scores_of(pair + 2))
        weight = jnp.exp(scores - jnp.max(scores, axis=-1, keepdims=True)).astype(BF16)
        v2 = qkv_ref[0, :, 2 * width + at : 2 * width + at + PAIR]
        summed = dot_plain(weight, jnp.concatenate([v2, ones], axis=1))
        top = jnp.where(low_half, summed[:ROWS, :PAIR], summed[ROWS:, :PAIR])
        below = jnp.where(low_half, summed[:ROWS, PAIR:], summed[ROWS:, PAIR:])
        mixed_ref[0, :, at : at + PAIR] = (top / below).astype(BF16)
    branch = dot_plain(mixed_ref[0], blocks[3]) + bias_ref[:, 2 * width :]
    row_true = true_positions(length, 0, ROWS, 0, "all")
    y = x + jnp.where(row_true, branch, 0.0)
    y_ref[0] = y.astype(y_ref.dtype)
    if not merge:
        unit, _ = norm_parts(y[cap])
        caption_ref[0] = (unit * next_gain_ref[...] + next_shift_ref[...]).astype(BF16)


def attend_backward_kernel(plan, weight_count, first, info, *refs):
    weights, refs = refs[:weight_count], refs[weight_count:]
    x_ref, gain_ref, shift_ref, qkv_ref, mixed_ref, grad_ref = refs[:6]
    if first:
        after_ref, next_gain_ref, *parts = refs[6:12]
        refs = refs[12:]
    else:
        refs = refs[6:]
    out_ref, gain_grad_ref, shift_grad_ref, bias_grad_ref = refs[:4]
    travel_refs = refs[4:8]
    if first:
        next_gain_grad_ref, next_shift_grad_ref, joined = refs[8], refs[9], refs[-1]
    else:
        caption_ref = refs[8]
    blocks, sems, normed_turned, mixed_turned, branch_all, projected, mixed_grad = refs[
        10 if first else 9 :
    ][:7]
    item = pl.program_id(0)
    items = pl.num_programs(0)
    length = info[item]
    section, core = info[items], info[items + 1]
    width = x_ref.shape[-1]
    here = pl.ds(pl.multiple_of(item * ROWS, ROWS), ROWS)
    cap = slice(CAP_FIRST, CAP_FIRST + CAP_ROWS)

    @pl.when(item == 0)
    def _():
        start_weights(info, items, weights, plan, blocks, sems)

    def add_to(ref, part):
        @pl.when(item == 0)
        def _():
            ref[...] = part

        @pl.when(item > 0)
        def _():
            ref[...] += part

    x = x_ref[0].astype(F32)
    unit, scale = norm_parts(x)
    normed = (unit * gain_ref[...] + shift_ref[...]).astype(BF16)
    incoming = grad_ref[0].astype(F32)
    if first:
        after_unit, after_scale = norm_parts(after_ref[0, cap])
        caption_grad = parts[0][...].astype(F32)
        for part in parts[1:]:
            caption_grad = caption_grad + part[...].astype(F32)
        joined[...] = incoming
        joined[cap] += norm_back(caption_grad, after_unit, after_scale, next_gain_ref[...])
        incoming = joined[...]
        add_to(next_gain_grad_ref, jnp.sum(caption_grad * after_unit, axis=0, keepdims=True))
        add_to(next_shift_grad_ref, jnp.sum(caption_grad, axis=0, keepdims=True))
    row_true = true_positions(length, 0, ROWS, 0, "all")
    branch = jnp.where(row_true, incoming, 0.0).astype(BF16)
    branch_all[here, :] = branch
    store_turned(normed_turned, normed.T, here, section, core)
    store_turned(mixed_turned, mixed_ref[0].T, here, section, core)

    @pl.when(item == 0)
    def _():
        for block in range(4):
            wait_block(blocks, block, sems)

    mixed_grad[...] = dot_last(branch, blocks[3]).astype(BF16)
    key_true = true_positions(length, 0, ROWS, 0, "all")
    _, even, odd = head_masks()

    def products_of(pair):
        at = pair * PAIR
        q2 = split_pair(qkv_ref[0, :, at : at + PAIR], even, odd)
        k2 = qkv_ref[0, :, width + at : width + at + PAIR]
        v2 = qkv_ref[0, :, 2 * width + at : 2 * width + at + PAIR]
        g2 = split_pair(mixed_grad[:, at : at + PAIR], even, odd)
        return q2, k2, g2, dot_last(k2, q2), dot_last(v2, g2)

    ahead = [products_of(0)]
    for pair in range(HEADS // 2):
        at = pair * PAIR
        q2, k2, g2, scores, weight_grad = ahead.pop(0)
        if pair + 1 < HEADS // 2:
            ahead.append(products_of(pair + 1))
        scores = jnp.where(key_true, scores, -1e9)
        weight = jnp.exp(scores - jnp.max(scores, axis=0, keepdims=True))
        weight = weight * (1.0 / jnp.sum(weight, axis=0, keepdims=True))
        product = weight * weight_grad
        along = jnp.sum(product, axis=0, keepdims=True)
        score_grad = (product - weight * along).astype(BF16)
        values_grad = dot_plain(weight.astype(BF16), g2).astype(BF16)
        keys_grad = dot_plain(score_grad, q2).astype(BF16)
        k2_split = split_pair(k2, even, odd)
        stacked = jnp.concatenate([score_grad[:, :ROWS], score_grad[:, ROWS:]], axis=0)
        queries_grad = dot_first(stacked, k2_split).astype(BF16)
        queries_grad = (queries_grad.astype(F32) * HEAD_DIM ** (-0.5)).astype(BF16)
        projected[here, at : at + PAIR] = queries_grad
        projected[here, width + at : width + at + PAIR] = keys_grad
        projected[here, 2 * width + at : 2 * width + at + PAIR] = values_grad
    normed_grad = dot_last(projected[here, :width], blocks[0])
    normed_grad += dot_last(projected[here, width : 2 * width], blocks[1])
    normed_grad += dot_last(projected[here, 2 * width :], blocks[2])
    out = (incoming + norm_back(normed_grad, unit, scale, gain_ref[...])).astype(BF16)
    out_ref[0] = out
    if not first:
        is_true = true_positions(length, CAP_FIRST, CAP_ROWS, 0, "caption")
        caption_ref[0] = jnp.where(is_true, out[cap].astype(F32), 0.0).astype(BF16)
    add_to(gain_grad_ref, jnp.sum(normed_grad * unit, axis=0, keepdims=True))
    add_to(shift_grad_ref, jnp.sum(normed_grad, axis=0, keepdims=True))

    @pl.when(item == items - 1)
    def _():
        for block in range(4):
            columns = slice(block * width, (block + 1) * width)
            left = normed_turned if block < 3 else mixed_turned
            right = projected[:, columns] if block < 3 else branch_all[...]
            put_travel(travel_refs, 0, columns, left, right)
        bias_grad_ref[:, :width] = column_sum(projected[:, :width])
        bias_grad_ref[:, width : 2 * width] = column_sum(projected[:, 2 * width :])
        bias_grad_ref[:, 2 * width :] = column_sum(branch_all[...])


SHORT = pl.CostEstimate(flops=0, bytes_accessed=100_000, transcendentals=0)
LONG = pl.CostEstimate(flops=30_000_000_000, bytes_accessed=30_000_000, transcendentals=0)
ANYWHERE = pl.BlockSpec(memory_space=pl.ANY)


def whole_block(shape):
    return pl.BlockSpec(shape, lambda step, info: (0,) * len(shape))


def item_block(shape):
    return pl.BlockSpec((1,) + shape[1:], lambda step, info: (step,) + (0,) * (len(shape) - 1))


def blocks_scratch(count, width):
    return [pltpu.VMEM((count, width, width), BF16), pltpu.SemaphoreType.DMA((count,))]


def attend_forward(x, info, weights, gain, shift, bias, merge=None, following=None):
    arrays, plan = weights
    items, _, width = x.shape
    row = whole_block((1, width))
    bias_row = whole_block((1, 3 * width))
    caption_shape = (items, CAP_ROWS, width)
    if merge is not None:
        before, part, outer = merge
        operands = (x, before, part, outer, gain, shift, bias)
        specs = [item_block(x.shape), item_block(x.shape), item_block(caption_shape)]
        specs += [row, row, row, bias_row]
        last_shape, kind, scratch = x.shape, BF16, [pltpu.VMEM((ROWS, width), F32)]
    else:
        operands = (x, gain, shift, bias, *following)
        specs = [item_block(x.shape), row, row, bias_row, row, row]
        last_shape, kind, scratch = caption_shape, F32, []
    return pl.pallas_call(
        partial(attend_forward_kernel, plan, len(arrays), merge is not None),
        grid_spec=pltpu.PrefetchScalarGridSpec(
            num_scalar_prefetch=1,
            grid=(items,),
            in_specs=[ANYWHERE] * len(arrays) + specs,
            out_specs=[
                item_block(x.shape),
                item_block((items, ROWS, 3 * width)),
                item_block((items, ROWS, width)),
                item_block(last_shape),
            ],
            scratch_shapes=blocks_scratch(4, width) + scratch,
        ),
        out_shape=[
            jax.ShapeDtypeStruct(x.shape, kind),
            jax.ShapeDtypeStruct((items, ROWS, 3 * width), BF16),
            jax.ShapeDtypeStruct((items, ROWS, width), BF16),
            jax.ShapeDtypeStruct(last_shape, BF16),
        ],
        compiler_params=pltpu.CompilerParams(vmem_limit_bytes=VMEM_BYTES),
        cost_estimate=SHORT,
        name="attend_forward",
    )(info, *arrays, *operands)


def attend_backward(x, info, weights, gain, shift, qkv, mixed, incoming, first=None):
    arrays, plan = weights
    items, _, width = x.shape
    half = width // 2
    row = whole_block((1, width))
    caption_shape = (items, CAP_ROWS, width)
    operands = (x, gain, shift, qkv, mixed, incoming)
    specs = [item_block(x.shape), row, row, item_block(qkv.shape), item_block(mixed.shape)]
    specs += [item_block(incoming.shape)]
    outs = [
        (item_block(x.shape), x.shape, BF16),
        (row, (1, width), F32),
        (row, (1, width), F32),
        (whole_block((1, 3 * width)), (1, 3 * width), F32),
    ]
    outs += [(whole_block((1, half // 2, 4 * width)), (1, half // 2, 4 * width), BF16)] * 4
    scratch = []
    if first is not None:
        after, next_gain, parts = first
        operands += (after, next_gain, *parts)
        caption_rows = pl.BlockSpec((CAP_ROWS, width), lambda step, info: (step, 0))
        specs += [item_block(after.shape), row] + [caption_rows] * 4
        outs += [(row, (1, width), F32)] * 2
        scratch = [pltpu.VMEM((ROWS, width), F32)]
    else:
        outs += [(item_block(caption_shape), caption_shape, BF16)]
    return pl.pallas_call(
        partial(attend_backward_kernel, plan, len(arrays), first is not None),
        grid_spec=pltpu.PrefetchScalarGridSpec(
            num_scalar_prefetch=1,
            grid=(items,),
            in_specs=[ANYWHERE] * len(arrays) + specs,
            out_specs=[spec for spec, _, _ in outs],
            scratch_shapes=blocks_scratch(4, width)
            + [
                pltpu.VMEM((width, items * ROWS), BF16),
                pltpu.VMEM((width, items * ROWS), BF16),
                pltpu.VMEM((items * ROWS, width), BF16),
                pltpu.VMEM((items * ROWS, 3 * width), BF16),
                pltpu.VMEM((ROWS, width), BF16),
            ]
            + scratch,
        ),
        out_shape=[jax.ShapeDtypeStruct(shape, kind) for _, shape, kind in outs],
        compiler_params=pltpu.CompilerParams(vmem_limit_bytes=VMEM_BYTES),
        cost_estimate=LONG,
        name="attend_backward",
    )(info, *arrays, *operands)


def normal_parts(u):
    t = pl.reciprocal(1.0 + 0.23164190 * jnp.abs(u), approx=True)
    bell = jnp.exp2((u * -0.7213475204444817) * u)
    poly = t * (
        0.127414796
        + t * (-0.142248368 + t * (0.7107068705 + t * (-0.7265760135 + t * 0.5307027145)))
    )
    tail = poly * bell
    return jnp.where(u < 0, tail, 1.0 - tail), bell


def inner_forward(normed, matrix, bias):
    inner = dot_plain(normed, matrix) + bias
    cumulative, bell = normal_parts(inner)
    slope = cumulative + (inner * 0.3989422804014327) * bell
    return (inner * cumulative).astype(BF16), slope.astype(BF16)


def expert_forward_kernel(plan, weight_count, count, kind, info, *refs):
    weights, refs = refs[:weight_count], refs[weight_count:]
    x_ref, gain_ref, shift_ref, inner_ref, outer_ref = refs[:5]
    y_ref, act_ref, slope_ref, blocks, sems, normed, total = refs[5:]
    step = pl.program_id(0)
    items, _, width = x_ref.shape

    @pl.when(step == 0)
    def _():
        start_weights(info, items, weights, plan, blocks, sems)
        for item in range(items):
            x = x_ref[item, :count].astype(BF16).astype(F32)
            unit, _ = norm_parts(x)
            normed[item * count : (item + 1) * count] = (
                unit * gain_ref[...] + shift_ref[...]
            ).astype(BF16)

    wait_block(blocks, step, sems)
    wait_block(blocks, step + 4, sems)
    for at in range(0, width, 256):
        columns = slice(at, at + 256)
        act, slope = inner_forward(normed[...], blocks[step, :, columns], inner_ref[:, columns])
        act_ref[:, columns] = act
        slope_ref[:, columns] = slope
    part = dot_plain(act_ref[...], blocks[step + 4])

    @pl.when(step == 0)
    def _():
        total[...] = part

    @pl.when(step > 0)
    def _():
        total[...] += part

    @pl.when(step == pl.num_programs(0) - 1)
    def _():
        for item in range(items):
            row_true = true_positions(info[item], 0, count, 0, kind)
            branch = total[item * count : (item + 1) * count] + outer_ref[...]
            x = x_ref[item, :count].astype(BF16).astype(F32)
            y_ref[item, :count] = (x + jnp.where(row_true, branch, 0.0)).astype(BF16)
            if count < ROWS:
                y_ref[item, count:] = jnp.zeros((ROWS - count, width), BF16)


def expert_backward_kernel(plan, weight_count, count, kind, info, *refs):
    weights, refs = refs[:weight_count], refs[weight_count:]
    x_ref, gain_ref, shift_ref, act_ref, slope_ref, grad_ref = refs[:6]
    out_ref, gain_grad_ref, shift_grad_ref, inner_grad_ref, outer_grad_ref = refs[6:11]
    travel_refs = refs[11:15]
    blocks, sems, normed_turned, branch_turned, branch, inner_all, total = refs[15:]
    step = pl.program_id(0)
    items, _, width = x_ref.shape
    section, core = info[items], info[items + 1]

    @pl.when(step == 0)
    def _():
        start_weights(info, items, weights, plan, blocks, sems)
        outer = None
        for item in range(items):
            here = slice(item * count, (item + 1) * count)
            unit, _ = norm_parts(x_ref[item, :count].astype(BF16).astype(F32))
            normed = (unit * gain_ref[...] + shift_ref[...]).astype(BF16)
            row_true = true_positions(info[item], 0, count, 0, kind)
            incoming = grad_ref[item, :count].astype(F32)
            masked = jnp.where(row_true, incoming, 0.0).astype(BF16)
            branch[here] = masked
            store_turned(normed_turned, normed.T, here, section, core)
            store_turned(branch_turned, masked.T, here, section, core)
            term = column_sum(masked)
            outer = term if outer is None else outer + term
        outer_grad_ref[...] = outer

    wait_block(blocks, step, sems)
    wait_block(blocks, step + 4, sems)
    for at in range(0, width, 256):
        columns = slice(at, at + 256)
        act_grad = dot_last(branch[...], blocks[step + 4, columns])
        inner = (slope_ref[:, columns].astype(F32) * act_grad).astype(BF16)
        inner_all[:, columns] = inner
        inner_grad_ref[:, columns] = column_sum(inner)
        put_travel(travel_refs, 0, columns, normed_turned, inner)
        put_travel(travel_refs, 1, columns, branch_turned, act_ref[:, columns])
    part = dot_last(inner_all[...], blocks[step])

    @pl.when(step == 0)
    def _():
        total[...] = part

    @pl.when(step > 0)
    def _():
        total[...] += part

    @pl.when(step == pl.num_programs(0) - 1)
    def _():
        gain_sum, shift_sum = None, None
        for item in range(items):
            unit, scale = norm_parts(x_ref[item, :count].astype(BF16).astype(F32))
            normed_grad = total[item * count : (item + 1) * count]
            gain_part = jnp.sum(normed_grad * unit, axis=0, keepdims=True)
            shift_part = jnp.sum(normed_grad, axis=0, keepdims=True)
            gain_sum = gain_part if gain_sum is None else gain_sum + gain_part
            shift_sum = shift_part if shift_sum is None else shift_sum + shift_part
            incoming = grad_ref[item, :count].astype(F32)
            hidden = incoming + norm_back(normed_grad, unit, scale, gain_ref[...])
            out_ref[item, :count] = hidden.astype(BF16)
            if count < ROWS:
                out_ref[item, count:] = grad_ref[item, count:]
        gain_grad_ref[...] = gain_sum
        shift_grad_ref[...] = shift_sum


def shared_forward_kernel(*refs):
    *rows_refs, inputs_ref, inner_ref, outputs_ref = refs[:7]
    *part_refs, normed, total = refs[7:]
    count = rows_refs[0].shape[0]
    step = pl.program_id(0)

    @pl.when(step == 0)
    def _():
        for index, ref in enumerate(rows_refs):
            normed[index * count : (index + 1) * count] = ref[...]
        total[...] = jnp.zeros_like(total)

    act, _ = inner_forward(normed[...], inputs_ref[...], inner_ref[...])
    total[...] += dot_plain(act, outputs_ref[...])

    @pl.when(step == pl.num_programs(0) - 1)
    def _():
        for index, ref in enumerate(part_refs):
            ref[...] = total[index * count : (index + 1) * count].astype(BF16)


def shared_backward_kernel(plan, weight_count, info, *refs):
    weights, refs = refs[:weight_count], refs[weight_count:]
    rows_refs, grad_refs, inner_ref = refs[:4], refs[4:8], refs[8]
    part_refs, (keep_ref, send_ref, inner_grad_ref, outer_grad_ref) = refs[9:13], refs[13:17]
    blocks, sems, normed, branch, matrix = refs[17:]
    count, width = rows_refs[0].shape
    half = width // 2
    first = info.shape[0] - 3
    core = info[first + 1]
    start_weights(info, first, weights, plan, blocks, sems)
    for index in range(SECTIONS):
        here = slice(index * count, (index + 1) * count)
        normed[here] = rows_refs[index][...]
        branch[here] = grad_refs[index][...]
    outer_grad_ref[...] = column_sum(grad_refs[0][...])
    wait_block(blocks, 0, sems)
    wait_block(blocks, 1, sems)
    part = None
    for at in range(0, width, 256):
        columns = slice(at, at + 256)
        act, slope = inner_forward(normed[...], blocks[0, :, columns], inner_ref[:, columns])
        act_grad = dot_last(branch[...], blocks[1, columns])
        inner = (slope.astype(F32) * act_grad).astype(BF16)
        inner_grad_ref[:, columns] = column_sum(inner)
        matrix[0, :, columns] = dot_first(normed[...], inner).astype(BF16)
        matrix[1, :, columns] = dot_first(branch[...], act).astype(BF16)
        term = dot_last(inner, blocks[0, :, columns])
        part = term if part is None else part + term
    for index, ref in enumerate(part_refs):
        ref[...] = part[index * count : (index + 1) * count].astype(BF16)
    quarter = half // 4
    for which in range(2):
        for group in range(4):
            columns = slice(group * width, (group + 1) * width)
            mine = pl.multiple_of(core * half, 16) + group * quarter
            other = pl.multiple_of((1 - core) * half, 16) + group * quarter
            keep_ref[which, :, columns] = matrix[which, pl.ds(pl.multiple_of(mine, 16), quarter)]
            send_ref[which, :, columns] = matrix[which, pl.ds(pl.multiple_of(other, 16), quarter)]


def chunk_columns(rows, width):
    return pl.BlockSpec((rows, width), lambda step, info: (0, step))


def expert_forward(x, info, weights, gain, shift, inner, outer, count, kind):
    arrays, plan = weights
    items, _, width = x.shape
    hidden = inner.shape[1]
    row = whole_block((1, width))
    return pl.pallas_call(
        partial(expert_forward_kernel, plan, len(arrays), count, kind),
        grid_spec=pltpu.PrefetchScalarGridSpec(
            num_scalar_prefetch=1,
            grid=(hidden // width,),
            in_specs=[ANYWHERE] * len(arrays)
            + [whole_block(x.shape), row, row, chunk_columns(1, width), row],
            out_specs=[
                whole_block((items, ROWS, width)),
                chunk_columns(items * count, width),
                chunk_columns(items * count, width),
            ],
            scratch_shapes=blocks_scratch(8, width)
            + [
                pltpu.VMEM((items * count, width), BF16),
                pltpu.VMEM((items * count, width), F32),
            ],
        ),
        out_shape=[
            jax.ShapeDtypeStruct((items, ROWS, width), BF16),
            jax.ShapeDtypeStruct((items * count, hidden), BF16),
            jax.ShapeDtypeStruct((items * count, hidden), BF16),
        ],
        compiler_params=pltpu.CompilerParams(vmem_limit_bytes=VMEM_BYTES),
        cost_estimate=SHORT,
        name="expert_forward_" + kind,
    )(info, *arrays, x, gain, shift, inner, outer)


def expert_backward(x, info, weights, gain, shift, act, slope, incoming, count, kind):
    arrays, plan = weights
    items, _, width = x.shape
    half = width // 2
    hidden = act.shape[1]
    row = whole_block((1, width))
    travel = pl.BlockSpec((2, half // 2, width), lambda step, info: (0, 0, step))
    return pl.pallas_call(
        partial(expert_backward_kernel, plan, len(arrays), count, kind),
        grid_spec=pltpu.PrefetchScalarGridSpec(
            num_scalar_prefetch=1,
            grid=(hidden // width,),
            in_specs=[ANYWHERE] * len(arrays)
            + [
                whole_block(x.shape),
                row,
                row,
                chunk_columns(items * count, width),
                chunk_columns(items * count, width),
                whole_block(incoming.shape),
            ],
            out_specs=[whole_block(incoming.shape), row, row, chunk_columns(1, width), row]
            + [travel] * 4,
            scratch_shapes=blocks_scratch(8, width)
            + [
                pltpu.VMEM((width, items * count), BF16),
                pltpu.VMEM((width, items * count), BF16),
                pltpu.VMEM((items * count, width), BF16),
                pltpu.VMEM((items * count, width), BF16),
                pltpu.VMEM((items * count, width), F32),
            ],
        ),
        out_shape=[
            jax.ShapeDtypeStruct(incoming.shape, BF16),
            jax.ShapeDtypeStruct((1, width), F32),
            jax.ShapeDtypeStruct((1, width), F32),
            jax.ShapeDtypeStruct((1, hidden), F32),
            jax.ShapeDtypeStruct((1, width), F32),
        ]
        + [jax.ShapeDtypeStruct((2, half // 2, hidden), BF16)] * 4,
        compiler_params=pltpu.CompilerParams(vmem_limit_bytes=VMEM_BYTES),
        cost_estimate=SHORT,
        name="expert_backward_" + kind,
    )(info, *arrays, x, gain, shift, act, slope, incoming)


IN_VMEM = pl.BlockSpec(memory_space=pltpu.VMEM)
IN_SMEM = pl.BlockSpec(memory_space=pltpu.SMEM)


def shared_forward(rows, inputs, inner, outputs):
    count, width = rows[0].shape
    total = SECTIONS * count
    hidden = inner.shape[1]
    return pl.pallas_call(
        shared_forward_kernel,
        grid=(hidden // width,),
        in_specs=[pl.BlockSpec(rows[0].shape, lambda step: (0, 0))] * 4
        + [
            pl.BlockSpec((width, width), lambda step: (0, step)),
            pl.BlockSpec((1, width), lambda step: (0, step)),
            pl.BlockSpec((width, width), lambda step: (step, 0)),
        ],
        out_specs=[pl.BlockSpec((count, width), lambda step: (0, 0))] * SECTIONS,
        scratch_shapes=[pltpu.VMEM((total, width), BF16), pltpu.VMEM((total, width), F32)],
        out_shape=[jax.ShapeDtypeStruct((count, width), BF16)] * SECTIONS,
        compiler_params=pltpu.CompilerParams(vmem_limit_bytes=VMEM_BYTES),
        cost_estimate=SHORT,
        name="shared_forward",
    )(*rows, inputs, inner, outputs)


def shared_backward(rows, grads, info, weights, inner):
    arrays, plan = weights
    count, width = rows[0].shape
    total = SECTIONS * count
    travel = (2, width // 8, 4 * width)
    return pl.pallas_call(
        partial(shared_backward_kernel, plan, len(arrays)),
        in_specs=[IN_SMEM] + [ANYWHERE] * len(arrays) + [IN_VMEM] * 9,
        out_specs=[IN_VMEM] * 8,
        scratch_shapes=blocks_scratch(2, width)
        + [
            pltpu.VMEM((total, width), BF16),
            pltpu.VMEM((total, width), BF16),
            pltpu.VMEM((2, width, width), BF16),
        ],
        out_shape=[
            *[jax.ShapeDtypeStruct((count, width), BF16)] * SECTIONS,
            jax.ShapeDtypeStruct(travel, BF16),
            jax.ShapeDtypeStruct(travel, BF16),
            jax.ShapeDtypeStruct((1, width), F32),
            jax.ShapeDtypeStruct((1, width), F32),
        ],
        compiler_params=pltpu.CompilerParams(vmem_limit_bytes=VMEM_BYTES),
        cost_estimate=SHORT,
        name="shared_backward",
    )(info, *arrays, *rows, *grads, inner)


def plane_turn(plane, planes):
    return ((plane & 1) << 1) | (plane >> 1) if planes == 4 else 0


def finish_kernel(planes, info, scale_ref, *refs):
    step = pl.program_id(0)
    mine, theirs, outs, placed = refs[:4], refs[4:8], refs[8:-1], refs[-1]
    count = mine[0].shape[0]
    width = placed.shape[1]
    half = width // 2
    at = info.shape[0] - 3
    section, core = info[at], info[at + 1]
    turn = plane_turn(info[at + 2], planes)
    turned = turn if count == 1 else jnp.where(section == 1, turn, 0)
    scale = scale_ref[0, 0]
    columns = pl.ds(pl.multiple_of((step ^ turned) * width, width), width)

    def place(which):
        def by_rows():
            for side, pieces in enumerate((mine, theirs)):
                for away, ref in enumerate(pieces):
                    for path in range(2):
                        row = (core ^ side) * half + path * (half // 2)
                        row = row + (section ^ away) * PIECE_ROWS
                        placed[pl.ds(pl.multiple_of(row, 16), PIECE_ROWS), :] = ref[
                            which, path * PIECE_ROWS : (path + 1) * PIECE_ROWS, columns
                        ].astype(F32)

        def by_columns():
            for side, pieces in enumerate((mine, theirs)):
                for away, ref in enumerate(pieces):

                    @pl.when(step == away)
                    def _(side=side, ref=ref):
                        for group in range(4):
                            quarter = half // 4
                            row = (core ^ side) * half + group * quarter
                            placed[pl.ds(pl.multiple_of(row, 16), quarter), :] = ref[
                                which, :, group * width : (group + 1) * width
                            ].astype(F32)

        if count == 1:
            by_rows()
        else:
            pl.when(section != 0)(by_rows)
            pl.when(section == 0)(by_columns)

    place(0)
    if count == 1:

        @pl.when(step < 3)
        def _():
            outs[0][0] = placed[...] / scale

        @pl.when(step == 3)
        def _():
            outs[1][0] = placed[...] / scale

    else:
        outs[0][0] = placed[...] / scale
        place(1)
        outs[1][0] = (placed[...] / scale).T


def finish(info, scale, mine, theirs, planes):
    count, _, hidden = mine[0].shape
    width = hidden // 4
    if count == 1:
        shapes = [(1, width, 3 * width), (1, width, width)]
        maps = [lambda step, info: (0, 0, jnp.minimum(step, 2)), lambda step, info: (0, 0, 0)]
    else:
        shapes = [(1, width, hidden), (1, hidden, width)]
        maps = [lambda step, info: (0, 0, step), lambda step, info: (0, step, 0)]
    return pl.pallas_call(
        partial(finish_kernel, planes),
        grid_spec=pltpu.PrefetchScalarGridSpec(
            num_scalar_prefetch=1,
            grid=(4,),
            in_specs=[IN_SMEM] + [whole_block(mine[0].shape)] * 8,
            out_specs=[pl.BlockSpec((1, width, width), at) for at in maps],
            scratch_shapes=[pltpu.VMEM((width, width), F32)],
        ),
        out_shape=[jax.ShapeDtypeStruct(shape, F32) for shape in shapes],
        compiler_params=pltpu.CompilerParams(vmem_limit_bytes=VMEM_BYTES),
        cost_estimate=SHORT,
        name="finish",
    )(info, scale, *mine, *theirs)


def pack_kernel(count, plan, info, *refs):
    sources, outs, sems = refs[:count], refs[count:-1], refs[-1]
    first = info.shape[0] - 3
    section, core, plane = info[first], info[first + 1], info[first + 2]
    half = outs[0].shape[1]
    for index, (out, choices) in enumerate(zip(outs, plan)):
        for at, at_plane, parts in choices:
            here = section == at
            if at_plane is not None:
                here = here & (plane == at_plane)

            @pl.when(here)
            def _(index=index, out=out, parts=parts):
                for block, part in enumerate(parts):
                    if part[0] == "own":
                        _, which, row, column = part
                        rows = pl.ds(pl.multiple_of(row + core * half, half), half)
                        source = sources[which].at[rows, pl.ds(column, out.shape[2])]
                    else:
                        source = sources[part[1]].at[block]
                    pltpu.make_async_copy(source, out.at[block], sems.at[index, block]).start()

    for index, out in enumerate(outs):
        for block in range(2):
            pltpu.make_async_copy(out.at[block], out.at[block], sems.at[index, block]).wait()


def pack(info, sources, plan, shape):
    return pl.pallas_call(
        partial(pack_kernel, len(sources), plan),
        in_specs=[IN_SMEM] + [ANYWHERE] * len(sources),
        out_specs=[IN_VMEM] * len(plan),
        scratch_shapes=[pltpu.SemaphoreType.DMA((len(plan), 2))],
        out_shape=[jax.ShapeDtypeStruct(shape, BF16)] * len(plan),
        cost_estimate=SHORT,
        name="pack",
    )(info, *sources)


def over_section(value, bits, sources=range(SECTIONS)):
    return lax.ppermute(value, "section", [(at, at ^ bits) for at in sources])


def over_core(value):
    return lax.ppermute(value, "core", [(0, 1), (1, 0)])


def over_plane(value, pairs):
    return lax.ppermute(value, "z", pairs)


def added(left, right):
    return (left.astype(F32) + right.astype(F32)).astype(BF16)


def after(value, *earlier):
    return lax.optimization_barrier((value,) + earlier)[0]


def under(outputs, *arrivals):
    joined = lax.optimization_barrier(tuple(outputs) + arrivals)
    return list(joined[: len(outputs)]), list(joined[len(outputs) :])


def by_section(section, values):
    result, last = None, None
    for at in sorted(values):
        if result is None:
            result = values[at]
        elif values[at] is not last:
            result = jnp.where(section >= at, values[at], result)
        last = values[at]
    return result


def total(*values):
    result = values[0].astype(F32)
    for value in values[1:]:
        result = result + value.astype(F32)
    return result.astype(BF16)


class Sums:
    def __init__(self, travel):
        self.stay, self.move, self.other_stay, self.other_move = travel
        self.size = self.stay.shape[1] // 2

    def cross(self, *earlier):
        if earlier:
            self.other_move = after(self.other_move, *earlier)
            self.other_stay = after(self.other_stay, *earlier)
        self.got_move, self.got_stay = over_core(self.other_move), over_core(self.other_stay)

    def first_sends(self):
        size = self.size
        self.sent = [
            total(self.move[:, at : at + size], self.got_move[:, at : at + size])
            for at in (0, size)
        ]
        return self.sent

    def second_sends(self, from_x, from_y):
        size, half = self.size, self.size // 2
        self.first = from_x, from_y
        to_y = total(self.stay[:, half:size], self.got_stay[:, half:size], from_x[:, half:])
        to_x = total(
            self.stay[:, size + half :], self.got_stay[:, size + half :], from_y[:, half:]
        )
        self.sent = [to_x, to_y]
        return self.sent

    def whole(self, from_x, from_y):
        size, half = self.size, self.size // 2
        parts = []
        for at, first, second in ((0, self.first[0], from_y), (size, self.first[1], from_x)):
            here = slice(at, at + half)
            parts.append(total(self.stay[:, here], self.got_stay[:, here], first[:, :half], second))
        return jnp.concatenate(parts, axis=1)


def over_links(sends):
    return [over_section(sends[0], 1), over_section(sends[1], 2)]


class Planes:
    def __init__(self, value, plane, planes):
        self.value, self.plane, self.planes, self.turn = value, plane, planes, 0

    def sends(self, *earlier):
        value = after(self.value, *earlier) if earlier else self.value
        if self.planes != 4:
            return (value,)
        bits = (1, 2, 2, 1)[self.turn]
        if self.turn < 2:
            bit = (self.plane & 1, self.plane >> 1)[self.turn]
            size = value.shape[-1] // 2
            value = lax.dynamic_slice_in_dim(value, (1 - bit) * size, size, value.ndim - 1)
        return (over_plane(value, [(at, at ^ bits) for at in range(4)]),)

    def take(self, arrived):
        if self.planes != 4:
            self.value = lax.psum(arrived, "z") if self.turn == 3 else arrived
        elif self.turn < 2:
            bit = (self.plane & 1, self.plane >> 1)[self.turn]
            size = self.value.shape[-1] // 2
            keep = lax.dynamic_slice_in_dim(self.value, bit * size, size, self.value.ndim - 1)
            self.value = added(keep, arrived)
        else:
            self.value = jnp.concatenate([self.value, arrived], axis=-1)
        self.turn += 1

    def in_order(self, value):
        if self.planes != 4:
            return value
        size, turn = value.shape[-1] // 4, plane_turn(self.plane, 4)
        parts = [
            lax.dynamic_slice_in_dim(value, (at ^ turn) * size, size, value.ndim - 1)
            for at in range(4)
        ]
        return jnp.concatenate(parts, axis=-1)


class Weights:
    def __init__(self, own, info, planes):
        self.own, self.info = own, info
        self.four = planes == 4
        self.plan = PLAN_FOUR if self.four else PLAN_ANY
        self.half, self.width = own[1].shape[0] // 2, own[1].shape[1]
        self.mine, self.theirs, self.arrived = {}, {}, {}

    def place(self, layer, block):
        if layer in "ac":
            return (0, 0, block * self.width) if block < 3 else (1, 0, 0)
        if layer == "g":
            return (2, 0, block * self.width) if block < 4 else (3, (block - 4) * self.width, 0)
        return (2, 0, block * self.width) if block < 4 else (3, (block - 4) * self.width, 0)

    def choices(self, sends, sources):
        result = []
        for at in range(SECTIONS):
            name = sends.get(at)
            if name is not None and HOMES[name[0]] != at:
                key = self.arrived[at, name]
                if key not in sources:
                    sources[key] = len(self.own) + len(sources)
                result.append((at, None, [("arrived", sources[key])] * 2))
                continue
            for plane in range(4) if name == "F" else (None,):
                piece = ("f" + str(plane)) if name == "F" else name or "a0"
                layer, index = piece[0], int(piece[1])
                if layer in "ac":
                    blocks = ATTEND_BLOCKS[index]
                else:
                    blocks = (index, 4 + index) if layer == "g" else EXPERT_BLOCKS[index]
                parts = [("own",) + self.place(layer, block) for block in blocks]
                result.append((at, plane, parts))
        return result

    def packed(self, wanted):
        sources = {}
        plan = [self.choices(sends, sources) for sends in wanted]
        arrays = list(self.own) + [self.mine[key] for key in sources]
        return pack(self.info, arrays, plan, (2, self.half, self.width))

    def sends(self, step):
        if step == "F":
            return [{at: "F" for at in range(SECTIONS)}]
        return [sends for sends in self.plan[step] if sends]

    def payloads(self, *steps):
        wanted = [sends for step in steps for sends in self.sends(step)]
        return list(self.packed(wanted))

    def move(self, step, payloads):
        links = [(link, sends) for link, sends in enumerate(self.plan[step]) if sends]
        for (link, sends), payload in zip(links, payloads):
            self.mine[step, link] = over_section(payload, link + 1, sorted(sends))
            for at, name in sends.items():
                self.arrived[at ^ (link + 1), name] = (step, link)
        return [(step, link) for link, _ in links]

    def move_planes(self, step):
        up, down = self.mine["plane", step - 1], self.mine["plane", 1 - step]
        up = over_plane(up, [(at, at + 1) for at in range(step - 1, 3)])
        down = over_plane(down, [(at, at - 1) for at in range(4 - step, 0, -1)])
        self.mine["plane", step], self.mine["plane", -step] = up, down
        return [("plane", step), ("plane", -step)]

    def cross(self, keys):
        for key in keys:
            self.theirs[key] = over_core(self.mine[key])
        return keys

    def join(self, outputs, mine=(), theirs=()):
        values = [self.mine[key] for key in mine] + [self.theirs[key] for key in theirs]
        outputs, values = under(outputs, *values)
        for key, value in zip(mine, values):
            self.mine[key] = value
        for key, value in zip(theirs, values[len(mine) :]):
            self.theirs[key] = value
        return outputs

    def layer(self, layer):
        arrays, places = list(self.own), {}

        def place(key):
            if key not in places:
                places[key] = len(arrays)
                arrays.extend([self.mine[key], self.theirs[key]])
            return places[key], places[key] + 1

        if layer in "ac":
            names = [(layer + str(index), ATTEND_BLOCKS[index]) for index in range(2)]
        else:
            names = [(layer + str(index), EXPERT_BLOCKS[index]) for index in range(4)]
        plan = []
        for at in range(SECTIONS):
            if layer == "g":
                names = [("g" + str(at), (0, 1))]
            if HOMES[layer] == at:
                steps = []
                for name, blocks in names:
                    for block in blocks:
                        source = block * 4 if layer == "g" else block
                        steps.append((block, ("own",) + self.place(layer, source)))
                plan.append((at, None, steps))
                continue
            by_plane = layer == "f" and self.four
            for plane in range(4) if by_plane else (None,):
                steps = []
                for index, (name, blocks) in enumerate(names):
                    key = ("plane", plane - index) if by_plane else self.arrived[at, name]
                    for which, block in enumerate(blocks):
                        steps.append((block, ("piece",) + place(key) + (which,)))
                plan.append((at, plane, steps))
        return arrays, plan


def per_device(
    tokens,
    caption_lengths,
    attend_gain,
    attend_shift,
    attend_inputs,
    attend_bias,
    attend_output,
    expert_gain,
    expert_shift,
    expert_inputs,
    expert_inner_bias,
    expert_outputs,
    expert_outer_bias,
    cotangent,
):
    section, core, plane = lax.axis_index("section"), lax.axis_index("core"), lax.axis_index("z")
    planes = lax.axis_size("z")
    items, positions, width = tokens.shape
    hidden = expert_inputs.shape[-1]
    info = [value.reshape(1).astype(jnp.int32) for value in (section, core, plane)]
    info = jnp.concatenate([caption_lengths] + info)
    weights = Weights(
        (attend_inputs[0], attend_output[0], expert_inputs[0], expert_outputs[0]), info, planes
    )

    def to_sections(value):
        return [value] + [over_section(value, bits) for bits in (1, 2, 3)]

    def items_of(part):
        return part.reshape(items, CAP_ROWS, width)

    keys = weights.move(0, weights.payloads(0))
    pad = ((0, 0), (0, ROWS - positions), (0, 0))
    x0 = jnp.pad(tokens, pad)
    last_grad = jnp.pad(cotangent, pad)
    rows = jnp.concatenate(
        [
            attend_gain,
            attend_shift,
            attend_bias,
            expert_gain,
            expert_shift,
            expert_inner_bias,
            expert_outer_bias,
            jnp.full((1, 128), jnp.sum(caption_lengths), F32),
        ],
        axis=1,
    )
    rows = to_sections(rows)
    x0, last_grad, *rows = weights.join([x0, last_grad, *rows], keys)
    keys1 = weights.move(1, weights.payloads(1))
    rows = jnp.concatenate(rows, axis=0)
    language_count = jnp.sum(rows[:, -128:], axis=0, keepdims=True)
    rows = [lax.dynamic_index_in_dim(rows, at ^ section, 0) for at in range(SECTIONS)]
    sizes = [width, width, 3 * width, width, width, hidden, width]
    ends = [sum(sizes[: at + 1]) for at in range(len(sizes))]
    used = [(0, 0), (0, 1), (0, 2), (0, 3), (0, 4), (0, 5), (1, 3), (1, 4), (1, 5), (1, 6)]
    used += [(0, 6), (2, 0), (2, 1), (2, 2), (3, 3), (3, 4), (3, 5), (3, 6)]
    kept = [rows[slot][:, ends[which] - sizes[which] : ends[which]] for slot, which in used]
    language_count, *kept = weights.join([language_count, *kept], keys1)
    kept = dict(zip(used, kept))

    def row(slot, which):
        return kept[slot, which]

    crossed = weights.cross(keys + keys1)
    sends = weights.payloads(2, "F") if weights.four else weights.payloads(2)
    sends, (info, language_count) = under(sends, info, language_count)
    keys = weights.move(2, sends[:2])
    info, language_count = weights.join(
        [info, language_count + over_core(language_count)], theirs=crossed
    )
    plane_keys = []
    if weights.four:
        weights.mine["plane", 0] = sends[2]
        plane_keys = weights.move_planes(1)
    attend0 = weights.layer("a")
    outputs = attend_forward(
        x0, info, attend0, row(0, 0), row(0, 1), row(0, 2), following=(row(0, 3), row(0, 4))
    )
    y0, qkv0, mixed0, caption_rows = weights.join(outputs, keys)
    caption_rows = to_sections(caption_rows.reshape(-1, width))
    sends = weights.payloads(3, 4) if weights.four else weights.payloads(3)
    caption_rows = weights.join(caption_rows, plane_keys)
    sends, caption_rows = under(sends, *caption_rows)
    early_keys = keys
    keys, sends = weights.move(3, sends[:2]), sends[2:]
    crossed = weights.cross(early_keys)
    if weights.four:
        keys += weights.move_planes(2)
    outputs = shared_forward(caption_rows, expert_inputs[0], expert_inner_bias, expert_outputs[0])
    part = weights.join(outputs, keys, crossed)
    (y0,) = weights.join([y0], theirs=weights.cross([(3, 0), (3, 1)]))
    branch = {at: over_section(part[at], at, [0]) for at in range(1, SECTIONS)}
    keys = weights.move_planes(3) if weights.four else []
    expert1 = weights.layer("e")
    outputs = expert_forward(
        y0, info, expert1, row(1, 3), row(1, 4), row(1, 5), row(1, 6), PATCH_ROWS, "patch"
    )
    outputs, moved = under(outputs, *branch.values())
    if weights.four:
        keys += [("plane", step) for step in range(-2, 3)]
    x2, act1, slope1 = weights.join(outputs, keys)
    branch = dict(zip(branch, moved))
    branch[0] = part[0]
    branch = items_of(by_section(section, branch))
    if weights.four:
        crossed = [("plane", step) for step in range(-3, 4)]
    else:
        for step in (4, 5):
            weights.move(step, weights.payloads(step))
        crossed = [(4, 0), (4, 1), (5, 0)]
    weights.cross(crossed)
    attend2 = weights.layer("c") if weights.four else None
    if not weights.four:
        (x2,) = weights.join([x2], theirs=crossed)
        attend2 = weights.layer("c")
    outputs = attend_forward(
        x2, info, attend2, row(2, 0), row(2, 1), row(2, 2), merge=(y0, branch, row(0, 6))
    )
    if weights.four:
        language_count += over_plane(language_count, [(at, at ^ 1) for at in range(4)])
    x3, qkv2, mixed2, x2, language_count = weights.join([*outputs, language_count], theirs=crossed)
    if weights.four:
        language_count += over_plane(language_count, [(at, at ^ 2) for at in range(4)])
    else:
        language_count = lax.psum(language_count, "z")
    expert3 = weights.layer("f")
    outputs = expert_forward(
        x3, info, expert3, row(3, 3), row(3, 4), row(3, 5), row(3, 6), ROWS, "all"
    )
    layer_output, act3, slope3, language_count = under([*outputs, language_count])[0]
    language_count = language_count[0, 0].astype(jnp.int32)
    vision_count = PATCHES * items * SECTIONS * 2 * planes
    counts = jnp.stack(
        [jnp.full((), vision_count, jnp.int32), language_count, language_count + vision_count]
    )

    def small_rows(values):
        flat = jnp.concatenate(values, axis=1)
        count = -(-flat.shape[1] // hidden)
        flat = jnp.pad(flat, ((0, 0), (0, count * hidden - flat.shape[1])))
        return flat.reshape(count, hidden)

    def to_home(sums):
        got = [by_section(section, sums)]
        for bits in (1, 2, 3):
            sends = {at ^ bits: sums[at] for at in sums}
            got.append(over_section(by_section(section, sends), bits, sorted(sends)))
        return got

    keys = []
    if weights.four:
        sends, (layer_output, last_grad) = under(sends, layer_output, last_grad)
        keys = weights.move(4, sends)
    outputs = expert_backward(
        x3, info, expert3, row(3, 3), row(3, 4), act3, slope3, last_grad, ROWS, "all"
    )
    outputs = weights.join(outputs, keys)
    crossed = weights.cross(keys)
    grad3, *small3 = outputs[:5]
    sums3 = Sums(outputs[5:])
    sums3.cross()
    moved = over_links(sums3.first_sends())
    grad3 = after(grad3, *sums3.sent)
    outputs = attend_backward(
        x2, info, attend2, row(2, 0), row(2, 1), qkv2, mixed2, grad3
    )
    outputs, moved = under(outputs, *moved, sums3.got_stay)
    outputs = weights.join(outputs, theirs=crossed)
    grad2, *small2 = outputs[:4]
    sums2, caption_grad = Sums(outputs[4:8]), outputs[8]
    caption_grads = to_sections(caption_grad.reshape(-1, width))
    sums3.got_stay = moved[2]
    moved3 = over_links(sums3.second_sends(*moved[:2]))
    grad2 = after(grad2, *sums3.sent)
    outputs = expert_backward(
        y0, info, expert1, row(1, 3), row(1, 4), act1, slope1, grad2, PATCH_ROWS, "patch"
    )
    outputs, caption_grads = under(outputs, *caption_grads)
    grad1, *small1 = outputs[:5]
    sums2.cross(grad1)
    sums1 = Sums(outputs[5:])
    sums1.cross()
    inner_quarter = lax.dynamic_slice(row(0, 5), (0, section * width), (1, width))
    sum3 = sums3.whole(*moved3)
    inner_quarter = after(inner_quarter, grad1, sum3)
    outputs = shared_backward(
        caption_rows, caption_grads, info, weights.layer("g"), inner_quarter
    )
    parts, (keep0, send0, inner_grad, outer_grad) = outputs[:4], outputs[4:]
    got = [over_section(parts[bits], bits) for bits in (1, 2, 3)]
    sends = [after(value, *parts) for value in sums1.first_sends()]
    moved1 = over_links(sends)
    keep0 = added(keep0, over_core(send0))
    early = lax.psum(jnp.concatenate([sum3, keep0], axis=0), "z")
    sends2 = [after(value, *sends) for value in sums2.first_sends()]
    moved2 = over_links(sends2)
    parts = [parts[0], *got]
    grad1 = after(grad1, keep0, *sends, *sends2)
    outputs = attend_backward(
        x0,
        info,
        attend0,
        row(0, 0),
        row(0, 1),
        qkv0,
        mixed0,
        grad1,
        first=(y0, row(0, 3), parts),
    )
    outputs, moved = under(outputs, *moved2, *moved1)
    moved2, moved1 = moved[:2], moved[2:]
    tokens_grad, *small_first = outputs[:4]
    sums_first, gain_grad, shift_grad = Sums(outputs[4:8]), outputs[8], outputs[9]
    sums_first.cross()
    inner_grad = lax.dynamic_update_slice(
        jnp.zeros((1, hidden), F32), inner_grad, (0, section * width)
    )
    small = small_rows(
        small_first + [gain_grad, shift_grad, inner_grad, outer_grad] + small2 + small1 + small3
    )
    small = added(small, over_core(small))
    to_x, to_y = sums_first.first_sends()
    to_x = jnp.concatenate([to_x[0], small], axis=0)
    sends = lax.optimization_barrier((*sums1.second_sends(*moved1), to_x, to_y))
    moved1, moved = over_links(sends[:2]), over_links(sends[2:])
    sum1 = sums1.whole(*moved1)
    size = to_y.shape[1]
    small = added(small, moved[0][size:])
    to_x, to_y = sums_first.second_sends(moved[0][None, :size], moved[1])
    early_x, early_y = sums2.second_sends(*moved2)
    to_x = jnp.concatenate([to_x[0], early_x[0]], axis=0)
    to_y = jnp.concatenate([to_y[0], early_y[0], small], axis=0)
    to_x, to_y = lax.optimization_barrier((to_x, to_y))
    moved = over_links((to_x, to_y))
    sum1, early, to_x, to_y = lax.optimization_barrier((sum1, early, to_x, to_y))
    planes1 = Planes(sum1, plane, planes)
    sent1 = planes1.sends()
    moved = lax.optimization_barrier(tuple(moved))
    size = early_x.shape[1]
    last = sums_first.whole(moved[0][None, :size], moved[1][None, :size])
    sum2 = sums2.whole(moved[0][None, size:], moved[1][None, size : 2 * size])
    small = added(small, moved[1][2 * size :])
    small_count = small.shape[0]
    eighth = last.shape[1]
    last = jnp.concatenate([last[0], sum2[0], small], axis=0)
    planes_last = Planes(last, plane, planes)
    home_early = to_home({0: after(early[2:], *moved), 3: after(early[:2], *moved)})
    planes_last.take(*planes_last.sends())
    planes1.take(*sent1)
    planes1.take(*planes1.sends())
    planes1.take(*planes1.sends())
    planes1.take(*planes1.sends())
    planes_last.take(*planes_last.sends())
    planes_last.take(*planes_last.sends())
    home_late = to_home({1: after(planes1.value, *home_early[1:3])})
    planes_last.take(*planes_last.sends())
    last = planes_last.value
    home_attend = to_home({0: last[None, :eighth], 2: last[None, eighth : 2 * eighth]})
    small = planes_last.in_order(last[2 * eighth :].astype(F32))

    as_float = counts.astype(F32)
    one = jnp.ones((), F32)
    attend_scales = jnp.stack([as_float[2], one, as_float[2], one])
    expert_scales = jnp.stack([as_float[1], as_float[0], one, as_float[2]])

    def placed(pieces, scales, *earlier):
        scale = lax.dynamic_index_in_dim(scales, section, 0).reshape(1, 1)
        theirs = []
        for piece in pieces:
            theirs.append(over_core(after(piece, theirs[-1]) if theirs else piece))
        if earlier:
            scale = after(scale, *earlier)
        return finish(info, scale, pieces, theirs, planes)

    blank = jnp.zeros_like(home_late[0])
    inputs_whole, outputs_whole = placed(
        [
            by_section(section, {0: early, 1: late, 2: blank, 3: early})
            for early, late in zip(home_early, home_late)
        ],
        expert_scales,
    )
    blank = jnp.zeros_like(home_attend[0])
    attend_whole, output_whole = placed(
        [by_section(section, {0: got, 1: blank, 2: got, 3: blank}) for got in home_attend],
        attend_scales,
        inputs_whole,
    )

    attend_size, expert_size = 5 * width, 3 * width + hidden
    cuts = [attend_size, attend_size + expert_size]
    cuts += [cuts[1] + attend_size, cuts[1] + attend_size + expert_size]
    small = jnp.split(small.reshape(-1)[: cuts[3] + expert_size], cuts)
    none_attend, none_expert = jnp.zeros_like(small[0]), jnp.zeros_like(small[1])
    attend_small = jnp.stack([small[0], none_attend, small[2], none_attend])
    expert_small = jnp.stack([small[1], small[3], none_expert, small[4]])
    attend_small = attend_small / attend_scales.reshape(-1, 1)
    expert_small = expert_small / expert_scales.reshape(-1, 1)
    attend_small = lax.dynamic_index_in_dim(attend_small, section, 0)
    expert_small = lax.dynamic_index_in_dim(expert_small, section, 0)
    return (
        layer_output[:, :positions],
        tokens_grad[:, :positions],
        attend_small[:, :width],
        attend_small[:, width : 2 * width],
        attend_whole,
        attend_small[:, 2 * width :],
        output_whole,
        expert_small[:, :width],
        expert_small[:, width : 2 * width],
        inputs_whole,
        expert_small[:, 2 * width : 2 * width + hidden],
        outputs_whole,
        expert_small[:, 2 * width + hidden :],
        counts,
    )


def solution(mesh):
    sections, groups = mesh.shape["section"], mesh.shape["dp"]
    split = Mesh(mesh.devices.reshape(sections, groups // 2, 2), ("section", "z", "core"))
    items = P(("section", "z", "core"), None, None)
    flat = P("section", None)
    matrix = P("section", None, None)
    placed = (
        items,
        P(("section", "z", "core")),
        flat,
        flat,
        matrix,
        flat,
        matrix,
        flat,
        flat,
        matrix,
        flat,
        matrix,
        flat,
        items,
    )
    return jax.shard_map(
        per_device,
        mesh=split,
        in_specs=placed,
        out_specs=(
            items,
            items,
            flat,
            flat,
            matrix,
            flat,
            matrix,
            flat,
            flat,
            matrix,
            flat,
            matrix,
            flat,
            P(),
        ),
        check_vma=False,
    )
```

```python
from functools import partial

import jax
import jax.numpy as jnp
from jax import lax
from jax.experimental import pallas as pl
from jax.experimental.pallas import tpu as pltpu
from jax.sharding import Mesh
from jax.sharding import PartitionSpec as P

HEADS = 12
HEAD_DIM = 64
PATCHES = 197
ROWS = 256
CAP_FIRST, CAP_ROWS = 192, 48
PATCH_ROWS = 208
PAIR = 2 * HEAD_DIM
SECTIONS = 4
PIECE_ROWS = 48
VMEM_BYTES = 58 * 1024 * 1024
F32 = jnp.float32
BF16 = jnp.bfloat16

PLAN_FOUR = (
    ({0: "a0", 1: "e0", 2: "c0", 3: "F"}, {0: "a1", 1: "e2", 2: "c0", 3: "F"}),
    ({0: "a1", 1: "e1", 2: "a1", 3: "e2"}, {0: "a0", 1: "a0", 2: "F", 3: "c0"}),
    ({0: "g3", 1: "e2", 2: "c1"}, {0: "e0", 1: "e3", 2: "c1"}),
    ({0: "g1", 1: "e3", 2: "e0", 3: "e3"}, {0: "e1", 1: "e1", 3: "c1"}),
    ({}, {0: "g2", 1: "g3"}),
)
PLAN_ANY = (
    ({0: "a0", 1: "e0", 2: "c0", 3: "f0"}, {0: "a1", 1: "e2", 2: "c0", 3: "f0"}),
    ({0: "a1", 1: "e1", 2: "a1", 3: "e2"}, {0: "a0", 1: "a0", 2: "c1", 3: "f1"}),
    ({0: "g3", 1: "e2", 2: "c1", 3: "f1"}, {0: "e0", 1: "e3", 2: "f0", 3: "f2"}),
    ({0: "g1", 1: "e3", 2: "e0", 3: "e3"}, {0: "e1", 1: "e1", 2: "f1", 3: "f3"}),
    ({0: "c1", 1: "f2", 3: "f2"}, {0: "g2", 1: "g3", 3: "c0"}),
    ({1: "f3", 3: "f3"}, {}),
)
HOMES = {"a": 0, "c": 2, "e": 1, "f": 3, "F": 3, "g": 0}
ATTEND_BLOCKS = ((0, 1), (2, 3))
EXPERT_BLOCKS = ((0, 1), (4, 5), (2, 3), (6, 7))


def dot_plain(left, right):
    return jnp.dot(left, right, preferred_element_type=F32)


def dot_last(left, right):
    return lax.dot_general(left, right, (((1,), (1,)), ((), ())), preferred_element_type=F32)


def dot_first(left, right):
    return lax.dot_general(left, right, (((0,), (0,)), ((), ())), preferred_element_type=F32)


def column_sum(matrix):
    return jnp.sum(matrix.astype(F32), axis=0, keepdims=True)


def norm_parts(rows):
    centre = rows - jnp.mean(rows, axis=-1, keepdims=True)
    scale = lax.rsqrt(jnp.mean(centre * centre, axis=-1, keepdims=True) + 1e-06)
    return centre * scale, scale


def norm_back(normed_grad, unit, scale, gain):
    unit_grad = normed_grad * gain
    along = jnp.mean(unit_grad * unit, axis=-1, keepdims=True)
    return scale * (unit_grad - jnp.mean(unit_grad, axis=-1, keepdims=True) - unit * along)


def true_positions(length, first, count, axis, kind):
    shape = (count, 1) if axis == 0 else (1, count)
    position = first + lax.broadcasted_iota(jnp.int32, shape, axis)
    patch = position < PATCHES
    if kind == "patch":
        return patch
    caption = (position >= PATCHES) & (position - PATCHES < length)
    return caption if kind == "caption" else patch | caption


def head_masks():
    lane = lax.broadcasted_iota(jnp.int32, (1, PAIR), 1)
    even = (lane < HEAD_DIM).astype(F32).astype(BF16)
    odd = (lane >= HEAD_DIM).astype(F32).astype(BF16)
    return lane < HEAD_DIM, even, odd


def split_pair(pair, even, odd):
    return jnp.concatenate([pair * even, pair * odd], axis=0)


def start_weights(info, first, refs, plan, blocks, sems):
    half = blocks.shape[1] // 2
    section, core, plane = info[first], info[first + 1], info[first + 2]
    for at, at_plane, steps in plan:
        here = section == at
        if at_plane is not None:
            here = here & (plane == at_plane)

        @pl.when(here)
        def _(steps=steps):
            for block, source in steps:
                if source[0] == "own":
                    _, which, row, column = source
                    width = blocks.shape[2]
                    for part in range(2):
                        pltpu.make_async_copy(
                            refs[which].at[
                                pl.ds(row + part * half, half), pl.ds(column, width)
                            ],
                            blocks.at[block, pl.ds(part * half, half)],
                            sems.at[block],
                        ).start()
                else:
                    _, mine, theirs, index = source
                    pltpu.make_async_copy(
                        refs[mine].at[index],
                        blocks.at[block, pl.ds(pl.multiple_of(core * half, half), half)],
                        sems.at[block],
                    ).start()
                    pltpu.make_async_copy(
                        refs[theirs].at[index],
                        blocks.at[block, pl.ds(pl.multiple_of((1 - core) * half, half), half)],
                        sems.at[block],
                    ).start()


def wait_block(blocks, block, sems):
    pltpu.make_async_copy(blocks.at[block], blocks.at[block], sems.at[block]).wait()


def store_turned(target, turned, columns, section, core):
    half = target.shape[0] // 2
    for piece in range(16):
        path, owner = (piece >> 2) & 1, piece & 3
        away = owner ^ section
        place = ((away & 1) << 1) | (away >> 1) if path == 0 else away
        row = ((piece >> 3) ^ core) * half + (place >> 1) * (half // 2)
        row = row + path * (half // 4) + (place & 1) * PIECE_ROWS
        target[pl.ds(pl.multiple_of(row, 16), PIECE_ROWS), columns] = turned[
            piece * PIECE_ROWS : (piece + 1) * PIECE_ROWS
        ]


def put_travel(refs, which, columns, left, right):
    half = left.shape[0] // 2
    for side in range(2):
        rows = dot_plain(left[side * half : (side + 1) * half], right).astype(BF16)
        refs[2 * side][which, :, columns] = rows[: half // 2]
        refs[2 * side + 1][which, :, columns] = rows[half // 2 :]


def attend_forward_kernel(plan, weight_count, merge, info, *refs):
    weights, refs = refs[:weight_count], refs[weight_count:]
    if merge:
        x_ref, before_ref, part_ref, outer_ref, gain_ref, shift_ref, bias_ref = refs[:7]
        y_ref, qkv_ref, mixed_ref, joined_ref, blocks, sems, joined = refs[7:]
    else:
        x_ref, gain_ref, shift_ref, bias_ref, next_gain_ref, next_shift_ref = refs[:6]
        y_ref, qkv_ref, mixed_ref, caption_ref, blocks, sems = refs[6:]
    item = pl.program_id(0)
    items = pl.num_programs(0)
    length = info[item]
    width = x_ref.shape[-1]

    @pl.when(item == 0)
    def _():
        start_weights(info, items, weights, plan, blocks, sems)

    cap = slice(CAP_FIRST, CAP_FIRST + CAP_ROWS)
    if merge:
        joined[...] = x_ref[0].astype(F32)
        branch = part_ref[0].astype(F32) + outer_ref[...]
        is_true = true_positions(length, CAP_FIRST, CAP_ROWS, 0, "caption")
        captions = before_ref[0, cap] + jnp.where(is_true, branch, 0.0)
        position = CAP_FIRST + lax.broadcasted_iota(jnp.int32, (CAP_ROWS, 1), 0)
        captions = captions.astype(BF16).astype(F32)
        joined[cap] = jnp.where(position < PATCHES, joined[cap], captions)
        x = joined[...]
        joined_ref[0] = x.astype(BF16)
    else:
        x = x_ref[0].astype(F32)
    unit, _ = norm_parts(x)
    normed = (unit * gain_ref[...] + shift_ref[...]).astype(BF16)

    @pl.when(item == 0)
    def _():
        for block in range(4):
            wait_block(blocks, block, sems)

    queries = dot_plain(normed, blocks[0]) + bias_ref[:, :width]
    qkv_ref[0, :, :width] = (queries * HEAD_DIM ** (-0.5)).astype(BF16)
    qkv_ref[0, :, width : 2 * width] = dot_plain(normed, blocks[1]).astype(BF16)
    values = dot_plain(normed, blocks[2]) + bias_ref[:, width : 2 * width]
    qkv_ref[0, :, 2 * width :] = values.astype(BF16)
    key_true = true_positions(length, 0, ROWS, 1, "all")
    low_half, even, odd = head_masks()
    ones = jnp.ones((ROWS, PAIR), BF16)

    def scores_of(pair):
        at = pair * PAIR
        q2 = qkv_ref[0, :, at : at + PAIR]
        k2 = qkv_ref[0, :, width + at : width + at + PAIR]
        return dot_last(split_pair(q2, even, odd), k2)

    ahead = [scores_of(0), scores_of(1)]
    for pair in range(HEADS // 2):
        at = pair * PAIR
        scores = jnp.where(key_true, ahead.pop(0), -1e9)
        if pair + 2 < HEADS // 2:
            ahead.append(scores_of(pair + 2))
        weight = jnp.exp(scores - jnp.max(scores, axis=-1, keepdims=True)).astype(BF16)
        v2 = qkv_ref[0, :, 2 * width + at : 2 * width + at + PAIR]
        summed = dot_plain(weight, jnp.concatenate([v2, ones], axis=1))
        top = jnp.where(low_half, summed[:ROWS, :PAIR], summed[ROWS:, :PAIR])
        below = jnp.where(low_half, summed[:ROWS, PAIR:], summed[ROWS:, PAIR:])
        mixed_ref[0, :, at : at + PAIR] = (top / below).astype(BF16)
    branch = dot_plain(mixed_ref[0], blocks[3]) + bias_ref[:, 2 * width :]
    row_true = true_positions(length, 0, ROWS, 0, "all")
    y = x + jnp.where(row_true, branch, 0.0)
    y_ref[0] = y.astype(y_ref.dtype)
    if not merge:
        unit, _ = norm_parts(y[cap])
        caption_ref[0] = (unit * next_gain_ref[...] + next_shift_ref[...]).astype(BF16)


def attend_backward_kernel(plan, weight_count, first, info, *refs):
    weights, refs = refs[:weight_count], refs[weight_count:]
    x_ref, gain_ref, shift_ref, qkv_ref, mixed_ref, grad_ref = refs[:6]
    if first:
        after_ref, next_gain_ref, *parts = refs[6:12]
        refs = refs[12:]
    else:
        refs = refs[6:]
    out_ref, gain_grad_ref, shift_grad_ref, bias_grad_ref = refs[:4]
    travel_refs = refs[4:8]
    if first:
        next_gain_grad_ref, next_shift_grad_ref, joined = refs[8], refs[9], refs[-1]
    else:
        caption_ref = refs[8]
    blocks, sems, normed_turned, mixed_turned, branch_all, projected, mixed_grad = refs[
        10 if first else 9 :
    ][:7]
    item = pl.program_id(0)
    items = pl.num_programs(0)
    length = info[item]
    section, core = info[items], info[items + 1]
    width = x_ref.shape[-1]
    here = pl.ds(pl.multiple_of(item * ROWS, ROWS), ROWS)
    cap = slice(CAP_FIRST, CAP_FIRST + CAP_ROWS)

    @pl.when(item == 0)
    def _():
        start_weights(info, items, weights, plan, blocks, sems)

    def add_to(ref, part):
        @pl.when(item == 0)
        def _():
            ref[...] = part

        @pl.when(item > 0)
        def _():
            ref[...] += part

    x = x_ref[0].astype(F32)
    unit, scale = norm_parts(x)
    normed = (unit * gain_ref[...] + shift_ref[...]).astype(BF16)
    incoming = grad_ref[0].astype(F32)
    if first:
        after_unit, after_scale = norm_parts(after_ref[0, cap])
        caption_grad = parts[0][...].astype(F32)
        for part in parts[1:]:
            caption_grad = caption_grad + part[...].astype(F32)
        joined[...] = incoming
        joined[cap] += norm_back(caption_grad, after_unit, after_scale, next_gain_ref[...])
        incoming = joined[...]
        add_to(next_gain_grad_ref, jnp.sum(caption_grad * after_unit, axis=0, keepdims=True))
        add_to(next_shift_grad_ref, jnp.sum(caption_grad, axis=0, keepdims=True))
    row_true = true_positions(length, 0, ROWS, 0, "all")
    branch = jnp.where(row_true, incoming, 0.0).astype(BF16)
    branch_all[here, :] = branch
    store_turned(normed_turned, normed.T, here, section, core)
    store_turned(mixed_turned, mixed_ref[0].T, here, section, core)

    @pl.when(item == 0)
    def _():
        for block in range(4):
            wait_block(blocks, block, sems)

    mixed_grad[...] = dot_last(branch, blocks[3]).astype(BF16)
    key_true = true_positions(length, 0, ROWS, 0, "all")
    _, even, odd = head_masks()

    def products_of(pair):
        at = pair * PAIR
        q2 = split_pair(qkv_ref[0, :, at : at + PAIR], even, odd)
        k2 = qkv_ref[0, :, width + at : width + at + PAIR]
        v2 = qkv_ref[0, :, 2 * width + at : 2 * width + at + PAIR]
        g2 = split_pair(mixed_grad[:, at : at + PAIR], even, odd)
        return q2, k2, g2, dot_last(k2, q2), dot_last(v2, g2)

    ahead = [products_of(0)]
    for pair in range(HEADS // 2):
        at = pair * PAIR
        q2, k2, g2, scores, weight_grad = ahead.pop(0)
        if pair + 1 < HEADS // 2:
            ahead.append(products_of(pair + 1))
        scores = jnp.where(key_true, scores, -1e9)
        weight = jnp.exp(scores - jnp.max(scores, axis=0, keepdims=True))
        weight = weight * (1.0 / jnp.sum(weight, axis=0, keepdims=True))
        product = weight * weight_grad
        along = jnp.sum(product, axis=0, keepdims=True)
        score_grad = (product - weight * along).astype(BF16)
        values_grad = dot_plain(weight.astype(BF16), g2).astype(BF16)
        keys_grad = dot_plain(score_grad, q2).astype(BF16)
        k2_split = split_pair(k2, even, odd)
        stacked = jnp.concatenate([score_grad[:, :ROWS], score_grad[:, ROWS:]], axis=0)
        queries_grad = dot_first(stacked, k2_split).astype(BF16)
        queries_grad = (queries_grad.astype(F32) * HEAD_DIM ** (-0.5)).astype(BF16)
        projected[here, at : at + PAIR] = queries_grad
        projected[here, width + at : width + at + PAIR] = keys_grad
        projected[here, 2 * width + at : 2 * width + at + PAIR] = values_grad
    normed_grad = dot_last(projected[here, :width], blocks[0])
    normed_grad += dot_last(projected[here, width : 2 * width], blocks[1])
    normed_grad += dot_last(projected[here, 2 * width :], blocks[2])
    out = (incoming + norm_back(normed_grad, unit, scale, gain_ref[...])).astype(BF16)
    out_ref[0] = out
    if not first:
        is_true = true_positions(length, CAP_FIRST, CAP_ROWS, 0, "caption")
        caption_ref[0] = jnp.where(is_true, out[cap].astype(F32), 0.0).astype(BF16)
    add_to(gain_grad_ref, jnp.sum(normed_grad * unit, axis=0, keepdims=True))
    add_to(shift_grad_ref, jnp.sum(normed_grad, axis=0, keepdims=True))

    @pl.when(item == items - 1)
    def _():
        for block in range(4):
            columns = slice(block * width, (block + 1) * width)
            left = normed_turned if block < 3 else mixed_turned
            right = projected[:, columns] if block < 3 else branch_all[...]
            put_travel(travel_refs, 0, columns, left, right)
        bias_grad_ref[:, :width] = column_sum(projected[:, :width])
        bias_grad_ref[:, width : 2 * width] = column_sum(projected[:, 2 * width :])
        bias_grad_ref[:, 2 * width :] = column_sum(branch_all[...])


SHORT = pl.CostEstimate(flops=0, bytes_accessed=100_000, transcendentals=0)
LONG = pl.CostEstimate(flops=30_000_000_000, bytes_accessed=30_000_000, transcendentals=0)
ANYWHERE = pl.BlockSpec(memory_space=pl.ANY)


def whole_block(shape):
    return pl.BlockSpec(shape, lambda step, info: (0,) * len(shape))


def item_block(shape):
    return pl.BlockSpec((1,) + shape[1:], lambda step, info: (step,) + (0,) * (len(shape) - 1))


def blocks_scratch(count, width):
    return [pltpu.VMEM((count, width, width), BF16), pltpu.SemaphoreType.DMA((count,))]


def attend_forward(x, info, weights, gain, shift, bias, merge=None, following=None):
    arrays, plan = weights
    items, _, width = x.shape
    row = whole_block((1, width))
    bias_row = whole_block((1, 3 * width))
    caption_shape = (items, CAP_ROWS, width)
    if merge is not None:
        before, part, outer = merge
        operands = (x, before, part, outer, gain, shift, bias)
        specs = [item_block(x.shape), item_block(x.shape), item_block(caption_shape)]
        specs += [row, row, row, bias_row]
        last_shape, kind, scratch = x.shape, BF16, [pltpu.VMEM((ROWS, width), F32)]
    else:
        operands = (x, gain, shift, bias, *following)
        specs = [item_block(x.shape), row, row, bias_row, row, row]
        last_shape, kind, scratch = caption_shape, F32, []
    return pl.pallas_call(
        partial(attend_forward_kernel, plan, len(arrays), merge is not None),
        grid_spec=pltpu.PrefetchScalarGridSpec(
            num_scalar_prefetch=1,
            grid=(items,),
            in_specs=[ANYWHERE] * len(arrays) + specs,
            out_specs=[
                item_block(x.shape),
                item_block((items, ROWS, 3 * width)),
                item_block((items, ROWS, width)),
                item_block(last_shape),
            ],
            scratch_shapes=blocks_scratch(4, width) + scratch,
        ),
        out_shape=[
            jax.ShapeDtypeStruct(x.shape, kind),
            jax.ShapeDtypeStruct((items, ROWS, 3 * width), BF16),
            jax.ShapeDtypeStruct((items, ROWS, width), BF16),
            jax.ShapeDtypeStruct(last_shape, BF16),
        ],
        compiler_params=pltpu.CompilerParams(vmem_limit_bytes=VMEM_BYTES),
        cost_estimate=SHORT,
        name="attend_forward",
    )(info, *arrays, *operands)


def attend_backward(x, info, weights, gain, shift, qkv, mixed, incoming, first=None):
    arrays, plan = weights
    items, _, width = x.shape
    half = width // 2
    row = whole_block((1, width))
    caption_shape = (items, CAP_ROWS, width)
    operands = (x, gain, shift, qkv, mixed, incoming)
    specs = [item_block(x.shape), row, row, item_block(qkv.shape), item_block(mixed.shape)]
    specs += [item_block(incoming.shape)]
    outs = [
        (item_block(x.shape), x.shape, BF16),
        (row, (1, width), F32),
        (row, (1, width), F32),
        (whole_block((1, 3 * width)), (1, 3 * width), F32),
    ]
    outs += [(whole_block((1, half // 2, 4 * width)), (1, half // 2, 4 * width), BF16)] * 4
    scratch = []
    if first is not None:
        after, next_gain, parts = first
        operands += (after, next_gain, *parts)
        caption_rows = pl.BlockSpec((CAP_ROWS, width), lambda step, info: (step, 0))
        specs += [item_block(after.shape), row] + [caption_rows] * 4
        outs += [(row, (1, width), F32)] * 2
        scratch = [pltpu.VMEM((ROWS, width), F32)]
    else:
        outs += [(item_block(caption_shape), caption_shape, BF16)]
    return pl.pallas_call(
        partial(attend_backward_kernel, plan, len(arrays), first is not None),
        grid_spec=pltpu.PrefetchScalarGridSpec(
            num_scalar_prefetch=1,
            grid=(items,),
            in_specs=[ANYWHERE] * len(arrays) + specs,
            out_specs=[spec for spec, _, _ in outs],
            scratch_shapes=blocks_scratch(4, width)
            + [
                pltpu.VMEM((width, items * ROWS), BF16),
                pltpu.VMEM((width, items * ROWS), BF16),
                pltpu.VMEM((items * ROWS, width), BF16),
                pltpu.VMEM((items * ROWS, 3 * width), BF16),
                pltpu.VMEM((ROWS, width), BF16),
            ]
            + scratch,
        ),
        out_shape=[jax.ShapeDtypeStruct(shape, kind) for _, shape, kind in outs],
        compiler_params=pltpu.CompilerParams(vmem_limit_bytes=VMEM_BYTES),
        cost_estimate=LONG,
        name="attend_backward",
    )(info, *arrays, *operands)


def normal_parts(u):
    t = pl.reciprocal(1.0 + 0.23164190 * jnp.abs(u), approx=True)
    bell = jnp.exp2((u * -0.7213475204444817) * u)
    poly = t * (
        0.127414796
        + t * (-0.142248368 + t * (0.7107068705 + t * (-0.7265760135 + t * 0.5307027145)))
    )
    tail = poly * bell
    return jnp.where(u < 0, tail, 1.0 - tail), bell


def inner_forward(normed, matrix, bias):
    inner = dot_plain(normed, matrix) + bias
    cumulative, bell = normal_parts(inner)
    slope = cumulative + (inner * 0.3989422804014327) * bell
    return (inner * cumulative).astype(BF16), slope.astype(BF16)


def expert_forward_kernel(plan, weight_count, count, kind, info, *refs):
    weights, refs = refs[:weight_count], refs[weight_count:]
    x_ref, gain_ref, shift_ref, inner_ref, outer_ref = refs[:5]
    y_ref, act_ref, slope_ref, blocks, sems, normed, total = refs[5:]
    step = pl.program_id(0)
    items, _, width = x_ref.shape

    @pl.when(step == 0)
    def _():
        start_weights(info, items, weights, plan, blocks, sems)
        for item in range(items):
            x = x_ref[item, :count].astype(BF16).astype(F32)
            unit, _ = norm_parts(x)
            normed[item * count : (item + 1) * count] = (
                unit * gain_ref[...] + shift_ref[...]
            ).astype(BF16)

    wait_block(blocks, step, sems)
    wait_block(blocks, step + 4, sems)
    for at in range(0, width, 256):
        columns = slice(at, at + 256)
        act, slope = inner_forward(normed[...], blocks[step, :, columns], inner_ref[:, columns])
        act_ref[:, columns] = act
        slope_ref[:, columns] = slope
    part = dot_plain(act_ref[...], blocks[step + 4])

    @pl.when(step == 0)
    def _():
        total[...] = part

    @pl.when(step > 0)
    def _():
        total[...] += part

    @pl.when(step == pl.num_programs(0) - 1)
    def _():
        for item in range(items):
            row_true = true_positions(info[item], 0, count, 0, kind)
            branch = total[item * count : (item + 1) * count] + outer_ref[...]
            x = x_ref[item, :count].astype(BF16).astype(F32)
            y_ref[item, :count] = (x + jnp.where(row_true, branch, 0.0)).astype(BF16)
            if count < ROWS:
                y_ref[item, count:] = jnp.zeros((ROWS - count, width), BF16)


def expert_backward_kernel(plan, weight_count, count, kind, info, *refs):
    weights, refs = refs[:weight_count], refs[weight_count:]
    x_ref, gain_ref, shift_ref, act_ref, slope_ref, grad_ref = refs[:6]
    out_ref, gain_grad_ref, shift_grad_ref, inner_grad_ref, outer_grad_ref = refs[6:11]
    travel_refs = refs[11:15]
    blocks, sems, normed_turned, branch_turned, branch, inner_all, total = refs[15:]
    step = pl.program_id(0)
    items, _, width = x_ref.shape
    section, core = info[items], info[items + 1]

    @pl.when(step == 0)
    def _():
        start_weights(info, items, weights, plan, blocks, sems)
        outer = None
        for item in range(items):
            here = slice(item * count, (item + 1) * count)
            unit, _ = norm_parts(x_ref[item, :count].astype(BF16).astype(F32))
            normed = (unit * gain_ref[...] + shift_ref[...]).astype(BF16)
            row_true = true_positions(info[item], 0, count, 0, kind)
            incoming = grad_ref[item, :count].astype(F32)
            masked = jnp.where(row_true, incoming, 0.0).astype(BF16)
            branch[here] = masked
            store_turned(normed_turned, normed.T, here, section, core)
            store_turned(branch_turned, masked.T, here, section, core)
            term = column_sum(masked)
            outer = term if outer is None else outer + term
        outer_grad_ref[...] = outer

    wait_block(blocks, step, sems)
    wait_block(blocks, step + 4, sems)
    for at in range(0, width, 256):
        columns = slice(at, at + 256)
        act_grad = dot_last(branch[...], blocks[step + 4, columns])
        inner = (slope_ref[:, columns].astype(F32) * act_grad).astype(BF16)
        inner_all[:, columns] = inner
        inner_grad_ref[:, columns] = column_sum(inner)
        put_travel(travel_refs, 0, columns, normed_turned, inner)
        put_travel(travel_refs, 1, columns, branch_turned, act_ref[:, columns])
    part = dot_last(inner_all[...], blocks[step])

    @pl.when(step == 0)
    def _():
        total[...] = part

    @pl.when(step > 0)
    def _():
        total[...] += part

    @pl.when(step == pl.num_programs(0) - 1)
    def _():
        gain_sum, shift_sum = None, None
        for item in range(items):
            unit, scale = norm_parts(x_ref[item, :count].astype(BF16).astype(F32))
            normed_grad = total[item * count : (item + 1) * count]
            gain_part = jnp.sum(normed_grad * unit, axis=0, keepdims=True)
            shift_part = jnp.sum(normed_grad, axis=0, keepdims=True)
            gain_sum = gain_part if gain_sum is None else gain_sum + gain_part
            shift_sum = shift_part if shift_sum is None else shift_sum + shift_part
            incoming = grad_ref[item, :count].astype(F32)
            hidden = incoming + norm_back(normed_grad, unit, scale, gain_ref[...])
            out_ref[item, :count] = hidden.astype(BF16)
            if count < ROWS:
                out_ref[item, count:] = grad_ref[item, count:]
        gain_grad_ref[...] = gain_sum
        shift_grad_ref[...] = shift_sum


def shared_forward_kernel(*refs):
    *rows_refs, inputs_ref, inner_ref, outputs_ref = refs[:7]
    *part_refs, normed, total = refs[7:]
    count = rows_refs[0].shape[0]
    step = pl.program_id(0)

    @pl.when(step == 0)
    def _():
        for index, ref in enumerate(rows_refs):
            normed[index * count : (index + 1) * count] = ref[...]
        total[...] = jnp.zeros_like(total)

    act, _ = inner_forward(normed[...], inputs_ref[...], inner_ref[...])
    total[...] += dot_plain(act, outputs_ref[...])

    @pl.when(step == pl.num_programs(0) - 1)
    def _():
        for index, ref in enumerate(part_refs):
            ref[...] = total[index * count : (index + 1) * count].astype(BF16)


def shared_backward_kernel(plan, weight_count, info, *refs):
    weights, refs = refs[:weight_count], refs[weight_count:]
    rows_refs, grad_refs, inner_ref = refs[:4], refs[4:8], refs[8]
    part_refs, (keep_ref, send_ref, inner_grad_ref, outer_grad_ref) = refs[9:13], refs[13:17]
    blocks, sems, normed, branch, matrix = refs[17:]
    count, width = rows_refs[0].shape
    half = width // 2
    first = info.shape[0] - 3
    core = info[first + 1]
    start_weights(info, first, weights, plan, blocks, sems)
    for index in range(SECTIONS):
        here = slice(index * count, (index + 1) * count)
        normed[here] = rows_refs[index][...]
        branch[here] = grad_refs[index][...]
    outer_grad_ref[...] = column_sum(grad_refs[0][...])
    wait_block(blocks, 0, sems)
    wait_block(blocks, 1, sems)
    part = None
    for at in range(0, width, 256):
        columns = slice(at, at + 256)
        act, slope = inner_forward(normed[...], blocks[0, :, columns], inner_ref[:, columns])
        act_grad = dot_last(branch[...], blocks[1, columns])
        inner = (slope.astype(F32) * act_grad).astype(BF16)
        inner_grad_ref[:, columns] = column_sum(inner)
        matrix[0, :, columns] = dot_first(normed[...], inner).astype(BF16)
        matrix[1, :, columns] = dot_first(branch[...], act).astype(BF16)
        term = dot_last(inner, blocks[0, :, columns])
        part = term if part is None else part + term
    for index, ref in enumerate(part_refs):
        ref[...] = part[index * count : (index + 1) * count].astype(BF16)
    quarter = half // 4
    for which in range(2):
        for group in range(4):
            columns = slice(group * width, (group + 1) * width)
            mine = pl.multiple_of(core * half, 16) + group * quarter
            other = pl.multiple_of((1 - core) * half, 16) + group * quarter
            keep_ref[which, :, columns] = matrix[which, pl.ds(pl.multiple_of(mine, 16), quarter)]
            send_ref[which, :, columns] = matrix[which, pl.ds(pl.multiple_of(other, 16), quarter)]


def chunk_columns(rows, width):
    return pl.BlockSpec((rows, width), lambda step, info: (0, step))


def expert_forward(x, info, weights, gain, shift, inner, outer, count, kind):
    arrays, plan = weights
    items, _, width = x.shape
    hidden = inner.shape[1]
    row = whole_block((1, width))
    return pl.pallas_call(
        partial(expert_forward_kernel, plan, len(arrays), count, kind),
        grid_spec=pltpu.PrefetchScalarGridSpec(
            num_scalar_prefetch=1,
            grid=(hidden // width,),
            in_specs=[ANYWHERE] * len(arrays)
            + [whole_block(x.shape), row, row, chunk_columns(1, width), row],
            out_specs=[
                whole_block((items, ROWS, width)),
                chunk_columns(items * count, width),
                chunk_columns(items * count, width),
            ],
            scratch_shapes=blocks_scratch(8, width)
            + [
                pltpu.VMEM((items * count, width), BF16),
                pltpu.VMEM((items * count, width), F32),
            ],
        ),
        out_shape=[
            jax.ShapeDtypeStruct((items, ROWS, width), BF16),
            jax.ShapeDtypeStruct((items * count, hidden), BF16),
            jax.ShapeDtypeStruct((items * count, hidden), BF16),
        ],
        compiler_params=pltpu.CompilerParams(vmem_limit_bytes=VMEM_BYTES),
        cost_estimate=SHORT,
        name="expert_forward_" + kind,
    )(info, *arrays, x, gain, shift, inner, outer)


def expert_backward(x, info, weights, gain, shift, act, slope, incoming, count, kind):
    arrays, plan = weights
    items, _, width = x.shape
    half = width // 2
    hidden = act.shape[1]
    row = whole_block((1, width))
    travel = pl.BlockSpec((2, half // 2, width), lambda step, info: (0, 0, step))
    return pl.pallas_call(
        partial(expert_backward_kernel, plan, len(arrays), count, kind),
        grid_spec=pltpu.PrefetchScalarGridSpec(
            num_scalar_prefetch=1,
            grid=(hidden // width,),
            in_specs=[ANYWHERE] * len(arrays)
            + [
                whole_block(x.shape),
                row,
                row,
                chunk_columns(items * count, width),
                chunk_columns(items * count, width),
                whole_block(incoming.shape),
            ],
            out_specs=[whole_block(incoming.shape), row, row, chunk_columns(1, width), row]
            + [travel] * 4,
            scratch_shapes=blocks_scratch(8, width)
            + [
                pltpu.VMEM((width, items * count), BF16),
                pltpu.VMEM((width, items * count), BF16),
                pltpu.VMEM((items * count, width), BF16),
                pltpu.VMEM((items * count, width), BF16),
                pltpu.VMEM((items * count, width), F32),
            ],
        ),
        out_shape=[
            jax.ShapeDtypeStruct(incoming.shape, BF16),
            jax.ShapeDtypeStruct((1, width), F32),
            jax.ShapeDtypeStruct((1, width), F32),
            jax.ShapeDtypeStruct((1, hidden), F32),
            jax.ShapeDtypeStruct((1, width), F32),
        ]
        + [jax.ShapeDtypeStruct((2, half // 2, hidden), BF16)] * 4,
        compiler_params=pltpu.CompilerParams(vmem_limit_bytes=VMEM_BYTES),
        cost_estimate=SHORT,
        name="expert_backward_" + kind,
    )(info, *arrays, x, gain, shift, act, slope, incoming)


IN_VMEM = pl.BlockSpec(memory_space=pltpu.VMEM)
IN_SMEM = pl.BlockSpec(memory_space=pltpu.SMEM)


def shared_forward(rows, inputs, inner, outputs):
    count, width = rows[0].shape
    total = SECTIONS * count
    hidden = inner.shape[1]
    return pl.pallas_call(
        shared_forward_kernel,
        grid=(hidden // width,),
        in_specs=[pl.BlockSpec(rows[0].shape, lambda step: (0, 0))] * 4
        + [
            pl.BlockSpec((width, width), lambda step: (0, step)),
            pl.BlockSpec((1, width), lambda step: (0, step)),
            pl.BlockSpec((width, width), lambda step: (step, 0)),
        ],
        out_specs=[pl.BlockSpec((count, width), lambda step: (0, 0))] * SECTIONS,
        scratch_shapes=[pltpu.VMEM((total, width), BF16), pltpu.VMEM((total, width), F32)],
        out_shape=[jax.ShapeDtypeStruct((count, width), BF16)] * SECTIONS,
        compiler_params=pltpu.CompilerParams(vmem_limit_bytes=VMEM_BYTES),
        cost_estimate=SHORT,
        name="shared_forward",
    )(*rows, inputs, inner, outputs)


def shared_backward(rows, grads, info, weights, inner):
    arrays, plan = weights
    count, width = rows[0].shape
    total = SECTIONS * count
    travel = (2, width // 8, 4 * width)
    return pl.pallas_call(
        partial(shared_backward_kernel, plan, len(arrays)),
        in_specs=[IN_SMEM] + [ANYWHERE] * len(arrays) + [IN_VMEM] * 9,
        out_specs=[IN_VMEM] * 8,
        scratch_shapes=blocks_scratch(2, width)
        + [
            pltpu.VMEM((total, width), BF16),
            pltpu.VMEM((total, width), BF16),
            pltpu.VMEM((2, width, width), BF16),
        ],
        out_shape=[
            *[jax.ShapeDtypeStruct((count, width), BF16)] * SECTIONS,
            jax.ShapeDtypeStruct(travel, BF16),
            jax.ShapeDtypeStruct(travel, BF16),
            jax.ShapeDtypeStruct((1, width), F32),
            jax.ShapeDtypeStruct((1, width), F32),
        ],
        compiler_params=pltpu.CompilerParams(vmem_limit_bytes=VMEM_BYTES),
        cost_estimate=SHORT,
        name="shared_backward",
    )(info, *arrays, *rows, *grads, inner)


def plane_turn(plane, planes):
    return ((plane & 1) << 1) | (plane >> 1) if planes == 4 else 0


def finish_kernel(planes, info, scale_ref, *refs):
    step = pl.program_id(0)
    mine, theirs, outs, placed = refs[:4], refs[4:8], refs[8:-1], refs[-1]
    count = mine[0].shape[0]
    width = placed.shape[1]
    half = width // 2
    at = info.shape[0] - 3
    section, core = info[at], info[at + 1]
    turn = plane_turn(info[at + 2], planes)
    turned = turn if count == 1 else jnp.where(section == 1, turn, 0)
    scale = scale_ref[0, 0]
    columns = pl.ds(pl.multiple_of((step ^ turned) * width, width), width)

    def place(which):
        def by_rows():
            for side, pieces in enumerate((mine, theirs)):
                for away, ref in enumerate(pieces):
                    for path in range(2):
                        row = (core ^ side) * half + path * (half // 2)
                        row = row + (section ^ away) * PIECE_ROWS
                        placed[pl.ds(pl.multiple_of(row, 16), PIECE_ROWS), :] = ref[
                            which, path * PIECE_ROWS : (path + 1) * PIECE_ROWS, columns
                        ].astype(F32)

        def by_columns():
            for side, pieces in enumerate((mine, theirs)):
                for away, ref in enumerate(pieces):

                    @pl.when(step == away)
                    def _(side=side, ref=ref):
                        for group in range(4):
                            quarter = half // 4
                            row = (core ^ side) * half + group * quarter
                            placed[pl.ds(pl.multiple_of(row, 16), quarter), :] = ref[
                                which, :, group * width : (group + 1) * width
                            ].astype(F32)

        if count == 1:
            by_rows()
        else:
            pl.when(section != 0)(by_rows)
            pl.when(section == 0)(by_columns)

    place(0)
    if count == 1:

        @pl.when(step < 3)
        def _():
            outs[0][0] = placed[...] / scale

        @pl.when(step == 3)
        def _():
            outs[1][0] = placed[...] / scale

    else:
        outs[0][0] = placed[...] / scale
        place(1)
        outs[1][0] = (placed[...] / scale).T


def finish(info, scale, mine, theirs, planes):
    count, _, hidden = mine[0].shape
    width = hidden // 4
    if count == 1:
        shapes = [(1, width, 3 * width), (1, width, width)]
        maps = [lambda step, info: (0, 0, jnp.minimum(step, 2)), lambda step, info: (0, 0, 0)]
    else:
        shapes = [(1, width, hidden), (1, hidden, width)]
        maps = [lambda step, info: (0, 0, step), lambda step, info: (0, step, 0)]
    return pl.pallas_call(
        partial(finish_kernel, planes),
        grid_spec=pltpu.PrefetchScalarGridSpec(
            num_scalar_prefetch=1,
            grid=(4,),
            in_specs=[IN_SMEM] + [whole_block(mine[0].shape)] * 8,
            out_specs=[pl.BlockSpec((1, width, width), at) for at in maps],
            scratch_shapes=[pltpu.VMEM((width, width), F32)],
        ),
        out_shape=[jax.ShapeDtypeStruct(shape, F32) for shape in shapes],
        compiler_params=pltpu.CompilerParams(vmem_limit_bytes=VMEM_BYTES),
        cost_estimate=SHORT,
        name="finish",
    )(info, scale, *mine, *theirs)


def pack_kernel(count, plan, info, *refs):
    sources, outs, sems = refs[:count], refs[count:-1], refs[-1]
    first = info.shape[0] - 3
    section, core, plane = info[first], info[first + 1], info[first + 2]
    half = outs[0].shape[1]
    for index, (out, choices) in enumerate(zip(outs, plan)):
        for at, at_plane, parts in choices:
            here = section == at
            if at_plane is not None:
                here = here & (plane == at_plane)

            @pl.when(here)
            def _(index=index, out=out, parts=parts):
                for block, part in enumerate(parts):
                    if part[0] == "own":
                        _, which, row, column = part
                        rows = pl.ds(pl.multiple_of(row + core * half, half), half)
                        source = sources[which].at[rows, pl.ds(column, out.shape[2])]
                    else:
                        source = sources[part[1]].at[block]
                    pltpu.make_async_copy(source, out.at[block], sems.at[index, block]).start()

    for index, out in enumerate(outs):
        for block in range(2):
            pltpu.make_async_copy(out.at[block], out.at[block], sems.at[index, block]).wait()


def pack(info, sources, plan, shape):
    return pl.pallas_call(
        partial(pack_kernel, len(sources), plan),
        in_specs=[IN_SMEM] + [ANYWHERE] * len(sources),
        out_specs=[IN_VMEM] * len(plan),
        scratch_shapes=[pltpu.SemaphoreType.DMA((len(plan), 2))],
        out_shape=[jax.ShapeDtypeStruct(shape, BF16)] * len(plan),
        cost_estimate=SHORT,
        name="pack",
    )(info, *sources)


def over_section(value, bits, sources=range(SECTIONS)):
    return lax.ppermute(value, "section", [(at, at ^ bits) for at in sources])


def over_core(value):
    return lax.ppermute(value, "core", [(0, 1), (1, 0)])


def over_plane(value, pairs):
    return lax.ppermute(value, "z", pairs)


def added(left, right):
    return (left.astype(F32) + right.astype(F32)).astype(BF16)


def after(value, *earlier):
    return lax.optimization_barrier((value,) + earlier)[0]


def under(outputs, *arrivals):
    joined = lax.optimization_barrier(tuple(outputs) + arrivals)
    return list(joined[: len(outputs)]), list(joined[len(outputs) :])


def by_section(section, values):
    result, last = None, None
    for at in sorted(values):
        if result is None:
            result = values[at]
        elif values[at] is not last:
            result = jnp.where(section >= at, values[at], result)
        last = values[at]
    return result


def total(*values):
    result = values[0].astype(F32)
    for value in values[1:]:
        result = result + value.astype(F32)
    return result.astype(BF16)


class Sums:
    def __init__(self, travel):
        self.stay, self.move, self.other_stay, self.other_move = travel
        self.size = self.stay.shape[1] // 2

    def cross(self, *earlier):
        if earlier:
            self.other_move = after(self.other_move, *earlier)
            self.other_stay = after(self.other_stay, *earlier)
        self.got_move, self.got_stay = over_core(self.other_move), over_core(self.other_stay)

    def first_sends(self):
        size = self.size
        self.sent = [
            total(self.move[:, at : at + size], self.got_move[:, at : at + size])
            for at in (0, size)
        ]
        return self.sent

    def second_sends(self, from_x, from_y):
        size, half = self.size, self.size // 2
        self.first = from_x, from_y
        to_y = total(self.stay[:, half:size], self.got_stay[:, half:size], from_x[:, half:])
        to_x = total(
            self.stay[:, size + half :], self.got_stay[:, size + half :], from_y[:, half:]
        )
        self.sent = [to_x, to_y]
        return self.sent

    def whole(self, from_x, from_y):
        size, half = self.size, self.size // 2
        parts = []
        for at, first, second in ((0, self.first[0], from_y), (size, self.first[1], from_x)):
            here = slice(at, at + half)
            parts.append(total(self.stay[:, here], self.got_stay[:, here], first[:, :half], second))
        return jnp.concatenate(parts, axis=1)


def over_links(sends):
    return [over_section(sends[0], 1), over_section(sends[1], 2)]


class Planes:
    def __init__(self, value, plane, planes):
        self.value, self.plane, self.planes, self.turn = value, plane, planes, 0

    def sends(self, *earlier):
        value = after(self.value, *earlier) if earlier else self.value
        if self.planes != 4:
            return (value,)
        bits = (1, 2, 2, 1)[self.turn]
        if self.turn < 2:
            bit = (self.plane & 1, self.plane >> 1)[self.turn]
            size = value.shape[-1] // 2
            value = lax.dynamic_slice_in_dim(value, (1 - bit) * size, size, value.ndim - 1)
        return (over_plane(value, [(at, at ^ bits) for at in range(4)]),)

    def take(self, arrived):
        if self.planes != 4:
            self.value = lax.psum(arrived, "z") if self.turn == 3 else arrived
        elif self.turn < 2:
            bit = (self.plane & 1, self.plane >> 1)[self.turn]
            size = self.value.shape[-1] // 2
            keep = lax.dynamic_slice_in_dim(self.value, bit * size, size, self.value.ndim - 1)
            self.value = added(keep, arrived)
        else:
            self.value = jnp.concatenate([self.value, arrived], axis=-1)
        self.turn += 1

    def in_order(self, value):
        if self.planes != 4:
            return value
        size, turn = value.shape[-1] // 4, plane_turn(self.plane, 4)
        parts = [
            lax.dynamic_slice_in_dim(value, (at ^ turn) * size, size, value.ndim - 1)
            for at in range(4)
        ]
        return jnp.concatenate(parts, axis=-1)


class Weights:
    def __init__(self, own, info, planes):
        self.own, self.info = own, info
        self.four = planes == 4
        self.plan = PLAN_FOUR if self.four else PLAN_ANY
        self.half, self.width = own[1].shape[0] // 2, own[1].shape[1]
        self.mine, self.theirs, self.arrived = {}, {}, {}

    def place(self, layer, block):
        if layer in "ac":
            return (0, 0, block * self.width) if block < 3 else (1, 0, 0)
        if layer == "g":
            return (2, 0, block * self.width) if block < 4 else (3, (block - 4) * self.width, 0)
        return (2, 0, block * self.width) if block < 4 else (3, (block - 4) * self.width, 0)

    def choices(self, sends, sources):
        result = []
        for at in range(SECTIONS):
            name = sends.get(at)
            if name is not None and HOMES[name[0]] != at:
                key = self.arrived[at, name]
                if key not in sources:
                    sources[key] = len(self.own) + len(sources)
                result.append((at, None, [("arrived", sources[key])] * 2))
                continue
            for plane in range(4) if name == "F" else (None,):
                piece = ("f" + str(plane)) if name == "F" else name or "a0"
                layer, index = piece[0], int(piece[1])
                if layer in "ac":
                    blocks = ATTEND_BLOCKS[index]
                else:
                    blocks = (index, 4 + index) if layer == "g" else EXPERT_BLOCKS[index]
                parts = [("own",) + self.place(layer, block) for block in blocks]
                result.append((at, plane, parts))
        return result

    def packed(self, wanted):
        sources = {}
        plan = [self.choices(sends, sources) for sends in wanted]
        arrays = list(self.own) + [self.mine[key] for key in sources]
        return pack(self.info, arrays, plan, (2, self.half, self.width))

    def sends(self, step):
        if step == "F":
            return [{at: "F" for at in range(SECTIONS)}]
        return [sends for sends in self.plan[step] if sends]

    def payloads(self, *steps):
        wanted = [sends for step in steps for sends in self.sends(step)]
        return list(self.packed(wanted))

    def move(self, step, payloads):
        links = [(link, sends) for link, sends in enumerate(self.plan[step]) if sends]
        for (link, sends), payload in zip(links, payloads):
            self.mine[step, link] = over_section(payload, link + 1, sorted(sends))
            for at, name in sends.items():
                self.arrived[at ^ (link + 1), name] = (step, link)
        return [(step, link) for link, _ in links]

    def move_planes(self, step):
        up, down = self.mine["plane", step - 1], self.mine["plane", 1 - step]
        up = over_plane(up, [(at, at + 1) for at in range(step - 1, 3)])
        down = over_plane(down, [(at, at - 1) for at in range(4 - step, 0, -1)])
        self.mine["plane", step], self.mine["plane", -step] = up, down
        return [("plane", step), ("plane", -step)]

    def cross(self, keys):
        for key in keys:
            self.theirs[key] = over_core(self.mine[key])
        return keys

    def join(self, outputs, mine=(), theirs=()):
        values = [self.mine[key] for key in mine] + [self.theirs[key] for key in theirs]
        outputs, values = under(outputs, *values)
        for key, value in zip(mine, values):
            self.mine[key] = value
        for key, value in zip(theirs, values[len(mine) :]):
            self.theirs[key] = value
        return outputs

    def layer(self, layer):
        arrays, places = list(self.own), {}

        def place(key):
            if key not in places:
                places[key] = len(arrays)
                arrays.extend([self.mine[key], self.theirs[key]])
            return places[key], places[key] + 1

        if layer in "ac":
            names = [(layer + str(index), ATTEND_BLOCKS[index]) for index in range(2)]
        else:
            names = [(layer + str(index), EXPERT_BLOCKS[index]) for index in range(4)]
        plan = []
        for at in range(SECTIONS):
            if layer == "g":
                names = [("g" + str(at), (0, 1))]
            if HOMES[layer] == at:
                steps = []
                for name, blocks in names:
                    for block in blocks:
                        source = block * 4 if layer == "g" else block
                        steps.append((block, ("own",) + self.place(layer, source)))
                plan.append((at, None, steps))
                continue
            by_plane = layer == "f" and self.four
            for plane in range(4) if by_plane else (None,):
                steps = []
                for index, (name, blocks) in enumerate(names):
                    key = ("plane", plane - index) if by_plane else self.arrived[at, name]
                    for which, block in enumerate(blocks):
                        steps.append((block, ("piece",) + place(key) + (which,)))
                plan.append((at, plane, steps))
        return arrays, plan


def per_device(
    tokens,
    caption_lengths,
    attend_gain,
    attend_shift,
    attend_inputs,
    attend_bias,
    attend_output,
    expert_gain,
    expert_shift,
    expert_inputs,
    expert_inner_bias,
    expert_outputs,
    expert_outer_bias,
    cotangent,
):
    section, core, plane = lax.axis_index("section"), lax.axis_index("core"), lax.axis_index("z")
    planes = lax.axis_size("z")
    items, positions, width = tokens.shape
    hidden = expert_inputs.shape[-1]
    info = [value.reshape(1).astype(jnp.int32) for value in (section, core, plane)]
    info = jnp.concatenate([caption_lengths] + info)
    weights = Weights(
        (attend_inputs[0], attend_output[0], expert_inputs[0], expert_outputs[0]), info, planes
    )

    def to_sections(value):
        return [value] + [over_section(value, bits) for bits in (1, 2, 3)]

    def items_of(part):
        return part.reshape(items, CAP_ROWS, width)

    keys = weights.move(0, weights.payloads(0))
    pad = ((0, 0), (0, ROWS - positions), (0, 0))
    x0 = jnp.pad(tokens, pad)
    last_grad = jnp.pad(cotangent, pad)
    rows = jnp.concatenate(
        [
            attend_gain,
            attend_shift,
            attend_bias,
            expert_gain,
            expert_shift,
            expert_inner_bias,
            expert_outer_bias,
            jnp.full((1, 128), jnp.sum(caption_lengths), F32),
        ],
        axis=1,
    )
    rows = to_sections(rows)
    x0, last_grad, *rows = weights.join([x0, last_grad, *rows], keys)
    keys1 = weights.move(1, weights.payloads(1))
    rows = jnp.concatenate(rows, axis=0)
    language_count = jnp.sum(rows[:, -128:], axis=0, keepdims=True)
    rows = [lax.dynamic_index_in_dim(rows, at ^ section, 0) for at in range(SECTIONS)]
    sizes = [width, width, 3 * width, width, width, hidden, width]
    ends = [sum(sizes[: at + 1]) for at in range(len(sizes))]
    used = [(0, 0), (0, 1), (0, 2), (0, 3), (0, 4), (0, 5), (1, 3), (1, 4), (1, 5), (1, 6)]
    used += [(0, 6), (2, 0), (2, 1), (2, 2), (3, 3), (3, 4), (3, 5), (3, 6)]
    kept = [rows[slot][:, ends[which] - sizes[which] : ends[which]] for slot, which in used]
    language_count, *kept = weights.join([language_count, *kept], keys1)
    kept = dict(zip(used, kept))

    def row(slot, which):
        return kept[slot, which]

    crossed = weights.cross(keys + keys1)
    sends = weights.payloads(2, "F") if weights.four else weights.payloads(2)
    sends, (info, language_count) = under(sends, info, language_count)
    keys = weights.move(2, sends[:2])
    info, language_count = weights.join(
        [info, language_count + over_core(language_count)], theirs=crossed
    )
    plane_keys = []
    if weights.four:
        weights.mine["plane", 0] = sends[2]
        plane_keys = weights.move_planes(1)
    attend0 = weights.layer("a")
    outputs = attend_forward(
        x0, info, attend0, row(0, 0), row(0, 1), row(0, 2), following=(row(0, 3), row(0, 4))
    )
    y0, qkv0, mixed0, caption_rows = weights.join(outputs, keys)
    caption_rows = to_sections(caption_rows.reshape(-1, width))
    sends = weights.payloads(3, 4) if weights.four else weights.payloads(3)
    caption_rows = weights.join(caption_rows, plane_keys)
    sends, caption_rows = under(sends, *caption_rows)
    early_keys = keys
    keys, sends = weights.move(3, sends[:2]), sends[2:]
    crossed = weights.cross(early_keys)
    if weights.four:
        keys += weights.move_planes(2)
    outputs = shared_forward(caption_rows, expert_inputs[0], expert_inner_bias, expert_outputs[0])
    part = weights.join(outputs, keys, crossed)
    (y0,) = weights.join([y0], theirs=weights.cross([(3, 0), (3, 1)]))
    branch = {at: over_section(part[at], at, [0]) for at in range(1, SECTIONS)}
    keys = weights.move_planes(3) if weights.four else []
    expert1 = weights.layer("e")
    outputs = expert_forward(
        y0, info, expert1, row(1, 3), row(1, 4), row(1, 5), row(1, 6), PATCH_ROWS, "patch"
    )
    outputs, moved = under(outputs, *branch.values())
    if weights.four:
        keys += [("plane", step) for step in range(-2, 3)]
    x2, act1, slope1 = weights.join(outputs, keys)
    branch = dict(zip(branch, moved))
    branch[0] = part[0]
    branch = items_of(by_section(section, branch))
    if weights.four:
        crossed = [("plane", step) for step in range(-3, 4)]
    else:
        for step in (4, 5):
            weights.move(step, weights.payloads(step))
        crossed = [(4, 0), (4, 1), (5, 0)]
    weights.cross(crossed)
    attend2 = weights.layer("c") if weights.four else None
    if not weights.four:
        (x2,) = weights.join([x2], theirs=crossed)
        attend2 = weights.layer("c")
    outputs = attend_forward(
        x2, info, attend2, row(2, 0), row(2, 1), row(2, 2), merge=(y0, branch, row(0, 6))
    )
    if weights.four:
        language_count += over_plane(language_count, [(at, at ^ 1) for at in range(4)])
    x3, qkv2, mixed2, x2, language_count = weights.join([*outputs, language_count], theirs=crossed)
    if weights.four:
        language_count += over_plane(language_count, [(at, at ^ 2) for at in range(4)])
    else:
        language_count = lax.psum(language_count, "z")
    expert3 = weights.layer("f")
    outputs = expert_forward(
        x3, info, expert3, row(3, 3), row(3, 4), row(3, 5), row(3, 6), ROWS, "all"
    )
    layer_output, act3, slope3, language_count = under([*outputs, language_count])[0]
    language_count = language_count[0, 0].astype(jnp.int32)
    vision_count = PATCHES * items * SECTIONS * 2 * planes
    counts = jnp.stack(
        [jnp.full((), vision_count, jnp.int32), language_count, language_count + vision_count]
    )

    def small_rows(values):
        flat = jnp.concatenate(values, axis=1)
        count = -(-flat.shape[1] // hidden)
        flat = jnp.pad(flat, ((0, 0), (0, count * hidden - flat.shape[1])))
        return flat.reshape(count, hidden)

    def to_home(sums, diagonal_last=False):
        got = [by_section(section, sums)]
        for bits in (1, 2, 3):
            sends = {at ^ bits: sums[at] for at in sums}
            payload = by_section(section, sends)
            if bits == 3 and diagonal_last:
                payload = after(payload, got[2])
            got.append(over_section(payload, bits, sorted(sends)))
        return got

    keys = []
    if weights.four:
        sends, (layer_output, last_grad) = under(sends, layer_output, last_grad)
        keys = weights.move(4, sends)
    outputs = expert_backward(
        x3, info, expert3, row(3, 3), row(3, 4), act3, slope3, last_grad, ROWS, "all"
    )
    outputs = weights.join(outputs, keys)
    crossed = weights.cross(keys)
    grad3, *small3 = outputs[:5]
    sums3 = Sums(outputs[5:])
    sums3.cross()
    moved = over_links(sums3.first_sends())
    grad3 = after(grad3, *sums3.sent)
    outputs = attend_backward(
        x2, info, attend2, row(2, 0), row(2, 1), qkv2, mixed2, grad3
    )
    outputs, moved = under(outputs, *moved, sums3.got_stay)
    outputs = weights.join(outputs, theirs=crossed)
    grad2, *small2 = outputs[:4]
    sums2, caption_grad = Sums(outputs[4:8]), outputs[8]
    caption_grads = to_sections(caption_grad.reshape(-1, width))
    sums3.got_stay = moved[2]
    moved3 = over_links(sums3.second_sends(*moved[:2]))
    grad2 = after(grad2, *sums3.sent)
    outputs = expert_backward(
        y0, info, expert1, row(1, 3), row(1, 4), act1, slope1, grad2, PATCH_ROWS, "patch"
    )
    outputs, caption_grads = under(outputs, *caption_grads)
    grad1, *small1 = outputs[:5]
    sums2.cross(grad1)
    sums1 = Sums(outputs[5:])
    sums1.cross()
    inner_quarter = lax.dynamic_slice(row(0, 5), (0, section * width), (1, width))
    sum3 = sums3.whole(*moved3)
    inner_quarter = after(inner_quarter, grad1, sum3)
    outputs = shared_backward(
        caption_rows, caption_grads, info, weights.layer("g"), inner_quarter
    )
    parts, (keep0, send0, inner_grad, outer_grad) = outputs[:4], outputs[4:]
    got = [over_section(parts[bits], bits) for bits in (1, 2, 3)]
    sends = [after(value, *parts) for value in sums1.first_sends()]
    moved1 = over_links(sends)
    keep0 = added(keep0, over_core(send0))
    early = lax.psum(jnp.concatenate([sum3, keep0], axis=0), "z")
    sends2 = [after(value, *sends) for value in sums2.first_sends()]
    moved2 = over_links(sends2)
    parts = [parts[0], *got]
    grad1 = after(grad1, keep0, *sends, *sends2)
    outputs = attend_backward(
        x0,
        info,
        attend0,
        row(0, 0),
        row(0, 1),
        qkv0,
        mixed0,
        grad1,
        first=(y0, row(0, 3), parts),
    )
    outputs, moved = under(outputs, *moved2, *moved1)
    moved2, moved1 = moved[:2], moved[2:]
    tokens_grad, *small_first = outputs[:4]
    sums_first, gain_grad, shift_grad = Sums(outputs[4:8]), outputs[8], outputs[9]
    sums_first.cross()
    inner_grad = lax.dynamic_update_slice(
        jnp.zeros((1, hidden), F32), inner_grad, (0, section * width)
    )
    small = small_rows(
        small_first + [gain_grad, shift_grad, inner_grad, outer_grad] + small2 + small1 + small3
    )
    small = added(small, over_core(small))
    to_x, to_y = sums_first.first_sends()
    to_x = jnp.concatenate([to_x[0], small], axis=0)
    sends = lax.optimization_barrier((*sums1.second_sends(*moved1), to_x, to_y))
    moved1, moved = over_links(sends[:2]), over_links(sends[2:])
    sum1, early = lax.optimization_barrier((sums1.whole(*moved1), early))
    planes1 = Planes(sum1, plane, planes)
    size = to_y.shape[1]
    small = added(small, moved[0][size:])
    to_x, to_y = sums_first.second_sends(moved[0][None, :size], moved[1])
    early_x, early_y = sums2.second_sends(*moved2)
    to_x = jnp.concatenate([to_x[0], early_x[0]], axis=0)
    to_y = jnp.concatenate([to_y[0], early_y[0], small], axis=0)
    to_x, to_y = lax.optimization_barrier((to_x, to_y))
    sent1 = planes1.sends()
    moved = lax.optimization_barrier(tuple(over_links((to_x, to_y))))
    size = early_x.shape[1]
    last = sums_first.whole(moved[0][None, :size], moved[1][None, :size])
    sum2 = sums2.whole(moved[0][None, size:], moved[1][None, size : 2 * size])
    small = added(small, moved[1][2 * size :])
    small_count = small.shape[0]
    eighth = last.shape[1]
    last = jnp.concatenate([last[0], sum2[0], small], axis=0)
    planes_last = Planes(last, plane, planes)
    home_early = to_home({0: after(early[2:], *moved), 3: after(early[:2], *moved)}, diagonal_last=True)
    planes_last.take(*planes_last.sends())
    planes1.take(*sent1)
    planes1.take(*planes1.sends())
    planes1.take(*planes1.sends())
    planes1.take(*planes1.sends())
    planes_last.take(*planes_last.sends())
    planes_last.take(*planes_last.sends())
    home_late = to_home({1: after(planes1.value, *home_early[1:3])})
    planes_last.take(*planes_last.sends())
    last = planes_last.value
    home_attend = to_home({0: last[None, :eighth], 2: last[None, eighth : 2 * eighth]})
    small = planes_last.in_order(last[2 * eighth :].astype(F32))

    as_float = counts.astype(F32)
    one = jnp.ones((), F32)
    attend_scales = jnp.stack([as_float[2], one, as_float[2], one])
    expert_scales = jnp.stack([as_float[1], as_float[0], one, as_float[2]])

    def placed(pieces, scales, *earlier):
        scale = lax.dynamic_index_in_dim(scales, section, 0).reshape(1, 1)
        theirs = []
        for piece in pieces:
            theirs.append(over_core(after(piece, theirs[-1]) if theirs else piece))
        if earlier:
            scale = after(scale, *earlier)
        return finish(info, scale, pieces, theirs, planes)

    blank = jnp.zeros_like(home_late[0])
    inputs_whole, outputs_whole = placed(
        [
            by_section(section, {0: early, 1: late, 2: blank, 3: early})
            for early, late in zip(home_early, home_late)
        ],
        expert_scales,
    )
    blank = jnp.zeros_like(home_attend[0])
    attend_whole, output_whole = placed(
        [by_section(section, {0: got, 1: blank, 2: got, 3: blank}) for got in home_attend],
        attend_scales,
        inputs_whole,
    )

    attend_size, expert_size = 5 * width, 3 * width + hidden
    cuts = [attend_size, attend_size + expert_size]
    cuts += [cuts[1] + attend_size, cuts[1] + attend_size + expert_size]
    small = jnp.split(small.reshape(-1)[: cuts[3] + expert_size], cuts)
    none_attend, none_expert = jnp.zeros_like(small[0]), jnp.zeros_like(small[1])
    attend_small = jnp.stack([small[0], none_attend, small[2], none_attend])
    expert_small = jnp.stack([small[1], small[3], none_expert, small[4]])
    attend_small = attend_small / attend_scales.reshape(-1, 1)
    expert_small = expert_small / expert_scales.reshape(-1, 1)
    attend_small = lax.dynamic_index_in_dim(attend_small, section, 0)
    expert_small = lax.dynamic_index_in_dim(expert_small, section, 0)
    return (
        layer_output[:, :positions],
        tokens_grad[:, :positions],
        attend_small[:, :width],
        attend_small[:, width : 2 * width],
        attend_whole,
        attend_small[:, 2 * width :],
        output_whole,
        expert_small[:, :width],
        expert_small[:, width : 2 * width],
        inputs_whole,
        expert_small[:, 2 * width : 2 * width + hidden],
        outputs_whole,
        expert_small[:, 2 * width + hidden :],
        counts,
    )


def solution(mesh):
    sections, groups = mesh.shape["section"], mesh.shape["dp"]
    split = Mesh(mesh.devices.reshape(sections, groups // 2, 2), ("section", "z", "core"))
    items = P(("section", "z", "core"), None, None)
    flat = P("section", None)
    matrix = P("section", None, None)
    placed = (
        items,
        P(("section", "z", "core")),
        flat,
        flat,
        matrix,
        flat,
        matrix,
        flat,
        flat,
        matrix,
        flat,
        matrix,
        flat,
        items,
    )
    return jax.shard_map(
        per_device,
        mesh=split,
        in_specs=placed,
        out_specs=(
            items,
            items,
            flat,
            flat,
            matrix,
            flat,
            matrix,
            flat,
            flat,
            matrix,
            flat,
            matrix,
            flat,
            P(),
        ),
        check_vma=False,
    )
```

```python
from functools import partial

import jax
import jax.numpy as jnp
from jax import lax
from jax.experimental import pallas as pl
from jax.experimental.pallas import tpu as pltpu
from jax.sharding import Mesh
from jax.sharding import PartitionSpec as P

HEADS = 12
HEAD_DIM = 64
PATCHES = 197
ROWS = 256
CAP_FIRST, CAP_ROWS = 192, 48
PATCH_ROWS = 208
PAIR = 2 * HEAD_DIM
SECTIONS = 4
PIECE_ROWS = 48
VMEM_BYTES = 58 * 1024 * 1024
F32 = jnp.float32
BF16 = jnp.bfloat16

PLAN_FOUR = (
    ({0: "a0", 1: "e0", 2: "c0", 3: "F"}, {0: "a1", 1: "e2", 2: "c0", 3: "F"}),
    ({0: "a1", 1: "e1", 2: "a1", 3: "e2"}, {0: "a0", 1: "a0", 2: "F", 3: "c0"}),
    ({0: "g3", 1: "e2", 2: "c1"}, {0: "e0", 1: "e3", 2: "c1"}),
    ({0: "g1", 1: "e3", 2: "e0", 3: "e3"}, {0: "e1", 1: "e1", 3: "c1"}),
    ({}, {0: "g2", 1: "g3"}),
)
PLAN_ANY = (
    ({0: "a0", 1: "e0", 2: "c0", 3: "f0"}, {0: "a1", 1: "e2", 2: "c0", 3: "f0"}),
    ({0: "a1", 1: "e1", 2: "a1", 3: "e2"}, {0: "a0", 1: "a0", 2: "c1", 3: "f1"}),
    ({0: "g3", 1: "e2", 2: "c1", 3: "f1"}, {0: "e0", 1: "e3", 2: "f0", 3: "f2"}),
    ({0: "g1", 1: "e3", 2: "e0", 3: "e3"}, {0: "e1", 1: "e1", 2: "f1", 3: "f3"}),
    ({0: "c1", 1: "f2", 3: "f2"}, {0: "g2", 1: "g3", 3: "c0"}),
    ({1: "f3", 3: "f3"}, {}),
)
HOMES = {"a": 0, "c": 2, "e": 1, "f": 3, "F": 3, "g": 0}
ATTEND_BLOCKS = ((0, 1), (2, 3))
EXPERT_BLOCKS = ((0, 1), (4, 5), (2, 3), (6, 7))


def dot_plain(left, right):
    return jnp.dot(left, right, preferred_element_type=F32)


def dot_last(left, right):
    return lax.dot_general(left, right, (((1,), (1,)), ((), ())), preferred_element_type=F32)


def dot_first(left, right):
    return lax.dot_general(left, right, (((0,), (0,)), ((), ())), preferred_element_type=F32)


def column_sum(matrix):
    return jnp.sum(matrix.astype(F32), axis=0, keepdims=True)


def norm_parts(rows):
    centre = rows - jnp.mean(rows, axis=-1, keepdims=True)
    scale = lax.rsqrt(jnp.mean(centre * centre, axis=-1, keepdims=True) + 1e-06)
    return centre * scale, scale


def norm_back(normed_grad, unit, scale, gain):
    unit_grad = normed_grad * gain
    along = jnp.mean(unit_grad * unit, axis=-1, keepdims=True)
    return scale * (unit_grad - jnp.mean(unit_grad, axis=-1, keepdims=True) - unit * along)


def true_positions(length, first, count, axis, kind):
    shape = (count, 1) if axis == 0 else (1, count)
    position = first + lax.broadcasted_iota(jnp.int32, shape, axis)
    patch = position < PATCHES
    if kind == "patch":
        return patch
    caption = (position >= PATCHES) & (position - PATCHES < length)
    return caption if kind == "caption" else patch | caption


def head_masks():
    lane = lax.broadcasted_iota(jnp.int32, (1, PAIR), 1)
    even = (lane < HEAD_DIM).astype(F32).astype(BF16)
    odd = (lane >= HEAD_DIM).astype(F32).astype(BF16)
    return lane < HEAD_DIM, even, odd


def split_pair(pair, even, odd):
    return jnp.concatenate([pair * even, pair * odd], axis=0)


def start_weights(info, first, refs, plan, blocks, sems):
    half = blocks.shape[1] // 2
    section, core, plane = info[first], info[first + 1], info[first + 2]
    for at, at_plane, steps in plan:
        here = section == at
        if at_plane is not None:
            here = here & (plane == at_plane)

        @pl.when(here)
        def _(steps=steps):
            for block, source in steps:
                if source[0] == "own":
                    _, which, row, column = source
                    width = blocks.shape[2]
                    for part in range(2):
                        pltpu.make_async_copy(
                            refs[which].at[
                                pl.ds(row + part * half, half), pl.ds(column, width)
                            ],
                            blocks.at[block, pl.ds(part * half, half)],
                            sems.at[block],
                        ).start()
                else:
                    _, mine, theirs, index = source
                    pltpu.make_async_copy(
                        refs[mine].at[index],
                        blocks.at[block, pl.ds(pl.multiple_of(core * half, half), half)],
                        sems.at[block],
                    ).start()
                    pltpu.make_async_copy(
                        refs[theirs].at[index],
                        blocks.at[block, pl.ds(pl.multiple_of((1 - core) * half, half), half)],
                        sems.at[block],
                    ).start()


def wait_block(blocks, block, sems):
    pltpu.make_async_copy(blocks.at[block], blocks.at[block], sems.at[block]).wait()


def store_turned(target, turned, columns, section, core):
    half = target.shape[0] // 2
    for piece in range(16):
        path, owner = (piece >> 2) & 1, piece & 3
        away = owner ^ section
        place = ((away & 1) << 1) | (away >> 1) if path == 0 else away
        row = ((piece >> 3) ^ core) * half + (place >> 1) * (half // 2)
        row = row + path * (half // 4) + (place & 1) * PIECE_ROWS
        target[pl.ds(pl.multiple_of(row, 16), PIECE_ROWS), columns] = turned[
            piece * PIECE_ROWS : (piece + 1) * PIECE_ROWS
        ]


def put_travel(refs, which, columns, left, right):
    half = left.shape[0] // 2
    for side in range(2):
        rows = dot_plain(left[side * half : (side + 1) * half], right).astype(BF16)
        refs[2 * side][which, :, columns] = rows[: half // 2]
        refs[2 * side + 1][which, :, columns] = rows[half // 2 :]


def attend_forward_kernel(plan, weight_count, merge, info, *refs):
    weights, refs = refs[:weight_count], refs[weight_count:]
    if merge:
        x_ref, before_ref, part_ref, outer_ref, gain_ref, shift_ref, bias_ref = refs[:7]
        y_ref, qkv_ref, mixed_ref, joined_ref, blocks, sems, joined = refs[7:]
    else:
        x_ref, gain_ref, shift_ref, bias_ref, next_gain_ref, next_shift_ref = refs[:6]
        y_ref, qkv_ref, mixed_ref, caption_ref, blocks, sems = refs[6:]
    item = pl.program_id(0)
    items = pl.num_programs(0)
    length = info[item]
    width = x_ref.shape[-1]

    @pl.when(item == 0)
    def _():
        start_weights(info, items, weights, plan, blocks, sems)

    cap = slice(CAP_FIRST, CAP_FIRST + CAP_ROWS)
    if merge:
        joined[...] = x_ref[0].astype(F32)
        branch = part_ref[0].astype(F32) + outer_ref[...]
        is_true = true_positions(length, CAP_FIRST, CAP_ROWS, 0, "caption")
        captions = before_ref[0, cap] + jnp.where(is_true, branch, 0.0)
        position = CAP_FIRST + lax.broadcasted_iota(jnp.int32, (CAP_ROWS, 1), 0)
        captions = captions.astype(BF16).astype(F32)
        joined[cap] = jnp.where(position < PATCHES, joined[cap], captions)
        x = joined[...]
        joined_ref[0] = x.astype(BF16)
    else:
        x = x_ref[0].astype(F32)
    unit, _ = norm_parts(x)
    normed = (unit * gain_ref[...] + shift_ref[...]).astype(BF16)

    @pl.when(item == 0)
    def _():
        for block in range(4):
            wait_block(blocks, block, sems)

    queries = dot_plain(normed, blocks[0]) + bias_ref[:, :width]
    qkv_ref[0, :, :width] = (queries * HEAD_DIM ** (-0.5)).astype(BF16)
    qkv_ref[0, :, width : 2 * width] = dot_plain(normed, blocks[1]).astype(BF16)
    values = dot_plain(normed, blocks[2]) + bias_ref[:, width : 2 * width]
    qkv_ref[0, :, 2 * width :] = values.astype(BF16)
    key_true = true_positions(length, 0, ROWS, 1, "all")
    low_half, even, odd = head_masks()
    ones = jnp.ones((ROWS, PAIR), BF16)

    def scores_of(pair):
        at = pair * PAIR
        q2 = qkv_ref[0, :, at : at + PAIR]
        k2 = qkv_ref[0, :, width + at : width + at + PAIR]
        return dot_last(split_pair(q2, even, odd), k2)

    ahead = [scores_of(0), scores_of(1)]
    for pair in range(HEADS // 2):
        at = pair * PAIR
        scores = jnp.where(key_true, ahead.pop(0), -1e9)
        if pair + 2 < HEADS // 2:
            ahead.append(scores_of(pair + 2))
        weight = jnp.exp(scores - jnp.max(scores, axis=-1, keepdims=True)).astype(BF16)
        v2 = qkv_ref[0, :, 2 * width + at : 2 * width + at + PAIR]
        summed = dot_plain(weight, jnp.concatenate([v2, ones], axis=1))
        top = jnp.where(low_half, summed[:ROWS, :PAIR], summed[ROWS:, :PAIR])
        below = jnp.where(low_half, summed[:ROWS, PAIR:], summed[ROWS:, PAIR:])
        mixed_ref[0, :, at : at + PAIR] = (top / below).astype(BF16)
    branch = dot_plain(mixed_ref[0], blocks[3]) + bias_ref[:, 2 * width :]
    row_true = true_positions(length, 0, ROWS, 0, "all")
    y = x + jnp.where(row_true, branch, 0.0)
    y_ref[0] = y.astype(y_ref.dtype)
    if not merge:
        unit, _ = norm_parts(y[cap])
        caption_ref[0] = (unit * next_gain_ref[...] + next_shift_ref[...]).astype(BF16)


def attend_backward_kernel(plan, weight_count, first, info, *refs):
    weights, refs = refs[:weight_count], refs[weight_count:]
    x_ref, gain_ref, shift_ref, qkv_ref, mixed_ref, grad_ref = refs[:6]
    if first:
        after_ref, next_gain_ref, *parts = refs[6:12]
        refs = refs[12:]
    else:
        refs = refs[6:]
    out_ref, gain_grad_ref, shift_grad_ref, bias_grad_ref = refs[:4]
    travel_refs = refs[4:8]
    if first:
        next_gain_grad_ref, next_shift_grad_ref, joined = refs[8], refs[9], refs[-1]
    else:
        caption_ref = refs[8]
    blocks, sems, normed_turned, mixed_turned, branch_all, projected, mixed_grad = refs[
        10 if first else 9 :
    ][:7]
    item = pl.program_id(0)
    items = pl.num_programs(0)
    length = info[item]
    section, core = info[items], info[items + 1]
    width = x_ref.shape[-1]
    here = pl.ds(pl.multiple_of(item * ROWS, ROWS), ROWS)
    cap = slice(CAP_FIRST, CAP_FIRST + CAP_ROWS)

    @pl.when(item == 0)
    def _():
        start_weights(info, items, weights, plan, blocks, sems)

    def add_to(ref, part):
        @pl.when(item == 0)
        def _():
            ref[...] = part

        @pl.when(item > 0)
        def _():
            ref[...] += part

    x = x_ref[0].astype(F32)
    unit, scale = norm_parts(x)
    normed = (unit * gain_ref[...] + shift_ref[...]).astype(BF16)
    incoming = grad_ref[0].astype(F32)
    if first:
        after_unit, after_scale = norm_parts(after_ref[0, cap])
        caption_grad = parts[0][...].astype(F32)
        for part in parts[1:]:
            caption_grad = caption_grad + part[...].astype(F32)
        joined[...] = incoming
        joined[cap] += norm_back(caption_grad, after_unit, after_scale, next_gain_ref[...])
        incoming = joined[...]
        add_to(next_gain_grad_ref, jnp.sum(caption_grad * after_unit, axis=0, keepdims=True))
        add_to(next_shift_grad_ref, jnp.sum(caption_grad, axis=0, keepdims=True))
    row_true = true_positions(length, 0, ROWS, 0, "all")
    branch = jnp.where(row_true, incoming, 0.0).astype(BF16)
    branch_all[here, :] = branch
    store_turned(normed_turned, normed.T, here, section, core)
    store_turned(mixed_turned, mixed_ref[0].T, here, section, core)

    @pl.when(item == 0)
    def _():
        for block in range(4):
            wait_block(blocks, block, sems)

    mixed_grad[...] = dot_last(branch, blocks[3]).astype(BF16)
    key_true = true_positions(length, 0, ROWS, 0, "all")
    _, even, odd = head_masks()

    def products_of(pair):
        at = pair * PAIR
        q2 = split_pair(qkv_ref[0, :, at : at + PAIR], even, odd)
        k2 = qkv_ref[0, :, width + at : width + at + PAIR]
        v2 = qkv_ref[0, :, 2 * width + at : 2 * width + at + PAIR]
        g2 = split_pair(mixed_grad[:, at : at + PAIR], even, odd)
        return q2, k2, g2, dot_last(k2, q2), dot_last(v2, g2)

    ahead = [products_of(0)]
    for pair in range(HEADS // 2):
        at = pair * PAIR
        q2, k2, g2, scores, weight_grad = ahead.pop(0)
        if pair + 1 < HEADS // 2:
            ahead.append(products_of(pair + 1))
        scores = jnp.where(key_true, scores, -1e9)
        weight = jnp.exp(scores - jnp.max(scores, axis=0, keepdims=True))
        weight = weight * (1.0 / jnp.sum(weight, axis=0, keepdims=True))
        product = weight * weight_grad
        along = jnp.sum(product, axis=0, keepdims=True)
        score_grad = (product - weight * along).astype(BF16)
        values_grad = dot_plain(weight.astype(BF16), g2).astype(BF16)
        keys_grad = dot_plain(score_grad, q2).astype(BF16)
        k2_split = split_pair(k2, even, odd)
        stacked = jnp.concatenate([score_grad[:, :ROWS], score_grad[:, ROWS:]], axis=0)
        queries_grad = dot_first(stacked, k2_split).astype(BF16)
        queries_grad = (queries_grad.astype(F32) * HEAD_DIM ** (-0.5)).astype(BF16)
        projected[here, at : at + PAIR] = queries_grad
        projected[here, width + at : width + at + PAIR] = keys_grad
        projected[here, 2 * width + at : 2 * width + at + PAIR] = values_grad
    normed_grad = dot_last(projected[here, :width], blocks[0])
    normed_grad += dot_last(projected[here, width : 2 * width], blocks[1])
    normed_grad += dot_last(projected[here, 2 * width :], blocks[2])
    out = (incoming + norm_back(normed_grad, unit, scale, gain_ref[...])).astype(BF16)
    out_ref[0] = out
    if not first:
        is_true = true_positions(length, CAP_FIRST, CAP_ROWS, 0, "caption")
        caption_ref[0] = jnp.where(is_true, out[cap].astype(F32), 0.0).astype(BF16)
    add_to(gain_grad_ref, jnp.sum(normed_grad * unit, axis=0, keepdims=True))
    add_to(shift_grad_ref, jnp.sum(normed_grad, axis=0, keepdims=True))

    @pl.when(item == items - 1)
    def _():
        for block in range(4):
            columns = slice(block * width, (block + 1) * width)
            left = normed_turned if block < 3 else mixed_turned
            right = projected[:, columns] if block < 3 else branch_all[...]
            put_travel(travel_refs, 0, columns, left, right)
        bias_grad_ref[:, :width] = column_sum(projected[:, :width])
        bias_grad_ref[:, width : 2 * width] = column_sum(projected[:, 2 * width :])
        bias_grad_ref[:, 2 * width :] = column_sum(branch_all[...])


SHORT = pl.CostEstimate(flops=0, bytes_accessed=100_000, transcendentals=0)
LONG = pl.CostEstimate(flops=30_000_000_000, bytes_accessed=30_000_000, transcendentals=0)
ANYWHERE = pl.BlockSpec(memory_space=pl.ANY)


def whole_block(shape):
    return pl.BlockSpec(shape, lambda step, info: (0,) * len(shape))


def item_block(shape):
    return pl.BlockSpec((1,) + shape[1:], lambda step, info: (step,) + (0,) * (len(shape) - 1))


def blocks_scratch(count, width):
    return [pltpu.VMEM((count, width, width), BF16), pltpu.SemaphoreType.DMA((count,))]


def attend_forward(x, info, weights, gain, shift, bias, merge=None, following=None):
    arrays, plan = weights
    items, _, width = x.shape
    row = whole_block((1, width))
    bias_row = whole_block((1, 3 * width))
    caption_shape = (items, CAP_ROWS, width)
    if merge is not None:
        before, part, outer = merge
        operands = (x, before, part, outer, gain, shift, bias)
        specs = [item_block(x.shape), item_block(x.shape), item_block(caption_shape)]
        specs += [row, row, row, bias_row]
        last_shape, kind, scratch = x.shape, BF16, [pltpu.VMEM((ROWS, width), F32)]
    else:
        operands = (x, gain, shift, bias, *following)
        specs = [item_block(x.shape), row, row, bias_row, row, row]
        last_shape, kind, scratch = caption_shape, F32, []
    return pl.pallas_call(
        partial(attend_forward_kernel, plan, len(arrays), merge is not None),
        grid_spec=pltpu.PrefetchScalarGridSpec(
            num_scalar_prefetch=1,
            grid=(items,),
            in_specs=[ANYWHERE] * len(arrays) + specs,
            out_specs=[
                item_block(x.shape),
                item_block((items, ROWS, 3 * width)),
                item_block((items, ROWS, width)),
                item_block(last_shape),
            ],
            scratch_shapes=blocks_scratch(4, width) + scratch,
        ),
        out_shape=[
            jax.ShapeDtypeStruct(x.shape, kind),
            jax.ShapeDtypeStruct((items, ROWS, 3 * width), BF16),
            jax.ShapeDtypeStruct((items, ROWS, width), BF16),
            jax.ShapeDtypeStruct(last_shape, BF16),
        ],
        compiler_params=pltpu.CompilerParams(vmem_limit_bytes=VMEM_BYTES),
        cost_estimate=SHORT,
        name="attend_forward",
    )(info, *arrays, *operands)


def attend_backward(x, info, weights, gain, shift, qkv, mixed, incoming, first=None):
    arrays, plan = weights
    items, _, width = x.shape
    half = width // 2
    row = whole_block((1, width))
    caption_shape = (items, CAP_ROWS, width)
    operands = (x, gain, shift, qkv, mixed, incoming)
    specs = [item_block(x.shape), row, row, item_block(qkv.shape), item_block(mixed.shape)]
    specs += [item_block(incoming.shape)]
    outs = [
        (item_block(x.shape), x.shape, BF16),
        (row, (1, width), F32),
        (row, (1, width), F32),
        (whole_block((1, 3 * width)), (1, 3 * width), F32),
    ]
    outs += [(whole_block((1, half // 2, 4 * width)), (1, half // 2, 4 * width), BF16)] * 4
    scratch = []
    if first is not None:
        after, next_gain, parts = first
        operands += (after, next_gain, *parts)
        caption_rows = pl.BlockSpec((CAP_ROWS, width), lambda step, info: (step, 0))
        specs += [item_block(after.shape), row] + [caption_rows] * 4
        outs += [(row, (1, width), F32)] * 2
        scratch = [pltpu.VMEM((ROWS, width), F32)]
    else:
        outs += [(item_block(caption_shape), caption_shape, BF16)]
    return pl.pallas_call(
        partial(attend_backward_kernel, plan, len(arrays), first is not None),
        grid_spec=pltpu.PrefetchScalarGridSpec(
            num_scalar_prefetch=1,
            grid=(items,),
            in_specs=[ANYWHERE] * len(arrays) + specs,
            out_specs=[spec for spec, _, _ in outs],
            scratch_shapes=blocks_scratch(4, width)
            + [
                pltpu.VMEM((width, items * ROWS), BF16),
                pltpu.VMEM((width, items * ROWS), BF16),
                pltpu.VMEM((items * ROWS, width), BF16),
                pltpu.VMEM((items * ROWS, 3 * width), BF16),
                pltpu.VMEM((ROWS, width), BF16),
            ]
            + scratch,
        ),
        out_shape=[jax.ShapeDtypeStruct(shape, kind) for _, shape, kind in outs],
        compiler_params=pltpu.CompilerParams(vmem_limit_bytes=VMEM_BYTES),
        cost_estimate=LONG,
        name="attend_backward",
    )(info, *arrays, *operands)


def normal_parts(u):
    t = pl.reciprocal(1.0 + 0.23164190 * jnp.abs(u), approx=True)
    bell = jnp.exp2((u * -0.7213475204444817) * u)
    poly = t * (
        0.127414796
        + t * (-0.142248368 + t * (0.7107068705 + t * (-0.7265760135 + t * 0.5307027145)))
    )
    tail = poly * bell
    return jnp.where(u < 0, tail, 1.0 - tail), bell


def inner_forward(normed, matrix, bias):
    inner = dot_plain(normed, matrix) + bias
    cumulative, bell = normal_parts(inner)
    slope = cumulative + (inner * 0.3989422804014327) * bell
    return (inner * cumulative).astype(BF16), slope.astype(BF16)


def expert_forward_kernel(plan, weight_count, count, kind, info, *refs):
    weights, refs = refs[:weight_count], refs[weight_count:]
    x_ref, gain_ref, shift_ref, inner_ref, outer_ref = refs[:5]
    y_ref, act_ref, slope_ref, blocks, sems, normed, total = refs[5:]
    step = pl.program_id(0)
    items, _, width = x_ref.shape

    @pl.when(step == 0)
    def _():
        start_weights(info, items, weights, plan, blocks, sems)
        for item in range(items):
            x = x_ref[item, :count].astype(BF16).astype(F32)
            unit, _ = norm_parts(x)
            normed[item * count : (item + 1) * count] = (
                unit * gain_ref[...] + shift_ref[...]
            ).astype(BF16)

    wait_block(blocks, step, sems)
    wait_block(blocks, step + 4, sems)
    for at in range(0, width, 256):
        columns = slice(at, at + 256)
        act, slope = inner_forward(normed[...], blocks[step, :, columns], inner_ref[:, columns])
        act_ref[:, columns] = act
        slope_ref[:, columns] = slope
    part = dot_plain(act_ref[...], blocks[step + 4])

    @pl.when(step == 0)
    def _():
        total[...] = part

    @pl.when(step > 0)
    def _():
        total[...] += part

    @pl.when(step == pl.num_programs(0) - 1)
    def _():
        for item in range(items):
            row_true = true_positions(info[item], 0, count, 0, kind)
            branch = total[item * count : (item + 1) * count] + outer_ref[...]
            x = x_ref[item, :count].astype(BF16).astype(F32)
            y_ref[item, :count] = (x + jnp.where(row_true, branch, 0.0)).astype(BF16)
            if count < ROWS:
                y_ref[item, count:] = jnp.zeros((ROWS - count, width), BF16)


def expert_backward_kernel(plan, weight_count, count, kind, info, *refs):
    weights, refs = refs[:weight_count], refs[weight_count:]
    x_ref, gain_ref, shift_ref, act_ref, slope_ref, grad_ref = refs[:6]
    out_ref, gain_grad_ref, shift_grad_ref, inner_grad_ref, outer_grad_ref = refs[6:11]
    travel_refs = refs[11:15]
    blocks, sems, normed_turned, branch_turned, branch, inner_all, total = refs[15:]
    step = pl.program_id(0)
    items, _, width = x_ref.shape
    section, core = info[items], info[items + 1]

    @pl.when(step == 0)
    def _():
        start_weights(info, items, weights, plan, blocks, sems)
        outer = None
        for item in range(items):
            here = slice(item * count, (item + 1) * count)
            unit, _ = norm_parts(x_ref[item, :count].astype(BF16).astype(F32))
            normed = (unit * gain_ref[...] + shift_ref[...]).astype(BF16)
            row_true = true_positions(info[item], 0, count, 0, kind)
            incoming = grad_ref[item, :count].astype(F32)
            masked = jnp.where(row_true, incoming, 0.0).astype(BF16)
            branch[here] = masked
            store_turned(normed_turned, normed.T, here, section, core)
            store_turned(branch_turned, masked.T, here, section, core)
            term = column_sum(masked)
            outer = term if outer is None else outer + term
        outer_grad_ref[...] = outer

    wait_block(blocks, step, sems)
    wait_block(blocks, step + 4, sems)
    for at in range(0, width, 256):
        columns = slice(at, at + 256)
        act_grad = dot_last(branch[...], blocks[step + 4, columns])
        inner = (slope_ref[:, columns].astype(F32) * act_grad).astype(BF16)
        inner_all[:, columns] = inner
        inner_grad_ref[:, columns] = column_sum(inner)
        put_travel(travel_refs, 0, columns, normed_turned, inner)
        put_travel(travel_refs, 1, columns, branch_turned, act_ref[:, columns])
    part = dot_last(inner_all[...], blocks[step])

    @pl.when(step == 0)
    def _():
        total[...] = part

    @pl.when(step > 0)
    def _():
        total[...] += part

    @pl.when(step == pl.num_programs(0) - 1)
    def _():
        gain_sum, shift_sum = None, None
        for item in range(items):
            unit, scale = norm_parts(x_ref[item, :count].astype(BF16).astype(F32))
            normed_grad = total[item * count : (item + 1) * count]
            gain_part = jnp.sum(normed_grad * unit, axis=0, keepdims=True)
            shift_part = jnp.sum(normed_grad, axis=0, keepdims=True)
            gain_sum = gain_part if gain_sum is None else gain_sum + gain_part
            shift_sum = shift_part if shift_sum is None else shift_sum + shift_part
            incoming = grad_ref[item, :count].astype(F32)
            hidden = incoming + norm_back(normed_grad, unit, scale, gain_ref[...])
            out_ref[item, :count] = hidden.astype(BF16)
            if count < ROWS:
                out_ref[item, count:] = grad_ref[item, count:]
        gain_grad_ref[...] = gain_sum
        shift_grad_ref[...] = shift_sum


def shared_forward_kernel(*refs):
    *rows_refs, inputs_ref, inner_ref, outputs_ref = refs[:7]
    *part_refs, normed, total = refs[7:]
    count = rows_refs[0].shape[0]
    step = pl.program_id(0)

    @pl.when(step == 0)
    def _():
        for index, ref in enumerate(rows_refs):
            normed[index * count : (index + 1) * count] = ref[...]
        total[...] = jnp.zeros_like(total)

    act, _ = inner_forward(normed[...], inputs_ref[...], inner_ref[...])
    total[...] += dot_plain(act, outputs_ref[...])

    @pl.when(step == pl.num_programs(0) - 1)
    def _():
        for index, ref in enumerate(part_refs):
            ref[...] = total[index * count : (index + 1) * count].astype(BF16)


def shared_backward_kernel(plan, weight_count, info, *refs):
    weights, refs = refs[:weight_count], refs[weight_count:]
    rows_refs, grad_refs, inner_ref = refs[:4], refs[4:8], refs[8]
    part_refs, (keep_ref, send_ref, inner_grad_ref, outer_grad_ref) = refs[9:13], refs[13:17]
    blocks, sems, normed, branch, matrix = refs[17:]
    count, width = rows_refs[0].shape
    half = width // 2
    first = info.shape[0] - 3
    core = info[first + 1]
    start_weights(info, first, weights, plan, blocks, sems)
    for index in range(SECTIONS):
        here = slice(index * count, (index + 1) * count)
        normed[here] = rows_refs[index][...]
        branch[here] = grad_refs[index][...]
    outer_grad_ref[...] = column_sum(grad_refs[0][...])
    wait_block(blocks, 0, sems)
    wait_block(blocks, 1, sems)
    part = None
    for at in range(0, width, 256):
        columns = slice(at, at + 256)
        act, slope = inner_forward(normed[...], blocks[0, :, columns], inner_ref[:, columns])
        act_grad = dot_last(branch[...], blocks[1, columns])
        inner = (slope.astype(F32) * act_grad).astype(BF16)
        inner_grad_ref[:, columns] = column_sum(inner)
        matrix[0, :, columns] = dot_first(normed[...], inner).astype(BF16)
        matrix[1, :, columns] = dot_first(branch[...], act).astype(BF16)
        term = dot_last(inner, blocks[0, :, columns])
        part = term if part is None else part + term
    for index, ref in enumerate(part_refs):
        ref[...] = part[index * count : (index + 1) * count].astype(BF16)
    quarter = half // 4
    for which in range(2):
        for group in range(4):
            columns = slice(group * width, (group + 1) * width)
            mine = pl.multiple_of(core * half, 16) + group * quarter
            other = pl.multiple_of((1 - core) * half, 16) + group * quarter
            keep_ref[which, :, columns] = matrix[which, pl.ds(pl.multiple_of(mine, 16), quarter)]
            send_ref[which, :, columns] = matrix[which, pl.ds(pl.multiple_of(other, 16), quarter)]


def chunk_columns(rows, width):
    return pl.BlockSpec((rows, width), lambda step, info: (0, step))


def expert_forward(x, info, weights, gain, shift, inner, outer, count, kind):
    arrays, plan = weights
    items, _, width = x.shape
    hidden = inner.shape[1]
    row = whole_block((1, width))
    return pl.pallas_call(
        partial(expert_forward_kernel, plan, len(arrays), count, kind),
        grid_spec=pltpu.PrefetchScalarGridSpec(
            num_scalar_prefetch=1,
            grid=(hidden // width,),
            in_specs=[ANYWHERE] * len(arrays)
            + [whole_block(x.shape), row, row, chunk_columns(1, width), row],
            out_specs=[
                whole_block((items, ROWS, width)),
                chunk_columns(items * count, width),
                chunk_columns(items * count, width),
            ],
            scratch_shapes=blocks_scratch(8, width)
            + [
                pltpu.VMEM((items * count, width), BF16),
                pltpu.VMEM((items * count, width), F32),
            ],
        ),
        out_shape=[
            jax.ShapeDtypeStruct((items, ROWS, width), BF16),
            jax.ShapeDtypeStruct((items * count, hidden), BF16),
            jax.ShapeDtypeStruct((items * count, hidden), BF16),
        ],
        compiler_params=pltpu.CompilerParams(vmem_limit_bytes=VMEM_BYTES),
        cost_estimate=SHORT,
        name="expert_forward_" + kind,
    )(info, *arrays, x, gain, shift, inner, outer)


def expert_backward(x, info, weights, gain, shift, act, slope, incoming, count, kind):
    arrays, plan = weights
    items, _, width = x.shape
    half = width // 2
    hidden = act.shape[1]
    row = whole_block((1, width))
    travel = pl.BlockSpec((2, half // 2, width), lambda step, info: (0, 0, step))
    return pl.pallas_call(
        partial(expert_backward_kernel, plan, len(arrays), count, kind),
        grid_spec=pltpu.PrefetchScalarGridSpec(
            num_scalar_prefetch=1,
            grid=(hidden // width,),
            in_specs=[ANYWHERE] * len(arrays)
            + [
                whole_block(x.shape),
                row,
                row,
                chunk_columns(items * count, width),
                chunk_columns(items * count, width),
                whole_block(incoming.shape),
            ],
            out_specs=[whole_block(incoming.shape), row, row, chunk_columns(1, width), row]
            + [travel] * 4,
            scratch_shapes=blocks_scratch(8, width)
            + [
                pltpu.VMEM((width, items * count), BF16),
                pltpu.VMEM((width, items * count), BF16),
                pltpu.VMEM((items * count, width), BF16),
                pltpu.VMEM((items * count, width), BF16),
                pltpu.VMEM((items * count, width), F32),
            ],
        ),
        out_shape=[
            jax.ShapeDtypeStruct(incoming.shape, BF16),
            jax.ShapeDtypeStruct((1, width), F32),
            jax.ShapeDtypeStruct((1, width), F32),
            jax.ShapeDtypeStruct((1, hidden), F32),
            jax.ShapeDtypeStruct((1, width), F32),
        ]
        + [jax.ShapeDtypeStruct((2, half // 2, hidden), BF16)] * 4,
        compiler_params=pltpu.CompilerParams(vmem_limit_bytes=VMEM_BYTES),
        cost_estimate=SHORT,
        name="expert_backward_" + kind,
    )(info, *arrays, x, gain, shift, act, slope, incoming)


IN_VMEM = pl.BlockSpec(memory_space=pltpu.VMEM)
IN_SMEM = pl.BlockSpec(memory_space=pltpu.SMEM)


def shared_forward(rows, inputs, inner, outputs):
    count, width = rows[0].shape
    total = SECTIONS * count
    hidden = inner.shape[1]
    return pl.pallas_call(
        shared_forward_kernel,
        grid=(hidden // width,),
        in_specs=[pl.BlockSpec(rows[0].shape, lambda step: (0, 0))] * 4
        + [
            pl.BlockSpec((width, width), lambda step: (0, step)),
            pl.BlockSpec((1, width), lambda step: (0, step)),
            pl.BlockSpec((width, width), lambda step: (step, 0)),
        ],
        out_specs=[pl.BlockSpec((count, width), lambda step: (0, 0))] * SECTIONS,
        scratch_shapes=[pltpu.VMEM((total, width), BF16), pltpu.VMEM((total, width), F32)],
        out_shape=[jax.ShapeDtypeStruct((count, width), BF16)] * SECTIONS,
        compiler_params=pltpu.CompilerParams(vmem_limit_bytes=VMEM_BYTES),
        cost_estimate=SHORT,
        name="shared_forward",
    )(*rows, inputs, inner, outputs)


def shared_backward(rows, grads, info, weights, inner):
    arrays, plan = weights
    count, width = rows[0].shape
    total = SECTIONS * count
    travel = (2, width // 8, 4 * width)
    return pl.pallas_call(
        partial(shared_backward_kernel, plan, len(arrays)),
        in_specs=[IN_SMEM] + [ANYWHERE] * len(arrays) + [IN_VMEM] * 9,
        out_specs=[IN_VMEM] * 8,
        scratch_shapes=blocks_scratch(2, width)
        + [
            pltpu.VMEM((total, width), BF16),
            pltpu.VMEM((total, width), BF16),
            pltpu.VMEM((2, width, width), BF16),
        ],
        out_shape=[
            *[jax.ShapeDtypeStruct((count, width), BF16)] * SECTIONS,
            jax.ShapeDtypeStruct(travel, BF16),
            jax.ShapeDtypeStruct(travel, BF16),
            jax.ShapeDtypeStruct((1, width), F32),
            jax.ShapeDtypeStruct((1, width), F32),
        ],
        compiler_params=pltpu.CompilerParams(vmem_limit_bytes=VMEM_BYTES),
        cost_estimate=SHORT,
        name="shared_backward",
    )(info, *arrays, *rows, *grads, inner)


def plane_turn(plane, planes):
    return ((plane & 1) << 1) | (plane >> 1) if planes == 4 else 0


def finish_kernel(planes, info, scale_ref, *refs):
    step = pl.program_id(0)
    mine, theirs, outs, placed = refs[:4], refs[4:8], refs[8:-1], refs[-1]
    count = mine[0].shape[0]
    width = placed.shape[1]
    half = width // 2
    at = info.shape[0] - 3
    section, core = info[at], info[at + 1]
    turn = plane_turn(info[at + 2], planes)
    turned = turn if count == 1 else jnp.where(section == 1, turn, 0)
    scale = scale_ref[0, 0]
    columns = pl.ds(pl.multiple_of((step ^ turned) * width, width), width)

    def place(which):
        def by_rows():
            for side, pieces in enumerate((mine, theirs)):
                for away, ref in enumerate(pieces):
                    for path in range(2):
                        row = (core ^ side) * half + path * (half // 2)
                        row = row + (section ^ away) * PIECE_ROWS
                        placed[pl.ds(pl.multiple_of(row, 16), PIECE_ROWS), :] = ref[
                            which, path * PIECE_ROWS : (path + 1) * PIECE_ROWS, columns
                        ].astype(F32)

        def by_columns():
            for side, pieces in enumerate((mine, theirs)):
                for away, ref in enumerate(pieces):

                    @pl.when(step == away)
                    def _(side=side, ref=ref):
                        for group in range(4):
                            quarter = half // 4
                            row = (core ^ side) * half + group * quarter
                            placed[pl.ds(pl.multiple_of(row, 16), quarter), :] = ref[
                                which, :, group * width : (group + 1) * width
                            ].astype(F32)

        if count == 1:
            by_rows()
        else:
            pl.when(section != 0)(by_rows)
            pl.when(section == 0)(by_columns)

    place(0)
    if count == 1:

        @pl.when(step < 3)
        def _():
            outs[0][0] = placed[...] / scale

        @pl.when(step == 3)
        def _():
            outs[1][0] = placed[...] / scale

    else:
        outs[0][0] = placed[...] / scale
        place(1)
        outs[1][0] = (placed[...] / scale).T


def finish(info, scale, mine, theirs, planes):
    count, _, hidden = mine[0].shape
    width = hidden // 4
    if count == 1:
        shapes = [(1, width, 3 * width), (1, width, width)]
        maps = [lambda step, info: (0, 0, jnp.minimum(step, 2)), lambda step, info: (0, 0, 0)]
    else:
        shapes = [(1, width, hidden), (1, hidden, width)]
        maps = [lambda step, info: (0, 0, step), lambda step, info: (0, step, 0)]
    return pl.pallas_call(
        partial(finish_kernel, planes),
        grid_spec=pltpu.PrefetchScalarGridSpec(
            num_scalar_prefetch=1,
            grid=(4,),
            in_specs=[IN_SMEM] + [whole_block(mine[0].shape)] * 8,
            out_specs=[pl.BlockSpec((1, width, width), at) for at in maps],
            scratch_shapes=[pltpu.VMEM((width, width), F32)],
        ),
        out_shape=[jax.ShapeDtypeStruct(shape, F32) for shape in shapes],
        compiler_params=pltpu.CompilerParams(vmem_limit_bytes=VMEM_BYTES),
        cost_estimate=SHORT,
        name="finish",
    )(info, scale, *mine, *theirs)


def pack_kernel(count, plan, info, *refs):
    sources, outs, sems = refs[:count], refs[count:-1], refs[-1]
    first = info.shape[0] - 3
    section, core, plane = info[first], info[first + 1], info[first + 2]
    half = outs[0].shape[1]
    for index, (out, choices) in enumerate(zip(outs, plan)):
        for at, at_plane, parts in choices:
            here = section == at
            if at_plane is not None:
                here = here & (plane == at_plane)

            @pl.when(here)
            def _(index=index, out=out, parts=parts):
                for block, part in enumerate(parts):
                    if part[0] == "own":
                        _, which, row, column = part
                        rows = pl.ds(pl.multiple_of(row + core * half, half), half)
                        source = sources[which].at[rows, pl.ds(column, out.shape[2])]
                    else:
                        source = sources[part[1]].at[block]
                    pltpu.make_async_copy(source, out.at[block], sems.at[index, block]).start()

    for index, out in enumerate(outs):
        for block in range(2):
            pltpu.make_async_copy(out.at[block], out.at[block], sems.at[index, block]).wait()


def pack(info, sources, plan, shape):
    return pl.pallas_call(
        partial(pack_kernel, len(sources), plan),
        in_specs=[IN_SMEM] + [ANYWHERE] * len(sources),
        out_specs=[IN_VMEM] * len(plan),
        scratch_shapes=[pltpu.SemaphoreType.DMA((len(plan), 2))],
        out_shape=[jax.ShapeDtypeStruct(shape, BF16)] * len(plan),
        cost_estimate=SHORT,
        name="pack",
    )(info, *sources)


def over_section(value, bits, sources=range(SECTIONS)):
    return lax.ppermute(value, "section", [(at, at ^ bits) for at in sources])


def over_core(value):
    return lax.ppermute(value, "core", [(0, 1), (1, 0)])


def over_plane(value, pairs):
    return lax.ppermute(value, "z", pairs)


def added(left, right):
    return (left.astype(F32) + right.astype(F32)).astype(BF16)


def after(value, *earlier):
    return lax.optimization_barrier((value,) + earlier)[0]


def under(outputs, *arrivals):
    joined = lax.optimization_barrier(tuple(outputs) + arrivals)
    return list(joined[: len(outputs)]), list(joined[len(outputs) :])


def by_section(section, values):
    result, last = None, None
    for at in sorted(values):
        if result is None:
            result = values[at]
        elif values[at] is not last:
            result = jnp.where(section >= at, values[at], result)
        last = values[at]
    return result


def total(*values):
    result = values[0].astype(F32)
    for value in values[1:]:
        result = result + value.astype(F32)
    return result.astype(BF16)


class Sums:
    def __init__(self, travel):
        self.stay, self.move, self.other_stay, self.other_move = travel
        self.size = self.stay.shape[1] // 2

    def cross(self, *earlier):
        if earlier:
            self.other_move = after(self.other_move, *earlier)
            self.other_stay = after(self.other_stay, *earlier)
        self.got_move, self.got_stay = over_core(self.other_move), over_core(self.other_stay)

    def first_sends(self):
        size = self.size
        self.sent = [
            total(self.move[:, at : at + size], self.got_move[:, at : at + size])
            for at in (0, size)
        ]
        return self.sent

    def second_sends(self, from_x, from_y):
        size, half = self.size, self.size // 2
        self.first = from_x, from_y
        to_y = total(self.stay[:, half:size], self.got_stay[:, half:size], from_x[:, half:])
        to_x = total(
            self.stay[:, size + half :], self.got_stay[:, size + half :], from_y[:, half:]
        )
        self.sent = [to_x, to_y]
        return self.sent

    def whole(self, from_x, from_y):
        size, half = self.size, self.size // 2
        parts = []
        for at, first, second in ((0, self.first[0], from_y), (size, self.first[1], from_x)):
            here = slice(at, at + half)
            parts.append(total(self.stay[:, here], self.got_stay[:, here], first[:, :half], second))
        return jnp.concatenate(parts, axis=1)


def over_links(sends):
    return [over_section(sends[0], 1), over_section(sends[1], 2)]


class Planes:
    def __init__(self, value, plane, planes):
        self.value, self.plane, self.planes, self.turn = value, plane, planes, 0

    def sends(self, *earlier):
        value = after(self.value, *earlier) if earlier else self.value
        if self.planes != 4:
            return (value,)
        bits = (1, 2, 2, 1)[self.turn]
        if self.turn < 2:
            bit = (self.plane & 1, self.plane >> 1)[self.turn]
            size = value.shape[-1] // 2
            value = lax.dynamic_slice_in_dim(value, (1 - bit) * size, size, value.ndim - 1)
        return (over_plane(value, [(at, at ^ bits) for at in range(4)]),)

    def take(self, arrived):
        if self.planes != 4:
            self.value = lax.psum(arrived, "z") if self.turn == 3 else arrived
        elif self.turn < 2:
            bit = (self.plane & 1, self.plane >> 1)[self.turn]
            size = self.value.shape[-1] // 2
            keep = lax.dynamic_slice_in_dim(self.value, bit * size, size, self.value.ndim - 1)
            self.value = added(keep, arrived)
        else:
            self.value = jnp.concatenate([self.value, arrived], axis=-1)
        self.turn += 1

    def in_order(self, value):
        if self.planes != 4:
            return value
        size, turn = value.shape[-1] // 4, plane_turn(self.plane, 4)
        parts = [
            lax.dynamic_slice_in_dim(value, (at ^ turn) * size, size, value.ndim - 1)
            for at in range(4)
        ]
        return jnp.concatenate(parts, axis=-1)


class Weights:
    def __init__(self, own, info, planes):
        self.own, self.info = own, info
        self.four = planes == 4
        self.plan = PLAN_FOUR if self.four else PLAN_ANY
        self.half, self.width = own[1].shape[0] // 2, own[1].shape[1]
        self.mine, self.theirs, self.arrived = {}, {}, {}

    def place(self, layer, block):
        if layer in "ac":
            return (0, 0, block * self.width) if block < 3 else (1, 0, 0)
        if layer == "g":
            return (2, 0, block * self.width) if block < 4 else (3, (block - 4) * self.width, 0)
        return (2, 0, block * self.width) if block < 4 else (3, (block - 4) * self.width, 0)

    def choices(self, sends, sources):
        result = []
        for at in range(SECTIONS):
            name = sends.get(at)
            if name is not None and HOMES[name[0]] != at:
                key = self.arrived[at, name]
                if key not in sources:
                    sources[key] = len(self.own) + len(sources)
                result.append((at, None, [("arrived", sources[key])] * 2))
                continue
            for plane in range(4) if name == "F" else (None,):
                piece = ("f" + str(plane)) if name == "F" else name or "a0"
                layer, index = piece[0], int(piece[1])
                if layer in "ac":
                    blocks = ATTEND_BLOCKS[index]
                else:
                    blocks = (index, 4 + index) if layer == "g" else EXPERT_BLOCKS[index]
                parts = [("own",) + self.place(layer, block) for block in blocks]
                result.append((at, plane, parts))
        return result

    def packed(self, wanted):
        sources = {}
        plan = [self.choices(sends, sources) for sends in wanted]
        arrays = list(self.own) + [self.mine[key] for key in sources]
        return pack(self.info, arrays, plan, (2, self.half, self.width))

    def sends(self, step):
        if step == "F":
            return [{at: "F" for at in range(SECTIONS)}]
        return [sends for sends in self.plan[step] if sends]

    def payloads(self, *steps):
        wanted = [sends for step in steps for sends in self.sends(step)]
        return list(self.packed(wanted))

    def move(self, step, payloads):
        links = [(link, sends) for link, sends in enumerate(self.plan[step]) if sends]
        for (link, sends), payload in zip(links, payloads):
            self.mine[step, link] = over_section(payload, link + 1, sorted(sends))
            for at, name in sends.items():
                self.arrived[at ^ (link + 1), name] = (step, link)
        return [(step, link) for link, _ in links]

    def move_planes(self, step):
        up, down = self.mine["plane", step - 1], self.mine["plane", 1 - step]
        up = over_plane(up, [(at, at + 1) for at in range(step - 1, 3)])
        down = over_plane(down, [(at, at - 1) for at in range(4 - step, 0, -1)])
        self.mine["plane", step], self.mine["plane", -step] = up, down
        return [("plane", step), ("plane", -step)]

    def cross(self, keys):
        for key in keys:
            self.theirs[key] = over_core(self.mine[key])
        return keys

    def join(self, outputs, mine=(), theirs=()):
        values = [self.mine[key] for key in mine] + [self.theirs[key] for key in theirs]
        outputs, values = under(outputs, *values)
        for key, value in zip(mine, values):
            self.mine[key] = value
        for key, value in zip(theirs, values[len(mine) :]):
            self.theirs[key] = value
        return outputs

    def layer(self, layer):
        arrays, places = list(self.own), {}

        def place(key):
            if key not in places:
                places[key] = len(arrays)
                arrays.extend([self.mine[key], self.theirs[key]])
            return places[key], places[key] + 1

        if layer in "ac":
            names = [(layer + str(index), ATTEND_BLOCKS[index]) for index in range(2)]
        else:
            names = [(layer + str(index), EXPERT_BLOCKS[index]) for index in range(4)]
        plan = []
        for at in range(SECTIONS):
            if layer == "g":
                names = [("g" + str(at), (0, 1))]
            if HOMES[layer] == at:
                steps = []
                for name, blocks in names:
                    for block in blocks:
                        source = block * 4 if layer == "g" else block
                        steps.append((block, ("own",) + self.place(layer, source)))
                plan.append((at, None, steps))
                continue
            by_plane = layer == "f" and self.four
            for plane in range(4) if by_plane else (None,):
                steps = []
                for index, (name, blocks) in enumerate(names):
                    key = ("plane", plane - index) if by_plane else self.arrived[at, name]
                    for which, block in enumerate(blocks):
                        steps.append((block, ("piece",) + place(key) + (which,)))
                plan.append((at, plane, steps))
        return arrays, plan


def per_device(
    tokens,
    caption_lengths,
    attend_gain,
    attend_shift,
    attend_inputs,
    attend_bias,
    attend_output,
    expert_gain,
    expert_shift,
    expert_inputs,
    expert_inner_bias,
    expert_outputs,
    expert_outer_bias,
    cotangent,
):
    section, core, plane = lax.axis_index("section"), lax.axis_index("core"), lax.axis_index("z")
    planes = lax.axis_size("z")
    items, positions, width = tokens.shape
    hidden = expert_inputs.shape[-1]
    info = [value.reshape(1).astype(jnp.int32) for value in (section, core, plane)]
    info = jnp.concatenate([caption_lengths] + info)
    weights = Weights(
        (attend_inputs[0], attend_output[0], expert_inputs[0], expert_outputs[0]), info, planes
    )

    def to_sections(value):
        return [value] + [over_section(value, bits) for bits in (1, 2, 3)]

    def items_of(part):
        return part.reshape(items, CAP_ROWS, width)

    keys = weights.move(0, weights.payloads(0))
    pad = ((0, 0), (0, ROWS - positions), (0, 0))
    x0 = jnp.pad(tokens, pad)
    last_grad = jnp.pad(cotangent, pad)
    rows = jnp.concatenate(
        [
            attend_gain,
            attend_shift,
            attend_bias,
            expert_gain,
            expert_shift,
            expert_inner_bias,
            expert_outer_bias,
            jnp.full((1, 128), jnp.sum(caption_lengths), F32),
        ],
        axis=1,
    )
    rows = to_sections(rows)
    x0, last_grad, *rows = weights.join([x0, last_grad, *rows], keys)
    keys1 = weights.move(1, weights.payloads(1))
    rows = jnp.concatenate(rows, axis=0)
    language_count = jnp.sum(rows[:, -128:], axis=0, keepdims=True)
    rows = [lax.dynamic_index_in_dim(rows, at ^ section, 0) for at in range(SECTIONS)]
    sizes = [width, width, 3 * width, width, width, hidden, width]
    ends = [sum(sizes[: at + 1]) for at in range(len(sizes))]
    used = [(0, 0), (0, 1), (0, 2), (0, 3), (0, 4), (0, 5), (1, 3), (1, 4), (1, 5), (1, 6)]
    used += [(0, 6), (2, 0), (2, 1), (2, 2), (3, 3), (3, 4), (3, 5), (3, 6)]
    kept = [rows[slot][:, ends[which] - sizes[which] : ends[which]] for slot, which in used]
    language_count, *kept = weights.join([language_count, *kept], keys1)
    kept = dict(zip(used, kept))

    def row(slot, which):
        return kept[slot, which]

    crossed = weights.cross(keys + keys1)
    sends = weights.payloads(2, "F") if weights.four else weights.payloads(2)
    sends, (info, language_count) = under(sends, info, language_count)
    keys = weights.move(2, sends[:2])
    info, language_count = weights.join(
        [info, language_count + over_core(language_count)], theirs=crossed
    )
    plane_keys = []
    if weights.four:
        weights.mine["plane", 0] = sends[2]
        plane_keys = weights.move_planes(1)
    attend0 = weights.layer("a")
    outputs = attend_forward(
        x0, info, attend0, row(0, 0), row(0, 1), row(0, 2), following=(row(0, 3), row(0, 4))
    )
    y0, qkv0, mixed0, caption_rows = weights.join(outputs, keys)
    caption_rows = to_sections(caption_rows.reshape(-1, width))
    sends = weights.payloads(3, 4) if weights.four else weights.payloads(3)
    caption_rows = weights.join(caption_rows, plane_keys)
    sends, caption_rows = under(sends, *caption_rows)
    early_keys = keys
    keys, sends = weights.move(3, sends[:2]), sends[2:]
    crossed = weights.cross(early_keys)
    if weights.four:
        keys += weights.move_planes(2)
    outputs = shared_forward(caption_rows, expert_inputs[0], expert_inner_bias, expert_outputs[0])
    part = weights.join(outputs, keys, crossed)
    (y0,) = weights.join([y0], theirs=weights.cross([(3, 0), (3, 1)]))
    branch = {at: over_section(part[at], at, [0]) for at in range(1, SECTIONS)}
    keys = weights.move_planes(3) if weights.four else []
    expert1 = weights.layer("e")
    outputs = expert_forward(
        y0, info, expert1, row(1, 3), row(1, 4), row(1, 5), row(1, 6), PATCH_ROWS, "patch"
    )
    outputs, moved = under(outputs, *branch.values())
    if weights.four:
        keys += [("plane", step) for step in range(-2, 3)]
    x2, act1, slope1 = weights.join(outputs, keys)
    branch = dict(zip(branch, moved))
    branch[0] = part[0]
    branch = items_of(by_section(section, branch))
    if weights.four:
        crossed = [("plane", step) for step in range(-3, 4)]
    else:
        for step in (4, 5):
            weights.move(step, weights.payloads(step))
        crossed = [(4, 0), (4, 1), (5, 0)]
    weights.cross(crossed)
    attend2 = weights.layer("c") if weights.four else None
    if not weights.four:
        (x2,) = weights.join([x2], theirs=crossed)
        attend2 = weights.layer("c")
    outputs = attend_forward(
        x2, info, attend2, row(2, 0), row(2, 1), row(2, 2), merge=(y0, branch, row(0, 6))
    )
    if weights.four:
        language_count += over_plane(language_count, [(at, at ^ 1) for at in range(4)])
    x3, qkv2, mixed2, x2, language_count = weights.join([*outputs, language_count], theirs=crossed)
    if weights.four:
        language_count += over_plane(language_count, [(at, at ^ 2) for at in range(4)])
    else:
        language_count = lax.psum(language_count, "z")
    expert3 = weights.layer("f")
    outputs = expert_forward(
        x3, info, expert3, row(3, 3), row(3, 4), row(3, 5), row(3, 6), ROWS, "all"
    )
    layer_output, act3, slope3, language_count = under([*outputs, language_count])[0]
    language_count = language_count[0, 0].astype(jnp.int32)
    vision_count = PATCHES * items * SECTIONS * 2 * planes
    counts = jnp.stack(
        [jnp.full((), vision_count, jnp.int32), language_count, language_count + vision_count]
    )

    def small_rows(values):
        flat = jnp.concatenate(values, axis=1)
        count = -(-flat.shape[1] // hidden)
        flat = jnp.pad(flat, ((0, 0), (0, count * hidden - flat.shape[1])))
        return flat.reshape(count, hidden)

    def to_home(sums, diagonal_last=False):
        got = [by_section(section, sums)]
        for bits in (1, 2, 3):
            sends = {at ^ bits: sums[at] for at in sums}
            payload = by_section(section, sends)
            if bits == 3 and diagonal_last:
                payload = after(payload, got[2])
            got.append(over_section(payload, bits, sorted(sends)))
        return got

    keys = []
    if weights.four:
        sends, (layer_output, last_grad) = under(sends, layer_output, last_grad)
        keys = weights.move(4, sends)
    outputs = expert_backward(
        x3, info, expert3, row(3, 3), row(3, 4), act3, slope3, last_grad, ROWS, "all"
    )
    outputs = weights.join(outputs, keys)
    crossed = weights.cross(keys)
    grad3, *small3 = outputs[:5]
    sums3 = Sums(outputs[5:])
    sums3.cross()
    moved = over_links(sums3.first_sends())
    grad3 = after(grad3, *sums3.sent)
    outputs = attend_backward(
        x2, info, attend2, row(2, 0), row(2, 1), qkv2, mixed2, grad3
    )
    outputs, moved = under(outputs, *moved, sums3.got_stay)
    outputs = weights.join(outputs, theirs=crossed)
    grad2, *small2 = outputs[:4]
    sums2, caption_grad = Sums(outputs[4:8]), outputs[8]
    caption_grads = to_sections(caption_grad.reshape(-1, width))
    sums3.got_stay = moved[2]
    moved3 = over_links(sums3.second_sends(*moved[:2]))
    grad2 = after(grad2, *sums3.sent)
    outputs = expert_backward(
        y0, info, expert1, row(1, 3), row(1, 4), act1, slope1, grad2, PATCH_ROWS, "patch"
    )
    outputs, caption_grads = under(outputs, *caption_grads)
    grad1, *small1 = outputs[:5]
    sums2.cross(grad1)
    sums1 = Sums(outputs[5:])
    sums1.cross()
    inner_quarter = lax.dynamic_slice(row(0, 5), (0, section * width), (1, width))
    sum3 = sums3.whole(*moved3)
    inner_quarter = after(inner_quarter, grad1, sum3)
    outputs = shared_backward(
        caption_rows, caption_grads, info, weights.layer("g"), inner_quarter
    )
    parts, (keep0, send0, inner_grad, outer_grad) = outputs[:4], outputs[4:]
    got = [over_section(parts[bits], bits) for bits in (1, 2, 3)]
    sends = [after(value, *parts) for value in sums1.first_sends()]
    moved1 = over_links(sends)
    keep0 = added(keep0, over_core(send0))
    early = lax.psum(jnp.concatenate([sum3, keep0], axis=0), "z")
    sends2 = [after(value, *sends) for value in sums2.first_sends()]
    moved2 = over_links(sends2)
    parts = [parts[0], *got]
    grad1 = after(grad1, keep0, *sends, *sends2)
    outputs = attend_backward(
        x0,
        info,
        attend0,
        row(0, 0),
        row(0, 1),
        qkv0,
        mixed0,
        grad1,
        first=(y0, row(0, 3), parts),
    )
    outputs, moved = under(outputs, *moved2, *moved1)
    moved2, moved1 = moved[:2], moved[2:]
    tokens_grad, *small_first = outputs[:4]
    sums_first, gain_grad, shift_grad = Sums(outputs[4:8]), outputs[8], outputs[9]
    sums_first.cross()
    inner_grad = lax.dynamic_update_slice(
        jnp.zeros((1, hidden), F32), inner_grad, (0, section * width)
    )
    small = small_rows(
        small_first + [gain_grad, shift_grad, inner_grad, outer_grad] + small2 + small1 + small3
    )
    small = added(small, over_core(small))
    to_x, to_y = sums_first.first_sends()
    to_x = jnp.concatenate([to_x[0], small], axis=0)
    sends = lax.optimization_barrier((*sums1.second_sends(*moved1), to_x, to_y))
    moved1, moved = over_links(sends[:2]), over_links(sends[2:])
    sum1, early = lax.optimization_barrier((sums1.whole(*moved1), early))
    planes1 = Planes(sum1, plane, planes)
    size = to_y.shape[1]
    small = added(small, moved[0][size:])
    to_x, to_y = sums_first.second_sends(moved[0][None, :size], moved[1])
    early_x, early_y = sums2.second_sends(*moved2)
    to_x = jnp.concatenate([to_x[0], early_x[0]], axis=0)
    to_y = jnp.concatenate([to_y[0], early_y[0], small], axis=0)
    to_x, to_y = lax.optimization_barrier((to_x, to_y))
    sent1 = planes1.sends()
    moved = lax.optimization_barrier(tuple(over_links((to_x, to_y))))
    size = early_x.shape[1]
    last = sums_first.whole(moved[0][None, :size], moved[1][None, :size])
    sum2 = sums2.whole(moved[0][None, size:], moved[1][None, size : 2 * size])
    small = added(small, moved[1][2 * size :])
    small_count = small.shape[0]
    eighth = last.shape[1]
    last = jnp.concatenate([last[0], sum2[0], small], axis=0)
    planes_last = Planes(last, plane, planes)
    home_early = to_home({0: after(early[2:], *moved), 3: after(early[:2], *moved)}, diagonal_last=True)
    planes_last.take(*planes_last.sends())
    planes1.take(*sent1)
    planes1.take(*planes1.sends())
    planes1.take(*planes1.sends())
    planes1.take(*planes1.sends())
    planes_last.take(*planes_last.sends())
    planes_last.take(*planes_last.sends())
    home_late = to_home({1: after(planes1.value, *home_early[1:3])})
    planes_last.take(*planes_last.sends())
    last = planes_last.value
    home_attend = to_home({0: last[None, :eighth], 2: last[None, eighth : 2 * eighth]})
    small = planes_last.in_order(last[2 * eighth :].astype(F32))

    as_float = counts.astype(F32)
    one = jnp.ones((), F32)
    attend_scales = jnp.stack([as_float[2], one, as_float[2], one])
    expert_scales = jnp.stack([as_float[1], as_float[0], one, as_float[2]])

    def placed(pieces, theirs, scales):
        scale = lax.dynamic_index_in_dim(scales, section, 0).reshape(1, 1)
        return finish(info, scale, pieces, theirs, planes)

    blank = jnp.zeros_like(home_late[0])
    pieces, theirs = [], []
    for early, late in zip(home_early, home_late):
        pieces.append(by_section(section, {0: early, 1: late, 2: blank, 3: early}))
        before = theirs[-1:] + (home_attend[1:3] if len(theirs) == 3 else [])
        theirs.append(over_core(after(pieces[-1], *before) if before else pieces[-1]))
    inputs_whole, outputs_whole = placed(pieces, theirs, expert_scales)
    inputs_whole, home_attend[3] = lax.optimization_barrier((inputs_whole, home_attend[3]))
    blank = jnp.zeros_like(home_attend[0])
    pieces = [by_section(section, {0: got, 1: blank, 2: got, 3: blank}) for got in home_attend]
    theirs = [over_core(piece) for piece in pieces]
    attend_whole, output_whole = placed(pieces, theirs, attend_scales)

    attend_size, expert_size = 5 * width, 3 * width + hidden
    cuts = [attend_size, attend_size + expert_size]
    cuts += [cuts[1] + attend_size, cuts[1] + attend_size + expert_size]
    small = jnp.split(small.reshape(-1)[: cuts[3] + expert_size], cuts)
    none_attend, none_expert = jnp.zeros_like(small[0]), jnp.zeros_like(small[1])
    attend_small = jnp.stack([small[0], none_attend, small[2], none_attend])
    expert_small = jnp.stack([small[1], small[3], none_expert, small[4]])
    attend_small = attend_small / attend_scales.reshape(-1, 1)
    expert_small = expert_small / expert_scales.reshape(-1, 1)
    attend_small = lax.dynamic_index_in_dim(attend_small, section, 0)
    expert_small = lax.dynamic_index_in_dim(expert_small, section, 0)
    return (
        layer_output[:, :positions],
        tokens_grad[:, :positions],
        attend_small[:, :width],
        attend_small[:, width : 2 * width],
        attend_whole,
        attend_small[:, 2 * width :],
        output_whole,
        expert_small[:, :width],
        expert_small[:, width : 2 * width],
        inputs_whole,
        expert_small[:, 2 * width : 2 * width + hidden],
        outputs_whole,
        expert_small[:, 2 * width + hidden :],
        counts,
    )


def solution(mesh):
    sections, groups = mesh.shape["section"], mesh.shape["dp"]
    split = Mesh(mesh.devices.reshape(sections, groups // 2, 2), ("section", "z", "core"))
    items = P(("section", "z", "core"), None, None)
    flat = P("section", None)
    matrix = P("section", None, None)
    placed = (
        items,
        P(("section", "z", "core")),
        flat,
        flat,
        matrix,
        flat,
        matrix,
        flat,
        flat,
        matrix,
        flat,
        matrix,
        flat,
        items,
    )
    return jax.shard_map(
        per_device,
        mesh=split,
        in_specs=placed,
        out_specs=(
            items,
            items,
            flat,
            flat,
            matrix,
            flat,
            matrix,
            flat,
            flat,
            matrix,
            flat,
            matrix,
            flat,
            P(),
        ),
        check_vma=False,
    )
```

```python
from functools import partial

import jax
import jax.numpy as jnp
from jax import lax
from jax.experimental import pallas as pl
from jax.experimental.pallas import tpu as pltpu
from jax.sharding import Mesh
from jax.sharding import PartitionSpec as P

HEADS = 12
HEAD_DIM = 64
PATCHES = 197
ROWS = 256
CAP_FIRST, CAP_ROWS = 192, 48
PATCH_ROWS = 208
PAIR = 2 * HEAD_DIM
SECTIONS = 4
PIECE_ROWS = 48
VMEM_BYTES = 58 * 1024 * 1024
F32 = jnp.float32
BF16 = jnp.bfloat16

PLAN_FOUR = (
    ({0: "a0", 1: "e0", 2: "c0", 3: "F"}, {0: "a1", 1: "e2", 2: "c0", 3: "F"}),
    ({0: "a1", 1: "e1", 2: "a1", 3: "e2"}, {0: "a0", 1: "a0", 2: "F", 3: "c0"}),
    ({0: "g3", 1: "e2", 2: "c1"}, {0: "e0", 1: "e3", 2: "c1"}),
    ({0: "g1", 1: "e3", 2: "e0", 3: "e3"}, {0: "e1", 1: "e1", 3: "c1"}),
    ({}, {0: "g2", 1: "g3"}),
)
PLAN_ANY = (
    ({0: "a0", 1: "e0", 2: "c0", 3: "f0"}, {0: "a1", 1: "e2", 2: "c0", 3: "f0"}),
    ({0: "a1", 1: "e1", 2: "a1", 3: "e2"}, {0: "a0", 1: "a0", 2: "c1", 3: "f1"}),
    ({0: "g3", 1: "e2", 2: "c1", 3: "f1"}, {0: "e0", 1: "e3", 2: "f0", 3: "f2"}),
    ({0: "g1", 1: "e3", 2: "e0", 3: "e3"}, {0: "e1", 1: "e1", 2: "f1", 3: "f3"}),
    ({0: "c1", 1: "f2", 3: "f2"}, {0: "g2", 1: "g3", 3: "c0"}),
    ({1: "f3", 3: "f3"}, {}),
)
HOMES = {"a": 0, "c": 2, "e": 1, "f": 3, "F": 3, "g": 0}
ATTEND_BLOCKS = ((0, 1), (2, 3))
EXPERT_BLOCKS = ((0, 1), (4, 5), (2, 3), (6, 7))


def dot_plain(left, right):
    return jnp.dot(left, right, preferred_element_type=F32)


def dot_last(left, right):
    return lax.dot_general(left, right, (((1,), (1,)), ((), ())), preferred_element_type=F32)


def dot_first(left, right):
    return lax.dot_general(left, right, (((0,), (0,)), ((), ())), preferred_element_type=F32)


def column_sum(matrix):
    return jnp.sum(matrix.astype(F32), axis=0, keepdims=True)


def norm_parts(rows):
    centre = rows - jnp.mean(rows, axis=-1, keepdims=True)
    scale = lax.rsqrt(jnp.mean(centre * centre, axis=-1, keepdims=True) + 1e-06)
    return centre * scale, scale


def norm_back(normed_grad, unit, scale, gain):
    unit_grad = normed_grad * gain
    along = jnp.mean(unit_grad * unit, axis=-1, keepdims=True)
    return scale * (unit_grad - jnp.mean(unit_grad, axis=-1, keepdims=True) - unit * along)


def true_positions(length, first, count, axis, kind):
    shape = (count, 1) if axis == 0 else (1, count)
    position = first + lax.broadcasted_iota(jnp.int32, shape, axis)
    patch = position < PATCHES
    if kind == "patch":
        return patch
    caption = (position >= PATCHES) & (position - PATCHES < length)
    return caption if kind == "caption" else patch | caption


def head_masks():
    lane = lax.broadcasted_iota(jnp.int32, (1, PAIR), 1)
    even = (lane < HEAD_DIM).astype(F32).astype(BF16)
    odd = (lane >= HEAD_DIM).astype(F32).astype(BF16)
    return lane < HEAD_DIM, even, odd


def split_pair(pair, even, odd):
    return jnp.concatenate([pair * even, pair * odd], axis=0)


def start_weights(info, first, refs, plan, blocks, sems):
    half = blocks.shape[1] // 2
    section, core, plane = info[first], info[first + 1], info[first + 2]
    for at, at_plane, steps in plan:
        here = section == at
        if at_plane is not None:
            here = here & (plane == at_plane)

        @pl.when(here)
        def _(steps=steps):
            for block, source in steps:
                if source[0] == "own":
                    _, which, row, column = source
                    width = blocks.shape[2]
                    for part in range(2):
                        pltpu.make_async_copy(
                            refs[which].at[
                                pl.ds(row + part * half, half), pl.ds(column, width)
                            ],
                            blocks.at[block, pl.ds(part * half, half)],
                            sems.at[block],
                        ).start()
                else:
                    _, mine, theirs, index = source
                    pltpu.make_async_copy(
                        refs[mine].at[index],
                        blocks.at[block, pl.ds(pl.multiple_of(core * half, half), half)],
                        sems.at[block],
                    ).start()
                    pltpu.make_async_copy(
                        refs[theirs].at[index],
                        blocks.at[block, pl.ds(pl.multiple_of((1 - core) * half, half), half)],
                        sems.at[block],
                    ).start()


def wait_block(blocks, block, sems):
    pltpu.make_async_copy(blocks.at[block], blocks.at[block], sems.at[block]).wait()


def store_turned(target, turned, columns, section, core):
    half = target.shape[0] // 2
    for piece in range(16):
        path, owner = (piece >> 2) & 1, piece & 3
        away = owner ^ section
        place = ((away & 1) << 1) | (away >> 1) if path == 0 else away
        row = ((piece >> 3) ^ core) * half + (place >> 1) * (half // 2)
        row = row + path * (half // 4) + (place & 1) * PIECE_ROWS
        target[pl.ds(pl.multiple_of(row, 16), PIECE_ROWS), columns] = turned[
            piece * PIECE_ROWS : (piece + 1) * PIECE_ROWS
        ]


def put_travel(refs, which, columns, left, right):
    half = left.shape[0] // 2
    for side in range(2):
        rows = dot_plain(left[side * half : (side + 1) * half], right).astype(BF16)
        refs[2 * side][which, :, columns] = rows[: half // 2]
        refs[2 * side + 1][which, :, columns] = rows[half // 2 :]


def attend_forward_kernel(plan, weight_count, merge, info, *refs):
    weights, refs = refs[:weight_count], refs[weight_count:]
    if merge:
        x_ref, before_ref, part_ref, outer_ref, gain_ref, shift_ref, bias_ref = refs[:7]
        y_ref, qkv_ref, mixed_ref, joined_ref, blocks, sems, joined = refs[7:]
    else:
        x_ref, gain_ref, shift_ref, bias_ref, next_gain_ref, next_shift_ref = refs[:6]
        y_ref, qkv_ref, mixed_ref, caption_ref, blocks, sems = refs[6:]
    item = pl.program_id(0)
    items = pl.num_programs(0)
    length = info[item]
    width = x_ref.shape[-1]

    @pl.when(item == 0)
    def _():
        start_weights(info, items, weights, plan, blocks, sems)

    cap = slice(CAP_FIRST, CAP_FIRST + CAP_ROWS)
    if merge:
        joined[...] = x_ref[0].astype(F32)
        branch = part_ref[0].astype(F32) + outer_ref[...]
        is_true = true_positions(length, CAP_FIRST, CAP_ROWS, 0, "caption")
        captions = before_ref[0, cap] + jnp.where(is_true, branch, 0.0)
        position = CAP_FIRST + lax.broadcasted_iota(jnp.int32, (CAP_ROWS, 1), 0)
        captions = captions.astype(BF16).astype(F32)
        joined[cap] = jnp.where(position < PATCHES, joined[cap], captions)
        x = joined[...]
        joined_ref[0] = x.astype(BF16)
    else:
        x = x_ref[0].astype(F32)
    unit, _ = norm_parts(x)
    normed = (unit * gain_ref[...] + shift_ref[...]).astype(BF16)

    @pl.when(item == 0)
    def _():
        for block in range(4):
            wait_block(blocks, block, sems)

    queries = dot_plain(normed, blocks[0]) + bias_ref[:, :width]
    qkv_ref[0, :, :width] = (queries * HEAD_DIM ** (-0.5)).astype(BF16)
    qkv_ref[0, :, width : 2 * width] = dot_plain(normed, blocks[1]).astype(BF16)
    values = dot_plain(normed, blocks[2]) + bias_ref[:, width : 2 * width]
    qkv_ref[0, :, 2 * width :] = values.astype(BF16)
    key_true = true_positions(length, 0, ROWS, 1, "all")
    low_half, even, odd = head_masks()
    ones = jnp.ones((ROWS, PAIR), BF16)

    def scores_of(pair):
        at = pair * PAIR
        q2 = qkv_ref[0, :, at : at + PAIR]
        k2 = qkv_ref[0, :, width + at : width + at + PAIR]
        return dot_last(split_pair(q2, even, odd), k2)

    ahead = [scores_of(0), scores_of(1)]
    for pair in range(HEADS // 2):
        at = pair * PAIR
        scores = jnp.where(key_true, ahead.pop(0), -1e9)
        if pair + 2 < HEADS // 2:
            ahead.append(scores_of(pair + 2))
        weight = jnp.exp(scores - jnp.max(scores, axis=-1, keepdims=True)).astype(BF16)
        v2 = qkv_ref[0, :, 2 * width + at : 2 * width + at + PAIR]
        summed = dot_plain(weight, jnp.concatenate([v2, ones], axis=1))
        top = jnp.where(low_half, summed[:ROWS, :PAIR], summed[ROWS:, :PAIR])
        below = jnp.where(low_half, summed[:ROWS, PAIR:], summed[ROWS:, PAIR:])
        mixed_ref[0, :, at : at + PAIR] = (top / below).astype(BF16)
    branch = dot_plain(mixed_ref[0], blocks[3]) + bias_ref[:, 2 * width :]
    row_true = true_positions(length, 0, ROWS, 0, "all")
    y = x + jnp.where(row_true, branch, 0.0)
    y_ref[0] = y.astype(y_ref.dtype)
    if not merge:
        unit, _ = norm_parts(y[cap])
        caption_ref[0] = (unit * next_gain_ref[...] + next_shift_ref[...]).astype(BF16)


def attend_backward_kernel(plan, weight_count, first, info, *refs):
    weights, refs = refs[:weight_count], refs[weight_count:]
    x_ref, gain_ref, shift_ref, qkv_ref, mixed_ref, grad_ref = refs[:6]
    if first:
        after_ref, next_gain_ref, *parts = refs[6:12]
        refs = refs[12:]
    else:
        refs = refs[6:]
    out_ref, gain_grad_ref, shift_grad_ref, bias_grad_ref = refs[:4]
    travel_refs = refs[4:8]
    if first:
        next_gain_grad_ref, next_shift_grad_ref, joined = refs[8], refs[9], refs[-1]
    else:
        caption_ref = refs[8]
    blocks, sems, normed_turned, mixed_turned, branch_all, projected, mixed_grad = refs[
        10 if first else 9 :
    ][:7]
    item = pl.program_id(0)
    items = pl.num_programs(0)
    length = info[item]
    section, core = info[items], info[items + 1]
    width = x_ref.shape[-1]
    here = pl.ds(pl.multiple_of(item * ROWS, ROWS), ROWS)
    cap = slice(CAP_FIRST, CAP_FIRST + CAP_ROWS)

    @pl.when(item == 0)
    def _():
        start_weights(info, items, weights, plan, blocks, sems)

    def add_to(ref, part):
        @pl.when(item == 0)
        def _():
            ref[...] = part

        @pl.when(item > 0)
        def _():
            ref[...] += part

    x = x_ref[0].astype(F32)
    unit, scale = norm_parts(x)
    normed = (unit * gain_ref[...] + shift_ref[...]).astype(BF16)
    incoming = grad_ref[0].astype(F32)
    if first:
        after_unit, after_scale = norm_parts(after_ref[0, cap])
        caption_grad = parts[0][...].astype(F32)
        for part in parts[1:]:
            caption_grad = caption_grad + part[...].astype(F32)
        joined[...] = incoming
        joined[cap] += norm_back(caption_grad, after_unit, after_scale, next_gain_ref[...])
        incoming = joined[...]
        add_to(next_gain_grad_ref, jnp.sum(caption_grad * after_unit, axis=0, keepdims=True))
        add_to(next_shift_grad_ref, jnp.sum(caption_grad, axis=0, keepdims=True))
    row_true = true_positions(length, 0, ROWS, 0, "all")
    branch = jnp.where(row_true, incoming, 0.0).astype(BF16)
    branch_all[here, :] = branch
    store_turned(normed_turned, normed.T, here, section, core)
    store_turned(mixed_turned, mixed_ref[0].T, here, section, core)

    @pl.when(item == 0)
    def _():
        for block in range(4):
            wait_block(blocks, block, sems)

    mixed_grad[...] = dot_last(branch, blocks[3]).astype(BF16)
    key_true = true_positions(length, 0, ROWS, 0, "all")
    _, even, odd = head_masks()

    def products_of(pair):
        at = pair * PAIR
        q2 = split_pair(qkv_ref[0, :, at : at + PAIR], even, odd)
        k2 = qkv_ref[0, :, width + at : width + at + PAIR]
        v2 = qkv_ref[0, :, 2 * width + at : 2 * width + at + PAIR]
        g2 = split_pair(mixed_grad[:, at : at + PAIR], even, odd)
        return q2, k2, g2, dot_last(k2, q2), dot_last(v2, g2)

    ahead = [products_of(0)]
    for pair in range(HEADS // 2):
        at = pair * PAIR
        q2, k2, g2, scores, weight_grad = ahead.pop(0)
        if pair + 1 < HEADS // 2:
            ahead.append(products_of(pair + 1))
        scores = jnp.where(key_true, scores, -1e9)
        weight = jnp.exp(scores - jnp.max(scores, axis=0, keepdims=True))
        weight = weight * (1.0 / jnp.sum(weight, axis=0, keepdims=True))
        product = weight * weight_grad
        along = jnp.sum(product, axis=0, keepdims=True)
        score_grad = (product - weight * along).astype(BF16)
        values_grad = dot_plain(weight.astype(BF16), g2).astype(BF16)
        keys_grad = dot_plain(score_grad, q2).astype(BF16)
        k2_split = split_pair(k2, even, odd)
        stacked = jnp.concatenate([score_grad[:, :ROWS], score_grad[:, ROWS:]], axis=0)
        queries_grad = dot_first(stacked, k2_split).astype(BF16)
        queries_grad = (queries_grad.astype(F32) * HEAD_DIM ** (-0.5)).astype(BF16)
        projected[here, at : at + PAIR] = queries_grad
        projected[here, width + at : width + at + PAIR] = keys_grad
        projected[here, 2 * width + at : 2 * width + at + PAIR] = values_grad
    normed_grad = dot_last(projected[here, :width], blocks[0])
    normed_grad += dot_last(projected[here, width : 2 * width], blocks[1])
    normed_grad += dot_last(projected[here, 2 * width :], blocks[2])
    out = (incoming + norm_back(normed_grad, unit, scale, gain_ref[...])).astype(BF16)
    out_ref[0] = out
    if not first:
        is_true = true_positions(length, CAP_FIRST, CAP_ROWS, 0, "caption")
        caption_ref[0] = jnp.where(is_true, out[cap].astype(F32), 0.0).astype(BF16)
    add_to(gain_grad_ref, jnp.sum(normed_grad * unit, axis=0, keepdims=True))
    add_to(shift_grad_ref, jnp.sum(normed_grad, axis=0, keepdims=True))

    @pl.when(item == items - 1)
    def _():
        for block in range(4):
            columns = slice(block * width, (block + 1) * width)
            left = normed_turned if block < 3 else mixed_turned
            right = projected[:, columns] if block < 3 else branch_all[...]
            put_travel(travel_refs, 0, columns, left, right)
        bias_grad_ref[:, :width] = column_sum(projected[:, :width])
        bias_grad_ref[:, width : 2 * width] = column_sum(projected[:, 2 * width :])
        bias_grad_ref[:, 2 * width :] = column_sum(branch_all[...])


SHORT = pl.CostEstimate(flops=0, bytes_accessed=100_000, transcendentals=0)
LONG = pl.CostEstimate(flops=30_000_000_000, bytes_accessed=30_000_000, transcendentals=0)
ANYWHERE = pl.BlockSpec(memory_space=pl.ANY)


def whole_block(shape):
    return pl.BlockSpec(shape, lambda step, info: (0,) * len(shape))


def item_block(shape):
    return pl.BlockSpec((1,) + shape[1:], lambda step, info: (step,) + (0,) * (len(shape) - 1))


def blocks_scratch(count, width):
    return [pltpu.VMEM((count, width, width), BF16), pltpu.SemaphoreType.DMA((count,))]


def attend_forward(x, info, weights, gain, shift, bias, merge=None, following=None):
    arrays, plan = weights
    items, _, width = x.shape
    row = whole_block((1, width))
    bias_row = whole_block((1, 3 * width))
    caption_shape = (items, CAP_ROWS, width)
    if merge is not None:
        before, part, outer = merge
        operands = (x, before, part, outer, gain, shift, bias)
        specs = [item_block(x.shape), item_block(x.shape), item_block(caption_shape)]
        specs += [row, row, row, bias_row]
        last_shape, kind, scratch = x.shape, BF16, [pltpu.VMEM((ROWS, width), F32)]
    else:
        operands = (x, gain, shift, bias, *following)
        specs = [item_block(x.shape), row, row, bias_row, row, row]
        last_shape, kind, scratch = caption_shape, F32, []
    return pl.pallas_call(
        partial(attend_forward_kernel, plan, len(arrays), merge is not None),
        grid_spec=pltpu.PrefetchScalarGridSpec(
            num_scalar_prefetch=1,
            grid=(items,),
            in_specs=[ANYWHERE] * len(arrays) + specs,
            out_specs=[
                item_block(x.shape),
                item_block((items, ROWS, 3 * width)),
                item_block((items, ROWS, width)),
                item_block(last_shape),
            ],
            scratch_shapes=blocks_scratch(4, width) + scratch,
        ),
        out_shape=[
            jax.ShapeDtypeStruct(x.shape, kind),
            jax.ShapeDtypeStruct((items, ROWS, 3 * width), BF16),
            jax.ShapeDtypeStruct((items, ROWS, width), BF16),
            jax.ShapeDtypeStruct(last_shape, BF16),
        ],
        compiler_params=pltpu.CompilerParams(vmem_limit_bytes=VMEM_BYTES),
        cost_estimate=SHORT,
        name="attend_forward",
    )(info, *arrays, *operands)


def attend_backward(x, info, weights, gain, shift, qkv, mixed, incoming, first=None):
    arrays, plan = weights
    items, _, width = x.shape
    half = width // 2
    row = whole_block((1, width))
    caption_shape = (items, CAP_ROWS, width)
    operands = (x, gain, shift, qkv, mixed, incoming)
    specs = [item_block(x.shape), row, row, item_block(qkv.shape), item_block(mixed.shape)]
    specs += [item_block(incoming.shape)]
    outs = [
        (item_block(x.shape), x.shape, BF16),
        (row, (1, width), F32),
        (row, (1, width), F32),
        (whole_block((1, 3 * width)), (1, 3 * width), F32),
    ]
    outs += [(whole_block((1, half // 2, 4 * width)), (1, half // 2, 4 * width), BF16)] * 4
    scratch = []
    if first is not None:
        after, next_gain, parts = first
        operands += (after, next_gain, *parts)
        caption_rows = pl.BlockSpec((CAP_ROWS, width), lambda step, info: (step, 0))
        specs += [item_block(after.shape), row] + [caption_rows] * 4
        outs += [(row, (1, width), F32)] * 2
        scratch = [pltpu.VMEM((ROWS, width), F32)]
    else:
        outs += [(item_block(caption_shape), caption_shape, BF16)]
    return pl.pallas_call(
        partial(attend_backward_kernel, plan, len(arrays), first is not None),
        grid_spec=pltpu.PrefetchScalarGridSpec(
            num_scalar_prefetch=1,
            grid=(items,),
            in_specs=[ANYWHERE] * len(arrays) + specs,
            out_specs=[spec for spec, _, _ in outs],
            scratch_shapes=blocks_scratch(4, width)
            + [
                pltpu.VMEM((width, items * ROWS), BF16),
                pltpu.VMEM((width, items * ROWS), BF16),
                pltpu.VMEM((items * ROWS, width), BF16),
                pltpu.VMEM((items * ROWS, 3 * width), BF16),
                pltpu.VMEM((ROWS, width), BF16),
            ]
            + scratch,
        ),
        out_shape=[jax.ShapeDtypeStruct(shape, kind) for _, shape, kind in outs],
        compiler_params=pltpu.CompilerParams(vmem_limit_bytes=VMEM_BYTES),
        cost_estimate=LONG,
        name="attend_backward",
    )(info, *arrays, *operands)


def normal_parts(u):
    t = pl.reciprocal(1.0 + 0.23164190 * jnp.abs(u), approx=True)
    bell = jnp.exp2((u * -0.7213475204444817) * u)
    poly = t * (
        0.127414796
        + t * (-0.142248368 + t * (0.7107068705 + t * (-0.7265760135 + t * 0.5307027145)))
    )
    tail = poly * bell
    return jnp.where(u < 0, tail, 1.0 - tail), bell


def inner_forward(normed, matrix, bias):
    inner = dot_plain(normed, matrix) + bias
    cumulative, bell = normal_parts(inner)
    slope = cumulative + (inner * 0.3989422804014327) * bell
    return (inner * cumulative).astype(BF16), slope.astype(BF16)


def expert_forward_kernel(plan, weight_count, count, kind, info, *refs):
    weights, refs = refs[:weight_count], refs[weight_count:]
    x_ref, gain_ref, shift_ref, inner_ref, outer_ref = refs[:5]
    y_ref, act_ref, slope_ref, blocks, sems, normed, total = refs[5:]
    step = pl.program_id(0)
    items, _, width = x_ref.shape

    @pl.when(step == 0)
    def _():
        start_weights(info, items, weights, plan, blocks, sems)
        for item in range(items):
            x = x_ref[item, :count].astype(BF16).astype(F32)
            unit, _ = norm_parts(x)
            normed[item * count : (item + 1) * count] = (
                unit * gain_ref[...] + shift_ref[...]
            ).astype(BF16)

    wait_block(blocks, step, sems)
    wait_block(blocks, step + 4, sems)
    for at in range(0, width, 256):
        columns = slice(at, at + 256)
        act, slope = inner_forward(normed[...], blocks[step, :, columns], inner_ref[:, columns])
        act_ref[:, columns] = act
        slope_ref[:, columns] = slope
    part = dot_plain(act_ref[...], blocks[step + 4])

    @pl.when(step == 0)
    def _():
        total[...] = part

    @pl.when(step > 0)
    def _():
        total[...] += part

    @pl.when(step == pl.num_programs(0) - 1)
    def _():
        for item in range(items):
            row_true = true_positions(info[item], 0, count, 0, kind)
            branch = total[item * count : (item + 1) * count] + outer_ref[...]
            x = x_ref[item, :count].astype(BF16).astype(F32)
            y_ref[item, :count] = (x + jnp.where(row_true, branch, 0.0)).astype(BF16)
            if count < ROWS:
                y_ref[item, count:] = jnp.zeros((ROWS - count, width), BF16)


def expert_backward_kernel(plan, weight_count, count, kind, info, *refs):
    weights, refs = refs[:weight_count], refs[weight_count:]
    x_ref, gain_ref, shift_ref, act_ref, slope_ref, grad_ref = refs[:6]
    out_ref, gain_grad_ref, shift_grad_ref, inner_grad_ref, outer_grad_ref = refs[6:11]
    travel_refs = refs[11:15]
    blocks, sems, normed_turned, branch_turned, branch, inner_all, total = refs[15:]
    step = pl.program_id(0)
    items, _, width = x_ref.shape
    section, core = info[items], info[items + 1]

    @pl.when(step == 0)
    def _():
        start_weights(info, items, weights, plan, blocks, sems)
        outer = None
        for item in range(items):
            here = slice(item * count, (item + 1) * count)
            unit, _ = norm_parts(x_ref[item, :count].astype(BF16).astype(F32))
            normed = (unit * gain_ref[...] + shift_ref[...]).astype(BF16)
            row_true = true_positions(info[item], 0, count, 0, kind)
            incoming = grad_ref[item, :count].astype(F32)
            masked = jnp.where(row_true, incoming, 0.0).astype(BF16)
            branch[here] = masked
            store_turned(normed_turned, normed.T, here, section, core)
            store_turned(branch_turned, masked.T, here, section, core)
            term = column_sum(masked)
            outer = term if outer is None else outer + term
        outer_grad_ref[...] = outer

    wait_block(blocks, step, sems)
    wait_block(blocks, step + 4, sems)
    for at in range(0, width, 256):
        columns = slice(at, at + 256)
        act_grad = dot_last(branch[...], blocks[step + 4, columns])
        inner = (slope_ref[:, columns].astype(F32) * act_grad).astype(BF16)
        inner_all[:, columns] = inner
        inner_grad_ref[:, columns] = column_sum(inner)
        put_travel(travel_refs, 0, columns, normed_turned, inner)
        put_travel(travel_refs, 1, columns, branch_turned, act_ref[:, columns])
    part = dot_last(inner_all[...], blocks[step])

    @pl.when(step == 0)
    def _():
        total[...] = part

    @pl.when(step > 0)
    def _():
        total[...] += part

    @pl.when(step == pl.num_programs(0) - 1)
    def _():
        gain_sum, shift_sum = None, None
        for item in range(items):
            unit, scale = norm_parts(x_ref[item, :count].astype(BF16).astype(F32))
            normed_grad = total[item * count : (item + 1) * count]
            gain_part = jnp.sum(normed_grad * unit, axis=0, keepdims=True)
            shift_part = jnp.sum(normed_grad, axis=0, keepdims=True)
            gain_sum = gain_part if gain_sum is None else gain_sum + gain_part
            shift_sum = shift_part if shift_sum is None else shift_sum + shift_part
            incoming = grad_ref[item, :count].astype(F32)
            hidden = incoming + norm_back(normed_grad, unit, scale, gain_ref[...])
            out_ref[item, :count] = hidden.astype(BF16)
            if count < ROWS:
                out_ref[item, count:] = grad_ref[item, count:]
        gain_grad_ref[...] = gain_sum
        shift_grad_ref[...] = shift_sum


def shared_forward_kernel(*refs):
    *rows_refs, inputs_ref, inner_ref, outputs_ref = refs[:7]
    *part_refs, normed, total = refs[7:]
    count = rows_refs[0].shape[0]
    step = pl.program_id(0)

    @pl.when(step == 0)
    def _():
        for index, ref in enumerate(rows_refs):
            normed[index * count : (index + 1) * count] = ref[...]
        total[...] = jnp.zeros_like(total)

    act, _ = inner_forward(normed[...], inputs_ref[...], inner_ref[...])
    total[...] += dot_plain(act, outputs_ref[...])

    @pl.when(step == pl.num_programs(0) - 1)
    def _():
        for index, ref in enumerate(part_refs):
            ref[...] = total[index * count : (index + 1) * count].astype(BF16)


def shared_backward_kernel(plan, weight_count, info, *refs):
    weights, refs = refs[:weight_count], refs[weight_count:]
    rows_refs, grad_refs, inner_ref = refs[:4], refs[4:8], refs[8]
    part_refs, (keep_ref, send_ref, inner_grad_ref, outer_grad_ref) = refs[9:13], refs[13:17]
    blocks, sems, normed, branch, matrix = refs[17:]
    count, width = rows_refs[0].shape
    half = width // 2
    first = info.shape[0] - 3
    core = info[first + 1]
    start_weights(info, first, weights, plan, blocks, sems)
    for index in range(SECTIONS):
        here = slice(index * count, (index + 1) * count)
        normed[here] = rows_refs[index][...]
        branch[here] = grad_refs[index][...]
    outer_grad_ref[...] = column_sum(grad_refs[0][...])
    wait_block(blocks, 0, sems)
    wait_block(blocks, 1, sems)
    part = None
    for at in range(0, width, 256):
        columns = slice(at, at + 256)
        act, slope = inner_forward(normed[...], blocks[0, :, columns], inner_ref[:, columns])
        act_grad = dot_last(branch[...], blocks[1, columns])
        inner = (slope.astype(F32) * act_grad).astype(BF16)
        inner_grad_ref[:, columns] = column_sum(inner)
        matrix[0, :, columns] = dot_first(normed[...], inner).astype(BF16)
        matrix[1, :, columns] = dot_first(branch[...], act).astype(BF16)
        term = dot_last(inner, blocks[0, :, columns])
        part = term if part is None else part + term
    for index, ref in enumerate(part_refs):
        ref[...] = part[index * count : (index + 1) * count].astype(BF16)
    quarter = half // 4
    for which in range(2):
        for group in range(4):
            columns = slice(group * width, (group + 1) * width)
            mine = pl.multiple_of(core * half, 16) + group * quarter
            other = pl.multiple_of((1 - core) * half, 16) + group * quarter
            keep_ref[which, :, columns] = matrix[which, pl.ds(pl.multiple_of(mine, 16), quarter)]
            send_ref[which, :, columns] = matrix[which, pl.ds(pl.multiple_of(other, 16), quarter)]


def chunk_columns(rows, width):
    return pl.BlockSpec((rows, width), lambda step, info: (0, step))


def expert_forward(x, info, weights, gain, shift, inner, outer, count, kind):
    arrays, plan = weights
    items, _, width = x.shape
    hidden = inner.shape[1]
    row = whole_block((1, width))
    return pl.pallas_call(
        partial(expert_forward_kernel, plan, len(arrays), count, kind),
        grid_spec=pltpu.PrefetchScalarGridSpec(
            num_scalar_prefetch=1,
            grid=(hidden // width,),
            in_specs=[ANYWHERE] * len(arrays)
            + [whole_block(x.shape), row, row, chunk_columns(1, width), row],
            out_specs=[
                whole_block((items, ROWS, width)),
                chunk_columns(items * count, width),
                chunk_columns(items * count, width),
            ],
            scratch_shapes=blocks_scratch(8, width)
            + [
                pltpu.VMEM((items * count, width), BF16),
                pltpu.VMEM((items * count, width), F32),
            ],
        ),
        out_shape=[
            jax.ShapeDtypeStruct((items, ROWS, width), BF16),
            jax.ShapeDtypeStruct((items * count, hidden), BF16),
            jax.ShapeDtypeStruct((items * count, hidden), BF16),
        ],
        compiler_params=pltpu.CompilerParams(vmem_limit_bytes=VMEM_BYTES),
        cost_estimate=SHORT,
        name="expert_forward_" + kind,
    )(info, *arrays, x, gain, shift, inner, outer)


def expert_backward(x, info, weights, gain, shift, act, slope, incoming, count, kind):
    arrays, plan = weights
    items, _, width = x.shape
    half = width // 2
    hidden = act.shape[1]
    row = whole_block((1, width))
    travel = pl.BlockSpec((2, half // 2, width), lambda step, info: (0, 0, step))
    return pl.pallas_call(
        partial(expert_backward_kernel, plan, len(arrays), count, kind),
        grid_spec=pltpu.PrefetchScalarGridSpec(
            num_scalar_prefetch=1,
            grid=(hidden // width,),
            in_specs=[ANYWHERE] * len(arrays)
            + [
                whole_block(x.shape),
                row,
                row,
                chunk_columns(items * count, width),
                chunk_columns(items * count, width),
                whole_block(incoming.shape),
            ],
            out_specs=[whole_block(incoming.shape), row, row, chunk_columns(1, width), row]
            + [travel] * 4,
            scratch_shapes=blocks_scratch(8, width)
            + [
                pltpu.VMEM((width, items * count), BF16),
                pltpu.VMEM((width, items * count), BF16),
                pltpu.VMEM((items * count, width), BF16),
                pltpu.VMEM((items * count, width), BF16),
                pltpu.VMEM((items * count, width), F32),
            ],
        ),
        out_shape=[
            jax.ShapeDtypeStruct(incoming.shape, BF16),
            jax.ShapeDtypeStruct((1, width), F32),
            jax.ShapeDtypeStruct((1, width), F32),
            jax.ShapeDtypeStruct((1, hidden), F32),
            jax.ShapeDtypeStruct((1, width), F32),
        ]
        + [jax.ShapeDtypeStruct((2, half // 2, hidden), BF16)] * 4,
        compiler_params=pltpu.CompilerParams(vmem_limit_bytes=VMEM_BYTES),
        cost_estimate=SHORT,
        name="expert_backward_" + kind,
    )(info, *arrays, x, gain, shift, act, slope, incoming)


IN_VMEM = pl.BlockSpec(memory_space=pltpu.VMEM)
IN_SMEM = pl.BlockSpec(memory_space=pltpu.SMEM)


def shared_forward(rows, inputs, inner, outputs):
    count, width = rows[0].shape
    total = SECTIONS * count
    hidden = inner.shape[1]
    return pl.pallas_call(
        shared_forward_kernel,
        grid=(hidden // width,),
        in_specs=[pl.BlockSpec(rows[0].shape, lambda step: (0, 0))] * 4
        + [
            pl.BlockSpec((width, width), lambda step: (0, step)),
            pl.BlockSpec((1, width), lambda step: (0, step)),
            pl.BlockSpec((width, width), lambda step: (step, 0)),
        ],
        out_specs=[pl.BlockSpec((count, width), lambda step: (0, 0))] * SECTIONS,
        scratch_shapes=[pltpu.VMEM((total, width), BF16), pltpu.VMEM((total, width), F32)],
        out_shape=[jax.ShapeDtypeStruct((count, width), BF16)] * SECTIONS,
        compiler_params=pltpu.CompilerParams(vmem_limit_bytes=VMEM_BYTES),
        cost_estimate=SHORT,
        name="shared_forward",
    )(*rows, inputs, inner, outputs)


def shared_backward(rows, grads, info, weights, inner):
    arrays, plan = weights
    count, width = rows[0].shape
    total = SECTIONS * count
    travel = (2, width // 8, 4 * width)
    return pl.pallas_call(
        partial(shared_backward_kernel, plan, len(arrays)),
        in_specs=[IN_SMEM] + [ANYWHERE] * len(arrays) + [IN_VMEM] * 9,
        out_specs=[IN_VMEM] * 8,
        scratch_shapes=blocks_scratch(2, width)
        + [
            pltpu.VMEM((total, width), BF16),
            pltpu.VMEM((total, width), BF16),
            pltpu.VMEM((2, width, width), BF16),
        ],
        out_shape=[
            *[jax.ShapeDtypeStruct((count, width), BF16)] * SECTIONS,
            jax.ShapeDtypeStruct(travel, BF16),
            jax.ShapeDtypeStruct(travel, BF16),
            jax.ShapeDtypeStruct((1, width), F32),
            jax.ShapeDtypeStruct((1, width), F32),
        ],
        compiler_params=pltpu.CompilerParams(vmem_limit_bytes=VMEM_BYTES),
        cost_estimate=SHORT,
        name="shared_backward",
    )(info, *arrays, *rows, *grads, inner)


def plane_turn(plane, planes):
    return ((plane & 1) << 1) | (plane >> 1) if planes == 4 else 0


def finish_kernel(planes, info, scale_ref, *refs):
    step = pl.program_id(0)
    mine, theirs, outs, placed = refs[:4], refs[4:8], refs[8:-1], refs[-1]
    count = mine[0].shape[0]
    width = placed.shape[1]
    half = width // 2
    at = info.shape[0] - 3
    section, core = info[at], info[at + 1]
    turn = plane_turn(info[at + 2], planes)
    turned = turn if count == 1 else jnp.where(section == 1, turn, 0)
    scale = scale_ref[0, 0]
    columns = pl.ds(pl.multiple_of((step ^ turned) * width, width), width)

    def place(which):
        def by_rows():
            for side, pieces in enumerate((mine, theirs)):
                for away, ref in enumerate(pieces):
                    for path in range(2):
                        row = (core ^ side) * half + path * (half // 2)
                        row = row + (section ^ away) * PIECE_ROWS
                        placed[pl.ds(pl.multiple_of(row, 16), PIECE_ROWS), :] = ref[
                            which, path * PIECE_ROWS : (path + 1) * PIECE_ROWS, columns
                        ].astype(F32)

        def by_columns():
            for side, pieces in enumerate((mine, theirs)):
                for away, ref in enumerate(pieces):

                    @pl.when(step == away)
                    def _(side=side, ref=ref):
                        for group in range(4):
                            quarter = half // 4
                            row = (core ^ side) * half + group * quarter
                            placed[pl.ds(pl.multiple_of(row, 16), quarter), :] = ref[
                                which, :, group * width : (group + 1) * width
                            ].astype(F32)

        if count == 1:
            by_rows()
        else:
            pl.when(section != 0)(by_rows)
            pl.when(section == 0)(by_columns)

    place(0)
    if count == 1:

        @pl.when(step < 3)
        def _():
            outs[0][0] = placed[...] / scale

        @pl.when(step == 3)
        def _():
            outs[1][0] = placed[...] / scale

    else:
        outs[0][0] = placed[...] / scale
        place(1)
        outs[1][0] = (placed[...] / scale).T


def finish(info, scale, mine, theirs, planes):
    count, _, hidden = mine[0].shape
    width = hidden // 4
    if count == 1:
        shapes = [(1, width, 3 * width), (1, width, width)]
        maps = [lambda step, info: (0, 0, jnp.minimum(step, 2)), lambda step, info: (0, 0, 0)]
    else:
        shapes = [(1, width, hidden), (1, hidden, width)]
        maps = [lambda step, info: (0, 0, step), lambda step, info: (0, step, 0)]
    return pl.pallas_call(
        partial(finish_kernel, planes),
        grid_spec=pltpu.PrefetchScalarGridSpec(
            num_scalar_prefetch=1,
            grid=(4,),
            in_specs=[IN_SMEM] + [whole_block(mine[0].shape)] * 8,
            out_specs=[pl.BlockSpec((1, width, width), at) for at in maps],
            scratch_shapes=[pltpu.VMEM((width, width), F32)],
        ),
        out_shape=[jax.ShapeDtypeStruct(shape, F32) for shape in shapes],
        compiler_params=pltpu.CompilerParams(vmem_limit_bytes=VMEM_BYTES),
        cost_estimate=SHORT,
        name="finish",
    )(info, scale, *mine, *theirs)


def pack_kernel(count, plan, info, *refs):
    sources, outs, sems = refs[:count], refs[count:-1], refs[-1]
    first = info.shape[0] - 3
    section, core, plane = info[first], info[first + 1], info[first + 2]
    half = outs[0].shape[1]
    for index, (out, choices) in enumerate(zip(outs, plan)):
        for at, at_plane, parts in choices:
            here = section == at
            if at_plane is not None:
                here = here & (plane == at_plane)

            @pl.when(here)
            def _(index=index, out=out, parts=parts):
                for block, part in enumerate(parts):
                    if part[0] == "own":
                        _, which, row, column = part
                        rows = pl.ds(pl.multiple_of(row + core * half, half), half)
                        source = sources[which].at[rows, pl.ds(column, out.shape[2])]
                    else:
                        source = sources[part[1]].at[block]
                    pltpu.make_async_copy(source, out.at[block], sems.at[index, block]).start()

    for index, out in enumerate(outs):
        for block in range(2):
            pltpu.make_async_copy(out.at[block], out.at[block], sems.at[index, block]).wait()


def pack(info, sources, plan, shape):
    return pl.pallas_call(
        partial(pack_kernel, len(sources), plan),
        in_specs=[IN_SMEM] + [ANYWHERE] * len(sources),
        out_specs=[IN_VMEM] * len(plan),
        scratch_shapes=[pltpu.SemaphoreType.DMA((len(plan), 2))],
        out_shape=[jax.ShapeDtypeStruct(shape, BF16)] * len(plan),
        cost_estimate=SHORT,
        name="pack",
    )(info, *sources)


def over_section(value, bits, sources=range(SECTIONS)):
    return lax.ppermute(value, "section", [(at, at ^ bits) for at in sources])


def over_core(value):
    return lax.ppermute(value, "core", [(0, 1), (1, 0)])


def over_plane(value, pairs):
    return lax.ppermute(value, "z", pairs)


def added(left, right):
    return (left.astype(F32) + right.astype(F32)).astype(BF16)


def after(value, *earlier):
    return lax.optimization_barrier((value,) + earlier)[0]


def under(outputs, *arrivals):
    joined = lax.optimization_barrier(tuple(outputs) + arrivals)
    return list(joined[: len(outputs)]), list(joined[len(outputs) :])


def by_section(section, values):
    result, last = None, None
    for at in sorted(values):
        if result is None:
            result = values[at]
        elif values[at] is not last:
            result = jnp.where(section >= at, values[at], result)
        last = values[at]
    return result


def total(*values):
    result = values[0].astype(F32)
    for value in values[1:]:
        result = result + value.astype(F32)
    return result.astype(BF16)


class Sums:
    def __init__(self, travel):
        self.stay, self.move, self.other_stay, self.other_move = travel
        self.size = self.stay.shape[1] // 2

    def cross(self, *earlier):
        if earlier:
            self.other_move = after(self.other_move, *earlier)
            self.other_stay = after(self.other_stay, *earlier)
        self.got_move, self.got_stay = over_core(self.other_move), over_core(self.other_stay)

    def first_sends(self):
        size = self.size
        self.sent = [
            total(self.move[:, at : at + size], self.got_move[:, at : at + size])
            for at in (0, size)
        ]
        return self.sent

    def second_sends(self, from_x, from_y):
        size, half = self.size, self.size // 2
        self.first = from_x, from_y
        to_y = total(self.stay[:, half:size], self.got_stay[:, half:size], from_x[:, half:])
        to_x = total(
            self.stay[:, size + half :], self.got_stay[:, size + half :], from_y[:, half:]
        )
        self.sent = [to_x, to_y]
        return self.sent

    def whole(self, from_x, from_y):
        size, half = self.size, self.size // 2
        parts = []
        for at, first, second in ((0, self.first[0], from_y), (size, self.first[1], from_x)):
            here = slice(at, at + half)
            parts.append(total(self.stay[:, here], self.got_stay[:, here], first[:, :half], second))
        return jnp.concatenate(parts, axis=1)


def over_links(sends):
    return [over_section(sends[0], 1), over_section(sends[1], 2)]


class Planes:
    def __init__(self, value, plane, planes):
        self.value, self.plane, self.planes, self.turn = value, plane, planes, 0

    def sends(self, *earlier):
        value = after(self.value, *earlier) if earlier else self.value
        if self.planes != 4:
            return (value,)
        bits = (1, 2, 2, 1)[self.turn]
        if self.turn < 2:
            bit = (self.plane & 1, self.plane >> 1)[self.turn]
            size = value.shape[-1] // 2
            value = lax.dynamic_slice_in_dim(value, (1 - bit) * size, size, value.ndim - 1)
        return (over_plane(value, [(at, at ^ bits) for at in range(4)]),)

    def take(self, arrived):
        if self.planes != 4:
            self.value = lax.psum(arrived, "z") if self.turn == 3 else arrived
        elif self.turn < 2:
            bit = (self.plane & 1, self.plane >> 1)[self.turn]
            size = self.value.shape[-1] // 2
            keep = lax.dynamic_slice_in_dim(self.value, bit * size, size, self.value.ndim - 1)
            self.value = added(keep, arrived)
        else:
            self.value = jnp.concatenate([self.value, arrived], axis=-1)
        self.turn += 1

    def in_order(self, value):
        if self.planes != 4:
            return value
        size, turn = value.shape[-1] // 4, plane_turn(self.plane, 4)
        parts = [
            lax.dynamic_slice_in_dim(value, (at ^ turn) * size, size, value.ndim - 1)
            for at in range(4)
        ]
        return jnp.concatenate(parts, axis=-1)


class Weights:
    def __init__(self, own, info, planes):
        self.own, self.info = own, info
        self.four = planes == 4
        self.plan = PLAN_FOUR if self.four else PLAN_ANY
        self.half, self.width = own[1].shape[0] // 2, own[1].shape[1]
        self.mine, self.theirs, self.arrived = {}, {}, {}

    def place(self, layer, block):
        if layer in "ac":
            return (0, 0, block * self.width) if block < 3 else (1, 0, 0)
        if layer == "g":
            return (2, 0, block * self.width) if block < 4 else (3, (block - 4) * self.width, 0)
        return (2, 0, block * self.width) if block < 4 else (3, (block - 4) * self.width, 0)

    def choices(self, sends, sources):
        result = []
        for at in range(SECTIONS):
            name = sends.get(at)
            if name is not None and HOMES[name[0]] != at:
                key = self.arrived[at, name]
                if key not in sources:
                    sources[key] = len(self.own) + len(sources)
                result.append((at, None, [("arrived", sources[key])] * 2))
                continue
            for plane in range(4) if name == "F" else (None,):
                piece = ("f" + str(plane)) if name == "F" else name or "a0"
                layer, index = piece[0], int(piece[1])
                if layer in "ac":
                    blocks = ATTEND_BLOCKS[index]
                else:
                    blocks = (index, 4 + index) if layer == "g" else EXPERT_BLOCKS[index]
                parts = [("own",) + self.place(layer, block) for block in blocks]
                result.append((at, plane, parts))
        return result

    def packed(self, wanted):
        sources = {}
        plan = [self.choices(sends, sources) for sends in wanted]
        arrays = list(self.own) + [self.mine[key] for key in sources]
        return pack(self.info, arrays, plan, (2, self.half, self.width))

    def sends(self, step):
        if step == "F":
            return [{at: "F" for at in range(SECTIONS)}]
        return [sends for sends in self.plan[step] if sends]

    def payloads(self, *steps):
        wanted = [sends for step in steps for sends in self.sends(step)]
        return list(self.packed(wanted))

    def move(self, step, payloads):
        links = [(link, sends) for link, sends in enumerate(self.plan[step]) if sends]
        for (link, sends), payload in zip(links, payloads):
            self.mine[step, link] = over_section(payload, link + 1, sorted(sends))
            for at, name in sends.items():
                self.arrived[at ^ (link + 1), name] = (step, link)
        return [(step, link) for link, _ in links]

    def move_planes(self, step):
        up, down = self.mine["plane", step - 1], self.mine["plane", 1 - step]
        up = over_plane(up, [(at, at + 1) for at in range(step - 1, 3)])
        down = over_plane(down, [(at, at - 1) for at in range(4 - step, 0, -1)])
        self.mine["plane", step], self.mine["plane", -step] = up, down
        return [("plane", step), ("plane", -step)]

    def cross(self, keys):
        for key in keys:
            self.theirs[key] = over_core(self.mine[key])
        return keys

    def join(self, outputs, mine=(), theirs=()):
        values = [self.mine[key] for key in mine] + [self.theirs[key] for key in theirs]
        outputs, values = under(outputs, *values)
        for key, value in zip(mine, values):
            self.mine[key] = value
        for key, value in zip(theirs, values[len(mine) :]):
            self.theirs[key] = value
        return outputs

    def layer(self, layer):
        arrays, places = list(self.own), {}

        def place(key):
            if key not in places:
                places[key] = len(arrays)
                arrays.extend([self.mine[key], self.theirs[key]])
            return places[key], places[key] + 1

        if layer in "ac":
            names = [(layer + str(index), ATTEND_BLOCKS[index]) for index in range(2)]
        else:
            names = [(layer + str(index), EXPERT_BLOCKS[index]) for index in range(4)]
        plan = []
        for at in range(SECTIONS):
            if layer == "g":
                names = [("g" + str(at), (0, 1))]
            if HOMES[layer] == at:
                steps = []
                for name, blocks in names:
                    for block in blocks:
                        source = block * 4 if layer == "g" else block
                        steps.append((block, ("own",) + self.place(layer, source)))
                plan.append((at, None, steps))
                continue
            by_plane = layer == "f" and self.four
            for plane in range(4) if by_plane else (None,):
                steps = []
                for index, (name, blocks) in enumerate(names):
                    key = ("plane", plane - index) if by_plane else self.arrived[at, name]
                    for which, block in enumerate(blocks):
                        steps.append((block, ("piece",) + place(key) + (which,)))
                plan.append((at, plane, steps))
        return arrays, plan


def per_device(
    tokens,
    caption_lengths,
    attend_gain,
    attend_shift,
    attend_inputs,
    attend_bias,
    attend_output,
    expert_gain,
    expert_shift,
    expert_inputs,
    expert_inner_bias,
    expert_outputs,
    expert_outer_bias,
    cotangent,
):
    section, core, plane = lax.axis_index("section"), lax.axis_index("core"), lax.axis_index("z")
    planes = lax.axis_size("z")
    items, positions, width = tokens.shape
    hidden = expert_inputs.shape[-1]
    info = [value.reshape(1).astype(jnp.int32) for value in (section, core, plane)]
    info = jnp.concatenate([caption_lengths] + info)
    weights = Weights(
        (attend_inputs[0], attend_output[0], expert_inputs[0], expert_outputs[0]), info, planes
    )

    def to_sections(value):
        return [value] + [over_section(value, bits) for bits in (1, 2, 3)]

    def items_of(part):
        return part.reshape(items, CAP_ROWS, width)

    keys = weights.move(0, weights.payloads(0))
    pad = ((0, 0), (0, ROWS - positions), (0, 0))
    x0 = jnp.pad(tokens, pad)
    last_grad = jnp.pad(cotangent, pad)
    rows = jnp.concatenate(
        [
            attend_gain,
            attend_shift,
            attend_bias,
            expert_gain,
            expert_shift,
            expert_inner_bias,
            expert_outer_bias,
            jnp.full((1, 128), jnp.sum(caption_lengths), F32),
        ],
        axis=1,
    )
    rows = to_sections(rows)
    x0, last_grad, *rows = weights.join([x0, last_grad, *rows], keys)
    keys1 = weights.move(1, weights.payloads(1))
    rows = jnp.concatenate(rows, axis=0)
    language_count = jnp.sum(rows[:, -128:], axis=0, keepdims=True)
    rows = [lax.dynamic_index_in_dim(rows, at ^ section, 0) for at in range(SECTIONS)]
    sizes = [width, width, 3 * width, width, width, hidden, width]
    ends = [sum(sizes[: at + 1]) for at in range(len(sizes))]
    used = [(0, 0), (0, 1), (0, 2), (0, 3), (0, 4), (0, 5), (1, 3), (1, 4), (1, 5), (1, 6)]
    used += [(0, 6), (2, 0), (2, 1), (2, 2), (3, 3), (3, 4), (3, 5), (3, 6)]
    kept = [rows[slot][:, ends[which] - sizes[which] : ends[which]] for slot, which in used]
    language_count, *kept = weights.join([language_count, *kept], keys1)
    kept = dict(zip(used, kept))

    def row(slot, which):
        return kept[slot, which]

    crossed = weights.cross(keys + keys1)
    sends = weights.payloads(2, "F") if weights.four else weights.payloads(2)
    sends, (info, language_count) = under(sends, info, language_count)
    keys = weights.move(2, sends[:2])
    info, language_count = weights.join(
        [info, language_count + over_core(language_count)], theirs=crossed
    )
    plane_keys = []
    if weights.four:
        weights.mine["plane", 0] = sends[2]
        plane_keys = weights.move_planes(1)
    attend0 = weights.layer("a")
    outputs = attend_forward(
        x0, info, attend0, row(0, 0), row(0, 1), row(0, 2), following=(row(0, 3), row(0, 4))
    )
    y0, qkv0, mixed0, caption_rows = weights.join(outputs, keys)
    caption_rows = to_sections(caption_rows.reshape(-1, width))
    sends = weights.payloads(3, 4) if weights.four else weights.payloads(3)
    caption_rows = weights.join(caption_rows, plane_keys)
    sends, caption_rows = under(sends, *caption_rows)
    early_keys = keys
    keys, sends = weights.move(3, sends[:2]), sends[2:]
    crossed = weights.cross(early_keys)
    if weights.four:
        keys += weights.move_planes(2)
    outputs = shared_forward(caption_rows, expert_inputs[0], expert_inner_bias, expert_outputs[0])
    part = weights.join(outputs, keys, crossed)
    (y0,) = weights.join([y0], theirs=weights.cross([(3, 0), (3, 1)]))
    branch = {at: over_section(part[at], at, [0]) for at in range(1, SECTIONS)}
    keys = weights.move_planes(3) if weights.four else []
    expert1 = weights.layer("e")
    outputs = expert_forward(
        y0, info, expert1, row(1, 3), row(1, 4), row(1, 5), row(1, 6), PATCH_ROWS, "patch"
    )
    outputs, moved = under(outputs, *branch.values())
    if weights.four:
        keys += [("plane", step) for step in range(-2, 3)]
    x2, act1, slope1 = weights.join(outputs, keys)
    branch = dict(zip(branch, moved))
    branch[0] = part[0]
    branch = items_of(by_section(section, branch))
    if weights.four:
        crossed = [("plane", step) for step in range(-3, 4)]
    else:
        for step in (4, 5):
            weights.move(step, weights.payloads(step))
        crossed = [(4, 0), (4, 1), (5, 0)]
    weights.cross(crossed)
    attend2 = weights.layer("c") if weights.four else None
    if not weights.four:
        (x2,) = weights.join([x2], theirs=crossed)
        attend2 = weights.layer("c")
    outputs = attend_forward(
        x2, info, attend2, row(2, 0), row(2, 1), row(2, 2), merge=(y0, branch, row(0, 6))
    )
    if weights.four:
        language_count += over_plane(language_count, [(at, at ^ 1) for at in range(4)])
    x3, qkv2, mixed2, x2, language_count = weights.join([*outputs, language_count], theirs=crossed)
    if weights.four:
        language_count += over_plane(language_count, [(at, at ^ 2) for at in range(4)])
    else:
        language_count = lax.psum(language_count, "z")
    expert3 = weights.layer("f")
    outputs = expert_forward(
        x3, info, expert3, row(3, 3), row(3, 4), row(3, 5), row(3, 6), 240, "all"
    )
    layer_output, act3, slope3, language_count = under([*outputs, language_count])[0]
    language_count = language_count[0, 0].astype(jnp.int32)
    vision_count = PATCHES * items * SECTIONS * 2 * planes
    counts = jnp.stack(
        [jnp.full((), vision_count, jnp.int32), language_count, language_count + vision_count]
    )

    def small_rows(values):
        flat = jnp.concatenate(values, axis=1)
        count = -(-flat.shape[1] // hidden)
        flat = jnp.pad(flat, ((0, 0), (0, count * hidden - flat.shape[1])))
        return flat.reshape(count, hidden)

    def to_home(sums, diagonal_last=False):
        got = [by_section(section, sums)]
        for bits in (1, 2, 3):
            sends = {at ^ bits: sums[at] for at in sums}
            payload = by_section(section, sends)
            if bits == 3 and diagonal_last:
                payload = after(payload, got[2])
            got.append(over_section(payload, bits, sorted(sends)))
        return got

    keys = []
    if weights.four:
        sends, (layer_output, last_grad) = under(sends, layer_output, last_grad)
        keys = weights.move(4, sends)
    outputs = expert_backward(
        x3, info, expert3, row(3, 3), row(3, 4), act3, slope3, last_grad, 240, "all"
    )
    outputs = weights.join(outputs, keys)
    crossed = weights.cross(keys)
    grad3, *small3 = outputs[:5]
    sums3 = Sums(outputs[5:])
    sums3.cross()
    moved = over_links(sums3.first_sends())
    grad3 = after(grad3, *sums3.sent)
    outputs = attend_backward(
        x2, info, attend2, row(2, 0), row(2, 1), qkv2, mixed2, grad3
    )
    outputs, moved = under(outputs, *moved, sums3.got_stay)
    outputs = weights.join(outputs, theirs=crossed)
    grad2, *small2 = outputs[:4]
    sums2, caption_grad = Sums(outputs[4:8]), outputs[8]
    caption_grads = to_sections(caption_grad.reshape(-1, width))
    sums3.got_stay = moved[2]
    moved3 = over_links(sums3.second_sends(*moved[:2]))
    grad2 = after(grad2, *sums3.sent)
    outputs = expert_backward(
        y0, info, expert1, row(1, 3), row(1, 4), act1, slope1, grad2, PATCH_ROWS, "patch"
    )
    outputs, caption_grads = under(outputs, *caption_grads)
    grad1, *small1 = outputs[:5]
    sums2.cross(grad1)
    sums1 = Sums(outputs[5:])
    sums1.cross()
    inner_quarter = lax.dynamic_slice(row(0, 5), (0, section * width), (1, width))
    sum3 = sums3.whole(*moved3)
    inner_quarter = after(inner_quarter, grad1, sum3)
    outputs = shared_backward(
        caption_rows, caption_grads, info, weights.layer("g"), inner_quarter
    )
    parts, (keep0, send0, inner_grad, outer_grad) = outputs[:4], outputs[4:]
    got = [over_section(parts[bits], bits) for bits in (1, 2, 3)]
    sends = [after(value, *parts) for value in sums1.first_sends()]
    moved1 = over_links(sends)
    keep0 = added(keep0, over_core(send0))
    early = lax.psum(jnp.concatenate([sum3, keep0], axis=0), "z")
    sends2 = [after(value, *sends) for value in sums2.first_sends()]
    moved2 = over_links(sends2)
    parts = [parts[0], *got]
    grad1 = after(grad1, keep0, *sends, *sends2)
    outputs = attend_backward(
        x0,
        info,
        attend0,
        row(0, 0),
        row(0, 1),
        qkv0,
        mixed0,
        grad1,
        first=(y0, row(0, 3), parts),
    )
    outputs, moved = under(outputs, *moved2, *moved1)
    moved2, moved1 = moved[:2], moved[2:]
    tokens_grad, *small_first = outputs[:4]
    sums_first, gain_grad, shift_grad = Sums(outputs[4:8]), outputs[8], outputs[9]
    sums_first.cross()
    inner_grad = lax.dynamic_update_slice(
        jnp.zeros((1, hidden), F32), inner_grad, (0, section * width)
    )
    small = small_rows(
        small_first + [gain_grad, shift_grad, inner_grad, outer_grad] + small2 + small1 + small3
    )
    small = added(small, over_core(small))
    to_x, to_y = sums_first.first_sends()
    to_x = jnp.concatenate([to_x[0], small], axis=0)
    sends = lax.optimization_barrier((*sums1.second_sends(*moved1), to_x, to_y))
    moved1, moved = over_links(sends[:2]), over_links(sends[2:])
    sum1, early = lax.optimization_barrier((sums1.whole(*moved1), early))
    planes1 = Planes(sum1, plane, planes)
    size = to_y.shape[1]
    small = added(small, moved[0][size:])
    to_x, to_y = sums_first.second_sends(moved[0][None, :size], moved[1])
    early_x, early_y = sums2.second_sends(*moved2)
    to_x = jnp.concatenate([to_x[0], early_x[0]], axis=0)
    to_y = jnp.concatenate([to_y[0], early_y[0], small], axis=0)
    to_x, to_y = lax.optimization_barrier((to_x, to_y))
    sent1 = planes1.sends()
    moved = lax.optimization_barrier(tuple(over_links((to_x, to_y))))
    size = early_x.shape[1]
    last = sums_first.whole(moved[0][None, :size], moved[1][None, :size])
    sum2 = sums2.whole(moved[0][None, size:], moved[1][None, size : 2 * size])
    small = added(small, moved[1][2 * size :])
    small_count = small.shape[0]
    eighth = last.shape[1]
    last = jnp.concatenate([last[0], sum2[0], small], axis=0)
    planes_last = Planes(last, plane, planes)
    home_early = to_home({0: after(early[2:], *moved), 3: after(early[:2], *moved)}, diagonal_last=True)
    planes_last.take(*planes_last.sends())
    planes1.take(*sent1)
    planes1.take(*planes1.sends())
    planes1.take(*planes1.sends())
    planes1.take(*planes1.sends())
    planes_last.take(*planes_last.sends())
    planes_last.take(*planes_last.sends())
    home_late = to_home({1: after(planes1.value, *home_early[1:3])})
    planes_last.take(*planes_last.sends())
    last = planes_last.value
    home_attend = to_home({0: last[None, :eighth], 2: last[None, eighth : 2 * eighth]})
    small = planes_last.in_order(last[2 * eighth :].astype(F32))

    as_float = counts.astype(F32)
    one = jnp.ones((), F32)
    attend_scales = jnp.stack([as_float[2], one, as_float[2], one])
    expert_scales = jnp.stack([as_float[1], as_float[0], one, as_float[2]])

    def placed(pieces, theirs, scales):
        scale = lax.dynamic_index_in_dim(scales, section, 0).reshape(1, 1)
        return finish(info, scale, pieces, theirs, planes)

    blank = jnp.zeros_like(home_late[0])
    pieces, theirs = [], []
    for early, late in zip(home_early, home_late):
        pieces.append(by_section(section, {0: early, 1: late, 2: blank, 3: early}))
        before = theirs[-1:] + (home_attend[1:3] if len(theirs) == 3 else [])
        theirs.append(over_core(after(pieces[-1], *before) if before else pieces[-1]))
    inputs_whole, outputs_whole = placed(pieces, theirs, expert_scales)
    inputs_whole, home_attend[3] = lax.optimization_barrier((inputs_whole, home_attend[3]))
    blank = jnp.zeros_like(home_attend[0])
    pieces = [by_section(section, {0: got, 1: blank, 2: got, 3: blank}) for got in home_attend]
    theirs = [over_core(piece) for piece in pieces]
    attend_whole, output_whole = placed(pieces, theirs, attend_scales)

    attend_size, expert_size = 5 * width, 3 * width + hidden
    cuts = [attend_size, attend_size + expert_size]
    cuts += [cuts[1] + attend_size, cuts[1] + attend_size + expert_size]
    small = jnp.split(small.reshape(-1)[: cuts[3] + expert_size], cuts)
    none_attend, none_expert = jnp.zeros_like(small[0]), jnp.zeros_like(small[1])
    attend_small = jnp.stack([small[0], none_attend, small[2], none_attend])
    expert_small = jnp.stack([small[1], small[3], none_expert, small[4]])
    attend_small = attend_small / attend_scales.reshape(-1, 1)
    expert_small = expert_small / expert_scales.reshape(-1, 1)
    attend_small = lax.dynamic_index_in_dim(attend_small, section, 0)
    expert_small = lax.dynamic_index_in_dim(expert_small, section, 0)
    return (
        layer_output[:, :positions],
        tokens_grad[:, :positions],
        attend_small[:, :width],
        attend_small[:, width : 2 * width],
        attend_whole,
        attend_small[:, 2 * width :],
        output_whole,
        expert_small[:, :width],
        expert_small[:, width : 2 * width],
        inputs_whole,
        expert_small[:, 2 * width : 2 * width + hidden],
        outputs_whole,
        expert_small[:, 2 * width + hidden :],
        counts,
    )


def solution(mesh):
    sections, groups = mesh.shape["section"], mesh.shape["dp"]
    split = Mesh(mesh.devices.reshape(sections, groups // 2, 2), ("section", "z", "core"))
    items = P(("section", "z", "core"), None, None)
    flat = P("section", None)
    matrix = P("section", None, None)
    placed = (
        items,
        P(("section", "z", "core")),
        flat,
        flat,
        matrix,
        flat,
        matrix,
        flat,
        flat,
        matrix,
        flat,
        matrix,
        flat,
        items,
    )
    return jax.shard_map(
        per_device,
        mesh=split,
        in_specs=placed,
        out_specs=(
            items,
            items,
            flat,
            flat,
            matrix,
            flat,
            matrix,
            flat,
            flat,
            matrix,
            flat,
            matrix,
            flat,
            P(),
        ),
        check_vma=False,
    )
```
